32 devices in a mesh: dp: 8 (over z, x), mp: 4 (over y, core).
Axes of the slice: x: 2, y: 2, z: 4, core: 2. Of those that a mesh axis runs over, the one named last changes fastest.
Arguments:
- frames: bfloat16 [128, 30, 4, 84, 84], P(('dp', 'mp')), may hold values from 0 to 1
- returns: float32 [128, 30], P(('dp', 'mp')), may hold values from 0 to 4
- actions: int32 [128, 30], P(('dp', 'mp')), may hold values from 0 to 17
- starts: int32 [128], P(('dp', 'mp')), may hold values from 0 to 4066
- lengths: int32 [128], P(('dp', 'mp')), may hold values from 1 to 30, as said below
- shared_weights: float32 [1010688], replicated
- shared_first: float32 [1010688], replicated, may hold values from -0.00012207031 to 0.00012207031
- shared_second: float32 [1010688], replicated, may hold values from 3.5589012e-10 to 1.4235605e-09
- split_weights: float32 [394240], P('mp')
- split_first: float32 [394240], P('mp'), may hold values from -0.00012207031 to 0.00012207031
- split_second: float32 [394240], P('mp'), may hold values from 3.5589012e-10 to 1.4235605e-09
Outputs:
- shared_new: float32 [1010688], replicated
- shared_first_new: float32 [1010688], replicated
- shared_second_new: float32 [1010688], replicated
- shared_low: bfloat16 [1010688], replicated
- split_new: float32 [394240], P('mp')
- split_first_new: float32 [394240], P('mp')
- split_second_new: float32 [394240], P('mp')
- split_low: bfloat16 [394240], P('mp')
- grad_norm: float32 [], replicated
- loss_sum: float32 [], replicated
- valid_count: float32 [], replicated
The draws below stay inside these ranges and needn't reach their ends.
Inputs may be any that keep to these rules, and one draw needn't show every extreme that they name: `lengths`: lengths are heavy-tailed and larger on later windows; the last window of all has 30.
All inputs are finite; a program needn't handle non-finite values.
Results may differ from the reference program's by a relative error of at most 0.001.
Values sent between devices are 32-bit elements; how exact they have to be, the bound alone decides.
A program may use at most 192 MiB of HBM per device.

```python
import math
import jax
import jax.numpy as jnp
import numpy as np
from jax import lax

D = 128
FF = 512
ACT = 18
C1 = 32
C2 = 64
TSTEPS = 4096
LAYERS = 2
K = 30
W_DEV = 4
STEP = 10
HD = 16
WINDOWS = 128
SPL = 394240
SHARED_RAW = 1010464
PSH = 1010688
N_DP = 8
N_MP = 4


def shared_layout_drawn():
    return [('conv_one', (C1, 4, 8, 8)), ('bias_one', (C1,)), ('conv_two', (C2, C1, 4, 4)), ('bias_two', (C2,)), ('conv_three', (C2, C2, 3, 3)), ('bias_three', (C2,)), ('encoder', (49 * C2, D)), ('vectors', (6 * LAYERS + 5, D)), ('action_table', (ACT, D)), ('time_table', (TSTEPS, D)), ('head', (D, ACT))]


def shared_profile():
    scales = {'conv_one': 256 ** (-0.5), 'bias_one': 0.2, 'conv_two': (16 * C1) ** (-0.5), 'bias_two': 0.2, 'conv_three': (9 * C2) ** (-0.5), 'bias_three': 0.2, 'encoder': (49 * C2) ** (-0.5), 'action_table': 1.0, 'time_table': 0.5, 'head': D ** (-0.5)}
    centers = []
    spreads = []
    for name, shape in shared_layout_drawn():
        count = math.prod(shape)
        if name == 'vectors':
            row_center = [1.0, 0.0, 1.0, 0.0, 0.0, 0.0] * LAYERS + [1.0, 0.0, 0.0, 0.0, 0.0]
            row_spread = [0.2, 0.3, 0.2, 0.3, 0.3, 0.3] * LAYERS + [0.2, 0.3, 1.0, 0.3, 0.3]
            centers.append(np.repeat(np.array(row_center, np.float32), D))
            spreads.append(np.repeat(np.array(row_spread, np.float32), D))
        else:
            centers.append(np.zeros(count, np.float32))
            spreads.append(np.full(count, scales[name], np.float32))
    tail = PSH - SHARED_RAW
    centers.append(np.zeros(tail, np.float32))
    spreads.append(np.ones(tail, np.float32))
    return (np.concatenate(centers), np.concatenate(spreads))


def draw_shared_weights(key, part):
    key = jax.random.fold_in(key, 21)
    centers, spreads = shared_profile()
    noise = jax.random.normal(key, (PSH,), jnp.float32)
    return jnp.asarray(centers) + jnp.asarray(spreads) * noise


def draw_split_weights(key, part):
    key = jax.random.fold_in(key, 33)
    narrow = D // N_MP
    hidden = FF // N_MP
    pieces = [np.full(D * 3 * narrow, D ** (-0.5), np.float32), np.full(narrow * D, 3.0 * D ** (-0.5), np.float32), np.full(D * hidden, D ** (-0.5), np.float32), np.full(hidden, 0.2, np.float32), np.full(hidden * D, FF ** (-0.5), np.float32)]
    profile = np.tile(np.concatenate(pieces), N_MP * LAYERS)
    noise = jax.random.normal(key, (SPL,), jnp.float32)
    return jnp.asarray(profile) * noise


def draw_lengths(key, part):
    key = jax.random.fold_in(key, 45)
    first_key, second_key = jax.random.split(key)
    index = jnp.arange(WINDOWS, dtype=jnp.int32)
    device = index // W_DEV
    row = device // N_MP
    column = device % N_MP
    ceiling = K * (N_DP - 1 + 2 * row) * (N_MP - 1 + 2 * column) // (9 * (N_DP - 1) * (N_MP - 1))
    ceiling = jnp.clip(ceiling, min(2, K), K)
    first = jax.random.randint(first_key, (WINDOWS,), 0, ceiling + 1)
    second = jax.random.randint(second_key, (WINDOWS,), 0, ceiling + 1)
    drawn = jnp.maximum(first * second // ceiling, 1)
    return jnp.where(index == WINDOWS - 1, K, drawn).astype(jnp.int32)


def plant(entries, stream_key, smallest, top_value):
    shape = entries.shape
    spot = [jax.random.randint(jax.random.fold_in(stream_key, axis), (), 0, shape[axis]) for axis in range(len(shape))]
    entries = entries.at[tuple(spot)].set(smallest)
    longest = shape.index(max(shape))
    spot[longest] = (spot[longest] + 1) % shape[longest]
    return entries.at[tuple(spot)].set(top_value)


def block_scale(stream_key, dims, cuts, smallest, high):
    level, own = 1.0, jax.random.fold_in(stream_key, 6)
    for axis_at, blocks in cuts:
        heights = jnp.exp(jax.random.uniform(jax.random.fold_in(own, axis_at), (blocks,), jnp.float32, smallest / len(cuts), high / len(cuts)))
        level = level * jnp.repeat(heights, dims[axis_at] // blocks).reshape([-1 if axis == axis_at else 1 for axis in range(len(dims))])
    return level


def gaussian(stream_key, dims, scale, most, cuts=(), held_as=jnp.bfloat16):
    values = scale * jax.random.normal(stream_key, dims, jnp.float32)
    if cuts:
        values = values * block_scale(stream_key, dims, cuts, -0.22, 0.18)
    return jnp.clip(values, -most, most).astype(held_as)


def setup_inputs(seed: int = 0) -> dict:
    seeds = jax.random.split(jax.random.key(seed), 12)
    frames = jnp.clip(1.0 * jax.random.uniform(seeds[0], (WINDOWS, K, 4, 84, 84), jnp.float32) ** block_scale(seeds[0], (WINDOWS, K, 4, 84, 84), ((0, 32),), -0.2, 0.2), 0.0, 1.0).astype(jnp.bfloat16)
    returns = jnp.clip(4.0 * jax.random.uniform(seeds[1], (WINDOWS, K), jnp.float32) ** block_scale(seeds[1], (WINDOWS, K), ((0, 32),), -0.2, 0.2), 0.0, 4.0)
    actions = plant(jax.random.randint(seeds[2], (WINDOWS, K), 0, ACT), jax.random.fold_in(seeds[2], 1), 0, ACT - 1).astype(jnp.int32)
    starts = plant(jax.random.randint(seeds[3], (WINDOWS,), 0, TSTEPS - K + 1), jax.random.fold_in(seeds[3], 1), 0, TSTEPS - K).astype(jnp.int32)
    lengths = draw_lengths(jax.random.fold_in(seeds[11], 71), 0)
    shared_weights = draw_shared_weights(jax.random.fold_in(seeds[11], 71), 0)
    shared_first = gaussian(seeds[6], (PSH,), (0.011 / (PSH + SPL) ** 0.5), 0.00012207031, (), jnp.float32)
    shared_second = jnp.clip(jnp.exp(jax.random.uniform(seeds[7], (PSH,), jnp.float32, math.log(3.558901229272493e-10), math.log(1.4235604917089972e-09))), 3.558901229272493e-10, 1.4235604917089972e-09)
    split_weights = draw_split_weights(jax.random.fold_in(seeds[11], 71), 0)
    split_first = gaussian(seeds[9], (SPL,), (0.011 / (PSH + SPL) ** 0.5), 0.00012207031, ((0, 4),), jnp.float32)
    split_second = jnp.clip(jnp.exp(math.log(1.4235604917089972e-09) - 1.3862944 * jax.random.uniform(seeds[10], (SPL,), jnp.float32) ** block_scale(seeds[10], (SPL,), ((0, 4),), -0.2, 0.2)), 3.558901229272493e-10, 1.4235604917089972e-09)
    return dict(frames=frames, returns=returns, actions=actions, starts=starts, lengths=lengths, shared_weights=shared_weights, shared_first=shared_first, shared_second=shared_second, split_weights=split_weights, split_first=split_first, split_second=split_second)


highest = lax.Precision.HIGHEST
clip_limit = 0.1
learn_rate = 0.05
beta_first = 0.9
beta_second = 0.95
adam_epsilon = 1e-08
weight_decay = 0.1

@jax.custom_vjp
def low(v):
    return lax.optimization_barrier(v.astype(jnp.bfloat16)).astype(jnp.float32)

@jax.custom_vjp
def low_back(v):
    return v

def low_keep(v):
    return (low(v), None)

def low_pass(kept, grad):
    return (grad,)

def back_keep(v):
    return (v, None)

def back_low(kept, grad):
    return (low(grad),)
low.defvjp(low_keep, low_pass)
low_back.defvjp(back_keep, back_low)

def shared_layout():
    return [('conv_one', (C1, 4, 8, 8)), ('bias_one', (C1,)), ('conv_two', (C2, C1, 4, 4)), ('bias_two', (C2,)), ('conv_three', (C2, C2, 3, 3)), ('bias_three', (C2,)), ('encoder', (49 * C2, D)), ('vectors', (6 * LAYERS + 5, D)), ('action_table', (ACT, D)), ('time_table', (TSTEPS, D)), ('head', (D, ACT))]

def unpack_shared(flat):
    params = {}
    offset = 0
    for name, shape in shared_layout():
        count = math.prod(shape)
        params[name] = flat[offset:offset + count].reshape(shape)
        offset += count
    return params

def span_layout(narrow, hidden):
    return [('qkv', (D, 3, narrow)), ('output', (narrow, D)), ('up', (D, hidden)), ('up_bias', (hidden,)), ('down', (hidden, D))]

def assemble(flat, copies, narrow, hidden):
    layout = span_layout(narrow, hidden)
    width = sum((math.prod(shape) for name, shape in layout))
    blocks = flat.reshape(copies, LAYERS, width)
    layers = []
    for layer in range(LAYERS):
        offset = 0
        pieces = {}
        for name, shape in layout:
            count = math.prod(shape)
            pieces[name] = blocks[:, layer, offset:offset + count].reshape((copies,) + shape)
            offset += count
        layers.append({'qkv': jnp.moveaxis(pieces['qkv'], 0, 2).reshape(D, 3, copies * narrow), 'output': pieces['output'].reshape(copies * narrow, D), 'up': jnp.moveaxis(pieces['up'], 0, 1).reshape(D, copies * hidden), 'up_bias': pieces['up_bias'].reshape(copies * hidden), 'down': pieces['down'].reshape(copies * hidden, D)})
    return layers

def conv_layer(images, kernel, bias, stride):
    result = lax.conv_general_dilated(images, kernel, (stride, stride), 'VALID', dimension_numbers=('NCHW', 'OIHW', 'NCHW'), precision=highest)
    return jax.nn.gelu(result + bias[None, :, None, None])

def embed_tokens(params, frames, returns, actions, starts):
    wins, steps = returns.shape
    images = frames.reshape(wins * steps, 4, 84, 84)
    hidden = conv_layer(images, params['conv_one'], params['bias_one'], 4)
    hidden = conv_layer(hidden, params['conv_two'], params['bias_two'], 2)
    hidden = conv_layer(hidden, params['conv_three'], params['bias_three'], 1)
    rows = params['vectors']
    base = 6 * LAYERS
    states = jnp.tanh(jnp.dot(hidden.reshape(wins * steps, -1), params['encoder'], precision=highest) + rows[base + 4])
    states = states.reshape(wins, steps, D)
    rewards = jnp.tanh(returns[:, :, None] * rows[base + 2] + rows[base + 3])
    picks = jax.nn.one_hot(actions, ACT, dtype=jnp.float32)
    moves = jnp.tanh(jnp.einsum('wsa,ad->wsd', picks, params['action_table'], precision=highest))
    places = starts[:, None] + jnp.arange(steps, dtype=jnp.int32)[None, :]
    times = jnp.take(params['time_table'], places, axis=0)
    tokens = jnp.stack([rewards, states, moves], axis=2) + times[:, :, None, :]
    return tokens.reshape(wins * 3 * steps, D)

def layer_norm(stream, gain, bias):
    centered = stream - lax.optimization_barrier(jnp.mean(stream, -1, keepdims=True))
    spread = lax.optimization_barrier(jnp.mean(centered * centered, -1, keepdims=True))
    return centered * lax.rsqrt(spread + 1e-05) * gain + bias

def attention(normed, qkv, output, lengths):
    wins = lengths.shape[0]
    tokens = normed.shape[0] // wins
    heads = qkv.shape[-1] // HD
    mixed = jnp.dot(normed, qkv.reshape(D, -1), precision=highest).reshape(wins, tokens, 3, heads, HD)
    query, keys, values = (mixed[:, :, 0], mixed[:, :, 1], mixed[:, :, 2])
    scores = jnp.einsum('wqhe,wkhe->whqk', query, keys, precision=highest) * HD ** (-0.5)
    place = jnp.arange(tokens, dtype=jnp.int32)
    allowed = (place[None, :, None] >= place[None, None, :]) & (place[None, None, :] < 3 * lengths[:, None, None])
    scores = jnp.where(allowed[:, None], scores, -1e+30)
    peak = lax.optimization_barrier(jnp.max(scores, -1, keepdims=True))
    weights = jnp.exp(scores - peak)
    weights = weights / lax.optimization_barrier(jnp.sum(weights, -1, keepdims=True))
    context = jnp.einsum('whqk,wkhe->wqhe', weights, values, precision=highest).reshape(wins * tokens, heads * HD)
    return jnp.dot(context, output, precision=highest)

def feed_forward(normed, up, up_bias, down):
    inner = jax.nn.gelu(jnp.dot(normed, up, precision=highest) + up_bias)
    return jnp.dot(inner, down, precision=highest)

def first_piece(stream, vectors, layer):
    return layer_norm(stream, vectors[6 * layer], vectors[6 * layer + 1])

def middle_piece(stream, mixed, vectors, layer):
    stream = stream + mixed + vectors[6 * layer + 4]
    return (stream, layer_norm(stream, vectors[6 * layer + 2], vectors[6 * layer + 3]))

def last_piece(stream, mixed, vectors, layer):
    return stream + mixed + vectors[6 * layer + 5]

def action_loss(stream, params, actions, lengths):
    rows = params['vectors']
    base = 6 * LAYERS
    wins, steps = actions.shape
    final = layer_norm(stream, rows[base], rows[base + 1]).reshape(wins, steps, 3, D)[:, :, 1]
    logits = jnp.einsum('wsd,da->wsa', final, params['head'], precision=highest)
    peak = lax.optimization_barrier(jnp.max(logits, -1, keepdims=True))
    total = jnp.log(lax.optimization_barrier(jnp.sum(jnp.exp(logits - peak), -1))) + peak[..., 0]
    picked = lax.optimization_barrier(jnp.sum(logits * jax.nn.one_hot(actions, ACT, dtype=jnp.float32), -1))
    valid = (jnp.arange(steps, dtype=jnp.int32)[None, :] < lengths[:, None]).astype(jnp.float32)
    return jnp.sum((total - picked) * valid)

def adam_update(weights, first, second, grads):
    first = beta_first * first + (1 - beta_first) * grads
    second = beta_second * second + (1 - beta_second) * grads * grads
    fix_one = 1 - beta_first ** STEP
    fix_two = 1 - beta_second ** STEP
    weights = weights - learn_rate * (first / fix_one / (jnp.sqrt(second / fix_two) + adam_epsilon) + weight_decay * weights)
    return (weights, first, second)

def group_loss(shared, split, frames, returns, actions, starts, lengths):
    params = unpack_shared(shared)
    layers = assemble(split, N_MP, D // N_MP, FF // N_MP)
    stream = embed_tokens(params, frames.astype(jnp.float32), returns, actions, starts)
    for layer in range(LAYERS):
        weights = layers[layer]
        normed = first_piece(stream, params['vectors'], layer)
        mixed = attention(normed, weights['qkv'], weights['output'], lengths)
        stream, normed = middle_piece(stream, mixed, params['vectors'], layer)
        mixed = feed_forward(normed, weights['up'], weights['up_bias'], weights['down'])
        stream = last_piece(stream, mixed, params['vectors'], layer)
    return action_loss(stream, params, actions, lengths)

def reference(frames, returns, actions, starts, lengths, shared_weights, shared_first, shared_second, split_weights, split_first, split_second):
    groups = N_DP
    valid_count = jnp.sum(lengths).astype(jnp.float32)
    blocks = (frames.reshape((groups, -1) + frames.shape[1:]), returns.reshape(groups, -1, K), actions.reshape(groups, -1, K), starts.reshape(groups, -1), lengths.reshape(groups, -1))

    def visit(carry, block):

        def local(shared, split):
            return group_loss(shared, split, block[0], block[1], block[2], block[3], block[4])
        loss, back = jax.vjp(local, shared_weights, split_weights)
        grad_shared, grad_split = back(1.0 / valid_count)
        return ((carry[0] + loss, carry[1] + grad_shared, carry[2] + grad_split), None)
    start = (jnp.zeros((), jnp.float32), jnp.zeros_like(shared_weights), jnp.zeros_like(split_weights))
    (loss_sum, grad_shared, grad_split), unused = lax.scan(visit, start, blocks)
    grad_norm = jnp.sqrt(jnp.sum(grad_shared * grad_shared) + jnp.sum(grad_split * grad_split))
    factor = jnp.minimum(1.0, clip_limit / (grad_norm + 1e-06))
    shared_new, shared_m, shared_v = adam_update(shared_weights, shared_first, shared_second, grad_shared * factor)
    split_new, split_m, split_v = adam_update(split_weights, split_first, split_second, grad_split * factor)
    return (shared_new, shared_m, shared_v, shared_new.astype(jnp.bfloat16), split_new, split_m, split_v, split_new.astype(jnp.bfloat16), grad_norm, loss_sum, valid_count)
```

```python
from functools import partial
import math

import jax
import jax.numpy as jnp
from jax import lax
from jax.sharding import PartitionSpec as P

D = 128
FF = 512
ACT = 18
C1 = 32
C2 = 64
TSTEPS = 4096
LAYERS = 2
STEP = 10
HD = 16


high = lax.Precision.HIGH
clip_limit = 0.1
learn_rate = 0.05
beta_first = 0.9
beta_second = 0.95
adam_epsilon = 1e-08
weight_decay = 0.1


def shared_layout():
    return [
        ("conv_one", (C1, 4, 8, 8)),
        ("bias_one", (C1,)),
        ("conv_two", (C2, C1, 4, 4)),
        ("bias_two", (C2,)),
        ("conv_three", (C2, C2, 3, 3)),
        ("bias_three", (C2,)),
        ("encoder", (49 * C2, D)),
        ("vectors", (6 * LAYERS + 5, D)),
        ("action_table", (ACT, D)),
        ("time_table", (TSTEPS, D)),
        ("head", (D, ACT)),
    ]


def unpack_shared(flat):
    params = {}
    offset = 0
    for name, shape in shared_layout():
        count = math.prod(shape)
        params[name] = flat[offset : offset + count].reshape(shape)
        offset += count
    return params


def pack_shared(grads, total):
    flat = jnp.concatenate([grads[name].reshape(-1) for name, shape in shared_layout()])
    return jnp.concatenate([flat, jnp.zeros((total - flat.shape[0],), jnp.float32)])


def span_layout(narrow, hidden):
    return [
        ("qkv", (D, 3, narrow)),
        ("output", (narrow, D)),
        ("up", (D, hidden)),
        ("up_bias", (hidden,)),
        ("down", (hidden, D)),
    ]


def assemble(flat, copies, narrow, hidden):
    layout = span_layout(narrow, hidden)
    width = sum((math.prod(shape) for name, shape in layout))
    blocks = flat.reshape(copies, LAYERS, width)
    layers = []
    for layer in range(LAYERS):
        offset = 0
        pieces = {}
        for name, shape in layout:
            count = math.prod(shape)
            pieces[name] = blocks[:, layer, offset : offset + count].reshape((copies,) + shape)
            offset += count
        layers.append(
            {
                "qkv": jnp.moveaxis(pieces["qkv"], 0, 2).reshape(D, 3, copies * narrow),
                "output": pieces["output"].reshape(copies * narrow, D),
                "up": jnp.moveaxis(pieces["up"], 0, 1).reshape(D, copies * hidden),
                "up_bias": pieces["up_bias"].reshape(copies * hidden),
                "down": pieces["down"].reshape(copies * hidden, D),
            }
        )
    return layers


def conv_layer(images, kernel, bias, stride):
    result = lax.conv_general_dilated(
        images,
        kernel,
        (stride, stride),
        "VALID",
        dimension_numbers=("NCHW", "OIHW", "NCHW"),
        precision=high,
    )
    return jax.nn.gelu(result + bias[None, :, None, None])


def embed_tokens(params, frames, returns, actions, starts):
    wins, steps = returns.shape
    images = frames.reshape(wins * steps, 4, 84, 84)
    hidden = conv_layer(images, params["conv_one"], params["bias_one"], 4)
    hidden = conv_layer(hidden, params["conv_two"], params["bias_two"], 2)
    hidden = conv_layer(hidden, params["conv_three"], params["bias_three"], 1)
    rows = params["vectors"]
    base = 6 * LAYERS
    states = jnp.tanh(
        jnp.dot(hidden.reshape(wins * steps, -1), params["encoder"], precision=high)
        + rows[base + 4]
    )
    states = states.reshape(wins, steps, D)
    rewards = jnp.tanh(returns[:, :, None] * rows[base + 2] + rows[base + 3])
    picks = jax.nn.one_hot(actions, ACT, dtype=jnp.float32)
    moves = jnp.tanh(jnp.einsum("wsa,ad->wsd", picks, params["action_table"], precision=high))
    places = starts[:, None] + jnp.arange(steps, dtype=jnp.int32)[None, :]
    times = jnp.take(params["time_table"], places, axis=0)
    tokens = jnp.stack([rewards, states, moves], axis=2) + times[:, :, None, :]
    return tokens.reshape(wins * 3 * steps, D)


def layer_norm(stream, gain, bias):
    centered = stream - jnp.mean(stream, -1, keepdims=True)
    spread = jnp.mean(centered * centered, -1, keepdims=True)
    return centered * lax.rsqrt(spread + 1e-05) * gain + bias


def attention(normed, qkv, output, lengths):
    wins = lengths.shape[0]
    tokens = normed.shape[0] // wins
    heads = qkv.shape[-1] // HD
    mixed = jnp.dot(normed, qkv.reshape(D, -1), precision=high).reshape(
        wins, tokens, 3, heads, HD
    )
    query, keys, values = (mixed[:, :, 0], mixed[:, :, 1], mixed[:, :, 2])
    scores = jnp.einsum("wqhe,wkhe->whqk", query, keys, precision=high) * HD ** (-0.5)
    place = jnp.arange(tokens, dtype=jnp.int32)
    allowed = (place[None, :, None] >= place[None, None, :]) & (
        place[None, None, :] < 3 * lengths[:, None, None]
    )
    scores = jnp.where(allowed[:, None], scores, -1e30)
    peak = jnp.max(scores, -1, keepdims=True)
    weights = jnp.exp(scores - peak)
    weights = weights / jnp.sum(weights, -1, keepdims=True)
    context = jnp.einsum("whqk,wkhe->wqhe", weights, values, precision=high).reshape(
        wins * tokens, heads * HD
    )
    return jnp.dot(context, output, precision=high)


def feed_forward(normed, up, up_bias, down):
    inner = jax.nn.gelu(jnp.dot(normed, up, precision=high) + up_bias)
    return jnp.dot(inner, down, precision=high)


def first_piece(stream, vectors, layer):
    return layer_norm(stream, vectors[6 * layer], vectors[6 * layer + 1])


def middle_piece(stream, mixed, vectors, layer):
    stream = stream + mixed + vectors[6 * layer + 4]
    return (stream, layer_norm(stream, vectors[6 * layer + 2], vectors[6 * layer + 3]))


def last_piece(stream, mixed, vectors, layer):
    return stream + mixed + vectors[6 * layer + 5]


def action_loss(stream, params, actions, lengths):
    rows = params["vectors"]
    base = 6 * LAYERS
    wins, steps = actions.shape
    final = layer_norm(stream, rows[base], rows[base + 1]).reshape(wins, steps, 3, D)[:, :, 1]
    logits = jnp.einsum("wsd,da->wsa", final, params["head"], precision=high)
    peak = jnp.max(logits, -1, keepdims=True)
    total = jnp.log(jnp.sum(jnp.exp(logits - peak), -1)) + peak[..., 0]
    picked = jnp.sum(logits * jax.nn.one_hot(actions, ACT, dtype=jnp.float32), -1)
    valid = (jnp.arange(steps, dtype=jnp.int32)[None, :] < lengths[:, None]).astype(jnp.float32)
    return jnp.sum((total - picked) * valid)


def adam_update(weights, first, second, grads):
    first = beta_first * first + (1 - beta_first) * grads
    second = beta_second * second + (1 - beta_second) * grads * grads
    fix_one = 1 - beta_first**STEP
    fix_two = 1 - beta_second**STEP
    weights = weights - learn_rate * (
        first / fix_one / (jnp.sqrt(second / fix_two) + adam_epsilon) + weight_decay * weights
    )
    return (weights, first, second)


def per_device(
    frames,
    returns,
    actions,
    starts,
    lengths,
    shared_weights,
    shared_first,
    shared_second,
    split_weights,
    split_first,
    split_second,
):
    parts = lax.axis_size("mp")
    narrow = D // parts
    hidden_width = FF // parts
    split_all = lax.all_gather(split_weights, "mp", axis=0, tiled=True)
    params = unpack_shared(shared_weights)
    images = frames.astype(jnp.float32)

    def local_loss(table, flat):
        layers = assemble(flat, parts, narrow, hidden_width)
        stream = embed_tokens(table, images, returns, actions, starts)
        for layer in range(LAYERS):
            weights = layers[layer]
            normed = first_piece(stream, table["vectors"], layer)
            mixed = attention(normed, weights["qkv"], weights["output"], lengths)
            stream, normed = middle_piece(stream, mixed, table["vectors"], layer)
            mixed = feed_forward(normed, weights["up"], weights["up_bias"], weights["down"])
            stream = last_piece(stream, mixed, table["vectors"], layer)
        return action_loss(stream, table, actions, lengths)

    loss_local, (grads, split_grad) = jax.value_and_grad(local_loss, argnums=(0, 1))(
        params, split_all
    )
    count_local = jnp.sum(lengths).astype(jnp.float32)
    pieces = [grads[name].reshape(-1) for name, shape in shared_layout()]
    raw = sum(piece.shape[0] for piece in pieces)
    total = shared_weights.shape[0]
    tail = jnp.zeros((total - raw,), jnp.float32)
    scalars = jnp.stack([loss_local, count_local])
    flat = jnp.concatenate(pieces + [tail, split_grad, scalars])
    summed = lax.psum(flat, ("dp", "mp"))
    loss_sum = summed[-2]
    valid_count = summed[-1]
    seed = 1.0 / valid_count
    summed = summed[:-2] * seed
    grad_norm = jnp.sqrt(jnp.sum(summed * summed))
    factor = jnp.minimum(1.0, clip_limit / (grad_norm + 1e-06))
    width = split_weights.shape[0]
    split_sum = lax.dynamic_slice(summed, (total + lax.axis_index("mp") * width,), (width,))
    split_new, split_m, split_v = adam_update(
        split_weights, split_first, split_second, split_sum * factor
    )
    shared_new, shared_m, shared_v = adam_update(
        shared_weights, shared_first, shared_second, summed[:total] * factor
    )
    return (
        shared_new,
        shared_m,
        shared_v,
        shared_new.astype(jnp.bfloat16),
        split_new,
        split_m,
        split_v,
        split_new.astype(jnp.bfloat16),
        grad_norm,
        loss_sum,
        valid_count,
    )


def solution(mesh):
    return jax.shard_map(
        per_device,
        mesh=mesh,
        in_specs=(
            P(("dp", "mp"), None, None, None, None),
            P(("dp", "mp"), None),
            P(("dp", "mp"), None),
            P(("dp", "mp")),
            P(("dp", "mp")),
            P(),
            P(),
            P(),
            P("mp"),
            P("mp"),
            P("mp"),
        ),
        out_specs=(P(), P(), P(), P(), P("mp"), P("mp"), P("mp"), P("mp"), P(), P(), P()),
        check_vma=False,
    )
```

```python
from functools import partial
import math

import jax
import jax.numpy as jnp
from jax import lax
from jax.experimental import pallas as pl
from jax.experimental.pallas import tpu as pltpu
from jax.sharding import PartitionSpec as P

D = 128
FF = 512
ACT = 18
C1 = 32
C2 = 64
TSTEPS = 4096
LAYERS = 2
STEP = 10
HD = 16


high = lax.Precision.HIGH
clip_limit = 0.1
learn_rate = 0.05
beta_first = 0.9
beta_second = 0.95
adam_epsilon = 1e-08
weight_decay = 0.1


def shared_layout():
    return [
        ("conv_one", (C1, 4, 8, 8)),
        ("bias_one", (C1,)),
        ("conv_two", (C2, C1, 4, 4)),
        ("bias_two", (C2,)),
        ("conv_three", (C2, C2, 3, 3)),
        ("bias_three", (C2,)),
        ("encoder", (49 * C2, D)),
        ("vectors", (6 * LAYERS + 5, D)),
        ("action_table", (ACT, D)),
        ("time_table", (TSTEPS, D)),
        ("head", (D, ACT)),
    ]


def unpack_shared(flat):
    params = {}
    offset = 0
    for name, shape in shared_layout():
        count = math.prod(shape)
        params[name] = flat[offset : offset + count].reshape(shape)
        offset += count
    return params


def pack_shared(grads, total):
    flat = jnp.concatenate([grads[name].reshape(-1) for name, shape in shared_layout()])
    return jnp.concatenate([flat, jnp.zeros((total - flat.shape[0],), jnp.float32)])


def span_layout(narrow, hidden):
    return [
        ("qkv", (D, 3, narrow)),
        ("output", (narrow, D)),
        ("up", (D, hidden)),
        ("up_bias", (hidden,)),
        ("down", (hidden, D)),
    ]


def assemble(flat, copies, narrow, hidden):
    layout = span_layout(narrow, hidden)
    width = sum((math.prod(shape) for name, shape in layout))
    blocks = flat.reshape(copies, LAYERS, width)
    layers = []
    for layer in range(LAYERS):
        offset = 0
        pieces = {}
        for name, shape in layout:
            count = math.prod(shape)
            pieces[name] = blocks[:, layer, offset : offset + count].reshape((copies,) + shape)
            offset += count
        layers.append(
            {
                "qkv": jnp.moveaxis(pieces["qkv"], 0, 2).reshape(D, 3, copies * narrow),
                "output": pieces["output"].reshape(copies * narrow, D),
                "up": jnp.moveaxis(pieces["up"], 0, 1).reshape(D, copies * hidden),
                "up_bias": pieces["up_bias"].reshape(copies * hidden),
                "down": pieces["down"].reshape(copies * hidden, D),
            }
        )
    return layers


def conv_layer(images, kernel, bias, stride):
    result = lax.conv_general_dilated(
        images,
        kernel,
        (stride, stride),
        "VALID",
        dimension_numbers=("NCHW", "OIHW", "NCHW"),
        precision=high,
    )
    return jax.nn.gelu(result + bias[None, :, None, None])


def embed_tokens(params, frames, returns, actions, times):
    wins, steps = returns.shape
    images = frames.reshape(wins * steps, 4, 84, 84)
    hidden = conv_layer(images, params["conv_one"], params["bias_one"], 4)
    hidden = conv_layer(hidden, params["conv_two"], params["bias_two"], 2)
    hidden = conv_layer(hidden, params["conv_three"], params["bias_three"], 1)
    rows = params["vectors"]
    base = 6 * LAYERS
    states = jnp.tanh(
        jnp.dot(hidden.reshape(wins * steps, -1), params["encoder"], precision=high)
        + rows[base + 4]
    )
    states = states.reshape(wins, steps, D)
    rewards = jnp.tanh(returns[:, :, None] * rows[base + 2] + rows[base + 3])
    picks = jax.nn.one_hot(actions, ACT, dtype=jnp.float32)
    moves = jnp.tanh(jnp.einsum("wsa,ad->wsd", picks, params["action_table"], precision=high))
    tokens = jnp.stack([rewards, states, moves], axis=2) + times[:, :, None, :]
    return tokens.reshape(wins * 3 * steps, D)


def layer_norm(stream, gain, bias):
    centered = stream - jnp.mean(stream, -1, keepdims=True)
    spread = jnp.mean(centered * centered, -1, keepdims=True)
    return centered * lax.rsqrt(spread + 1e-05) * gain + bias


def attention(normed, qkv, output, lengths):
    wins = lengths.shape[0]
    tokens = normed.shape[0] // wins
    heads = qkv.shape[-1] // HD
    mixed = jnp.dot(normed, qkv.reshape(D, -1), precision=high).reshape(
        wins, tokens, 3, heads, HD
    )
    query, keys, values = (mixed[:, :, 0], mixed[:, :, 1], mixed[:, :, 2])
    scores = jnp.einsum("wqhe,wkhe->whqk", query, keys, precision=high) * HD ** (-0.5)
    place = jnp.arange(tokens, dtype=jnp.int32)
    allowed = (place[None, :, None] >= place[None, None, :]) & (
        place[None, None, :] < 3 * lengths[:, None, None]
    )
    scores = jnp.where(allowed[:, None], scores, -1e30)
    peak = jnp.max(scores, -1, keepdims=True)
    weights = jnp.exp(scores - peak)
    weights = weights / jnp.sum(weights, -1, keepdims=True)
    context = jnp.einsum("whqk,wkhe->wqhe", weights, values, precision=high).reshape(
        wins * tokens, heads * HD
    )
    return jnp.dot(context, output, precision=high)


def feed_forward(normed, up, up_bias, down):
    inner = jax.nn.gelu(jnp.dot(normed, up, precision=high) + up_bias)
    return jnp.dot(inner, down, precision=high)


def first_piece(stream, vectors, layer):
    return layer_norm(stream, vectors[6 * layer], vectors[6 * layer + 1])


def middle_piece(stream, mixed, vectors, layer):
    stream = stream + mixed + vectors[6 * layer + 4]
    return (stream, layer_norm(stream, vectors[6 * layer + 2], vectors[6 * layer + 3]))


def last_piece(stream, mixed, vectors, layer):
    return stream + mixed + vectors[6 * layer + 5]


def action_loss(stream, params, actions, lengths):
    rows = params["vectors"]
    base = 6 * LAYERS
    wins, steps = actions.shape
    final = layer_norm(stream, rows[base], rows[base + 1]).reshape(wins, steps, 3, D)[:, :, 1]
    logits = jnp.einsum("wsd,da->wsa", final, params["head"], precision=high)
    peak = jnp.max(logits, -1, keepdims=True)
    total = jnp.log(jnp.sum(jnp.exp(logits - peak), -1)) + peak[..., 0]
    picked = jnp.sum(logits * jax.nn.one_hot(actions, ACT, dtype=jnp.float32), -1)
    valid = (jnp.arange(steps, dtype=jnp.int32)[None, :] < lengths[:, None]).astype(jnp.float32)
    return jnp.sum((total - picked) * valid)


def bit_orders(dp_size, mp_size):
    dp_bits = [("dp", k) for k in range(dp_size.bit_length() - 1)]
    mp_bits = [("mp", k) for k in range(mp_size.bit_length() - 1)]
    core, ys = mp_bits[:1], mp_bits[1:]
    middle = len(dp_bits) // 3
    xs, zs = dp_bits[:middle], dp_bits[middle:]
    return [core + xs + zs + ys, core + zs + ys + xs, core + ys + xs + zs]


def reduce_kernel(plan, *refs):
    inputs, steps = plan["inputs"], plan["steps"]
    ins = refs[: len(inputs)]
    out_shared, out_split, out_square = refs[len(inputs) : len(inputs) + 3]
    (work, landing, total, split_total, tiles, tile_in) = refs[len(inputs) + 3 : len(inputs) + 9]
    (load_sem, send_sem, recv_sem, tile_send, tile_recv, store_sem) = refs[len(inputs) + 9 :]
    spots = {"dp": lax.axis_index("dp"), "mp": lax.axis_index("mp")}

    def value(bit):
        return lax.rem(lax.div(spots[bit[0]], 1 << bit[1]), 2)

    def partner(bit):
        axis, k = bit
        other = spots[axis] + (1 - 2 * value(bit)) * (1 << k)
        place = dict(spots)
        place[axis] = other
        return (place["dp"], place["mp"])

    loads = []
    for number, (start, rows) in enumerate(inputs):
        loads.append(
            pltpu.make_async_copy(
                ins[number], work.at[pl.ds(start, rows)], load_sem.at[number]
            )
        )
        loads[-1].start()
    for start, rows in plan["blank"]:
        work[pl.ds(start, rows)] = jnp.zeros((rows, 128), jnp.float32)
    barrier = pltpu.get_barrier_semaphore()
    bits = plan["bits"]
    for bit in bits:
        pl.semaphore_signal(
            barrier, inc=1, device_id=partner(bit), device_id_type=pl.DeviceIdType.MESH
        )
    pl.semaphore_wait(barrier, len(bits))
    for load in loads:
        load.wait()

    def add_rows(target, start, source_start, rows):
        chunk = math.gcd(rows, 64)

        def body(turn, carry):
            spot = pl.multiple_of(start + turn * chunk, 8)
            place = pl.multiple_of(source_start + turn * chunk, 8)
            target[pl.ds(spot, chunk)] = (
                target[pl.ds(spot, chunk)] + landing[pl.ds(place, chunk)]
            )
            return carry

        lax.fori_loop(0, rows // chunk, body, 0)

    streams = plan["streams"]
    where = [stream["base"] for stream in streams]
    sizes = [stream["rows"] for stream in streams]
    flights = [None] * len(streams)
    landings = [stream["landing"] for stream in streams]
    slot = 0
    for step in range(steps):
        for number, stream in enumerate(streams):
            if flights[number] is not None:
                copy, half, land, keep = flights[number]
                copy.wait()
                add_rows(work, keep, land, half)
                where[number] = keep
            bit = stream["order"][step]
            half = sizes[number] // 2
            mine = value(bit)
            keep = where[number] + mine * half
            give = where[number] + (1 - mine) * half
            copy = pltpu.make_async_remote_copy(
                src_ref=work.at[pl.ds(pl.multiple_of(give, 8), half)],
                dst_ref=landing.at[pl.ds(landings[number], half)],
                send_sem=send_sem.at[slot],
                recv_sem=recv_sem.at[slot],
                device_id=partner(bit),
                device_id_type=pl.DeviceIdType.MESH,
            )
            copy.start()
            slot += 1
            flights[number] = (copy, half, landings[number], keep)
            landings[number] += half
            sizes[number] = half
    backs = [list(reversed(stream["order"][stream["shared"] :])) for stream in streams]
    spaces = []
    for number, stream in enumerate(streams):
        copy, half, land, keep = flights[number]
        copy.wait()
        add_rows(work, keep, land, half)
        where[number] = keep
        if stream["shared"]:
            spaces.append(split_total)
            low = keep
            for bit in stream["order"][: stream["shared"]]:
                pass
            rows = half
            offset = jnp.int32(0)
            size = stream["rows"] >> stream["shared"]
            for bit in stream["order"][stream["shared"] :]:
                size //= 2
                offset = offset + value(bit) * size
            split_total[pl.ds(pl.multiple_of(offset, 8), rows)] = work[
                pl.ds(pl.multiple_of(keep, 8), rows)
            ]
            held = work[pl.ds(pl.multiple_of(keep, 8), rows)]
            squares = held * held
            tiles[0] = jnp.sum(squares.reshape(rows // 8, 8, 128), axis=0)
            where[number] = offset
        else:
            spaces.append(total)
            total[pl.ds(pl.multiple_of(keep, 8), half)] = work[
                pl.ds(pl.multiple_of(keep, 8), half)
            ]
    flights = [None] * len(streams)
    tile_flight = None
    for step in range(steps):
        if tile_flight is not None:
            tile_flight.wait()
            tiles[step] = tiles[step - 1] + tile_in[step - 1]
        tile_flight = pltpu.make_async_remote_copy(
            src_ref=tiles.at[step],
            dst_ref=tile_in.at[step],
            send_sem=tile_send.at[step],
            recv_sem=tile_recv.at[step],
            device_id=partner(bits[step]),
            device_id_type=pl.DeviceIdType.MESH,
        )
        tile_flight.start()
        for number, stream in enumerate(streams):
            if flights[number] is not None:
                copy, low, size = flights[number]
                copy.wait()
                where[number] = low
                sizes[number] = size
                flights[number] = None
            if step >= len(backs[number]):
                continue
            bit = backs[number][step]
            rows = sizes[number]
            region = spaces[number].at[pl.ds(pl.multiple_of(where[number], 8), rows)]
            copy = pltpu.make_async_remote_copy(
                src_ref=region,
                dst_ref=region,
                send_sem=send_sem.at[slot],
                recv_sem=recv_sem.at[slot],
                device_id=partner(bit),
                device_id_type=pl.DeviceIdType.MESH,
            )
            copy.start()
            slot += 1
            flights[number] = (copy, where[number] - value(bit) * rows, rows * 2)
    tile_flight.wait()
    out_square[...] = tiles[steps - 1] + tile_in[steps - 1]
    stores = []
    for number, stream in enumerate(streams):
        if flights[number] is not None:
            flights[number][0].wait()
    shared_rows = total.shape[0]
    stores.append(
        pltpu.make_async_copy(total, out_shared.at[pl.ds(0, shared_rows)], store_sem.at[0])
    )
    stores.append(pltpu.make_async_copy(split_total, out_split, store_sem.at[1]))
    for store in stores:
        store.start()
    for store in stores:
        store.wait()


def reduce_all(pieces, split_blocks, dp_size, mp_size, out_rows, collective_id):
    orders = bit_orders(dp_size, mp_size)
    bits = orders[0]
    steps = len(bits)
    grain = 8 << steps
    used = max(start + array.shape[0] for start, array in pieces)
    half = -(-used // (2 * grain)) * grain
    shared_rows = 2 * half
    span = split_blocks[0].shape[0]
    split_grain = 8 * dp_size
    block = -(-span // split_grain) * split_grain
    inputs, arrays, blank = [], [], []
    reach = 0
    for start, array in pieces:
        if start > reach:
            blank.append((reach, start - reach))
        inputs.append((start, array.shape[0]))
        arrays.append(array)
        reach = start + array.shape[0]
    if shared_rows > reach:
        blank.append((reach, shared_rows - reach))
    shared_steps = mp_size.bit_length() - 1
    for number in range(mp_size):
        turned = 0
        for k in range(shared_steps):
            turned |= ((number >> k) & 1) << (shared_steps - 1 - k)
        start = shared_rows + turned * block
        inputs.append((start, span))
        arrays.append(split_blocks[number])
        if block > span:
            blank.append((start + span, block - span))
    split_rows = mp_size * block
    work_rows = shared_rows + split_rows
    streams = [
        dict(base=0, rows=half, order=orders[0], shared=0, landing=0),
        dict(base=half, rows=half, order=orders[1], shared=0, landing=half),
        dict(
            base=shared_rows,
            rows=split_rows,
            order=orders[2],
            shared=shared_steps,
            landing=shared_rows,
        ),
    ]
    plan = dict(inputs=inputs, blank=blank, streams=streams, bits=bits, steps=steps)
    copies = 3 * 2 * steps
    return pl.pallas_call(
        partial(reduce_kernel, plan),
        out_shape=(
            jax.ShapeDtypeStruct((out_rows, 128), jnp.float32),
            jax.ShapeDtypeStruct((block, 128), jnp.float32),
            jax.ShapeDtypeStruct((8, 128), jnp.float32),
        ),
        in_specs=[pl.BlockSpec(memory_space=pl.ANY)] * len(arrays),
        out_specs=(
            pl.BlockSpec(memory_space=pl.ANY),
            pl.BlockSpec(memory_space=pl.ANY),
            pl.BlockSpec(memory_space=pltpu.VMEM),
        ),
        scratch_shapes=[
            pltpu.VMEM((work_rows, 128), jnp.float32),
            pltpu.VMEM((work_rows, 128), jnp.float32),
            pltpu.VMEM((shared_rows, 128), jnp.float32),
            pltpu.VMEM((block, 128), jnp.float32),
            pltpu.VMEM((steps, 8, 128), jnp.float32),
            pltpu.VMEM((steps, 8, 128), jnp.float32),
            pltpu.SemaphoreType.DMA((len(arrays),)),
            pltpu.SemaphoreType.DMA((copies,)),
            pltpu.SemaphoreType.DMA((copies,)),
            pltpu.SemaphoreType.DMA((steps,)),
            pltpu.SemaphoreType.DMA((steps,)),
            pltpu.SemaphoreType.DMA((2,)),
        ],
        compiler_params=pltpu.CompilerParams(
            collective_id=collective_id,
            has_side_effects=True,
            vmem_limit_bytes=56 * 1024 * 1024,
        ),
        name="reduce_gradients",
    )(*arrays)


def spans(fast_rows):
    places = {}
    at = 0
    for name, rows in [
        ("encoder", 3136),
        ("conv", 616),
        ("vectors", 24),
        ("action_table", 24),
        ("head", 24),
        ("scalars", 8),
        ("times", fast_rows),
    ]:
        places[name] = (at, rows)
        at += rows
    return places, at


FLAT_ROWS = 7896
BLOCK_ROWS = 512
LATE = 609


def adam_kernel(
    fast_rows,
    most_rows,
    starts_ref,
    lengths_ref,
    flag_ref,
    reduced_ref,
    split_ref,
    square_ref,
    weight_ref,
    first_ref,
    second_ref,
    split_weight_ref,
    split_first_ref,
    split_second_ref,
    new_ref,
    new_first_ref,
    new_second_ref,
    split_new_ref,
    split_new_first_ref,
    split_new_second_ref,
    scalar_ref,
    pulled,
    flat,
    factor_ref,
    edge_ref,
    pull_sem,
):
    step = pl.program_id(0)
    places, fast_total = spans(fast_rows)
    lane = lax.broadcasted_iota(jnp.int32, (1, 128), 1)

    def update(weights, first, second, grads):
        first = beta_first * first + (1 - beta_first) * grads
        second = beta_second * second + (1 - beta_second) * grads * grads
        fix_one = 1 - beta_first**STEP
        fix_two = 1 - beta_second**STEP
        weights = weights - learn_rate * (
            first / fix_one / (jnp.sqrt(second / fix_two) + adam_epsilon) + weight_decay * weights
        )
        return weights, first, second

    @pl.when(step == 0)
    def prepare():
        pull = pltpu.make_async_copy(
            reduced_ref.at[pl.ds(0, fast_total)], pulled.at[pl.ds(0, fast_total)], pull_sem
        )
        pull.start()
        times_at = LATE + 35
        table_at = LATE + 17 + ACT

        def wipe(turn, carry):
            flat[pl.ds(pl.multiple_of(turn * 64, 64), 64)] = jnp.zeros((64, 128), jnp.float32)
            return carry

        lax.fori_loop(0, flat.shape[0] // 64, wipe, 0)
        pull.wait()
        squares = jnp.zeros((8, 128), jnp.float32)

        def fold(rows):
            return jnp.sum((rows * rows).reshape(-1, 8, 128), axis=0)

        def conv_rows(turn, carry):
            spot = pl.multiple_of(turn * 56, 8)
            held = pulled[pl.ds(places["conv"][0] + spot, 56)]
            flat[pl.ds(8 + spot, 56)] = held
            return carry + fold(held)

        squares = lax.fori_loop(0, 616 // 56, conv_rows, squares)
        edge_ref[...] = flat[LATE : LATE + 16]

        def encoder_rows(turn, carry):
            spot = pl.multiple_of(turn * 64, 64)
            held = pulled[pl.ds(spot, 64)]
            flat[pl.ds(8 + LATE + spot, 64)] = pltpu.roll(held, 32, 1)
            return carry + fold(held)

        squares = lax.fori_loop(0, 3136 // 64, encoder_rows, squares)
        for name, at, rows in [
            ("vectors", LATE + 3136, 17),
            ("action_table", LATE + 3153, ACT),
            ("head", LATE + 3171 + TSTEPS, ACT),
        ]:
            held = pulled[places[name][0] : places[name][0] + 24]
            squares = squares + fold(held)
            flat[8 + at : 8 + at + rows] = pltpu.roll(held, 32, 1)[:rows]
        time_at = 8 + LATE + 3171

        @pl.when(flag_ref[0] > 0)
        def scatter():
            windows = starts_ref.shape[0]

            def window(number, offset):
                length = lengths_ref[number]
                start = starts_ref[number]

                def chunk(turn, carry):
                    rows = pulled[pl.ds(places["times"][0] + offset + turn * 8, 8)]
                    left = length - turn * 8
                    keep = lax.broadcasted_iota(jnp.int32, (8, 1), 0) < left
                    spot = pl.ds(time_at + start + turn * 8, 8)
                    flat[spot] = flat[spot] + jnp.where(keep, pltpu.roll(rows, 32, 1), 0.0)
                    return carry

                lax.fori_loop(0, lax.div(length + 7, 8), chunk, 0)
                return offset + length

            lax.fori_loop(0, windows, window, jnp.int32(0))

        @pl.when(flag_ref[0] <= 0)
        def whole_table():
            pull_table = pltpu.make_async_copy(
                reduced_ref.at[pl.ds(places["times"][0], TSTEPS)],
                pulled.at[pl.ds(places["times"][0], TSTEPS)],
                pull_sem,
            )
            pull_table.start()
            pull_table.wait()

            def rows_in(turn, carry):
                spot = pl.multiple_of(turn * 64, 64)
                held = pulled[pl.ds(places["times"][0] + spot, 64)]
                flat[pl.ds(time_at + spot, 64)] = pltpu.roll(held, 32, 1)
                return carry

            lax.fori_loop(0, TSTEPS // 64, rows_in, 0)

        def time_squares(turn, carry):
            return carry + fold(flat[pl.ds(time_at + turn * 64, 64)])

        squares = lax.fori_loop(0, TSTEPS // 64, time_squares, squares)
        squares = squares + square_ref[...]
        count = jnp.float32(0)
        whole = lax.fori_loop(
            0, lengths_ref.shape[0], lambda k, c: c + lengths_ref[k], jnp.int32(0)
        )
        count = jnp.full((1, 128), whole.astype(jnp.float32))
        scalars = pulled[places["scalars"][0] : places["scalars"][0] + 8]
        total = jnp.sum(jnp.sum(squares, axis=0, keepdims=True), axis=1, keepdims=True)
        seed = 1.0 / count
        norm = jnp.sqrt(jnp.broadcast_to(total, (1, 128))) * seed
        factor = jnp.minimum(1.0, clip_limit / (norm + 1e-06)) * seed
        factor_ref[...] = jnp.broadcast_to(factor, (8, 128))
        loss = jnp.broadcast_to(scalars[0:1, 0:1], (1, 128))
        row = lax.broadcasted_iota(jnp.int32, (8, 128), 0)
        scalar_ref[...] = jnp.where(row == 0, norm, jnp.where(row == 1, loss, count))
        split_rows = split_weight_ref.shape[0]
        outs = update(
            split_weight_ref[...],
            split_first_ref[...],
            split_second_ref[...],
            split_ref[0:split_rows] * factor,
        )
        split_new_ref[...], split_new_first_ref[...], split_new_second_ref[...] = outs

    base = pl.multiple_of(step * BLOCK_ROWS, BLOCK_ROWS)
    factor = factor_ref[0:1]
    own = flat[pl.ds(8 + base, BLOCK_ROWS)]
    before = flat[pl.ds(7 + base, BLOCK_ROWS)]
    row = lax.broadcasted_iota(jnp.int32, (BLOCK_ROWS, 1), 0) + base
    late = row >= LATE
    before = jnp.where(row == LATE, edge_ref[8:9], before)
    grads = jnp.where(late & (lane < 32), before, own)
    outs = update(weight_ref[...], first_ref[...], second_ref[...], grads * factor)
    new_ref[...], new_first_ref[...], new_second_ref[...] = outs


def adam_all(
    starts, lengths, flag, reduced, split_grad, square, shared, split, fast_rows
):
    places, fast_total = spans(fast_rows)
    most = places["times"][0] + TSTEPS
    grid = -(-FLAT_ROWS // BLOCK_ROWS)
    flat_spec = pl.BlockSpec((BLOCK_ROWS, 128), lambda i, *_: (i, 0))
    split_rows = split[0].shape[0]

    def whole(shape):
        return pl.BlockSpec(shape, lambda i, *_: (0,) * len(shape))

    split_spec = whole((split_rows, 128))
    shared_out = jax.ShapeDtypeStruct((FLAT_ROWS, 128), jnp.float32)
    split_out = jax.ShapeDtypeStruct((split_rows, 128), jnp.float32)
    return pl.pallas_call(
        partial(adam_kernel, fast_rows, most),
        grid_spec=pltpu.PrefetchScalarGridSpec(
            num_scalar_prefetch=3,
            grid=(grid,),
            in_specs=[
                pl.BlockSpec(memory_space=pl.ANY),
                whole(split_grad.shape),
                whole((8, 128)),
                flat_spec,
                flat_spec,
                flat_spec,
                split_spec,
                split_spec,
                split_spec,
            ],
            out_specs=[flat_spec] * 3 + [split_spec] * 3 + [whole((8, 128))],
            scratch_shapes=[
                pltpu.VMEM((most, 128), jnp.float32),
                pltpu.VMEM((grid * BLOCK_ROWS + 64, 128), jnp.float32),
                pltpu.VMEM((8, 128), jnp.float32),
                pltpu.VMEM((16, 128), jnp.float32),
                pltpu.SemaphoreType.DMA,
            ],
        ),
        out_shape=[shared_out] * 3
        + [split_out] * 3
        + [jax.ShapeDtypeStruct((8, 128), jnp.float32)],
        compiler_params=pltpu.CompilerParams(vmem_limit_bytes=48 * 1024 * 1024),
        name="adam_update",
    )(starts, lengths, flag, reduced, split_grad, square, *shared, *split)


def valid_slots(lengths, steps, room):
    ends = jnp.cumsum(lengths)
    slot = jnp.arange(room, dtype=jnp.int32)
    window = jnp.sum((slot[:, None] >= ends[None, :]).astype(jnp.int32), axis=1)
    window = jnp.minimum(window, lengths.shape[0] - 1)
    begin = (ends - lengths)[window]
    return window, jnp.minimum(slot - begin, steps - 1), ends[-1]


FAST_ROWS = 776


def per_device(
    frames,
    returns,
    actions,
    starts,
    lengths,
    shared_weights,
    shared_first,
    shared_second,
    split_weights,
    split_first,
    split_second,
):
    dp_size, mp_size = lax.axis_size("dp"), lax.axis_size("mp")
    narrow = D // mp_size
    hidden_width = FF // mp_size
    wins, steps = returns.shape
    room = 128
    split_all = lax.all_gather(split_weights, "mp", axis=0, tiled=True)
    index_own = jnp.concatenate([starts, lengths]).astype(jnp.float32)
    index_all = lax.all_gather(index_own, ("dp", "mp"), axis=0).astype(jnp.int32)
    starts_all = index_all[:, :wins].reshape(-1)
    lengths_all = index_all[:, wins:].reshape(-1)
    params = unpack_shared(shared_weights)
    images = frames.astype(jnp.float32)
    places = starts[:, None] + jnp.arange(steps, dtype=jnp.int32)[None, :]
    times = jnp.take(params["time_table"], places, axis=0)

    def local_loss(table, flat, times):
        layers = assemble(flat, mp_size, narrow, hidden_width)
        stream = embed_tokens(table, images, returns, actions, times)
        for layer in range(LAYERS):
            weights = layers[layer]
            normed = first_piece(stream, table["vectors"], layer)
            mixed = attention(normed, weights["qkv"], weights["output"], lengths)
            stream, normed = middle_piece(stream, mixed, table["vectors"], layer)
            mixed = feed_forward(normed, weights["up"], weights["up_bias"], weights["down"])
            stream = last_piece(stream, mixed, table["vectors"], layer)
        return action_loss(stream, table, actions, lengths)

    loss_local, (grads, split_grad, time_grad) = jax.value_and_grad(local_loss, argnums=(0, 1, 2))(
        params, split_all, times
    )

    def padded(flat, rows):
        return jnp.pad(flat.reshape(-1), (0, rows * 128 - flat.size)).reshape(rows, 128)

    conv_names = ["conv_one", "bias_one", "conv_two", "bias_two", "conv_three", "bias_three"]
    conv_flat = jnp.concatenate([grads[name].reshape(-1) for name in conv_names])
    small = jnp.concatenate(
        [
            padded(conv_flat, 616),
            padded(grads["vectors"], 24),
            padded(grads["action_table"], 24),
            padded(grads["head"], 24),
            jnp.broadcast_to(loss_local, (8, 128)),
        ]
    )
    width = split_weights.shape[0]
    split_rows = -(-width // 128)
    split_pad = -(-split_rows // 8) * 8
    split_blocks = [
        padded(split_grad[number * width : (number + 1) * width], split_pad)
        for number in range(mp_size)
    ]
    window, moment, used = valid_slots(lengths, steps, room)
    slot = jnp.arange(room, dtype=jnp.int32)
    packed = time_grad.reshape(wins * steps, D)[window * steps + moment]
    packed = jnp.where((slot < used)[:, None], packed, 0.0)
    spots, fast_total = spans(FAST_ROWS)
    out_rows = spots["times"][0] + TSTEPS
    out_rows = -(-out_rows // 4096) * 4096
    rows_all = jnp.sum(lengths_all)
    fast = rows_all <= FAST_ROWS
    me = lax.axis_index("dp") * mp_size + lax.axis_index("mp")
    skipped = jnp.sum(
        jnp.where(jnp.arange(lengths_all.shape[0]) < me * wins, lengths_all, 0)
    )

    def compact(operands):
        encoder, small, packed, blocks = operands
        field = jnp.zeros((FAST_ROWS + room, D), jnp.float32)
        field = lax.dynamic_update_slice(field, packed, (jnp.minimum(skipped, FAST_ROWS), 0))
        pieces = [(0, encoder), (3136, small), (spots["times"][0], field[:FAST_ROWS])]
        return reduce_all(pieces, blocks, dp_size, mp_size, out_rows, 1)

    def whole(operands):
        encoder, small, packed, blocks = operands
        spot = starts[window] + moment
        field = jnp.zeros((TSTEPS, D), jnp.float32).at[spot].add(packed)
        pieces = [(0, encoder), (3136, small), (spots["times"][0], field)]
        return reduce_all(pieces, blocks, dp_size, mp_size, out_rows, 2)

    reduced, split_sum, square = lax.cond(
        fast, compact, whole, (grads["encoder"], small, packed, split_blocks)
    )

    def rows_of(flat):
        return padded(flat, split_rows) if width % 128 else flat.reshape(split_rows, 128)

    shared_view = [a.reshape(FLAT_ROWS, 128) for a in (shared_weights, shared_first, shared_second)]
    split_view = [rows_of(a) for a in (split_weights, split_first, split_second)]
    results = adam_all(
        starts_all,
        lengths_all,
        fast.astype(jnp.int32).reshape(1),
        reduced,
        split_sum,
        square,
        shared_view,
        split_view,
        FAST_ROWS,
    )
    shared_out = [a.reshape(-1) for a in results[:3]]
    split_out = [a.reshape(-1)[:width] for a in results[3:6]]
    scalars = results[6]
    return (
        *shared_out,
        shared_out[0].astype(jnp.bfloat16),
        *split_out,
        split_out[0].astype(jnp.bfloat16),
        scalars[0, 0],
        scalars[1, 0],
        scalars[2, 0],
    )


def solution(mesh):
    return jax.shard_map(
        per_device,
        mesh=mesh,
        in_specs=(
            P(("dp", "mp"), None, None, None, None),
            P(("dp", "mp"), None),
            P(("dp", "mp"), None),
            P(("dp", "mp")),
            P(("dp", "mp")),
            P(),
            P(),
            P(),
            P("mp"),
            P("mp"),
            P("mp"),
        ),
        out_specs=(P(), P(), P(), P(), P("mp"), P("mp"), P("mp"), P("mp"), P(), P(), P()),
        check_vma=False,
    )
```

```python
from functools import partial
import math

import jax
import jax.numpy as jnp
from jax import lax
from jax.experimental import pallas as pl
from jax.experimental.pallas import tpu as pltpu
from jax.sharding import PartitionSpec as P

D = 128
FF = 512
ACT = 18
C1 = 32
C2 = 64
TSTEPS = 4096
LAYERS = 2
STEP = 10
HD = 16


clip_limit = 0.1
learn_rate = 0.05
beta_first = 0.9
beta_second = 0.95
adam_epsilon = 1e-08
weight_decay = 0.1


def span_layout(narrow, hidden):
    return [
        ("qkv", (D, 3, narrow)),
        ("output", (narrow, D)),
        ("up", (D, hidden)),
        ("up_bias", (hidden,)),
        ("down", (hidden, D)),
    ]


def assemble(flat, copies, narrow, hidden):
    layout = span_layout(narrow, hidden)
    width = sum((math.prod(shape) for name, shape in layout))
    blocks = flat.reshape(copies, LAYERS, width)
    layers = []
    for layer in range(LAYERS):
        offset = 0
        pieces = {}
        for name, shape in layout:
            count = math.prod(shape)
            pieces[name] = blocks[:, layer, offset : offset + count].reshape((copies,) + shape)
            offset += count
        layers.append(
            {
                "qkv": jnp.moveaxis(pieces["qkv"], 0, 2).reshape(D, 3, copies * narrow),
                "output": pieces["output"].reshape(copies * narrow, D),
                "up": jnp.moveaxis(pieces["up"], 0, 1).reshape(D, copies * hidden),
                "up_bias": pieces["up_bias"].reshape(copies * hidden),
                "down": pieces["down"].reshape(copies * hidden, D),
            }
        )
    return layers


GROUP = 16
ROOM = 128
HALF = 64
BF16 = jnp.bfloat16
F32 = jnp.float32


def gelu_value(x):
    inner = 0.7978845608028654 * (x + 0.044715 * (x * x * x))
    return 0.5 * x * (1.0 + jnp.tanh(inner))


def gelu_both(x):
    square = x * x
    turn = jnp.tanh(0.7978845608028654 * x * (1.0 + 0.044715 * square))
    half = 0.5 * (1.0 + turn)
    slope = half + 0.5 * x * (1.0 - turn * turn) * (
        0.7978845608028654 * (1.0 + 3 * 0.044715 * square)
    )
    return x * half, slope


def two_parts(x):
    high = x.astype(BF16)
    return high, (x - high.astype(F32)).astype(BF16)


def pair(x):
    return jnp.concatenate(two_parts(x), axis=-1)


def fold_pair(x):
    return x[:, :128] + x[:, 128:]


def dot(a, b):
    return lax.dot_general(a, b, (((1,), (0,)), ((), ())), preferred_element_type=F32)


def dot_rows(a, b):
    return lax.dot_general(a, b, (((0,), (0,)), ((), ())), preferred_element_type=F32)


def lanes():
    return lax.broadcasted_iota(jnp.int32, (1, 128), 1)


def conv_biases(flat_ref):
    lane = lanes()
    one = jnp.where(lane < 32, flat_ref[64:65], 0.0)
    one = one + pltpu.roll(one, 32, 1)
    one = one + pltpu.roll(one, 64, 1)
    two = jnp.where(lane < 64, pltpu.roll(flat_ref[320:321], 96, 1), 0.0)
    two = two + pltpu.roll(two, 64, 1)
    three = jnp.where(
        lane < 32,
        pltpu.roll(flat_ref[608:609], 32, 1),
        jnp.where(lane < 64, pltpu.roll(flat_ref[609:610], 32, 1), 0.0),
    )
    three = three + pltpu.roll(three, 64, 1)
    return one, two, three


def spread_one(one_ref, put):
    turned = jnp.transpose(one_ref[...])
    lane = lax.broadcasted_iota(jnp.int32, (8, 128), 1)
    row = lax.broadcasted_iota(jnp.int32, (8, 128), 0)
    low = row < 4
    column = lax.shift_right_logical(lane, 5)
    for ky in range(8):
        for c in range(4):
            held = turned[c * 64 + ky * 8 : c * 64 + ky * 8 + 8]
            wide = jnp.concatenate([held] * 4, axis=1)
            flipped = jnp.concatenate([wide[4:], wide[:4]], axis=0)
            zero = jnp.zeros((8, 128), F32)
            first = jnp.where(column == 0, wide, jnp.where((column == 1) & ~low, flipped, zero))
            second = jnp.where(
                column == 2,
                wide,
                jnp.where(((column == 1) & low) | ((column == 3) & ~low), flipped, zero),
            )
            third = jnp.where((column == 3) & low, flipped, zero)
            put(ky * 128 + c * 32, jnp.concatenate([first, second, third, zero], axis=0))


def spread_two(two_ref, turned, put):
    lane = lax.broadcasted_iota(jnp.int32, (32, 128), 1)
    for j in range(4):
        block = jnp.transpose(two_ref[:, j * 128 : (j + 1) * 128])
        turned[j * 128 : (j + 1) * 128] = jnp.concatenate([block, block], axis=1)
    for ky in range(4):
        rows = [turned[pl.ds(ky * 4 + kx, 32, stride=16)] for kx in range(4)]
        for i in range(8):
            left = rows[i] if i < 4 else jnp.zeros((32, 128), F32)
            right = rows[i - 2] if 2 <= i < 6 else jnp.zeros((32, 128), F32)
            put(ky * 256 + i * 32, jnp.where(lane < 64, left, right))


def spread_three(three_ref, turned, put):
    lane = lax.broadcasted_iota(jnp.int32, (64, 128), 1)
    for j in range(5):
        wide = min(128, 576 - j * 128)
        block = jnp.transpose(three_ref[:, j * 128 : j * 128 + wide])
        turned[j * 128 : j * 128 + wide] = jnp.concatenate([block, block], axis=1)
    for ky in range(3):
        rows = [turned[pl.ds(ky * 3 + kx, 64, stride=9)] for kx in range(3)]
        for i in range(4):
            left = rows[i] if i < 3 else jnp.zeros((64, 128), F32)
            right = rows[i - 1] if i >= 1 else jnp.zeros((64, 128), F32)
            put(ky * 256 + i * 64, jnp.where(lane < 64, left, right))


def last_masks():
    return lanes() < 64


def conv_forward_kernel(
    lengths_ref,
    frames_ref,
    flat_ref,
    one_ref,
    two_ref,
    three_ref,
    picked_ref,
    z_one_ref,
    z_two_ref,
    z_three_ref,
    held,
    wide,
    picked,
    z_one,
    z_two,
    z_three,
    h_one,
    h_two,
    w_one,
    w_two,
    w_three,
    choose,
    turned,
    frame_sem,
    out_sem,
):
    wins = lengths_ref.shape[0]
    steps = frames_ref.shape[1]
    used = jnp.int32(0)
    for w in range(wins):
        used = used + lengths_ref[w]
    groups = lax.div(used + (GROUP - 1), GROUP)

    def frame_copy(group, spot, slot):
        state = jnp.minimum(group * GROUP + spot, used - 1)
        window, begin, end = jnp.int32(0), jnp.int32(0), jnp.int32(0)
        for w in range(wins - 1):
            end = end + lengths_ref[w]
            window = jnp.where(state >= end, w + 1, window)
            begin = jnp.where(state >= end, end, begin)
        return pltpu.make_async_copy(
            frames_ref.at[window, state - begin], held.at[slot, spot], frame_sem.at[slot, spot]
        )

    def fetch(group, slot):
        def one(spot, carry):
            frame_copy(group, spot, slot).start()
            return carry

        lax.fori_loop(0, GROUP, one, 0)

    fetch(0, 0)
    h_one[...] = jnp.zeros(h_one.shape, BF16)

    def put_one(row, block):
        w_one[row : row + 32] = pair(block)

    def put_two(row, block):
        w_two[row : row + 32] = pair(block)

    def put_three(row, block):
        w_three[row : row + 64] = pair(block)

    spread_one(one_ref, put_one)
    spread_two(two_ref, turned, put_two)
    spread_three(three_ref, turned, put_three)
    bias_one, bias_two, bias_three = conv_biases(flat_ref)
    row = lax.broadcasted_iota(jnp.int32, (128, 640), 0)
    column = lax.broadcasted_iota(jnp.int32, (128, 640), 1)
    place = jnp.bitwise_and(column, 31)
    channel = jnp.bitwise_and(lax.shift_right_logical(column, 5), 3)
    block = lax.shift_right_logical(column, 7)
    right = (row == 16 * block + place) & (place < 20)
    for c in range(4):
        choose[c * 128 : (c + 1) * 128] = jnp.where(right & (channel == c), 1.0, 0.0).astype(BF16)

    def one_group(group, carry):
        slot = lax.rem(group, 2)

        @pl.when(group + 1 < groups)
        def ahead():
            fetch(group + 1, 1 - slot)

        def lay(spot, carry):
            frame_copy(group, spot, slot).wait()
            for c in range(4):
                image = held[slot, spot, c].astype(F32)
                image = jnp.concatenate([image, jnp.zeros((84, 44), F32)], axis=1)
                wide[c, pl.ds(spot, 84, stride=GROUP), :] = image
            return carry

        lax.fori_loop(0, GROUP, lay, 0)
        for part in range(3):
            rows = [wide[c, part * 448 : (part + 1) * 448].astype(BF16) for c in range(4)]
            result = dot(jnp.concatenate(rows, axis=1), choose[...])
            picked[part * 7 : (part + 1) * 7] = result.astype(BF16).reshape(7, 4, GROUP, 640)
        keep_picked = pltpu.make_async_copy(picked, picked_ref.at[group], out_sem.at[0])
        keep_picked.start()
        for q in range(5):
            pieces = [
                picked[j : j + 20, b, :, q * 128 : (q + 1) * 128].reshape(20 * GROUP, 128)
                for j in range(2)
                for b in range(4)
            ]
            z = fold_pair(dot(jnp.concatenate(pieces, axis=1), w_one[...])) + bias_one
            z_one[:, :, q] = z.reshape(10, 2, GROUP, 128)
            high, low = two_parts(gelu_value(z))
            h_one[0, :, :, q] = high.reshape(10, 2, GROUP, 128)
            h_one[1, :, :, q] = low.reshape(10, 2, GROUP, 128)
        keep_one = pltpu.make_async_copy(z_one, z_one_ref.at[group], out_sem.at[1])
        keep_one.start()
        total = jnp.zeros((45 * GROUP, 128), F32)
        for part in range(2):
            pieces = []
            for j in range(2):
                for b in range(2):
                    pieces.append(h_one[part, j : j + 9, b, 0:5].reshape(45 * GROUP, 128))
                    pieces.append(h_one[part, j : j + 9, b, 1:6].reshape(45 * GROUP, 128))
            total = total + fold_pair(dot(jnp.concatenate(pieces, axis=1), w_two[...]))
        z = (total + bias_two).reshape(9, 5, GROUP, 128)
        z_two[...] = z
        h = gelu_value(z)
        high, low = two_parts(h)
        h_two[0] = high
        h_two[1] = low
        edge = jnp.where(last_masks(), h[:, 4].reshape(9 * GROUP, 128), 0.0)
        high, low = two_parts(edge)
        h_two[0, :, 4] = high.reshape(9, GROUP, 128)
        h_two[1, :, 4] = low.reshape(9, GROUP, 128)
        keep_two = pltpu.make_async_copy(z_two, z_two_ref.at[group], out_sem.at[2])
        keep_two.start()
        total = jnp.zeros((28 * GROUP, 128), F32)
        for part in range(2):
            pieces = []
            for ky in range(3):
                pieces.append(h_two[part, ky : ky + 7, 0:4].reshape(28 * GROUP, 128))
                pieces.append(h_two[part, ky : ky + 7, 1:5].reshape(28 * GROUP, 128))
            total = total + fold_pair(dot(jnp.concatenate(pieces, axis=1), w_three[...]))
        z_three[...] = (total + bias_three).reshape(28, GROUP, 128)
        spot = pl.multiple_of(group * GROUP, GROUP)
        keep_three = pltpu.make_async_copy(
            z_three, z_three_ref.at[:, pl.ds(spot, GROUP)], out_sem.at[3]
        )
        keep_three.start()
        keep_picked.wait()
        keep_one.wait()
        keep_two.wait()
        keep_three.wait()
        return carry

    lax.fori_loop(0, groups, one_group, 0)


def conv_forward(lengths, frames, flat, one, two, three):
    most = ROOM // GROUP
    any_spec = pl.BlockSpec(memory_space=pl.ANY)
    vmem = pl.BlockSpec(memory_space=pltpu.VMEM)
    return pl.pallas_call(
        conv_forward_kernel,
        in_specs=[
            pl.BlockSpec(memory_space=pltpu.SMEM),
            any_spec,
            vmem,
            vmem,
            vmem,
            vmem,
        ],
        out_specs=[any_spec] * 4,
        out_shape=[
            jax.ShapeDtypeStruct((most, 21, 4, GROUP, 640), BF16),
            jax.ShapeDtypeStruct((most, 10, 2, 5, GROUP, 128), F32),
            jax.ShapeDtypeStruct((most, 9, 5, GROUP, 128), F32),
            jax.ShapeDtypeStruct((28, ROOM, 128), F32),
        ],
        scratch_shapes=[
            pltpu.VMEM((2, GROUP, 4, 84, 84), BF16),
            pltpu.VMEM((4, 84 * GROUP, 128), F32),
            pltpu.VMEM((21, 4, GROUP, 640), BF16),
            pltpu.VMEM((10, 2, 5, GROUP, 128), F32),
            pltpu.VMEM((9, 5, GROUP, 128), F32),
            pltpu.VMEM((28, GROUP, 128), F32),
            pltpu.VMEM((2, 10, 2, 6, GROUP, 128), BF16),
            pltpu.VMEM((2, 9, 5, GROUP, 128), BF16),
            pltpu.VMEM((1024, 256), BF16),
            pltpu.VMEM((1024, 256), BF16),
            pltpu.VMEM((768, 256), BF16),
            pltpu.VMEM((512, 640), BF16),
            pltpu.VMEM((576, 128), F32),
            pltpu.SemaphoreType.DMA((2, GROUP)),
            pltpu.SemaphoreType.DMA((4,)),
        ],
        compiler_params=pltpu.CompilerParams(vmem_limit_bytes=48 * 1024 * 1024),
        name="conv_forward",
    )(lengths, frames, flat, one, two, three)


def gather_one(total, out):
    lane = lax.broadcasted_iota(jnp.int32, (32, 128), 1)
    halves = [jnp.zeros((32, 128), F32) for side in range(2)]
    for ky in range(8):
        held = total[0:128, ky * 128 : (ky + 1) * 128] + total[128:256, ky * 128 : (ky + 1) * 128]
        summed = held[0:32]
        for o in range(1, 4):
            summed = summed + pltpu.roll(held[32 * o : 32 * o + 32], 128 - 4 * o, 1)
        for c in range(4):
            spot = (c % 2) * 64 + ky * 8
            shift = (spot - c * 32) % 128
            moved = pltpu.roll(summed, shift, 1) if shift else summed
            inside = (lane >= spot) & (lane < spot + 8)
            halves[c // 2] = halves[c // 2] + jnp.where(inside, moved, 0.0)
    out[:, 0:128] = halves[0]
    out[:, 128:256] = halves[1]


def gather_two(total, turned, out):
    lane = lax.broadcasted_iota(jnp.int32, (64, 128), 1)
    for ky in range(4):
        near = total[0:128, ky * 256 : ky * 256 + 128] + total[128:256, ky * 256 : ky * 256 + 128]
        far = (
            total[0:128, ky * 256 + 128 : ky * 256 + 256]
            + total[128:256, ky * 256 + 128 : ky * 256 + 256]
        )
        summed = near[0:64] + jnp.where(
            lane < 64, pltpu.roll(near[64:128], 64, 1), pltpu.roll(far[64:128], 64, 1)
        )
        flipped = jnp.transpose(jnp.concatenate([summed, jnp.zeros((64, 128), F32)], axis=0))
        for kx in range(4):
            turned[pl.ds(ky * 4 + kx, 32, stride=16), :] = flipped[kx * 32 : (kx + 1) * 32]
    for j in range(4):
        out[:, j * 128 : (j + 1) * 128] = jnp.transpose(turned[j * 128 : (j + 1) * 128])[0:64]


def gather_three(total, turned, out):
    lane = lax.broadcasted_iota(jnp.int32, (64, 128), 1)
    blank = jnp.zeros((64, 128), F32)
    for ky in range(3):
        near = total[0:128, ky * 256 : ky * 256 + 128] + total[128:256, ky * 256 : ky * 256 + 128]
        far = (
            total[0:128, ky * 256 + 128 : ky * 256 + 256]
            + total[128:256, ky * 256 + 128 : ky * 256 + 256]
        )
        first = near[0:64] + jnp.where(
            lane < 64, pltpu.roll(near[64:128], 64, 1), pltpu.roll(far[64:128], 64, 1)
        )
        second = far[0:64] + pltpu.roll(far[64:128], 64, 1)
        flipped = jnp.transpose(jnp.concatenate([first, blank], axis=0))
        turned[pl.ds(ky * 3, 64, stride=9), :] = flipped[0:64]
        turned[pl.ds(ky * 3 + 1, 64, stride=9), :] = flipped[64:128]
        flipped = jnp.transpose(jnp.concatenate([second, blank], axis=0))
        turned[pl.ds(ky * 3 + 2, 64, stride=9), :] = flipped[0:64]
    for j in range(5):
        wide = min(128, 576 - j * 128)
        out[:, j * 128 : j * 128 + wide] = jnp.transpose(turned[j * 128 : j * 128 + wide])[0:64]


def conv_backward_kernel(
    lengths_ref,
    picked_ref,
    z_one_ref,
    z_two_ref,
    d_three_ref,
    two_ref,
    three_ref,
    one_out,
    two_out,
    three_out,
    bias_out,
    picked,
    z_one,
    z_two,
    d_three,
    h_one,
    h_two,
    slope_one,
    pad_three,
    pad_two,
    d_one,
    v_two,
    v_three,
    spread,
    turned,
    total_one,
    total_two,
    total_three,
    load_sem,
):
    used = jnp.int32(0)
    for w in range(lengths_ref.shape[0]):
        used = used + lengths_ref[w]
    groups = lax.div(used + (GROUP - 1), GROUP)

    def loads(group, slot):
        spot = pl.multiple_of(group * GROUP, GROUP)
        return [
            pltpu.make_async_copy(picked_ref.at[group], picked.at[slot], load_sem.at[slot, 0]),
            pltpu.make_async_copy(z_one_ref.at[group], z_one.at[slot], load_sem.at[slot, 1]),
            pltpu.make_async_copy(z_two_ref.at[group], z_two.at[slot], load_sem.at[slot, 2]),
            pltpu.make_async_copy(
                d_three_ref.at[:, pl.ds(spot, GROUP)], d_three.at[slot], load_sem.at[slot, 3]
            ),
        ]

    for load in loads(0, 0):
        load.start()

    def put_two(row, block):
        spread[row : row + 32] = block

    def put_three(row, block):
        spread[row : row + 64] = block

    spread_two(two_ref, turned, put_two)
    for b in range(2):
        for j in range(2):
            for side in range(2):
                source = (2 * j + b) * 256 + side * 128
                target = (b * 2 + j) * 256 + side * 128
                v_two[target : target + 128] = pair(jnp.transpose(spread[source : source + 128]))
    spread_three(three_ref, turned, put_three)
    for part in range(6):
        rows = pl.ds(part * 128, 128)
        v_three[rows] = pair(jnp.transpose(spread[rows]))
    total_one[...] = jnp.zeros(total_one.shape, F32)
    total_two[...] = jnp.zeros(total_two.shape, F32)
    total_three[...] = jnp.zeros(total_three.shape, F32)
    bias_out[...] = jnp.zeros(bias_out.shape, F32)
    h_one[...] = jnp.zeros(h_one.shape, BF16)
    pad_two[...] = jnp.zeros(pad_two.shape, BF16)
    pad_three[...] = jnp.zeros(pad_three.shape, BF16)

    def fold(rows):
        return jnp.sum(rows.reshape(-1, 8, 128), axis=0)

    def one_group(group, carry):
        slot = lax.rem(group, 2)

        @pl.when(group + 1 < groups)
        def ahead():
            for load in loads(group + 1, 1 - slot):
                load.start()

        for load in loads(group, slot):
            load.wait()
        rows = d_three[slot].reshape(28 * GROUP, 128)
        bias_out[2] += fold(rows)
        both = pair(rows)
        pad_three[0, 2:9, 1:5] = both[:, :128].reshape(7, 4, GROUP, 128)
        pad_three[1, 2:9, 1:5] = both[:, 128:].reshape(7, 4, GROUP, 128)
        h, slope_two = gelu_both(z_two[slot])
        high, low = two_parts(h)
        h_two[0] = high
        h_two[1] = low
        edge = jnp.where(last_masks(), h[:, 4].reshape(9 * GROUP, 128), 0.0)
        high, low = two_parts(edge)
        h_two[0, :, 4] = high.reshape(9, GROUP, 128)
        h_two[1, :, 4] = low.reshape(9, GROUP, 128)
        for part in range(2):
            pieces = []
            for ky in range(3):
                pieces.append(h_two[part, ky : ky + 7, 0:4].reshape(28 * GROUP, 128))
                pieces.append(h_two[part, ky : ky + 7, 1:5].reshape(28 * GROUP, 128))
            total_three[...] += dot_rows(both, jnp.concatenate(pieces, axis=1))
        spill = jnp.zeros((45 * GROUP, 128), F32)
        for part in range(2):
            pieces = []
            for ky in range(3):
                pieces.append(pad_three[part, 2 - ky : 11 - ky, 1:6].reshape(45 * GROUP, 128))
                pieces.append(pad_three[part, 2 - ky : 11 - ky, 0:5].reshape(45 * GROUP, 128))
            spill = spill + fold_pair(dot(jnp.concatenate(pieces, axis=1), v_three[...]))
        rows = spill * slope_two.reshape(45 * GROUP, 128)
        bias_out[1] += fold(rows)
        both = pair(rows)
        pad_two[0, 1:10, 1:6] = both[:, :128].reshape(9, 5, GROUP, 128)
        pad_two[1, 1:10, 1:6] = both[:, 128:].reshape(9, 5, GROUP, 128)
        for q in range(5):
            h, slope = gelu_both(z_one[slot, :, :, q])
            high, low = two_parts(h)
            h_one[0, :, :, q] = high
            h_one[1, :, :, q] = low
            slope_one[:, :, q] = slope
        for part in range(2):
            pieces = []
            for j in range(2):
                for b in range(2):
                    pieces.append(h_one[part, j : j + 9, b, 0:5].reshape(45 * GROUP, 128))
                    pieces.append(h_one[part, j : j + 9, b, 1:6].reshape(45 * GROUP, 128))
            total_two[...] += dot_rows(both, jnp.concatenate(pieces, axis=1))
        for b in range(2):
            spill = jnp.zeros((50 * GROUP, 128), F32)
            for part in range(2):
                pieces = []
                for j in range(2):
                    pieces.append(pad_two[part, 1 - j : 11 - j, 1:6].reshape(50 * GROUP, 128))
                    pieces.append(pad_two[part, 1 - j : 11 - j, 0:5].reshape(50 * GROUP, 128))
                spill = spill + fold_pair(
                    dot(jnp.concatenate(pieces, axis=1), v_two[b * 512 : (b + 1) * 512])
                )
            rows = spill * slope_one[:, b].reshape(50 * GROUP, 128)
            bias_out[0] += fold(rows)
            d_one[:, b] = pair(rows).reshape(10, 5, GROUP, 256)
        for q in range(5):
            pieces = [
                picked[slot, j : j + 20, b, :, q * 128 : (q + 1) * 128].reshape(20 * GROUP, 128)
                for j in range(2)
                for b in range(4)
            ]
            total_one[...] += dot_rows(
                d_one[:, :, q].reshape(20 * GROUP, 256), jnp.concatenate(pieces, axis=1)
            )
        return carry

    lax.fori_loop(0, groups, one_group, 0)
    gather_one(total_one, one_out)
    gather_two(total_two, turned, two_out)
    gather_three(total_three, turned, three_out)
    sums = [jnp.sum(bias_out[k], axis=0, keepdims=True) for k in range(3)]
    sums[0] = sums[0] + pltpu.roll(sums[0], 64, 1)
    sums[0] = sums[0] + pltpu.roll(sums[0], 32, 1)
    sums[1] = sums[1] + pltpu.roll(sums[1], 64, 1)
    sums[2] = sums[2] + pltpu.roll(sums[2], 64, 1)
    for k in range(3):
        bias_out[k] = jnp.broadcast_to(sums[k], (8, 128))


def conv_backward(lengths, picked, z_one, z_two, d_three, two, three):
    any_spec = pl.BlockSpec(memory_space=pl.ANY)
    vmem = pl.BlockSpec(memory_space=pltpu.VMEM)
    return pl.pallas_call(
        conv_backward_kernel,
        in_specs=[pl.BlockSpec(memory_space=pltpu.SMEM)] + [any_spec] * 4 + [vmem] * 2,
        out_specs=[vmem] * 4,
        out_shape=[
            jax.ShapeDtypeStruct((32, 256), F32),
            jax.ShapeDtypeStruct((64, 512), F32),
            jax.ShapeDtypeStruct((64, 576), F32),
            jax.ShapeDtypeStruct((3, 8, 128), F32),
        ],
        scratch_shapes=[
            pltpu.VMEM((2, 21, 4, GROUP, 640), BF16),
            pltpu.VMEM((2, 10, 2, 5, GROUP, 128), F32),
            pltpu.VMEM((2, 9, 5, GROUP, 128), F32),
            pltpu.VMEM((2, 28, GROUP, 128), F32),
            pltpu.VMEM((2, 10, 2, 6, GROUP, 128), BF16),
            pltpu.VMEM((2, 9, 5, GROUP, 128), BF16),
            pltpu.VMEM((10, 2, 5, GROUP, 128), F32),
            pltpu.VMEM((2, 11, 6, GROUP, 128), BF16),
            pltpu.VMEM((2, 11, 6, GROUP, 128), BF16),
            pltpu.VMEM((10, 2, 5, GROUP, 256), BF16),
            pltpu.VMEM((1024, 256), BF16),
            pltpu.VMEM((768, 256), BF16),
            pltpu.VMEM((1024, 128), F32),
            pltpu.VMEM((576, 128), F32),
            pltpu.VMEM((256, 1024), F32),
            pltpu.VMEM((256, 1024), F32),
            pltpu.VMEM((256, 768), F32),
            pltpu.SemaphoreType.DMA((2, 4)),
        ],
        compiler_params=pltpu.CompilerParams(vmem_limit_bytes=48 * 1024 * 1024),
        name="conv_backward",
    )(lengths, picked, z_one, z_two, d_three, two, three)


HIGH = lax.Precision.HIGH
VECTORS_ROW = 3745
TIME_ROW = 3780


def mm(a, b):
    return lax.dot_general(
        a, b, (((1,), (0,)), ((), ())), precision=HIGH, preferred_element_type=F32
    )


def mm_nt(a, b):
    return lax.dot_general(
        a, b, (((1,), (1,)), ((), ())), precision=HIGH, preferred_element_type=F32
    )


def mm_tn(a, b):
    return lax.dot_general(
        a, b, (((0,), (0,)), ((), ())), precision=HIGH, preferred_element_type=F32
    )


def norm_parts(stream):
    centered = stream - jnp.mean(stream, -1, keepdims=True)
    spread = jnp.mean(centered * centered, -1, keepdims=True)
    scale = lax.rsqrt(spread + 1e-05)
    return centered * scale, scale


def norm_back(grad, unit, scale, gain):
    grad = grad * gain
    inner = jnp.mean(grad * unit, -1, keepdims=True)
    return scale * (grad - jnp.mean(grad, -1, keepdims=True) - unit * inner)


def column_sum(x):
    return jnp.sum(x, axis=0, keepdims=True)


def unpack_split(split_ref, qkv, output, up, up_bias, down):
    lane = lax.broadcasted_iota(jnp.int32, (32, 128), 1)
    for layer in range(LAYERS):
        base = layer * 385
        kinds = [[jnp.zeros((32, 128), F32) for j in range(4)] for kind in range(3)]
        for m in range(4):
            rows = [split_ref[m, pl.ds(base + k, 32, stride=3), :] for k in range(3)]
            inside = (lane >= 32 * m) & (lane < 32 * m + 32)
            for j in range(4):
                for kind in range(3):
                    spot = j * 96 + kind * 32
                    source = rows[spot // 128]
                    shift = (32 * m - spot % 128) % 128
                    moved = pltpu.roll(source, shift, 1) if shift else source
                    kinds[kind][j] = jnp.where(inside, moved, kinds[kind][j])
            output[layer, 32 * m : 32 * m + 32] = split_ref[m, base + 96 : base + 128]
            up[layer, :, 128 * m : 128 * m + 128] = split_ref[m, base + 128 : base + 256]
            up_bias[layer, :, 128 * m : 128 * m + 128] = split_ref[m, base + 256 : base + 257]
            down[layer, 128 * m : 128 * m + 128] = split_ref[m, base + 257 : base + 385]
        for kind in range(3):
            for j in range(4):
                qkv[layer, kind, pl.ds(j, 32, stride=4), :] = kinds[kind][j]


def pack_split(out_ref, qkv, output, up, up_bias, down):
    lane = lax.broadcasted_iota(jnp.int32, (32, 128), 1)
    for layer in range(LAYERS):
        base = layer * 385
        parts = [[qkv[layer, kind, pl.ds(j, 32, stride=4), :] for j in range(4)] for kind in range(3)]
        for m in range(4):
            rows = [jnp.zeros((32, 128), F32) for k in range(3)]
            for j in range(4):
                for kind in range(3):
                    spot = j * 96 + kind * 32
                    low = spot % 128
                    shift = (low - 32 * m) % 128
                    moved = pltpu.roll(parts[kind][j], shift, 1) if shift else parts[kind][j]
                    inside = (lane >= low) & (lane < low + 32)
                    rows[spot // 128] = jnp.where(inside, moved, rows[spot // 128])
            for k in range(3):
                out_ref[m, pl.ds(base + k, 32, stride=3), :] = rows[k]
            out_ref[m, base + 96 : base + 128] = output[layer, 32 * m : 32 * m + 32]
            out_ref[m, base + 128 : base + 256] = up[layer, :, 128 * m : 128 * m + 128]
            out_ref[m, base + 256 : base + 257] = up_bias[layer, :, 128 * m : 128 * m + 128]
            out_ref[m, base + 257 : base + 385] = down[layer, 128 * m : 128 * m + 128]
    for m in range(4):
        out_ref[m, 770:776] = jnp.zeros((6, 128), F32)


def former_body(
    slots,
    used,
    lengths_ref,
    returns_ref,
    actions_ref,
    head_ref,
    z_ref,
    small,
    times_all,
    encoder,
    weights,
    d_three_ref,
    d_encoder_ref,
    d_vectors_ref,
    d_actions_ref,
    d_head_ref,
    d_times_ref,
    loss_ref,
    grads,
    chances,
    kept,
    flats,
):
    qkv, output, up, up_bias, down = weights
    d_qkv, d_output, d_up, d_up_bias, d_down = grads
    rows = 3 * slots
    wins, steps = returns_ref.shape
    vec = [small[k : k + 1] for k in range(17)]
    table = small[17 : 17 + ACT]
    slot = lax.broadcasted_iota(jnp.int32, (slots, 1), 0)
    window = jnp.zeros((slots, 1), jnp.int32)
    begin = jnp.zeros((slots, 1), jnp.int32)
    end = jnp.int32(0)
    for w in range(wins - 1):
        end = end + lengths_ref[w]
        window = jnp.where(slot >= end, w + 1, window)
        begin = jnp.where(slot >= end, end, begin)
    moment = slot - begin
    valid = slot < used
    time_lane = lax.broadcasted_iota(jnp.int32, (slots, steps), 1)
    amount = jnp.zeros((slots, 1), F32)
    action = jnp.zeros((slots, 1), jnp.int32)
    for w in range(wins):
        here = (time_lane == moment) & (window == w)
        amount = amount + jnp.sum(
            jnp.where(here, returns_ref[w : w + 1], 0.0), axis=1, keepdims=True
        )
        action = action + jnp.sum(jnp.where(here, actions_ref[w : w + 1], 0), axis=1, keepdims=True)
    lane = lax.broadcasted_iota(jnp.int32, (slots, 128), 1)
    picks = jnp.where((lane == action) & valid, 1.0, 0.0)
    reward = jnp.tanh(amount * vec[14] + vec[15])
    table = jnp.concatenate([table, jnp.zeros((128 - ACT, 128), F32)], axis=0)
    move = jnp.tanh(mm(picks, table))
    sum_state = jnp.zeros((slots, 128), F32)
    for k in range(28):
        z = jnp.where(valid, z_ref[k, 0:slots], 0.0)
        high, low = two_parts(gelu_value(z))
        flats[0, 0:slots, k * 128 : (k + 1) * 128] = high
        flats[1, 0:slots, k * 128 : (k + 1) * 128] = low
    for part in range(2):
        sum_state = sum_state + fold_pair(dot(flats[part, 0:slots], encoder[...]))
    state = jnp.tanh(sum_state + vec[16])
    times = times_all[0:slots]
    stream = jnp.concatenate([reward + times, state + times, move + times], axis=0)

    def ids(axis):
        shape = (rows, 1) if axis == 0 else (1, rows)
        number = lax.broadcasted_iota(jnp.int32, shape, axis)
        kind = jnp.where(number >= 2 * slots, 2, jnp.where(number >= slots, 1, 0))
        return number - kind * slots, kind

    (slot_q, kind_q), (slot_k, kind_k) = ids(0), ids(1)

    def begin_of(slot_ids):
        found = jnp.zeros(slot_ids.shape, jnp.int32)
        end = jnp.int32(0)
        for w in range(wins - 1):
            end = end + lengths_ref[w]
            found = jnp.where(slot_ids >= end, end, found)
        return found

    order_q = slot_q * 3 + kind_q
    order_k = slot_k * 3 + kind_k
    allowed = (order_q >= order_k) & (slot_k >= begin_of(slot_q)) & (slot_k < used)
    head_of = lax.shift_right_logical(lax.broadcasted_iota(jnp.int32, (1, 128), 1), 4)
    heads = D // HD
    tape = []
    for layer in range(LAYERS):
        gains = vec[6 * layer : 6 * layer + 6]
        unit_one, scale_one = norm_parts(stream)
        normed = unit_one * gains[0] + gains[1]
        kept[layer, 0, 0:rows] = mm(normed, qkv[layer, 0]) * 0.25
        kept[layer, 1, 0:rows] = mm(normed, qkv[layer, 1])
        kept[layer, 2, 0:rows] = mm(normed, qkv[layer, 2])
        kept[layer, 3, 0:rows] = jnp.zeros((rows, 128), F32)

        def attend(head, carry, layer=layer):
            mine = head_of == head
            query = jnp.where(mine, kept[layer, 0, 0:rows], 0.0)
            scores = jnp.where(allowed, mm_nt(query, kept[layer, 1, 0:rows]), -1e30)
            peak = jnp.max(scores, -1, keepdims=True)
            chance = jnp.exp(scores - peak)
            chance = chance / jnp.sum(chance, -1, keepdims=True)
            chances[layer * heads + head, 0:rows, 0:rows] = chance
            seen = mm(chance, kept[layer, 2, 0:rows])
            kept[layer, 3, 0:rows] += jnp.where(mine, seen, 0.0)
            return carry

        lax.fori_loop(0, heads, attend, 0)
        context = kept[layer, 3, 0:rows]
        stream = stream + mm(context, output[layer]) + gains[4]
        unit_two, scale_two = norm_parts(stream)
        normed_two = unit_two * gains[2] + gains[3]
        inner, slope = gelu_both(mm(normed_two, up[layer]) + up_bias[layer])
        stream = stream + mm(inner, down[layer]) + gains[5]
        tape.append((unit_one, scale_one, unit_two, scale_two, inner, slope))
    end_stream = stream[slots : 2 * slots]
    unit, scale = norm_parts(end_stream)
    final = unit * vec[12] + vec[13]
    logits = jnp.where(lane < ACT, mm(final, head_ref[...]), -1e30)
    peak = jnp.max(logits, -1, keepdims=True)
    powers = jnp.exp(logits - peak)
    total = jnp.sum(powers, -1, keepdims=True)
    chosen = jnp.sum(jnp.where(lane == action, logits, 0.0), -1, keepdims=True)
    terms = jnp.where(valid, jnp.log(total) + peak - chosen, 0.0)
    loss_ref[...] = jnp.broadcast_to(jnp.sum(terms, axis=0, keepdims=True), (8, 128))
    d_logits = jnp.where(valid, powers / total, 0.0) - picks
    d_head_ref[...] = mm_tn(final, d_logits)
    d_final = mm_nt(d_logits, head_ref[...])
    d_vec = [None] * 17
    d_vec[12] = column_sum(d_final * unit)
    d_vec[13] = column_sum(d_final)
    d_end = norm_back(d_final, unit, scale, vec[12])
    blank = jnp.zeros((slots, 128), F32)
    d_stream = jnp.concatenate([blank, d_end, blank], axis=0)
    for layer in reversed(range(LAYERS)):
        unit_one, scale_one, unit_two, scale_two, inner, slope = tape[layer]
        gains = vec[6 * layer : 6 * layer + 6]
        d_vec[6 * layer + 5] = column_sum(d_stream)
        d_down[layer] = mm_tn(inner, d_stream)
        d_inner = mm_nt(d_stream, down[layer]) * slope
        d_up_bias[layer] = column_sum(d_inner)
        normed_two = unit_two * gains[2] + gains[3]
        d_up[layer] = mm_tn(normed_two, d_inner)
        d_normed = mm_nt(d_inner, up[layer])
        d_vec[6 * layer + 2] = column_sum(d_normed * unit_two)
        d_vec[6 * layer + 3] = column_sum(d_normed)
        d_stream = d_stream + norm_back(d_normed, unit_two, scale_two, gains[2])
        d_vec[6 * layer + 4] = column_sum(d_stream)
        d_output[layer] = mm_tn(kept[layer, 3, 0:rows], d_stream)
        kept[layer, 3, 0:rows] = mm_nt(d_stream, output[layer])
        for k in range(3):
            kept[layer, 4 + k, 0:rows] = jnp.zeros((rows, 128), F32)

        def attend_back(head, carry, layer=layer):
            mine = head_of == head
            chance = chances[layer * heads + head, 0:rows, 0:rows]
            d_seen = jnp.where(mine, kept[layer, 3, 0:rows], 0.0)
            d_chance = mm_nt(d_seen, kept[layer, 2, 0:rows])
            base = jnp.sum(d_chance * chance, -1, keepdims=True)
            d_scores = chance * (d_chance - base)
            query = jnp.where(mine, kept[layer, 0, 0:rows], 0.0)
            kept[layer, 4, 0:rows] += jnp.where(mine, mm(d_scores, kept[layer, 1, 0:rows]), 0.0)
            kept[layer, 5, 0:rows] += mm_tn(d_scores, query)
            kept[layer, 6, 0:rows] += mm_tn(chance, d_seen)
            return carry

        lax.fori_loop(0, heads, attend_back, 0)
        normed = unit_one * gains[0] + gains[1]
        d_normed = jnp.zeros((rows, 128), F32)
        for k in range(3):
            held = kept[layer, 4 + k, 0:rows]
            held = held * 0.25 if k == 0 else held
            d_qkv[layer, k] = mm_tn(normed, held)
            d_normed = d_normed + mm_nt(held, qkv[layer, k])
        d_vec[6 * layer] = column_sum(d_normed * unit_one)
        d_vec[6 * layer + 1] = column_sum(d_normed)
        d_stream = d_stream + norm_back(d_normed, unit_one, scale_one, gains[0])
    d_reward, d_state, d_move = (d_stream[k * slots : (k + 1) * slots] for k in range(3))
    d_times_ref[0:slots] = jnp.where(valid, d_reward + d_state + d_move, 0.0)
    d_reward = d_reward * (1.0 - reward * reward)
    d_vec[14] = column_sum(d_reward * amount)
    d_vec[15] = column_sum(d_reward)
    d_move = d_move * (1.0 - move * move)
    d_actions_ref[...] = mm_tn(picks, d_move)[0:24]
    d_state = jnp.where(valid, d_state * (1.0 - state * state), 0.0)
    d_vec[16] = column_sum(d_state)
    d_vectors_ref[...] = jnp.concatenate(d_vec + [jnp.zeros((7, 128), F32)], axis=0)
    high, low = two_parts(d_state)
    twice = jnp.concatenate([high, high], axis=1)
    both = jnp.concatenate([high, low], axis=1)
    nt = (((1,), (1,)), ((), ()))
    for k in range(28):
        held = encoder[k * 128 : (k + 1) * 128]
        d_flat = lax.dot_general(twice, held, nt, preferred_element_type=F32)
        d_flat = d_flat + lax.dot_general(low, held[:, :128], nt, preferred_element_type=F32)
        z = jnp.where(valid, z_ref[k, 0:slots], 0.0)
        d_three_ref[k, 0:slots] = d_flat * gelu_both(z)[1]
        piece = slice(k * 128, (k + 1) * 128)
        d_block = fold_pair(
            dot_rows(flats[0, 0:slots, piece], both) + dot_rows(flats[1, 0:slots, piece], both)
        )
        y, v = divmod(k, 4)
        for o in range(2):
            if 2 * v + o < 7:
                d_encoder_ref[pl.ds(y * 7 + 2 * v + o, 64, stride=49), :] = d_block[
                    o * 64 : (o + 1) * 64
                ]


def former_kernel(
    packed,
    lengths_ref,
    starts_ref,
    returns_ref,
    actions_ref,
    head_ref,
    z_ref,
    flat_ref,
    *refs,
):
    if packed:
        split_ref, refs = refs[0], refs[1:]
    else:
        given, refs = refs[:5], refs[5:]
    (d_three_ref, d_encoder_ref, d_vectors_ref, d_actions_ref, d_head_ref) = refs[:5]
    (d_times_ref, loss_ref), refs = refs[5:7], refs[7:]
    if packed:
        d_split_ref, refs = refs[0], refs[1:]
        weights, grads, refs = refs[:5], refs[5:10], refs[10:]
    else:
        grads, refs = refs[:5], refs[5:]
        weights = given
    (raw, near, small, rows_raw, times_all, encoder, chances, kept, flats, sem) = refs
    used = jnp.int32(0)
    wins = lengths_ref.shape[0]
    for w in range(wins):
        used = used + lengths_ref[w]
    copies = [
        pltpu.make_async_copy(flat_ref.at[pl.ds(608, 3144)], raw, sem.at[0]),
        pltpu.make_async_copy(flat_ref.at[pl.ds(3744, 48)], rows_raw.at[wins], sem.at[1]),
    ]
    offsets = []
    for w in range(wins):
        row = TIME_ROW + starts_ref[w]
        low = pl.multiple_of(lax.div(row, 8) * 8, 8)
        offsets.append(row - low)
        copies.append(
            pltpu.make_async_copy(
                flat_ref.at[pl.ds(low, 40)], rows_raw.at[w, pl.ds(0, 40)], sem.at[2 + w]
            )
        )
    for copy in copies:
        copy.start()
    if packed:
        unpack_split(split_ref, *weights)
    for copy in copies:
        copy.wait()
    lane = lanes()

    def straight(first, second):
        return jnp.where(lane < 96, pltpu.roll(first, 96, 1), pltpu.roll(second, 96, 1))

    def turn(step, carry):
        spot = pl.multiple_of(step * 64, 64)
        near[pl.ds(spot, 64)] = straight(raw[pl.ds(spot + 1, 64)], raw[pl.ds(spot + 2, 64)])
        return carry

    lax.fori_loop(0, 49, turn, 0)
    for k in range(28):
        y, v = divmod(k, 4)
        halves = []
        for o in range(2):
            if 2 * v + o < 7:
                halves.append(near[pl.ds(y * 7 + 2 * v + o, 64, stride=49), :])
            else:
                halves.append(jnp.zeros((64, 128), F32))
        encoder[k * 128 : (k + 1) * 128] = pair(jnp.concatenate(halves, axis=0))
    small[...] = straight(rows_raw[wins, 1:41], rows_raw[wins, 2:42])
    times_all[...] = jnp.zeros(times_all.shape, F32)
    begin = 0
    row = lax.broadcasted_iota(jnp.int32, (32, 1), 0)
    for w in range(wins):
        rows = straight(
            rows_raw[w, pl.ds(offsets[w], 32)], rows_raw[w, pl.ds(offsets[w] + 1, 32)]
        )
        times_all[pl.ds(begin, 32)] = jnp.where(row < lengths_ref[w], rows, 0.0)
        begin = begin + lengths_ref[w]
    d_times_ref[...] = jnp.zeros(d_times_ref.shape, F32)

    def run(slots):
        former_body(
            slots,
            used,
            lengths_ref,
            returns_ref,
            actions_ref,
            head_ref,
            z_ref,
            small,
            times_all,
            encoder,
            weights,
            d_three_ref,
            d_encoder_ref,
            d_vectors_ref,
            d_actions_ref,
            d_head_ref,
            d_times_ref,
            loss_ref,
            grads,
            chances,
            kept,
            flats,
        )

    @pl.when(used <= HALF)
    def few():
        run(HALF)

    @pl.when(used > HALF)
    def many():
        run(ROOM)

    if packed:
        pack_split(d_split_ref, *grads)


def former(lengths, starts, returns, actions, head, z_three, flat, weights, packed):
    smem = pl.BlockSpec(memory_space=pltpu.SMEM)
    vmem = pl.BlockSpec(memory_space=pltpu.VMEM)
    any_spec = pl.BlockSpec(memory_space=pl.ANY)
    wins = lengths.shape[0]
    canonical = [
        (LAYERS, 3, 128, 128),
        (LAYERS, 128, 128),
        (LAYERS, 128, FF),
        (LAYERS, 1, FF),
        (LAYERS, FF, 128),
    ]
    outs = [
        (28, ROOM, 128),
        (3136, 128),
        (24, 128),
        (24, 128),
        (128, 128),
        (ROOM, 128),
        (8, 128),
    ]
    outs += [(4, 776, 128)] if packed else canonical
    scratch = [pltpu.VMEM(shape, F32) for shape in canonical] * 2 if packed else []
    rows = 3 * ROOM
    scratch += [
        pltpu.VMEM((3144, 128), F32),
        pltpu.VMEM((3136, 128), F32),
        pltpu.VMEM((40, 128), F32),
        pltpu.VMEM((wins + 1, 48, 128), F32),
        pltpu.VMEM((ROOM + 32, 128), F32),
        pltpu.VMEM((3584, 256), BF16),
        pltpu.VMEM((LAYERS * 8, rows, rows), F32),
        pltpu.VMEM((LAYERS, 7, rows, 128), F32),
        pltpu.VMEM((2, ROOM, 3584), BF16),
        pltpu.SemaphoreType.DMA((wins + 2,)),
    ]
    return pl.pallas_call(
        partial(former_kernel, packed),
        in_specs=[smem, smem] + [vmem] * 4 + [any_spec] + [vmem] * len(weights),
        out_specs=[vmem] * len(outs),
        out_shape=[jax.ShapeDtypeStruct(shape, F32) for shape in outs],
        scratch_shapes=scratch,
        compiler_params=pltpu.CompilerParams(vmem_limit_bytes=60 * 1024 * 1024),
        name="transformer_step",
    )(lengths, starts, returns, actions, head, z_three, flat, *weights)


def bit_orders(dp_size, mp_size):
    dp_bits = [("dp", k) for k in range(dp_size.bit_length() - 1)]
    mp_bits = [("mp", k) for k in range(mp_size.bit_length() - 1)]
    core, ys = mp_bits[:1], mp_bits[1:]
    middle = len(dp_bits) // 3
    xs, zs = dp_bits[:middle], dp_bits[middle:]
    return [core + xs + zs + ys, core + zs + ys + xs, core + ys + xs + zs]


def reduce_kernel(plan, *refs):
    inputs, steps = plan["inputs"], plan["steps"]
    ins = refs[: len(inputs)]
    out_shared, out_split, out_square = refs[len(inputs) : len(inputs) + 3]
    (work, landing, total, split_total, tiles, tile_in) = refs[len(inputs) + 3 : len(inputs) + 9]
    (load_sem, send_sem, recv_sem, tile_send, tile_recv, store_sem) = refs[len(inputs) + 9 :]
    spots = {"dp": lax.axis_index("dp"), "mp": lax.axis_index("mp")}

    def value(bit):
        return lax.rem(lax.div(spots[bit[0]], 1 << bit[1]), 2)

    def partner(bit):
        axis, k = bit
        other = spots[axis] + (1 - 2 * value(bit)) * (1 << k)
        place = dict(spots)
        place[axis] = other
        return (place["dp"], place["mp"])

    loads = []
    for number, (start, rows) in enumerate(inputs):
        loads.append(
            pltpu.make_async_copy(
                ins[number], work.at[pl.ds(start, rows)], load_sem.at[number]
            )
        )
        loads[-1].start()
    for start, rows in plan["blank"]:
        work[pl.ds(start, rows)] = jnp.zeros((rows, 128), jnp.float32)
    barrier = pltpu.get_barrier_semaphore()
    bits = plan["bits"]
    for bit in bits:
        pl.semaphore_signal(
            barrier, inc=1, device_id=partner(bit), device_id_type=pl.DeviceIdType.MESH
        )
    pl.semaphore_wait(barrier, len(bits))
    for load in loads:
        load.wait()

    def add_rows(target, start, source_start, rows):
        chunk = math.gcd(rows, 64)

        def body(turn, carry):
            spot = pl.multiple_of(start + turn * chunk, 8)
            place = pl.multiple_of(source_start + turn * chunk, 8)
            target[pl.ds(spot, chunk)] = (
                target[pl.ds(spot, chunk)] + landing[pl.ds(place, chunk)]
            )
            return carry

        lax.fori_loop(0, rows // chunk, body, 0)

    streams = plan["streams"]
    where = [stream["base"] for stream in streams]
    sizes = [stream["rows"] for stream in streams]
    flights = [None] * len(streams)
    landings = [stream["landing"] for stream in streams]
    slot = 0
    for step in range(steps):
        for number, stream in enumerate(streams):
            if flights[number] is not None:
                copy, half, land, keep = flights[number]
                copy.wait()
                add_rows(work, keep, land, half)
                where[number] = keep
            bit = stream["order"][step]
            half = sizes[number] // 2
            mine = value(bit)
            keep = where[number] + mine * half
            give = where[number] + (1 - mine) * half
            copy = pltpu.make_async_remote_copy(
                src_ref=work.at[pl.ds(pl.multiple_of(give, 8), half)],
                dst_ref=landing.at[pl.ds(landings[number], half)],
                send_sem=send_sem.at[slot],
                recv_sem=recv_sem.at[slot],
                device_id=partner(bit),
                device_id_type=pl.DeviceIdType.MESH,
            )
            copy.start()
            slot += 1
            flights[number] = (copy, half, landings[number], keep)
            landings[number] += half
            sizes[number] = half
    backs = [list(reversed(stream["order"][stream["shared"] :])) for stream in streams]
    spaces = []
    for number, stream in enumerate(streams):
        copy, half, land, keep = flights[number]
        copy.wait()
        add_rows(work, keep, land, half)
        where[number] = keep
        if stream["shared"]:
            spaces.append(split_total)
            low = keep
            for bit in stream["order"][: stream["shared"]]:
                pass
            rows = half
            offset = jnp.int32(0)
            size = stream["rows"] >> stream["shared"]
            for bit in stream["order"][stream["shared"] :]:
                size //= 2
                offset = offset + value(bit) * size
            split_total[pl.ds(pl.multiple_of(offset, 8), rows)] = work[
                pl.ds(pl.multiple_of(keep, 8), rows)
            ]
            held = work[pl.ds(pl.multiple_of(keep, 8), rows)]
            squares = held * held
            tiles[0] = jnp.sum(squares.reshape(rows // 8, 8, 128), axis=0)
            where[number] = offset
        else:
            spaces.append(total)
            total[pl.ds(pl.multiple_of(keep, 8), half)] = work[
                pl.ds(pl.multiple_of(keep, 8), half)
            ]
    flights = [None] * len(streams)
    tile_flight = None
    for step in range(steps):
        if tile_flight is not None:
            tile_flight.wait()
            tiles[step] = tiles[step - 1] + tile_in[step - 1]
        tile_flight = pltpu.make_async_remote_copy(
            src_ref=tiles.at[step],
            dst_ref=tile_in.at[step],
            send_sem=tile_send.at[step],
            recv_sem=tile_recv.at[step],
            device_id=partner(bits[step]),
            device_id_type=pl.DeviceIdType.MESH,
        )
        tile_flight.start()
        for number, stream in enumerate(streams):
            if flights[number] is not None:
                copy, low, size = flights[number]
                copy.wait()
                where[number] = low
                sizes[number] = size
                flights[number] = None
            if step >= len(backs[number]):
                continue
            bit = backs[number][step]
            rows = sizes[number]
            region = spaces[number].at[pl.ds(pl.multiple_of(where[number], 8), rows)]
            copy = pltpu.make_async_remote_copy(
                src_ref=region,
                dst_ref=region,
                send_sem=send_sem.at[slot],
                recv_sem=recv_sem.at[slot],
                device_id=partner(bit),
                device_id_type=pl.DeviceIdType.MESH,
            )
            copy.start()
            slot += 1
            flights[number] = (copy, where[number] - value(bit) * rows, rows * 2)
    tile_flight.wait()
    out_square[...] = tiles[steps - 1] + tile_in[steps - 1]
    stores = []
    for number, stream in enumerate(streams):
        if flights[number] is not None:
            flights[number][0].wait()
    shared_rows = total.shape[0]
    stores.append(
        pltpu.make_async_copy(total, out_shared.at[pl.ds(0, shared_rows)], store_sem.at[0])
    )
    stores.append(pltpu.make_async_copy(split_total, out_split, store_sem.at[1]))
    for store in stores:
        store.start()
    for store in stores:
        store.wait()


def reduce_all(pieces, split_blocks, dp_size, mp_size, out_rows, collective_id):
    orders = bit_orders(dp_size, mp_size)
    bits = orders[0]
    steps = len(bits)
    grain = 8 << steps
    used = max(start + array.shape[0] for start, array in pieces)
    half = -(-used // (2 * grain)) * grain
    shared_rows = 2 * half
    span = split_blocks[0].shape[0]
    split_grain = 8 * dp_size
    block = -(-span // split_grain) * split_grain
    inputs, arrays, blank = [], [], []
    reach = 0
    for start, array in pieces:
        if start > reach:
            blank.append((reach, start - reach))
        inputs.append((start, array.shape[0]))
        arrays.append(array)
        reach = start + array.shape[0]
    if shared_rows > reach:
        blank.append((reach, shared_rows - reach))
    shared_steps = mp_size.bit_length() - 1
    for number in range(mp_size):
        turned = 0
        for k in range(shared_steps):
            turned |= ((number >> k) & 1) << (shared_steps - 1 - k)
        start = shared_rows + turned * block
        inputs.append((start, span))
        arrays.append(split_blocks[number])
        if block > span:
            blank.append((start + span, block - span))
    split_rows = mp_size * block
    work_rows = shared_rows + split_rows
    streams = [
        dict(base=0, rows=half, order=orders[0], shared=0, landing=0),
        dict(base=half, rows=half, order=orders[1], shared=0, landing=half),
        dict(
            base=shared_rows,
            rows=split_rows,
            order=orders[2],
            shared=shared_steps,
            landing=shared_rows,
        ),
    ]
    plan = dict(inputs=inputs, blank=blank, streams=streams, bits=bits, steps=steps)
    copies = 3 * 2 * steps
    return pl.pallas_call(
        partial(reduce_kernel, plan),
        out_shape=(
            jax.ShapeDtypeStruct((out_rows, 128), jnp.float32),
            jax.ShapeDtypeStruct((block, 128), jnp.float32),
            jax.ShapeDtypeStruct((8, 128), jnp.float32),
        ),
        in_specs=[pl.BlockSpec(memory_space=pl.ANY)] * len(arrays),
        out_specs=(
            pl.BlockSpec(memory_space=pl.ANY),
            pl.BlockSpec(memory_space=pl.ANY),
            pl.BlockSpec(memory_space=pltpu.VMEM),
        ),
        scratch_shapes=[
            pltpu.VMEM((work_rows, 128), jnp.float32),
            pltpu.VMEM((work_rows, 128), jnp.float32),
            pltpu.VMEM((shared_rows, 128), jnp.float32),
            pltpu.VMEM((block, 128), jnp.float32),
            pltpu.VMEM((steps, 8, 128), jnp.float32),
            pltpu.VMEM((steps, 8, 128), jnp.float32),
            pltpu.SemaphoreType.DMA((len(arrays),)),
            pltpu.SemaphoreType.DMA((copies,)),
            pltpu.SemaphoreType.DMA((copies,)),
            pltpu.SemaphoreType.DMA((steps,)),
            pltpu.SemaphoreType.DMA((steps,)),
            pltpu.SemaphoreType.DMA((2,)),
        ],
        compiler_params=pltpu.CompilerParams(
            collective_id=collective_id,
            has_side_effects=True,
            vmem_limit_bytes=56 * 1024 * 1024,
        ),
        name="reduce_gradients",
    )(*arrays)


def spans(fast_rows):
    places = {}
    at = 0
    for name, rows in [
        ("encoder", 3136),
        ("conv", 616),
        ("vectors", 24),
        ("action_table", 24),
        ("head", 24),
        ("scalars", 8),
        ("index", 8),
        ("times", fast_rows),
    ]:
        places[name] = (at, rows)
        at += rows
    return places, at


FLAT_ROWS = 7896
BLOCK_ROWS = 512
LATE = 609


def adam_kernel(
    fast_rows,
    most_rows,
    lengths_ref,
    flag_ref,
    reduced_ref,
    split_ref,
    square_ref,
    weight_ref,
    first_ref,
    second_ref,
    split_weight_ref,
    split_first_ref,
    split_second_ref,
    new_ref,
    new_first_ref,
    new_second_ref,
    split_new_ref,
    split_new_first_ref,
    split_new_second_ref,
    scalar_ref,
    pulled,
    flat,
    factor_ref,
    edge_ref,
    pull_sem,
):
    step = pl.program_id(0)
    places, fast_total = spans(fast_rows)
    lane = lax.broadcasted_iota(jnp.int32, (1, 128), 1)

    def update(weights, first, second, grads):
        first = beta_first * first + (1 - beta_first) * grads
        second = beta_second * second + (1 - beta_second) * grads * grads
        fix_one = 1 - beta_first**STEP
        fix_two = 1 - beta_second**STEP
        weights = weights - learn_rate * (
            first / fix_one / (jnp.sqrt(second / fix_two) + adam_epsilon) + weight_decay * weights
        )
        return weights, first, second

    @pl.when(step == 0)
    def prepare():
        pull = pltpu.make_async_copy(
            reduced_ref.at[pl.ds(0, fast_total)], pulled.at[pl.ds(0, fast_total)], pull_sem
        )
        pull.start()

        def wipe(turn, carry):
            flat[pl.ds(pl.multiple_of(turn * 64, 64), 64)] = jnp.zeros((64, 128), jnp.float32)
            return carry

        lax.fori_loop(0, flat.shape[0] // 64, wipe, 0)
        pull.wait()
        squares = jnp.zeros((8, 128), jnp.float32)

        def fold(rows):
            return jnp.sum((rows * rows).reshape(-1, 8, 128), axis=0)

        def conv_rows(turn, carry):
            spot = pl.multiple_of(turn * 56, 8)
            held = pulled[pl.ds(places["conv"][0] + spot, 56)]
            flat[pl.ds(8 + spot, 56)] = held
            return carry + fold(held)

        squares = lax.fori_loop(0, 616 // 56, conv_rows, squares)
        edge_ref[...] = flat[LATE : LATE + 16]

        def encoder_rows(turn, carry):
            spot = pl.multiple_of(turn * 64, 64)
            held = pulled[pl.ds(spot, 64)]
            flat[pl.ds(8 + LATE + spot, 64)] = pltpu.roll(held, 32, 1)
            return carry + fold(held)

        squares = lax.fori_loop(0, 3136 // 64, encoder_rows, squares)
        for name, at, rows in [
            ("vectors", LATE + 3136, 17),
            ("action_table", LATE + 3153, ACT),
            ("head", LATE + 3171 + TSTEPS, ACT),
        ]:
            held = pulled[places[name][0] : places[name][0] + 24]
            squares = squares + fold(held)
            flat[8 + at : 8 + at + rows] = pltpu.roll(held, 32, 1)[:rows]
        time_at = 8 + LATE + 3171

        @pl.when(flag_ref[0] > 0)
        def scatter():
            low = places["times"][0]
            spots = pulled[places["index"][0] : places["index"][0] + 8]
            rows = pltpu.roll(pulled[low : low + fast_rows], 32, 1)
            rows = pair(rows)
            chunk = 512

            def table(turn, carry):
                base = turn * chunk
                place = (lax.broadcasted_iota(jnp.int32, (chunk, 128), 0) + base).astype(F32)
                picks = [
                    jnp.where(place == spots[k : k + 1], 1.0, 0.0).astype(BF16)
                    for k in range(fast_rows // 128)
                ]
                held = fold_pair(dot(jnp.concatenate(picks, axis=1), rows))
                flat[pl.ds(time_at + base, chunk)] = held
                return carry

            lax.fori_loop(0, TSTEPS // chunk, table, 0)

        @pl.when(flag_ref[0] <= 0)
        def whole_table():
            pull_table = pltpu.make_async_copy(
                reduced_ref.at[pl.ds(places["times"][0], TSTEPS)],
                pulled.at[pl.ds(places["times"][0], TSTEPS)],
                pull_sem,
            )
            pull_table.start()
            pull_table.wait()

            def rows_in(turn, carry):
                spot = pl.multiple_of(turn * 64, 64)
                held = pulled[pl.ds(places["times"][0] + spot, 64)]
                flat[pl.ds(time_at + spot, 64)] = pltpu.roll(held, 32, 1)
                return carry

            lax.fori_loop(0, TSTEPS // 64, rows_in, 0)

        def time_squares(turn, carry):
            return carry + fold(flat[pl.ds(time_at + turn * 64, 64)])

        squares = lax.fori_loop(0, TSTEPS // 64, time_squares, squares)
        squares = squares + square_ref[...]
        count = jnp.float32(0)
        whole = lax.fori_loop(
            0, lengths_ref.shape[0], lambda k, c: c + lengths_ref[k], jnp.int32(0)
        )
        count = jnp.full((1, 128), whole.astype(jnp.float32))
        scalars = pulled[places["scalars"][0] : places["scalars"][0] + 8]
        total = jnp.sum(jnp.sum(squares, axis=0, keepdims=True), axis=1, keepdims=True)
        seed = 1.0 / count
        norm = jnp.sqrt(jnp.broadcast_to(total, (1, 128))) * seed
        factor = jnp.minimum(1.0, clip_limit / (norm + 1e-06)) * seed
        factor_ref[...] = jnp.broadcast_to(factor, (8, 128))
        loss = jnp.broadcast_to(scalars[0:1, 0:1], (1, 128))
        row = lax.broadcasted_iota(jnp.int32, (8, 128), 0)
        scalar_ref[...] = jnp.where(row == 0, norm, jnp.where(row == 1, loss, count))
        split_rows = split_weight_ref.shape[0]
        outs = update(
            split_weight_ref[...],
            split_first_ref[...],
            split_second_ref[...],
            split_ref[0:split_rows] * factor,
        )
        split_new_ref[...], split_new_first_ref[...], split_new_second_ref[...] = outs

    base = pl.multiple_of(step * BLOCK_ROWS, BLOCK_ROWS)
    factor = factor_ref[0:1]
    own = flat[pl.ds(8 + base, BLOCK_ROWS)]
    before = flat[pl.ds(7 + base, BLOCK_ROWS)]
    row = lax.broadcasted_iota(jnp.int32, (BLOCK_ROWS, 1), 0) + base
    late = row >= LATE
    before = jnp.where(row == LATE, edge_ref[8:9], before)
    grads = jnp.where(late & (lane < 32), before, own)
    outs = update(weight_ref[...], first_ref[...], second_ref[...], grads * factor)
    new_ref[...], new_first_ref[...], new_second_ref[...] = outs


def adam_all(
    lengths, flag, reduced, split_grad, square, shared, split, fast_rows
):
    places, fast_total = spans(fast_rows)
    most = places["times"][0] + TSTEPS
    grid = -(-FLAT_ROWS // BLOCK_ROWS)
    flat_spec = pl.BlockSpec((BLOCK_ROWS, 128), lambda i, *_: (i, 0))
    split_rows = split[0].shape[0]

    def whole(shape):
        return pl.BlockSpec(shape, lambda i, *_: (0,) * len(shape))

    split_spec = whole((split_rows, 128))
    shared_out = jax.ShapeDtypeStruct((FLAT_ROWS, 128), jnp.float32)
    split_out = jax.ShapeDtypeStruct((split_rows, 128), jnp.float32)
    return pl.pallas_call(
        partial(adam_kernel, fast_rows, most),
        grid_spec=pltpu.PrefetchScalarGridSpec(
            num_scalar_prefetch=2,
            grid=(grid,),
            in_specs=[
                pl.BlockSpec(memory_space=pl.ANY),
                whole(split_grad.shape),
                whole((8, 128)),
                flat_spec,
                flat_spec,
                flat_spec,
                split_spec,
                split_spec,
                split_spec,
            ],
            out_specs=[flat_spec] * 3 + [split_spec] * 3 + [whole((8, 128))],
            scratch_shapes=[
                pltpu.VMEM((most, 128), jnp.float32),
                pltpu.VMEM((grid * BLOCK_ROWS + 64, 128), jnp.float32),
                pltpu.VMEM((8, 128), jnp.float32),
                pltpu.VMEM((16, 128), jnp.float32),
                pltpu.SemaphoreType.DMA,
            ],
        ),
        out_shape=[shared_out] * 3
        + [split_out] * 3
        + [jax.ShapeDtypeStruct((8, 128), jnp.float32)],
        compiler_params=pltpu.CompilerParams(vmem_limit_bytes=48 * 1024 * 1024),
        name="adam_update",
    )(lengths, flag, reduced, split_grad, square, *shared, *split)


FAST_ROWS = 768


def valid_slots(lengths, steps):
    ends = jnp.cumsum(lengths)
    slot = jnp.arange(ROOM, dtype=jnp.int32)
    past = slot[:, None] >= ends[None, :-1]
    begin = jnp.sum(jnp.where(past, lengths[None, :-1], 0), axis=1)
    return past, jnp.minimum(slot - begin, steps - 1), ends[-1]


def per_device(
    frames,
    returns,
    actions,
    starts,
    lengths,
    shared_weights,
    shared_first,
    shared_second,
    split_weights,
    split_first,
    split_second,
):
    dp_size, mp_size = lax.axis_size("dp"), lax.axis_size("mp")
    narrow = D // mp_size
    hidden_width = FF // mp_size
    wins, steps = returns.shape
    width = split_weights.shape[0]
    split_rows = width // 128
    packed = narrow == 32
    own_rows = split_weights.reshape(split_rows, 128)
    split_all = lax.all_gather(own_rows, "mp", axis=0)
    lengths_all = lax.all_gather(lengths.astype(F32), ("dp", "mp"), axis=0)
    lengths_all = lengths_all.reshape(-1).astype(jnp.int32)
    flat = shared_weights.reshape(FLAT_ROWS, 128)
    one = shared_weights[:8192].reshape(32, 256)
    two = shared_weights[8224:40992].reshape(64, 512)
    three = shared_weights[41056:77920].reshape(64, 576)
    head = jnp.pad(shared_weights[1008160:1010464].reshape(128, ACT), ((0, 0), (0, 128 - ACT)))
    picked, z_one, z_two, z_three = conv_forward(lengths, frames, flat, one, two, three)
    if packed:
        weights = [split_all]
    else:
        layers, layers_back = jax.vjp(
            lambda held: assemble(held, mp_size, narrow, hidden_width), split_all.reshape(-1)
        )
        weights = [
            jnp.stack([layer["qkv"].transpose(1, 0, 2) for layer in layers]),
            jnp.stack([layer["output"] for layer in layers]),
            jnp.stack([layer["up"] for layer in layers]),
            jnp.stack([layer["up_bias"][None] for layer in layers]),
            jnp.stack([layer["down"] for layer in layers]),
        ]
    results = former(lengths, starts, returns, actions, head, z_three, flat, weights, packed)
    d_three, d_encoder, d_vectors, d_actions, d_head, d_times, loss = results[:7]
    if packed:
        split_blocks = [results[7][m] for m in range(mp_size)]
    else:
        d_qkv, d_output, d_up, d_up_bias, d_down = results[7:]
        grad_layers = [
            dict(
                qkv=d_qkv[layer].transpose(1, 0, 2),
                output=d_output[layer],
                up=d_up[layer],
                up_bias=d_up_bias[layer, 0],
                down=d_down[layer],
            )
            for layer in range(LAYERS)
        ]
        gathered = layers_back(grad_layers)[0].reshape(mp_size, split_rows, 128)
        pad_rows = -split_rows % 8
        split_blocks = [jnp.pad(gathered[m], ((0, pad_rows), (0, 0))) for m in range(mp_size)]
    d_one, d_two, d_conv, d_bias = conv_backward(
        lengths, picked, z_one, z_two, d_three, two, three
    )
    conv_flat = jnp.concatenate(
        [
            d_one.reshape(-1),
            d_bias[0, 0, :32],
            d_two.reshape(-1),
            d_bias[1, 0, :64],
            d_conv.reshape(-1),
            d_bias[2, 0, :64],
            jnp.zeros((616 * 128 - 77984,), F32),
        ]
    )
    d_head = jnp.pad(d_head[:, :ACT].reshape(ACT, 128), ((0, 24 - ACT), (0, 0)))
    pieces = [
        ("encoder", d_encoder),
        ("conv", conv_flat.reshape(616, 128)),
        ("vectors", d_vectors),
        ("action_table", d_actions),
        ("head", d_head),
        ("scalars", loss),
    ]
    past, moment, used = valid_slots(lengths, steps)
    slot = jnp.arange(ROOM, dtype=jnp.int32)
    gaps = starts[1:] - starts[:-1]
    spot = moment + starts[0] + jnp.sum(jnp.where(past, gaps[None, :], 0), axis=1)
    me = lax.axis_index("dp") * mp_size + lax.axis_index("mp")
    skipped = jnp.sum(
        jnp.where(jnp.arange(lengths_all.shape[0]) < me * wins, lengths_all, 0)
    )
    fast = jnp.sum(lengths_all) <= FAST_ROWS
    places, fast_total = spans(FAST_ROWS)
    out_rows = -(-(places["times"][0] + TSTEPS) // 4096) * 4096

    def total_of(field, index, collective_id):
        laid = [(places[name][0], array) for name, array in pieces]
        laid += [(places["index"][0], index), (places["times"][0], field)]
        return reduce_all(laid, split_blocks, dp_size, mp_size, out_rows, collective_id)

    def compact(operands):
        rows, spots = operands
        at = jnp.minimum(skipped, FAST_ROWS)
        field = jnp.zeros((FAST_ROWS + ROOM, D), F32)
        field = lax.dynamic_update_slice(field, rows, (at, 0))[:FAST_ROWS]
        index = jnp.zeros((1024 + ROOM,), F32)
        index = lax.dynamic_update_slice(index, spots, (at,))[:1024].reshape(8, 128)
        return total_of(field, index, 1)

    def whole(operands):
        rows, spots = operands
        field = jnp.zeros((TSTEPS, D), F32).at[spots.astype(jnp.int32)].add(rows)
        return total_of(field, jnp.zeros((8, 128), F32), 2)

    spots = jnp.where(slot < used, spot, 0).astype(F32)
    reduced, split_sum, square = lax.cond(fast, compact, whole, (d_times, spots))
    shared_view = [a.reshape(FLAT_ROWS, 128) for a in (shared_weights, shared_first, shared_second)]
    split_view = [a.reshape(split_rows, 128) for a in (split_weights, split_first, split_second)]
    updated = adam_all(
        lengths_all,
        fast.astype(jnp.int32).reshape(1),
        reduced,
        split_sum,
        square,
        shared_view,
        split_view,
        FAST_ROWS,
    )
    shared_out = [a.reshape(-1) for a in updated[:3]]
    split_out = [a.reshape(-1) for a in updated[3:6]]
    scalars = updated[6]
    return (
        *shared_out,
        shared_out[0].astype(BF16),
        *split_out,
        split_out[0].astype(BF16),
        scalars[0, 0],
        scalars[1, 0],
        scalars[2, 0],
    )


def solution(mesh):
    return jax.shard_map(
        per_device,
        mesh=mesh,
        in_specs=(
            P(("dp", "mp"), None, None, None, None),
            P(("dp", "mp"), None),
            P(("dp", "mp"), None),
            P(("dp", "mp")),
            P(("dp", "mp")),
            P(),
            P(),
            P(),
            P("mp"),
            P("mp"),
            P("mp"),
        ),
        out_specs=(P(), P(), P(), P(), P("mp"), P("mp"), P("mp"), P("mp"), P(), P(), P()),
        check_vma=False,
    )
```

```python
from functools import partial
import math

import jax
import jax.numpy as jnp
from jax import lax
from jax.experimental import pallas as pl
from jax.experimental.pallas import tpu as pltpu
from jax.sharding import PartitionSpec as P

D = 128
FF = 512
ACT = 18
C1 = 32
C2 = 64
TSTEPS = 4096
LAYERS = 2
STEP = 10
HD = 16


clip_limit = 0.1
learn_rate = 0.05
beta_first = 0.9
beta_second = 0.95
adam_epsilon = 1e-08
weight_decay = 0.1


def span_layout(narrow, hidden):
    return [
        ("qkv", (D, 3, narrow)),
        ("output", (narrow, D)),
        ("up", (D, hidden)),
        ("up_bias", (hidden,)),
        ("down", (hidden, D)),
    ]


def assemble(flat, copies, narrow, hidden):
    layout = span_layout(narrow, hidden)
    width = sum((math.prod(shape) for name, shape in layout))
    blocks = flat.reshape(copies, LAYERS, width)
    layers = []
    for layer in range(LAYERS):
        offset = 0
        pieces = {}
        for name, shape in layout:
            count = math.prod(shape)
            pieces[name] = blocks[:, layer, offset : offset + count].reshape((copies,) + shape)
            offset += count
        layers.append(
            {
                "qkv": jnp.moveaxis(pieces["qkv"], 0, 2).reshape(D, 3, copies * narrow),
                "output": pieces["output"].reshape(copies * narrow, D),
                "up": jnp.moveaxis(pieces["up"], 0, 1).reshape(D, copies * hidden),
                "up_bias": pieces["up_bias"].reshape(copies * hidden),
                "down": pieces["down"].reshape(copies * hidden, D),
            }
        )
    return layers


GROUP = 16
ROOM = 128
HALF = 64
BF16 = jnp.bfloat16
F32 = jnp.float32


def gelu_value(x):
    inner = 0.7978845608028654 * (x + 0.044715 * (x * x * x))
    return 0.5 * x * (1.0 + jnp.tanh(inner))


def gelu_both(x):
    square = x * x
    turn = jnp.tanh(0.7978845608028654 * x * (1.0 + 0.044715 * square))
    half = 0.5 * (1.0 + turn)
    slope = half + 0.5 * x * (1.0 - turn * turn) * (
        0.7978845608028654 * (1.0 + 3 * 0.044715 * square)
    )
    return x * half, slope


def two_parts(x):
    high = x.astype(BF16)
    return high, (x - high.astype(F32)).astype(BF16)


def pair(x):
    return jnp.concatenate(two_parts(x), axis=-1)


def fold_pair(x):
    return x[:, :128] + x[:, 128:]


def dot(a, b):
    return lax.dot_general(a, b, (((1,), (0,)), ((), ())), preferred_element_type=F32)


def dot_rows(a, b):
    return lax.dot_general(a, b, (((0,), (0,)), ((), ())), preferred_element_type=F32)


def lanes():
    return lax.broadcasted_iota(jnp.int32, (1, 128), 1)


def conv_biases(flat_ref):
    lane = lanes()
    one = jnp.where(lane < 32, flat_ref[64:65], 0.0)
    one = one + pltpu.roll(one, 32, 1)
    one = one + pltpu.roll(one, 64, 1)
    two = jnp.where(lane < 64, pltpu.roll(flat_ref[320:321], 96, 1), 0.0)
    two = two + pltpu.roll(two, 64, 1)
    three = jnp.where(
        lane < 32,
        pltpu.roll(flat_ref[608:609], 32, 1),
        jnp.where(lane < 64, pltpu.roll(flat_ref[609:610], 32, 1), 0.0),
    )
    three = three + pltpu.roll(three, 64, 1)
    return one, two, three


def spread_one(one_ref, put):
    turned = jnp.transpose(one_ref[...])
    lane = lax.broadcasted_iota(jnp.int32, (8, 128), 1)
    row = lax.broadcasted_iota(jnp.int32, (8, 128), 0)
    low = row < 4
    column = lax.shift_right_logical(lane, 5)
    for ky in range(8):
        for c in range(4):
            held = turned[c * 64 + ky * 8 : c * 64 + ky * 8 + 8]
            wide = jnp.concatenate([held] * 4, axis=1)
            flipped = jnp.concatenate([wide[4:], wide[:4]], axis=0)
            zero = jnp.zeros((8, 128), F32)
            first = jnp.where(column == 0, wide, jnp.where((column == 1) & ~low, flipped, zero))
            second = jnp.where(
                column == 2,
                wide,
                jnp.where(((column == 1) & low) | ((column == 3) & ~low), flipped, zero),
            )
            third = jnp.where((column == 3) & low, flipped, zero)
            put(ky * 128 + c * 32, jnp.concatenate([first, second, third, zero], axis=0))


def spread_two(two_ref, turned, put):
    lane = lax.broadcasted_iota(jnp.int32, (32, 128), 1)
    for j in range(4):
        block = jnp.transpose(two_ref[:, j * 128 : (j + 1) * 128])
        turned[j * 128 : (j + 1) * 128] = jnp.concatenate([block, block], axis=1)
    for ky in range(4):
        rows = [turned[pl.ds(ky * 4 + kx, 32, stride=16)] for kx in range(4)]
        for i in range(8):
            left = rows[i] if i < 4 else jnp.zeros((32, 128), F32)
            right = rows[i - 2] if 2 <= i < 6 else jnp.zeros((32, 128), F32)
            put(ky * 256 + i * 32, jnp.where(lane < 64, left, right))


def spread_three(three_ref, turned, put):
    lane = lax.broadcasted_iota(jnp.int32, (64, 128), 1)
    for j in range(5):
        wide = min(128, 576 - j * 128)
        block = jnp.transpose(three_ref[:, j * 128 : j * 128 + wide])
        turned[j * 128 : j * 128 + wide] = jnp.concatenate([block, block], axis=1)
    for ky in range(3):
        rows = [turned[pl.ds(ky * 3 + kx, 64, stride=9)] for kx in range(3)]
        for i in range(4):
            left = rows[i] if i < 3 else jnp.zeros((64, 128), F32)
            right = rows[i - 1] if i >= 1 else jnp.zeros((64, 128), F32)
            put(ky * 256 + i * 64, jnp.where(lane < 64, left, right))


def last_masks():
    return lanes() < 64


def conv_forward_kernel(
    lengths_ref,
    frames_ref,
    flat_ref,
    one_ref,
    two_ref,
    three_ref,
    picked_ref,
    z_one_ref,
    z_two_ref,
    z_three_ref,
    held,
    wide,
    picked,
    z_one,
    z_two,
    z_three,
    h_one,
    h_two,
    w_one,
    w_two,
    w_three,
    choose,
    turned,
    frame_sem,
    out_sem,
):
    wins = lengths_ref.shape[0]
    steps = frames_ref.shape[1]
    used = jnp.int32(0)
    for w in range(wins):
        used = used + lengths_ref[w]
    groups = lax.div(used + (GROUP - 1), GROUP)

    def frame_copy(group, spot, slot):
        state = jnp.minimum(group * GROUP + spot, used - 1)
        window, begin, end = jnp.int32(0), jnp.int32(0), jnp.int32(0)
        for w in range(wins - 1):
            end = end + lengths_ref[w]
            window = jnp.where(state >= end, w + 1, window)
            begin = jnp.where(state >= end, end, begin)
        return pltpu.make_async_copy(
            frames_ref.at[window, state - begin], held.at[slot, spot], frame_sem.at[slot, spot]
        )

    def fetch(group, slot):
        def one(spot, carry):
            frame_copy(group, spot, slot).start()
            return carry

        lax.fori_loop(0, GROUP, one, 0)

    fetch(0, 0)
    h_one[...] = jnp.zeros(h_one.shape, BF16)

    def put_one(row, block):
        w_one[row : row + 32] = pair(block)

    def put_two(row, block):
        w_two[row : row + 32] = pair(block)

    def put_three(row, block):
        w_three[row : row + 64] = pair(block)

    spread_one(one_ref, put_one)
    spread_two(two_ref, turned, put_two)
    spread_three(three_ref, turned, put_three)
    bias_one, bias_two, bias_three = conv_biases(flat_ref)
    row = lax.broadcasted_iota(jnp.int32, (128, 640), 0)
    column = lax.broadcasted_iota(jnp.int32, (128, 640), 1)
    place = jnp.bitwise_and(column, 31)
    channel = jnp.bitwise_and(lax.shift_right_logical(column, 5), 3)
    block = lax.shift_right_logical(column, 7)
    right = (row == 16 * block + place) & (place < 20)
    for c in range(4):
        choose[c * 128 : (c + 1) * 128] = jnp.where(right & (channel == c), 1.0, 0.0).astype(BF16)

    def one_group(group, carry):
        slot = lax.rem(group, 2)

        @pl.when(group + 1 < groups)
        def ahead():
            fetch(group + 1, 1 - slot)

        def lay(spot, carry):
            frame_copy(group, spot, slot).wait()
            image = held[slot, spot].astype(F32).reshape(336, 84)
            image = jnp.concatenate([image, jnp.zeros((336, 44), F32)], axis=1)
            wide[pl.ds(spot, 336, stride=GROUP), :] = image
            return carry

        lax.fori_loop(0, GROUP, lay, 0)
        for part in range(3):
            rows = wide[part * 1792 : (part + 1) * 1792].reshape(28, 4, GROUP, 128)
            rows = [rows[:, c].reshape(448, 128).astype(BF16) for c in range(4)]
            result = dot(jnp.concatenate(rows, axis=1), choose[...])
            picked[part * 7 : (part + 1) * 7] = result.astype(BF16).reshape(7, 4, GROUP, 640)
        keep_picked = pltpu.make_async_copy(picked, picked_ref.at[group], out_sem.at[0])
        keep_picked.start()
        for q in range(5):
            pieces = [
                picked[j : j + 20, b, :, q * 128 : (q + 1) * 128].reshape(20 * GROUP, 128)
                for j in range(2)
                for b in range(4)
            ]
            z = fold_pair(dot(jnp.concatenate(pieces, axis=1), w_one[...])) + bias_one
            z_one[:, :, q] = z.reshape(10, 2, GROUP, 128)
            high, low = two_parts(gelu_value(z))
            h_one[0, :, :, q] = high.reshape(10, 2, GROUP, 128)
            h_one[1, :, :, q] = low.reshape(10, 2, GROUP, 128)
        keep_one = pltpu.make_async_copy(z_one, z_one_ref.at[group], out_sem.at[1])
        keep_one.start()
        total = jnp.zeros((45 * GROUP, 128), F32)
        for part in range(2):
            pieces = []
            for j in range(2):
                for b in range(2):
                    pieces.append(h_one[part, j : j + 9, b, 0:5].reshape(45 * GROUP, 128))
                    pieces.append(h_one[part, j : j + 9, b, 1:6].reshape(45 * GROUP, 128))
            total = total + fold_pair(dot(jnp.concatenate(pieces, axis=1), w_two[...]))
        z = (total + bias_two).reshape(9, 5, GROUP, 128)
        z_two[...] = z
        h = gelu_value(z)
        high, low = two_parts(h)
        h_two[0] = high
        h_two[1] = low
        edge = jnp.where(last_masks(), h[:, 4].reshape(9 * GROUP, 128), 0.0)
        high, low = two_parts(edge)
        h_two[0, :, 4] = high.reshape(9, GROUP, 128)
        h_two[1, :, 4] = low.reshape(9, GROUP, 128)
        keep_two = pltpu.make_async_copy(z_two, z_two_ref.at[group], out_sem.at[2])
        keep_two.start()
        total = jnp.zeros((28 * GROUP, 128), F32)
        for part in range(2):
            pieces = []
            for ky in range(3):
                pieces.append(h_two[part, ky : ky + 7, 0:4].reshape(28 * GROUP, 128))
                pieces.append(h_two[part, ky : ky + 7, 1:5].reshape(28 * GROUP, 128))
            total = total + fold_pair(dot(jnp.concatenate(pieces, axis=1), w_three[...]))
        z_three[...] = (total + bias_three).reshape(28, GROUP, 128)
        spot = pl.multiple_of(group * GROUP, GROUP)
        keep_three = pltpu.make_async_copy(
            z_three, z_three_ref.at[:, pl.ds(spot, GROUP)], out_sem.at[3]
        )
        keep_three.start()
        keep_picked.wait()
        keep_one.wait()
        keep_two.wait()
        keep_three.wait()
        return carry

    lax.fori_loop(0, groups, one_group, 0)


def conv_forward(lengths, frames, flat, one, two, three):
    most = ROOM // GROUP
    any_spec = pl.BlockSpec(memory_space=pl.ANY)
    vmem = pl.BlockSpec(memory_space=pltpu.VMEM)
    return pl.pallas_call(
        conv_forward_kernel,
        in_specs=[
            pl.BlockSpec(memory_space=pltpu.SMEM),
            any_spec,
            vmem,
            vmem,
            vmem,
            vmem,
        ],
        out_specs=[any_spec] * 4,
        out_shape=[
            jax.ShapeDtypeStruct((most, 21, 4, GROUP, 640), BF16),
            jax.ShapeDtypeStruct((most, 10, 2, 5, GROUP, 128), F32),
            jax.ShapeDtypeStruct((most, 9, 5, GROUP, 128), F32),
            jax.ShapeDtypeStruct((28, ROOM, 128), F32),
        ],
        scratch_shapes=[
            pltpu.VMEM((2, GROUP, 84, 4, 84), BF16),
            pltpu.VMEM((336 * GROUP, 128), F32),
            pltpu.VMEM((21, 4, GROUP, 640), BF16),
            pltpu.VMEM((10, 2, 5, GROUP, 128), F32),
            pltpu.VMEM((9, 5, GROUP, 128), F32),
            pltpu.VMEM((28, GROUP, 128), F32),
            pltpu.VMEM((2, 10, 2, 6, GROUP, 128), BF16),
            pltpu.VMEM((2, 9, 5, GROUP, 128), BF16),
            pltpu.VMEM((1024, 256), BF16),
            pltpu.VMEM((1024, 256), BF16),
            pltpu.VMEM((768, 256), BF16),
            pltpu.VMEM((512, 640), BF16),
            pltpu.VMEM((576, 128), F32),
            pltpu.SemaphoreType.DMA((2, GROUP)),
            pltpu.SemaphoreType.DMA((4,)),
        ],
        compiler_params=pltpu.CompilerParams(vmem_limit_bytes=48 * 1024 * 1024),
        name="conv_forward",
    )(lengths, frames.transpose(0, 1, 3, 2, 4), flat, one, two, three)


def gather_one(total, out):
    lane = lax.broadcasted_iota(jnp.int32, (32, 128), 1)
    halves = [jnp.zeros((32, 128), F32) for side in range(2)]
    for ky in range(8):
        held = total[0:128, ky * 128 : (ky + 1) * 128] + total[128:256, ky * 128 : (ky + 1) * 128]
        summed = held[0:32]
        for o in range(1, 4):
            summed = summed + pltpu.roll(held[32 * o : 32 * o + 32], 128 - 4 * o, 1)
        for c in range(4):
            spot = (c % 2) * 64 + ky * 8
            shift = (spot - c * 32) % 128
            moved = pltpu.roll(summed, shift, 1) if shift else summed
            inside = (lane >= spot) & (lane < spot + 8)
            halves[c // 2] = halves[c // 2] + jnp.where(inside, moved, 0.0)
    out[:, 0:128] = halves[0]
    out[:, 128:256] = halves[1]


def gather_two(total, turned, out):
    lane = lax.broadcasted_iota(jnp.int32, (64, 128), 1)
    for ky in range(4):
        near = total[0:128, ky * 256 : ky * 256 + 128] + total[128:256, ky * 256 : ky * 256 + 128]
        far = (
            total[0:128, ky * 256 + 128 : ky * 256 + 256]
            + total[128:256, ky * 256 + 128 : ky * 256 + 256]
        )
        summed = near[0:64] + jnp.where(
            lane < 64, pltpu.roll(near[64:128], 64, 1), pltpu.roll(far[64:128], 64, 1)
        )
        flipped = jnp.transpose(jnp.concatenate([summed, jnp.zeros((64, 128), F32)], axis=0))
        for kx in range(4):
            turned[pl.ds(ky * 4 + kx, 32, stride=16), :] = flipped[kx * 32 : (kx + 1) * 32]
    for j in range(4):
        out[:, j * 128 : (j + 1) * 128] = jnp.transpose(turned[j * 128 : (j + 1) * 128])[0:64]


def gather_three(total, turned, out):
    lane = lax.broadcasted_iota(jnp.int32, (64, 128), 1)
    blank = jnp.zeros((64, 128), F32)
    for ky in range(3):
        near = total[0:128, ky * 256 : ky * 256 + 128] + total[128:256, ky * 256 : ky * 256 + 128]
        far = (
            total[0:128, ky * 256 + 128 : ky * 256 + 256]
            + total[128:256, ky * 256 + 128 : ky * 256 + 256]
        )
        first = near[0:64] + jnp.where(
            lane < 64, pltpu.roll(near[64:128], 64, 1), pltpu.roll(far[64:128], 64, 1)
        )
        second = far[0:64] + pltpu.roll(far[64:128], 64, 1)
        flipped = jnp.transpose(jnp.concatenate([first, blank], axis=0))
        turned[pl.ds(ky * 3, 64, stride=9), :] = flipped[0:64]
        turned[pl.ds(ky * 3 + 1, 64, stride=9), :] = flipped[64:128]
        flipped = jnp.transpose(jnp.concatenate([second, blank], axis=0))
        turned[pl.ds(ky * 3 + 2, 64, stride=9), :] = flipped[0:64]
    for j in range(5):
        wide = min(128, 576 - j * 128)
        out[:, j * 128 : j * 128 + wide] = jnp.transpose(turned[j * 128 : j * 128 + wide])[0:64]


def conv_backward_kernel(
    lengths_ref,
    picked_ref,
    z_one_ref,
    z_two_ref,
    d_three_ref,
    two_ref,
    three_ref,
    one_out,
    two_out,
    three_out,
    bias_out,
    picked,
    z_one,
    z_two,
    d_three,
    h_one,
    h_two,
    slope_one,
    pad_three,
    pad_two,
    d_one,
    v_two,
    v_three,
    spread,
    turned,
    total_one,
    total_two,
    total_three,
    load_sem,
):
    used = jnp.int32(0)
    for w in range(lengths_ref.shape[0]):
        used = used + lengths_ref[w]
    groups = lax.div(used + (GROUP - 1), GROUP)

    def loads(group, slot):
        spot = pl.multiple_of(group * GROUP, GROUP)
        return [
            pltpu.make_async_copy(picked_ref.at[group], picked.at[slot], load_sem.at[slot, 0]),
            pltpu.make_async_copy(z_one_ref.at[group], z_one.at[slot], load_sem.at[slot, 1]),
            pltpu.make_async_copy(z_two_ref.at[group], z_two.at[slot], load_sem.at[slot, 2]),
            pltpu.make_async_copy(
                d_three_ref.at[:, pl.ds(spot, GROUP)], d_three.at[slot], load_sem.at[slot, 3]
            ),
        ]

    for load in loads(0, 0):
        load.start()

    def put_two(row, block):
        spread[row : row + 32] = block

    def put_three(row, block):
        spread[row : row + 64] = block

    spread_two(two_ref, turned, put_two)
    for b in range(2):
        for j in range(2):
            for side in range(2):
                source = (2 * j + b) * 256 + side * 128
                target = (b * 2 + j) * 256 + side * 128
                v_two[target : target + 128] = pair(jnp.transpose(spread[source : source + 128]))
    spread_three(three_ref, turned, put_three)
    for part in range(6):
        rows = pl.ds(part * 128, 128)
        v_three[rows] = pair(jnp.transpose(spread[rows]))
    total_one[...] = jnp.zeros(total_one.shape, F32)
    total_two[...] = jnp.zeros(total_two.shape, F32)
    total_three[...] = jnp.zeros(total_three.shape, F32)
    bias_out[...] = jnp.zeros(bias_out.shape, F32)
    h_one[...] = jnp.zeros(h_one.shape, BF16)
    pad_two[...] = jnp.zeros(pad_two.shape, BF16)
    pad_three[...] = jnp.zeros(pad_three.shape, BF16)

    def fold(rows):
        return jnp.sum(rows.reshape(-1, 8, 128), axis=0)

    def one_group(group, carry):
        slot = lax.rem(group, 2)

        @pl.when(group + 1 < groups)
        def ahead():
            for load in loads(group + 1, 1 - slot):
                load.start()

        for load in loads(group, slot):
            load.wait()
        rows = d_three[slot].reshape(28 * GROUP, 128)
        bias_out[2] += fold(rows)
        both = pair(rows)
        pad_three[0, 2:9, 1:5] = both[:, :128].reshape(7, 4, GROUP, 128)
        pad_three[1, 2:9, 1:5] = both[:, 128:].reshape(7, 4, GROUP, 128)
        h, slope_two = gelu_both(z_two[slot])
        high, low = two_parts(h)
        h_two[0] = high
        h_two[1] = low
        edge = jnp.where(last_masks(), h[:, 4].reshape(9 * GROUP, 128), 0.0)
        high, low = two_parts(edge)
        h_two[0, :, 4] = high.reshape(9, GROUP, 128)
        h_two[1, :, 4] = low.reshape(9, GROUP, 128)
        for part in range(2):
            pieces = []
            for ky in range(3):
                pieces.append(h_two[part, ky : ky + 7, 0:4].reshape(28 * GROUP, 128))
                pieces.append(h_two[part, ky : ky + 7, 1:5].reshape(28 * GROUP, 128))
            total_three[...] += dot_rows(both, jnp.concatenate(pieces, axis=1))
        spill = jnp.zeros((45 * GROUP, 128), F32)
        for part in range(2):
            pieces = []
            for ky in range(3):
                pieces.append(pad_three[part, 2 - ky : 11 - ky, 1:6].reshape(45 * GROUP, 128))
                pieces.append(pad_three[part, 2 - ky : 11 - ky, 0:5].reshape(45 * GROUP, 128))
            spill = spill + fold_pair(dot(jnp.concatenate(pieces, axis=1), v_three[...]))
        rows = spill * slope_two.reshape(45 * GROUP, 128)
        bias_out[1] += fold(rows)
        both = pair(rows)
        pad_two[0, 1:10, 1:6] = both[:, :128].reshape(9, 5, GROUP, 128)
        pad_two[1, 1:10, 1:6] = both[:, 128:].reshape(9, 5, GROUP, 128)
        for q in range(5):
            h, slope = gelu_both(z_one[slot, :, :, q])
            high, low = two_parts(h)
            h_one[0, :, :, q] = high
            h_one[1, :, :, q] = low
            slope_one[:, :, q] = slope
        for part in range(2):
            pieces = []
            for j in range(2):
                for b in range(2):
                    pieces.append(h_one[part, j : j + 9, b, 0:5].reshape(45 * GROUP, 128))
                    pieces.append(h_one[part, j : j + 9, b, 1:6].reshape(45 * GROUP, 128))
            total_two[...] += dot_rows(both, jnp.concatenate(pieces, axis=1))
        for b in range(2):
            spill = jnp.zeros((50 * GROUP, 128), F32)
            for part in range(2):
                pieces = []
                for j in range(2):
                    pieces.append(pad_two[part, 1 - j : 11 - j, 1:6].reshape(50 * GROUP, 128))
                    pieces.append(pad_two[part, 1 - j : 11 - j, 0:5].reshape(50 * GROUP, 128))
                spill = spill + fold_pair(
                    dot(jnp.concatenate(pieces, axis=1), v_two[b * 512 : (b + 1) * 512])
                )
            rows = spill * slope_one[:, b].reshape(50 * GROUP, 128)
            bias_out[0] += fold(rows)
            d_one[:, b] = pair(rows).reshape(10, 5, GROUP, 256)
        for q in range(5):
            pieces = [
                picked[slot, j : j + 20, b, :, q * 128 : (q + 1) * 128].reshape(20 * GROUP, 128)
                for j in range(2)
                for b in range(4)
            ]
            total_one[...] += dot_rows(
                d_one[:, :, q].reshape(20 * GROUP, 256), jnp.concatenate(pieces, axis=1)
            )
        return carry

    lax.fori_loop(0, groups, one_group, 0)
    gather_one(total_one, one_out)
    gather_two(total_two, turned, two_out)
    gather_three(total_three, turned, three_out)
    sums = [jnp.sum(bias_out[k], axis=0, keepdims=True) for k in range(3)]
    sums[0] = sums[0] + pltpu.roll(sums[0], 64, 1)
    sums[0] = sums[0] + pltpu.roll(sums[0], 32, 1)
    sums[1] = sums[1] + pltpu.roll(sums[1], 64, 1)
    sums[2] = sums[2] + pltpu.roll(sums[2], 64, 1)
    for k in range(3):
        bias_out[k] = jnp.broadcast_to(sums[k], (8, 128))


def conv_backward(lengths, picked, z_one, z_two, d_three, two, three):
    any_spec = pl.BlockSpec(memory_space=pl.ANY)
    vmem = pl.BlockSpec(memory_space=pltpu.VMEM)
    return pl.pallas_call(
        conv_backward_kernel,
        in_specs=[pl.BlockSpec(memory_space=pltpu.SMEM)] + [any_spec] * 4 + [vmem] * 2,
        out_specs=[vmem] * 4,
        out_shape=[
            jax.ShapeDtypeStruct((32, 256), F32),
            jax.ShapeDtypeStruct((64, 512), F32),
            jax.ShapeDtypeStruct((64, 576), F32),
            jax.ShapeDtypeStruct((3, 8, 128), F32),
        ],
        scratch_shapes=[
            pltpu.VMEM((2, 21, 4, GROUP, 640), BF16),
            pltpu.VMEM((2, 10, 2, 5, GROUP, 128), F32),
            pltpu.VMEM((2, 9, 5, GROUP, 128), F32),
            pltpu.VMEM((2, 28, GROUP, 128), F32),
            pltpu.VMEM((2, 10, 2, 6, GROUP, 128), BF16),
            pltpu.VMEM((2, 9, 5, GROUP, 128), BF16),
            pltpu.VMEM((10, 2, 5, GROUP, 128), F32),
            pltpu.VMEM((2, 11, 6, GROUP, 128), BF16),
            pltpu.VMEM((2, 11, 6, GROUP, 128), BF16),
            pltpu.VMEM((10, 2, 5, GROUP, 256), BF16),
            pltpu.VMEM((1024, 256), BF16),
            pltpu.VMEM((768, 256), BF16),
            pltpu.VMEM((1024, 128), F32),
            pltpu.VMEM((576, 128), F32),
            pltpu.VMEM((256, 1024), F32),
            pltpu.VMEM((256, 1024), F32),
            pltpu.VMEM((256, 768), F32),
            pltpu.SemaphoreType.DMA((2, 4)),
        ],
        compiler_params=pltpu.CompilerParams(vmem_limit_bytes=48 * 1024 * 1024),
        name="conv_backward",
    )(lengths, picked, z_one, z_two, d_three, two, three)


HIGH = lax.Precision.HIGH
VECTORS_ROW = 3745
TIME_ROW = 3780


def mm(a, b):
    return lax.dot_general(
        a, b, (((1,), (0,)), ((), ())), precision=HIGH, preferred_element_type=F32
    )


def mm_nt(a, b):
    return lax.dot_general(
        a, b, (((1,), (1,)), ((), ())), precision=HIGH, preferred_element_type=F32
    )


def mm_tn(a, b):
    return lax.dot_general(
        a, b, (((0,), (0,)), ((), ())), precision=HIGH, preferred_element_type=F32
    )


def dot_nt(a, b):
    return lax.dot_general(a, b, (((1,), (1,)), ((), ())), preferred_element_type=F32)


def norm_parts(stream):
    centered = stream - jnp.mean(stream, -1, keepdims=True)
    spread = jnp.mean(centered * centered, -1, keepdims=True)
    scale = lax.rsqrt(spread + 1e-05)
    return centered * scale, scale


def norm_back(grad, unit, scale, gain):
    grad = grad * gain
    inner = jnp.mean(grad * unit, -1, keepdims=True)
    return scale * (grad - jnp.mean(grad, -1, keepdims=True) - unit * inner)


def column_sum(x):
    return jnp.sum(x, axis=0, keepdims=True)


def unpack_split(split_ref, qkv, output, up, up_bias, down):
    lane = lax.broadcasted_iota(jnp.int32, (32, 128), 1)
    for layer in range(LAYERS):
        base = layer * 385
        kinds = [[jnp.zeros((32, 128), F32) for j in range(4)] for kind in range(3)]
        for m in range(4):
            rows = [split_ref[m, pl.ds(base + k, 32, stride=3), :] for k in range(3)]
            inside = (lane >= 32 * m) & (lane < 32 * m + 32)
            for j in range(4):
                for kind in range(3):
                    spot = j * 96 + kind * 32
                    source = rows[spot // 128]
                    shift = (32 * m - spot % 128) % 128
                    moved = pltpu.roll(source, shift, 1) if shift else source
                    kinds[kind][j] = jnp.where(inside, moved, kinds[kind][j])
            output[layer, 32 * m : 32 * m + 32] = split_ref[m, base + 96 : base + 128]
            up[layer, :, 128 * m : 128 * m + 128] = split_ref[m, base + 128 : base + 256]
            up_bias[layer, :, 128 * m : 128 * m + 128] = split_ref[m, base + 256 : base + 257]
            down[layer, 128 * m : 128 * m + 128] = split_ref[m, base + 257 : base + 385]
        for kind in range(3):
            for j in range(4):
                qkv[layer, kind, pl.ds(j, 32, stride=4), :] = kinds[kind][j]


def pack_split(out_ref, qkv, output, up, up_bias, down):
    lane = lax.broadcasted_iota(jnp.int32, (32, 128), 1)
    for layer in range(LAYERS):
        base = layer * 385
        parts = [[qkv[layer, kind, pl.ds(j, 32, stride=4), :] for j in range(4)] for kind in range(3)]
        for m in range(4):
            rows = [jnp.zeros((32, 128), F32) for k in range(3)]
            for j in range(4):
                for kind in range(3):
                    spot = j * 96 + kind * 32
                    low = spot % 128
                    shift = (low - 32 * m) % 128
                    moved = pltpu.roll(parts[kind][j], shift, 1) if shift else parts[kind][j]
                    inside = (lane >= low) & (lane < low + 32)
                    rows[spot // 128] = jnp.where(inside, moved, rows[spot // 128])
            for k in range(3):
                out_ref[m, pl.ds(base + k, 32, stride=3), :] = rows[k]
            out_ref[m, base + 96 : base + 128] = output[layer, 32 * m : 32 * m + 32]
            out_ref[m, base + 128 : base + 256] = up[layer, :, 128 * m : 128 * m + 128]
            out_ref[m, base + 256 : base + 257] = up_bias[layer, :, 128 * m : 128 * m + 128]
            out_ref[m, base + 257 : base + 385] = down[layer, 128 * m : 128 * m + 128]
    for m in range(4):
        out_ref[m, 770:776] = jnp.zeros((6, 128), F32)


def former_body(
    slots,
    used,
    lengths_ref,
    returns_ref,
    actions_ref,
    head_ref,
    z_ref,
    small,
    times_all,
    encoder,
    weights,
    d_three_ref,
    d_encoder_ref,
    d_vectors_ref,
    d_actions_ref,
    d_head_ref,
    d_times_ref,
    loss_ref,
    grads,
    chances,
    kept,
    sums,
    flats,
):
    qkv, output, up, up_bias, down = weights
    d_qkv, d_output, d_up, d_up_bias, d_down = grads
    rows = 3 * slots
    wins, steps = returns_ref.shape
    vec = [small[k : k + 1] for k in range(17)]
    table = small[17 : 17 + ACT]
    slot = lax.broadcasted_iota(jnp.int32, (slots, 1), 0)
    window = jnp.zeros((slots, 1), jnp.int32)
    begin = jnp.zeros((slots, 1), jnp.int32)
    end = jnp.int32(0)
    for w in range(wins - 1):
        end = end + lengths_ref[w]
        window = jnp.where(slot >= end, w + 1, window)
        begin = jnp.where(slot >= end, end, begin)
    moment = slot - begin
    valid = slot < used
    time_lane = lax.broadcasted_iota(jnp.int32, (slots, steps), 1)
    amount = jnp.zeros((slots, 1), F32)
    action = jnp.zeros((slots, 1), jnp.int32)
    for w in range(wins):
        here = (time_lane == moment) & (window == w)
        amount = amount + jnp.sum(
            jnp.where(here, returns_ref[w : w + 1], 0.0), axis=1, keepdims=True
        )
        action = action + jnp.sum(jnp.where(here, actions_ref[w : w + 1], 0), axis=1, keepdims=True)
    lane = lax.broadcasted_iota(jnp.int32, (slots, 128), 1)
    picks = jnp.where((lane == action) & valid, 1.0, 0.0)
    reward = jnp.tanh(amount * vec[14] + vec[15])
    table = jnp.concatenate([table, jnp.zeros((128 - ACT, 128), F32)], axis=0)
    move = jnp.tanh(mm(picks, table))
    sum_state = jnp.zeros((slots, 128), F32)
    for k in range(28):
        z = jnp.where(valid, z_ref[k, 0:slots], 0.0)
        high, low = two_parts(gelu_value(z))
        flats[0, 0:slots, k * 128 : (k + 1) * 128] = high
        flats[1, 0:slots, k * 128 : (k + 1) * 128] = low
    for part in range(2):
        sum_state = sum_state + fold_pair(dot(flats[part, 0:slots], encoder[...]))
    state = jnp.tanh(sum_state + vec[16])
    times = times_all[0:slots]
    stream = jnp.concatenate([reward + times, state + times, move + times], axis=0)

    def ids(axis):
        shape = (rows, 1) if axis == 0 else (1, rows)
        number = lax.broadcasted_iota(jnp.int32, shape, axis)
        kind = jnp.where(number >= 2 * slots, 2, jnp.where(number >= slots, 1, 0))
        return number - kind * slots, kind

    (slot_q, kind_q), (slot_k, kind_k) = ids(0), ids(1)

    def begin_of(slot_ids):
        found = jnp.zeros(slot_ids.shape, jnp.int32)
        end = jnp.int32(0)
        for w in range(wins - 1):
            end = end + lengths_ref[w]
            found = jnp.where(slot_ids >= end, end, found)
        return found

    order_q = slot_q * 3 + kind_q
    order_k = slot_k * 3 + kind_k
    allowed = (order_q >= order_k) & (slot_k >= begin_of(slot_q)) & (slot_k < used)
    head_of = lax.shift_right_logical(lax.broadcasted_iota(jnp.int32, (1, 128), 1), 4)
    heads = D // HD
    batch = 4 if slots <= HALF else 2

    def masked(x, masks):
        return jnp.concatenate([jnp.where(mask, x, jnp.zeros_like(x)) for mask in masks], axis=0)

    def unmasked(x, masks):
        held = jnp.where(masks[0], x[0:rows], 0.0)
        for k in range(1, batch):
            held = held + jnp.where(masks[k], x[k * rows : (k + 1) * rows], 0.0)
        return held

    tape = []
    for layer in range(LAYERS):
        gains = vec[6 * layer : 6 * layer + 6]
        unit_one, scale_one = norm_parts(stream)
        normed = unit_one * gains[0] + gains[1]
        wide = jnp.concatenate([qkv[layer, k] for k in range(3)], axis=1)
        mixed = mm(normed, wide)
        query_high, query_low = two_parts(mixed[:, :128] * 0.25)
        keys, values = pair(mixed[:, 128:256]), pair(mixed[:, 256:])
        kept[layer, 0, 0:rows] = query_high
        kept[layer, 1, 0:rows] = query_low
        for k in range(2):
            kept[layer, 2 + k, 0:rows] = keys[:, k * 128 : (k + 1) * 128]
            kept[layer, 4 + k, 0:rows] = values[:, k * 128 : (k + 1) * 128]
        sums[0, 0:rows] = jnp.zeros((rows, 128), F32)

        def attend(turn, carry, layer=layer):
            masks = [head_of == turn * batch + k for k in range(batch)]
            parts = [masked(kept[layer, k, 0:rows], masks) for k in range(2)]
            keys = [kept[layer, 2 + k, 0:rows] for k in range(2)]
            values = [kept[layer, 4 + k, 0:rows] for k in range(2)]
            scores = dot_nt(
                jnp.concatenate([parts[0], parts[0]], axis=1), jnp.concatenate(keys, axis=1)
            )
            scores = (scores + dot_nt(parts[1], keys[0])).reshape(batch, rows, rows)
            scores = jnp.where(allowed[None], scores, -1e30)
            peak = jnp.max(scores, -1, keepdims=True)
            chance = jnp.exp(scores - peak)
            chance = chance / jnp.sum(chance, -1, keepdims=True)
            high, low = two_parts(chance.reshape(batch * rows, rows))
            spot = pl.ds(pl.multiple_of(turn * (batch * rows), 64), batch * rows)
            chances[layer, 0, spot, 0:rows] = high
            chances[layer, 1, spot, 0:rows] = low
            seen = fold_pair(dot(high, jnp.concatenate(values, axis=1))) + dot(low, values[0])
            sums[0, 0:rows] += unmasked(seen, masks)
            return carry

        lax.fori_loop(0, heads // batch, attend, 0)
        context = sums[0, 0:rows]
        stream = stream + mm(context, output[layer]) + gains[4]
        unit_two, scale_two = norm_parts(stream)
        normed_two = unit_two * gains[2] + gains[3]
        inner, slope = gelu_both(mm(normed_two, up[layer]) + up_bias[layer])
        stream = stream + mm(inner, down[layer]) + gains[5]
        tape.append((unit_one, scale_one, unit_two, scale_two, inner, slope, context))
    end_stream = stream[slots : 2 * slots]
    unit, scale = norm_parts(end_stream)
    final = unit * vec[12] + vec[13]
    logits = jnp.where(lane < ACT, mm(final, head_ref[...]), -1e30)
    peak = jnp.max(logits, -1, keepdims=True)
    powers = jnp.exp(logits - peak)
    total = jnp.sum(powers, -1, keepdims=True)
    chosen = jnp.sum(jnp.where(lane == action, logits, 0.0), -1, keepdims=True)
    terms = jnp.where(valid, jnp.log(total) + peak - chosen, 0.0)
    loss_ref[...] = jnp.broadcast_to(jnp.sum(terms, axis=0, keepdims=True), (8, 128))
    d_logits = jnp.where(valid, powers / total, 0.0) - picks
    d_head_ref[...] = mm_tn(final, d_logits)
    d_final = mm_nt(d_logits, head_ref[...])
    d_vec = [None] * 17
    d_vec[12] = column_sum(d_final * unit)
    d_vec[13] = column_sum(d_final)
    d_end = norm_back(d_final, unit, scale, vec[12])
    blank = jnp.zeros((slots, 128), F32)
    d_stream = jnp.concatenate([blank, d_end, blank], axis=0)
    for layer in reversed(range(LAYERS)):
        unit_one, scale_one, unit_two, scale_two, inner, slope, context = tape[layer]
        gains = vec[6 * layer : 6 * layer + 6]
        d_vec[6 * layer + 5] = column_sum(d_stream)
        d_down[layer] = mm_tn(inner, d_stream)
        d_inner = mm_nt(d_stream, down[layer]) * slope
        d_up_bias[layer] = column_sum(d_inner)
        normed_two = unit_two * gains[2] + gains[3]
        d_up[layer] = mm_tn(normed_two, d_inner)
        d_normed = mm_nt(d_inner, up[layer])
        d_vec[6 * layer + 2] = column_sum(d_normed * unit_two)
        d_vec[6 * layer + 3] = column_sum(d_normed)
        d_stream = d_stream + norm_back(d_normed, unit_two, scale_two, gains[2])
        d_vec[6 * layer + 4] = column_sum(d_stream)
        d_output[layer] = mm_tn(context, d_stream)
        d_context = mm_nt(d_stream, output[layer])
        bases = d_context * context
        high, low = two_parts(d_context)
        for k in range(3):
            sums[k, 0:rows] = jnp.zeros((rows, 128), F32)
        kept[layer, 6, 0:rows] = high
        kept[layer, 7, 0:rows] = low
        sums[3, 0:rows] = bases

        def attend_back(turn, carry, layer=layer):
            masks = [head_of == turn * batch + k for k in range(batch)]
            query = [masked(kept[layer, k, 0:rows], masks) for k in range(2)]
            keys = [kept[layer, 2 + k, 0:rows] for k in range(2)]
            values = [kept[layer, 4 + k, 0:rows] for k in range(2)]
            d_seen = [masked(kept[layer, 6 + k, 0:rows], masks) for k in range(2)]
            base = jnp.sum(masked(sums[3, 0:rows], masks), -1, keepdims=True)
            spot = pl.ds(pl.multiple_of(turn * (batch * rows), 64), batch * rows)
            chance = [chances[layer, k, spot, 0:rows] for k in range(2)]
            d_chance = dot_nt(
                jnp.concatenate([d_seen[0], d_seen[0]], axis=1), jnp.concatenate(values, axis=1)
            )
            d_chance = d_chance + dot_nt(d_seen[1], values[0])
            d_scores = (chance[0].astype(F32) + chance[1].astype(F32)) * (d_chance - base)
            high, low = two_parts(d_scores)
            d_query = fold_pair(dot(high, jnp.concatenate(keys, axis=1))) + dot(low, keys[0])
            sums[0, 0:rows] += unmasked(d_query, masks)
            d_keys = fold_pair(dot_rows(high, jnp.concatenate(query, axis=1)))
            sums[1, 0:rows] += d_keys + dot_rows(low, query[0])
            d_values = fold_pair(dot_rows(chance[0], jnp.concatenate(d_seen, axis=1)))
            sums[2, 0:rows] += d_values + dot_rows(chance[1], d_seen[0])
            return carry

        lax.fori_loop(0, heads // batch, attend_back, 0)
        normed = unit_one * gains[0] + gains[1]
        d_mixed = jnp.concatenate(
            [sums[0, 0:rows] * 0.25, sums[1, 0:rows], sums[2, 0:rows]], axis=1
        )
        wide = jnp.concatenate([qkv[layer, k] for k in range(3)], axis=1)
        d_wide = mm_tn(normed, d_mixed)
        for k in range(3):
            d_qkv[layer, k] = d_wide[:, k * 128 : (k + 1) * 128]
        d_normed = mm_nt(d_mixed, wide)
        d_vec[6 * layer] = column_sum(d_normed * unit_one)
        d_vec[6 * layer + 1] = column_sum(d_normed)
        d_stream = d_stream + norm_back(d_normed, unit_one, scale_one, gains[0])
    d_reward, d_state, d_move = (d_stream[k * slots : (k + 1) * slots] for k in range(3))
    d_times_ref[0:slots] = jnp.where(valid, d_reward + d_state + d_move, 0.0)
    d_reward = d_reward * (1.0 - reward * reward)
    d_vec[14] = column_sum(d_reward * amount)
    d_vec[15] = column_sum(d_reward)
    d_move = d_move * (1.0 - move * move)
    d_actions_ref[...] = mm_tn(picks, d_move)[0:24]
    d_state = jnp.where(valid, d_state * (1.0 - state * state), 0.0)
    d_vec[16] = column_sum(d_state)
    d_vectors_ref[...] = jnp.concatenate(d_vec + [jnp.zeros((7, 128), F32)], axis=0)
    high, low = two_parts(d_state)
    twice = jnp.concatenate([high, high], axis=1)
    both = jnp.concatenate([high, low], axis=1)
    d_flat = dot_nt(twice, encoder[...]) + dot_nt(low, encoder[:, 0:128])
    d_block = dot_rows(flats[0, 0:slots], both) + dot_rows(flats[1, 0:slots], both)
    d_block = fold_pair(d_block)
    for k in range(28):
        z = jnp.where(valid, z_ref[k, 0:slots], 0.0)
        d_three_ref[k, 0:slots] = d_flat[:, k * 128 : (k + 1) * 128] * gelu_both(z)[1]
        y, v = divmod(k, 4)
        for o in range(2):
            if 2 * v + o < 7:
                d_encoder_ref[pl.ds(y * 7 + 2 * v + o, 64, stride=49), :] = d_block[
                    k * 128 + o * 64 : k * 128 + (o + 1) * 64
                ]


def former_kernel(
    packed,
    lengths_ref,
    starts_ref,
    returns_ref,
    actions_ref,
    head_ref,
    z_ref,
    flat_ref,
    *refs,
):
    if packed:
        split_ref, refs = refs[0], refs[1:]
    else:
        given, refs = refs[:5], refs[5:]
    (d_three_ref, d_encoder_ref, d_vectors_ref, d_actions_ref, d_head_ref) = refs[:5]
    (d_times_ref, loss_ref), refs = refs[5:7], refs[7:]
    if packed:
        d_split_ref, refs = refs[0], refs[1:]
        weights, grads, refs = refs[:5], refs[5:10], refs[10:]
    else:
        grads, refs = refs[:5], refs[5:]
        weights = given
    (raw, near, small, rows_raw, times_all, encoder, chances, kept, sums, flats, sem) = refs
    used = jnp.int32(0)
    wins = lengths_ref.shape[0]
    for w in range(wins):
        used = used + lengths_ref[w]
    copies = [
        pltpu.make_async_copy(flat_ref.at[pl.ds(608, 3144)], raw, sem.at[0]),
        pltpu.make_async_copy(flat_ref.at[pl.ds(3744, 48)], rows_raw.at[wins], sem.at[1]),
    ]
    offsets = []
    for w in range(wins):
        row = TIME_ROW + starts_ref[w]
        low = pl.multiple_of(lax.div(row, 8) * 8, 8)
        offsets.append(row - low)
        copies.append(
            pltpu.make_async_copy(
                flat_ref.at[pl.ds(low, 40)], rows_raw.at[w, pl.ds(0, 40)], sem.at[2 + w]
            )
        )
    for copy in copies:
        copy.start()
    if packed:
        unpack_split(split_ref, *weights)
    for copy in copies:
        copy.wait()
    lane = lanes()

    def straight(first, second):
        return jnp.where(lane < 96, pltpu.roll(first, 96, 1), pltpu.roll(second, 96, 1))

    def turn(step, carry):
        spot = pl.multiple_of(step * 64, 64)
        near[pl.ds(spot, 64)] = straight(raw[pl.ds(spot + 1, 64)], raw[pl.ds(spot + 2, 64)])
        return carry

    lax.fori_loop(0, 49, turn, 0)
    for k in range(28):
        y, v = divmod(k, 4)
        halves = []
        for o in range(2):
            if 2 * v + o < 7:
                halves.append(near[pl.ds(y * 7 + 2 * v + o, 64, stride=49), :])
            else:
                halves.append(jnp.zeros((64, 128), F32))
        encoder[k * 128 : (k + 1) * 128] = pair(jnp.concatenate(halves, axis=0))
    small[...] = straight(rows_raw[wins, 1:41], rows_raw[wins, 2:42])
    times_all[...] = jnp.zeros(times_all.shape, F32)
    begin = 0
    row = lax.broadcasted_iota(jnp.int32, (32, 1), 0)
    for w in range(wins):
        rows = straight(
            rows_raw[w, pl.ds(offsets[w], 32)], rows_raw[w, pl.ds(offsets[w] + 1, 32)]
        )
        times_all[pl.ds(begin, 32)] = jnp.where(row < lengths_ref[w], rows, 0.0)
        begin = begin + lengths_ref[w]
    d_times_ref[...] = jnp.zeros(d_times_ref.shape, F32)

    def run(slots):
        former_body(
            slots,
            used,
            lengths_ref,
            returns_ref,
            actions_ref,
            head_ref,
            z_ref,
            small,
            times_all,
            encoder,
            weights,
            d_three_ref,
            d_encoder_ref,
            d_vectors_ref,
            d_actions_ref,
            d_head_ref,
            d_times_ref,
            loss_ref,
            grads,
            chances,
            kept,
            sums,
            flats,
        )

    @pl.when(used <= HALF)
    def few():
        run(HALF)

    @pl.when(used > HALF)
    def many():
        run(ROOM)

    if packed:
        pack_split(d_split_ref, *grads)


def former(lengths, starts, returns, actions, head, z_three, flat, weights, packed):
    smem = pl.BlockSpec(memory_space=pltpu.SMEM)
    vmem = pl.BlockSpec(memory_space=pltpu.VMEM)
    any_spec = pl.BlockSpec(memory_space=pl.ANY)
    wins = lengths.shape[0]
    canonical = [
        (LAYERS, 3, 128, 128),
        (LAYERS, 128, 128),
        (LAYERS, 128, FF),
        (LAYERS, 1, FF),
        (LAYERS, FF, 128),
    ]
    outs = [
        (28, ROOM, 128),
        (3136, 128),
        (24, 128),
        (24, 128),
        (128, 128),
        (ROOM, 128),
        (8, 128),
    ]
    outs += [(4, 776, 128)] if packed else canonical
    scratch = [pltpu.VMEM(shape, F32) for shape in canonical] * 2 if packed else []
    rows = 3 * ROOM
    scratch += [
        pltpu.VMEM((3144, 128), F32),
        pltpu.VMEM((3136, 128), F32),
        pltpu.VMEM((40, 128), F32),
        pltpu.VMEM((wins + 1, 48, 128), F32),
        pltpu.VMEM((ROOM + 32, 128), F32),
        pltpu.VMEM((3584, 256), BF16),
        pltpu.VMEM((LAYERS, 2, 8 * rows, rows), BF16),
        pltpu.VMEM((LAYERS, 8, rows, 128), BF16),
        pltpu.VMEM((4, rows, 128), F32),
        pltpu.VMEM((2, ROOM, 3584), BF16),
        pltpu.SemaphoreType.DMA((wins + 2,)),
    ]
    return pl.pallas_call(
        partial(former_kernel, packed),
        in_specs=[smem, smem] + [vmem] * 4 + [any_spec] + [vmem] * len(weights),
        out_specs=[vmem] * len(outs),
        out_shape=[jax.ShapeDtypeStruct(shape, F32) for shape in outs],
        scratch_shapes=scratch,
        compiler_params=pltpu.CompilerParams(vmem_limit_bytes=60 * 1024 * 1024),
        name="transformer_step",
    )(lengths, starts, returns, actions, head, z_three, flat, *weights)


def bit_orders(dp_size, mp_size):
    dp_bits = [("dp", k) for k in range(dp_size.bit_length() - 1)]
    mp_bits = [("mp", k) for k in range(mp_size.bit_length() - 1)]
    core, ys = mp_bits[:1], mp_bits[1:]
    middle = len(dp_bits) // 3
    xs, zs = dp_bits[:middle], dp_bits[middle:]
    return [core + xs + zs + ys, core + zs + ys + xs, core + ys + xs + zs]


def reduce_kernel(plan, *refs):
    inputs, steps = plan["inputs"], plan["steps"]
    ins = refs[: len(inputs)]
    out_shared, out_split, out_square = refs[len(inputs) : len(inputs) + 3]
    (work, landing, total, split_total, tiles, tile_in) = refs[len(inputs) + 3 : len(inputs) + 9]
    (load_sem, send_sem, recv_sem, tile_send, tile_recv, store_sem) = refs[len(inputs) + 9 :]
    spots = {"dp": lax.axis_index("dp"), "mp": lax.axis_index("mp")}

    def value(bit):
        return lax.rem(lax.div(spots[bit[0]], 1 << bit[1]), 2)

    def partner(bit):
        axis, k = bit
        other = spots[axis] + (1 - 2 * value(bit)) * (1 << k)
        place = dict(spots)
        place[axis] = other
        return (place["dp"], place["mp"])

    loads = []
    for number, (start, rows) in enumerate(inputs):
        loads.append(
            pltpu.make_async_copy(
                ins[number], work.at[pl.ds(start, rows)], load_sem.at[number]
            )
        )
        loads[-1].start()
    for start, rows in plan["blank"]:
        work[pl.ds(start, rows)] = jnp.zeros((rows, 128), jnp.float32)
    barrier = pltpu.get_barrier_semaphore()
    bits = plan["bits"]
    for bit in bits:
        pl.semaphore_signal(
            barrier, inc=1, device_id=partner(bit), device_id_type=pl.DeviceIdType.MESH
        )
    pl.semaphore_wait(barrier, len(bits))
    for load in loads:
        load.wait()

    def add_rows(target, start, source_start, rows):
        chunk = math.gcd(rows, 64)

        def body(turn, carry):
            spot = pl.multiple_of(start + turn * chunk, 8)
            place = pl.multiple_of(source_start + turn * chunk, 8)
            target[pl.ds(spot, chunk)] = (
                target[pl.ds(spot, chunk)] + landing[pl.ds(place, chunk)]
            )
            return carry

        lax.fori_loop(0, rows // chunk, body, 0)

    streams = plan["streams"]
    where = [stream["base"] for stream in streams]
    sizes = [stream["rows"] for stream in streams]
    flights = [None] * len(streams)
    landings = [stream["landing"] for stream in streams]
    slot = 0
    for step in range(steps):
        for number, stream in enumerate(streams):
            if flights[number] is not None:
                copy, half, land, keep = flights[number]
                copy.wait()
                add_rows(work, keep, land, half)
                where[number] = keep
            bit = stream["order"][step]
            half = sizes[number] // 2
            mine = value(bit)
            keep = where[number] + mine * half
            give = where[number] + (1 - mine) * half
            copy = pltpu.make_async_remote_copy(
                src_ref=work.at[pl.ds(pl.multiple_of(give, 8), half)],
                dst_ref=landing.at[pl.ds(landings[number], half)],
                send_sem=send_sem.at[slot],
                recv_sem=recv_sem.at[slot],
                device_id=partner(bit),
                device_id_type=pl.DeviceIdType.MESH,
            )
            copy.start()
            slot += 1
            flights[number] = (copy, half, landings[number], keep)
            landings[number] += half
            sizes[number] = half
    backs = [list(reversed(stream["order"][stream["shared"] :])) for stream in streams]
    spaces = []
    for number, stream in enumerate(streams):
        copy, half, land, keep = flights[number]
        copy.wait()
        add_rows(work, keep, land, half)
        where[number] = keep
        if stream["shared"]:
            spaces.append(split_total)
            low = keep
            for bit in stream["order"][: stream["shared"]]:
                pass
            rows = half
            offset = jnp.int32(0)
            size = stream["rows"] >> stream["shared"]
            for bit in stream["order"][stream["shared"] :]:
                size //= 2
                offset = offset + value(bit) * size
            split_total[pl.ds(pl.multiple_of(offset, 8), rows)] = work[
                pl.ds(pl.multiple_of(keep, 8), rows)
            ]
            held = work[pl.ds(pl.multiple_of(keep, 8), rows)]
            squares = held * held
            tiles[0] = jnp.sum(squares.reshape(rows // 8, 8, 128), axis=0)
            where[number] = offset
        else:
            spaces.append(total)
            total[pl.ds(pl.multiple_of(keep, 8), half)] = work[
                pl.ds(pl.multiple_of(keep, 8), half)
            ]
    flights = [None] * len(streams)
    tile_flight = None
    for step in range(steps):
        if tile_flight is not None:
            tile_flight.wait()
            tiles[step] = tiles[step - 1] + tile_in[step - 1]
        tile_flight = pltpu.make_async_remote_copy(
            src_ref=tiles.at[step],
            dst_ref=tile_in.at[step],
            send_sem=tile_send.at[step],
            recv_sem=tile_recv.at[step],
            device_id=partner(bits[step]),
            device_id_type=pl.DeviceIdType.MESH,
        )
        tile_flight.start()
        for number, stream in enumerate(streams):
            if flights[number] is not None:
                copy, low, size = flights[number]
                copy.wait()
                where[number] = low
                sizes[number] = size
                flights[number] = None
            if step >= len(backs[number]):
                continue
            bit = backs[number][step]
            rows = sizes[number]
            region = spaces[number].at[pl.ds(pl.multiple_of(where[number], 8), rows)]
            copy = pltpu.make_async_remote_copy(
                src_ref=region,
                dst_ref=region,
                send_sem=send_sem.at[slot],
                recv_sem=recv_sem.at[slot],
                device_id=partner(bit),
                device_id_type=pl.DeviceIdType.MESH,
            )
            copy.start()
            slot += 1
            flights[number] = (copy, where[number] - value(bit) * rows, rows * 2)
    tile_flight.wait()
    out_square[...] = tiles[steps - 1] + tile_in[steps - 1]
    stores = []
    for number, stream in enumerate(streams):
        if flights[number] is not None:
            flights[number][0].wait()
    shared_rows = total.shape[0]
    stores.append(
        pltpu.make_async_copy(total, out_shared.at[pl.ds(0, shared_rows)], store_sem.at[0])
    )
    stores.append(pltpu.make_async_copy(split_total, out_split, store_sem.at[1]))
    for store in stores:
        store.start()
    for store in stores:
        store.wait()


def reduce_all(pieces, split_blocks, dp_size, mp_size, out_rows, collective_id):
    orders = bit_orders(dp_size, mp_size)
    bits = orders[0]
    steps = len(bits)
    grain = 8 << steps
    used = max(start + array.shape[0] for start, array in pieces)
    half = -(-used // (2 * grain)) * grain
    shared_rows = 2 * half
    span = split_blocks[0].shape[0]
    split_grain = 8 * dp_size
    block = -(-span // split_grain) * split_grain
    inputs, arrays, blank = [], [], []
    reach = 0
    for start, array in pieces:
        if start > reach:
            blank.append((reach, start - reach))
        inputs.append((start, array.shape[0]))
        arrays.append(array)
        reach = start + array.shape[0]
    if shared_rows > reach:
        blank.append((reach, shared_rows - reach))
    shared_steps = mp_size.bit_length() - 1
    for number in range(mp_size):
        turned = 0
        for k in range(shared_steps):
            turned |= ((number >> k) & 1) << (shared_steps - 1 - k)
        start = shared_rows + turned * block
        inputs.append((start, span))
        arrays.append(split_blocks[number])
        if block > span:
            blank.append((start + span, block - span))
    split_rows = mp_size * block
    work_rows = shared_rows + split_rows
    streams = [
        dict(base=0, rows=half, order=orders[0], shared=0, landing=0),
        dict(base=half, rows=half, order=orders[1], shared=0, landing=half),
        dict(
            base=shared_rows,
            rows=split_rows,
            order=orders[2],
            shared=shared_steps,
            landing=shared_rows,
        ),
    ]
    plan = dict(inputs=inputs, blank=blank, streams=streams, bits=bits, steps=steps)
    copies = 3 * 2 * steps
    return pl.pallas_call(
        partial(reduce_kernel, plan),
        out_shape=(
            jax.ShapeDtypeStruct((out_rows, 128), jnp.float32),
            jax.ShapeDtypeStruct((block, 128), jnp.float32),
            jax.ShapeDtypeStruct((8, 128), jnp.float32),
        ),
        in_specs=[pl.BlockSpec(memory_space=pl.ANY)] * len(arrays),
        out_specs=(
            pl.BlockSpec(memory_space=pl.ANY),
            pl.BlockSpec(memory_space=pl.ANY),
            pl.BlockSpec(memory_space=pltpu.VMEM),
        ),
        scratch_shapes=[
            pltpu.VMEM((work_rows, 128), jnp.float32),
            pltpu.VMEM((work_rows, 128), jnp.float32),
            pltpu.VMEM((shared_rows, 128), jnp.float32),
            pltpu.VMEM((block, 128), jnp.float32),
            pltpu.VMEM((steps, 8, 128), jnp.float32),
            pltpu.VMEM((steps, 8, 128), jnp.float32),
            pltpu.SemaphoreType.DMA((len(arrays),)),
            pltpu.SemaphoreType.DMA((copies,)),
            pltpu.SemaphoreType.DMA((copies,)),
            pltpu.SemaphoreType.DMA((steps,)),
            pltpu.SemaphoreType.DMA((steps,)),
            pltpu.SemaphoreType.DMA((2,)),
        ],
        compiler_params=pltpu.CompilerParams(
            collective_id=collective_id,
            has_side_effects=True,
            vmem_limit_bytes=56 * 1024 * 1024,
        ),
        name="reduce_gradients",
    )(*arrays)


def spans(fast_rows):
    places = {}
    at = 0
    for name, rows in [
        ("encoder", 3136),
        ("conv", 616),
        ("vectors", 24),
        ("action_table", 24),
        ("head", 24),
        ("scalars", 8),
        ("index", 8),
        ("times", fast_rows),
    ]:
        places[name] = (at, rows)
        at += rows
    return places, at


FLAT_ROWS = 7896
BLOCK_ROWS = 512
LATE = 609


def adam_kernel(
    fast_rows,
    most_rows,
    lengths_ref,
    flag_ref,
    reduced_ref,
    split_ref,
    square_ref,
    weight_ref,
    first_ref,
    second_ref,
    split_weight_ref,
    split_first_ref,
    split_second_ref,
    new_ref,
    new_first_ref,
    new_second_ref,
    low_ref,
    split_new_ref,
    split_new_first_ref,
    split_new_second_ref,
    scalar_ref,
    pulled,
    flat,
    factor_ref,
    edge_ref,
    pull_sem,
):
    step = pl.program_id(0)
    places, fast_total = spans(fast_rows)
    lane = lax.broadcasted_iota(jnp.int32, (1, 128), 1)

    def update(weights, first, second, grads):
        first = beta_first * first + (1 - beta_first) * grads
        second = beta_second * second + (1 - beta_second) * grads * grads
        fix_one = 1.0 / (1 - beta_first**STEP)
        fix_two = 1.0 / (1 - beta_second**STEP)
        weights = weights - learn_rate * (
            first * fix_one / (jnp.sqrt(second * fix_two) + adam_epsilon) + weight_decay * weights
        )
        return weights, first, second

    @pl.when(step == 0)
    def prepare():
        pull = pltpu.make_async_copy(
            reduced_ref.at[pl.ds(0, fast_total)], pulled.at[pl.ds(0, fast_total)], pull_sem
        )
        pull.start()

        def wipe(turn, carry):
            flat[pl.ds(pl.multiple_of(turn * 64, 64), 64)] = jnp.zeros((64, 128), jnp.float32)
            return carry

        lax.fori_loop(0, flat.shape[0] // 64, wipe, 0)
        pull.wait()
        squares = jnp.zeros((8, 128), jnp.float32)

        def fold(rows):
            return jnp.sum((rows * rows).reshape(-1, 8, 128), axis=0)

        def conv_rows(turn, carry):
            spot = pl.multiple_of(turn * 56, 8)
            held = pulled[pl.ds(places["conv"][0] + spot, 56)]
            flat[pl.ds(8 + spot, 56)] = held
            return carry + fold(held)

        squares = lax.fori_loop(0, 616 // 56, conv_rows, squares)
        edge_ref[...] = flat[LATE : LATE + 16]

        def encoder_rows(turn, carry):
            spot = pl.multiple_of(turn * 64, 64)
            held = pulled[pl.ds(spot, 64)]
            flat[pl.ds(8 + LATE + spot, 64)] = pltpu.roll(held, 32, 1)
            return carry + fold(held)

        squares = lax.fori_loop(0, 3136 // 64, encoder_rows, squares)
        for name, at, rows in [
            ("vectors", LATE + 3136, 17),
            ("action_table", LATE + 3153, ACT),
            ("head", LATE + 3171 + TSTEPS, ACT),
        ]:
            held = pulled[places[name][0] : places[name][0] + 24]
            squares = squares + fold(held)
            flat[8 + at : 8 + at + rows] = pltpu.roll(held, 32, 1)[:rows]
        time_at = 8 + LATE + 3171

        @pl.when(flag_ref[0] > 0)
        def scatter():
            low = places["times"][0]
            spots = pulled[places["index"][0] : places["index"][0] + 8]
            rows = pltpu.roll(pulled[low : low + fast_rows], 32, 1)
            rows = pair(rows)
            chunk = 512

            def table(turn, carry):
                base = turn * chunk
                place = (lax.broadcasted_iota(jnp.int32, (chunk, 128), 0) + base).astype(F32)
                picks = [
                    jnp.where(place == spots[k : k + 1], 1.0, 0.0).astype(BF16)
                    for k in range(fast_rows // 128)
                ]
                held = fold_pair(dot(jnp.concatenate(picks, axis=1), rows))
                flat[pl.ds(time_at + base, chunk)] = held
                return carry

            lax.fori_loop(0, TSTEPS // chunk, table, 0)

        @pl.when(flag_ref[0] <= 0)
        def whole_table():
            pull_table = pltpu.make_async_copy(
                reduced_ref.at[pl.ds(places["times"][0], TSTEPS)],
                pulled.at[pl.ds(places["times"][0], TSTEPS)],
                pull_sem,
            )
            pull_table.start()
            pull_table.wait()

            def rows_in(turn, carry):
                spot = pl.multiple_of(turn * 64, 64)
                held = pulled[pl.ds(places["times"][0] + spot, 64)]
                flat[pl.ds(time_at + spot, 64)] = pltpu.roll(held, 32, 1)
                return carry

            lax.fori_loop(0, TSTEPS // 64, rows_in, 0)

        def time_squares(turn, carry):
            return carry + fold(flat[pl.ds(time_at + turn * 64, 64)])

        squares = lax.fori_loop(0, TSTEPS // 64, time_squares, squares)
        squares = squares + square_ref[...]
        count = jnp.float32(0)
        whole = lax.fori_loop(
            0, lengths_ref.shape[0], lambda k, c: c + lengths_ref[k], jnp.int32(0)
        )
        count = jnp.full((1, 128), whole.astype(jnp.float32))
        scalars = pulled[places["scalars"][0] : places["scalars"][0] + 8]
        total = jnp.sum(jnp.sum(squares, axis=0, keepdims=True), axis=1, keepdims=True)
        seed = 1.0 / count
        norm = jnp.sqrt(jnp.broadcast_to(total, (1, 128))) * seed
        factor = jnp.minimum(1.0, clip_limit / (norm + 1e-06)) * seed
        factor_ref[...] = jnp.broadcast_to(factor, (8, 128))
        loss = jnp.broadcast_to(scalars[0:1, 0:1], (1, 128))
        row = lax.broadcasted_iota(jnp.int32, (8, 128), 0)
        scalar_ref[...] = jnp.where(row == 0, norm, jnp.where(row == 1, loss, count))
        split_rows = split_weight_ref.shape[0]
        outs = update(
            split_weight_ref[...],
            split_first_ref[...],
            split_second_ref[...],
            split_ref[0:split_rows] * factor,
        )
        split_new_ref[...], split_new_first_ref[...], split_new_second_ref[...] = outs

    base = pl.multiple_of(step * BLOCK_ROWS, BLOCK_ROWS)
    factor = factor_ref[0:1]
    own = flat[pl.ds(8 + base, BLOCK_ROWS)]
    before = flat[pl.ds(7 + base, BLOCK_ROWS)]
    row = lax.broadcasted_iota(jnp.int32, (BLOCK_ROWS, 1), 0) + base
    late = row >= LATE
    before = jnp.where(row == LATE, edge_ref[8:9], before)
    grads = jnp.where(late & (lane < 32), before, own)
    outs = update(weight_ref[...], first_ref[...], second_ref[...], grads * factor)
    new_ref[...], new_first_ref[...], new_second_ref[...] = outs
    low_ref[...] = outs[0].astype(BF16)


def adam_all(
    lengths, flag, reduced, split_grad, square, shared, split, fast_rows
):
    places, fast_total = spans(fast_rows)
    most = places["times"][0] + TSTEPS
    grid = -(-FLAT_ROWS // BLOCK_ROWS)
    flat_spec = pl.BlockSpec((BLOCK_ROWS, 128), lambda i, *_: (i, 0))
    split_rows = split[0].shape[0]

    def whole(shape):
        return pl.BlockSpec(shape, lambda i, *_: (0,) * len(shape))

    split_spec = whole((split_rows, 128))
    shared_out = jax.ShapeDtypeStruct((FLAT_ROWS, 128), jnp.float32)
    split_out = jax.ShapeDtypeStruct((split_rows, 128), jnp.float32)
    return pl.pallas_call(
        partial(adam_kernel, fast_rows, most),
        grid_spec=pltpu.PrefetchScalarGridSpec(
            num_scalar_prefetch=2,
            grid=(grid,),
            in_specs=[
                pl.BlockSpec(memory_space=pl.ANY),
                whole(split_grad.shape),
                whole((8, 128)),
                flat_spec,
                flat_spec,
                flat_spec,
                split_spec,
                split_spec,
                split_spec,
            ],
            out_specs=[flat_spec] * 4 + [split_spec] * 3 + [whole((8, 128))],
            scratch_shapes=[
                pltpu.VMEM((most, 128), jnp.float32),
                pltpu.VMEM((grid * BLOCK_ROWS + 64, 128), jnp.float32),
                pltpu.VMEM((8, 128), jnp.float32),
                pltpu.VMEM((16, 128), jnp.float32),
                pltpu.SemaphoreType.DMA,
            ],
        ),
        out_shape=[shared_out] * 3
        + [jax.ShapeDtypeStruct((FLAT_ROWS, 128), BF16)]
        + [split_out] * 3
        + [jax.ShapeDtypeStruct((8, 128), jnp.float32)],
        compiler_params=pltpu.CompilerParams(vmem_limit_bytes=48 * 1024 * 1024),
        name="adam_update",
    )(lengths, flag, reduced, split_grad, square, *shared, *split)


FAST_ROWS = 768


def valid_slots(lengths, steps):
    ends = jnp.cumsum(lengths)
    slot = jnp.arange(ROOM, dtype=jnp.int32)
    past = slot[:, None] >= ends[None, :-1]
    begin = jnp.sum(jnp.where(past, lengths[None, :-1], 0), axis=1)
    return past, jnp.minimum(slot - begin, steps - 1), ends[-1]


def per_device(
    frames,
    returns,
    actions,
    starts,
    lengths,
    shared_weights,
    shared_first,
    shared_second,
    split_weights,
    split_first,
    split_second,
):
    dp_size, mp_size = lax.axis_size("dp"), lax.axis_size("mp")
    narrow = D // mp_size
    hidden_width = FF // mp_size
    wins, steps = returns.shape
    width = split_weights.shape[0]
    split_rows = width // 128
    packed = narrow == 32
    own_rows = split_weights.reshape(split_rows, 128)
    split_all = lax.all_gather(own_rows, "mp", axis=0)
    own_lengths = jnp.broadcast_to(lengths.astype(F32)[:, None, None], (wins, 8, 128))
    own_lengths = lax.optimization_barrier(own_lengths)
    lengths_all = lax.all_gather(own_lengths, ("dp", "mp"), axis=0)
    lengths_all = lax.optimization_barrier(lengths_all)
    lengths_all = lengths_all[:, :, 0, 0].reshape(-1).astype(jnp.int32)
    flat = shared_weights.reshape(FLAT_ROWS, 128)
    one = shared_weights[:8192].reshape(32, 256)
    two = shared_weights[8224:40992].reshape(64, 512)
    three = shared_weights[41056:77920].reshape(64, 576)
    head = jnp.pad(shared_weights[1008160:1010464].reshape(128, ACT), ((0, 0), (0, 128 - ACT)))
    picked, z_one, z_two, z_three = conv_forward(lengths, frames, flat, one, two, three)
    if packed:
        weights = [split_all]
    else:
        layers, layers_back = jax.vjp(
            lambda held: assemble(held, mp_size, narrow, hidden_width), split_all.reshape(-1)
        )
        weights = [
            jnp.stack([layer["qkv"].transpose(1, 0, 2) for layer in layers]),
            jnp.stack([layer["output"] for layer in layers]),
            jnp.stack([layer["up"] for layer in layers]),
            jnp.stack([layer["up_bias"][None] for layer in layers]),
            jnp.stack([layer["down"] for layer in layers]),
        ]
    results = former(lengths, starts, returns, actions, head, z_three, flat, weights, packed)
    d_three, d_encoder, d_vectors, d_actions, d_head, d_times, loss = results[:7]
    if packed:
        split_blocks = [results[7][m] for m in range(mp_size)]
    else:
        d_qkv, d_output, d_up, d_up_bias, d_down = results[7:]
        grad_layers = [
            dict(
                qkv=d_qkv[layer].transpose(1, 0, 2),
                output=d_output[layer],
                up=d_up[layer],
                up_bias=d_up_bias[layer, 0],
                down=d_down[layer],
            )
            for layer in range(LAYERS)
        ]
        gathered = layers_back(grad_layers)[0].reshape(mp_size, split_rows, 128)
        pad_rows = -split_rows % 8
        split_blocks = [jnp.pad(gathered[m], ((0, pad_rows), (0, 0))) for m in range(mp_size)]
    d_one, d_two, d_conv, d_bias = conv_backward(
        lengths, picked, z_one, z_two, d_three, two, three
    )
    conv_flat = jnp.concatenate(
        [
            d_one.reshape(-1),
            d_bias[0, 0, :32],
            d_two.reshape(-1),
            d_bias[1, 0, :64],
            d_conv.reshape(-1),
            d_bias[2, 0, :64],
            jnp.zeros((616 * 128 - 77984,), F32),
        ]
    )
    d_head = jnp.pad(d_head[:, :ACT].reshape(ACT, 128), ((0, 24 - ACT), (0, 0)))
    pieces = [
        ("encoder", d_encoder),
        ("conv", conv_flat.reshape(616, 128)),
        ("vectors", d_vectors),
        ("action_table", d_actions),
        ("head", d_head),
        ("scalars", loss),
    ]
    past, moment, used = valid_slots(lengths, steps)
    slot = jnp.arange(ROOM, dtype=jnp.int32)
    gaps = starts[1:] - starts[:-1]
    spot = moment + starts[0] + jnp.sum(jnp.where(past, gaps[None, :], 0), axis=1)
    me = lax.axis_index("dp") * mp_size + lax.axis_index("mp")
    skipped = jnp.sum(
        jnp.where(jnp.arange(lengths_all.shape[0]) < me * wins, lengths_all, 0)
    )
    fast = jnp.sum(lengths_all) <= FAST_ROWS
    places, fast_total = spans(FAST_ROWS)
    out_rows = -(-(places["times"][0] + TSTEPS) // 4096) * 4096

    def total_of(field, index, collective_id):
        laid = [(places[name][0], array) for name, array in pieces]
        laid += [(places["index"][0], index), (places["times"][0], field)]
        return reduce_all(laid, split_blocks, dp_size, mp_size, out_rows, collective_id)

    def compact(operands):
        rows, spots = operands
        at = jnp.minimum(skipped, FAST_ROWS)
        field = jnp.zeros((FAST_ROWS + ROOM, D), F32)
        field = lax.dynamic_update_slice(field, rows, (at, 0))[:FAST_ROWS]
        index = jnp.zeros((1024 + ROOM,), F32)
        index = lax.dynamic_update_slice(index, spots, (at,))[:1024].reshape(8, 128)
        return total_of(field, index, 1)

    def whole(operands):
        rows, spots = operands
        field = jnp.zeros((TSTEPS, D), F32).at[spots.astype(jnp.int32)].add(rows)
        return total_of(field, jnp.zeros((8, 128), F32), 2)

    spots = jnp.where(slot < used, spot, 0).astype(F32)
    reduced, split_sum, square = lax.cond(fast, compact, whole, (d_times, spots))
    shared_view = [a.reshape(FLAT_ROWS, 128) for a in (shared_weights, shared_first, shared_second)]
    split_view = [a.reshape(split_rows, 128) for a in (split_weights, split_first, split_second)]
    updated = adam_all(
        lengths_all,
        fast.astype(jnp.int32).reshape(1),
        reduced,
        split_sum,
        square,
        shared_view,
        split_view,
        FAST_ROWS,
    )
    shared_out = [a.reshape(-1) for a in updated[:4]]
    split_out = [a.reshape(-1) for a in updated[4:7]]
    scalars = updated[7]
    return (
        *shared_out,
        *split_out,
        split_out[0].astype(BF16),
        scalars[0, 0],
        scalars[1, 0],
        scalars[2, 0],
    )


def solution(mesh):
    return jax.shard_map(
        per_device,
        mesh=mesh,
        in_specs=(
            P(("dp", "mp"), None, None, None, None),
            P(("dp", "mp"), None),
            P(("dp", "mp"), None),
            P(("dp", "mp")),
            P(("dp", "mp")),
            P(),
            P(),
            P(),
            P("mp"),
            P("mp"),
            P("mp"),
        ),
        out_specs=(P(), P(), P(), P(), P("mp"), P("mp"), P("mp"), P("mp"), P(), P(), P()),
        check_vma=False,
    )
```

```python
from functools import partial
import math

import jax
import jax.numpy as jnp
from jax import lax
from jax.experimental import pallas as pl
from jax.experimental.pallas import tpu as pltpu
from jax.sharding import PartitionSpec as P

D = 128
FF = 512
ACT = 18
C1 = 32
C2 = 64
TSTEPS = 4096
LAYERS = 2
STEP = 10
HD = 16


clip_limit = 0.1
learn_rate = 0.05
beta_first = 0.9
beta_second = 0.95
adam_epsilon = 1e-08
weight_decay = 0.1


def span_layout(narrow, hidden):
    return [
        ("qkv", (D, 3, narrow)),
        ("output", (narrow, D)),
        ("up", (D, hidden)),
        ("up_bias", (hidden,)),
        ("down", (hidden, D)),
    ]


def assemble(flat, copies, narrow, hidden):
    layout = span_layout(narrow, hidden)
    width = sum((math.prod(shape) for name, shape in layout))
    blocks = flat.reshape(copies, LAYERS, width)
    layers = []
    for layer in range(LAYERS):
        offset = 0
        pieces = {}
        for name, shape in layout:
            count = math.prod(shape)
            pieces[name] = blocks[:, layer, offset : offset + count].reshape((copies,) + shape)
            offset += count
        layers.append(
            {
                "qkv": jnp.moveaxis(pieces["qkv"], 0, 2).reshape(D, 3, copies * narrow),
                "output": pieces["output"].reshape(copies * narrow, D),
                "up": jnp.moveaxis(pieces["up"], 0, 1).reshape(D, copies * hidden),
                "up_bias": pieces["up_bias"].reshape(copies * hidden),
                "down": pieces["down"].reshape(copies * hidden, D),
            }
        )
    return layers


GROUP = 16
ROOM = 128
HALF = 64
BF16 = jnp.bfloat16
F32 = jnp.float32


def gelu_value(x):
    inner = 0.7978845608028654 * (x + 0.044715 * (x * x * x))
    return 0.5 * x * (1.0 + jnp.tanh(inner))


def gelu_both(x):
    square = x * x
    turn = jnp.tanh(0.7978845608028654 * x * (1.0 + 0.044715 * square))
    half = 0.5 * (1.0 + turn)
    slope = half + 0.5 * x * (1.0 - turn * turn) * (
        0.7978845608028654 * (1.0 + 3 * 0.044715 * square)
    )
    return x * half, slope


def two_parts(x):
    high = x.astype(BF16)
    return high, (x - high.astype(F32)).astype(BF16)


def pair(x):
    return jnp.concatenate(two_parts(x), axis=-1)


def fold_pair(x):
    return x[:, :128] + x[:, 128:]


def dot(a, b):
    return lax.dot_general(a, b, (((1,), (0,)), ((), ())), preferred_element_type=F32)


def dot_rows(a, b):
    return lax.dot_general(a, b, (((0,), (0,)), ((), ())), preferred_element_type=F32)


def lanes():
    return lax.broadcasted_iota(jnp.int32, (1, 128), 1)


def conv_biases(flat_ref):
    lane = lanes()
    one = jnp.where(lane < 32, flat_ref[64:65], 0.0)
    one = one + pltpu.roll(one, 32, 1)
    one = one + pltpu.roll(one, 64, 1)
    two = jnp.where(lane < 64, pltpu.roll(flat_ref[320:321], 96, 1), 0.0)
    two = two + pltpu.roll(two, 64, 1)
    three = jnp.where(
        lane < 32,
        pltpu.roll(flat_ref[608:609], 32, 1),
        jnp.where(lane < 64, pltpu.roll(flat_ref[609:610], 32, 1), 0.0),
    )
    three = three + pltpu.roll(three, 64, 1)
    return one, two, three


def spread_one(one_ref, put):
    turned = jnp.transpose(one_ref[...])
    lane = lax.broadcasted_iota(jnp.int32, (8, 128), 1)
    row = lax.broadcasted_iota(jnp.int32, (8, 128), 0)
    low = row < 4
    column = lax.shift_right_logical(lane, 5)
    for ky in range(8):
        for c in range(4):
            held = turned[c * 64 + ky * 8 : c * 64 + ky * 8 + 8]
            wide = jnp.concatenate([held] * 4, axis=1)
            flipped = jnp.concatenate([wide[4:], wide[:4]], axis=0)
            zero = jnp.zeros((8, 128), F32)
            first = jnp.where(column == 0, wide, jnp.where((column == 1) & ~low, flipped, zero))
            second = jnp.where(
                column == 2,
                wide,
                jnp.where(((column == 1) & low) | ((column == 3) & ~low), flipped, zero),
            )
            third = jnp.where((column == 3) & low, flipped, zero)
            put(ky * 128 + c * 32, jnp.concatenate([first, second, third, zero], axis=0))


def spread_two(two_ref, turned, put):
    lane = lax.broadcasted_iota(jnp.int32, (32, 128), 1)
    for j in range(4):
        block = jnp.transpose(two_ref[:, j * 128 : (j + 1) * 128])
        turned[j * 128 : (j + 1) * 128] = jnp.concatenate([block, block], axis=1)
    for ky in range(4):
        rows = [turned[pl.ds(ky * 4 + kx, 32, stride=16)] for kx in range(4)]
        for i in range(8):
            left = rows[i] if i < 4 else jnp.zeros((32, 128), F32)
            right = rows[i - 2] if 2 <= i < 6 else jnp.zeros((32, 128), F32)
            put(ky * 256 + i * 32, jnp.where(lane < 64, left, right))


def spread_three(three_ref, turned, put):
    lane = lax.broadcasted_iota(jnp.int32, (64, 128), 1)
    for j in range(5):
        wide = min(128, 576 - j * 128)
        block = jnp.transpose(three_ref[:, j * 128 : j * 128 + wide])
        turned[j * 128 : j * 128 + wide] = jnp.concatenate([block, block], axis=1)
    for ky in range(3):
        rows = [turned[pl.ds(ky * 3 + kx, 64, stride=9)] for kx in range(3)]
        for i in range(4):
            left = rows[i] if i < 3 else jnp.zeros((64, 128), F32)
            right = rows[i - 1] if i >= 1 else jnp.zeros((64, 128), F32)
            put(ky * 256 + i * 64, jnp.where(lane < 64, left, right))


def last_masks():
    return lanes() < 64


def conv_forward_kernel(
    lengths_ref,
    frames_ref,
    flat_ref,
    one_ref,
    two_ref,
    three_ref,
    picked_ref,
    z_one_ref,
    z_two_ref,
    z_three_ref,
    held,
    wide,
    picked,
    z_one,
    z_two,
    z_three,
    h_one,
    h_two,
    w_one,
    w_two,
    w_three,
    choose,
    turned,
    frame_sem,
    out_sem,
):
    wins = lengths_ref.shape[0]
    steps = frames_ref.shape[1]
    used = jnp.int32(0)
    for w in range(wins):
        used = used + lengths_ref[w]
    groups = lax.div(used + (GROUP - 1), GROUP)

    def frame_copy(group, spot, slot):
        state = jnp.minimum(group * GROUP + spot, used - 1)
        window, begin, end = jnp.int32(0), jnp.int32(0), jnp.int32(0)
        for w in range(wins - 1):
            end = end + lengths_ref[w]
            window = jnp.where(state >= end, w + 1, window)
            begin = jnp.where(state >= end, end, begin)
        return pltpu.make_async_copy(
            frames_ref.at[window, state - begin], held.at[slot, spot], frame_sem.at[slot, spot]
        )

    def fetch(group, slot):
        def one(spot, carry):
            frame_copy(group, spot, slot).start()
            return carry

        lax.fori_loop(0, GROUP, one, 0)

    fetch(0, 0)
    h_one[...] = jnp.zeros(h_one.shape, BF16)

    def put_one(row, block):
        w_one[row : row + 32] = pair(block)

    def put_two(row, block):
        w_two[row : row + 32] = pair(block)

    def put_three(row, block):
        w_three[row : row + 64] = pair(block)

    spread_one(one_ref, put_one)
    spread_two(two_ref, turned, put_two)
    spread_three(three_ref, turned, put_three)
    bias_one, bias_two, bias_three = conv_biases(flat_ref)
    row = lax.broadcasted_iota(jnp.int32, (128, 640), 0)
    column = lax.broadcasted_iota(jnp.int32, (128, 640), 1)
    place = jnp.bitwise_and(column, 31)
    channel = jnp.bitwise_and(lax.shift_right_logical(column, 5), 3)
    block = lax.shift_right_logical(column, 7)
    right = (row == 16 * block + place) & (place < 20)
    for c in range(4):
        choose[c * 128 : (c + 1) * 128] = jnp.where(right & (channel == c), 1.0, 0.0).astype(BF16)

    def one_group(group, carry):
        slot = lax.rem(group, 2)

        @pl.when(group + 1 < groups)
        def ahead():
            fetch(group + 1, 1 - slot)

        def lay(spot, carry):
            frame_copy(group, spot, slot).wait()
            image = held[slot, spot].astype(F32).reshape(336, 84)
            image = jnp.concatenate([image, jnp.zeros((336, 44), F32)], axis=1)
            wide[pl.ds(spot, 336, stride=GROUP), :] = image
            return carry

        lax.fori_loop(0, GROUP, lay, 0)
        for part in range(3):
            rows = wide[part * 1792 : (part + 1) * 1792].reshape(28, 4, GROUP, 128)
            rows = [rows[:, c].reshape(448, 128).astype(BF16) for c in range(4)]
            result = dot(jnp.concatenate(rows, axis=1), choose[...])
            picked[part * 7 : (part + 1) * 7] = result.astype(BF16).reshape(7, 4, GROUP, 640)
        keep_picked = pltpu.make_async_copy(picked, picked_ref.at[group], out_sem.at[0])
        keep_picked.start()
        for q in range(5):
            pieces = [
                picked[j : j + 20, b, :, q * 128 : (q + 1) * 128].reshape(20 * GROUP, 128)
                for j in range(2)
                for b in range(4)
            ]
            z = fold_pair(dot(jnp.concatenate(pieces, axis=1), w_one[...])) + bias_one
            z_one[:, :, q] = z.reshape(10, 2, GROUP, 128)
            high, low = two_parts(gelu_value(z))
            h_one[0, :, :, q] = high.reshape(10, 2, GROUP, 128)
            h_one[1, :, :, q] = low.reshape(10, 2, GROUP, 128)
        keep_one = pltpu.make_async_copy(z_one, z_one_ref.at[group], out_sem.at[1])
        keep_one.start()
        total = jnp.zeros((45 * GROUP, 128), F32)
        for part in range(2):
            pieces = []
            for j in range(2):
                for b in range(2):
                    pieces.append(h_one[part, j : j + 9, b, 0:5].reshape(45 * GROUP, 128))
                    pieces.append(h_one[part, j : j + 9, b, 1:6].reshape(45 * GROUP, 128))
            total = total + fold_pair(dot(jnp.concatenate(pieces, axis=1), w_two[...]))
        z = (total + bias_two).reshape(9, 5, GROUP, 128)
        z_two[...] = z
        h = gelu_value(z)
        high, low = two_parts(h)
        h_two[0] = high
        h_two[1] = low
        edge = jnp.where(last_masks(), h[:, 4].reshape(9 * GROUP, 128), 0.0)
        high, low = two_parts(edge)
        h_two[0, :, 4] = high.reshape(9, GROUP, 128)
        h_two[1, :, 4] = low.reshape(9, GROUP, 128)
        keep_two = pltpu.make_async_copy(z_two, z_two_ref.at[group], out_sem.at[2])
        keep_two.start()
        total = jnp.zeros((28 * GROUP, 128), F32)
        for part in range(2):
            pieces = []
            for ky in range(3):
                pieces.append(h_two[part, ky : ky + 7, 0:4].reshape(28 * GROUP, 128))
                pieces.append(h_two[part, ky : ky + 7, 1:5].reshape(28 * GROUP, 128))
            total = total + fold_pair(dot(jnp.concatenate(pieces, axis=1), w_three[...]))
        z_three[...] = (total + bias_three).reshape(28, GROUP, 128)
        spot = pl.multiple_of(group * GROUP, GROUP)
        keep_three = pltpu.make_async_copy(
            z_three, z_three_ref.at[:, pl.ds(spot, GROUP)], out_sem.at[3]
        )
        keep_three.start()
        keep_picked.wait()
        keep_one.wait()
        keep_two.wait()
        keep_three.wait()
        return carry

    lax.fori_loop(0, groups, one_group, 0)


def conv_forward(lengths, frames, flat, one, two, three):
    most = ROOM // GROUP
    any_spec = pl.BlockSpec(memory_space=pl.ANY)
    vmem = pl.BlockSpec(memory_space=pltpu.VMEM)
    return pl.pallas_call(
        conv_forward_kernel,
        in_specs=[
            pl.BlockSpec(memory_space=pltpu.SMEM),
            any_spec,
            vmem,
            vmem,
            vmem,
            vmem,
        ],
        out_specs=[any_spec] * 4,
        out_shape=[
            jax.ShapeDtypeStruct((most, 21, 4, GROUP, 640), BF16),
            jax.ShapeDtypeStruct((most, 10, 2, 5, GROUP, 128), F32),
            jax.ShapeDtypeStruct((most, 9, 5, GROUP, 128), F32),
            jax.ShapeDtypeStruct((28, ROOM, 128), F32),
        ],
        scratch_shapes=[
            pltpu.VMEM((2, GROUP, 84, 4, 84), BF16),
            pltpu.VMEM((336 * GROUP, 128), F32),
            pltpu.VMEM((21, 4, GROUP, 640), BF16),
            pltpu.VMEM((10, 2, 5, GROUP, 128), F32),
            pltpu.VMEM((9, 5, GROUP, 128), F32),
            pltpu.VMEM((28, GROUP, 128), F32),
            pltpu.VMEM((2, 10, 2, 6, GROUP, 128), BF16),
            pltpu.VMEM((2, 9, 5, GROUP, 128), BF16),
            pltpu.VMEM((1024, 256), BF16),
            pltpu.VMEM((1024, 256), BF16),
            pltpu.VMEM((768, 256), BF16),
            pltpu.VMEM((512, 640), BF16),
            pltpu.VMEM((576, 128), F32),
            pltpu.SemaphoreType.DMA((2, GROUP)),
            pltpu.SemaphoreType.DMA((4,)),
        ],
        compiler_params=pltpu.CompilerParams(vmem_limit_bytes=48 * 1024 * 1024),
        name="conv_forward",
    )(lengths, frames.transpose(0, 1, 3, 2, 4), flat, one, two, three)


def gather_one(total, out):
    lane = lax.broadcasted_iota(jnp.int32, (32, 128), 1)
    halves = [jnp.zeros((32, 128), F32) for side in range(2)]
    for ky in range(8):
        held = total[0:128, ky * 128 : (ky + 1) * 128] + total[128:256, ky * 128 : (ky + 1) * 128]
        summed = held[0:32]
        for o in range(1, 4):
            summed = summed + pltpu.roll(held[32 * o : 32 * o + 32], 128 - 4 * o, 1)
        for c in range(4):
            spot = (c % 2) * 64 + ky * 8
            shift = (spot - c * 32) % 128
            moved = pltpu.roll(summed, shift, 1) if shift else summed
            inside = (lane >= spot) & (lane < spot + 8)
            halves[c // 2] = halves[c // 2] + jnp.where(inside, moved, 0.0)
    out[:, 0:128] = halves[0]
    out[:, 128:256] = halves[1]


def gather_two(total, turned, out):
    lane = lax.broadcasted_iota(jnp.int32, (64, 128), 1)
    for ky in range(4):
        near = total[0:128, ky * 256 : ky * 256 + 128] + total[128:256, ky * 256 : ky * 256 + 128]
        far = (
            total[0:128, ky * 256 + 128 : ky * 256 + 256]
            + total[128:256, ky * 256 + 128 : ky * 256 + 256]
        )
        summed = near[0:64] + jnp.where(
            lane < 64, pltpu.roll(near[64:128], 64, 1), pltpu.roll(far[64:128], 64, 1)
        )
        flipped = jnp.transpose(jnp.concatenate([summed, jnp.zeros((64, 128), F32)], axis=0))
        for kx in range(4):
            turned[pl.ds(ky * 4 + kx, 32, stride=16), :] = flipped[kx * 32 : (kx + 1) * 32]
    for j in range(4):
        out[:, j * 128 : (j + 1) * 128] = jnp.transpose(turned[j * 128 : (j + 1) * 128])[0:64]


def gather_three(total, turned, out):
    lane = lax.broadcasted_iota(jnp.int32, (64, 128), 1)
    blank = jnp.zeros((64, 128), F32)
    for ky in range(3):
        near = total[0:128, ky * 256 : ky * 256 + 128] + total[128:256, ky * 256 : ky * 256 + 128]
        far = (
            total[0:128, ky * 256 + 128 : ky * 256 + 256]
            + total[128:256, ky * 256 + 128 : ky * 256 + 256]
        )
        first = near[0:64] + jnp.where(
            lane < 64, pltpu.roll(near[64:128], 64, 1), pltpu.roll(far[64:128], 64, 1)
        )
        second = far[0:64] + pltpu.roll(far[64:128], 64, 1)
        flipped = jnp.transpose(jnp.concatenate([first, blank], axis=0))
        turned[pl.ds(ky * 3, 64, stride=9), :] = flipped[0:64]
        turned[pl.ds(ky * 3 + 1, 64, stride=9), :] = flipped[64:128]
        flipped = jnp.transpose(jnp.concatenate([second, blank], axis=0))
        turned[pl.ds(ky * 3 + 2, 64, stride=9), :] = flipped[0:64]
    for j in range(5):
        wide = min(128, 576 - j * 128)
        out[:, j * 128 : j * 128 + wide] = jnp.transpose(turned[j * 128 : j * 128 + wide])[0:64]


def conv_backward_kernel(
    lengths_ref,
    picked_ref,
    z_one_ref,
    z_two_ref,
    d_three_ref,
    two_ref,
    three_ref,
    one_out,
    two_out,
    three_out,
    bias_out,
    picked,
    z_one,
    z_two,
    d_three,
    h_one,
    h_two,
    slope_one,
    pad_three,
    pad_two,
    d_one,
    v_two,
    v_three,
    spread,
    turned,
    total_one,
    total_two,
    total_three,
    load_sem,
):
    used = jnp.int32(0)
    for w in range(lengths_ref.shape[0]):
        used = used + lengths_ref[w]
    groups = lax.div(used + (GROUP - 1), GROUP)

    def loads(group, slot):
        spot = pl.multiple_of(group * GROUP, GROUP)
        return [
            pltpu.make_async_copy(picked_ref.at[group], picked.at[slot], load_sem.at[slot, 0]),
            pltpu.make_async_copy(z_one_ref.at[group], z_one.at[slot], load_sem.at[slot, 1]),
            pltpu.make_async_copy(z_two_ref.at[group], z_two.at[slot], load_sem.at[slot, 2]),
            pltpu.make_async_copy(
                d_three_ref.at[:, pl.ds(spot, GROUP)], d_three.at[slot], load_sem.at[slot, 3]
            ),
        ]

    for load in loads(0, 0):
        load.start()

    def put_two(row, block):
        spread[row : row + 32] = block

    def put_three(row, block):
        spread[row : row + 64] = block

    spread_two(two_ref, turned, put_two)
    for b in range(2):
        for j in range(2):
            for side in range(2):
                source = (2 * j + b) * 256 + side * 128
                target = (b * 2 + j) * 256 + side * 128
                v_two[target : target + 128] = pair(jnp.transpose(spread[source : source + 128]))
    spread_three(three_ref, turned, put_three)
    for part in range(6):
        rows = pl.ds(part * 128, 128)
        v_three[rows] = pair(jnp.transpose(spread[rows]))
    total_one[...] = jnp.zeros(total_one.shape, F32)
    total_two[...] = jnp.zeros(total_two.shape, F32)
    total_three[...] = jnp.zeros(total_three.shape, F32)
    bias_out[...] = jnp.zeros(bias_out.shape, F32)
    h_one[...] = jnp.zeros(h_one.shape, BF16)
    pad_two[...] = jnp.zeros(pad_two.shape, BF16)
    pad_three[...] = jnp.zeros(pad_three.shape, BF16)

    def fold(rows):
        return jnp.sum(rows.reshape(-1, 8, 128), axis=0)

    def one_group(group, carry):
        slot = lax.rem(group, 2)

        @pl.when(group + 1 < groups)
        def ahead():
            for load in loads(group + 1, 1 - slot):
                load.start()

        for load in loads(group, slot):
            load.wait()
        rows = d_three[slot].reshape(28 * GROUP, 128)
        bias_out[2] += fold(rows)
        both = pair(rows)
        pad_three[0, 2:9, 1:5] = both[:, :128].reshape(7, 4, GROUP, 128)
        pad_three[1, 2:9, 1:5] = both[:, 128:].reshape(7, 4, GROUP, 128)
        h, slope_two = gelu_both(z_two[slot])
        high, low = two_parts(h)
        h_two[0] = high
        h_two[1] = low
        edge = jnp.where(last_masks(), h[:, 4].reshape(9 * GROUP, 128), 0.0)
        high, low = two_parts(edge)
        h_two[0, :, 4] = high.reshape(9, GROUP, 128)
        h_two[1, :, 4] = low.reshape(9, GROUP, 128)
        for part in range(2):
            pieces = []
            for ky in range(3):
                pieces.append(h_two[part, ky : ky + 7, 0:4].reshape(28 * GROUP, 128))
                pieces.append(h_two[part, ky : ky + 7, 1:5].reshape(28 * GROUP, 128))
            total_three[...] += dot_rows(both, jnp.concatenate(pieces, axis=1))
        spill = jnp.zeros((45 * GROUP, 128), F32)
        for part in range(2):
            pieces = []
            for ky in range(3):
                pieces.append(pad_three[part, 2 - ky : 11 - ky, 1:6].reshape(45 * GROUP, 128))
                pieces.append(pad_three[part, 2 - ky : 11 - ky, 0:5].reshape(45 * GROUP, 128))
            spill = spill + fold_pair(dot(jnp.concatenate(pieces, axis=1), v_three[...]))
        rows = spill * slope_two.reshape(45 * GROUP, 128)
        bias_out[1] += fold(rows)
        both = pair(rows)
        pad_two[0, 1:10, 1:6] = both[:, :128].reshape(9, 5, GROUP, 128)
        pad_two[1, 1:10, 1:6] = both[:, 128:].reshape(9, 5, GROUP, 128)
        for q in range(5):
            h, slope = gelu_both(z_one[slot, :, :, q])
            high, low = two_parts(h)
            h_one[0, :, :, q] = high
            h_one[1, :, :, q] = low
            slope_one[:, :, q] = slope
        for part in range(2):
            pieces = []
            for j in range(2):
                for b in range(2):
                    pieces.append(h_one[part, j : j + 9, b, 0:5].reshape(45 * GROUP, 128))
                    pieces.append(h_one[part, j : j + 9, b, 1:6].reshape(45 * GROUP, 128))
            total_two[...] += dot_rows(both, jnp.concatenate(pieces, axis=1))
        for b in range(2):
            spill = jnp.zeros((50 * GROUP, 128), F32)
            for part in range(2):
                pieces = []
                for j in range(2):
                    pieces.append(pad_two[part, 1 - j : 11 - j, 1:6].reshape(50 * GROUP, 128))
                    pieces.append(pad_two[part, 1 - j : 11 - j, 0:5].reshape(50 * GROUP, 128))
                spill = spill + fold_pair(
                    dot(jnp.concatenate(pieces, axis=1), v_two[b * 512 : (b + 1) * 512])
                )
            rows = spill * slope_one[:, b].reshape(50 * GROUP, 128)
            bias_out[0] += fold(rows)
            d_one[:, b] = pair(rows).reshape(10, 5, GROUP, 256)
        for q in range(5):
            pieces = [
                picked[slot, j : j + 20, b, :, q * 128 : (q + 1) * 128].reshape(20 * GROUP, 128)
                for j in range(2)
                for b in range(4)
            ]
            total_one[...] += dot_rows(
                d_one[:, :, q].reshape(20 * GROUP, 256), jnp.concatenate(pieces, axis=1)
            )
        return carry

    lax.fori_loop(0, groups, one_group, 0)
    gather_one(total_one, one_out)
    gather_two(total_two, turned, two_out)
    gather_three(total_three, turned, three_out)
    sums = [jnp.sum(bias_out[k], axis=0, keepdims=True) for k in range(3)]
    sums[0] = sums[0] + pltpu.roll(sums[0], 64, 1)
    sums[0] = sums[0] + pltpu.roll(sums[0], 32, 1)
    sums[1] = sums[1] + pltpu.roll(sums[1], 64, 1)
    sums[2] = sums[2] + pltpu.roll(sums[2], 64, 1)
    for k in range(3):
        bias_out[k] = jnp.broadcast_to(sums[k], (8, 128))


def conv_backward(lengths, picked, z_one, z_two, d_three, two, three):
    any_spec = pl.BlockSpec(memory_space=pl.ANY)
    vmem = pl.BlockSpec(memory_space=pltpu.VMEM)
    return pl.pallas_call(
        conv_backward_kernel,
        in_specs=[pl.BlockSpec(memory_space=pltpu.SMEM)] + [any_spec] * 4 + [vmem] * 2,
        out_specs=[vmem] * 4,
        out_shape=[
            jax.ShapeDtypeStruct((32, 256), F32),
            jax.ShapeDtypeStruct((64, 512), F32),
            jax.ShapeDtypeStruct((64, 576), F32),
            jax.ShapeDtypeStruct((3, 8, 128), F32),
        ],
        scratch_shapes=[
            pltpu.VMEM((2, 21, 4, GROUP, 640), BF16),
            pltpu.VMEM((2, 10, 2, 5, GROUP, 128), F32),
            pltpu.VMEM((2, 9, 5, GROUP, 128), F32),
            pltpu.VMEM((2, 28, GROUP, 128), F32),
            pltpu.VMEM((2, 10, 2, 6, GROUP, 128), BF16),
            pltpu.VMEM((2, 9, 5, GROUP, 128), BF16),
            pltpu.VMEM((10, 2, 5, GROUP, 128), F32),
            pltpu.VMEM((2, 11, 6, GROUP, 128), BF16),
            pltpu.VMEM((2, 11, 6, GROUP, 128), BF16),
            pltpu.VMEM((10, 2, 5, GROUP, 256), BF16),
            pltpu.VMEM((1024, 256), BF16),
            pltpu.VMEM((768, 256), BF16),
            pltpu.VMEM((1024, 128), F32),
            pltpu.VMEM((576, 128), F32),
            pltpu.VMEM((256, 1024), F32),
            pltpu.VMEM((256, 1024), F32),
            pltpu.VMEM((256, 768), F32),
            pltpu.SemaphoreType.DMA((2, 4)),
        ],
        compiler_params=pltpu.CompilerParams(vmem_limit_bytes=48 * 1024 * 1024),
        name="conv_backward",
    )(lengths, picked, z_one, z_two, d_three, two, three)


HIGH = lax.Precision.HIGH
VECTORS_ROW = 3745
TIME_ROW = 3780


def mm(a, b):
    return lax.dot_general(
        a, b, (((1,), (0,)), ((), ())), precision=HIGH, preferred_element_type=F32
    )


def mm_nt(a, b):
    return lax.dot_general(
        a, b, (((1,), (1,)), ((), ())), precision=HIGH, preferred_element_type=F32
    )


def mm_tn(a, b):
    return lax.dot_general(
        a, b, (((0,), (0,)), ((), ())), precision=HIGH, preferred_element_type=F32
    )


def dot_nt(a, b):
    return lax.dot_general(a, b, (((1,), (1,)), ((), ())), preferred_element_type=F32)


def norm_parts(stream):
    centered = stream - jnp.mean(stream, -1, keepdims=True)
    spread = jnp.mean(centered * centered, -1, keepdims=True)
    scale = lax.rsqrt(spread + 1e-05)
    return centered * scale, scale


def norm_back(grad, unit, scale, gain):
    grad = grad * gain
    inner = jnp.mean(grad * unit, -1, keepdims=True)
    return scale * (grad - jnp.mean(grad, -1, keepdims=True) - unit * inner)


def column_sum(x):
    return jnp.sum(x, axis=0, keepdims=True)


def unpack_split(split_ref, qkv, output, up, up_bias, down):
    lane = lax.broadcasted_iota(jnp.int32, (32, 128), 1)
    for layer in range(LAYERS):
        base = layer * 385
        kinds = [[jnp.zeros((32, 128), F32) for j in range(4)] for kind in range(3)]
        for m in range(4):
            rows = [split_ref[m, pl.ds(base + k, 32, stride=3), :] for k in range(3)]
            inside = (lane >= 32 * m) & (lane < 32 * m + 32)
            for j in range(4):
                for kind in range(3):
                    spot = j * 96 + kind * 32
                    source = rows[spot // 128]
                    shift = (32 * m - spot % 128) % 128
                    moved = pltpu.roll(source, shift, 1) if shift else source
                    kinds[kind][j] = jnp.where(inside, moved, kinds[kind][j])
            output[layer, 32 * m : 32 * m + 32] = split_ref[m, base + 96 : base + 128]
            up[layer, :, 128 * m : 128 * m + 128] = split_ref[m, base + 128 : base + 256]
            up_bias[layer, :, 128 * m : 128 * m + 128] = split_ref[m, base + 256 : base + 257]
            down[layer, 128 * m : 128 * m + 128] = split_ref[m, base + 257 : base + 385]
        for kind in range(3):
            for j in range(4):
                qkv[layer, kind, pl.ds(j, 32, stride=4), :] = kinds[kind][j]


def pack_split(out_ref, qkv, output, up, up_bias, down):
    lane = lax.broadcasted_iota(jnp.int32, (32, 128), 1)
    for layer in range(LAYERS):
        base = layer * 385
        parts = [[qkv[layer, kind, pl.ds(j, 32, stride=4), :] for j in range(4)] for kind in range(3)]
        for m in range(4):
            rows = [jnp.zeros((32, 128), F32) for k in range(3)]
            for j in range(4):
                for kind in range(3):
                    spot = j * 96 + kind * 32
                    low = spot % 128
                    shift = (low - 32 * m) % 128
                    moved = pltpu.roll(parts[kind][j], shift, 1) if shift else parts[kind][j]
                    inside = (lane >= low) & (lane < low + 32)
                    rows[spot // 128] = jnp.where(inside, moved, rows[spot // 128])
            for k in range(3):
                out_ref[m, pl.ds(base + k, 32, stride=3), :] = rows[k]
            out_ref[m, base + 96 : base + 128] = output[layer, 32 * m : 32 * m + 32]
            out_ref[m, base + 128 : base + 256] = up[layer, :, 128 * m : 128 * m + 128]
            out_ref[m, base + 256 : base + 257] = up_bias[layer, :, 128 * m : 128 * m + 128]
            out_ref[m, base + 257 : base + 385] = down[layer, 128 * m : 128 * m + 128]
    for m in range(4):
        out_ref[m, 770:784] = jnp.zeros((14, 128), F32)


def former_body(
    slots,
    used,
    lengths_ref,
    returns_ref,
    actions_ref,
    head_ref,
    z_ref,
    small,
    times_all,
    encoder,
    weights,
    d_three_ref,
    d_encoder_ref,
    d_vectors_ref,
    d_actions_ref,
    d_head_ref,
    d_times_ref,
    loss_ref,
    grads,
    chances,
    kept,
    sums,
    flats,
):
    qkv, output, up, up_bias, down = weights
    d_qkv, d_output, d_up, d_up_bias, d_down = grads
    rows = 3 * slots
    wins, steps = returns_ref.shape
    vec = [small[k : k + 1] for k in range(17)]
    table = small[17 : 17 + ACT]
    slot = lax.broadcasted_iota(jnp.int32, (slots, 1), 0)
    window = jnp.zeros((slots, 1), jnp.int32)
    begin = jnp.zeros((slots, 1), jnp.int32)
    end = jnp.int32(0)
    for w in range(wins - 1):
        end = end + lengths_ref[w]
        window = jnp.where(slot >= end, w + 1, window)
        begin = jnp.where(slot >= end, end, begin)
    moment = slot - begin
    valid = slot < used
    time_lane = lax.broadcasted_iota(jnp.int32, (slots, steps), 1)
    amount = jnp.zeros((slots, 1), F32)
    action = jnp.zeros((slots, 1), jnp.int32)
    for w in range(wins):
        here = (time_lane == moment) & (window == w)
        amount = amount + jnp.sum(
            jnp.where(here, returns_ref[w : w + 1], 0.0), axis=1, keepdims=True
        )
        action = action + jnp.sum(jnp.where(here, actions_ref[w : w + 1], 0), axis=1, keepdims=True)
    lane = lax.broadcasted_iota(jnp.int32, (slots, 128), 1)
    picks = jnp.where((lane == action) & valid, 1.0, 0.0)
    reward = jnp.tanh(amount * vec[14] + vec[15])
    table = jnp.concatenate([table, jnp.zeros((128 - ACT, 128), F32)], axis=0)
    move = jnp.tanh(mm(picks, table))
    sum_state = jnp.zeros((slots, 128), F32)
    for k in range(28):
        z = jnp.where(valid, z_ref[k, 0:slots], 0.0)
        high, low = two_parts(gelu_value(z))
        flats[0, 0:slots, k * 128 : (k + 1) * 128] = high
        flats[1, 0:slots, k * 128 : (k + 1) * 128] = low
    for part in range(2):
        sum_state = sum_state + fold_pair(dot(flats[part, 0:slots], encoder[...]))
    state = jnp.tanh(sum_state + vec[16])
    times = times_all[0:slots]
    stream = jnp.concatenate([reward + times, state + times, move + times], axis=0)

    def ids(axis):
        shape = (rows, 1) if axis == 0 else (1, rows)
        number = lax.broadcasted_iota(jnp.int32, shape, axis)
        kind = jnp.where(number >= 2 * slots, 2, jnp.where(number >= slots, 1, 0))
        return number - kind * slots, kind

    (slot_q, kind_q), (slot_k, kind_k) = ids(0), ids(1)

    def begin_of(slot_ids):
        found = jnp.zeros(slot_ids.shape, jnp.int32)
        end = jnp.int32(0)
        for w in range(wins - 1):
            end = end + lengths_ref[w]
            found = jnp.where(slot_ids >= end, end, found)
        return found

    order_q = slot_q * 3 + kind_q
    order_k = slot_k * 3 + kind_k
    allowed = (order_q >= order_k) & (slot_k >= begin_of(slot_q)) & (slot_k < used)
    head_of = lax.shift_right_logical(lax.broadcasted_iota(jnp.int32, (1, 128), 1), 4)
    heads = D // HD
    batch = 4 if slots <= HALF else 2

    def masked(x, masks):
        return jnp.concatenate([jnp.where(mask, x, jnp.zeros_like(x)) for mask in masks], axis=0)

    def unmasked(x, masks):
        held = jnp.where(masks[0], x[0:rows], 0.0)
        for k in range(1, batch):
            held = held + jnp.where(masks[k], x[k * rows : (k + 1) * rows], 0.0)
        return held

    tape = []
    for layer in range(LAYERS):
        gains = vec[6 * layer : 6 * layer + 6]
        unit_one, scale_one = norm_parts(stream)
        normed = unit_one * gains[0] + gains[1]
        wide = jnp.concatenate([qkv[layer, k] for k in range(3)], axis=1)
        mixed = mm(normed, wide)
        query_high, query_low = two_parts(mixed[:, :128] * 0.25)
        keys, values = pair(mixed[:, 128:256]), pair(mixed[:, 256:])
        kept[layer, 0, 0:rows] = query_high
        kept[layer, 1, 0:rows] = query_low
        for k in range(2):
            kept[layer, 2 + k, 0:rows] = keys[:, k * 128 : (k + 1) * 128]
            kept[layer, 4 + k, 0:rows] = values[:, k * 128 : (k + 1) * 128]
        sums[0, 0:rows] = jnp.zeros((rows, 128), F32)

        def attend(turn, carry, layer=layer):
            masks = [head_of == turn * batch + k for k in range(batch)]
            parts = [masked(kept[layer, k, 0:rows], masks) for k in range(2)]
            keys = [kept[layer, 2 + k, 0:rows] for k in range(2)]
            values = [kept[layer, 4 + k, 0:rows] for k in range(2)]
            scores = dot_nt(
                jnp.concatenate([parts[0], parts[0]], axis=1), jnp.concatenate(keys, axis=1)
            )
            scores = (scores + dot_nt(parts[1], keys[0])).reshape(batch, rows, rows)
            scores = jnp.where(allowed[None], scores, -1e30)
            peak = jnp.max(scores, -1, keepdims=True)
            chance = jnp.exp(scores - peak)
            chance = chance / jnp.sum(chance, -1, keepdims=True)
            high, low = two_parts(chance.reshape(batch * rows, rows))
            spot = pl.ds(pl.multiple_of(turn * (batch * rows), 64), batch * rows)
            chances[layer, 0, spot, 0:rows] = high
            chances[layer, 1, spot, 0:rows] = low
            seen = fold_pair(dot(high, jnp.concatenate(values, axis=1))) + dot(low, values[0])
            sums[0, 0:rows] += unmasked(seen, masks)
            return carry

        lax.fori_loop(0, heads // batch, attend, 0)
        context = sums[0, 0:rows]
        stream = stream + mm(context, output[layer]) + gains[4]
        unit_two, scale_two = norm_parts(stream)
        normed_two = unit_two * gains[2] + gains[3]
        inner, slope = gelu_both(mm(normed_two, up[layer]) + up_bias[layer])
        stream = stream + mm(inner, down[layer]) + gains[5]
        tape.append((unit_one, scale_one, unit_two, scale_two, inner, slope, context))
    end_stream = stream[slots : 2 * slots]
    unit, scale = norm_parts(end_stream)
    final = unit * vec[12] + vec[13]
    logits = jnp.where(lane < ACT, mm(final, head_ref[...]), -1e30)
    peak = jnp.max(logits, -1, keepdims=True)
    powers = jnp.exp(logits - peak)
    total = jnp.sum(powers, -1, keepdims=True)
    chosen = jnp.sum(jnp.where(lane == action, logits, 0.0), -1, keepdims=True)
    terms = jnp.where(valid, jnp.log(total) + peak - chosen, 0.0)
    loss_ref[...] = jnp.broadcast_to(jnp.sum(terms, axis=0, keepdims=True), (8, 128))
    d_logits = jnp.where(valid, powers / total, 0.0) - picks
    d_head_ref[...] = mm_tn(final, d_logits)
    d_final = mm_nt(d_logits, head_ref[...])
    d_vec = [None] * 17
    d_vec[12] = column_sum(d_final * unit)
    d_vec[13] = column_sum(d_final)
    d_end = norm_back(d_final, unit, scale, vec[12])
    blank = jnp.zeros((slots, 128), F32)
    d_stream = jnp.concatenate([blank, d_end, blank], axis=0)
    for layer in reversed(range(LAYERS)):
        unit_one, scale_one, unit_two, scale_two, inner, slope, context = tape[layer]
        gains = vec[6 * layer : 6 * layer + 6]
        d_vec[6 * layer + 5] = column_sum(d_stream)
        d_down[layer] = mm_tn(inner, d_stream)
        d_inner = mm_nt(d_stream, down[layer]) * slope
        d_up_bias[layer] = column_sum(d_inner)
        normed_two = unit_two * gains[2] + gains[3]
        d_up[layer] = mm_tn(normed_two, d_inner)
        d_normed = mm_nt(d_inner, up[layer])
        d_vec[6 * layer + 2] = column_sum(d_normed * unit_two)
        d_vec[6 * layer + 3] = column_sum(d_normed)
        d_stream = d_stream + norm_back(d_normed, unit_two, scale_two, gains[2])
        d_vec[6 * layer + 4] = column_sum(d_stream)
        d_output[layer] = mm_tn(context, d_stream)
        d_context = mm_nt(d_stream, output[layer])
        bases = d_context * context
        high, low = two_parts(d_context)
        for k in range(3):
            sums[k, 0:rows] = jnp.zeros((rows, 128), F32)
        kept[layer, 6, 0:rows] = high
        kept[layer, 7, 0:rows] = low
        sums[3, 0:rows] = bases

        def attend_back(turn, carry, layer=layer):
            masks = [head_of == turn * batch + k for k in range(batch)]
            query = [masked(kept[layer, k, 0:rows], masks) for k in range(2)]
            keys = [kept[layer, 2 + k, 0:rows] for k in range(2)]
            values = [kept[layer, 4 + k, 0:rows] for k in range(2)]
            d_seen = [masked(kept[layer, 6 + k, 0:rows], masks) for k in range(2)]
            base = jnp.sum(masked(sums[3, 0:rows], masks), -1, keepdims=True)
            spot = pl.ds(pl.multiple_of(turn * (batch * rows), 64), batch * rows)
            chance = [chances[layer, k, spot, 0:rows] for k in range(2)]
            d_chance = dot_nt(
                jnp.concatenate([d_seen[0], d_seen[0]], axis=1), jnp.concatenate(values, axis=1)
            )
            d_chance = d_chance + dot_nt(d_seen[1], values[0])
            d_scores = (chance[0].astype(F32) + chance[1].astype(F32)) * (d_chance - base)
            high, low = two_parts(d_scores)
            d_query = fold_pair(dot(high, jnp.concatenate(keys, axis=1))) + dot(low, keys[0])
            sums[0, 0:rows] += unmasked(d_query, masks)
            d_keys = fold_pair(dot_rows(high, jnp.concatenate(query, axis=1)))
            sums[1, 0:rows] += d_keys + dot_rows(low, query[0])
            d_values = fold_pair(dot_rows(chance[0], jnp.concatenate(d_seen, axis=1)))
            sums[2, 0:rows] += d_values + dot_rows(chance[1], d_seen[0])
            return carry

        lax.fori_loop(0, heads // batch, attend_back, 0)
        normed = unit_one * gains[0] + gains[1]
        d_mixed = jnp.concatenate(
            [sums[0, 0:rows] * 0.25, sums[1, 0:rows], sums[2, 0:rows]], axis=1
        )
        wide = jnp.concatenate([qkv[layer, k] for k in range(3)], axis=1)
        d_wide = mm_tn(normed, d_mixed)
        for k in range(3):
            d_qkv[layer, k] = d_wide[:, k * 128 : (k + 1) * 128]
        d_normed = mm_nt(d_mixed, wide)
        d_vec[6 * layer] = column_sum(d_normed * unit_one)
        d_vec[6 * layer + 1] = column_sum(d_normed)
        d_stream = d_stream + norm_back(d_normed, unit_one, scale_one, gains[0])
    d_reward, d_state, d_move = (d_stream[k * slots : (k + 1) * slots] for k in range(3))
    d_times_ref[0:slots] = jnp.where(valid, d_reward + d_state + d_move, 0.0)
    d_reward = d_reward * (1.0 - reward * reward)
    d_vec[14] = column_sum(d_reward * amount)
    d_vec[15] = column_sum(d_reward)
    d_move = d_move * (1.0 - move * move)
    d_actions_ref[...] = mm_tn(picks, d_move)[0:24]
    d_state = jnp.where(valid, d_state * (1.0 - state * state), 0.0)
    d_vec[16] = column_sum(d_state)
    d_vectors_ref[...] = jnp.concatenate(d_vec + [jnp.zeros((7, 128), F32)], axis=0)
    high, low = two_parts(d_state)
    twice = jnp.concatenate([high, high], axis=1)
    both = jnp.concatenate([high, low], axis=1)
    d_flat = dot_nt(twice, encoder[...]) + dot_nt(low, encoder[:, 0:128])
    d_block = dot_rows(flats[0, 0:slots], both) + dot_rows(flats[1, 0:slots], both)
    d_block = fold_pair(d_block)
    for k in range(28):
        z = jnp.where(valid, z_ref[k, 0:slots], 0.0)
        d_three_ref[k, 0:slots] = d_flat[:, k * 128 : (k + 1) * 128] * gelu_both(z)[1]
        y, v = divmod(k, 4)
        for o in range(2):
            if 2 * v + o < 7:
                d_encoder_ref[pl.ds(y * 7 + 2 * v + o, 64, stride=49), :] = d_block[
                    k * 128 + o * 64 : k * 128 + (o + 1) * 64
                ]


def former_kernel(
    packed,
    lengths_ref,
    starts_ref,
    returns_ref,
    actions_ref,
    head_ref,
    z_ref,
    flat_ref,
    *refs,
):
    if packed:
        split_ref, refs = refs[0], refs[1:]
    else:
        given, refs = refs[:5], refs[5:]
    (d_three_ref, d_vectors_ref, d_actions_ref, d_head_ref) = refs[:4]
    (d_times_ref, loss_ref), refs = refs[4:6], refs[6:]
    if packed:
        parts, refs = refs[:4], refs[4:]
        d_encoder_ref, d_split, part_sem, refs = refs[0], refs[1], refs[2], refs[3:]
        weights, grads, refs = refs[:5], refs[5:10], refs[10:]
    else:
        d_encoder_ref, grads, refs = refs[0], refs[1:6], refs[6:]
        weights = given
    (raw, near, small, rows_raw, times_all, encoder, chances, kept, sums, flats, sem) = refs
    used = jnp.int32(0)
    wins = lengths_ref.shape[0]
    for w in range(wins):
        used = used + lengths_ref[w]
    copies = [
        pltpu.make_async_copy(flat_ref.at[pl.ds(608, 3144)], raw, sem.at[0]),
        pltpu.make_async_copy(flat_ref.at[pl.ds(3744, 48)], rows_raw.at[wins], sem.at[1]),
    ]
    offsets = []
    for w in range(wins):
        row = TIME_ROW + starts_ref[w]
        low = pl.multiple_of(lax.div(row, 8) * 8, 8)
        offsets.append(row - low)
        copies.append(
            pltpu.make_async_copy(
                flat_ref.at[pl.ds(low, 40)], rows_raw.at[w, pl.ds(0, 40)], sem.at[2 + w]
            )
        )
    for copy in copies:
        copy.start()
    if packed:
        unpack_split(split_ref, *weights)
    for copy in copies:
        copy.wait()
    lane = lanes()

    def straight(first, second):
        return jnp.where(lane < 96, pltpu.roll(first, 96, 1), pltpu.roll(second, 96, 1))

    def turn(step, carry):
        spot = pl.multiple_of(step * 64, 64)
        near[pl.ds(spot, 64)] = straight(raw[pl.ds(spot + 1, 64)], raw[pl.ds(spot + 2, 64)])
        return carry

    lax.fori_loop(0, 49, turn, 0)
    for k in range(28):
        y, v = divmod(k, 4)
        halves = []
        for o in range(2):
            if 2 * v + o < 7:
                halves.append(near[pl.ds(y * 7 + 2 * v + o, 64, stride=49), :])
            else:
                halves.append(jnp.zeros((64, 128), F32))
        encoder[k * 128 : (k + 1) * 128] = pair(jnp.concatenate(halves, axis=0))
    small[...] = straight(rows_raw[wins, 1:41], rows_raw[wins, 2:42])
    times_all[...] = jnp.zeros(times_all.shape, F32)
    begin = 0
    row = lax.broadcasted_iota(jnp.int32, (32, 1), 0)
    for w in range(wins):
        rows = straight(
            rows_raw[w, pl.ds(offsets[w], 32)], rows_raw[w, pl.ds(offsets[w] + 1, 32)]
        )
        times_all[pl.ds(begin, 32)] = jnp.where(row < lengths_ref[w], rows, 0.0)
        begin = begin + lengths_ref[w]
    d_times_ref[...] = jnp.zeros(d_times_ref.shape, F32)

    def run(slots):
        former_body(
            slots,
            used,
            lengths_ref,
            returns_ref,
            actions_ref,
            head_ref,
            z_ref,
            small,
            times_all,
            encoder,
            weights,
            d_three_ref,
            d_encoder_ref,
            d_vectors_ref,
            d_actions_ref,
            d_head_ref,
            d_times_ref,
            loss_ref,
            grads,
            chances,
            kept,
            sums,
            flats,
        )

    @pl.when(used <= HALF)
    def few():
        run(HALF)

    @pl.when(used > HALF)
    def many():
        run(ROOM)

    if packed:
        me = lax.axis_index("mp")
        copies = []
        for k in range(4):
            m = jnp.bitwise_xor(me, k)
            quarter = pl.ds(pl.multiple_of(m * 784, 8), 784)
            copies.append((d_encoder_ref.at[quarter], parts[k].at[pl.ds(784, 784)]))
            copies.append((d_split.at[m], parts[k].at[pl.ds(0, 784)]))
        copies = [
            pltpu.make_async_copy(source, target, part_sem.at[number])
            for number, (source, target) in enumerate(copies)
        ]
        for copy in copies[::2]:
            copy.start()
        pack_split(d_split, *grads)
        for copy in copies[1::2]:
            copy.start()
        for copy in copies:
            copy.wait()


def former(lengths, starts, returns, actions, head, z_three, flat, weights, packed):
    smem = pl.BlockSpec(memory_space=pltpu.SMEM)
    vmem = pl.BlockSpec(memory_space=pltpu.VMEM)
    any_spec = pl.BlockSpec(memory_space=pl.ANY)
    wins = lengths.shape[0]
    canonical = [
        (LAYERS, 3, 128, 128),
        (LAYERS, 128, 128),
        (LAYERS, 128, FF),
        (LAYERS, 1, FF),
        (LAYERS, FF, 128),
    ]
    outs = [(28, ROOM, 128), (24, 128), (24, 128), (128, 128), (ROOM, 128), (8, 128)]
    out_specs = [vmem] * len(outs)
    if packed:
        outs += [(1568, 128)] * 4
        out_specs += [any_spec] * 4
        scratch = [pltpu.VMEM((3136, 128), F32), pltpu.VMEM((4, 784, 128), F32)]
        scratch += [pltpu.SemaphoreType.DMA((8,))]
        scratch += [pltpu.VMEM(shape, F32) for shape in canonical] * 2
    else:
        outs += [(3136, 128)] + canonical
        out_specs += [vmem] * 6
        scratch = []
    rows = 3 * ROOM
    scratch += [
        pltpu.VMEM((3144, 128), F32),
        pltpu.VMEM((3136, 128), F32),
        pltpu.VMEM((40, 128), F32),
        pltpu.VMEM((wins + 1, 48, 128), F32),
        pltpu.VMEM((ROOM + 32, 128), F32),
        pltpu.VMEM((3584, 256), BF16),
        pltpu.VMEM((LAYERS, 2, 8 * rows, rows), BF16),
        pltpu.VMEM((LAYERS, 8, rows, 128), BF16),
        pltpu.VMEM((4, rows, 128), F32),
        pltpu.VMEM((2, ROOM, 3584), BF16),
        pltpu.SemaphoreType.DMA((wins + 2,)),
    ]
    return pl.pallas_call(
        partial(former_kernel, packed),
        in_specs=[smem, smem] + [vmem] * 4 + [any_spec] + [vmem] * len(weights),
        out_specs=out_specs,
        out_shape=[jax.ShapeDtypeStruct(shape, F32) for shape in outs],
        scratch_shapes=scratch,
        compiler_params=pltpu.CompilerParams(vmem_limit_bytes=60 * 1024 * 1024),
        name="transformer_step",
    )(lengths, starts, returns, actions, head, z_three, flat, *weights)


CONV_ROWS = 616
SMALL = [("conv", CONV_ROWS), ("vectors", 24), ("action_table", 24), ("head", 24), ("loss", 8)]
FIELD_ROWS = 8208
TABLE_AT = CONV_ROWS + 3136 + 17 + ACT


def round_up(number, grain):
    return -(-number // grain) * grain


def chunk_of(rows):
    return max(size for size in range(8, 65, 8) if rows % size == 0)


def mesh_bits(dp_size, mp_size):
    dp_bits = [("dp", k) for k in range(dp_size.bit_length() - 1)]
    mp_bits = [("mp", k) for k in range(mp_size.bit_length() - 1)]
    middle = len(dp_bits) // 3
    return mp_bits[:1], mp_bits[1:], dp_bits[:middle], dp_bits[middle:]


def reduce_kernel(plan, lengths_ref, starts_ref, times_ref, *refs):
    mp_size, span, quarter = plan["mp_size"], plan["span"], plan["quarter"]
    parts, refs = refs[:mp_size], refs[mp_size:]
    smalls, refs = refs[: len(SMALL)], refs[len(SMALL) :]
    (field_out, split_out, square_out, length_out, loss_out), refs = refs[:5], refs[5:]
    (stage, work, landing, split_total, own_total, small_total, time_total), refs = (
        refs[:7],
        refs[7:],
    )
    (field, meta, meta_in, tiles, tile_in), refs = refs[:5], refs[5:]
    load_sem, send_sem, recv_sem, store_sem = refs
    spots = {"dp": lax.axis_index("dp"), "mp": lax.axis_index("mp")}
    cores, ys, xs, zs = plan["bits"]
    bits = cores + ys + xs + zs
    dp_first = xs + zs
    dp_second = zs[:1] + xs + zs[1:]
    wins = lengths_ref.shape[0]
    slots = iter(range(plan["copies"]))

    def value(bit):
        return lax.rem(lax.div(spots[bit[0]], 1 << bit[1]), 2)

    def partner(bit):
        axis, k = bit
        place = dict(spots)
        place[axis] = spots[axis] + (1 - 2 * value(bit)) * (1 << k)
        return (place["dp"], place["mp"])

    def send(source, target, bit):
        slot = next(slots)
        copy = pltpu.make_async_remote_copy(
            src_ref=source,
            dst_ref=target,
            send_sem=send_sem.at[slot],
            recv_sem=recv_sem.at[slot],
            device_id=partner(bit),
            device_id_type=pl.DeviceIdType.MESH,
        )
        copy.start()
        return copy

    loads = []
    for k in range(mp_size):
        loads.append(pltpu.make_async_copy(parts[k], stage.at[k], load_sem.at[k]))
    small_at, place = {}, 0
    for number, (name, rows) in enumerate(SMALL):
        small_at[name] = place
        target = work.at[pl.ds(plan["small"] + place, rows)]
        loads.append(pltpu.make_async_copy(smalls[number], target, load_sem.at[mp_size + number]))
        place += rows
    for load in loads:
        load.start()

    def wipe(target, start, rows):
        if rows > 0:
            target[start : start + rows] = jnp.zeros((rows, 128), F32)

    wipe(work, plan["small"] + place, plan["small_rows"] - place)
    wipe(work, plan["split"] + span, plan["split_rows"] - span)
    wipe(work, plan["own"] + quarter, plan["own_rows"] - quarter)
    barrier = pltpu.get_barrier_semaphore()
    for bit in bits:
        pl.semaphore_signal(
            barrier, inc=1, device_id=partner(bit), device_id_type=pl.DeviceIdType.MESH
        )
    pl.semaphore_wait(barrier, len(bits))

    tile_place = lax.broadcasted_iota(jnp.int32, (8, 128), 0) * 128
    tile_place = tile_place + lax.broadcasted_iota(jnp.int32, (8, 128), 1)
    me = spots["dp"] * mp_size + spots["mp"]
    for number, ref in enumerate((lengths_ref, starts_ref)):
        tile = jnp.zeros((8, 128), F32)
        for w in range(wins):
            amount = ref[w].astype(F32)
            tile = tile + jnp.where(tile_place == me * wins + w, amount, 0.0)
        meta[0, number * 8 : number * 8 + 8] = tile
    meta_flight = send(meta.at[0], meta_in.at[0], bits[0])

    def add_into(target, start, pieces, rows):
        chunk = chunk_of(rows)

        def body(turn, carry):
            spot = pl.multiple_of(start + turn * chunk, 8)
            held = target[pl.ds(spot, chunk)]
            for source, at in pieces:
                held = held + source[pl.ds(pl.multiple_of(at + turn * chunk, 8), chunk)]
            target[pl.ds(spot, chunk)] = held
            return carry

        lax.fori_loop(0, rows // chunk, body, 0)

    def copy_rows(target, start, source, at, rows):
        chunk = chunk_of(rows)

        def body(turn, carry):
            held = source[pl.ds(pl.multiple_of(at + turn * chunk, 8), chunk)]
            target[pl.ds(pl.multiple_of(start + turn * chunk, 8), chunk)] = held
            return carry

        lax.fori_loop(0, rows // chunk, body, 0)

    for load in loads:
        load.wait()
    for target, at, rows in [(plan["split"], 0, span), (plan["own"], span, quarter)]:
        copy_rows(work, target, stage.at[0], at, rows)
        add_into(work, target, [(stage.at[k], at) for k in range(1, mp_size)], rows)

    class Stream:
        def __init__(self, base, rows, order, total, total_at):
            self.base, self.size, self.order = base, rows, order
            self.total, self.at = total, total_at
            self.land = base
            self.flight = None
            self.step = 0
            self.start = base

        def halve(self):
            if self.flight is not None:
                copy, half, land, keep = self.flight
                copy.wait()
                add_into(work, keep, [(landing, land)], half)
                self.base, self.size, self.flight = keep, half, None
            if self.step < len(self.order):
                bit = self.order[self.step]
                half = self.size // 2
                mine = value(bit)
                keep = self.base + mine * half
                give = pl.multiple_of(self.base + (1 - mine) * half, 8)
                copy = send(
                    work.at[pl.ds(give, half)], landing.at[pl.ds(self.land, half)], bit
                )
                self.flight = (copy, half, self.land, keep)
                self.land += half
                self.step += 1

        def turn(self):
            self.at = self.at + (self.base - self.start)
            copy_rows(self.total, self.at, work, self.base, self.size)
            self.step = 0

        def double(self):
            if self.flight is not None:
                copy, low = self.flight
                copy.wait()
                self.at, self.size, self.flight = low, self.size * 2, None
            if self.step < len(self.order):
                bit = self.order[len(self.order) - 1 - self.step]
                region = self.total.at[pl.ds(pl.multiple_of(self.at, 8), self.size)]
                copy = send(region, region, bit)
                self.flight = (copy, self.at - value(bit) * self.size)
                self.step += 1

        def squares(self, limit):
            held = work[pl.ds(pl.multiple_of(self.base, 8), self.size)]
            if limit is not None:
                row = lax.broadcasted_iota(jnp.int32, (self.size, 1), 0)
                held = jnp.where(row + (self.base - self.start) < limit, held, 0.0)
            return jnp.sum((held * held).reshape(self.size // 8, 8, 128), axis=0)

    first, second = plan["cut"]
    own_one = Stream(plan["own"], first, dp_first, own_total, 0)
    own_two = Stream(plan["own"] + first, plan["own_rows"] - first, dp_second, own_total, first)
    split_one = Stream(plan["split"], second, dp_first, split_total, 0)
    split_two = Stream(
        plan["split"] + second, plan["split_rows"] - second, dp_second, split_total, second
    )
    small = Stream(plan["small"], plan["small_rows"], bits, small_total, 0)
    times = Stream(plan["times"], plan["time_rows"], bits, time_total, 0)
    large = [own_one, own_two, split_one, split_two]
    for stream in large + [small]:
        stream.halve()
    for step in range(1, len(bits) + 1):
        meta_flight.wait()
        meta[step] = meta[step - 1] + meta_in[step - 1]
        if step < len(bits):
            meta_flight = send(meta.at[step], meta_in.at[step], bits[step])
    lengths = meta[len(bits), 0:8]
    starts = meta[len(bits), 8:16]
    length_out[...] = lengths
    rows = plan["time_rows"]
    before = jnp.sum(jnp.where(tile_place < me * wins, lengths, 0.0), axis=0, keepdims=True)
    before = jnp.sum(before, axis=1, keepdims=True)
    mine = jnp.sum(
        jnp.where(
            (tile_place >= me * wins) & (tile_place < (me + 1) * wins), lengths, 0.0
        ),
        axis=0,
        keepdims=True,
    )
    mine = jnp.sum(mine, axis=1, keepdims=True)
    row = lax.broadcasted_iota(jnp.int32, (rows, 128), 0).astype(F32)
    lane = lax.broadcasted_iota(jnp.int32, (rows, 128), 1).astype(F32)
    picks = jnp.where((row == lane + before) & (lane < mine), 1.0, 0.0)
    placed = lax.dot_general(
        picks,
        times_ref[...],
        (((1,), (0,)), ((), ())),
        precision=lax.Precision.HIGHEST,
        preferred_element_type=F32,
    )
    work[plan["times"] : plan["times"] + rows] = placed
    times.halve()
    for step in range(len(dp_first)):
        for stream in large + [small, times]:
            stream.halve()
    squares = jnp.zeros((8, 128), F32)
    for stream in large:
        squares = squares + stream.squares(None)
        stream.turn()
        stream.double()
    for step in range(len(dp_first), len(bits)):
        for stream in large:
            stream.double()
        small.halve()
        times.halve()
    squares = squares + small.squares(small_at["loss"])
    for stream in (small, times):
        stream.turn()
        stream.double()
    tiles[0] = squares
    tile_flight = send(tiles.at[0], tile_in.at[0], bits[0])

    def move_tile(step):
        tile_flight.wait()
        tiles[step] = tiles[step - 1] + tile_in[step - 1]
        if step < len(bits):
            return send(tiles.at[step], tile_in.at[step], bits[step])
        return None

    rounds = 1
    while large[0].flight is not None or large[0].step < len(dp_first):
        for stream in large:
            stream.double()
        if rounds < len(bits) + 1:
            tile_flight = move_tile(rounds)
            rounds += 1
        small.double()
        times.double()
    gather_bits = ys + cores
    own_place = CONV_ROWS + spots["mp"] * quarter
    copy_rows(field, own_place, own_total, 0, quarter)
    flights = {}

    def pass_on(offset, reach):
        for number in range(reach, len(gather_bits)):
            bit = gather_bits[number]
            index = spots["mp"]
            for other in gather_bits:
                if offset & (1 << other[1]):
                    index = index + (1 - 2 * value(other)) * (1 << other[1])
            region = field.at[pl.ds(pl.multiple_of(CONV_ROWS + index * quarter, 8), quarter)]
            flights[(offset, number)] = send(region, region, bit)

    pass_on(0, 0)
    while rounds < len(bits) + 1:
        tile_flight = move_tile(rounds)
        rounds += 1
        small.double()
        times.double()
    while small.flight is not None:
        small.double()
        times.double()
    square_out[0:8] = tiles[len(bits)]
    for name, at, count in [
        ("conv", 0, CONV_ROWS),
        ("vectors", CONV_ROWS + 3136, 17),
        ("action_table", CONV_ROWS + 3153, ACT),
        ("head", TABLE_AT + TSTEPS, ACT),
    ]:
        held = small_total[small_at[name] : small_at[name] + count]
        field[at : at + count] = held
    loss_out[...] = small_total[small_at["loss"] : small_at["loss"] + 8]
    end = TABLE_AT + TSTEPS + ACT
    field[end:FIELD_ROWS] = jnp.zeros((FIELD_ROWS - end, 128), F32)
    windows = plan["windows"]
    window = lax.broadcasted_iota(jnp.int32, (windows, 1), 0)
    lane = lax.broadcasted_iota(jnp.int32, (1, 128), 1)
    begin = jnp.zeros((windows, 1), F32)
    length = jnp.zeros((windows, 1), F32)
    start = jnp.zeros((windows, 1), F32)
    for k in range(-(-windows // 128)):
        here = lane + 128 * k
        begin = begin + jnp.sum(
            jnp.where(here < window, lengths[k : k + 1], 0.0), axis=1, keepdims=True
        )
        own = here == window
        length = length + jnp.sum(jnp.where(own, lengths[k : k + 1], 0.0), axis=1, keepdims=True)
        start = start + jnp.sum(jnp.where(own, starts[k : k + 1], 0.0), axis=1, keepdims=True)
    held = pair(time_total[...])
    table_of = []
    for k in range(rows // 128):
        place = lax.broadcasted_iota(jnp.int32, (windows, 128), 1).astype(F32) + 128.0 * k
        away = place - begin
        inside = (away >= 0.0) & (away < length)
        table_of.append(
            jnp.sum(jnp.where(inside, start + away, 0.0), axis=0, keepdims=True)
            + jnp.where(jnp.sum(jnp.where(inside, 1.0, 0.0), axis=0, keepdims=True) > 0, 0.0, -1.0)
        )
    chunk = 512
    time_squares = jnp.zeros((8, 128), F32)
    for turn in range(TSTEPS // chunk):
        place = (lax.broadcasted_iota(jnp.int32, (chunk, 128), 0) + turn * chunk).astype(F32)
        picks = [jnp.where(place == spot, 1.0, 0.0).astype(BF16) for spot in table_of]
        result = fold_pair(dot(jnp.concatenate(picks, axis=1), held))
        field[TABLE_AT + turn * chunk : TABLE_AT + (turn + 1) * chunk] = result
        time_squares = time_squares + jnp.sum(
            (result * result).reshape(chunk // 8, 8, 128), axis=0
        )
    square_out[8:16] = time_squares
    late = CONV_ROWS + 3136
    stores = [
        (field.at[pl.ds(0, CONV_ROWS)], field_out.at[pl.ds(0, CONV_ROWS)]),
        (field.at[pl.ds(late, FIELD_ROWS - late)], field_out.at[pl.ds(late, FIELD_ROWS - late)]),
        (split_total.at[pl.ds(0, span)], split_out),
    ]
    stores = [
        pltpu.make_async_copy(source, target, store_sem.at[number])
        for number, (source, target) in enumerate(stores)
    ]
    for store in stores:
        store.start()
    held_offsets = [0]
    for number, bit in enumerate(gather_bits):
        arrived = []
        for offset in held_offsets:
            flights[(offset, number)].wait()
            arrived.append(offset | (1 << bit[1]))
        held_offsets += arrived
        for offset in arrived:
            pass_on(offset, number + 1)
    last = pltpu.make_async_copy(
        field.at[pl.ds(CONV_ROWS, 3136)], field_out.at[pl.ds(CONV_ROWS, 3136)], store_sem.at[3]
    )
    last.start()
    for store in stores + [last]:
        store.wait()


def reduce_all(lengths, starts, times, parts, smalls, dp_size, mp_size, span, windows):
    bits = mesh_bits(dp_size, mp_size)
    steps = sum(len(part) for part in bits)
    dp_steps = dp_size.bit_length() - 1
    quarter = 3136 // mp_size
    dp_grain = 8 * dp_size
    grain = 8 * dp_size * mp_size
    own_rows = round_up(quarter, dp_grain)
    split_rows = round_up(span, dp_grain)
    small_rows = round_up(sum(rows for name, rows in SMALL), grain)
    time_rows = round_up(FAST_ROWS, grain)
    places, at = {}, 0
    for name, rows in [
        ("split", split_rows),
        ("own", own_rows),
        ("small", small_rows),
        ("times", time_rows),
    ]:
        places[name] = at
        at += rows
    cut = (round_up(own_rows // 2, dp_grain), round_up(split_rows // 2, dp_grain))
    copies = 4 * 2 * dp_steps + 2 * 2 * steps + 2 * steps + mp_size - 1
    plan = dict(
        places,
        mp_size=mp_size,
        span=span,
        quarter=quarter,
        bits=bits,
        copies=copies,
        split_rows=split_rows,
        own_rows=own_rows,
        small_rows=small_rows,
        time_rows=time_rows,
        cut=cut,
        windows=windows,
    )
    smem = pl.BlockSpec(memory_space=pltpu.SMEM)
    vmem = pl.BlockSpec(memory_space=pltpu.VMEM)
    any_spec = pl.BlockSpec(memory_space=pl.ANY)
    inputs = len(parts) + len(smalls)
    return pl.pallas_call(
        partial(reduce_kernel, plan),
        in_specs=[smem, smem, vmem] + [any_spec] * inputs,
        out_specs=[any_spec, any_spec, vmem, vmem, vmem],
        out_shape=[
            jax.ShapeDtypeStruct((FIELD_ROWS, 128), F32),
            jax.ShapeDtypeStruct((span, 128), F32),
            jax.ShapeDtypeStruct((16, 128), F32),
            jax.ShapeDtypeStruct((8, 128), F32),
            jax.ShapeDtypeStruct((8, 128), F32),
        ],
        scratch_shapes=[
            pltpu.VMEM((mp_size, span + quarter, 128), F32),
            pltpu.VMEM((at, 128), F32),
            pltpu.VMEM((at, 128), F32),
            pltpu.VMEM((split_rows, 128), F32),
            pltpu.VMEM((own_rows, 128), F32),
            pltpu.VMEM((small_rows, 128), F32),
            pltpu.VMEM((time_rows, 128), F32),
            pltpu.VMEM((FIELD_ROWS, 128), F32),
            pltpu.VMEM((steps + 1, 16, 128), F32),
            pltpu.VMEM((steps, 16, 128), F32),
            pltpu.VMEM((steps + 1, 8, 128), F32),
            pltpu.VMEM((steps, 8, 128), F32),
            pltpu.SemaphoreType.DMA((inputs,)),
            pltpu.SemaphoreType.DMA((copies,)),
            pltpu.SemaphoreType.DMA((copies,)),
            pltpu.SemaphoreType.DMA((4,)),
        ],
        compiler_params=pltpu.CompilerParams(
            collective_id=1, has_side_effects=True, vmem_limit_bytes=56 * 1024 * 1024
        ),
        name="reduce_gradients",
    )(lengths, starts, times, *parts, *smalls)


FLAT_ROWS = 7896
BLOCK_ROWS = 512
LATE = 609


def adam_kernel(
    field_ref,
    split_ref,
    square_ref,
    length_ref,
    loss_ref,
    weight_ref,
    first_ref,
    second_ref,
    split_weight_ref,
    split_first_ref,
    split_second_ref,
    new_ref,
    new_first_ref,
    new_second_ref,
    low_ref,
    split_new_ref,
    split_new_first_ref,
    split_new_second_ref,
    scalar_ref,
    pulled,
    factor_ref,
    pull_sem,
):
    step = pl.program_id(0)
    last = pl.num_programs(0) - 1
    lane = lax.broadcasted_iota(jnp.int32, (1, 128), 1)

    def pull(block, slot):
        start = pl.multiple_of(block * BLOCK_ROWS, BLOCK_ROWS)
        return pltpu.make_async_copy(
            field_ref.at[pl.ds(start, BLOCK_ROWS + 8)], pulled.at[slot], pull_sem.at[slot]
        )

    def update(weights, first, second, grads):
        first = beta_first * first + (1 - beta_first) * grads
        second = beta_second * second + (1 - beta_second) * grads * grads
        fix_one = 1.0 / (1 - beta_first**STEP)
        fix_two = 1.0 / (1 - beta_second**STEP)
        weights = weights - learn_rate * (
            first * fix_one / (jnp.sqrt(second * fix_two) + adam_epsilon) + weight_decay * weights
        )
        return weights, first, second

    def sum_of(tile):
        held = jnp.sum(jnp.sum(tile, axis=0, keepdims=True), axis=1, keepdims=True)
        return jnp.broadcast_to(held, (1, 128))

    slot = lax.rem(step, 2)

    @pl.when(step == 0)
    def prepare():
        pull(0, 0).start()
        count = sum_of(length_ref[...])
        seed = 1.0 / count
        norm = jnp.sqrt(sum_of(square_ref[...])) * seed
        factor = jnp.minimum(1.0, clip_limit / (norm + 1e-06)) * seed
        factor_ref[...] = jnp.broadcast_to(factor, (8, 128))
        loss = loss_ref[0:1]
        row = lax.broadcasted_iota(jnp.int32, (8, 128), 0)
        scalar_ref[...] = jnp.where(row == 0, norm, jnp.where(row == 1, loss, count))

    @pl.when(step < last)
    def ahead():
        pull(step + 1, 1 - slot).start()

    @pl.when(step == last)
    def split():
        rows = split_weight_ref.shape[0]
        outs = update(
            split_weight_ref[...],
            split_first_ref[...],
            split_second_ref[...],
            split_ref[0:rows] * factor_ref[0:1],
        )
        split_new_ref[...], split_new_first_ref[...], split_new_second_ref[...] = outs

    pull(step, slot).wait()
    early = pulled[slot, 0:BLOCK_ROWS]
    own = pltpu.roll(pulled[slot, 7 : BLOCK_ROWS + 7], 32, 1)
    before = pltpu.roll(pulled[slot, 6 : BLOCK_ROWS + 6], 32, 1)
    row = lax.broadcasted_iota(jnp.int32, (BLOCK_ROWS, 1), 0) + step * BLOCK_ROWS
    grads = jnp.where(lane < 32, jnp.where(row == LATE, early, before), own)
    grads = jnp.where(row < LATE, early, grads)
    outs = update(weight_ref[...], first_ref[...], second_ref[...], grads * factor_ref[0:1])
    new_ref[...], new_first_ref[...], new_second_ref[...] = outs
    low_ref[...] = outs[0].astype(BF16)


def adam_all(field, split_grad, square, length, loss, shared, split):
    grid = -(-FLAT_ROWS // BLOCK_ROWS)
    flat_spec = pl.BlockSpec((BLOCK_ROWS, 128), lambda i: (i, 0))
    split_rows = split[0].shape[0]

    def whole(shape):
        return pl.BlockSpec(shape, lambda i: (0,) * len(shape))

    split_spec = whole((split_rows, 128))
    shared_out = jax.ShapeDtypeStruct((FLAT_ROWS, 128), F32)
    split_out = jax.ShapeDtypeStruct((split_rows, 128), F32)
    return pl.pallas_call(
        adam_kernel,
        grid=(grid,),
        in_specs=[
            pl.BlockSpec(memory_space=pl.ANY),
            whole(split_grad.shape),
            whole((16, 128)),
            whole((8, 128)),
            whole((8, 128)),
            flat_spec,
            flat_spec,
            flat_spec,
            split_spec,
            split_spec,
            split_spec,
        ],
        out_specs=[flat_spec] * 4 + [split_spec] * 3 + [whole((8, 128))],
        out_shape=[shared_out] * 3
        + [jax.ShapeDtypeStruct((FLAT_ROWS, 128), BF16)]
        + [split_out] * 3
        + [jax.ShapeDtypeStruct((8, 128), F32)],
        scratch_shapes=[
            pltpu.VMEM((2, BLOCK_ROWS + 8, 128), F32),
            pltpu.VMEM((8, 128), F32),
            pltpu.SemaphoreType.DMA((2,)),
        ],
        compiler_params=pltpu.CompilerParams(vmem_limit_bytes=48 * 1024 * 1024),
        name="adam_update",
    )(field, split_grad, square, length, loss, *shared, *split)


FAST_ROWS = 768


def valid_slots(lengths, steps):
    ends = jnp.cumsum(lengths)
    slot = jnp.arange(ROOM, dtype=jnp.int32)
    past = slot[:, None] >= ends[None, :-1]
    begin = jnp.sum(jnp.where(past, lengths[None, :-1], 0), axis=1)
    return past, jnp.minimum(slot - begin, steps - 1), ends[-1]


def per_device(
    frames,
    returns,
    actions,
    starts,
    lengths,
    shared_weights,
    shared_first,
    shared_second,
    split_weights,
    split_first,
    split_second,
):
    dp_size, mp_size = lax.axis_size("dp"), lax.axis_size("mp")
    narrow = D // mp_size
    hidden_width = FF // mp_size
    wins, steps = returns.shape
    width = split_weights.shape[0]
    split_rows = width // 128
    packed = narrow == 32
    own_rows = split_weights.reshape(split_rows, 128)
    split_all = lax.all_gather(own_rows, "mp", axis=0)
    flat = shared_weights.reshape(FLAT_ROWS, 128)
    one = shared_weights[:8192].reshape(32, 256)
    two = shared_weights[8224:40992].reshape(64, 512)
    three = shared_weights[41056:77920].reshape(64, 576)
    head = jnp.pad(shared_weights[1008160:1010464].reshape(128, ACT), ((0, 0), (0, 128 - ACT)))
    picked, z_one, z_two, z_three = conv_forward(lengths, frames, flat, one, two, three)
    if packed:
        weights = [split_all]
    else:
        layers, layers_back = jax.vjp(
            lambda held: assemble(held, mp_size, narrow, hidden_width), split_all.reshape(-1)
        )
        weights = [
            jnp.stack([layer["qkv"].transpose(1, 0, 2) for layer in layers]),
            jnp.stack([layer["output"] for layer in layers]),
            jnp.stack([layer["up"] for layer in layers]),
            jnp.stack([layer["up_bias"][None] for layer in layers]),
            jnp.stack([layer["down"] for layer in layers]),
        ]
    results = former(lengths, starts, returns, actions, head, z_three, flat, weights, packed)
    d_three, d_vectors, d_actions, d_head, d_times, loss = results[:6]
    quarter = 3136 // mp_size
    if packed:
        parts = results[6:]
    else:
        d_encoder, d_qkv, d_output, d_up, d_up_bias, d_down = results[6:]
        grad_layers = [
            dict(
                qkv=d_qkv[layer].transpose(1, 0, 2),
                output=d_output[layer],
                up=d_up[layer],
                up_bias=d_up_bias[layer, 0],
                down=d_down[layer],
            )
            for layer in range(LAYERS)
        ]
        gathered = layers_back(grad_layers)[0].reshape(mp_size, split_rows, 128)
        gathered = jnp.pad(gathered, ((0, 0), (0, quarter - split_rows), (0, 0)))
        encoder = d_encoder.reshape(mp_size, quarter, 128)
        every = jnp.concatenate([gathered, encoder], axis=1)
        me = lax.axis_index("mp")
        parts = [
            lax.dynamic_index_in_dim(every, jnp.bitwise_xor(me, k), 0, keepdims=False)
            for k in range(mp_size)
        ]
    arrived = [parts[0]]
    for k in range(1, mp_size):
        turn = [(index, index ^ k) for index in range(mp_size)]
        arrived.append(lax.ppermute(parts[k], "mp", turn))
    d_one, d_two, d_conv, d_bias = conv_backward(
        lengths, picked, z_one, z_two, d_three, two, three
    )
    conv_flat = jnp.concatenate(
        [
            d_one.reshape(-1),
            d_bias[0, 0, :32],
            d_two.reshape(-1),
            d_bias[1, 0, :64],
            d_conv.reshape(-1),
            d_bias[2, 0, :64],
            jnp.zeros((616 * 128 - 77984,), F32),
        ]
    )
    d_head = jnp.pad(d_head[:, :ACT].reshape(ACT, 128), ((0, 24 - ACT), (0, 0)))
    smalls = [conv_flat.reshape(616, 128), d_vectors, d_actions, d_head, loss]
    field, split_sum, square, length_tile, loss_tile = reduce_all(
        lengths,
        starts,
        d_times,
        arrived,
        smalls,
        dp_size,
        mp_size,
        quarter,
        wins * dp_size * mp_size,
    )

    def whole(operands):
        field, square = operands
        past, moment, used = valid_slots(lengths, steps)
        gaps = starts[1:] - starts[:-1]
        spot = moment + starts[0] + jnp.sum(jnp.where(past, gaps[None, :], 0), axis=1)
        spot = jnp.where(jnp.arange(ROOM) < used, spot, 0)
        table = lax.psum(jnp.zeros((TSTEPS, D), F32).at[spot].add(d_times), ("dp", "mp"))
        field = lax.dynamic_update_slice(field, table, (TABLE_AT, 0))
        late = jnp.sum((table * table).reshape(-1, 8, 128), axis=0)
        return field, jnp.concatenate([square[:8], late])

    field, square = lax.cond(
        jnp.sum(length_tile) > FAST_ROWS, whole, lambda operands: operands, (field, square)
    )
    shared_view = [a.reshape(FLAT_ROWS, 128) for a in (shared_weights, shared_first, shared_second)]
    split_view = [a.reshape(split_rows, 128) for a in (split_weights, split_first, split_second)]
    updated = adam_all(
        field, split_sum, square, length_tile, loss_tile, shared_view, split_view
    )
    shared_out = [a.reshape(-1) for a in updated[:4]]
    split_out = [a.reshape(-1) for a in updated[4:7]]
    scalars = updated[7]
    return (
        *shared_out,
        *split_out,
        split_out[0].astype(BF16),
        scalars[0, 0],
        scalars[1, 0],
        scalars[2, 0],
    )


def solution(mesh):
    return jax.shard_map(
        per_device,
        mesh=mesh,
        in_specs=(
            P(("dp", "mp"), None, None, None, None),
            P(("dp", "mp"), None),
            P(("dp", "mp"), None),
            P(("dp", "mp")),
            P(("dp", "mp")),
            P(),
            P(),
            P(),
            P("mp"),
            P("mp"),
            P("mp"),
        ),
        out_specs=(P(), P(), P(), P(), P("mp"), P("mp"), P("mp"), P("mp"), P(), P(), P()),
        check_vma=False,
    )
```

```python
from functools import partial
import math

import jax
import jax.numpy as jnp
from jax import lax
from jax.experimental import pallas as pl
from jax.experimental.pallas import tpu as pltpu
from jax.sharding import PartitionSpec as P

D = 128
FF = 512
ACT = 18
C1 = 32
C2 = 64
TSTEPS = 4096
LAYERS = 2
STEP = 10
HD = 16


clip_limit = 0.1
learn_rate = 0.05
beta_first = 0.9
beta_second = 0.95
adam_epsilon = 1e-08
weight_decay = 0.1


def span_layout(narrow, hidden):
    return [
        ("qkv", (D, 3, narrow)),
        ("output", (narrow, D)),
        ("up", (D, hidden)),
        ("up_bias", (hidden,)),
        ("down", (hidden, D)),
    ]


def assemble(flat, copies, narrow, hidden):
    layout = span_layout(narrow, hidden)
    width = sum((math.prod(shape) for name, shape in layout))
    blocks = flat.reshape(copies, LAYERS, width)
    layers = []
    for layer in range(LAYERS):
        offset = 0
        pieces = {}
        for name, shape in layout:
            count = math.prod(shape)
            pieces[name] = blocks[:, layer, offset : offset + count].reshape((copies,) + shape)
            offset += count
        layers.append(
            {
                "qkv": jnp.moveaxis(pieces["qkv"], 0, 2).reshape(D, 3, copies * narrow),
                "output": pieces["output"].reshape(copies * narrow, D),
                "up": jnp.moveaxis(pieces["up"], 0, 1).reshape(D, copies * hidden),
                "up_bias": pieces["up_bias"].reshape(copies * hidden),
                "down": pieces["down"].reshape(copies * hidden, D),
            }
        )
    return layers


GROUP = 16
CONV_ROWS = 616
ROOM = 128
HALF = 64
BF16 = jnp.bfloat16
F32 = jnp.float32


def gelu_value(x):
    inner = 0.7978845608028654 * (x + 0.044715 * (x * x * x))
    return 0.5 * x * (1.0 + jnp.tanh(inner))


def gelu_both(x):
    square = x * x
    turn = jnp.tanh(0.7978845608028654 * x * (1.0 + 0.044715 * square))
    half = 0.5 * (1.0 + turn)
    slope = half + 0.5 * x * (1.0 - turn * turn) * (
        0.7978845608028654 * (1.0 + 3 * 0.044715 * square)
    )
    return x * half, slope


def two_parts(x):
    high = x.astype(BF16)
    return high, (x - high.astype(F32)).astype(BF16)


def pair(x):
    return jnp.concatenate(two_parts(x), axis=-1)


def fold_pair(x):
    return x[:, :128] + x[:, 128:]


def dot(a, b):
    return lax.dot_general(a, b, (((1,), (0,)), ((), ())), preferred_element_type=F32)


def dot_rows(a, b):
    return lax.dot_general(a, b, (((0,), (0,)), ((), ())), preferred_element_type=F32)


def lanes():
    return lax.broadcasted_iota(jnp.int32, (1, 128), 1)


def conv_biases(flat_ref):
    lane = lanes()
    one = jnp.where(lane < 32, flat_ref[64:65], 0.0)
    one = one + pltpu.roll(one, 32, 1)
    one = one + pltpu.roll(one, 64, 1)
    two = jnp.where(lane < 64, pltpu.roll(flat_ref[320:321], 96, 1), 0.0)
    two = two + pltpu.roll(two, 64, 1)
    three = jnp.where(
        lane < 32,
        pltpu.roll(flat_ref[608:609], 32, 1),
        jnp.where(lane < 64, pltpu.roll(flat_ref[609:610], 32, 1), 0.0),
    )
    three = three + pltpu.roll(three, 64, 1)
    return one, two, three


def shifted(ref, start, rows, lane):
    first = pltpu.roll(ref[start : start + rows], 128 - lane, 1)
    second = pltpu.roll(ref[start + 1 : start + 1 + rows], 128 - lane, 1)
    return jnp.where(lanes() < 128 - lane, first, second)


def spread_one(flat_ref, put):
    halves = [jnp.transpose(flat_ref[pl.ds(side, 32, stride=2), :]) for side in range(2)]
    turned = jnp.concatenate(halves, axis=0)
    lane = lax.broadcasted_iota(jnp.int32, (8, 128), 1)
    row = lax.broadcasted_iota(jnp.int32, (8, 128), 0)
    low = row < 4
    column = lax.shift_right_logical(lane, 5)
    for ky in range(8):
        for c in range(4):
            held = turned[c * 64 + ky * 8 : c * 64 + ky * 8 + 8]
            wide = jnp.concatenate([held] * 4, axis=1)
            flipped = jnp.concatenate([wide[4:], wide[:4]], axis=0)
            zero = jnp.zeros((8, 128), F32)
            first = jnp.where(column == 0, wide, jnp.where((column == 1) & ~low, flipped, zero))
            second = jnp.where(
                column == 2,
                wide,
                jnp.where(((column == 1) & low) | ((column == 3) & ~low), flipped, zero),
            )
            third = jnp.where((column == 3) & low, flipped, zero)
            put(ky * 128 + c * 32, jnp.concatenate([first, second, third, zero], axis=0))


def spread_two(flat_ref, rows_ref, turned, put):
    lane = lax.broadcasted_iota(jnp.int32, (32, 128), 1)
    rows_ref[0:256] = shifted(flat_ref, 64, 256, 32)
    for j in range(4):
        block = jnp.transpose(rows_ref[pl.ds(j, 64, stride=4), :])
        turned[j * 128 : (j + 1) * 128] = jnp.concatenate([block, block], axis=1)
    for ky in range(4):
        rows = [turned[pl.ds(ky * 4 + kx, 32, stride=16)] for kx in range(4)]
        for i in range(8):
            left = rows[i] if i < 4 else jnp.zeros((32, 128), F32)
            right = rows[i - 2] if 2 <= i < 6 else jnp.zeros((32, 128), F32)
            put(ky * 256 + i * 32, jnp.where(lane < 64, left, right))


def spread_three(flat_ref, rows_ref, turned, put):
    lane = lax.broadcasted_iota(jnp.int32, (64, 128), 1)
    side = lax.broadcasted_iota(jnp.int32, (32, 128), 1) < 64
    rows_ref[0:288] = shifted(flat_ref, 320, 288, 96)
    nine = [rows_ref[pl.ds(k, 32, stride=9), :] for k in range(9)]
    flips = [pltpu.roll(nine[4 + k], 64, 1) for k in range(5)]
    for j in range(5):
        wide = min(128, 576 - j * 128)
        rows_ref[pl.ds(0, 32, stride=2), :] = nine[j]
        rows_ref[pl.ds(1, 32, stride=2), :] = (
            jnp.where(side, flips[j], flips[j + 1]) if j < 4 else flips[4]
        )
        block = jnp.transpose(rows_ref[0:64])[0:wide]
        turned[j * 128 : j * 128 + wide] = jnp.concatenate([block, block], axis=1)
    for ky in range(3):
        rows = [turned[pl.ds(ky * 3 + kx, 64, stride=9)] for kx in range(3)]
        for i in range(4):
            left = rows[i] if i < 3 else jnp.zeros((64, 128), F32)
            right = rows[i - 1] if i >= 1 else jnp.zeros((64, 128), F32)
            put(ky * 256 + i * 64, jnp.where(lane < 64, left, right))


def last_masks():
    return lanes() < 64


def conv_forward_kernel(
    lengths_ref,
    frames_ref,
    shared_ref,
    picked_ref,
    z_one_ref,
    z_two_ref,
    z_three_ref,
    flat_ref,
    held,
    wide,
    picked,
    z_one,
    z_two,
    z_three,
    h_one,
    h_two,
    w_one,
    w_two,
    w_three,
    choose,
    rows_ref,
    turned,
    frame_sem,
    out_sem,
):
    wins = lengths_ref.shape[0]
    steps = frames_ref.shape[1]
    used = jnp.int32(0)
    for w in range(wins):
        used = used + lengths_ref[w]
    groups = lax.div(used + (GROUP - 1), GROUP)

    def frame_copy(group, spot, slot):
        state = jnp.minimum(group * GROUP + spot, used - 1)
        window, begin, end = jnp.int32(0), jnp.int32(0), jnp.int32(0)
        for w in range(wins - 1):
            end = end + lengths_ref[w]
            window = jnp.where(state >= end, w + 1, window)
            begin = jnp.where(state >= end, end, begin)
        return pltpu.make_async_copy(
            frames_ref.at[window, state - begin], held.at[slot, spot], frame_sem.at[slot, spot]
        )

    def fetch(group, slot):
        def one(spot, carry):
            frame_copy(group, spot, slot).start()
            return carry

        lax.fori_loop(0, GROUP, one, 0)

    weights = pltpu.make_async_copy(
        shared_ref.at[pl.ds(0, CONV_ROWS)], flat_ref, out_sem.at[4]
    )
    weights.start()
    fetch(0, 0)
    h_one[...] = jnp.zeros(h_one.shape, BF16)

    def put_one(row, block):
        w_one[row : row + 32] = pair(block)

    def put_two(row, block):
        w_two[row : row + 32] = pair(block)

    def put_three(row, block):
        w_three[row : row + 64] = pair(block)

    weights.wait()
    spread_one(flat_ref, put_one)
    spread_two(flat_ref, rows_ref, turned, put_two)
    spread_three(flat_ref, rows_ref, turned, put_three)
    bias_one, bias_two, bias_three = conv_biases(flat_ref)
    row = lax.broadcasted_iota(jnp.int32, (128, 640), 0)
    column = lax.broadcasted_iota(jnp.int32, (128, 640), 1)
    place = jnp.bitwise_and(column, 31)
    channel = jnp.bitwise_and(lax.shift_right_logical(column, 5), 3)
    block = lax.shift_right_logical(column, 7)
    right = (row == 16 * block + place) & (place < 20)
    for c in range(4):
        choose[c * 128 : (c + 1) * 128] = jnp.where(right & (channel == c), 1.0, 0.0).astype(BF16)

    def one_group(group, carry):
        slot = lax.rem(group, 2)

        @pl.when(group + 1 < groups)
        def ahead():
            fetch(group + 1, 1 - slot)

        def lay(spot, carry):
            frame_copy(group, spot, slot).wait()
            image = held[slot, spot].astype(F32).reshape(336, 84)
            image = jnp.concatenate([image, jnp.zeros((336, 44), F32)], axis=1)
            wide[pl.ds(spot, 336, stride=GROUP), :] = image
            return carry

        lax.fori_loop(0, GROUP, lay, 0)
        for part in range(3):
            rows = wide[part * 1792 : (part + 1) * 1792].reshape(28, 4, GROUP, 128)
            rows = [rows[:, c].reshape(448, 128).astype(BF16) for c in range(4)]
            result = dot(jnp.concatenate(rows, axis=1), choose[...])
            picked[part * 7 : (part + 1) * 7] = result.astype(BF16).reshape(7, 4, GROUP, 640)
        keep_picked = pltpu.make_async_copy(picked, picked_ref.at[group], out_sem.at[0])
        keep_picked.start()
        for q in range(5):
            pieces = [
                picked[j : j + 20, b, :, q * 128 : (q + 1) * 128].reshape(20 * GROUP, 128)
                for j in range(2)
                for b in range(4)
            ]
            z = fold_pair(dot(jnp.concatenate(pieces, axis=1), w_one[...])) + bias_one
            z_one[:, :, q] = z.reshape(10, 2, GROUP, 128)
            high, low = two_parts(gelu_value(z))
            h_one[0, :, :, q] = high.reshape(10, 2, GROUP, 128)
            h_one[1, :, :, q] = low.reshape(10, 2, GROUP, 128)
        keep_one = pltpu.make_async_copy(z_one, z_one_ref.at[group], out_sem.at[1])
        keep_one.start()
        total = jnp.zeros((45 * GROUP, 128), F32)
        for part in range(2):
            pieces = []
            for j in range(2):
                for b in range(2):
                    pieces.append(h_one[part, j : j + 9, b, 0:5].reshape(45 * GROUP, 128))
                    pieces.append(h_one[part, j : j + 9, b, 1:6].reshape(45 * GROUP, 128))
            total = total + fold_pair(dot(jnp.concatenate(pieces, axis=1), w_two[...]))
        z = (total + bias_two).reshape(9, 5, GROUP, 128)
        z_two[...] = z
        h = gelu_value(z)
        high, low = two_parts(h)
        h_two[0] = high
        h_two[1] = low
        edge = jnp.where(last_masks(), h[:, 4].reshape(9 * GROUP, 128), 0.0)
        high, low = two_parts(edge)
        h_two[0, :, 4] = high.reshape(9, GROUP, 128)
        h_two[1, :, 4] = low.reshape(9, GROUP, 128)
        keep_two = pltpu.make_async_copy(z_two, z_two_ref.at[group], out_sem.at[2])
        keep_two.start()
        total = jnp.zeros((28 * GROUP, 128), F32)
        for part in range(2):
            pieces = []
            for ky in range(3):
                pieces.append(h_two[part, ky : ky + 7, 0:4].reshape(28 * GROUP, 128))
                pieces.append(h_two[part, ky : ky + 7, 1:5].reshape(28 * GROUP, 128))
            total = total + fold_pair(dot(jnp.concatenate(pieces, axis=1), w_three[...]))
        z_three[...] = (total + bias_three).reshape(28, GROUP, 128)
        spot = pl.multiple_of(group * GROUP, GROUP)
        keep_three = pltpu.make_async_copy(
            z_three, z_three_ref.at[:, pl.ds(spot, GROUP)], out_sem.at[3]
        )
        keep_three.start()
        keep_picked.wait()
        keep_one.wait()
        keep_two.wait()
        keep_three.wait()
        return carry

    lax.fori_loop(0, groups, one_group, 0)


def conv_forward(lengths, frames, flat):
    most = ROOM // GROUP
    any_spec = pl.BlockSpec(memory_space=pl.ANY)
    hbm = pl.BlockSpec(memory_space=pltpu.HBM)
    return pl.pallas_call(
        conv_forward_kernel,
        in_specs=[
            pl.BlockSpec(memory_space=pltpu.SMEM),
            any_spec,
            any_spec,
        ],
        out_specs=[hbm] * 4,
        out_shape=[
            jax.ShapeDtypeStruct((most, 21, 4, GROUP, 640), BF16),
            jax.ShapeDtypeStruct((most, 10, 2, 5, GROUP, 128), F32),
            jax.ShapeDtypeStruct((most, 9, 5, GROUP, 128), F32),
            jax.ShapeDtypeStruct((28, ROOM, 128), F32),
        ],
        scratch_shapes=[
            pltpu.VMEM((CONV_ROWS, 128), F32),
            pltpu.VMEM((2, GROUP, 84, 4, 84), BF16),
            pltpu.VMEM((336 * GROUP, 128), F32),
            pltpu.VMEM((21, 4, GROUP, 640), BF16),
            pltpu.VMEM((10, 2, 5, GROUP, 128), F32),
            pltpu.VMEM((9, 5, GROUP, 128), F32),
            pltpu.VMEM((28, GROUP, 128), F32),
            pltpu.VMEM((2, 10, 2, 6, GROUP, 128), BF16),
            pltpu.VMEM((2, 9, 5, GROUP, 128), BF16),
            pltpu.VMEM((1024, 256), BF16),
            pltpu.VMEM((1024, 256), BF16),
            pltpu.VMEM((768, 256), BF16),
            pltpu.VMEM((512, 640), BF16),
            pltpu.VMEM((288, 128), F32),
            pltpu.VMEM((576, 128), F32),
            pltpu.SemaphoreType.DMA((2, GROUP)),
            pltpu.SemaphoreType.DMA((5,)),
        ],
        compiler_params=pltpu.CompilerParams(vmem_limit_bytes=48 * 1024 * 1024),
        name="conv_forward",
    )(lengths, frames.transpose(0, 1, 3, 2, 4), flat)


def gather_one(total, out):
    lane = lax.broadcasted_iota(jnp.int32, (32, 128), 1)
    halves = [jnp.zeros((32, 128), F32) for side in range(2)]
    for ky in range(8):
        held = total[0:128, ky * 128 : (ky + 1) * 128] + total[128:256, ky * 128 : (ky + 1) * 128]
        summed = held[0:32]
        for o in range(1, 4):
            summed = summed + pltpu.roll(held[32 * o : 32 * o + 32], 128 - 4 * o, 1)
        for c in range(4):
            spot = (c % 2) * 64 + ky * 8
            shift = (spot - c * 32) % 128
            moved = pltpu.roll(summed, shift, 1) if shift else summed
            inside = (lane >= spot) & (lane < spot + 8)
            halves[c // 2] = halves[c // 2] + jnp.where(inside, moved, 0.0)
    for side in range(2):
        out[pl.ds(side, 32, stride=2), :] = halves[side]


def gather_two(total, turned, rows_ref, out):
    lane = lax.broadcasted_iota(jnp.int32, (64, 128), 1)
    for ky in range(4):
        near = total[0:128, ky * 256 : ky * 256 + 128] + total[128:256, ky * 256 : ky * 256 + 128]
        far = (
            total[0:128, ky * 256 + 128 : ky * 256 + 256]
            + total[128:256, ky * 256 + 128 : ky * 256 + 256]
        )
        summed = near[0:64] + jnp.where(
            lane < 64, pltpu.roll(near[64:128], 64, 1), pltpu.roll(far[64:128], 64, 1)
        )
        flipped = jnp.transpose(jnp.concatenate([summed, jnp.zeros((64, 128), F32)], axis=0))
        for kx in range(4):
            turned[pl.ds(ky * 4 + kx, 32, stride=16), :] = flipped[kx * 32 : (kx + 1) * 32]
    rows_ref[0:8] = jnp.zeros((8, 128), F32)
    rows_ref[264:272] = jnp.zeros((8, 128), F32)
    for j in range(4):
        block = jnp.transpose(turned[j * 128 : (j + 1) * 128])[0:64]
        rows_ref[pl.ds(8 + j, 64, stride=4), :] = block
    own = pltpu.roll(rows_ref[8:265], 32, 1)
    before = pltpu.roll(rows_ref[7:264], 32, 1)
    out[64:321] = jnp.where(lanes() >= 32, own, before)


def gather_three(total, turned, rows_ref, out):
    lane = lax.broadcasted_iota(jnp.int32, (64, 128), 1)
    side = lax.broadcasted_iota(jnp.int32, (32, 128), 1) < 64
    blank = jnp.zeros((64, 128), F32)
    for ky in range(3):
        near = total[0:128, ky * 256 : ky * 256 + 128] + total[128:256, ky * 256 : ky * 256 + 128]
        far = (
            total[0:128, ky * 256 + 128 : ky * 256 + 256]
            + total[128:256, ky * 256 + 128 : ky * 256 + 256]
        )
        first = near[0:64] + jnp.where(
            lane < 64, pltpu.roll(near[64:128], 64, 1), pltpu.roll(far[64:128], 64, 1)
        )
        second = far[0:64] + pltpu.roll(far[64:128], 64, 1)
        flipped = jnp.transpose(jnp.concatenate([first, blank], axis=0))
        turned[pl.ds(ky * 3, 64, stride=9), :] = flipped[0:64]
        turned[pl.ds(ky * 3 + 1, 64, stride=9), :] = flipped[64:128]
        flipped = jnp.transpose(jnp.concatenate([second, blank], axis=0))
        turned[pl.ds(ky * 3 + 2, 64, stride=9), :] = flipped[0:64]
    turned[576:640] = blank
    evens, odds = [], []
    for j in range(5):
        rows_ref[0:64] = jnp.transpose(turned[j * 128 : (j + 1) * 128])[0:64]
        evens.append(rows_ref[pl.ds(0, 32, stride=2), :])
        odds.append(pltpu.roll(rows_ref[pl.ds(1, 32, stride=2), :], 64, 1))
    rows_ref[0:8] = jnp.zeros((8, 128), F32)
    rows_ref[296:304] = jnp.zeros((8, 128), F32)
    for k in range(9):
        if k < 4:
            held = evens[k]
        elif k == 4:
            held = jnp.where(side, evens[4], odds[0])
        else:
            held = jnp.where(side, odds[k - 5], odds[k - 4])
        rows_ref[pl.ds(8 + k, 32, stride=9), :] = held
    own = pltpu.roll(rows_ref[8:297], 96, 1)
    before = pltpu.roll(rows_ref[7:296], 96, 1)
    edge = out[320:321]
    out[320:609] = jnp.where(lanes() >= 96, own, before)
    out[320:321] = out[320:321] + edge


def conv_backward_kernel(
    lengths_ref,
    picked_ref,
    z_one_ref,
    z_two_ref,
    d_three_ref,
    shared_ref,
    flat_out,
    flat_ref,
    picked,
    z_one,
    z_two,
    d_three,
    h_one,
    h_two,
    slope_one,
    pad_three,
    pad_two,
    d_one,
    v_two,
    v_three,
    spread,
    rows_ref,
    turned,
    bias_out,
    total_one,
    total_two,
    total_three,
    load_sem,
    weight_sem,
):
    used = jnp.int32(0)
    for w in range(lengths_ref.shape[0]):
        used = used + lengths_ref[w]
    groups = lax.div(used + (GROUP - 1), GROUP)

    def loads(group, slot):
        spot = pl.multiple_of(group * GROUP, GROUP)
        return [
            pltpu.make_async_copy(picked_ref.at[group], picked.at[slot], load_sem.at[slot, 0]),
            pltpu.make_async_copy(z_one_ref.at[group], z_one.at[slot], load_sem.at[slot, 1]),
            pltpu.make_async_copy(z_two_ref.at[group], z_two.at[slot], load_sem.at[slot, 2]),
            pltpu.make_async_copy(
                d_three_ref.at[:, pl.ds(spot, GROUP)], d_three.at[slot], load_sem.at[slot, 3]
            ),
        ]

    weights = pltpu.make_async_copy(
        shared_ref.at[pl.ds(0, CONV_ROWS)], flat_ref, weight_sem
    )
    weights.start()
    for load in loads(0, 0):
        load.start()

    def put_two(row, block):
        spread[row : row + 32] = block

    def put_three(row, block):
        spread[row : row + 64] = block

    weights.wait()
    spread_two(flat_ref, rows_ref, turned, put_two)
    for b in range(2):
        for j in range(2):
            for side in range(2):
                source = (2 * j + b) * 256 + side * 128
                target = (b * 2 + j) * 256 + side * 128
                v_two[target : target + 128] = pair(jnp.transpose(spread[source : source + 128]))
    spread_three(flat_ref, rows_ref, turned, put_three)
    for part in range(6):
        rows = pl.ds(part * 128, 128)
        v_three[rows] = pair(jnp.transpose(spread[rows]))
    total_one[...] = jnp.zeros(total_one.shape, F32)
    total_two[...] = jnp.zeros(total_two.shape, F32)
    total_three[...] = jnp.zeros(total_three.shape, F32)
    bias_out[...] = jnp.zeros(bias_out.shape, F32)
    h_one[...] = jnp.zeros(h_one.shape, BF16)
    pad_two[...] = jnp.zeros(pad_two.shape, BF16)
    pad_three[...] = jnp.zeros(pad_three.shape, BF16)

    def fold(rows):
        return jnp.sum(rows.reshape(-1, 8, 128), axis=0)

    def one_group(group, carry):
        slot = lax.rem(group, 2)

        @pl.when(group + 1 < groups)
        def ahead():
            for load in loads(group + 1, 1 - slot):
                load.start()

        for load in loads(group, slot):
            load.wait()
        rows = d_three[slot].reshape(28 * GROUP, 128)
        bias_out[2] += fold(rows)
        both = pair(rows)
        pad_three[0, 2:9, 1:5] = both[:, :128].reshape(7, 4, GROUP, 128)
        pad_three[1, 2:9, 1:5] = both[:, 128:].reshape(7, 4, GROUP, 128)
        h, slope_two = gelu_both(z_two[slot])
        high, low = two_parts(h)
        h_two[0] = high
        h_two[1] = low
        edge = jnp.where(last_masks(), h[:, 4].reshape(9 * GROUP, 128), 0.0)
        high, low = two_parts(edge)
        h_two[0, :, 4] = high.reshape(9, GROUP, 128)
        h_two[1, :, 4] = low.reshape(9, GROUP, 128)
        for part in range(2):
            pieces = []
            for ky in range(3):
                pieces.append(h_two[part, ky : ky + 7, 0:4].reshape(28 * GROUP, 128))
                pieces.append(h_two[part, ky : ky + 7, 1:5].reshape(28 * GROUP, 128))
            total_three[...] += dot_rows(both, jnp.concatenate(pieces, axis=1))
        spill = jnp.zeros((45 * GROUP, 128), F32)
        for part in range(2):
            pieces = []
            for ky in range(3):
                pieces.append(pad_three[part, 2 - ky : 11 - ky, 1:6].reshape(45 * GROUP, 128))
                pieces.append(pad_three[part, 2 - ky : 11 - ky, 0:5].reshape(45 * GROUP, 128))
            spill = spill + fold_pair(dot(jnp.concatenate(pieces, axis=1), v_three[...]))
        rows = spill * slope_two.reshape(45 * GROUP, 128)
        bias_out[1] += fold(rows)
        both = pair(rows)
        pad_two[0, 1:10, 1:6] = both[:, :128].reshape(9, 5, GROUP, 128)
        pad_two[1, 1:10, 1:6] = both[:, 128:].reshape(9, 5, GROUP, 128)
        for q in range(5):
            h, slope = gelu_both(z_one[slot, :, :, q])
            high, low = two_parts(h)
            h_one[0, :, :, q] = high
            h_one[1, :, :, q] = low
            slope_one[:, :, q] = slope
        for part in range(2):
            pieces = []
            for j in range(2):
                for b in range(2):
                    pieces.append(h_one[part, j : j + 9, b, 0:5].reshape(45 * GROUP, 128))
                    pieces.append(h_one[part, j : j + 9, b, 1:6].reshape(45 * GROUP, 128))
            total_two[...] += dot_rows(both, jnp.concatenate(pieces, axis=1))
        for b in range(2):
            spill = jnp.zeros((50 * GROUP, 128), F32)
            for part in range(2):
                pieces = []
                for j in range(2):
                    pieces.append(pad_two[part, 1 - j : 11 - j, 1:6].reshape(50 * GROUP, 128))
                    pieces.append(pad_two[part, 1 - j : 11 - j, 0:5].reshape(50 * GROUP, 128))
                spill = spill + fold_pair(
                    dot(jnp.concatenate(pieces, axis=1), v_two[b * 512 : (b + 1) * 512])
                )
            rows = spill * slope_one[:, b].reshape(50 * GROUP, 128)
            bias_out[0] += fold(rows)
            d_one[:, b] = pair(rows).reshape(10, 5, GROUP, 256)
        for q in range(5):
            pieces = [
                picked[slot, j : j + 20, b, :, q * 128 : (q + 1) * 128].reshape(20 * GROUP, 128)
                for j in range(2)
                for b in range(4)
            ]
            total_one[...] += dot_rows(
                d_one[:, :, q].reshape(20 * GROUP, 256), jnp.concatenate(pieces, axis=1)
            )
        return carry

    lax.fori_loop(0, groups, one_group, 0)
    gather_one(total_one, flat_out)
    gather_two(total_two, turned, rows_ref, flat_out)
    gather_three(total_three, turned, rows_ref, flat_out)
    lane = lanes()
    sums = [jnp.sum(bias_out[k], axis=0, keepdims=True) for k in range(3)]
    sums[0] = sums[0] + pltpu.roll(sums[0], 64, 1)
    sums[0] = sums[0] + pltpu.roll(sums[0], 32, 1)
    sums[1] = jnp.where(lane < 64, sums[1] + pltpu.roll(sums[1], 64, 1), 0.0)
    sums[2] = jnp.where(lane < 64, sums[2] + pltpu.roll(sums[2], 64, 1), 0.0)
    flat_out[64:65] = jnp.where(lane < 32, sums[0], flat_out[64:65])
    flat_out[320:321] = flat_out[320:321] + pltpu.roll(sums[1], 32, 1)
    late = pltpu.roll(sums[2], 96, 1)
    flat_out[608:609] = flat_out[608:609] + jnp.where(lane >= 96, late, 0.0)
    row = lax.broadcasted_iota(jnp.int32, (7, 128), 0)
    flat_out[609:616] = jnp.where((row == 0) & (lane < 32), late, 0.0)


def conv_backward(lengths, picked, z_one, z_two, d_three, flat):
    hbm = pl.BlockSpec(memory_space=pltpu.HBM)
    vmem = pl.BlockSpec(memory_space=pltpu.VMEM)
    return pl.pallas_call(
        conv_backward_kernel,
        in_specs=[pl.BlockSpec(memory_space=pltpu.SMEM)] + [hbm] * 5,
        out_specs=vmem,
        out_shape=jax.ShapeDtypeStruct((CONV_ROWS, 128), F32),
        scratch_shapes=[
            pltpu.VMEM((CONV_ROWS, 128), F32),
            pltpu.VMEM((2, 21, 4, GROUP, 640), BF16),
            pltpu.VMEM((2, 10, 2, 5, GROUP, 128), F32),
            pltpu.VMEM((2, 9, 5, GROUP, 128), F32),
            pltpu.VMEM((2, 28, GROUP, 128), F32),
            pltpu.VMEM((2, 10, 2, 6, GROUP, 128), BF16),
            pltpu.VMEM((2, 9, 5, GROUP, 128), BF16),
            pltpu.VMEM((10, 2, 5, GROUP, 128), F32),
            pltpu.VMEM((2, 11, 6, GROUP, 128), BF16),
            pltpu.VMEM((2, 11, 6, GROUP, 128), BF16),
            pltpu.VMEM((10, 2, 5, GROUP, 256), BF16),
            pltpu.VMEM((1024, 256), BF16),
            pltpu.VMEM((768, 256), BF16),
            pltpu.VMEM((1024, 128), F32),
            pltpu.VMEM((304, 128), F32),
            pltpu.VMEM((640, 128), F32),
            pltpu.VMEM((3, 8, 128), F32),
            pltpu.VMEM((256, 1024), F32),
            pltpu.VMEM((256, 1024), F32),
            pltpu.VMEM((256, 768), F32),
            pltpu.SemaphoreType.DMA((2, 4)),
            pltpu.SemaphoreType.DMA,
        ],
        compiler_params=pltpu.CompilerParams(vmem_limit_bytes=48 * 1024 * 1024),
        name="conv_backward",
    )(lengths, picked, z_one, z_two, d_three, flat)


HIGH = lax.Precision.HIGH
VECTORS_ROW = 3745
TIME_ROW = 3780


def mm(a, b):
    return lax.dot_general(
        a, b, (((1,), (0,)), ((), ())), precision=HIGH, preferred_element_type=F32
    )


def mm_nt(a, b):
    return lax.dot_general(
        a, b, (((1,), (1,)), ((), ())), precision=HIGH, preferred_element_type=F32
    )


def mm_tn(a, b):
    return lax.dot_general(
        a, b, (((0,), (0,)), ((), ())), precision=HIGH, preferred_element_type=F32
    )


def dot_nt(a, b):
    return lax.dot_general(a, b, (((1,), (1,)), ((), ())), preferred_element_type=F32)


def norm_parts(stream):
    centered = stream - jnp.mean(stream, -1, keepdims=True)
    spread = jnp.mean(centered * centered, -1, keepdims=True)
    scale = lax.rsqrt(spread + 1e-05)
    return centered * scale, scale


def norm_back(grad, unit, scale, gain):
    grad = grad * gain
    inner = jnp.mean(grad * unit, -1, keepdims=True)
    return scale * (grad - jnp.mean(grad, -1, keepdims=True) - unit * inner)


def column_sum(x):
    return jnp.sum(x, axis=0, keepdims=True)


def head_places():
    number = lax.broadcasted_iota(jnp.int32, (128, 128), 0) * ACT
    lane = lax.broadcasted_iota(jnp.int32, (128, 128), 1)
    row = lax.shift_right_logical(number, 7)
    return row + jnp.where(lane < jnp.bitwise_and(number, 127), 1, 0)


def roll_rows(held, sign):
    number = lax.broadcasted_iota(jnp.int32, (128, 128), 0) * ACT
    for k in range(7):
        moved = pltpu.roll(held, (sign * (1 << k)) % 128, 1)
        held = jnp.where(jnp.bitwise_and(number, 1 << k) > 0, moved, held)
    return held


def square_head(rows):
    place = head_places()
    held = jnp.zeros((128, 128), F32)
    for k in range(ACT):
        held = jnp.where(place == k, rows[k : k + 1], held)
    held = roll_rows(held, -1)
    lane = lax.broadcasted_iota(jnp.int32, (128, 128), 1)
    return jnp.where(lane < ACT, held, 0.0)


def flat_head(grads):
    place = head_places()
    lane = lax.broadcasted_iota(jnp.int32, (128, 128), 1)
    held = roll_rows(jnp.where(lane < ACT, grads, 0.0), 1)
    rows = [
        jnp.sum(jnp.where(place == k, held, 0.0), axis=0, keepdims=True) for k in range(ACT)
    ]
    return jnp.concatenate(rows + [jnp.zeros((24 - ACT, 128), F32)], axis=0)


def unpack_split(split_ref, qkv, output, up, up_bias, down):
    lane = lax.broadcasted_iota(jnp.int32, (32, 128), 1)
    for layer in range(LAYERS):
        base = layer * 385
        kinds = [[jnp.zeros((32, 128), F32) for j in range(4)] for kind in range(3)]
        for m in range(4):
            rows = [split_ref[m, pl.ds(base + k, 32, stride=3), :] for k in range(3)]
            inside = (lane >= 32 * m) & (lane < 32 * m + 32)
            for j in range(4):
                for kind in range(3):
                    spot = j * 96 + kind * 32
                    source = rows[spot // 128]
                    shift = (32 * m - spot % 128) % 128
                    moved = pltpu.roll(source, shift, 1) if shift else source
                    kinds[kind][j] = jnp.where(inside, moved, kinds[kind][j])
            output[layer, 32 * m : 32 * m + 32] = split_ref[m, base + 96 : base + 128]
            up[layer, :, 128 * m : 128 * m + 128] = split_ref[m, base + 128 : base + 256]
            up_bias[layer, :, 128 * m : 128 * m + 128] = split_ref[m, base + 256 : base + 257]
            down[layer, 128 * m : 128 * m + 128] = split_ref[m, base + 257 : base + 385]
        for kind in range(3):
            for j in range(4):
                qkv[layer, kind, pl.ds(j, 32, stride=4), :] = kinds[kind][j]


def pack_split(out_ref, qkv, output, up, up_bias, down):
    lane = lax.broadcasted_iota(jnp.int32, (32, 128), 1)
    for layer in range(LAYERS):
        base = layer * 385
        parts = [[qkv[layer, kind, pl.ds(j, 32, stride=4), :] for j in range(4)] for kind in range(3)]
        for m in range(4):
            rows = [jnp.zeros((32, 128), F32) for k in range(3)]
            for j in range(4):
                for kind in range(3):
                    spot = j * 96 + kind * 32
                    low = spot % 128
                    shift = (low - 32 * m) % 128
                    moved = pltpu.roll(parts[kind][j], shift, 1) if shift else parts[kind][j]
                    inside = (lane >= low) & (lane < low + 32)
                    rows[spot // 128] = jnp.where(inside, moved, rows[spot // 128])
            for k in range(3):
                out_ref[m, pl.ds(base + k, 32, stride=3), :] = rows[k]
            out_ref[m, base + 96 : base + 128] = output[layer, 32 * m : 32 * m + 32]
            out_ref[m, base + 128 : base + 256] = up[layer, :, 128 * m : 128 * m + 128]
            out_ref[m, base + 256 : base + 257] = up_bias[layer, :, 128 * m : 128 * m + 128]
            out_ref[m, base + 257 : base + 385] = down[layer, 128 * m : 128 * m + 128]
    for m in range(4):
        out_ref[m, 770:784] = jnp.zeros((14, 128), F32)


def former_body(
    slots,
    used,
    lengths_ref,
    returns_ref,
    actions_ref,
    head_ref,
    z_ref,
    small,
    times_all,
    encoder,
    weights,
    d_three_ref,
    d_encoder_ref,
    d_small_ref,
    d_times_ref,
    grads,
    chances,
    kept,
    sums,
    flats,
):
    qkv, output, up, up_bias, down = weights
    d_qkv, d_output, d_up, d_up_bias, d_down = grads
    rows = 3 * slots
    wins, steps = returns_ref.shape
    vec = [small[k : k + 1] for k in range(17)]
    table = small[17 : 17 + ACT]
    slot = lax.broadcasted_iota(jnp.int32, (slots, 1), 0)
    window = jnp.zeros((slots, 1), jnp.int32)
    begin = jnp.zeros((slots, 1), jnp.int32)
    end = jnp.int32(0)
    for w in range(wins - 1):
        end = end + lengths_ref[w]
        window = jnp.where(slot >= end, w + 1, window)
        begin = jnp.where(slot >= end, end, begin)
    moment = slot - begin
    valid = slot < used
    time_lane = lax.broadcasted_iota(jnp.int32, (slots, steps), 1)
    amount = jnp.zeros((slots, 1), F32)
    action = jnp.zeros((slots, 1), jnp.int32)
    for w in range(wins):
        here = (time_lane == moment) & (window == w)
        amount = amount + jnp.sum(
            jnp.where(here, returns_ref[w : w + 1], 0.0), axis=1, keepdims=True
        )
        action = action + jnp.sum(jnp.where(here, actions_ref[w : w + 1], 0), axis=1, keepdims=True)
    lane = lax.broadcasted_iota(jnp.int32, (slots, 128), 1)
    picks = jnp.where((lane == action) & valid, 1.0, 0.0)
    reward = jnp.tanh(amount * vec[14] + vec[15])
    table = jnp.concatenate([table, jnp.zeros((128 - ACT, 128), F32)], axis=0)
    move = jnp.tanh(mm(picks, table))
    sum_state = jnp.zeros((slots, 128), F32)
    for k in range(28):
        z = jnp.where(valid, z_ref[k, 0:slots], 0.0)
        high, low = two_parts(gelu_value(z))
        flats[0, 0:slots, k * 128 : (k + 1) * 128] = high
        flats[1, 0:slots, k * 128 : (k + 1) * 128] = low
    for part in range(2):
        sum_state = sum_state + fold_pair(dot(flats[part, 0:slots], encoder[...]))
    state = jnp.tanh(sum_state + vec[16])
    times = times_all[0:slots]
    stream = jnp.concatenate([reward + times, state + times, move + times], axis=0)

    def ids(axis):
        shape = (rows, 1) if axis == 0 else (1, rows)
        number = lax.broadcasted_iota(jnp.int32, shape, axis)
        kind = jnp.where(number >= 2 * slots, 2, jnp.where(number >= slots, 1, 0))
        return number - kind * slots, kind

    (slot_q, kind_q), (slot_k, kind_k) = ids(0), ids(1)

    def begin_of(slot_ids):
        found = jnp.zeros(slot_ids.shape, jnp.int32)
        end = jnp.int32(0)
        for w in range(wins - 1):
            end = end + lengths_ref[w]
            found = jnp.where(slot_ids >= end, end, found)
        return found

    order_q = slot_q * 3 + kind_q
    order_k = slot_k * 3 + kind_k
    allowed = (order_q >= order_k) & (slot_k >= begin_of(slot_q)) & (slot_k < used)
    head_of = lax.shift_right_logical(lax.broadcasted_iota(jnp.int32, (1, 128), 1), 4)
    heads = D // HD
    batch = 4 if slots <= HALF else 2

    def masked(x, masks):
        return jnp.concatenate([jnp.where(mask, x, jnp.zeros_like(x)) for mask in masks], axis=0)

    def unmasked(x, masks):
        held = jnp.where(masks[0], x[0:rows], 0.0)
        for k in range(1, batch):
            held = held + jnp.where(masks[k], x[k * rows : (k + 1) * rows], 0.0)
        return held

    tape = []
    for layer in range(LAYERS):
        gains = vec[6 * layer : 6 * layer + 6]
        unit_one, scale_one = norm_parts(stream)
        normed = unit_one * gains[0] + gains[1]
        wide = jnp.concatenate([qkv[layer, k] for k in range(3)], axis=1)
        mixed = mm(normed, wide)
        query_high, query_low = two_parts(mixed[:, :128] * 0.25)
        keys, values = pair(mixed[:, 128:256]), pair(mixed[:, 256:])
        kept[layer, 0, 0:rows] = query_high
        kept[layer, 1, 0:rows] = query_low
        for k in range(2):
            kept[layer, 2 + k, 0:rows] = keys[:, k * 128 : (k + 1) * 128]
            kept[layer, 4 + k, 0:rows] = values[:, k * 128 : (k + 1) * 128]
        sums[0, 0:rows] = jnp.zeros((rows, 128), F32)

        def attend(turn, carry, layer=layer):
            masks = [head_of == turn * batch + k for k in range(batch)]
            parts = [masked(kept[layer, k, 0:rows], masks) for k in range(2)]
            keys = [kept[layer, 2 + k, 0:rows] for k in range(2)]
            values = [kept[layer, 4 + k, 0:rows] for k in range(2)]
            scores = dot_nt(
                jnp.concatenate([parts[0], parts[0]], axis=1), jnp.concatenate(keys, axis=1)
            )
            scores = (scores + dot_nt(parts[1], keys[0])).reshape(batch, rows, rows)
            scores = jnp.where(allowed[None], scores, -1e30)
            peak = jnp.max(scores, -1, keepdims=True)
            chance = jnp.exp(scores - peak)
            chance = chance / jnp.sum(chance, -1, keepdims=True)
            high, low = two_parts(chance.reshape(batch * rows, rows))
            spot = pl.ds(pl.multiple_of(turn * (batch * rows), 64), batch * rows)
            chances[layer, 0, spot, 0:rows] = high
            chances[layer, 1, spot, 0:rows] = low
            seen = fold_pair(dot(high, jnp.concatenate(values, axis=1))) + dot(low, values[0])
            sums[0, 0:rows] += unmasked(seen, masks)
            return carry

        lax.fori_loop(0, heads // batch, attend, 0)
        context = sums[0, 0:rows]
        stream = stream + mm(context, output[layer]) + gains[4]
        unit_two, scale_two = norm_parts(stream)
        normed_two = unit_two * gains[2] + gains[3]
        inner, slope = gelu_both(mm(normed_two, up[layer]) + up_bias[layer])
        stream = stream + mm(inner, down[layer]) + gains[5]
        tape.append((unit_one, scale_one, unit_two, scale_two, inner, slope, context))
    end_stream = stream[slots : 2 * slots]
    unit, scale = norm_parts(end_stream)
    final = unit * vec[12] + vec[13]
    logits = jnp.where(lane < ACT, mm(final, head_ref[...]), -1e30)
    peak = jnp.max(logits, -1, keepdims=True)
    powers = jnp.exp(logits - peak)
    total = jnp.sum(powers, -1, keepdims=True)
    chosen = jnp.sum(jnp.where(lane == action, logits, 0.0), -1, keepdims=True)
    terms = jnp.where(valid, jnp.log(total) + peak - chosen, 0.0)
    loss = jnp.sum(terms, axis=0, keepdims=True)
    d_small_ref[72:80] = jnp.broadcast_to(loss, (8, 128))
    d_logits = jnp.where(valid, powers / total, 0.0) - picks
    d_small_ref[48:72] = flat_head(mm_tn(final, d_logits))
    d_final = mm_nt(d_logits, head_ref[...])
    d_vec = [None] * 17
    d_vec[12] = column_sum(d_final * unit)
    d_vec[13] = column_sum(d_final)
    d_end = norm_back(d_final, unit, scale, vec[12])
    blank = jnp.zeros((slots, 128), F32)
    d_stream = jnp.concatenate([blank, d_end, blank], axis=0)
    for layer in reversed(range(LAYERS)):
        unit_one, scale_one, unit_two, scale_two, inner, slope, context = tape[layer]
        gains = vec[6 * layer : 6 * layer + 6]
        d_vec[6 * layer + 5] = column_sum(d_stream)
        d_down[layer] = mm_tn(inner, d_stream)
        d_inner = mm_nt(d_stream, down[layer]) * slope
        d_up_bias[layer] = column_sum(d_inner)
        normed_two = unit_two * gains[2] + gains[3]
        d_up[layer] = mm_tn(normed_two, d_inner)
        d_normed = mm_nt(d_inner, up[layer])
        d_vec[6 * layer + 2] = column_sum(d_normed * unit_two)
        d_vec[6 * layer + 3] = column_sum(d_normed)
        d_stream = d_stream + norm_back(d_normed, unit_two, scale_two, gains[2])
        d_vec[6 * layer + 4] = column_sum(d_stream)
        d_output[layer] = mm_tn(context, d_stream)
        d_context = mm_nt(d_stream, output[layer])
        bases = d_context * context
        high, low = two_parts(d_context)
        for k in range(3):
            sums[k, 0:rows] = jnp.zeros((rows, 128), F32)
        kept[layer, 6, 0:rows] = high
        kept[layer, 7, 0:rows] = low
        sums[3, 0:rows] = bases

        def attend_back(turn, carry, layer=layer):
            masks = [head_of == turn * batch + k for k in range(batch)]
            query = [masked(kept[layer, k, 0:rows], masks) for k in range(2)]
            keys = [kept[layer, 2 + k, 0:rows] for k in range(2)]
            values = [kept[layer, 4 + k, 0:rows] for k in range(2)]
            d_seen = [masked(kept[layer, 6 + k, 0:rows], masks) for k in range(2)]
            base = jnp.sum(masked(sums[3, 0:rows], masks), -1, keepdims=True)
            spot = pl.ds(pl.multiple_of(turn * (batch * rows), 64), batch * rows)
            chance = [chances[layer, k, spot, 0:rows] for k in range(2)]
            d_chance = dot_nt(
                jnp.concatenate([d_seen[0], d_seen[0]], axis=1), jnp.concatenate(values, axis=1)
            )
            d_chance = d_chance + dot_nt(d_seen[1], values[0])
            d_scores = (chance[0].astype(F32) + chance[1].astype(F32)) * (d_chance - base)
            high, low = two_parts(d_scores)
            d_query = fold_pair(dot(high, jnp.concatenate(keys, axis=1))) + dot(low, keys[0])
            sums[0, 0:rows] += unmasked(d_query, masks)
            d_keys = fold_pair(dot_rows(high, jnp.concatenate(query, axis=1)))
            sums[1, 0:rows] += d_keys + dot_rows(low, query[0])
            d_values = fold_pair(dot_rows(chance[0], jnp.concatenate(d_seen, axis=1)))
            sums[2, 0:rows] += d_values + dot_rows(chance[1], d_seen[0])
            return carry

        lax.fori_loop(0, heads // batch, attend_back, 0)
        normed = unit_one * gains[0] + gains[1]
        d_mixed = jnp.concatenate(
            [sums[0, 0:rows] * 0.25, sums[1, 0:rows], sums[2, 0:rows]], axis=1
        )
        wide = jnp.concatenate([qkv[layer, k] for k in range(3)], axis=1)
        d_wide = mm_tn(normed, d_mixed)
        for k in range(3):
            d_qkv[layer, k] = d_wide[:, k * 128 : (k + 1) * 128]
        d_normed = mm_nt(d_mixed, wide)
        d_vec[6 * layer] = column_sum(d_normed * unit_one)
        d_vec[6 * layer + 1] = column_sum(d_normed)
        d_stream = d_stream + norm_back(d_normed, unit_one, scale_one, gains[0])
    d_reward, d_state, d_move = (d_stream[k * slots : (k + 1) * slots] for k in range(3))
    d_times_ref[0:slots] = jnp.where(valid, d_reward + d_state + d_move, 0.0)
    d_reward = d_reward * (1.0 - reward * reward)
    d_vec[14] = column_sum(d_reward * amount)
    d_vec[15] = column_sum(d_reward)
    d_move = d_move * (1.0 - move * move)
    d_small_ref[24:48] = mm_tn(picks, d_move)[0:24]
    d_state = jnp.where(valid, d_state * (1.0 - state * state), 0.0)
    d_vec[16] = column_sum(d_state)
    d_small_ref[0:24] = jnp.concatenate(d_vec + [jnp.zeros((7, 128), F32)], axis=0)
    high, low = two_parts(d_state)
    twice = jnp.concatenate([high, high], axis=1)
    both = jnp.concatenate([high, low], axis=1)
    d_flat = dot_nt(twice, encoder[...]) + dot_nt(low, encoder[:, 0:128])
    d_block = dot_rows(flats[0, 0:slots], both) + dot_rows(flats[1, 0:slots], both)
    d_block = fold_pair(d_block)
    for k in range(28):
        z = jnp.where(valid, z_ref[k, 0:slots], 0.0)
        d_three_ref[k, 0:slots] = d_flat[:, k * 128 : (k + 1) * 128] * gelu_both(z)[1]
        y, v = divmod(k, 4)
        for o in range(2):
            if 2 * v + o < 7:
                d_encoder_ref[pl.ds(y * 7 + 2 * v + o, 64, stride=49), :] = d_block[
                    k * 128 + o * 64 : k * 128 + (o + 1) * 64
                ]


def former_kernel(
    packed,
    lengths_ref,
    starts_ref,
    index_ref,
    returns_ref,
    actions_ref,
    z_from,
    flat_ref,
    *refs,
):
    if packed:
        split_ref, refs = refs[0], refs[1:]
    else:
        given, refs = refs[:5], refs[5:]
    (d_three_to, rows_ref), refs = refs[:2], refs[2:]
    if packed:
        parts, refs = refs[:4], refs[4:]
        (d_encoder_ref, d_small_ref, d_split, part_sem), refs = refs[:4], refs[4:]
        weights, grads, refs = refs[:5], refs[5:10], refs[10:]
    else:
        (d_encoder_ref, d_small_ref), grads, refs = refs[:2], refs[2:7], refs[7:]
        weights = given
    (raw, near, small, rows_raw, times_all, encoder, chances, kept, sums, flats), refs = (
        refs[:10],
        refs[10:],
    )
    z_ref, d_three_ref, head_ref, sem = refs
    used = jnp.int32(0)
    wins = lengths_ref.shape[0]
    for w in range(wins):
        used = used + lengths_ref[w]

    def z_copy(slots):
        return pltpu.make_async_copy(
            z_from.at[:, pl.ds(0, slots)], z_ref.at[:, pl.ds(0, slots)], sem.at[wins + 3]
        )

    def z_back(slots):
        return pltpu.make_async_copy(
            d_three_ref.at[:, pl.ds(0, slots)], d_three_to.at[:, pl.ds(0, slots)], sem.at[wins + 3]
        )

    copies = [
        pltpu.make_async_copy(flat_ref.at[pl.ds(608, 3144)], raw, sem.at[0]),
        pltpu.make_async_copy(flat_ref.at[pl.ds(3744, 48)], rows_raw.at[wins], sem.at[1]),
        pltpu.make_async_copy(
            flat_ref.at[pl.ds(7872, 24)], rows_raw.at[wins + 1, pl.ds(0, 24)], sem.at[2]
        ),
    ]
    offsets = []
    for w in range(wins):
        row = TIME_ROW + starts_ref[w]
        low = pl.multiple_of(lax.div(row, 8) * 8, 8)
        offsets.append(row - low)
        copies.append(
            pltpu.make_async_copy(
                flat_ref.at[pl.ds(low, 40)], rows_raw.at[w, pl.ds(0, 40)], sem.at[3 + w]
            )
        )
    for copy in copies:
        copy.start()

    @pl.when(used <= HALF)
    def few_states():
        z_copy(HALF).start()

    @pl.when(used > HALF)
    def many_states():
        z_copy(ROOM).start()

    if packed:
        unpack_split(split_ref, *weights)
    for copy in copies:
        copy.wait()
    lane = lanes()

    def straight(first, second):
        return jnp.where(lane < 96, pltpu.roll(first, 96, 1), pltpu.roll(second, 96, 1))

    def turn(step, carry):
        spot = pl.multiple_of(step * 64, 64)
        near[pl.ds(spot, 64)] = straight(raw[pl.ds(spot + 1, 64)], raw[pl.ds(spot + 2, 64)])
        return carry

    lax.fori_loop(0, 49, turn, 0)
    for k in range(28):
        y, v = divmod(k, 4)
        halves = []
        for o in range(2):
            if 2 * v + o < 7:
                halves.append(near[pl.ds(y * 7 + 2 * v + o, 64, stride=49), :])
            else:
                halves.append(jnp.zeros((64, 128), F32))
        encoder[k * 128 : (k + 1) * 128] = pair(jnp.concatenate(halves, axis=0))
    small[...] = straight(rows_raw[wins, 1:41], rows_raw[wins, 2:42])
    head_ref[...] = square_head(
        straight(rows_raw[wins + 1, 4:22], rows_raw[wins + 1, 5:23])
    )
    times_all[...] = jnp.zeros(times_all.shape, F32)
    begin = 0
    row = lax.broadcasted_iota(jnp.int32, (32, 1), 0)
    for w in range(wins):
        rows = straight(
            rows_raw[w, pl.ds(offsets[w], 32)], rows_raw[w, pl.ds(offsets[w] + 1, 32)]
        )
        times_all[pl.ds(begin, 32)] = jnp.where(row < lengths_ref[w], rows, 0.0)
        begin = begin + lengths_ref[w]
    rows_ref[...] = jnp.zeros(rows_ref.shape, F32)
    note = jnp.zeros((1, 128), F32)
    for w in range(wins):
        note = jnp.where(lane == w, lengths_ref[w].astype(F32), note)
        note = jnp.where(lane == wins + w, starts_ref[w].astype(F32), note)
    rows_ref[ROOM : ROOM + 1] = note
    d_small_ref[...] = jnp.zeros(d_small_ref.shape, F32)

    def run(slots):
        z_copy(slots).wait()
        former_body(
            slots,
            used,
            lengths_ref,
            returns_ref,
            actions_ref,
            head_ref,
            z_ref,
            small,
            times_all,
            encoder,
            weights,
            d_three_ref,
            d_encoder_ref,
            d_small_ref,
            rows_ref,
            grads,
            chances,
            kept,
            sums,
            flats,
        )
        z_back(slots).start()

    @pl.when(used <= HALF)
    def few():
        run(HALF)

    @pl.when(used > HALF)
    def many():
        run(ROOM)

    if packed:
        me = index_ref[0]
        count = d_small_ref.shape[0] // 4
        early, late = [], []
        for k in range(4):
            m = jnp.bitwise_xor(me, k)
            quarter = pl.ds(pl.multiple_of(m * 784, 8), 784)
            share = pl.ds(pl.multiple_of(m * count, 8), count)
            early.append((d_encoder_ref.at[quarter], parts[k].at[pl.ds(784, 784)]))
            early.append((d_small_ref.at[share], parts[k].at[pl.ds(1568, count)]))
            late.append((d_split.at[m], parts[k].at[pl.ds(0, 784)]))
        copies = [
            pltpu.make_async_copy(source, target, part_sem.at[number])
            for number, (source, target) in enumerate(early + late)
        ]
        for copy in copies[:8]:
            copy.start()
        pack_split(d_split, *grads)
        for copy in copies[8:]:
            copy.start()
        for copy in copies:
            copy.wait()

    @pl.when(used <= HALF)
    def few_end():
        z_back(HALF).wait()

    @pl.when(used > HALF)
    def many_end():
        z_back(ROOM).wait()


def former(lengths, starts, index, returns, actions, z_three, flat, weights, small_rows, packed):
    smem = pl.BlockSpec(memory_space=pltpu.SMEM)
    vmem = pl.BlockSpec(memory_space=pltpu.VMEM)
    hbm = pl.BlockSpec(memory_space=pltpu.HBM)
    wins = lengths.shape[0]
    canonical = [
        (LAYERS, 3, 128, 128),
        (LAYERS, 128, 128),
        (LAYERS, 128, FF),
        (LAYERS, 1, FF),
        (LAYERS, FF, 128),
    ]
    outs, out_specs = [(28, ROOM, 128), (ROOM + 8, 128)], [hbm, vmem]
    if packed:
        outs += [(1568 + small_rows // 4, 128)] * 4
        out_specs += [hbm] * 4
        scratch = [
            pltpu.VMEM((3136, 128), F32),
            pltpu.VMEM((small_rows, 128), F32),
            pltpu.VMEM((4, 784, 128), F32),
        ]
        scratch += [pltpu.SemaphoreType.DMA((12,))]
        scratch += [pltpu.VMEM(shape, F32) for shape in canonical] * 2
    else:
        outs += [(3136, 128), (small_rows, 128)] + canonical
        out_specs += [vmem] * 7
        scratch = []
    rows = 3 * ROOM
    scratch += [
        pltpu.VMEM((3144, 128), F32),
        pltpu.VMEM((3136, 128), F32),
        pltpu.VMEM((40, 128), F32),
        pltpu.VMEM((wins + 2, 48, 128), F32),
        pltpu.VMEM((ROOM + 32, 128), F32),
        pltpu.VMEM((3584, 256), BF16),
        pltpu.VMEM((LAYERS, 2, 8 * rows, rows), BF16),
        pltpu.VMEM((LAYERS, 8, rows, 128), BF16),
        pltpu.VMEM((4, rows, 128), F32),
        pltpu.VMEM((2, ROOM, 3584), BF16),
        pltpu.VMEM((28, ROOM, 128), F32),
        pltpu.VMEM((28, ROOM, 128), F32),
        pltpu.VMEM((128, 128), F32),
        pltpu.SemaphoreType.DMA((wins + 4,)),
    ]
    return pl.pallas_call(
        partial(former_kernel, packed),
        in_specs=[smem] * 3 + [vmem] * 2 + [hbm] * 2 + [vmem] * len(weights),
        out_specs=out_specs,
        out_shape=[jax.ShapeDtypeStruct(shape, F32) for shape in outs],
        scratch_shapes=scratch,
        compiler_params=pltpu.CompilerParams(vmem_limit_bytes=60 * 1024 * 1024),
        name="transformer_step",
    )(lengths, starts, index, returns, actions, z_three, flat, *weights)


SMALL = [("vectors", 24), ("action_table", 24), ("head", 24), ("loss", 8)]
FIELD_ROWS = 8200
TABLE_AT = CONV_ROWS + 3136 + 17 + ACT
FAST_ROWS = 768


def round_up(number, grain):
    return -(-number // grain) * grain


def chunk_of(rows):
    return max(size for size in range(8, 65, 8) if rows % size == 0)


def mesh_bits(dp_size, mp_size):
    dp_bits = [("dp", k) for k in range(dp_size.bit_length() - 1)]
    mp_bits = [("mp", k) for k in range(mp_size.bit_length() - 1)]
    middle = len(dp_bits) // 3
    return mp_bits[:1], mp_bits[1:], dp_bits[:middle], dp_bits[middle:]


def reduce_kernel(plan, *refs):
    mp_size, devices, wins = plan["mp_size"], plan["devices"], plan["wins"]
    quarter, share = plan["quarter"], plan["share"]
    parts, (conv_ref, rows_ref), refs = refs[:mp_size], refs[mp_size : mp_size + 2], refs[mp_size + 2 :]
    (field_out, split_out, square_out, count_out, loss_out), refs = refs[:5], refs[5:]
    (stage, work, landing, split_total, own_total, conv_total, small_total), refs = (
        refs[:7],
        refs[7:],
    )
    (field, rows_in, before_ref, count_ref, compact, tiles, tile_in), refs = refs[:7], refs[7:]
    load_sem, send_sem, recv_sem, store_sem = refs
    spots = {"dp": lax.axis_index("dp"), "mp": lax.axis_index("mp")}
    cores, ys, xs, zs = plan["bits"]
    bits = cores + ys + xs + zs
    dp_first = xs + zs
    dp_second = zs[:1] + xs + zs[1:]
    slots = iter(range(plan["copies"]))

    def value(bit):
        return lax.rem(lax.div(spots[bit[0]], 1 << bit[1]), 2)

    def partner(bit):
        axis, k = bit
        place = dict(spots)
        place[axis] = spots[axis] + (1 - 2 * value(bit)) * (1 << k)
        return (place["dp"], place["mp"])

    def send(source, target, bit):
        slot = next(slots)
        copy = pltpu.make_async_remote_copy(
            src_ref=source,
            dst_ref=target,
            send_sem=send_sem.at[slot],
            recv_sem=recv_sem.at[slot],
            device_id=partner(bit),
            device_id_type=pl.DeviceIdType.MESH,
        )
        copy.start()
        return copy

    loads = [
        pltpu.make_async_copy(parts[k], stage.at[k], load_sem.at[k]) for k in range(mp_size)
    ]
    loads.append(
        pltpu.make_async_copy(
            conv_ref, work.at[pl.ds(plan["conv"], CONV_ROWS)], load_sem.at[mp_size]
        )
    )
    rows_load = pltpu.make_async_copy(rows_ref, rows_in, load_sem.at[mp_size + 1])
    for load in loads + [rows_load]:
        load.start()

    def wipe(target, start, rows):
        if rows > 0:
            target[start : start + rows] = jnp.zeros((rows, 128), F32)

    wipe(work, plan["conv"] + CONV_ROWS, plan["conv_rows"] - CONV_ROWS)
    wipe(work, plan["split"] + quarter, plan["split_rows"] - quarter)
    wipe(work, plan["own"] + quarter + share, plan["own_rows"] - quarter - share)
    barrier = pltpu.get_barrier_semaphore()
    for bit in bits:
        pl.semaphore_signal(
            barrier, inc=1, device_id=partner(bit), device_id_type=pl.DeviceIdType.MESH
        )
    pl.semaphore_wait(barrier, len(bits))

    def add_into(target, start, pieces, rows):
        chunk = chunk_of(rows)

        def body(turn, carry):
            spot = pl.multiple_of(start + turn * chunk, 8)
            held = target[pl.ds(spot, chunk)]
            for source, at in pieces:
                held = held + source[pl.ds(pl.multiple_of(at + turn * chunk, 8), chunk)]
            target[pl.ds(spot, chunk)] = held
            return carry

        lax.fori_loop(0, rows // chunk, body, 0)

    def copy_rows(target, start, source, at, rows):
        chunk = chunk_of(rows)

        def body(turn, carry):
            held = source[pl.ds(pl.multiple_of(at + turn * chunk, 8), chunk)]
            target[pl.ds(pl.multiple_of(start + turn * chunk, 8), chunk)] = held
            return carry

        lax.fori_loop(0, rows // chunk, body, 0)

    class Stream:
        def __init__(self, base, rows, order, total, total_at):
            self.base, self.size, self.order = base, rows, order
            self.total, self.at = total, total_at
            self.land = base
            self.flight = None
            self.step = 0
            self.start = base

        def halve(self):
            if self.flight is not None:
                copy, half, land, keep = self.flight
                copy.wait()
                add_into(work, keep, [(landing, land)], half)
                self.base, self.size, self.flight = keep, half, None
            if self.step < len(self.order):
                bit = self.order[self.step]
                half = self.size // 2
                mine = value(bit)
                keep = self.base + mine * half
                give = pl.multiple_of(self.base + (1 - mine) * half, 8)
                copy = send(
                    work.at[pl.ds(give, half)], landing.at[pl.ds(self.land, half)], bit
                )
                self.flight = (copy, half, self.land, keep)
                self.land += half
                self.step += 1

        def turn(self):
            self.at = self.at + (self.base - self.start)
            copy_rows(self.total, self.at, work, self.base, self.size)
            self.step = 0

        def double(self):
            if self.flight is not None:
                copy, low = self.flight
                copy.wait()
                self.at, self.size, self.flight = low, self.size * 2, None
            if self.step < len(self.order):
                bit = self.order[len(self.order) - 1 - self.step]
                region = self.total.at[pl.ds(pl.multiple_of(self.at, 8), self.size)]
                copy = send(region, region, bit)
                self.flight = (copy, self.at - value(bit) * self.size)
                self.step += 1

        def squares(self, keep):
            held = work[pl.ds(pl.multiple_of(self.base, 8), self.size)]
            if keep is not None:
                row = lax.broadcasted_iota(jnp.int32, (self.size, 1), 0)
                held = jnp.where(keep(row + self.base), held, 0.0)
            return jnp.sum((held * held).reshape(self.size // 8, 8, 128), axis=0)

    def keep_own(row):
        place = row - plan["own"] - quarter
        return (place < 0) | (place + spots["mp"] * share < 72)

    def sum_parts(target, at, rows):
        copy_rows(work, target, stage.at[0], at, rows)
        add_into(work, target, [(stage.at[k], at) for k in range(1, mp_size)], rows)

    first, second = plan["cut"]
    own = [
        Stream(plan["own"], first, dp_first, own_total, 0),
        Stream(plan["own"] + first, plan["own_rows"] - first, dp_second, own_total, first),
    ]
    split = [
        Stream(plan["split"], second, dp_first, split_total, 0),
        Stream(
            plan["split"] + second, plan["split_rows"] - second, dp_second, split_total, second
        ),
    ]
    conv = Stream(plan["conv"], plan["conv_rows"], bits, conv_total, 0)
    for load in loads:
        load.wait()
    sum_parts(plan["own"], quarter, quarter)
    sum_parts(plan["own"] + quarter, 2 * quarter, share)
    for stream in own + [conv]:
        stream.halve()
    sum_parts(plan["split"], 0, quarter)
    steps = len(dp_first)
    for step in range(steps):
        for stream in own + [conv]:
            stream.halve()
        if step == 0:
            for stream in split:
                stream.halve()
    squares = jnp.zeros((8, 128), F32)
    for stream in own:
        squares = squares + stream.squares(keep_own)
        stream.turn()
        stream.double()
    for step in range(steps):
        for stream in own:
            stream.double()
        conv.halve()
        for stream in split:
            stream.halve()
    gather_bits = ys + cores
    copy_rows(field, CONV_ROWS + spots["mp"] * quarter, own_total, 0, quarter)
    copy_rows(small_total, spots["mp"] * share, own_total, quarter, share)
    flights = {}

    def pass_on(offset, reach):
        for number in range(reach, len(gather_bits)):
            bit = gather_bits[number]
            index = spots["mp"]
            for other in gather_bits:
                if offset & (1 << other[1]):
                    index = index + (1 - 2 * value(other)) * (1 << other[1])
            large = field.at[pl.ds(pl.multiple_of(CONV_ROWS + index * quarter, 8), quarter)]
            small = small_total.at[pl.ds(pl.multiple_of(index * share, 8), share)]
            flights[(offset, number)] = (send(large, large, bit), send(small, small, bit))

    pass_on(0, 0)
    while conv.flight is not None:
        conv.halve()
    squares = squares + conv.squares(None)
    for stream in split:
        squares = squares + stream.squares(None)
        stream.turn()
        stream.double()
    conv.turn()
    conv.double()
    tiles[0] = squares
    tile_flight = send(tiles.at[0], tile_in.at[0], bits[0])
    rows_load.wait()
    stride = ROOM + 8
    notes = rows_in[pl.ds(ROOM, devices, stride=stride), :]
    lane = lax.broadcasted_iota(jnp.int32, (devices, 128), 1)
    columns = [
        jnp.sum(jnp.where(lane == k, notes, 0.0), axis=1, keepdims=True) for k in range(2 * wins)
    ]
    amount = sum(columns[1:wins], columns[0])
    near = lax.broadcasted_iota(jnp.int32, (devices, devices), 0)
    far = lax.broadcasted_iota(jnp.int32, (devices, devices), 1)
    across = jnp.sum(jnp.where(near == far, amount, 0.0), axis=0, keepdims=True)
    before = jnp.sum(jnp.where(far < near, across, 0.0), axis=1, keepdims=True)
    before_ref[...] = jnp.broadcast_to(before, (devices, 128))
    count_ref[...] = jnp.broadcast_to(amount, (devices, 128))
    whole = jnp.sum(amount, axis=0, keepdims=True)
    count_out[...] = jnp.broadcast_to(whole, (8, 128))
    compact[...] = jnp.zeros((FAST_ROWS, 128), F32)
    row_place = lax.broadcasted_iota(jnp.int32, (FAST_ROWS, 128), 0).astype(F32)
    row_place = row_place - lax.broadcasted_iota(jnp.int32, (FAST_ROWS, 128), 1).astype(F32)
    lane_place = lax.broadcasted_iota(jnp.int32, (1, 128), 1).astype(F32)

    def collect(step, carry):
        picks, held = [], []
        for k in range(2):
            device = step * 2 + k
            there = before_ref[pl.ds(device, 1)]
            there = jnp.where(lane_place < count_ref[pl.ds(device, 1)], there, -10000.0)
            picks.append(jnp.where(row_place == there, 1.0, 0.0).astype(BF16))
            held.append(pair(rows_in[pl.ds(pl.multiple_of(device * stride, 8), ROOM)]))
        found = dot(jnp.concatenate(picks, axis=1), jnp.concatenate(held, axis=0))
        compact[...] += fold_pair(found)
        return carry

    lax.fori_loop(0, devices // 2, collect, 0)
    table_of = []
    for k in range(FAST_ROWS // 128):
        place = lax.broadcasted_iota(jnp.int32, (devices, 128), 1).astype(F32) + 128.0 * k
        begin = before
        spot = jnp.full((1, 128), -1.0, F32)
        for w in range(wins):
            away = place - begin
            inside = (away >= 0.0) & (away < columns[w])
            found = jnp.where(inside, columns[wins + w] + away + 1.0, 0.0)
            spot = spot + jnp.sum(found, axis=0, keepdims=True)
            begin = begin + columns[w]
        table_of.append(spot)
    rounds = 1

    def advance():
        nonlocal tile_flight, rounds
        for stream in split + [conv]:
            stream.double()
        if rounds <= len(bits):
            tile_flight.wait()
            tiles[rounds] = tiles[rounds - 1] + tile_in[rounds - 1]
            if rounds < len(bits):
                tile_flight = send(tiles.at[rounds], tile_in.at[rounds], bits[rounds])
            rounds += 1

    advance()
    held = pair(compact[...])
    chunk = 512
    time_squares = jnp.zeros((8, 128), F32)
    for turn in range(TSTEPS // chunk):
        place = (lax.broadcasted_iota(jnp.int32, (chunk, 128), 0) + turn * chunk).astype(F32)
        picks = [jnp.where(place == spot, 1.0, 0.0).astype(BF16) for spot in table_of]
        result = fold_pair(dot(jnp.concatenate(picks, axis=1), held))
        field[TABLE_AT + turn * chunk : TABLE_AT + (turn + 1) * chunk] = result
        time_squares = time_squares + jnp.sum(
            (result * result).reshape(chunk // 8, 8, 128), axis=0
        )
        if turn % 2 == 1:
            advance()
    square_out[8:16] = time_squares
    end = TABLE_AT + TSTEPS + ACT
    field[end:FIELD_ROWS] = jnp.zeros((FIELD_ROWS - end, 128), F32)
    while rounds <= len(bits) or conv.flight is not None:
        advance()
    square_out[0:8] = tiles[len(bits)]
    field[0:CONV_ROWS] = conv_total[0:CONV_ROWS]
    late = CONV_ROWS + 3136
    table_end = TABLE_AT + TSTEPS
    low, high = TABLE_AT // 8 * 8 + 8, table_end // 8 * 8

    def store(source, target, number):
        copy = pltpu.make_async_copy(source, target, store_sem.at[number])
        copy.start()
        return copy

    def store_field(start, stop, number):
        rows = pl.ds(start, stop - start)
        return store(field.at[rows], field_out.at[rows], number)

    stores = [
        store_field(0, CONV_ROWS, 0),
        store_field(low, high, 1),
        store(split_total.at[pl.ds(0, quarter)], split_out, 2),
    ]
    held_offsets = [0]
    for number, bit in enumerate(gather_bits):
        arrived = []
        for offset in held_offsets:
            for flight in flights[(offset, number)]:
                flight.wait()
            arrived.append(offset | (1 << bit[1]))
        held_offsets += arrived
        for offset in arrived:
            pass_on(offset, number + 1)
    for at, name_at, count in [(late, 0, 17), (late + 17, 24, ACT), (table_end, 48, ACT)]:
        field[at : at + count] = small_total[name_at : name_at + count]
    loss_out[...] = small_total[72:80]
    stores += [
        store_field(CONV_ROWS, late, 3),
        store_field(late, low, 4),
        store_field(high, FIELD_ROWS, 5),
    ]
    for copy in stores:
        copy.wait()


def reduce_all(parts, conv, rows, dp_size, mp_size, wins):
    bits = mesh_bits(dp_size, mp_size)
    steps = sum(len(part) for part in bits)
    dp_steps = dp_size.bit_length() - 1
    devices = dp_size * mp_size
    quarter = 3136 // mp_size
    share = parts[0].shape[0] - 2 * quarter
    dp_grain = 8 * dp_size
    own_rows = round_up(quarter + share, dp_grain)
    split_rows = round_up(quarter, dp_grain)
    conv_rows = round_up(CONV_ROWS, 8 * devices)
    places, at = {}, 0
    for name, size in [("split", split_rows), ("own", own_rows), ("conv", conv_rows)]:
        places[name] = at
        at += size
    cut = (round_up(own_rows // 2, dp_grain), round_up(split_rows // 2, dp_grain))
    copies = 4 * 2 * dp_steps + 2 * steps + steps + 2 * (mp_size - 1)
    plan = dict(
        places,
        mp_size=mp_size,
        devices=devices,
        wins=wins,
        quarter=quarter,
        share=share,
        bits=bits,
        copies=copies,
        split_rows=split_rows,
        own_rows=own_rows,
        conv_rows=conv_rows,
        cut=cut,
    )
    vmem = pl.BlockSpec(memory_space=pltpu.VMEM)
    hbm = pl.BlockSpec(memory_space=pltpu.HBM)
    any_spec = pl.BlockSpec(memory_space=pl.ANY)
    rows = rows.reshape(devices * (ROOM + 8), 128)
    return pl.pallas_call(
        partial(reduce_kernel, plan),
        in_specs=[any_spec] * (mp_size + 2),
        out_specs=[hbm, hbm, vmem, vmem, vmem],
        out_shape=[
            jax.ShapeDtypeStruct((FIELD_ROWS, 128), F32),
            jax.ShapeDtypeStruct((quarter, 128), F32),
            jax.ShapeDtypeStruct((16, 128), F32),
            jax.ShapeDtypeStruct((8, 128), F32),
            jax.ShapeDtypeStruct((8, 128), F32),
        ],
        scratch_shapes=[
            pltpu.VMEM((mp_size, 2 * quarter + share, 128), F32),
            pltpu.VMEM((at, 128), F32),
            pltpu.VMEM((at, 128), F32),
            pltpu.VMEM((split_rows, 128), F32),
            pltpu.VMEM((own_rows, 128), F32),
            pltpu.VMEM((conv_rows, 128), F32),
            pltpu.VMEM((share * mp_size, 128), F32),
            pltpu.VMEM((FIELD_ROWS, 128), F32),
            pltpu.VMEM(rows.shape, F32),
            pltpu.VMEM((devices, 128), F32),
            pltpu.VMEM((devices, 128), F32),
            pltpu.VMEM((FAST_ROWS, 128), F32),
            pltpu.VMEM((steps + 1, 8, 128), F32),
            pltpu.VMEM((steps, 8, 128), F32),
            pltpu.SemaphoreType.DMA((mp_size + 2,)),
            pltpu.SemaphoreType.DMA((copies,)),
            pltpu.SemaphoreType.DMA((copies,)),
            pltpu.SemaphoreType.DMA((6,)),
        ],
        compiler_params=pltpu.CompilerParams(
            collective_id=1, has_side_effects=True, vmem_limit_bytes=40 * 1024 * 1024
        ),
        name="reduce_gradients",
    )(*parts, conv, rows)


FLAT_ROWS = 7896
BLOCK_ROWS = 1024
LATE = 609


def adam_kernel(
    field_ref,
    split_ref,
    square_ref,
    count_ref,
    loss_ref,
    weight_ref,
    first_ref,
    second_ref,
    split_weight_ref,
    split_first_ref,
    split_second_ref,
    new_ref,
    new_first_ref,
    new_second_ref,
    low_ref,
    split_new_ref,
    split_new_first_ref,
    split_new_second_ref,
    scalar_ref,
    pulled,
    factor_ref,
    pull_sem,
):
    step = pl.program_id(0)
    last = pl.num_programs(0) - 1
    lane = lax.broadcasted_iota(jnp.int32, (1, 128), 1)

    def pull(block, slot):
        start = pl.multiple_of(block * BLOCK_ROWS, BLOCK_ROWS)
        return pltpu.make_async_copy(
            field_ref.at[pl.ds(start, BLOCK_ROWS + 8)], pulled.at[slot], pull_sem.at[slot]
        )

    def update(weights, first, second, grads):
        first = beta_first * first + (1 - beta_first) * grads
        second = beta_second * second + (1 - beta_second) * grads * grads
        fix_one = 1.0 / (1 - beta_first**STEP)
        fix_two = 1.0 / (1 - beta_second**STEP)
        weights = weights - learn_rate * (
            first * fix_one / (jnp.sqrt(second * fix_two) + adam_epsilon) + weight_decay * weights
        )
        return weights, first, second

    def sum_of(tile):
        held = jnp.sum(jnp.sum(tile, axis=0, keepdims=True), axis=1, keepdims=True)
        return jnp.broadcast_to(held, (1, 128))

    slot = lax.rem(step, 2)

    @pl.when(step == 0)
    def prepare():
        pull(0, 0).start()
        count = count_ref[0:1]
        seed = 1.0 / count
        norm = jnp.sqrt(sum_of(square_ref[...])) * seed
        factor = jnp.minimum(1.0, clip_limit / (norm + 1e-06)) * seed
        factor_ref[...] = jnp.broadcast_to(factor, (8, 128))
        loss = loss_ref[0:1]
        row = lax.broadcasted_iota(jnp.int32, (8, 128), 0)
        scalar_ref[...] = jnp.where(row == 0, norm, jnp.where(row == 1, loss, count))

    @pl.when(step < last)
    def ahead():
        pull(step + 1, 1 - slot).start()

    @pl.when(step == last)
    def split():
        rows = split_weight_ref.shape[0]
        outs = update(
            split_weight_ref[...],
            split_first_ref[...],
            split_second_ref[...],
            split_ref[0:rows] * factor_ref[0:1],
        )
        split_new_ref[...], split_new_first_ref[...], split_new_second_ref[...] = outs

    pull(step, slot).wait()
    early = pulled[slot, 0:BLOCK_ROWS]
    own = pltpu.roll(pulled[slot, 7 : BLOCK_ROWS + 7], 32, 1)
    before = pltpu.roll(pulled[slot, 6 : BLOCK_ROWS + 6], 32, 1)
    row = lax.broadcasted_iota(jnp.int32, (BLOCK_ROWS, 1), 0) + step * BLOCK_ROWS
    grads = jnp.where(lane < 32, jnp.where(row == LATE, early, before), own)
    grads = jnp.where(row < LATE, early, grads)
    outs = update(weight_ref[...], first_ref[...], second_ref[...], grads * factor_ref[0:1])
    new_ref[...], new_first_ref[...], new_second_ref[...] = outs
    low_ref[...] = outs[0].astype(BF16)


def adam_all(field, split_grad, square, count, loss, shared, split):
    grid = -(-FLAT_ROWS // BLOCK_ROWS)
    flat_spec = pl.BlockSpec((BLOCK_ROWS, 128), lambda i: (i, 0))
    split_rows = split[0].shape[0]

    def whole(shape):
        return pl.BlockSpec(shape, lambda i: (0,) * len(shape))

    split_spec = whole((split_rows, 128))
    shared_out = jax.ShapeDtypeStruct((FLAT_ROWS, 128), F32)
    split_out = jax.ShapeDtypeStruct((split_rows, 128), F32)
    return pl.pallas_call(
        adam_kernel,
        grid=(grid,),
        in_specs=[
            pl.BlockSpec(memory_space=pl.ANY),
            whole(split_grad.shape),
            whole((16, 128)),
            whole((8, 128)),
            whole((8, 128)),
            flat_spec,
            flat_spec,
            flat_spec,
            split_spec,
            split_spec,
            split_spec,
        ],
        out_specs=[flat_spec] * 4 + [split_spec] * 3 + [whole((8, 128))],
        out_shape=[shared_out] * 3
        + [jax.ShapeDtypeStruct((FLAT_ROWS, 128), BF16)]
        + [split_out] * 3
        + [jax.ShapeDtypeStruct((8, 128), F32)],
        scratch_shapes=[
            pltpu.VMEM((2, BLOCK_ROWS + 8, 128), F32),
            pltpu.VMEM((8, 128), F32),
            pltpu.SemaphoreType.DMA((2,)),
        ],
        compiler_params=pltpu.CompilerParams(vmem_limit_bytes=48 * 1024 * 1024),
        name="adam_update",
    )(field, split_grad, square, count, loss, *shared, *split)


def valid_slots(lengths, steps):
    ends = jnp.cumsum(lengths)
    slot = jnp.arange(ROOM, dtype=jnp.int32)
    past = slot[:, None] >= ends[None, :-1]
    begin = jnp.sum(jnp.where(past, lengths[None, :-1], 0), axis=1)
    return past, jnp.minimum(slot - begin, steps - 1), ends[-1]


def per_device(
    frames,
    returns,
    actions,
    starts,
    lengths,
    shared_weights,
    shared_first,
    shared_second,
    split_weights,
    split_first,
    split_second,
):
    dp_size, mp_size = lax.axis_size("dp"), lax.axis_size("mp")
    narrow = D // mp_size
    hidden_width = FF // mp_size
    wins, steps = returns.shape
    width = split_weights.shape[0]
    split_rows = width // 128
    packed = narrow == 32
    own_rows = split_weights.reshape(split_rows, 128)
    split_all = lax.all_gather(own_rows, "mp", axis=0)
    flat = shared_weights.reshape(FLAT_ROWS, 128)
    picked, z_one, z_two, z_three = conv_forward(lengths, frames, flat)
    if packed:
        weights = [split_all]
    else:
        layers, layers_back = jax.vjp(
            lambda held: assemble(held, mp_size, narrow, hidden_width), split_all.reshape(-1)
        )
        weights = [
            jnp.stack([layer["qkv"].transpose(1, 0, 2) for layer in layers]),
            jnp.stack([layer["output"] for layer in layers]),
            jnp.stack([layer["up"] for layer in layers]),
            jnp.stack([layer["up_bias"][None] for layer in layers]),
            jnp.stack([layer["down"] for layer in layers]),
        ]
    small_rows = round_up(sum(rows for name, rows in SMALL), 8 * mp_size)
    index = lax.axis_index("mp").reshape(1)
    results = former(
        lengths, starts, index, returns, actions, z_three, flat, weights, small_rows, packed
    )
    d_three, rows = results[:2]
    rows_all = lax.all_gather(rows, ("dp", "mp"), axis=0)
    quarter = 3136 // mp_size
    if packed:
        parts = results[2:]
    else:
        d_encoder, d_small, d_qkv, d_output, d_up, d_up_bias, d_down = results[2:]
        grad_layers = [
            dict(
                qkv=d_qkv[layer].transpose(1, 0, 2),
                output=d_output[layer],
                up=d_up[layer],
                up_bias=d_up_bias[layer, 0],
                down=d_down[layer],
            )
            for layer in range(LAYERS)
        ]
        gathered = layers_back(grad_layers)[0].reshape(mp_size, split_rows, 128)
        gathered = jnp.pad(gathered, ((0, 0), (0, quarter - split_rows), (0, 0)))
        encoder = d_encoder.reshape(mp_size, quarter, 128)
        small = d_small.reshape(mp_size, -1, 128)
        every = jnp.concatenate([gathered, encoder, small], axis=1)
        parts = [
            lax.dynamic_index_in_dim(every, jnp.bitwise_xor(index[0], k), 0, keepdims=False)
            for k in range(mp_size)
        ]
    arrived = [parts[0]]
    for k in range(1, mp_size):
        turn = [(index, index ^ k) for index in range(mp_size)]
        arrived.append(lax.ppermute(parts[k], "mp", turn))
    d_conv = conv_backward(lengths, picked, z_one, z_two, d_three, flat)
    field, split_sum, square, count, loss = reduce_all(
        arrived, d_conv, rows_all, dp_size, mp_size, wins
    )

    def whole(operands):
        field, square = operands
        past, moment, used = valid_slots(lengths, steps)
        gaps = starts[1:] - starts[:-1]
        spot = moment + starts[0] + jnp.sum(jnp.where(past, gaps[None, :], 0), axis=1)
        spot = jnp.where(jnp.arange(ROOM) < used, spot, 0)
        table = jnp.zeros((TSTEPS, D), F32).at[spot].add(rows[:ROOM])
        table = lax.psum(table, ("dp", "mp"))
        field = lax.dynamic_update_slice(field, table, (TABLE_AT, 0))
        late = jnp.sum((table * table).reshape(-1, 8, 128), axis=0)
        return field, jnp.concatenate([square[:8], late])

    field, square = lax.cond(
        count[0, 0] > FAST_ROWS, whole, lambda operands: operands, (field, square)
    )
    shared_view = [a.reshape(FLAT_ROWS, 128) for a in (shared_weights, shared_first, shared_second)]
    split_view = [a.reshape(split_rows, 128) for a in (split_weights, split_first, split_second)]
    updated = adam_all(
        field, split_sum, square, count, loss, shared_view, split_view
    )
    shared_out = [a.reshape(-1) for a in updated[:4]]
    split_out = [a.reshape(-1) for a in updated[4:7]]
    scalars = updated[7]
    return (
        *shared_out,
        *split_out,
        split_out[0].astype(BF16),
        scalars[0, 0],
        scalars[1, 0],
        scalars[2, 0],
    )


def solution(mesh):
    return jax.shard_map(
        per_device,
        mesh=mesh,
        in_specs=(
            P(("dp", "mp"), None, None, None, None),
            P(("dp", "mp"), None),
            P(("dp", "mp"), None),
            P(("dp", "mp")),
            P(("dp", "mp")),
            P(),
            P(),
            P(),
            P("mp"),
            P("mp"),
            P("mp"),
        ),
        out_specs=(P(), P(), P(), P(), P("mp"), P("mp"), P("mp"), P("mp"), P(), P(), P()),
        check_vma=False,
    )
```

```python
from functools import partial
import math

import jax
import jax.numpy as jnp
from jax import lax
from jax.experimental import pallas as pl
from jax.experimental.pallas import tpu as pltpu
from jax.sharding import PartitionSpec as P

D = 128
FF = 512
ACT = 18
C1 = 32
C2 = 64
TSTEPS = 4096
LAYERS = 2
STEP = 10
HD = 16


clip_limit = 0.1
learn_rate = 0.05
beta_first = 0.9
beta_second = 0.95
adam_epsilon = 1e-08
weight_decay = 0.1


def span_layout(narrow, hidden):
    return [
        ("qkv", (D, 3, narrow)),
        ("output", (narrow, D)),
        ("up", (D, hidden)),
        ("up_bias", (hidden,)),
        ("down", (hidden, D)),
    ]


def assemble(flat, copies, narrow, hidden):
    layout = span_layout(narrow, hidden)
    width = sum((math.prod(shape) for name, shape in layout))
    blocks = flat.reshape(copies, LAYERS, width)
    layers = []
    for layer in range(LAYERS):
        offset = 0
        pieces = {}
        for name, shape in layout:
            count = math.prod(shape)
            pieces[name] = blocks[:, layer, offset : offset + count].reshape((copies,) + shape)
            offset += count
        layers.append(
            {
                "qkv": jnp.moveaxis(pieces["qkv"], 0, 2).reshape(D, 3, copies * narrow),
                "output": pieces["output"].reshape(copies * narrow, D),
                "up": jnp.moveaxis(pieces["up"], 0, 1).reshape(D, copies * hidden),
                "up_bias": pieces["up_bias"].reshape(copies * hidden),
                "down": pieces["down"].reshape(copies * hidden, D),
            }
        )
    return layers


GROUP = 16
CONV_ROWS = 616
ROOM = 128
HALF = 64
BF16 = jnp.bfloat16
F32 = jnp.float32


def gelu_value(x):
    inner = 0.7978845608028654 * (x + 0.044715 * (x * x * x))
    return 0.5 * x * (1.0 + jnp.tanh(inner))


def gelu_both(x):
    square = x * x
    turn = jnp.tanh(0.7978845608028654 * x * (1.0 + 0.044715 * square))
    half = 0.5 * (1.0 + turn)
    slope = half + 0.5 * x * (1.0 - turn * turn) * (
        0.7978845608028654 * (1.0 + 3 * 0.044715 * square)
    )
    return x * half, slope


def two_parts(x):
    high = x.astype(BF16)
    return high, (x - high.astype(F32)).astype(BF16)


def pair(x):
    return jnp.concatenate(two_parts(x), axis=-1)


def fold_pair(x):
    return x[:, :128] + x[:, 128:]


def dot(a, b):
    return lax.dot_general(a, b, (((1,), (0,)), ((), ())), preferred_element_type=F32)


def dot_rows(a, b):
    return lax.dot_general(a, b, (((0,), (0,)), ((), ())), preferred_element_type=F32)


def lanes():
    return lax.broadcasted_iota(jnp.int32, (1, 128), 1)


def conv_biases(flat_ref):
    lane = lanes()
    one = jnp.where(lane < 32, flat_ref[64:65], 0.0)
    one = one + pltpu.roll(one, 32, 1)
    one = one + pltpu.roll(one, 64, 1)
    two = jnp.where(lane < 64, pltpu.roll(flat_ref[320:321], 96, 1), 0.0)
    two = two + pltpu.roll(two, 64, 1)
    three = jnp.where(
        lane < 32,
        pltpu.roll(flat_ref[608:609], 32, 1),
        jnp.where(lane < 64, pltpu.roll(flat_ref[609:610], 32, 1), 0.0),
    )
    three = three + pltpu.roll(three, 64, 1)
    return one, two, three


def shifted(ref, start, rows, lane):
    first = pltpu.roll(ref[start : start + rows], 128 - lane, 1)
    second = pltpu.roll(ref[start + 1 : start + 1 + rows], 128 - lane, 1)
    return jnp.where(lanes() < 128 - lane, first, second)


def spread_one(flat_ref, put):
    halves = [jnp.transpose(flat_ref[pl.ds(side, 32, stride=2), :]) for side in range(2)]
    turned = jnp.concatenate(halves, axis=0)
    lane = lax.broadcasted_iota(jnp.int32, (8, 128), 1)
    row = lax.broadcasted_iota(jnp.int32, (8, 128), 0)
    low = row < 4
    column = lax.shift_right_logical(lane, 5)
    for ky in range(8):
        for c in range(4):
            held = turned[c * 64 + ky * 8 : c * 64 + ky * 8 + 8]
            wide = jnp.concatenate([held] * 4, axis=1)
            flipped = jnp.concatenate([wide[4:], wide[:4]], axis=0)
            zero = jnp.zeros((8, 128), F32)
            first = jnp.where(column == 0, wide, jnp.where((column == 1) & ~low, flipped, zero))
            second = jnp.where(
                column == 2,
                wide,
                jnp.where(((column == 1) & low) | ((column == 3) & ~low), flipped, zero),
            )
            third = jnp.where((column == 3) & low, flipped, zero)
            put(ky * 128 + c * 32, jnp.concatenate([first, second, third, zero], axis=0))


def spread_two(flat_ref, rows_ref, turned, put):
    lane = lax.broadcasted_iota(jnp.int32, (32, 128), 1)
    rows_ref[0:256] = shifted(flat_ref, 64, 256, 32)
    for j in range(4):
        block = jnp.transpose(rows_ref[pl.ds(j, 64, stride=4), :])
        turned[j * 128 : (j + 1) * 128] = jnp.concatenate([block, block], axis=1)
    for ky in range(4):
        rows = [turned[pl.ds(ky * 4 + kx, 32, stride=16)] for kx in range(4)]
        for i in range(8):
            left = rows[i] if i < 4 else jnp.zeros((32, 128), F32)
            right = rows[i - 2] if 2 <= i < 6 else jnp.zeros((32, 128), F32)
            put(ky * 256 + i * 32, jnp.where(lane < 64, left, right))


def spread_three(flat_ref, rows_ref, turned, put):
    lane = lax.broadcasted_iota(jnp.int32, (64, 128), 1)
    side = lax.broadcasted_iota(jnp.int32, (32, 128), 1) < 64
    rows_ref[0:288] = shifted(flat_ref, 320, 288, 96)
    nine = [rows_ref[pl.ds(k, 32, stride=9), :] for k in range(9)]
    flips = [pltpu.roll(nine[4 + k], 64, 1) for k in range(5)]
    for j in range(5):
        wide = min(128, 576 - j * 128)
        rows_ref[pl.ds(0, 32, stride=2), :] = nine[j]
        rows_ref[pl.ds(1, 32, stride=2), :] = (
            jnp.where(side, flips[j], flips[j + 1]) if j < 4 else flips[4]
        )
        block = jnp.transpose(rows_ref[0:64])[0:wide]
        turned[j * 128 : j * 128 + wide] = jnp.concatenate([block, block], axis=1)
    for ky in range(3):
        rows = [turned[pl.ds(ky * 3 + kx, 64, stride=9)] for kx in range(3)]
        for i in range(4):
            left = rows[i] if i < 3 else jnp.zeros((64, 128), F32)
            right = rows[i - 1] if i >= 1 else jnp.zeros((64, 128), F32)
            put(ky * 256 + i * 64, jnp.where(lane < 64, left, right))


def last_masks():
    return lanes() < 64


def conv_forward_kernel(
    lengths_ref,
    frames_ref,
    shared_ref,
    picked_ref,
    z_one_ref,
    z_two_ref,
    z_three_ref,
    flat_ref,
    held,
    wide,
    picked,
    z_one,
    z_two,
    z_three,
    h_one,
    h_two,
    w_one,
    w_two,
    w_three,
    choose,
    rows_ref,
    turned,
    frame_sem,
    out_sem,
):
    wins = lengths_ref.shape[0]
    steps = frames_ref.shape[1]
    used = jnp.int32(0)
    for w in range(wins):
        used = used + lengths_ref[w]
    groups = lax.div(used + (GROUP - 1), GROUP)

    def frame_copy(group, spot, slot):
        state = jnp.minimum(group * GROUP + spot, used - 1)
        window, begin, end = jnp.int32(0), jnp.int32(0), jnp.int32(0)
        for w in range(wins - 1):
            end = end + lengths_ref[w]
            window = jnp.where(state >= end, w + 1, window)
            begin = jnp.where(state >= end, end, begin)
        return pltpu.make_async_copy(
            frames_ref.at[window, state - begin], held.at[slot, spot], frame_sem.at[slot, spot]
        )

    def fetch(group, slot):
        def one(spot, carry):
            frame_copy(group, spot, slot).start()
            return carry

        lax.fori_loop(0, GROUP, one, 0)

    weights = pltpu.make_async_copy(
        shared_ref.at[pl.ds(0, CONV_ROWS)], flat_ref, out_sem.at[4]
    )
    weights.start()
    fetch(0, 0)
    h_one[...] = jnp.zeros(h_one.shape, BF16)

    def put_one(row, block):
        w_one[row : row + 32] = pair(block)

    def put_two(row, block):
        w_two[row : row + 32] = pair(block)

    def put_three(row, block):
        w_three[row : row + 64] = pair(block)

    weights.wait()
    spread_one(flat_ref, put_one)
    spread_two(flat_ref, rows_ref, turned, put_two)
    spread_three(flat_ref, rows_ref, turned, put_three)
    bias_one, bias_two, bias_three = conv_biases(flat_ref)
    row = lax.broadcasted_iota(jnp.int32, (128, 640), 0)
    column = lax.broadcasted_iota(jnp.int32, (128, 640), 1)
    place = jnp.bitwise_and(column, 31)
    channel = jnp.bitwise_and(lax.shift_right_logical(column, 5), 3)
    block = lax.shift_right_logical(column, 7)
    right = (row == 16 * block + place) & (place < 20)
    for c in range(4):
        choose[c * 128 : (c + 1) * 128] = jnp.where(right & (channel == c), 1.0, 0.0).astype(BF16)

    def one_group(group, carry):
        slot = lax.rem(group, 2)

        @pl.when(group + 1 < groups)
        def ahead():
            fetch(group + 1, 1 - slot)

        def lay(step, carry):
            spots = [step * 4 + k for k in range(4)]
            for spot in spots:
                frame_copy(group, spot, slot).wait()
            for spot in spots:
                image = held[slot, spot].astype(F32).reshape(336, 84)
                image = jnp.concatenate([image, jnp.zeros((336, 44), F32)], axis=1)
                wide[pl.ds(spot, 336, stride=GROUP), :] = image
            return carry

        lax.fori_loop(0, GROUP // 4, lay, 0)
        for part in range(3):
            rows = wide[part * 1792 : (part + 1) * 1792].reshape(28, 4, GROUP, 128)
            rows = [rows[:, c].reshape(448, 128).astype(BF16) for c in range(4)]
            result = dot(jnp.concatenate(rows, axis=1), choose[...])
            picked[part * 7 : (part + 1) * 7] = result.astype(BF16).reshape(7, 4, GROUP, 640)
        keep_picked = pltpu.make_async_copy(picked, picked_ref.at[group], out_sem.at[0])
        keep_picked.start()
        for q in range(5):
            pieces = [
                picked[j : j + 20, b, :, q * 128 : (q + 1) * 128].reshape(20 * GROUP, 128)
                for j in range(2)
                for b in range(4)
            ]
            z = fold_pair(dot(jnp.concatenate(pieces, axis=1), w_one[...])) + bias_one
            z_one[:, :, q] = z.reshape(10, 2, GROUP, 128)
            high, low = two_parts(gelu_value(z))
            h_one[0, :, :, q] = high.reshape(10, 2, GROUP, 128)
            h_one[1, :, :, q] = low.reshape(10, 2, GROUP, 128)
        keep_one = pltpu.make_async_copy(z_one, z_one_ref.at[group], out_sem.at[1])
        keep_one.start()
        total = jnp.zeros((45 * GROUP, 128), F32)
        for part in range(2):
            pieces = []
            for j in range(2):
                for b in range(2):
                    pieces.append(h_one[part, j : j + 9, b, 0:5].reshape(45 * GROUP, 128))
                    pieces.append(h_one[part, j : j + 9, b, 1:6].reshape(45 * GROUP, 128))
            total = total + fold_pair(dot(jnp.concatenate(pieces, axis=1), w_two[...]))
        z = (total + bias_two).reshape(9, 5, GROUP, 128)
        z_two[...] = z
        h = gelu_value(z)
        high, low = two_parts(h)
        h_two[0] = high
        h_two[1] = low
        edge = jnp.where(last_masks(), h[:, 4].reshape(9 * GROUP, 128), 0.0)
        high, low = two_parts(edge)
        h_two[0, :, 4] = high.reshape(9, GROUP, 128)
        h_two[1, :, 4] = low.reshape(9, GROUP, 128)
        keep_two = pltpu.make_async_copy(z_two, z_two_ref.at[group], out_sem.at[2])
        keep_two.start()
        total = jnp.zeros((28 * GROUP, 128), F32)
        for part in range(2):
            pieces = []
            for ky in range(3):
                pieces.append(h_two[part, ky : ky + 7, 0:4].reshape(28 * GROUP, 128))
                pieces.append(h_two[part, ky : ky + 7, 1:5].reshape(28 * GROUP, 128))
            total = total + fold_pair(dot(jnp.concatenate(pieces, axis=1), w_three[...]))
        z_three[...] = (total + bias_three).reshape(28, GROUP, 128)
        spot = pl.multiple_of(group * GROUP, GROUP)
        keep_three = pltpu.make_async_copy(
            z_three, z_three_ref.at[:, pl.ds(spot, GROUP)], out_sem.at[3]
        )
        keep_three.start()
        keep_picked.wait()
        keep_one.wait()
        keep_two.wait()
        keep_three.wait()
        return carry

    lax.fori_loop(0, groups, one_group, 0)


def conv_forward(lengths, frames, flat):
    most = ROOM // GROUP
    any_spec = pl.BlockSpec(memory_space=pl.ANY)
    hbm = pl.BlockSpec(memory_space=pltpu.HBM)
    return pl.pallas_call(
        conv_forward_kernel,
        in_specs=[
            pl.BlockSpec(memory_space=pltpu.SMEM),
            any_spec,
            any_spec,
        ],
        out_specs=[hbm] * 4,
        out_shape=[
            jax.ShapeDtypeStruct((most, 21, 4, GROUP, 640), BF16),
            jax.ShapeDtypeStruct((most, 10, 2, 5, GROUP, 128), F32),
            jax.ShapeDtypeStruct((most, 9, 5, GROUP, 128), F32),
            jax.ShapeDtypeStruct((28, ROOM, 128), F32),
        ],
        scratch_shapes=[
            pltpu.VMEM((CONV_ROWS, 128), F32),
            pltpu.VMEM((2, GROUP, 84, 4, 84), BF16),
            pltpu.VMEM((336 * GROUP, 128), F32),
            pltpu.VMEM((21, 4, GROUP, 640), BF16),
            pltpu.VMEM((10, 2, 5, GROUP, 128), F32),
            pltpu.VMEM((9, 5, GROUP, 128), F32),
            pltpu.VMEM((28, GROUP, 128), F32),
            pltpu.VMEM((2, 10, 2, 6, GROUP, 128), BF16),
            pltpu.VMEM((2, 9, 5, GROUP, 128), BF16),
            pltpu.VMEM((1024, 256), BF16),
            pltpu.VMEM((1024, 256), BF16),
            pltpu.VMEM((768, 256), BF16),
            pltpu.VMEM((512, 640), BF16),
            pltpu.VMEM((288, 128), F32),
            pltpu.VMEM((576, 128), F32),
            pltpu.SemaphoreType.DMA((2, GROUP)),
            pltpu.SemaphoreType.DMA((5,)),
        ],
        compiler_params=pltpu.CompilerParams(vmem_limit_bytes=48 * 1024 * 1024),
        name="conv_forward",
    )(lengths, frames.transpose(0, 1, 3, 2, 4), flat)


def gather_one(total, out):
    lane = lax.broadcasted_iota(jnp.int32, (32, 128), 1)
    halves = [jnp.zeros((32, 128), F32) for side in range(2)]
    for ky in range(8):
        held = total[0:128, ky * 128 : (ky + 1) * 128] + total[128:256, ky * 128 : (ky + 1) * 128]
        summed = held[0:32]
        for o in range(1, 4):
            summed = summed + pltpu.roll(held[32 * o : 32 * o + 32], 128 - 4 * o, 1)
        for c in range(4):
            spot = (c % 2) * 64 + ky * 8
            shift = (spot - c * 32) % 128
            moved = pltpu.roll(summed, shift, 1) if shift else summed
            inside = (lane >= spot) & (lane < spot + 8)
            halves[c // 2] = halves[c // 2] + jnp.where(inside, moved, 0.0)
    for side in range(2):
        out[pl.ds(side, 32, stride=2), :] = halves[side]


def gather_two(total, turned, rows_ref, out):
    lane = lax.broadcasted_iota(jnp.int32, (64, 128), 1)
    for ky in range(4):
        near = total[0:128, ky * 256 : ky * 256 + 128] + total[128:256, ky * 256 : ky * 256 + 128]
        far = (
            total[0:128, ky * 256 + 128 : ky * 256 + 256]
            + total[128:256, ky * 256 + 128 : ky * 256 + 256]
        )
        summed = near[0:64] + jnp.where(
            lane < 64, pltpu.roll(near[64:128], 64, 1), pltpu.roll(far[64:128], 64, 1)
        )
        flipped = jnp.transpose(jnp.concatenate([summed, jnp.zeros((64, 128), F32)], axis=0))
        for kx in range(4):
            turned[pl.ds(ky * 4 + kx, 32, stride=16), :] = flipped[kx * 32 : (kx + 1) * 32]
    rows_ref[0:8] = jnp.zeros((8, 128), F32)
    rows_ref[264:272] = jnp.zeros((8, 128), F32)
    for j in range(4):
        block = jnp.transpose(turned[j * 128 : (j + 1) * 128])[0:64]
        rows_ref[pl.ds(8 + j, 64, stride=4), :] = block
    own = pltpu.roll(rows_ref[8:265], 32, 1)
    before = pltpu.roll(rows_ref[7:264], 32, 1)
    out[64:321] = jnp.where(lanes() >= 32, own, before)


def gather_three(total, turned, rows_ref, out):
    lane = lax.broadcasted_iota(jnp.int32, (64, 128), 1)
    side = lax.broadcasted_iota(jnp.int32, (32, 128), 1) < 64
    blank = jnp.zeros((64, 128), F32)
    for ky in range(3):
        near = total[0:128, ky * 256 : ky * 256 + 128] + total[128:256, ky * 256 : ky * 256 + 128]
        far = (
            total[0:128, ky * 256 + 128 : ky * 256 + 256]
            + total[128:256, ky * 256 + 128 : ky * 256 + 256]
        )
        first = near[0:64] + jnp.where(
            lane < 64, pltpu.roll(near[64:128], 64, 1), pltpu.roll(far[64:128], 64, 1)
        )
        second = far[0:64] + pltpu.roll(far[64:128], 64, 1)
        flipped = jnp.transpose(jnp.concatenate([first, blank], axis=0))
        turned[pl.ds(ky * 3, 64, stride=9), :] = flipped[0:64]
        turned[pl.ds(ky * 3 + 1, 64, stride=9), :] = flipped[64:128]
        flipped = jnp.transpose(jnp.concatenate([second, blank], axis=0))
        turned[pl.ds(ky * 3 + 2, 64, stride=9), :] = flipped[0:64]
    turned[576:640] = blank
    evens, odds = [], []
    for j in range(5):
        rows_ref[0:64] = jnp.transpose(turned[j * 128 : (j + 1) * 128])[0:64]
        evens.append(rows_ref[pl.ds(0, 32, stride=2), :])
        odds.append(pltpu.roll(rows_ref[pl.ds(1, 32, stride=2), :], 64, 1))
    rows_ref[0:8] = jnp.zeros((8, 128), F32)
    rows_ref[296:304] = jnp.zeros((8, 128), F32)
    for k in range(9):
        if k < 4:
            held = evens[k]
        elif k == 4:
            held = jnp.where(side, evens[4], odds[0])
        else:
            held = jnp.where(side, odds[k - 5], odds[k - 4])
        rows_ref[pl.ds(8 + k, 32, stride=9), :] = held
    own = pltpu.roll(rows_ref[8:297], 96, 1)
    before = pltpu.roll(rows_ref[7:296], 96, 1)
    edge = out[320:321]
    out[320:609] = jnp.where(lanes() >= 96, own, before)
    out[320:321] = out[320:321] + edge


def conv_backward_kernel(
    lengths_ref,
    picked_ref,
    z_one_ref,
    z_two_ref,
    d_three_ref,
    shared_ref,
    flat_out,
    flat_ref,
    picked,
    z_one,
    z_two,
    d_three,
    h_one,
    h_two,
    slope_one,
    pad_three,
    pad_two,
    d_one,
    v_two,
    v_three,
    spread,
    rows_ref,
    turned,
    bias_out,
    total_one,
    total_two,
    total_three,
    load_sem,
    weight_sem,
):
    used = jnp.int32(0)
    for w in range(lengths_ref.shape[0]):
        used = used + lengths_ref[w]
    groups = lax.div(used + (GROUP - 1), GROUP)

    def loads(group, slot):
        spot = pl.multiple_of(group * GROUP, GROUP)
        return [
            pltpu.make_async_copy(picked_ref.at[group], picked.at[slot], load_sem.at[slot, 0]),
            pltpu.make_async_copy(z_one_ref.at[group], z_one.at[slot], load_sem.at[slot, 1]),
            pltpu.make_async_copy(z_two_ref.at[group], z_two.at[slot], load_sem.at[slot, 2]),
            pltpu.make_async_copy(
                d_three_ref.at[:, pl.ds(spot, GROUP)], d_three.at[slot], load_sem.at[slot, 3]
            ),
        ]

    weights = pltpu.make_async_copy(
        shared_ref.at[pl.ds(0, CONV_ROWS)], flat_ref, weight_sem
    )
    weights.start()
    for load in loads(0, 0):
        load.start()

    def put_two(row, block):
        spread[row : row + 32] = block

    def put_three(row, block):
        spread[row : row + 64] = block

    weights.wait()
    spread_two(flat_ref, rows_ref, turned, put_two)
    for b in range(2):
        for j in range(2):
            for side in range(2):
                source = (2 * j + b) * 256 + side * 128
                target = (b * 2 + j) * 256 + side * 128
                v_two[target : target + 128] = pair(jnp.transpose(spread[source : source + 128]))
    spread_three(flat_ref, rows_ref, turned, put_three)
    for part in range(6):
        rows = pl.ds(part * 128, 128)
        v_three[rows] = pair(jnp.transpose(spread[rows]))
    total_one[...] = jnp.zeros(total_one.shape, F32)
    total_two[...] = jnp.zeros(total_two.shape, F32)
    total_three[...] = jnp.zeros(total_three.shape, F32)
    bias_out[...] = jnp.zeros(bias_out.shape, F32)
    h_one[...] = jnp.zeros(h_one.shape, BF16)
    pad_two[...] = jnp.zeros(pad_two.shape, BF16)
    pad_three[...] = jnp.zeros(pad_three.shape, BF16)

    def fold(rows):
        return jnp.sum(rows.reshape(-1, 8, 128), axis=0)

    def one_group(group, carry):
        slot = lax.rem(group, 2)

        @pl.when(group + 1 < groups)
        def ahead():
            for load in loads(group + 1, 1 - slot):
                load.start()

        for load in loads(group, slot):
            load.wait()
        rows = d_three[slot].reshape(28 * GROUP, 128)
        bias_out[2] += fold(rows)
        both = pair(rows)
        pad_three[0, 2:9, 1:5] = both[:, :128].reshape(7, 4, GROUP, 128)
        pad_three[1, 2:9, 1:5] = both[:, 128:].reshape(7, 4, GROUP, 128)
        h, slope_two = gelu_both(z_two[slot])
        high, low = two_parts(h)
        h_two[0] = high
        h_two[1] = low
        edge = jnp.where(last_masks(), h[:, 4].reshape(9 * GROUP, 128), 0.0)
        high, low = two_parts(edge)
        h_two[0, :, 4] = high.reshape(9, GROUP, 128)
        h_two[1, :, 4] = low.reshape(9, GROUP, 128)
        for part in range(2):
            pieces = []
            for ky in range(3):
                pieces.append(h_two[part, ky : ky + 7, 0:4].reshape(28 * GROUP, 128))
                pieces.append(h_two[part, ky : ky + 7, 1:5].reshape(28 * GROUP, 128))
            total_three[...] += dot_rows(both, jnp.concatenate(pieces, axis=1))
        spill = jnp.zeros((45 * GROUP, 128), F32)
        for part in range(2):
            pieces = []
            for ky in range(3):
                pieces.append(pad_three[part, 2 - ky : 11 - ky, 1:6].reshape(45 * GROUP, 128))
                pieces.append(pad_three[part, 2 - ky : 11 - ky, 0:5].reshape(45 * GROUP, 128))
            spill = spill + fold_pair(dot(jnp.concatenate(pieces, axis=1), v_three[...]))
        rows = spill * slope_two.reshape(45 * GROUP, 128)
        bias_out[1] += fold(rows)
        both = pair(rows)
        pad_two[0, 1:10, 1:6] = both[:, :128].reshape(9, 5, GROUP, 128)
        pad_two[1, 1:10, 1:6] = both[:, 128:].reshape(9, 5, GROUP, 128)
        for q in range(5):
            h, slope = gelu_both(z_one[slot, :, :, q])
            high, low = two_parts(h)
            h_one[0, :, :, q] = high
            h_one[1, :, :, q] = low
            slope_one[:, :, q] = slope
        for part in range(2):
            pieces = []
            for j in range(2):
                for b in range(2):
                    pieces.append(h_one[part, j : j + 9, b, 0:5].reshape(45 * GROUP, 128))
                    pieces.append(h_one[part, j : j + 9, b, 1:6].reshape(45 * GROUP, 128))
            total_two[...] += dot_rows(both, jnp.concatenate(pieces, axis=1))
        for b in range(2):
            spill = jnp.zeros((50 * GROUP, 128), F32)
            for part in range(2):
                pieces = []
                for j in range(2):
                    pieces.append(pad_two[part, 1 - j : 11 - j, 1:6].reshape(50 * GROUP, 128))
                    pieces.append(pad_two[part, 1 - j : 11 - j, 0:5].reshape(50 * GROUP, 128))
                spill = spill + fold_pair(
                    dot(jnp.concatenate(pieces, axis=1), v_two[b * 512 : (b + 1) * 512])
                )
            rows = spill * slope_one[:, b].reshape(50 * GROUP, 128)
            bias_out[0] += fold(rows)
            d_one[:, b] = pair(rows).reshape(10, 5, GROUP, 256)
        for q in range(5):
            pieces = [
                picked[slot, j : j + 20, b, :, q * 128 : (q + 1) * 128].reshape(20 * GROUP, 128)
                for j in range(2)
                for b in range(4)
            ]
            total_one[...] += dot_rows(
                d_one[:, :, q].reshape(20 * GROUP, 256), jnp.concatenate(pieces, axis=1)
            )
        return carry

    lax.fori_loop(0, groups, one_group, 0)
    gather_one(total_one, flat_out)
    gather_two(total_two, turned, rows_ref, flat_out)
    gather_three(total_three, turned, rows_ref, flat_out)
    lane = lanes()
    sums = [jnp.sum(bias_out[k], axis=0, keepdims=True) for k in range(3)]
    sums[0] = sums[0] + pltpu.roll(sums[0], 64, 1)
    sums[0] = sums[0] + pltpu.roll(sums[0], 32, 1)
    sums[1] = jnp.where(lane < 64, sums[1] + pltpu.roll(sums[1], 64, 1), 0.0)
    sums[2] = jnp.where(lane < 64, sums[2] + pltpu.roll(sums[2], 64, 1), 0.0)
    flat_out[64:65] = jnp.where(lane < 32, sums[0], flat_out[64:65])
    flat_out[320:321] = flat_out[320:321] + pltpu.roll(sums[1], 32, 1)
    late = pltpu.roll(sums[2], 96, 1)
    flat_out[608:609] = flat_out[608:609] + jnp.where(lane >= 96, late, 0.0)
    row = lax.broadcasted_iota(jnp.int32, (7, 128), 0)
    flat_out[609:616] = jnp.where((row == 0) & (lane < 32), late, 0.0)


def conv_backward(lengths, picked, z_one, z_two, d_three, flat):
    hbm = pl.BlockSpec(memory_space=pltpu.HBM)
    vmem = pl.BlockSpec(memory_space=pltpu.VMEM)
    return pl.pallas_call(
        conv_backward_kernel,
        in_specs=[pl.BlockSpec(memory_space=pltpu.SMEM)] + [hbm] * 5,
        out_specs=vmem,
        out_shape=jax.ShapeDtypeStruct((CONV_ROWS, 128), F32),
        scratch_shapes=[
            pltpu.VMEM((CONV_ROWS, 128), F32),
            pltpu.VMEM((2, 21, 4, GROUP, 640), BF16),
            pltpu.VMEM((2, 10, 2, 5, GROUP, 128), F32),
            pltpu.VMEM((2, 9, 5, GROUP, 128), F32),
            pltpu.VMEM((2, 28, GROUP, 128), F32),
            pltpu.VMEM((2, 10, 2, 6, GROUP, 128), BF16),
            pltpu.VMEM((2, 9, 5, GROUP, 128), BF16),
            pltpu.VMEM((10, 2, 5, GROUP, 128), F32),
            pltpu.VMEM((2, 11, 6, GROUP, 128), BF16),
            pltpu.VMEM((2, 11, 6, GROUP, 128), BF16),
            pltpu.VMEM((10, 2, 5, GROUP, 256), BF16),
            pltpu.VMEM((1024, 256), BF16),
            pltpu.VMEM((768, 256), BF16),
            pltpu.VMEM((1024, 128), F32),
            pltpu.VMEM((304, 128), F32),
            pltpu.VMEM((640, 128), F32),
            pltpu.VMEM((3, 8, 128), F32),
            pltpu.VMEM((256, 1024), F32),
            pltpu.VMEM((256, 1024), F32),
            pltpu.VMEM((256, 768), F32),
            pltpu.SemaphoreType.DMA((2, 4)),
            pltpu.SemaphoreType.DMA,
        ],
        compiler_params=pltpu.CompilerParams(vmem_limit_bytes=48 * 1024 * 1024),
        name="conv_backward",
    )(lengths, picked, z_one, z_two, d_three, flat)


HIGH = lax.Precision.HIGH
VECTORS_ROW = 3745
TIME_ROW = 3780


def mm(a, b):
    return lax.dot_general(
        a, b, (((1,), (0,)), ((), ())), precision=HIGH, preferred_element_type=F32
    )


def mm_nt(a, b):
    return lax.dot_general(
        a, b, (((1,), (1,)), ((), ())), precision=HIGH, preferred_element_type=F32
    )


def mm_tn(a, b):
    return lax.dot_general(
        a, b, (((0,), (0,)), ((), ())), precision=HIGH, preferred_element_type=F32
    )


def dot_nt(a, b):
    return lax.dot_general(a, b, (((1,), (1,)), ((), ())), preferred_element_type=F32)


def norm_parts(stream):
    centered = stream - jnp.mean(stream, -1, keepdims=True)
    spread = jnp.mean(centered * centered, -1, keepdims=True)
    scale = lax.rsqrt(spread + 1e-05)
    return centered * scale, scale


def norm_back(grad, unit, scale, gain):
    grad = grad * gain
    inner = jnp.mean(grad * unit, -1, keepdims=True)
    return scale * (grad - jnp.mean(grad, -1, keepdims=True) - unit * inner)


def column_sum(x):
    return jnp.sum(x, axis=0, keepdims=True)


def head_places():
    number = lax.broadcasted_iota(jnp.int32, (128, 128), 0) * ACT
    lane = lax.broadcasted_iota(jnp.int32, (128, 128), 1)
    row = lax.shift_right_logical(number, 7)
    return row + jnp.where(lane < jnp.bitwise_and(number, 127), 1, 0)


def roll_rows(held, sign):
    number = lax.broadcasted_iota(jnp.int32, (128, 128), 0) * ACT
    for k in range(7):
        moved = pltpu.roll(held, (sign * (1 << k)) % 128, 1)
        held = jnp.where(jnp.bitwise_and(number, 1 << k) > 0, moved, held)
    return held


def square_head(rows):
    place = head_places()
    held = jnp.zeros((128, 128), F32)
    for k in range(ACT):
        held = jnp.where(place == k, rows[k : k + 1], held)
    held = roll_rows(held, -1)
    lane = lax.broadcasted_iota(jnp.int32, (128, 128), 1)
    return jnp.where(lane < ACT, held, 0.0)


def flat_head(grads):
    place = head_places()
    lane = lax.broadcasted_iota(jnp.int32, (128, 128), 1)
    held = roll_rows(jnp.where(lane < ACT, grads, 0.0), 1)
    rows = [
        jnp.sum(jnp.where(place == k, held, 0.0), axis=0, keepdims=True) for k in range(ACT)
    ]
    return jnp.concatenate(rows + [jnp.zeros((24 - ACT, 128), F32)], axis=0)


def unpack_split(split_ref, qkv, output, up, up_bias, down):
    lane = lax.broadcasted_iota(jnp.int32, (32, 128), 1)
    for layer in range(LAYERS):
        base = layer * 385
        kinds = [[jnp.zeros((32, 128), F32) for j in range(4)] for kind in range(3)]
        for m in range(4):
            rows = [split_ref[m, pl.ds(base + k, 32, stride=3), :] for k in range(3)]
            inside = (lane >= 32 * m) & (lane < 32 * m + 32)
            for j in range(4):
                for kind in range(3):
                    spot = j * 96 + kind * 32
                    source = rows[spot // 128]
                    shift = (32 * m - spot % 128) % 128
                    moved = pltpu.roll(source, shift, 1) if shift else source
                    kinds[kind][j] = jnp.where(inside, moved, kinds[kind][j])
            output[layer, 32 * m : 32 * m + 32] = split_ref[m, base + 96 : base + 128]
            up[layer, :, 128 * m : 128 * m + 128] = split_ref[m, base + 128 : base + 256]
            up_bias[layer, :, 128 * m : 128 * m + 128] = split_ref[m, base + 256 : base + 257]
            down[layer, 128 * m : 128 * m + 128] = split_ref[m, base + 257 : base + 385]
        for kind in range(3):
            for j in range(4):
                qkv[layer, kind, pl.ds(j, 32, stride=4), :] = kinds[kind][j]


def pack_split(out_ref, qkv, output, up, up_bias, down):
    lane = lax.broadcasted_iota(jnp.int32, (32, 128), 1)
    for layer in range(LAYERS):
        base = layer * 385
        parts = [[qkv[layer, kind, pl.ds(j, 32, stride=4), :] for j in range(4)] for kind in range(3)]
        for m in range(4):
            rows = [jnp.zeros((32, 128), F32) for k in range(3)]
            for j in range(4):
                for kind in range(3):
                    spot = j * 96 + kind * 32
                    low = spot % 128
                    shift = (low - 32 * m) % 128
                    moved = pltpu.roll(parts[kind][j], shift, 1) if shift else parts[kind][j]
                    inside = (lane >= low) & (lane < low + 32)
                    rows[spot // 128] = jnp.where(inside, moved, rows[spot // 128])
            for k in range(3):
                out_ref[m, pl.ds(base + k, 32, stride=3), :] = rows[k]
            out_ref[m, base + 96 : base + 128] = output[layer, 32 * m : 32 * m + 32]
            out_ref[m, base + 128 : base + 256] = up[layer, :, 128 * m : 128 * m + 128]
            out_ref[m, base + 256 : base + 257] = up_bias[layer, :, 128 * m : 128 * m + 128]
            out_ref[m, base + 257 : base + 385] = down[layer, 128 * m : 128 * m + 128]
    for m in range(4):
        out_ref[m, 770:784] = jnp.zeros((14, 128), F32)


def former_body(
    slots,
    used,
    lengths_ref,
    returns_ref,
    actions_ref,
    head_ref,
    z_ref,
    small,
    times_all,
    encoder,
    weights,
    d_three_ref,
    d_encoder_ref,
    d_small_ref,
    d_times_ref,
    grads,
    chances,
    kept,
    sums,
    flats,
):
    qkv, output, up, up_bias, down = weights
    d_qkv, d_output, d_up, d_up_bias, d_down = grads
    rows = 3 * slots
    wins, steps = returns_ref.shape
    vec = [small[k : k + 1] for k in range(17)]
    table = small[17 : 17 + ACT]
    slot = lax.broadcasted_iota(jnp.int32, (slots, 1), 0)
    window = jnp.zeros((slots, 1), jnp.int32)
    begin = jnp.zeros((slots, 1), jnp.int32)
    end = jnp.int32(0)
    for w in range(wins - 1):
        end = end + lengths_ref[w]
        window = jnp.where(slot >= end, w + 1, window)
        begin = jnp.where(slot >= end, end, begin)
    moment = slot - begin
    valid = slot < used
    time_lane = lax.broadcasted_iota(jnp.int32, (slots, steps), 1)
    amount = jnp.zeros((slots, 1), F32)
    action = jnp.zeros((slots, 1), jnp.int32)
    for w in range(wins):
        here = (time_lane == moment) & (window == w)
        amount = amount + jnp.sum(
            jnp.where(here, returns_ref[w : w + 1], 0.0), axis=1, keepdims=True
        )
        action = action + jnp.sum(jnp.where(here, actions_ref[w : w + 1], 0), axis=1, keepdims=True)
    lane = lax.broadcasted_iota(jnp.int32, (slots, 128), 1)
    picks = jnp.where((lane == action) & valid, 1.0, 0.0)
    reward = jnp.tanh(amount * vec[14] + vec[15])
    table = jnp.concatenate([table, jnp.zeros((128 - ACT, 128), F32)], axis=0)
    move = jnp.tanh(mm(picks, table))
    sum_state = jnp.zeros((slots, 128), F32)
    for k in range(28):
        z = jnp.where(valid, z_ref[k, 0:slots], 0.0)
        high, low = two_parts(gelu_value(z))
        flats[0, 0:slots, k * 128 : (k + 1) * 128] = high
        flats[1, 0:slots, k * 128 : (k + 1) * 128] = low
    for part in range(2):
        sum_state = sum_state + fold_pair(dot(flats[part, 0:slots], encoder[...]))
    state = jnp.tanh(sum_state + vec[16])
    times = times_all[0:slots]
    stream = jnp.concatenate([reward + times, state + times, move + times], axis=0)

    def ids(axis):
        shape = (rows, 1) if axis == 0 else (1, rows)
        number = lax.broadcasted_iota(jnp.int32, shape, axis)
        kind = jnp.where(number >= 2 * slots, 2, jnp.where(number >= slots, 1, 0))
        return number - kind * slots, kind

    (slot_q, kind_q), (slot_k, kind_k) = ids(0), ids(1)

    def begin_of(slot_ids):
        found = jnp.zeros(slot_ids.shape, jnp.int32)
        end = jnp.int32(0)
        for w in range(wins - 1):
            end = end + lengths_ref[w]
            found = jnp.where(slot_ids >= end, end, found)
        return found

    order_q = slot_q * 3 + kind_q
    order_k = slot_k * 3 + kind_k
    allowed = (order_q >= order_k) & (slot_k >= begin_of(slot_q)) & (slot_k < used)
    head_of = lax.shift_right_logical(lax.broadcasted_iota(jnp.int32, (1, 128), 1), 4)
    heads = D // HD
    batch = 4 if slots <= HALF else 2

    def masked(x, masks):
        return jnp.concatenate([jnp.where(mask, x, jnp.zeros_like(x)) for mask in masks], axis=0)

    def unmasked(x, masks):
        held = jnp.where(masks[0], x[0:rows], 0.0)
        for k in range(1, batch):
            held = held + jnp.where(masks[k], x[k * rows : (k + 1) * rows], 0.0)
        return held

    tape = []
    for layer in range(LAYERS):
        gains = vec[6 * layer : 6 * layer + 6]
        unit_one, scale_one = norm_parts(stream)
        normed = unit_one * gains[0] + gains[1]
        wide = jnp.concatenate([qkv[layer, k] for k in range(3)], axis=1)
        mixed = mm(normed, wide)
        query_high, query_low = two_parts(mixed[:, :128] * 0.25)
        keys, values = pair(mixed[:, 128:256]), pair(mixed[:, 256:])
        kept[layer, 0, 0:rows] = query_high
        kept[layer, 1, 0:rows] = query_low
        for k in range(2):
            kept[layer, 2 + k, 0:rows] = keys[:, k * 128 : (k + 1) * 128]
            kept[layer, 4 + k, 0:rows] = values[:, k * 128 : (k + 1) * 128]
        sums[0, 0:rows] = jnp.zeros((rows, 128), F32)

        def attend(turn, carry, layer=layer):
            masks = [head_of == turn * batch + k for k in range(batch)]
            parts = [masked(kept[layer, k, 0:rows], masks) for k in range(2)]
            keys = [kept[layer, 2 + k, 0:rows] for k in range(2)]
            values = [kept[layer, 4 + k, 0:rows] for k in range(2)]
            scores = dot_nt(
                jnp.concatenate([parts[0], parts[0]], axis=1), jnp.concatenate(keys, axis=1)
            )
            scores = (scores + dot_nt(parts[1], keys[0])).reshape(batch, rows, rows)
            scores = jnp.where(allowed[None], scores, -1e30)
            peak = jnp.max(scores, -1, keepdims=True)
            chance = jnp.exp(scores - peak)
            chance = chance / jnp.sum(chance, -1, keepdims=True)
            high, low = two_parts(chance.reshape(batch * rows, rows))
            spot = pl.ds(pl.multiple_of(turn * (batch * rows), 64), batch * rows)
            chances[layer, 0, spot, 0:rows] = high
            chances[layer, 1, spot, 0:rows] = low
            seen = fold_pair(dot(high, jnp.concatenate(values, axis=1))) + dot(low, values[0])
            sums[0, 0:rows] += unmasked(seen, masks)
            return carry

        lax.fori_loop(0, heads // batch, attend, 0)
        context = sums[0, 0:rows]
        stream = stream + mm(context, output[layer]) + gains[4]
        unit_two, scale_two = norm_parts(stream)
        normed_two = unit_two * gains[2] + gains[3]
        inner, slope = gelu_both(mm(normed_two, up[layer]) + up_bias[layer])
        stream = stream + mm(inner, down[layer]) + gains[5]
        tape.append((unit_one, scale_one, unit_two, scale_two, inner, slope, context))
    end_stream = stream[slots : 2 * slots]
    unit, scale = norm_parts(end_stream)
    final = unit * vec[12] + vec[13]
    logits = jnp.where(lane < ACT, mm(final, head_ref[...]), -1e30)
    peak = jnp.max(logits, -1, keepdims=True)
    powers = jnp.exp(logits - peak)
    total = jnp.sum(powers, -1, keepdims=True)
    chosen = jnp.sum(jnp.where(lane == action, logits, 0.0), -1, keepdims=True)
    terms = jnp.where(valid, jnp.log(total) + peak - chosen, 0.0)
    loss = jnp.sum(terms, axis=0, keepdims=True)
    d_small_ref[72:80] = jnp.broadcast_to(loss, (8, 128))
    d_logits = jnp.where(valid, powers / total, 0.0) - picks
    d_small_ref[48:72] = flat_head(mm_tn(final, d_logits))
    d_final = mm_nt(d_logits, head_ref[...])
    d_vec = [None] * 17
    d_vec[12] = column_sum(d_final * unit)
    d_vec[13] = column_sum(d_final)
    d_end = norm_back(d_final, unit, scale, vec[12])
    blank = jnp.zeros((slots, 128), F32)
    d_stream = jnp.concatenate([blank, d_end, blank], axis=0)
    for layer in reversed(range(LAYERS)):
        unit_one, scale_one, unit_two, scale_two, inner, slope, context = tape[layer]
        gains = vec[6 * layer : 6 * layer + 6]
        d_vec[6 * layer + 5] = column_sum(d_stream)
        d_down[layer] = mm_tn(inner, d_stream)
        d_inner = mm_nt(d_stream, down[layer]) * slope
        d_up_bias[layer] = column_sum(d_inner)
        normed_two = unit_two * gains[2] + gains[3]
        d_up[layer] = mm_tn(normed_two, d_inner)
        d_normed = mm_nt(d_inner, up[layer])
        d_vec[6 * layer + 2] = column_sum(d_normed * unit_two)
        d_vec[6 * layer + 3] = column_sum(d_normed)
        d_stream = d_stream + norm_back(d_normed, unit_two, scale_two, gains[2])
        d_vec[6 * layer + 4] = column_sum(d_stream)
        d_output[layer] = mm_tn(context, d_stream)
        d_context = mm_nt(d_stream, output[layer])
        bases = d_context * context
        high, low = two_parts(d_context)
        for k in range(3):
            sums[k, 0:rows] = jnp.zeros((rows, 128), F32)
        kept[layer, 6, 0:rows] = high
        kept[layer, 7, 0:rows] = low
        sums[3, 0:rows] = bases

        def attend_back(turn, carry, layer=layer):
            masks = [head_of == turn * batch + k for k in range(batch)]
            query = [masked(kept[layer, k, 0:rows], masks) for k in range(2)]
            keys = [kept[layer, 2 + k, 0:rows] for k in range(2)]
            values = [kept[layer, 4 + k, 0:rows] for k in range(2)]
            d_seen = [masked(kept[layer, 6 + k, 0:rows], masks) for k in range(2)]
            base = jnp.sum(masked(sums[3, 0:rows], masks), -1, keepdims=True)
            spot = pl.ds(pl.multiple_of(turn * (batch * rows), 64), batch * rows)
            chance = [chances[layer, k, spot, 0:rows] for k in range(2)]
            d_chance = dot_nt(
                jnp.concatenate([d_seen[0], d_seen[0]], axis=1), jnp.concatenate(values, axis=1)
            )
            d_chance = d_chance + dot_nt(d_seen[1], values[0])
            d_scores = (chance[0].astype(F32) + chance[1].astype(F32)) * (d_chance - base)
            high, low = two_parts(d_scores)
            d_query = fold_pair(dot(high, jnp.concatenate(keys, axis=1))) + dot(low, keys[0])
            sums[0, 0:rows] += unmasked(d_query, masks)
            d_keys = fold_pair(dot_rows(high, jnp.concatenate(query, axis=1)))
            sums[1, 0:rows] += d_keys + dot_rows(low, query[0])
            d_values = fold_pair(dot_rows(chance[0], jnp.concatenate(d_seen, axis=1)))
            sums[2, 0:rows] += d_values + dot_rows(chance[1], d_seen[0])
            return carry

        lax.fori_loop(0, heads // batch, attend_back, 0)
        normed = unit_one * gains[0] + gains[1]
        d_mixed = jnp.concatenate(
            [sums[0, 0:rows] * 0.25, sums[1, 0:rows], sums[2, 0:rows]], axis=1
        )
        wide = jnp.concatenate([qkv[layer, k] for k in range(3)], axis=1)
        d_wide = mm_tn(normed, d_mixed)
        for k in range(3):
            d_qkv[layer, k] = d_wide[:, k * 128 : (k + 1) * 128]
        d_normed = mm_nt(d_mixed, wide)
        d_vec[6 * layer] = column_sum(d_normed * unit_one)
        d_vec[6 * layer + 1] = column_sum(d_normed)
        d_stream = d_stream + norm_back(d_normed, unit_one, scale_one, gains[0])
    d_reward, d_state, d_move = (d_stream[k * slots : (k + 1) * slots] for k in range(3))
    d_times_ref[0:slots] = jnp.where(valid, d_reward + d_state + d_move, 0.0)
    d_reward = d_reward * (1.0 - reward * reward)
    d_vec[14] = column_sum(d_reward * amount)
    d_vec[15] = column_sum(d_reward)
    d_move = d_move * (1.0 - move * move)
    d_small_ref[24:48] = mm_tn(picks, d_move)[0:24]
    d_state = jnp.where(valid, d_state * (1.0 - state * state), 0.0)
    d_vec[16] = column_sum(d_state)
    d_small_ref[0:24] = jnp.concatenate(d_vec + [jnp.zeros((7, 128), F32)], axis=0)
    high, low = two_parts(d_state)
    twice = jnp.concatenate([high, high], axis=1)
    both = jnp.concatenate([high, low], axis=1)
    d_flat = dot_nt(twice, encoder[...]) + dot_nt(low, encoder[:, 0:128])
    d_block = dot_rows(flats[0, 0:slots], both) + dot_rows(flats[1, 0:slots], both)
    d_block = fold_pair(d_block)
    for k in range(28):
        z = jnp.where(valid, z_ref[k, 0:slots], 0.0)
        d_three_ref[k, 0:slots] = d_flat[:, k * 128 : (k + 1) * 128] * gelu_both(z)[1]
        y, v = divmod(k, 4)
        for o in range(2):
            if 2 * v + o < 7:
                d_encoder_ref[pl.ds(y * 7 + 2 * v + o, 64, stride=49), :] = d_block[
                    k * 128 + o * 64 : k * 128 + (o + 1) * 64
                ]


def former_kernel(
    packed,
    lengths_ref,
    starts_ref,
    index_ref,
    returns_ref,
    actions_ref,
    z_from,
    flat_ref,
    *refs,
):
    if packed:
        split_ref, refs = refs[0], refs[1:]
    else:
        given, refs = refs[:5], refs[5:]
    (d_three_to, rows_ref), refs = refs[:2], refs[2:]
    if packed:
        parts, refs = refs[:4], refs[4:]
        (d_encoder_ref, d_small_ref, d_split), refs = refs[:3], refs[3:]
        weights, grads, refs = refs[:5], refs[5:10], refs[10:]
    else:
        (d_encoder_ref, d_small_ref), grads, refs = refs[:2], refs[2:7], refs[7:]
        weights = given
    (raw, near, small, rows_raw, times_all, encoder, chances, kept, sums, flats), refs = (
        refs[:10],
        refs[10:],
    )
    z_ref, d_three_ref, head_ref, sem = refs
    used = jnp.int32(0)
    wins = lengths_ref.shape[0]
    for w in range(wins):
        used = used + lengths_ref[w]

    def z_copy(slots):
        return pltpu.make_async_copy(
            z_from.at[:, pl.ds(0, slots)], z_ref.at[:, pl.ds(0, slots)], sem.at[wins + 3]
        )

    def z_back(slots):
        return pltpu.make_async_copy(
            d_three_ref.at[:, pl.ds(0, slots)], d_three_to.at[:, pl.ds(0, slots)], sem.at[wins + 3]
        )

    copies = [
        pltpu.make_async_copy(flat_ref.at[pl.ds(608, 3144)], raw, sem.at[0]),
        pltpu.make_async_copy(flat_ref.at[pl.ds(3744, 48)], rows_raw.at[wins], sem.at[1]),
        pltpu.make_async_copy(
            flat_ref.at[pl.ds(7872, 24)], rows_raw.at[wins + 1, pl.ds(0, 24)], sem.at[2]
        ),
    ]
    offsets = []
    for w in range(wins):
        row = TIME_ROW + starts_ref[w]
        low = pl.multiple_of(lax.div(row, 8) * 8, 8)
        offsets.append(row - low)
        copies.append(
            pltpu.make_async_copy(
                flat_ref.at[pl.ds(low, 40)], rows_raw.at[w, pl.ds(0, 40)], sem.at[3 + w]
            )
        )
    for copy in copies:
        copy.start()

    @pl.when(used <= HALF)
    def few_states():
        z_copy(HALF).start()

    @pl.when(used > HALF)
    def many_states():
        z_copy(ROOM).start()

    if packed:
        unpack_split(split_ref, *weights)
    for copy in copies:
        copy.wait()
    lane = lanes()

    def straight(first, second):
        return jnp.where(lane < 96, pltpu.roll(first, 96, 1), pltpu.roll(second, 96, 1))

    def turn(step, carry):
        spot = pl.multiple_of(step * 64, 64)
        near[pl.ds(spot, 64)] = straight(raw[pl.ds(spot + 1, 64)], raw[pl.ds(spot + 2, 64)])
        return carry

    lax.fori_loop(0, 49, turn, 0)
    for k in range(28):
        y, v = divmod(k, 4)
        halves = []
        for o in range(2):
            if 2 * v + o < 7:
                halves.append(near[pl.ds(y * 7 + 2 * v + o, 64, stride=49), :])
            else:
                halves.append(jnp.zeros((64, 128), F32))
        encoder[k * 128 : (k + 1) * 128] = pair(jnp.concatenate(halves, axis=0))
    small[...] = straight(rows_raw[wins, 1:41], rows_raw[wins, 2:42])
    head_ref[...] = square_head(
        straight(rows_raw[wins + 1, 4:22], rows_raw[wins + 1, 5:23])
    )
    times_all[...] = jnp.zeros(times_all.shape, F32)
    begin = 0
    row = lax.broadcasted_iota(jnp.int32, (32, 1), 0)
    for w in range(wins):
        rows = straight(
            rows_raw[w, pl.ds(offsets[w], 32)], rows_raw[w, pl.ds(offsets[w] + 1, 32)]
        )
        times_all[pl.ds(begin, 32)] = jnp.where(row < lengths_ref[w], rows, 0.0)
        begin = begin + lengths_ref[w]
    rows_ref[...] = jnp.zeros(rows_ref.shape, F32)
    note = jnp.zeros((1, 128), F32)
    for w in range(wins):
        note = jnp.where(lane == w, lengths_ref[w].astype(F32), note)
        note = jnp.where(lane == wins + w, starts_ref[w].astype(F32), note)
    rows_ref[ROOM : ROOM + 1] = note
    d_small_ref[...] = jnp.zeros(d_small_ref.shape, F32)

    def run(slots):
        z_copy(slots).wait()
        former_body(
            slots,
            used,
            lengths_ref,
            returns_ref,
            actions_ref,
            head_ref,
            z_ref,
            small,
            times_all,
            encoder,
            weights,
            d_three_ref,
            d_encoder_ref,
            d_small_ref,
            rows_ref,
            grads,
            chances,
            kept,
            sums,
            flats,
        )
        z_back(slots).start()

    @pl.when(used <= HALF)
    def few():
        run(HALF)

    @pl.when(used > HALF)
    def many():
        run(ROOM)

    if packed:
        me = index_ref[0]
        count = d_small_ref.shape[0] // 4
        pack_split(d_split, *grads)
        for k in range(4):
            m = jnp.bitwise_xor(me, k)
            parts[k][0:784] = d_split[m]
            parts[k][784:1568] = d_encoder_ref[pl.ds(pl.multiple_of(m * 784, 8), 784)]
            parts[k][1568 : 1568 + count] = d_small_ref[
                pl.ds(pl.multiple_of(m * count, 8), count)
            ]

    @pl.when(used <= HALF)
    def few_end():
        z_back(HALF).wait()

    @pl.when(used > HALF)
    def many_end():
        z_back(ROOM).wait()


def former(lengths, starts, index, returns, actions, z_three, flat, weights, small_rows, packed):
    smem = pl.BlockSpec(memory_space=pltpu.SMEM)
    vmem = pl.BlockSpec(memory_space=pltpu.VMEM)
    hbm = pl.BlockSpec(memory_space=pltpu.HBM)
    wins = lengths.shape[0]
    canonical = [
        (LAYERS, 3, 128, 128),
        (LAYERS, 128, 128),
        (LAYERS, 128, FF),
        (LAYERS, 1, FF),
        (LAYERS, FF, 128),
    ]
    outs, out_specs = [(28, ROOM, 128), (ROOM + 8, 128)], [hbm, vmem]
    if packed:
        outs += [(1568 + small_rows // 4, 128)] * 4
        out_specs += [vmem] * 4
        scratch = [
            pltpu.VMEM((3136, 128), F32),
            pltpu.VMEM((small_rows, 128), F32),
            pltpu.VMEM((4, 784, 128), F32),
        ]
        scratch += [pltpu.VMEM(shape, F32) for shape in canonical] * 2
    else:
        outs += [(3136, 128), (small_rows, 128)] + canonical
        out_specs += [vmem] * 7
        scratch = []
    rows = 3 * ROOM
    scratch += [
        pltpu.VMEM((3144, 128), F32),
        pltpu.VMEM((3136, 128), F32),
        pltpu.VMEM((40, 128), F32),
        pltpu.VMEM((wins + 2, 48, 128), F32),
        pltpu.VMEM((ROOM + 32, 128), F32),
        pltpu.VMEM((3584, 256), BF16),
        pltpu.VMEM((LAYERS, 2, 8 * rows, rows), BF16),
        pltpu.VMEM((LAYERS, 8, rows, 128), BF16),
        pltpu.VMEM((4, rows, 128), F32),
        pltpu.VMEM((2, ROOM, 3584), BF16),
        pltpu.VMEM((28, ROOM, 128), F32),
        pltpu.VMEM((28, ROOM, 128), F32),
        pltpu.VMEM((128, 128), F32),
        pltpu.SemaphoreType.DMA((wins + 4,)),
    ]
    return pl.pallas_call(
        partial(former_kernel, packed),
        in_specs=[smem] * 3 + [vmem] * 2 + [hbm] * 2 + [vmem] * len(weights),
        out_specs=out_specs,
        out_shape=[jax.ShapeDtypeStruct(shape, F32) for shape in outs],
        scratch_shapes=scratch,
        compiler_params=pltpu.CompilerParams(vmem_limit_bytes=60 * 1024 * 1024),
        name="transformer_step",
    )(lengths, starts, index, returns, actions, z_three, flat, *weights)


SMALL = [("vectors", 24), ("action_table", 24), ("head", 24), ("loss", 8)]
FIELD_ROWS = 8200
EARLY_ROWS = CONV_ROWS + 3136
TABLE_AT = CONV_ROWS + 3136 + 17 + ACT


def round_up(number, grain):
    return -(-number // grain) * grain


def chunk_of(rows):
    return max(size for size in range(8, 65, 8) if rows % size == 0)


def mesh_bits(dp_size, mp_size):
    dp_bits = [("dp", k) for k in range(dp_size.bit_length() - 1)]
    mp_bits = [("mp", k) for k in range(mp_size.bit_length() - 1)]
    middle = len(dp_bits) // 3
    return mp_bits[:1], mp_bits[1:], dp_bits[:middle], dp_bits[middle:]


def reduce_kernel(plan, *refs):
    mp_size, quarter, share = plan["mp_size"], plan["quarter"], plan["share"]
    parts, conv_ref, refs = refs[:mp_size], refs[mp_size], refs[mp_size + 1 :]
    (early_out, small_out, split_out, square_out), refs = refs[:4], refs[4:]
    (stage, work, landing, split_total, own_total, conv_total, tiles, tile_in) = refs[:8]
    load_sem, send_sem, recv_sem, store_sem = refs[8:]
    spots = {"dp": lax.axis_index("dp"), "mp": lax.axis_index("mp")}
    cores, ys, xs, zs = plan["bits"]
    bits = cores + ys + xs + zs
    dp_first = xs + zs
    dp_second = zs[:1] + xs + zs[1:]
    slots = iter(range(plan["copies"]))

    def value(bit):
        return lax.rem(lax.div(spots[bit[0]], 1 << bit[1]), 2)

    def partner(bit):
        axis, k = bit
        place = dict(spots)
        place[axis] = spots[axis] + (1 - 2 * value(bit)) * (1 << k)
        return (place["dp"], place["mp"])

    def send(source, target, bit):
        slot = next(slots)
        copy = pltpu.make_async_remote_copy(
            src_ref=source,
            dst_ref=target,
            send_sem=send_sem.at[slot],
            recv_sem=recv_sem.at[slot],
            device_id=partner(bit),
            device_id_type=pl.DeviceIdType.MESH,
        )
        copy.start()
        return copy

    loads = [
        pltpu.make_async_copy(parts[k], stage.at[k], load_sem.at[k]) for k in range(mp_size)
    ]
    loads.append(
        pltpu.make_async_copy(
            conv_ref, work.at[pl.ds(plan["conv"], CONV_ROWS)], load_sem.at[mp_size]
        )
    )
    for load in loads:
        load.start()

    def wipe(target, start, rows):
        if rows > 0:
            target[start : start + rows] = jnp.zeros((rows, 128), F32)

    wipe(work, plan["conv"] + CONV_ROWS, plan["conv_rows"] - CONV_ROWS)
    wipe(work, plan["split"] + quarter, plan["split_rows"] - quarter)
    wipe(work, plan["own"] + quarter + share, plan["own_rows"] - quarter - share)
    barrier = pltpu.get_barrier_semaphore()
    for bit in bits:
        pl.semaphore_signal(
            barrier, inc=1, device_id=partner(bit), device_id_type=pl.DeviceIdType.MESH
        )
    pl.semaphore_wait(barrier, len(bits))

    def add_into(target, start, pieces, rows):
        chunk = chunk_of(rows)

        def body(turn, carry):
            spot = pl.multiple_of(start + turn * chunk, 8)
            held = target[pl.ds(spot, chunk)]
            for source, at in pieces:
                held = held + source[pl.ds(pl.multiple_of(at + turn * chunk, 8), chunk)]
            target[pl.ds(spot, chunk)] = held
            return carry

        lax.fori_loop(0, rows // chunk, body, 0)

    def copy_rows(target, start, source, at, rows):
        chunk = chunk_of(rows)

        def body(turn, carry):
            held = source[pl.ds(pl.multiple_of(at + turn * chunk, 8), chunk)]
            target[pl.ds(pl.multiple_of(start + turn * chunk, 8), chunk)] = held
            return carry

        lax.fori_loop(0, rows // chunk, body, 0)

    class Stream:
        def __init__(self, base, rows, order, total, total_at):
            self.base, self.size, self.order = base, rows, order
            self.total, self.at = total, total_at
            self.land = base
            self.flight = None
            self.step = 0
            self.start = base

        def halve(self):
            if self.flight is not None:
                copy, half, land, keep = self.flight
                copy.wait()
                add_into(work, keep, [(landing, land)], half)
                self.base, self.size, self.flight = keep, half, None
            if self.step < len(self.order):
                bit = self.order[self.step]
                half = self.size // 2
                mine = value(bit)
                keep = self.base + mine * half
                give = pl.multiple_of(self.base + (1 - mine) * half, 8)
                copy = send(
                    work.at[pl.ds(give, half)], landing.at[pl.ds(self.land, half)], bit
                )
                self.flight = (copy, half, self.land, keep)
                self.land += half
                self.step += 1

        def turn(self):
            self.at = self.at + (self.base - self.start)
            copy_rows(self.total, self.at, work, self.base, self.size)
            self.step = 0

        def double(self):
            if self.flight is not None:
                copy, low = self.flight
                copy.wait()
                self.at, self.size, self.flight = low, self.size * 2, None
            if self.step < len(self.order):
                bit = self.order[len(self.order) - 1 - self.step]
                region = self.total.at[pl.ds(pl.multiple_of(self.at, 8), self.size)]
                copy = send(region, region, bit)
                self.flight = (copy, self.at - value(bit) * self.size)
                self.step += 1

        def squares(self, keep):
            held = work[pl.ds(pl.multiple_of(self.base, 8), self.size)]
            if keep is not None:
                row = lax.broadcasted_iota(jnp.int32, (self.size, 1), 0)
                held = jnp.where(keep(row + self.base), held, 0.0)
            return jnp.sum((held * held).reshape(self.size // 8, 8, 128), axis=0)

    def keep_own(row):
        place = row - plan["own"] - quarter
        return (place < 0) | (place + spots["mp"] * share < 72)

    def sum_parts(target, at, rows):
        copy_rows(work, target, stage.at[0], at, rows)
        add_into(work, target, [(stage.at[k], at) for k in range(1, mp_size)], rows)

    class Quarter:
        def __init__(self, stream, offset, order):
            self.at = stream.base - stream.start + offset
            self.size, self.order = stream.size, order
            self.held, self.flights, self.step = [0], [], 0
            copy_rows(own_total.at[spots["mp"]], self.at, work, stream.base, stream.size)

        def region(self, offset):
            index = spots["mp"]
            for other in cores + ys:
                if offset & (1 << other[1]):
                    index = index + (1 - 2 * value(other)) * (1 << other[1])
            return own_total.at[index, pl.ds(pl.multiple_of(self.at, 8), self.size)]

        def double(self):
            if self.flights:
                for copy in self.flights:
                    copy.wait()
                bit = self.order[self.step - 1]
                if bit[0] == "dp":
                    self.at = self.at - value(bit) * self.size
                    self.size *= 2
                else:
                    self.held = self.held + [offset | (1 << bit[1]) for offset in self.held]
                self.flights = []
            if self.step < len(self.order):
                bit = self.order[self.step]
                for offset in self.held:
                    region = self.region(offset)
                    self.flights.append(send(region, region, bit))
                self.step += 1

    first, second = plan["cut"]
    own = [
        Stream(plan["own"], first, dp_first, own_total, 0),
        Stream(plan["own"] + first, plan["own_rows"] - first, dp_second, own_total, first),
    ]
    split = [
        Stream(plan["split"], second, dp_first, split_total, 0),
        Stream(
            plan["split"] + second, plan["split_rows"] - second, dp_second, split_total, second
        ),
    ]
    conv = Stream(plan["conv"], plan["conv_rows"], bits, conv_total, 0)
    for load in loads:
        load.wait()
    sum_parts(plan["own"], quarter, quarter)
    sum_parts(plan["own"] + quarter, 2 * quarter, share)
    for stream in own + [conv]:
        stream.halve()
    sum_parts(plan["split"], 0, quarter)
    steps = len(dp_first)
    for step in range(steps):
        for stream in own + [conv]:
            stream.halve()
        if step == 0:
            for stream in split:
                stream.halve()
    squares = jnp.zeros((8, 128), F32)
    for stream in own:
        squares = squares + stream.squares(keep_own)
    orders = [
        list(reversed(dp_first)) + ys + cores,
        list(reversed(dp_second[1:])) + ys + dp_second[:1] + cores,
    ]
    quarters = [Quarter(own[0], 0, orders[0]), Quarter(own[1], first, orders[1])]
    for piece in quarters:
        piece.double()
    for step in range(steps):
        for piece in quarters:
            piece.double()
        conv.halve()
        for stream in split:
            stream.halve()
    for stream in split:
        squares = squares + stream.squares(None)
        stream.turn()
        stream.double()
    while conv.flight is not None:
        for piece in quarters:
            piece.double()
        conv.halve()
    squares = squares + conv.squares(None)
    conv.turn()
    conv.double()
    tiles[0] = squares
    tile_flight = send(tiles.at[0], tile_in.at[0], bits[0])
    rounds = 1
    while rounds <= len(bits) or conv.flight is not None or quarters[0].flights:
        for stream in quarters + [conv] + split:
            stream.double()
        if rounds <= len(bits):
            tile_flight.wait()
            tiles[rounds] = tiles[rounds - 1] + tile_in[rounds - 1]
            if rounds < len(bits):
                tile_flight = send(tiles.at[rounds], tile_in.at[rounds], bits[rounds])
        rounds += 1
    square_out[...] = tiles[len(bits)]
    stores = [
        (conv_total.at[pl.ds(0, CONV_ROWS)], early_out.at[pl.ds(0, CONV_ROWS)]),
        (split_total.at[pl.ds(0, quarter)], split_out),
    ]
    for m in range(mp_size):
        rows = pl.ds(CONV_ROWS + m * quarter, quarter)
        stores.append((own_total.at[m, pl.ds(0, quarter)], early_out.at[rows]))
        rows = pl.ds(m * share, share)
        stores.append((own_total.at[m, pl.ds(quarter, share)], small_out.at[rows]))
    stores = [
        pltpu.make_async_copy(source, target, store_sem.at[number])
        for number, (source, target) in enumerate(stores)
    ]
    for copy in stores:
        copy.start()
    for copy in stores:
        copy.wait()


def reduce_all(parts, conv, dp_size, mp_size):
    bits = mesh_bits(dp_size, mp_size)
    steps = sum(len(part) for part in bits)
    dp_steps = dp_size.bit_length() - 1
    quarter = 3136 // mp_size
    share = parts[0].shape[0] - 2 * quarter
    dp_grain = 8 * dp_size
    own_rows = round_up(quarter + share, dp_grain)
    split_rows = round_up(quarter, dp_grain)
    conv_rows = round_up(CONV_ROWS, 8 * dp_size * mp_size)
    places, at = {}, 0
    for name, size in [("split", split_rows), ("own", own_rows), ("conv", conv_rows)]:
        places[name] = at
        at += size
    cut = (round_up(own_rows // 2, dp_grain), round_up(split_rows // 2, dp_grain))
    copies = 6 * dp_steps + 2 * steps + steps + 2 * (dp_steps + mp_size * mp_size)
    plan = dict(
        places,
        mp_size=mp_size,
        quarter=quarter,
        share=share,
        bits=bits,
        copies=copies,
        split_rows=split_rows,
        own_rows=own_rows,
        conv_rows=conv_rows,
        cut=cut,
    )
    vmem = pl.BlockSpec(memory_space=pltpu.VMEM)
    hbm = pl.BlockSpec(memory_space=pltpu.HBM)
    any_spec = pl.BlockSpec(memory_space=pl.ANY)
    return pl.pallas_call(
        partial(reduce_kernel, plan),
        in_specs=[hbm] * (mp_size + 1),
        out_specs=[any_spec, any_spec, any_spec, vmem],
        out_shape=[
            jax.ShapeDtypeStruct((EARLY_ROWS, 128), F32),
            jax.ShapeDtypeStruct((share * mp_size, 128), F32),
            jax.ShapeDtypeStruct((quarter, 128), F32),
            jax.ShapeDtypeStruct((8, 128), F32),
        ],
        scratch_shapes=[
            pltpu.VMEM((mp_size, 2 * quarter + share, 128), F32),
            pltpu.VMEM((at, 128), F32),
            pltpu.VMEM((at, 128), F32),
            pltpu.VMEM((split_rows, 128), F32),
            pltpu.VMEM((mp_size, own_rows, 128), F32),
            pltpu.VMEM((conv_rows, 128), F32),
            pltpu.VMEM((steps + 1, 8, 128), F32),
            pltpu.VMEM((steps, 8, 128), F32),
            pltpu.SemaphoreType.DMA((mp_size + 1,)),
            pltpu.SemaphoreType.DMA((copies,)),
            pltpu.SemaphoreType.DMA((copies,)),
            pltpu.SemaphoreType.DMA((2 + 2 * mp_size,)),
        ],
        compiler_params=pltpu.CompilerParams(
            collective_id=1, has_side_effects=True, vmem_limit_bytes=20 * 1024 * 1024
        ),
        name="reduce_gradients",
    )(*parts, conv)


FLAT_ROWS = 7896
BLOCK_ROWS = 1024
LATE = 609
SPAN = 40


def adam_kernel(
    wins,
    early_ref,
    rows_ref,
    small_ref,
    split_ref,
    square_ref,
    weight_ref,
    first_ref,
    second_ref,
    split_weight_ref,
    split_first_ref,
    split_second_ref,
    new_ref,
    new_first_ref,
    new_second_ref,
    low_ref,
    split_new_ref,
    split_new_first_ref,
    split_new_second_ref,
    scalar_ref,
    field,
    rows,
    notes,
    marks,
    pulled,
    factor_ref,
    pull_sem,
    load_sem,
):
    step = pl.program_id(0)
    last = pl.num_programs(0) - 1
    lane = lax.broadcasted_iota(jnp.int32, (1, 128), 1)

    def pull(block, slot):
        start = pl.multiple_of(block * BLOCK_ROWS, BLOCK_ROWS)
        return pltpu.make_async_copy(
            field.at[pl.ds(start, BLOCK_ROWS + 8)], pulled.at[slot], pull_sem.at[slot]
        )

    def update(weights, first, second, grads):
        first = beta_first * first + (1 - beta_first) * grads
        second = beta_second * second + (1 - beta_second) * grads * grads
        fix_one = 1.0 / (1 - beta_first**STEP)
        fix_two = 1.0 / (1 - beta_second**STEP)
        weights = weights - learn_rate * (
            first * fix_one / (jnp.sqrt(second * fix_two) + adam_epsilon) + weight_decay * weights
        )
        return weights, first, second

    def sum_of(tile):
        held = jnp.sum(jnp.sum(tile, axis=0, keepdims=True), axis=1, keepdims=True)
        return jnp.broadcast_to(held, (1, 128))

    slot = lax.rem(step, 2)

    @pl.when(step == 0)
    def prepare():
        load_rows = pltpu.make_async_copy(rows_ref, rows, load_sem.at[0])
        load_early = pltpu.make_async_copy(
            early_ref, field.at[pl.ds(0, EARLY_ROWS)], load_sem.at[1]
        )
        load_rows.start()
        load_early.start()
        late = FIELD_ROWS - EARLY_ROWS
        field[EARLY_ROWS:FIELD_ROWS] = jnp.zeros((late, 128), F32)
        load_rows.wait()
        stride = ROOM + 8
        devices = rows.shape[0] // stride
        notes[...] = rows[pl.ds(ROOM, devices, stride=stride), :]
        mark = pltpu.make_async_copy(notes, marks, load_sem.at[2])
        mark.start()
        mark.wait()
        place = lax.broadcasted_iota(jnp.int32, (SPAN, ROOM), 0)
        slot_of = lax.broadcasted_iota(jnp.int32, (SPAN, ROOM), 1)

        def scatter(turn, carry):
            spots, found = [], []
            for k in range(4):
                device = turn * 4 + k
                begin = jnp.int32(0)
                picks = []
                for w in range(wins):
                    length = marks[device, w].astype(jnp.int32)
                    row = marks[device, wins + w].astype(jnp.int32) + TABLE_AT
                    low = lax.div(row, 8) * 8
                    inside = (slot_of >= begin) & (slot_of < begin + length)
                    inside = inside & (place - slot_of == row - low - begin)
                    picks.append(jnp.where(inside, 1.0, 0.0).astype(BF16))
                    spots.append(low)
                    begin = begin + length
                held = pair(rows[pl.ds(pl.multiple_of(device * stride, 8), ROOM)])
                found.append(fold_pair(dot(jnp.concatenate(picks, axis=0), held)))
            for k in range(4):
                for w in range(wins):
                    spot = pl.ds(pl.multiple_of(spots[k * wins + w], 8), SPAN)
                    field[spot] = field[spot] + found[k][w * SPAN : (w + 1) * SPAN]
            return carry

        lax.fori_loop(0, devices // 4, scatter, 0)

        def fold(turn, carry):
            spot = pl.multiple_of(EARLY_ROWS + turn * 64, 8)
            held = field[pl.ds(spot, 64)]
            return carry + jnp.sum((held * held).reshape(8, 8, 128), axis=0)

        squares = lax.fori_loop(0, late // 64, fold, square_ref[...])
        at = EARLY_ROWS
        for name_at, count in [(0, 17), (24, ACT)]:
            field[at : at + count] = small_ref[name_at : name_at + count]
            at += count
        at = TABLE_AT + TSTEPS
        field[at : at + ACT] = small_ref[48 : 48 + ACT]
        lane_all = lax.broadcasted_iota(jnp.int32, notes.shape, 1)
        count = sum_of(jnp.where(lane_all < wins, notes[...], 0.0))
        seed = 1.0 / count
        norm = jnp.sqrt(sum_of(squares)) * seed
        factor = jnp.minimum(1.0, clip_limit / (norm + 1e-06)) * seed
        factor_ref[...] = jnp.broadcast_to(factor, (8, 128))
        loss = small_ref[72:73]
        row = lax.broadcasted_iota(jnp.int32, (8, 128), 0)
        scalar_ref[...] = jnp.where(row == 0, norm, jnp.where(row == 1, loss, count))
        load_early.wait()
        pull(0, 0).start()

    @pl.when(step < last)
    def ahead():
        pull(step + 1, 1 - slot).start()

    @pl.when(step == last)
    def split():
        count = split_weight_ref.shape[0]
        outs = update(
            split_weight_ref[...],
            split_first_ref[...],
            split_second_ref[...],
            split_ref[0:count] * factor_ref[0:1],
        )
        split_new_ref[...], split_new_first_ref[...], split_new_second_ref[...] = outs

    pull(step, slot).wait()
    early = pulled[slot, 0:BLOCK_ROWS]
    own = pltpu.roll(pulled[slot, 7 : BLOCK_ROWS + 7], 32, 1)
    before = pltpu.roll(pulled[slot, 6 : BLOCK_ROWS + 6], 32, 1)
    row = lax.broadcasted_iota(jnp.int32, (BLOCK_ROWS, 1), 0) + step * BLOCK_ROWS
    grads = jnp.where(lane < 32, jnp.where(row == LATE, early, before), own)
    grads = jnp.where(row < LATE, early, grads)
    outs = update(weight_ref[...], first_ref[...], second_ref[...], grads * factor_ref[0:1])
    new_ref[...], new_first_ref[...], new_second_ref[...] = outs
    low_ref[...] = outs[0].astype(BF16)


def adam_all(early, rows, small, split_grad, square, shared, split, wins):
    grid = -(-FLAT_ROWS // BLOCK_ROWS)
    flat_spec = pl.BlockSpec((BLOCK_ROWS, 128), lambda i: (i, 0))
    split_rows = split[0].shape[0]
    devices = rows.shape[0]

    def whole(shape):
        return pl.BlockSpec(shape, lambda i: (0,) * len(shape))

    split_spec = whole((split_rows, 128))
    shared_out = jax.ShapeDtypeStruct((FLAT_ROWS, 128), F32)
    split_out = jax.ShapeDtypeStruct((split_rows, 128), F32)
    any_spec = pl.BlockSpec(memory_space=pl.ANY)
    return pl.pallas_call(
        partial(adam_kernel, wins),
        grid=(grid,),
        in_specs=[
            any_spec,
            any_spec,
            whole(small.shape),
            whole(split_grad.shape),
            whole((8, 128)),
            flat_spec,
            flat_spec,
            flat_spec,
            split_spec,
            split_spec,
            split_spec,
        ],
        out_specs=[flat_spec] * 4 + [split_spec] * 3 + [whole((8, 128))],
        out_shape=[shared_out] * 3
        + [jax.ShapeDtypeStruct((FLAT_ROWS, 128), BF16)]
        + [split_out] * 3
        + [jax.ShapeDtypeStruct((8, 128), F32)],
        scratch_shapes=[
            pltpu.VMEM((FIELD_ROWS, 128), F32),
            pltpu.VMEM((devices * (ROOM + 8), 128), F32),
            pltpu.VMEM((devices, 128), F32),
            pltpu.SMEM((devices, 128), F32),
            pltpu.VMEM((2, BLOCK_ROWS + 8, 128), F32),
            pltpu.VMEM((8, 128), F32),
            pltpu.SemaphoreType.DMA((2,)),
            pltpu.SemaphoreType.DMA((3,)),
        ],
        compiler_params=pltpu.CompilerParams(vmem_limit_bytes=48 * 1024 * 1024),
        name="adam_update",
    )(
        early,
        rows.reshape(devices * (ROOM + 8), 128),
        small,
        split_grad,
        square,
        *shared,
        *split,
    )


def per_device(
    frames,
    returns,
    actions,
    starts,
    lengths,
    shared_weights,
    shared_first,
    shared_second,
    split_weights,
    split_first,
    split_second,
):
    dp_size, mp_size = lax.axis_size("dp"), lax.axis_size("mp")
    narrow = D // mp_size
    hidden_width = FF // mp_size
    wins, steps = returns.shape
    width = split_weights.shape[0]
    split_rows = width // 128
    packed = narrow == 32
    own_rows = split_weights.reshape(split_rows, 128)
    split_all = lax.all_gather(own_rows, "mp", axis=0)
    flat = shared_weights.reshape(FLAT_ROWS, 128)
    picked, z_one, z_two, z_three = conv_forward(lengths, frames, flat)
    if packed:
        weights = [split_all]
    else:
        layers, layers_back = jax.vjp(
            lambda held: assemble(held, mp_size, narrow, hidden_width), split_all.reshape(-1)
        )
        weights = [
            jnp.stack([layer["qkv"].transpose(1, 0, 2) for layer in layers]),
            jnp.stack([layer["output"] for layer in layers]),
            jnp.stack([layer["up"] for layer in layers]),
            jnp.stack([layer["up_bias"][None] for layer in layers]),
            jnp.stack([layer["down"] for layer in layers]),
        ]
    small_rows = round_up(sum(rows for name, rows in SMALL), 8 * mp_size)
    index = lax.axis_index("mp").reshape(1)
    results = former(
        lengths, starts, index, returns, actions, z_three, flat, weights, small_rows, packed
    )
    d_three, rows = results[:2]
    rows_all = lax.all_gather(rows, ("dp", "mp"), axis=0)
    quarter = 3136 // mp_size
    if packed:
        parts = results[2:]
    else:
        d_encoder, d_small, d_qkv, d_output, d_up, d_up_bias, d_down = results[2:]
        grad_layers = [
            dict(
                qkv=d_qkv[layer].transpose(1, 0, 2),
                output=d_output[layer],
                up=d_up[layer],
                up_bias=d_up_bias[layer, 0],
                down=d_down[layer],
            )
            for layer in range(LAYERS)
        ]
        gathered = layers_back(grad_layers)[0].reshape(mp_size, split_rows, 128)
        gathered = jnp.pad(gathered, ((0, 0), (0, quarter - split_rows), (0, 0)))
        encoder = d_encoder.reshape(mp_size, quarter, 128)
        small = d_small.reshape(mp_size, -1, 128)
        every = jnp.concatenate([gathered, encoder, small], axis=1)
        parts = [
            lax.dynamic_index_in_dim(every, jnp.bitwise_xor(index[0], k), 0, keepdims=False)
            for k in range(mp_size)
        ]
    arrived = [parts[0]]
    for k in range(1, mp_size):
        turn = [(index, index ^ k) for index in range(mp_size)]
        arrived.append(lax.ppermute(parts[k], "mp", turn))
    d_conv = conv_backward(lengths, picked, z_one, z_two, d_three, flat)
    early, small, split_sum, square = reduce_all(arrived, d_conv, dp_size, mp_size)
    shared_view = [a.reshape(FLAT_ROWS, 128) for a in (shared_weights, shared_first, shared_second)]
    split_view = [a.reshape(split_rows, 128) for a in (split_weights, split_first, split_second)]
    updated = adam_all(
        early, rows_all, small, split_sum, square, shared_view, split_view, wins
    )
    shared_out = [a.reshape(-1) for a in updated[:4]]
    split_out = [a.reshape(-1) for a in updated[4:7]]
    scalars = updated[7]
    return (
        *shared_out,
        *split_out,
        split_out[0].astype(BF16),
        scalars[0, 0],
        scalars[1, 0],
        scalars[2, 0],
    )


def solution(mesh):
    return jax.shard_map(
        per_device,
        mesh=mesh,
        in_specs=(
            P(("dp", "mp"), None, None, None, None),
            P(("dp", "mp"), None),
            P(("dp", "mp"), None),
            P(("dp", "mp")),
            P(("dp", "mp")),
            P(),
            P(),
            P(),
            P("mp"),
            P("mp"),
            P("mp"),
        ),
        out_specs=(P(), P(), P(), P(), P("mp"), P("mp"), P("mp"), P("mp"), P(), P(), P()),
        check_vma=False,
    )
```

```python
from functools import partial
import math

import jax
import jax.numpy as jnp
from jax import lax
from jax.experimental import pallas as pl
from jax.experimental.pallas import tpu as pltpu
from jax.sharding import PartitionSpec as P

D = 128
FF = 512
ACT = 18
C1 = 32
C2 = 64
TSTEPS = 4096
LAYERS = 2
STEP = 10
HD = 16


clip_limit = 0.1
learn_rate = 0.05
beta_first = 0.9
beta_second = 0.95
adam_epsilon = 1e-08
weight_decay = 0.1


def span_layout(narrow, hidden):
    return [
        ("qkv", (D, 3, narrow)),
        ("output", (narrow, D)),
        ("up", (D, hidden)),
        ("up_bias", (hidden,)),
        ("down", (hidden, D)),
    ]


def assemble(flat, copies, narrow, hidden):
    layout = span_layout(narrow, hidden)
    width = sum((math.prod(shape) for name, shape in layout))
    blocks = flat.reshape(copies, LAYERS, width)
    layers = []
    for layer in range(LAYERS):
        offset = 0
        pieces = {}
        for name, shape in layout:
            count = math.prod(shape)
            pieces[name] = blocks[:, layer, offset : offset + count].reshape((copies,) + shape)
            offset += count
        layers.append(
            {
                "qkv": jnp.moveaxis(pieces["qkv"], 0, 2).reshape(D, 3, copies * narrow),
                "output": pieces["output"].reshape(copies * narrow, D),
                "up": jnp.moveaxis(pieces["up"], 0, 1).reshape(D, copies * hidden),
                "up_bias": pieces["up_bias"].reshape(copies * hidden),
                "down": pieces["down"].reshape(copies * hidden, D),
            }
        )
    return layers


GROUP = 16
CONV_ROWS = 616
ROOM = 128
HALF = 64
BF16 = jnp.bfloat16
F32 = jnp.float32


def gelu_value(x):
    inner = 0.7978845608028654 * (x + 0.044715 * (x * x * x))
    return 0.5 * x * (1.0 + jnp.tanh(inner))


def gelu_both(x):
    square = x * x
    turn = jnp.tanh(0.7978845608028654 * x * (1.0 + 0.044715 * square))
    half = 0.5 * (1.0 + turn)
    slope = half + 0.5 * x * (1.0 - turn * turn) * (
        0.7978845608028654 * (1.0 + 3 * 0.044715 * square)
    )
    return x * half, slope


def two_parts(x):
    high = x.astype(BF16)
    return high, (x - high.astype(F32)).astype(BF16)


def pair(x):
    return jnp.concatenate(two_parts(x), axis=-1)


def fold_pair(x):
    return x[:, :128] + x[:, 128:]


def dot(a, b):
    return lax.dot_general(a, b, (((1,), (0,)), ((), ())), preferred_element_type=F32)


def dot_rows(a, b):
    return lax.dot_general(a, b, (((0,), (0,)), ((), ())), preferred_element_type=F32)


def lanes():
    return lax.broadcasted_iota(jnp.int32, (1, 128), 1)


def conv_biases(flat_ref):
    lane = lanes()
    one = jnp.where(lane < 32, flat_ref[64:65], 0.0)
    one = one + pltpu.roll(one, 32, 1)
    one = one + pltpu.roll(one, 64, 1)
    two = jnp.where(lane < 64, pltpu.roll(flat_ref[320:321], 96, 1), 0.0)
    two = two + pltpu.roll(two, 64, 1)
    three = jnp.where(
        lane < 32,
        pltpu.roll(flat_ref[608:609], 32, 1),
        jnp.where(lane < 64, pltpu.roll(flat_ref[609:610], 32, 1), 0.0),
    )
    three = three + pltpu.roll(three, 64, 1)
    return one, two, three


def shifted(ref, start, rows, lane):
    first = pltpu.roll(ref[start : start + rows], 128 - lane, 1)
    second = pltpu.roll(ref[start + 1 : start + 1 + rows], 128 - lane, 1)
    return jnp.where(lanes() < 128 - lane, first, second)


def spread_one(flat_ref, put):
    halves = [jnp.transpose(flat_ref[pl.ds(side, 32, stride=2), :]) for side in range(2)]
    turned = jnp.concatenate(halves, axis=0)
    lane = lax.broadcasted_iota(jnp.int32, (8, 128), 1)
    row = lax.broadcasted_iota(jnp.int32, (8, 128), 0)
    low = row < 4
    column = lax.shift_right_logical(lane, 5)
    for ky in range(8):
        for c in range(4):
            held = turned[c * 64 + ky * 8 : c * 64 + ky * 8 + 8]
            wide = jnp.concatenate([held] * 4, axis=1)
            flipped = jnp.concatenate([wide[4:], wide[:4]], axis=0)
            zero = jnp.zeros((8, 128), F32)
            first = jnp.where(column == 0, wide, jnp.where((column == 1) & ~low, flipped, zero))
            second = jnp.where(
                column == 2,
                wide,
                jnp.where(((column == 1) & low) | ((column == 3) & ~low), flipped, zero),
            )
            third = jnp.where((column == 3) & low, flipped, zero)
            put(ky * 128 + c * 32, jnp.concatenate([first, second, third, zero], axis=0))


def spread_two(flat_ref, rows_ref, turned, put):
    lane = lax.broadcasted_iota(jnp.int32, (32, 128), 1)
    rows_ref[0:256] = shifted(flat_ref, 64, 256, 32)
    for j in range(4):
        block = jnp.transpose(rows_ref[pl.ds(j, 64, stride=4), :])
        turned[j * 128 : (j + 1) * 128] = jnp.concatenate([block, block], axis=1)
    for ky in range(4):
        rows = [turned[pl.ds(ky * 4 + kx, 32, stride=16)] for kx in range(4)]
        for i in range(8):
            left = rows[i] if i < 4 else jnp.zeros((32, 128), F32)
            right = rows[i - 2] if 2 <= i < 6 else jnp.zeros((32, 128), F32)
            put(ky * 256 + i * 32, jnp.where(lane < 64, left, right))


def spread_three(flat_ref, rows_ref, turned, put):
    lane = lax.broadcasted_iota(jnp.int32, (64, 128), 1)
    side = lax.broadcasted_iota(jnp.int32, (32, 128), 1) < 64
    rows_ref[0:288] = shifted(flat_ref, 320, 288, 96)
    nine = [rows_ref[pl.ds(k, 32, stride=9), :] for k in range(9)]
    flips = [pltpu.roll(nine[4 + k], 64, 1) for k in range(5)]
    for j in range(5):
        wide = min(128, 576 - j * 128)
        rows_ref[pl.ds(0, 32, stride=2), :] = nine[j]
        rows_ref[pl.ds(1, 32, stride=2), :] = (
            jnp.where(side, flips[j], flips[j + 1]) if j < 4 else flips[4]
        )
        block = jnp.transpose(rows_ref[0:64])[0:wide]
        turned[j * 128 : j * 128 + wide] = jnp.concatenate([block, block], axis=1)
    for ky in range(3):
        rows = [turned[pl.ds(ky * 3 + kx, 64, stride=9)] for kx in range(3)]
        for i in range(4):
            left = rows[i] if i < 3 else jnp.zeros((64, 128), F32)
            right = rows[i - 1] if i >= 1 else jnp.zeros((64, 128), F32)
            put(ky * 256 + i * 64, jnp.where(lane < 64, left, right))


def last_masks():
    return lanes() < 64


def conv_forward_kernel(
    lengths_ref,
    frames_ref,
    shared_ref,
    picked_ref,
    z_one_ref,
    z_two_ref,
    z_three_ref,
    flat_ref,
    held,
    wide,
    picked,
    z_one,
    z_two,
    z_three,
    h_one,
    h_two,
    w_one,
    w_two,
    w_three,
    choose,
    rows_ref,
    turned,
    frame_sem,
    out_sem,
):
    wins = lengths_ref.shape[0]
    steps = frames_ref.shape[1]
    used = jnp.int32(0)
    for w in range(wins):
        used = used + lengths_ref[w]
    groups = lax.div(used + (GROUP - 1), GROUP)

    def frame_copy(group, spot, slot):
        state = jnp.minimum(group * GROUP + spot, used - 1)
        window, begin, end = jnp.int32(0), jnp.int32(0), jnp.int32(0)
        for w in range(wins - 1):
            end = end + lengths_ref[w]
            window = jnp.where(state >= end, w + 1, window)
            begin = jnp.where(state >= end, end, begin)
        return pltpu.make_async_copy(
            frames_ref.at[window, state - begin], held.at[slot, spot], frame_sem.at[slot, spot]
        )

    def fetch(group, slot):
        def one(spot, carry):
            frame_copy(group, spot, slot).start()
            return carry

        lax.fori_loop(0, GROUP, one, 0)

    weights = pltpu.make_async_copy(
        shared_ref.at[pl.ds(0, CONV_ROWS)], flat_ref, out_sem.at[4]
    )
    weights.start()
    fetch(0, 0)
    h_one[...] = jnp.zeros(h_one.shape, BF16)

    def put_one(row, block):
        w_one[row : row + 32] = pair(block)

    def put_two(row, block):
        w_two[row : row + 32] = pair(block)

    def put_three(row, block):
        w_three[row : row + 64] = pair(block)

    weights.wait()
    spread_one(flat_ref, put_one)
    spread_two(flat_ref, rows_ref, turned, put_two)
    spread_three(flat_ref, rows_ref, turned, put_three)
    bias_one, bias_two, bias_three = conv_biases(flat_ref)
    row = lax.broadcasted_iota(jnp.int32, (128, 640), 0)
    column = lax.broadcasted_iota(jnp.int32, (128, 640), 1)
    place = jnp.bitwise_and(column, 31)
    channel = jnp.bitwise_and(lax.shift_right_logical(column, 5), 3)
    block = lax.shift_right_logical(column, 7)
    right = (row == 16 * block + place) & (place < 20)
    for c in range(4):
        choose[c * 128 : (c + 1) * 128] = jnp.where(right & (channel == c), 1.0, 0.0).astype(BF16)

    def one_group(group, carry):
        slot = lax.rem(group, 2)

        @pl.when(group + 1 < groups)
        def ahead():
            fetch(group + 1, 1 - slot)

        def lay(step, carry):
            spots = [step * 4 + k for k in range(4)]
            for spot in spots:
                frame_copy(group, spot, slot).wait()
            for spot in spots:
                image = held[slot, spot].astype(F32).reshape(336, 84)
                image = jnp.concatenate([image, jnp.zeros((336, 44), F32)], axis=1)
                wide[pl.ds(spot, 336, stride=GROUP), :] = image
            return carry

        lax.fori_loop(0, GROUP // 4, lay, 0)
        for part in range(3):
            rows = wide[part * 1792 : (part + 1) * 1792].reshape(28, 4, GROUP, 128)
            rows = [rows[:, c].reshape(448, 128).astype(BF16) for c in range(4)]
            result = dot(jnp.concatenate(rows, axis=1), choose[...])
            picked[part * 7 : (part + 1) * 7] = result.astype(BF16).reshape(7, 4, GROUP, 640)
        keep_picked = pltpu.make_async_copy(picked, picked_ref.at[group], out_sem.at[0])
        keep_picked.start()
        for q in range(5):
            pieces = [
                picked[j : j + 20, b, :, q * 128 : (q + 1) * 128].reshape(20 * GROUP, 128)
                for j in range(2)
                for b in range(4)
            ]
            z = fold_pair(dot(jnp.concatenate(pieces, axis=1), w_one[...])) + bias_one
            z_one[:, :, q] = z.reshape(10, 2, GROUP, 128)
            high, low = two_parts(gelu_value(z))
            h_one[0, :, :, q] = high.reshape(10, 2, GROUP, 128)
            h_one[1, :, :, q] = low.reshape(10, 2, GROUP, 128)
        keep_one = pltpu.make_async_copy(z_one, z_one_ref.at[group], out_sem.at[1])
        keep_one.start()
        total = jnp.zeros((45 * GROUP, 128), F32)
        for part in range(2):
            pieces = []
            for j in range(2):
                for b in range(2):
                    pieces.append(h_one[part, j : j + 9, b, 0:5].reshape(45 * GROUP, 128))
                    pieces.append(h_one[part, j : j + 9, b, 1:6].reshape(45 * GROUP, 128))
            total = total + fold_pair(dot(jnp.concatenate(pieces, axis=1), w_two[...]))
        z = (total + bias_two).reshape(9, 5, GROUP, 128)
        z_two[...] = z
        h = gelu_value(z)
        high, low = two_parts(h)
        h_two[0] = high
        h_two[1] = low
        edge = jnp.where(last_masks(), h[:, 4].reshape(9 * GROUP, 128), 0.0)
        high, low = two_parts(edge)
        h_two[0, :, 4] = high.reshape(9, GROUP, 128)
        h_two[1, :, 4] = low.reshape(9, GROUP, 128)
        keep_two = pltpu.make_async_copy(z_two, z_two_ref.at[group], out_sem.at[2])
        keep_two.start()
        total = jnp.zeros((28 * GROUP, 128), F32)
        for part in range(2):
            pieces = []
            for ky in range(3):
                pieces.append(h_two[part, ky : ky + 7, 0:4].reshape(28 * GROUP, 128))
                pieces.append(h_two[part, ky : ky + 7, 1:5].reshape(28 * GROUP, 128))
            total = total + fold_pair(dot(jnp.concatenate(pieces, axis=1), w_three[...]))
        z_three[...] = (total + bias_three).reshape(28, GROUP, 128)
        spot = pl.multiple_of(group * GROUP, GROUP)
        keep_three = pltpu.make_async_copy(
            z_three, z_three_ref.at[:, pl.ds(spot, GROUP)], out_sem.at[3]
        )
        keep_three.start()
        keep_picked.wait()
        keep_one.wait()
        keep_two.wait()
        keep_three.wait()
        return carry

    lax.fori_loop(0, groups, one_group, 0)


def conv_forward(lengths, frames, flat):
    most = ROOM // GROUP
    any_spec = pl.BlockSpec(memory_space=pl.ANY)
    hbm = pl.BlockSpec(memory_space=pltpu.HBM)
    return pl.pallas_call(
        conv_forward_kernel,
        in_specs=[
            pl.BlockSpec(memory_space=pltpu.SMEM),
            any_spec,
            any_spec,
        ],
        out_specs=[hbm] * 4,
        out_shape=[
            jax.ShapeDtypeStruct((most, 21, 4, GROUP, 640), BF16),
            jax.ShapeDtypeStruct((most, 10, 2, 5, GROUP, 128), F32),
            jax.ShapeDtypeStruct((most, 9, 5, GROUP, 128), F32),
            jax.ShapeDtypeStruct((28, ROOM, 128), F32),
        ],
        scratch_shapes=[
            pltpu.VMEM((CONV_ROWS, 128), F32),
            pltpu.VMEM((2, GROUP, 84, 4, 84), BF16),
            pltpu.VMEM((336 * GROUP, 128), F32),
            pltpu.VMEM((21, 4, GROUP, 640), BF16),
            pltpu.VMEM((10, 2, 5, GROUP, 128), F32),
            pltpu.VMEM((9, 5, GROUP, 128), F32),
            pltpu.VMEM((28, GROUP, 128), F32),
            pltpu.VMEM((2, 10, 2, 6, GROUP, 128), BF16),
            pltpu.VMEM((2, 9, 5, GROUP, 128), BF16),
            pltpu.VMEM((1024, 256), BF16),
            pltpu.VMEM((1024, 256), BF16),
            pltpu.VMEM((768, 256), BF16),
            pltpu.VMEM((512, 640), BF16),
            pltpu.VMEM((288, 128), F32),
            pltpu.VMEM((576, 128), F32),
            pltpu.SemaphoreType.DMA((2, GROUP)),
            pltpu.SemaphoreType.DMA((5,)),
        ],
        compiler_params=pltpu.CompilerParams(vmem_limit_bytes=32 * 1024 * 1024),
        name="conv_forward",
    )(lengths, frames.transpose(0, 1, 3, 2, 4), flat)


def gather_one(total, out):
    lane = lax.broadcasted_iota(jnp.int32, (32, 128), 1)
    halves = [jnp.zeros((32, 128), F32) for side in range(2)]
    for ky in range(8):
        held = total[0:128, ky * 128 : (ky + 1) * 128] + total[128:256, ky * 128 : (ky + 1) * 128]
        summed = held[0:32]
        for o in range(1, 4):
            summed = summed + pltpu.roll(held[32 * o : 32 * o + 32], 128 - 4 * o, 1)
        for c in range(4):
            spot = (c % 2) * 64 + ky * 8
            shift = (spot - c * 32) % 128
            moved = pltpu.roll(summed, shift, 1) if shift else summed
            inside = (lane >= spot) & (lane < spot + 8)
            halves[c // 2] = halves[c // 2] + jnp.where(inside, moved, 0.0)
    for side in range(2):
        out[pl.ds(side, 32, stride=2), :] = halves[side]


def gather_two(total, turned, rows_ref, out):
    lane = lax.broadcasted_iota(jnp.int32, (64, 128), 1)
    for ky in range(4):
        near = total[0:128, ky * 256 : ky * 256 + 128] + total[128:256, ky * 256 : ky * 256 + 128]
        far = (
            total[0:128, ky * 256 + 128 : ky * 256 + 256]
            + total[128:256, ky * 256 + 128 : ky * 256 + 256]
        )
        summed = near[0:64] + jnp.where(
            lane < 64, pltpu.roll(near[64:128], 64, 1), pltpu.roll(far[64:128], 64, 1)
        )
        flipped = jnp.transpose(jnp.concatenate([summed, jnp.zeros((64, 128), F32)], axis=0))
        for kx in range(4):
            turned[pl.ds(ky * 4 + kx, 32, stride=16), :] = flipped[kx * 32 : (kx + 1) * 32]
    rows_ref[0:8] = jnp.zeros((8, 128), F32)
    rows_ref[264:272] = jnp.zeros((8, 128), F32)
    for j in range(4):
        block = jnp.transpose(turned[j * 128 : (j + 1) * 128])[0:64]
        rows_ref[pl.ds(8 + j, 64, stride=4), :] = block
    own = pltpu.roll(rows_ref[8:265], 32, 1)
    before = pltpu.roll(rows_ref[7:264], 32, 1)
    out[64:321] = jnp.where(lanes() >= 32, own, before)


def gather_three(total, turned, rows_ref, out):
    lane = lax.broadcasted_iota(jnp.int32, (64, 128), 1)
    side = lax.broadcasted_iota(jnp.int32, (32, 128), 1) < 64
    blank = jnp.zeros((64, 128), F32)
    for ky in range(3):
        near = total[0:128, ky * 256 : ky * 256 + 128] + total[128:256, ky * 256 : ky * 256 + 128]
        far = (
            total[0:128, ky * 256 + 128 : ky * 256 + 256]
            + total[128:256, ky * 256 + 128 : ky * 256 + 256]
        )
        first = near[0:64] + jnp.where(
            lane < 64, pltpu.roll(near[64:128], 64, 1), pltpu.roll(far[64:128], 64, 1)
        )
        second = far[0:64] + pltpu.roll(far[64:128], 64, 1)
        flipped = jnp.transpose(jnp.concatenate([first, blank], axis=0))
        turned[pl.ds(ky * 3, 64, stride=9), :] = flipped[0:64]
        turned[pl.ds(ky * 3 + 1, 64, stride=9), :] = flipped[64:128]
        flipped = jnp.transpose(jnp.concatenate([second, blank], axis=0))
        turned[pl.ds(ky * 3 + 2, 64, stride=9), :] = flipped[0:64]
    turned[576:640] = blank
    evens, odds = [], []
    for j in range(5):
        rows_ref[0:64] = jnp.transpose(turned[j * 128 : (j + 1) * 128])[0:64]
        evens.append(rows_ref[pl.ds(0, 32, stride=2), :])
        odds.append(pltpu.roll(rows_ref[pl.ds(1, 32, stride=2), :], 64, 1))
    rows_ref[0:8] = jnp.zeros((8, 128), F32)
    rows_ref[296:304] = jnp.zeros((8, 128), F32)
    for k in range(9):
        if k < 4:
            held = evens[k]
        elif k == 4:
            held = jnp.where(side, evens[4], odds[0])
        else:
            held = jnp.where(side, odds[k - 5], odds[k - 4])
        rows_ref[pl.ds(8 + k, 32, stride=9), :] = held
    own = pltpu.roll(rows_ref[8:297], 96, 1)
    before = pltpu.roll(rows_ref[7:296], 96, 1)
    edge = out[320:321]
    out[320:609] = jnp.where(lanes() >= 96, own, before)
    out[320:321] = out[320:321] + edge


def conv_backward_kernel(
    lengths_ref,
    picked_ref,
    z_one_ref,
    z_two_ref,
    d_three_ref,
    shared_ref,
    flat_out,
    flat_ref,
    picked,
    z_one,
    z_two,
    d_three,
    h_one,
    h_two,
    slope_one,
    pad_three,
    pad_two,
    d_one,
    v_two,
    v_three,
    spread,
    rows_ref,
    turned,
    bias_out,
    total_one,
    total_two,
    total_three,
    load_sem,
    weight_sem,
):
    used = jnp.int32(0)
    for w in range(lengths_ref.shape[0]):
        used = used + lengths_ref[w]
    groups = lax.div(used + (GROUP - 1), GROUP)

    def loads(group, slot):
        spot = pl.multiple_of(group * GROUP, GROUP)
        return [
            pltpu.make_async_copy(picked_ref.at[group], picked.at[slot], load_sem.at[slot, 0]),
            pltpu.make_async_copy(z_one_ref.at[group], z_one.at[slot], load_sem.at[slot, 1]),
            pltpu.make_async_copy(z_two_ref.at[group], z_two.at[slot], load_sem.at[slot, 2]),
            pltpu.make_async_copy(
                d_three_ref.at[:, pl.ds(spot, GROUP)], d_three.at[slot], load_sem.at[slot, 3]
            ),
        ]

    weights = pltpu.make_async_copy(
        shared_ref.at[pl.ds(0, CONV_ROWS)], flat_ref, weight_sem
    )
    weights.start()
    for load in loads(0, 0):
        load.start()

    def put_two(row, block):
        spread[row : row + 32] = block

    def put_three(row, block):
        spread[row : row + 64] = block

    weights.wait()
    spread_two(flat_ref, rows_ref, turned, put_two)
    for b in range(2):
        for j in range(2):
            for side in range(2):
                source = (2 * j + b) * 256 + side * 128
                target = (b * 2 + j) * 256 + side * 128
                v_two[target : target + 128] = pair(jnp.transpose(spread[source : source + 128]))
    spread_three(flat_ref, rows_ref, turned, put_three)
    for part in range(6):
        rows = pl.ds(part * 128, 128)
        v_three[rows] = pair(jnp.transpose(spread[rows]))
    total_one[...] = jnp.zeros(total_one.shape, F32)
    total_two[...] = jnp.zeros(total_two.shape, F32)
    total_three[...] = jnp.zeros(total_three.shape, F32)
    bias_out[...] = jnp.zeros(bias_out.shape, F32)
    h_one[...] = jnp.zeros(h_one.shape, BF16)
    pad_two[...] = jnp.zeros(pad_two.shape, BF16)
    pad_three[...] = jnp.zeros(pad_three.shape, BF16)

    def fold(rows):
        return jnp.sum(rows.reshape(-1, 8, 128), axis=0)

    def one_group(group, carry):
        slot = lax.rem(group, 2)

        @pl.when(group + 1 < groups)
        def ahead():
            for load in loads(group + 1, 1 - slot):
                load.start()

        for load in loads(group, slot):
            load.wait()
        rows = d_three[slot].reshape(28 * GROUP, 128)
        bias_out[2] += fold(rows)
        both = pair(rows)
        pad_three[0, 2:9, 1:5] = both[:, :128].reshape(7, 4, GROUP, 128)
        pad_three[1, 2:9, 1:5] = both[:, 128:].reshape(7, 4, GROUP, 128)
        h, slope_two = gelu_both(z_two[slot])
        high, low = two_parts(h)
        h_two[0] = high
        h_two[1] = low
        edge = jnp.where(last_masks(), h[:, 4].reshape(9 * GROUP, 128), 0.0)
        high, low = two_parts(edge)
        h_two[0, :, 4] = high.reshape(9, GROUP, 128)
        h_two[1, :, 4] = low.reshape(9, GROUP, 128)
        for part in range(2):
            pieces = []
            for ky in range(3):
                pieces.append(h_two[part, ky : ky + 7, 0:4].reshape(28 * GROUP, 128))
                pieces.append(h_two[part, ky : ky + 7, 1:5].reshape(28 * GROUP, 128))
            total_three[...] += dot_rows(both, jnp.concatenate(pieces, axis=1))
        spill = jnp.zeros((45 * GROUP, 128), F32)
        for part in range(2):
            pieces = []
            for ky in range(3):
                pieces.append(pad_three[part, 2 - ky : 11 - ky, 1:6].reshape(45 * GROUP, 128))
                pieces.append(pad_three[part, 2 - ky : 11 - ky, 0:5].reshape(45 * GROUP, 128))
            spill = spill + fold_pair(dot(jnp.concatenate(pieces, axis=1), v_three[...]))
        rows = spill * slope_two.reshape(45 * GROUP, 128)
        bias_out[1] += fold(rows)
        both = pair(rows)
        pad_two[0, 1:10, 1:6] = both[:, :128].reshape(9, 5, GROUP, 128)
        pad_two[1, 1:10, 1:6] = both[:, 128:].reshape(9, 5, GROUP, 128)
        for q in range(5):
            h, slope = gelu_both(z_one[slot, :, :, q])
            high, low = two_parts(h)
            h_one[0, :, :, q] = high
            h_one[1, :, :, q] = low
            slope_one[:, :, q] = slope
        for part in range(2):
            pieces = []
            for j in range(2):
                for b in range(2):
                    pieces.append(h_one[part, j : j + 9, b, 0:5].reshape(45 * GROUP, 128))
                    pieces.append(h_one[part, j : j + 9, b, 1:6].reshape(45 * GROUP, 128))
            total_two[...] += dot_rows(both, jnp.concatenate(pieces, axis=1))
        for b in range(2):
            spill = jnp.zeros((50 * GROUP, 128), F32)
            for part in range(2):
                pieces = []
                for j in range(2):
                    pieces.append(pad_two[part, 1 - j : 11 - j, 1:6].reshape(50 * GROUP, 128))
                    pieces.append(pad_two[part, 1 - j : 11 - j, 0:5].reshape(50 * GROUP, 128))
                spill = spill + fold_pair(
                    dot(jnp.concatenate(pieces, axis=1), v_two[b * 512 : (b + 1) * 512])
                )
            rows = spill * slope_one[:, b].reshape(50 * GROUP, 128)
            bias_out[0] += fold(rows)
            d_one[:, b] = pair(rows).reshape(10, 5, GROUP, 256)
        for q in range(5):
            pieces = [
                picked[slot, j : j + 20, b, :, q * 128 : (q + 1) * 128].reshape(20 * GROUP, 128)
                for j in range(2)
                for b in range(4)
            ]
            total_one[...] += dot_rows(
                d_one[:, :, q].reshape(20 * GROUP, 256), jnp.concatenate(pieces, axis=1)
            )
        return carry

    lax.fori_loop(0, groups, one_group, 0)
    gather_one(total_one, flat_out)
    gather_two(total_two, turned, rows_ref, flat_out)
    gather_three(total_three, turned, rows_ref, flat_out)
    lane = lanes()
    sums = [jnp.sum(bias_out[k], axis=0, keepdims=True) for k in range(3)]
    sums[0] = sums[0] + pltpu.roll(sums[0], 64, 1)
    sums[0] = sums[0] + pltpu.roll(sums[0], 32, 1)
    sums[1] = jnp.where(lane < 64, sums[1] + pltpu.roll(sums[1], 64, 1), 0.0)
    sums[2] = jnp.where(lane < 64, sums[2] + pltpu.roll(sums[2], 64, 1), 0.0)
    flat_out[64:65] = jnp.where(lane < 32, sums[0], flat_out[64:65])
    flat_out[320:321] = flat_out[320:321] + pltpu.roll(sums[1], 32, 1)
    late = pltpu.roll(sums[2], 96, 1)
    flat_out[608:609] = flat_out[608:609] + jnp.where(lane >= 96, late, 0.0)
    row = lax.broadcasted_iota(jnp.int32, (7, 128), 0)
    flat_out[609:616] = jnp.where((row == 0) & (lane < 32), late, 0.0)


def conv_backward(lengths, picked, z_one, z_two, d_three, flat):
    hbm = pl.BlockSpec(memory_space=pltpu.HBM)
    vmem = pl.BlockSpec(memory_space=pltpu.VMEM)
    return pl.pallas_call(
        conv_backward_kernel,
        in_specs=[pl.BlockSpec(memory_space=pltpu.SMEM)] + [hbm] * 5,
        out_specs=vmem,
        out_shape=jax.ShapeDtypeStruct((CONV_ROWS, 128), F32),
        scratch_shapes=[
            pltpu.VMEM((CONV_ROWS, 128), F32),
            pltpu.VMEM((2, 21, 4, GROUP, 640), BF16),
            pltpu.VMEM((2, 10, 2, 5, GROUP, 128), F32),
            pltpu.VMEM((2, 9, 5, GROUP, 128), F32),
            pltpu.VMEM((2, 28, GROUP, 128), F32),
            pltpu.VMEM((2, 10, 2, 6, GROUP, 128), BF16),
            pltpu.VMEM((2, 9, 5, GROUP, 128), BF16),
            pltpu.VMEM((10, 2, 5, GROUP, 128), F32),
            pltpu.VMEM((2, 11, 6, GROUP, 128), BF16),
            pltpu.VMEM((2, 11, 6, GROUP, 128), BF16),
            pltpu.VMEM((10, 2, 5, GROUP, 256), BF16),
            pltpu.VMEM((1024, 256), BF16),
            pltpu.VMEM((768, 256), BF16),
            pltpu.VMEM((1024, 128), F32),
            pltpu.VMEM((304, 128), F32),
            pltpu.VMEM((640, 128), F32),
            pltpu.VMEM((3, 8, 128), F32),
            pltpu.VMEM((256, 1024), F32),
            pltpu.VMEM((256, 1024), F32),
            pltpu.VMEM((256, 768), F32),
            pltpu.SemaphoreType.DMA((2, 4)),
            pltpu.SemaphoreType.DMA,
        ],
        compiler_params=pltpu.CompilerParams(vmem_limit_bytes=32 * 1024 * 1024),
        name="conv_backward",
    )(lengths, picked, z_one, z_two, d_three, flat)


HIGH = lax.Precision.HIGH
VECTORS_ROW = 3745
TIME_ROW = 3780


def mm(a, b):
    return lax.dot_general(
        a, b, (((1,), (0,)), ((), ())), precision=HIGH, preferred_element_type=F32
    )


def mm_nt(a, b):
    return lax.dot_general(
        a, b, (((1,), (1,)), ((), ())), precision=HIGH, preferred_element_type=F32
    )


def mm_tn(a, b):
    return lax.dot_general(
        a, b, (((0,), (0,)), ((), ())), precision=HIGH, preferred_element_type=F32
    )


def dot_nt(a, b):
    return lax.dot_general(a, b, (((1,), (1,)), ((), ())), preferred_element_type=F32)


def norm_parts(stream):
    centered = stream - jnp.mean(stream, -1, keepdims=True)
    spread = jnp.mean(centered * centered, -1, keepdims=True)
    scale = lax.rsqrt(spread + 1e-05)
    return centered * scale, scale


def norm_back(grad, unit, scale, gain):
    grad = grad * gain
    inner = jnp.mean(grad * unit, -1, keepdims=True)
    return scale * (grad - jnp.mean(grad, -1, keepdims=True) - unit * inner)


def column_sum(x):
    return jnp.sum(x, axis=0, keepdims=True)


def head_places():
    number = lax.broadcasted_iota(jnp.int32, (128, 128), 0) * ACT
    lane = lax.broadcasted_iota(jnp.int32, (128, 128), 1)
    row = lax.shift_right_logical(number, 7)
    return row + jnp.where(lane < jnp.bitwise_and(number, 127), 1, 0)


def roll_rows(held, sign):
    number = lax.broadcasted_iota(jnp.int32, (128, 128), 0) * ACT
    for k in range(7):
        moved = pltpu.roll(held, (sign * (1 << k)) % 128, 1)
        held = jnp.where(jnp.bitwise_and(number, 1 << k) > 0, moved, held)
    return held


def square_head(rows):
    place = head_places()
    held = jnp.zeros((128, 128), F32)
    for k in range(ACT):
        held = jnp.where(place == k, rows[k : k + 1], held)
    held = roll_rows(held, -1)
    lane = lax.broadcasted_iota(jnp.int32, (128, 128), 1)
    return jnp.where(lane < ACT, held, 0.0)


def flat_head(grads):
    place = head_places()
    lane = lax.broadcasted_iota(jnp.int32, (128, 128), 1)
    held = roll_rows(jnp.where(lane < ACT, grads, 0.0), 1)
    rows = [
        jnp.sum(jnp.where(place == k, held, 0.0), axis=0, keepdims=True) for k in range(ACT)
    ]
    return jnp.concatenate(rows + [jnp.zeros((24 - ACT, 128), F32)], axis=0)


def unpack_split(split_ref, qkv, output, up, up_bias, down):
    lane = lax.broadcasted_iota(jnp.int32, (32, 128), 1)
    for layer in range(LAYERS):
        base = layer * 385
        kinds = [[jnp.zeros((32, 128), F32) for j in range(4)] for kind in range(3)]
        for m in range(4):
            rows = [split_ref[m, pl.ds(base + k, 32, stride=3), :] for k in range(3)]
            inside = (lane >= 32 * m) & (lane < 32 * m + 32)
            for j in range(4):
                for kind in range(3):
                    spot = j * 96 + kind * 32
                    source = rows[spot // 128]
                    shift = (32 * m - spot % 128) % 128
                    moved = pltpu.roll(source, shift, 1) if shift else source
                    kinds[kind][j] = jnp.where(inside, moved, kinds[kind][j])
            output[layer, 32 * m : 32 * m + 32] = split_ref[m, base + 96 : base + 128]
            up[layer, :, 128 * m : 128 * m + 128] = split_ref[m, base + 128 : base + 256]
            up_bias[layer, :, 128 * m : 128 * m + 128] = split_ref[m, base + 256 : base + 257]
            down[layer, 128 * m : 128 * m + 128] = split_ref[m, base + 257 : base + 385]
        for kind in range(3):
            for j in range(4):
                qkv[layer, kind, pl.ds(j, 32, stride=4), :] = kinds[kind][j]


def pack_split(out_ref, qkv, output, up, up_bias, down):
    lane = lax.broadcasted_iota(jnp.int32, (32, 128), 1)
    for layer in range(LAYERS):
        base = layer * 385
        parts = [[qkv[layer, kind, pl.ds(j, 32, stride=4), :] for j in range(4)] for kind in range(3)]
        for m in range(4):
            rows = [jnp.zeros((32, 128), F32) for k in range(3)]
            for j in range(4):
                for kind in range(3):
                    spot = j * 96 + kind * 32
                    low = spot % 128
                    shift = (low - 32 * m) % 128
                    moved = pltpu.roll(parts[kind][j], shift, 1) if shift else parts[kind][j]
                    inside = (lane >= low) & (lane < low + 32)
                    rows[spot // 128] = jnp.where(inside, moved, rows[spot // 128])
            for k in range(3):
                out_ref[m, pl.ds(base + k, 32, stride=3), :] = rows[k]
            out_ref[m, base + 96 : base + 128] = output[layer, 32 * m : 32 * m + 32]
            out_ref[m, base + 128 : base + 256] = up[layer, :, 128 * m : 128 * m + 128]
            out_ref[m, base + 256 : base + 257] = up_bias[layer, :, 128 * m : 128 * m + 128]
            out_ref[m, base + 257 : base + 385] = down[layer, 128 * m : 128 * m + 128]
    for m in range(4):
        out_ref[m, 770:784] = jnp.zeros((14, 128), F32)


def former_body(
    slots,
    used,
    lengths_ref,
    returns_ref,
    actions_ref,
    head_ref,
    z_ref,
    small,
    times_all,
    encoder,
    weights,
    d_three_ref,
    d_encoder_ref,
    d_small_ref,
    d_times_ref,
    grads,
    chances,
    kept,
    sums,
    flats,
):
    qkv, output, up, up_bias, down = weights
    d_qkv, d_output, d_up, d_up_bias, d_down = grads
    rows = 3 * slots
    wins, steps = returns_ref.shape
    vec = [small[k : k + 1] for k in range(17)]
    table = small[17 : 17 + ACT]
    slot = lax.broadcasted_iota(jnp.int32, (slots, 1), 0)
    window = jnp.zeros((slots, 1), jnp.int32)
    begin = jnp.zeros((slots, 1), jnp.int32)
    end = jnp.int32(0)
    for w in range(wins - 1):
        end = end + lengths_ref[w]
        window = jnp.where(slot >= end, w + 1, window)
        begin = jnp.where(slot >= end, end, begin)
    moment = slot - begin
    valid = slot < used
    time_lane = lax.broadcasted_iota(jnp.int32, (slots, steps), 1)
    amount = jnp.zeros((slots, 1), F32)
    action = jnp.zeros((slots, 1), jnp.int32)
    for w in range(wins):
        here = (time_lane == moment) & (window == w)
        amount = amount + jnp.sum(
            jnp.where(here, returns_ref[w : w + 1], 0.0), axis=1, keepdims=True
        )
        action = action + jnp.sum(jnp.where(here, actions_ref[w : w + 1], 0), axis=1, keepdims=True)
    lane = lax.broadcasted_iota(jnp.int32, (slots, 128), 1)
    picks = jnp.where((lane == action) & valid, 1.0, 0.0)
    reward = jnp.tanh(amount * vec[14] + vec[15])
    table = jnp.concatenate([table, jnp.zeros((128 - ACT, 128), F32)], axis=0)
    move = jnp.tanh(mm(picks, table))
    sum_state = jnp.zeros((slots, 128), F32)
    for k in range(28):
        z = jnp.where(valid, z_ref[k, 0:slots], 0.0)
        high, low = two_parts(gelu_value(z))
        flats[0, 0:slots, k * 128 : (k + 1) * 128] = high
        flats[1, 0:slots, k * 128 : (k + 1) * 128] = low
    for part in range(2):
        sum_state = sum_state + fold_pair(dot(flats[part, 0:slots], encoder[...]))
    state = jnp.tanh(sum_state + vec[16])
    times = times_all[0:slots]
    stream = jnp.concatenate([reward + times, state + times, move + times], axis=0)

    def ids(axis):
        shape = (rows, 1) if axis == 0 else (1, rows)
        number = lax.broadcasted_iota(jnp.int32, shape, axis)
        kind = jnp.where(number >= 2 * slots, 2, jnp.where(number >= slots, 1, 0))
        return number - kind * slots, kind

    (slot_q, kind_q), (slot_k, kind_k) = ids(0), ids(1)

    def begin_of(slot_ids):
        found = jnp.zeros(slot_ids.shape, jnp.int32)
        end = jnp.int32(0)
        for w in range(wins - 1):
            end = end + lengths_ref[w]
            found = jnp.where(slot_ids >= end, end, found)
        return found

    order_q = slot_q * 3 + kind_q
    order_k = slot_k * 3 + kind_k
    allowed = (order_q >= order_k) & (slot_k >= begin_of(slot_q)) & (slot_k < used)
    head_of = lax.shift_right_logical(lax.broadcasted_iota(jnp.int32, (1, 128), 1), 4)
    heads = D // HD
    batch = 4 if slots <= HALF else 2

    def masked(x, masks):
        return jnp.concatenate([jnp.where(mask, x, jnp.zeros_like(x)) for mask in masks], axis=0)

    def unmasked(x, masks):
        held = jnp.where(masks[0], x[0:rows], 0.0)
        for k in range(1, batch):
            held = held + jnp.where(masks[k], x[k * rows : (k + 1) * rows], 0.0)
        return held

    tape = []
    for layer in range(LAYERS):
        gains = vec[6 * layer : 6 * layer + 6]
        unit_one, scale_one = norm_parts(stream)
        normed = unit_one * gains[0] + gains[1]
        wide = jnp.concatenate([qkv[layer, k] for k in range(3)], axis=1)
        mixed = mm(normed, wide)
        query_high, query_low = two_parts(mixed[:, :128] * 0.25)
        keys, values = pair(mixed[:, 128:256]), pair(mixed[:, 256:])
        kept[layer, 0, 0:rows] = query_high
        kept[layer, 1, 0:rows] = query_low
        for k in range(2):
            kept[layer, 2 + k, 0:rows] = keys[:, k * 128 : (k + 1) * 128]
            kept[layer, 4 + k, 0:rows] = values[:, k * 128 : (k + 1) * 128]
        sums[0, 0:rows] = jnp.zeros((rows, 128), F32)

        def attend(turn, carry, layer=layer):
            masks = [head_of == turn * batch + k for k in range(batch)]
            parts = [masked(kept[layer, k, 0:rows], masks) for k in range(2)]
            keys = [kept[layer, 2 + k, 0:rows] for k in range(2)]
            values = [kept[layer, 4 + k, 0:rows] for k in range(2)]
            scores = dot_nt(
                jnp.concatenate([parts[0], parts[0]], axis=1), jnp.concatenate(keys, axis=1)
            )
            scores = (scores + dot_nt(parts[1], keys[0])).reshape(batch, rows, rows)
            scores = jnp.where(allowed[None], scores, -1e30)
            peak = jnp.max(scores, -1, keepdims=True)
            chance = jnp.exp(scores - peak)
            chance = chance / jnp.sum(chance, -1, keepdims=True)
            high, low = two_parts(chance.reshape(batch * rows, rows))
            spot = pl.ds(pl.multiple_of(turn * (batch * rows), 64), batch * rows)
            chances[layer, 0, spot, 0:rows] = high
            chances[layer, 1, spot, 0:rows] = low
            seen = fold_pair(dot(high, jnp.concatenate(values, axis=1))) + dot(low, values[0])
            sums[0, 0:rows] += unmasked(seen, masks)
            return carry

        lax.fori_loop(0, heads // batch, attend, 0)
        context = sums[0, 0:rows]
        stream = stream + mm(context, output[layer]) + gains[4]
        unit_two, scale_two = norm_parts(stream)
        normed_two = unit_two * gains[2] + gains[3]
        inner, slope = gelu_both(mm(normed_two, up[layer]) + up_bias[layer])
        stream = stream + mm(inner, down[layer]) + gains[5]
        tape.append((unit_one, scale_one, unit_two, scale_two, inner, slope, context))
    end_stream = stream[slots : 2 * slots]
    unit, scale = norm_parts(end_stream)
    final = unit * vec[12] + vec[13]
    logits = jnp.where(lane < ACT, mm(final, head_ref[...]), -1e30)
    peak = jnp.max(logits, -1, keepdims=True)
    powers = jnp.exp(logits - peak)
    total = jnp.sum(powers, -1, keepdims=True)
    chosen = jnp.sum(jnp.where(lane == action, logits, 0.0), -1, keepdims=True)
    terms = jnp.where(valid, jnp.log(total) + peak - chosen, 0.0)
    loss = jnp.sum(terms, axis=0, keepdims=True)
    d_small_ref[72:80] = jnp.broadcast_to(loss, (8, 128))
    d_logits = jnp.where(valid, powers / total, 0.0) - picks
    d_small_ref[48:72] = flat_head(mm_tn(final, d_logits))
    d_final = mm_nt(d_logits, head_ref[...])
    d_vec = [None] * 17
    d_vec[12] = column_sum(d_final * unit)
    d_vec[13] = column_sum(d_final)
    d_end = norm_back(d_final, unit, scale, vec[12])
    blank = jnp.zeros((slots, 128), F32)
    d_stream = jnp.concatenate([blank, d_end, blank], axis=0)
    for layer in reversed(range(LAYERS)):
        unit_one, scale_one, unit_two, scale_two, inner, slope, context = tape[layer]
        gains = vec[6 * layer : 6 * layer + 6]
        d_vec[6 * layer + 5] = column_sum(d_stream)
        d_down[layer] = mm_tn(inner, d_stream)
        d_inner = mm_nt(d_stream, down[layer]) * slope
        d_up_bias[layer] = column_sum(d_inner)
        normed_two = unit_two * gains[2] + gains[3]
        d_up[layer] = mm_tn(normed_two, d_inner)
        d_normed = mm_nt(d_inner, up[layer])
        d_vec[6 * layer + 2] = column_sum(d_normed * unit_two)
        d_vec[6 * layer + 3] = column_sum(d_normed)
        d_stream = d_stream + norm_back(d_normed, unit_two, scale_two, gains[2])
        d_vec[6 * layer + 4] = column_sum(d_stream)
        d_output[layer] = mm_tn(context, d_stream)
        d_context = mm_nt(d_stream, output[layer])
        bases = d_context * context
        high, low = two_parts(d_context)
        for k in range(3):
            sums[k, 0:rows] = jnp.zeros((rows, 128), F32)
        kept[layer, 6, 0:rows] = high
        kept[layer, 7, 0:rows] = low
        sums[3, 0:rows] = bases

        def attend_back(turn, carry, layer=layer):
            masks = [head_of == turn * batch + k for k in range(batch)]
            query = [masked(kept[layer, k, 0:rows], masks) for k in range(2)]
            keys = [kept[layer, 2 + k, 0:rows] for k in range(2)]
            values = [kept[layer, 4 + k, 0:rows] for k in range(2)]
            d_seen = [masked(kept[layer, 6 + k, 0:rows], masks) for k in range(2)]
            base = jnp.sum(masked(sums[3, 0:rows], masks), -1, keepdims=True)
            spot = pl.ds(pl.multiple_of(turn * (batch * rows), 64), batch * rows)
            chance = [chances[layer, k, spot, 0:rows] for k in range(2)]
            d_chance = dot_nt(
                jnp.concatenate([d_seen[0], d_seen[0]], axis=1), jnp.concatenate(values, axis=1)
            )
            d_chance = d_chance + dot_nt(d_seen[1], values[0])
            d_scores = (chance[0].astype(F32) + chance[1].astype(F32)) * (d_chance - base)
            high, low = two_parts(d_scores)
            d_query = fold_pair(dot(high, jnp.concatenate(keys, axis=1))) + dot(low, keys[0])
            sums[0, 0:rows] += unmasked(d_query, masks)
            d_keys = fold_pair(dot_rows(high, jnp.concatenate(query, axis=1)))
            sums[1, 0:rows] += d_keys + dot_rows(low, query[0])
            d_values = fold_pair(dot_rows(chance[0], jnp.concatenate(d_seen, axis=1)))
            sums[2, 0:rows] += d_values + dot_rows(chance[1], d_seen[0])
            return carry

        lax.fori_loop(0, heads // batch, attend_back, 0)
        normed = unit_one * gains[0] + gains[1]
        d_mixed = jnp.concatenate(
            [sums[0, 0:rows] * 0.25, sums[1, 0:rows], sums[2, 0:rows]], axis=1
        )
        wide = jnp.concatenate([qkv[layer, k] for k in range(3)], axis=1)
        d_wide = mm_tn(normed, d_mixed)
        for k in range(3):
            d_qkv[layer, k] = d_wide[:, k * 128 : (k + 1) * 128]
        d_normed = mm_nt(d_mixed, wide)
        d_vec[6 * layer] = column_sum(d_normed * unit_one)
        d_vec[6 * layer + 1] = column_sum(d_normed)
        d_stream = d_stream + norm_back(d_normed, unit_one, scale_one, gains[0])
    d_reward, d_state, d_move = (d_stream[k * slots : (k + 1) * slots] for k in range(3))
    d_times_ref[0:slots] = jnp.where(valid, d_reward + d_state + d_move, 0.0)
    d_reward = d_reward * (1.0 - reward * reward)
    d_vec[14] = column_sum(d_reward * amount)
    d_vec[15] = column_sum(d_reward)
    d_move = d_move * (1.0 - move * move)
    d_small_ref[24:48] = mm_tn(picks, d_move)[0:24]
    d_state = jnp.where(valid, d_state * (1.0 - state * state), 0.0)
    d_vec[16] = column_sum(d_state)
    d_small_ref[0:24] = jnp.concatenate(d_vec + [jnp.zeros((7, 128), F32)], axis=0)
    high, low = two_parts(d_state)
    twice = jnp.concatenate([high, high], axis=1)
    both = jnp.concatenate([high, low], axis=1)
    d_flat = dot_nt(twice, encoder[...]) + dot_nt(low, encoder[:, 0:128])
    d_block = dot_rows(flats[0, 0:slots], both) + dot_rows(flats[1, 0:slots], both)
    d_block = fold_pair(d_block)
    for k in range(28):
        z = jnp.where(valid, z_ref[k, 0:slots], 0.0)
        d_three_ref[k, 0:slots] = d_flat[:, k * 128 : (k + 1) * 128] * gelu_both(z)[1]
        y, v = divmod(k, 4)
        for o in range(2):
            if 2 * v + o < 7:
                d_encoder_ref[pl.ds(y * 7 + 2 * v + o, 64, stride=49), :] = d_block[
                    k * 128 + o * 64 : k * 128 + (o + 1) * 64
                ]


def former_kernel(
    packed,
    lengths_ref,
    starts_ref,
    index_ref,
    returns_ref,
    actions_ref,
    z_from,
    flat_ref,
    *refs,
):
    if packed:
        split_ref, refs = refs[0], refs[1:]
    else:
        given, refs = refs[:5], refs[5:]
    (d_three_to, rows_ref), refs = refs[:2], refs[2:]
    if packed:
        parts, refs = refs[:8], refs[8:]
        (d_encoder_ref, d_small_ref, d_split), refs = refs[:3], refs[3:]
        weights, grads, refs = refs[:5], refs[5:10], refs[10:]
    else:
        (d_encoder_ref, d_small_ref), grads, refs = refs[:2], refs[2:7], refs[7:]
        weights = given
    (raw, near, small, rows_raw, times_all, encoder, chances, kept, sums, flats), refs = (
        refs[:10],
        refs[10:],
    )
    z_ref, d_three_ref, head_ref, sem = refs
    used = jnp.int32(0)
    wins = lengths_ref.shape[0]
    for w in range(wins):
        used = used + lengths_ref[w]

    def z_copy(slots):
        return pltpu.make_async_copy(
            z_from.at[:, pl.ds(0, slots)], z_ref.at[:, pl.ds(0, slots)], sem.at[wins + 3]
        )

    def z_back(slots):
        return pltpu.make_async_copy(
            d_three_ref.at[:, pl.ds(0, slots)], d_three_to.at[:, pl.ds(0, slots)], sem.at[wins + 3]
        )

    copies = [
        pltpu.make_async_copy(flat_ref.at[pl.ds(608, 3144)], raw, sem.at[0]),
        pltpu.make_async_copy(flat_ref.at[pl.ds(3744, 48)], rows_raw.at[wins], sem.at[1]),
        pltpu.make_async_copy(
            flat_ref.at[pl.ds(7872, 24)], rows_raw.at[wins + 1, pl.ds(0, 24)], sem.at[2]
        ),
    ]
    offsets = []
    for w in range(wins):
        row = TIME_ROW + starts_ref[w]
        low = pl.multiple_of(lax.div(row, 8) * 8, 8)
        offsets.append(row - low)
        copies.append(
            pltpu.make_async_copy(
                flat_ref.at[pl.ds(low, 40)], rows_raw.at[w, pl.ds(0, 40)], sem.at[3 + w]
            )
        )
    for copy in copies:
        copy.start()

    @pl.when(used <= HALF)
    def few_states():
        z_copy(HALF).start()

    @pl.when(used > HALF)
    def many_states():
        z_copy(ROOM).start()

    if packed:
        unpack_split(split_ref, *weights)
    for copy in copies:
        copy.wait()
    lane = lanes()

    def straight(first, second):
        return jnp.where(lane < 96, pltpu.roll(first, 96, 1), pltpu.roll(second, 96, 1))

    def turn(step, carry):
        spot = pl.multiple_of(step * 64, 64)
        near[pl.ds(spot, 64)] = straight(raw[pl.ds(spot + 1, 64)], raw[pl.ds(spot + 2, 64)])
        return carry

    lax.fori_loop(0, 49, turn, 0)
    for k in range(28):
        y, v = divmod(k, 4)
        halves = []
        for o in range(2):
            if 2 * v + o < 7:
                halves.append(near[pl.ds(y * 7 + 2 * v + o, 64, stride=49), :])
            else:
                halves.append(jnp.zeros((64, 128), F32))
        encoder[k * 128 : (k + 1) * 128] = pair(jnp.concatenate(halves, axis=0))
    small[...] = straight(rows_raw[wins, 1:41], rows_raw[wins, 2:42])
    head_ref[...] = square_head(
        straight(rows_raw[wins + 1, 4:22], rows_raw[wins + 1, 5:23])
    )
    times_all[...] = jnp.zeros(times_all.shape, F32)
    begin = 0
    row = lax.broadcasted_iota(jnp.int32, (32, 1), 0)
    for w in range(wins):
        rows = straight(
            rows_raw[w, pl.ds(offsets[w], 32)], rows_raw[w, pl.ds(offsets[w] + 1, 32)]
        )
        times_all[pl.ds(begin, 32)] = jnp.where(row < lengths_ref[w], rows, 0.0)
        begin = begin + lengths_ref[w]
    rows_ref[...] = jnp.zeros(rows_ref.shape, F32)
    note = jnp.zeros((1, 128), F32)
    for w in range(wins):
        note = jnp.where(lane == w, lengths_ref[w].astype(F32), note)
        note = jnp.where(lane == wins + w, starts_ref[w].astype(F32), note)
    rows_ref[ROOM : ROOM + 1] = note
    d_small_ref[...] = jnp.zeros(d_small_ref.shape, F32)

    def run(slots):
        z_copy(slots).wait()
        former_body(
            slots,
            used,
            lengths_ref,
            returns_ref,
            actions_ref,
            head_ref,
            z_ref,
            small,
            times_all,
            encoder,
            weights,
            d_three_ref,
            d_encoder_ref,
            d_small_ref,
            rows_ref,
            grads,
            chances,
            kept,
            sums,
            flats,
        )
        z_back(slots).start()

    @pl.when(used <= HALF)
    def few():
        run(HALF)

    @pl.when(used > HALF)
    def many():
        run(ROOM)

    if packed:
        count = d_small_ref.shape[0] // 4
        pack_split(d_split, *grads)
        for k in range(4):
            parts[k][...] = d_split[jnp.bitwise_xor(index_ref[0], k)]
            e = jnp.bitwise_xor(index_ref[1], k)
            held = d_encoder_ref[pl.ds(pl.multiple_of(e * 784, 8), 784)]
            parts[4 + k][0:784] = held
            held = d_small_ref[pl.ds(pl.multiple_of(e * count, 8), count)]
            parts[4 + k][784 : 784 + count] = held

    @pl.when(used <= HALF)
    def few_end():
        z_back(HALF).wait()

    @pl.when(used > HALF)
    def many_end():
        z_back(ROOM).wait()


def former(lengths, starts, index, returns, actions, z_three, flat, weights, small_rows, packed):
    smem = pl.BlockSpec(memory_space=pltpu.SMEM)
    vmem = pl.BlockSpec(memory_space=pltpu.VMEM)
    hbm = pl.BlockSpec(memory_space=pltpu.HBM)
    wins = lengths.shape[0]
    canonical = [
        (LAYERS, 3, 128, 128),
        (LAYERS, 128, 128),
        (LAYERS, 128, FF),
        (LAYERS, 1, FF),
        (LAYERS, FF, 128),
    ]
    outs, out_specs = [(28, ROOM, 128), (ROOM + 8, 128)], [hbm, vmem]
    if packed:
        outs += [(784, 128)] * 4 + [(784 + small_rows // 4, 128)] * 4
        out_specs += [vmem] * 8
        scratch = [
            pltpu.VMEM((3136, 128), F32),
            pltpu.VMEM((small_rows, 128), F32),
            pltpu.VMEM((4, 784, 128), F32),
        ]
        scratch += [pltpu.VMEM(shape, F32) for shape in canonical] * 2
    else:
        outs += [(3136, 128), (small_rows, 128)] + canonical
        out_specs += [vmem] * 7
        scratch = []
    rows = 3 * ROOM
    scratch += [
        pltpu.VMEM((3144, 128), F32),
        pltpu.VMEM((3136, 128), F32),
        pltpu.VMEM((40, 128), F32),
        pltpu.VMEM((wins + 2, 48, 128), F32),
        pltpu.VMEM((ROOM + 32, 128), F32),
        pltpu.VMEM((3584, 256), BF16),
        pltpu.VMEM((LAYERS, 2, 8 * rows, rows), BF16),
        pltpu.VMEM((LAYERS, 8, rows, 128), BF16),
        pltpu.VMEM((4, rows, 128), F32),
        pltpu.VMEM((2, ROOM, 3584), BF16),
        pltpu.VMEM((28, ROOM, 128), F32),
        pltpu.VMEM((28, ROOM, 128), F32),
        pltpu.VMEM((128, 128), F32),
        pltpu.SemaphoreType.DMA((wins + 4,)),
    ]
    return pl.pallas_call(
        partial(former_kernel, packed),
        in_specs=[smem] * 3 + [vmem] * 2 + [hbm] * 2 + [vmem] * len(weights),
        out_specs=out_specs,
        out_shape=[jax.ShapeDtypeStruct(shape, F32) for shape in outs],
        scratch_shapes=scratch,
        compiler_params=pltpu.CompilerParams(vmem_limit_bytes=46 * 1024 * 1024),
        name="transformer_step",
    )(lengths, starts, index, returns, actions, z_three, flat, *weights)


SMALL = [("vectors", 24), ("action_table", 24), ("head", 24), ("loss", 8)]
FIELD_ROWS = 8200
EARLY_ROWS = CONV_ROWS + 3136
TABLE_AT = CONV_ROWS + 3136 + 17 + ACT


def round_up(number, grain):
    return -(-number // grain) * grain


def chunk_of(tiles):
    return max(size for size in range(1, 9) if tiles % size == 0)


def mesh_bits(dp_size, mp_size):
    dp_bits = [("dp", k) for k in range(dp_size.bit_length() - 1)]
    mp_bits = [("mp", k) for k in range(mp_size.bit_length() - 1)]
    middle = (len(dp_bits) - 1) // 2
    return mp_bits[:1], mp_bits[1:], dp_bits[:middle], dp_bits[middle:]


def reduce_kernel(plan, *refs):
    mp_size, quarter, share = plan["mp_size"], plan["quarter"], plan["share"]
    split_parts, own_parts, conv_ref = refs[:mp_size], refs[mp_size : 2 * mp_size], refs[2 * mp_size]
    refs = refs[2 * mp_size + 1 :]
    (early_out, small_out, split_out, square_out), refs = refs[:4], refs[4:]
    (split_stage, own_stage, work, landing, split_total, own_total, conv_total), refs = (
        refs[:7],
        refs[7:],
    )
    tiles, tile_in, load_sem, send_sem, recv_sem, store_sem = refs
    spots = {"dp": lax.axis_index("dp"), "mp": lax.axis_index("mp")}
    cores, ys, xs, zs = plan["bits"]
    bits = cores + ys + xs + zs
    slots = iter(range(plan["copies"]))

    def value(bit):
        return lax.rem(lax.div(spots[bit[0]], 1 << bit[1]), 2)

    def partner(bit):
        axis, k = bit
        place = dict(spots)
        place[axis] = spots[axis] + (1 - 2 * value(bit)) * (1 << k)
        return (place["dp"], place["mp"])

    def send(source, target, bit):
        slot = next(slots)
        copy = pltpu.make_async_remote_copy(
            src_ref=source,
            dst_ref=target,
            send_sem=send_sem.at[slot],
            recv_sem=recv_sem.at[slot],
            device_id=partner(bit),
            device_id_type=pl.DeviceIdType.MESH,
        )
        copy.start()
        return copy

    loads = []
    for k in range(mp_size):
        for parts, stage in ((own_parts, own_stage), (split_parts, split_stage)):
            copy = pltpu.make_async_copy(parts[k], stage.at[k], load_sem.at[len(loads)])
            loads.append(copy)
    conv_tiles = CONV_ROWS // 8
    target = work.at[pl.ds(plan["conv"], conv_tiles)]
    loads.append(pltpu.make_async_copy(conv_ref, target, load_sem.at[len(loads)]))
    for load in loads:
        load.start()

    def wipe(target, start, count):
        if count > 0:
            target[start : start + count] = jnp.zeros((count, 8, 128), F32)

    wipe(work, plan["conv"] + conv_tiles, plan["conv_size"] - conv_tiles)
    wipe(work, plan["split"] + quarter, plan["split_size"] - quarter)
    wipe(work, plan["own"] + quarter + share, plan["own_size"] - quarter - share)
    barrier = pltpu.get_barrier_semaphore()
    for bit in bits:
        pl.semaphore_signal(
            barrier, inc=1, device_id=partner(bit), device_id_type=pl.DeviceIdType.MESH
        )
    pl.semaphore_wait(barrier, len(bits))

    def sum_into(target, start, pieces, count):
        chunk = chunk_of(count)

        def body(turn, carry):
            held = pieces[0][0][pl.ds(pieces[0][1] + turn * chunk, chunk)]
            for source, at in pieces[1:]:
                held = held + source[pl.ds(at + turn * chunk, chunk)]
            target[pl.ds(start + turn * chunk, chunk)] = held
            return carry

        lax.fori_loop(0, count // chunk, body, 0)

    class Stream:
        def __init__(self, base, size, order, total, total_at):
            self.base, self.size, self.order = base, size, order
            self.total, self.at = total, total_at
            self.land = base
            self.flight = None
            self.step = 0
            self.start = base

        def halve(self):
            if self.flight is not None:
                copy, half, land, keep = self.flight
                copy.wait()
                sum_into(work, keep, [(work, keep), (landing, land)], half)
                self.base, self.size, self.flight = keep, half, None
            if self.step < len(self.order):
                bit = self.order[self.step]
                half = self.size // 2
                mine = value(bit)
                keep = self.base + mine * half
                give = self.base + (1 - mine) * half
                copy = send(
                    work.at[pl.ds(give, half)], landing.at[pl.ds(self.land, half)], bit
                )
                self.flight = (copy, half, self.land, keep)
                self.land += half
                self.step += 1

        def turn(self):
            self.at = self.at + (self.base - self.start)
            sum_into(self.total, self.at, [(work, self.base)], self.size)
            self.step = 0

        def double(self):
            if self.flight is not None:
                copy, low = self.flight
                copy.wait()
                self.at, self.size, self.flight = low, self.size * 2, None
            if self.step < len(self.order):
                bit = self.order[len(self.order) - 1 - self.step]
                region = self.total.at[pl.ds(self.at, self.size)]
                copy = send(region, region, bit)
                self.flight = (copy, self.at - value(bit) * self.size)
                self.step += 1

        def squares(self, keep):
            held = work[pl.ds(self.base, self.size)]
            if keep is not None:
                tile = lax.broadcasted_iota(jnp.int32, (self.size, 8, 128), 0)
                held = jnp.where(keep(tile + self.base), held, 0.0)
            return jnp.sum(held * held, axis=0)

    sharing = cores + xs
    seat = sum(value(bit) * (1 << k) for k, bit in enumerate(sharing))

    def keep_own(tile):
        place = tile - plan["own"] - quarter
        return (place < 0) | (place + seat * share < 9)

    class Quarter:
        def __init__(self, stream, offset, order):
            self.at = stream.base - stream.start + offset
            self.size, self.order = stream.size, order
            self.held, self.flights, self.step = [0], [], 0
            sum_into(own_total.at[seat], self.at, [(work, stream.base)], stream.size)

        def region(self, offset):
            index = seat
            for k, bit in enumerate(sharing):
                if offset & (1 << k):
                    index = index + (1 - 2 * value(bit)) * (1 << k)
            return own_total.at[index, pl.ds(self.at, self.size)]

        def double(self):
            if self.flights:
                for copy in self.flights:
                    copy.wait()
                bit = self.order[self.step - 1]
                if bit in sharing:
                    turned = 1 << sharing.index(bit)
                    self.held = self.held + [offset | turned for offset in self.held]
                else:
                    self.at = self.at - value(bit) * self.size
                    self.size *= 2
                self.flights = []
            if self.step < len(self.order):
                bit = self.order[self.step]
                for offset in self.held:
                    region = self.region(offset)
                    self.flights.append(send(region, region, bit))
                self.step += 1

    first, second = plan["cut"]
    own_first, own_second = ys + zs, zs[:1] + ys + zs[1:]
    split_first, split_second = xs + zs, zs[:1] + xs + zs[1:]
    own = [
        Stream(plan["own"], first, own_first, None, 0),
        Stream(plan["own"] + first, plan["own_size"] - first, own_second, None, 0),
    ]
    split = [
        Stream(plan["split"], second, split_first, split_total, 0),
        Stream(
            plan["split"] + second,
            plan["split_size"] - second,
            split_second,
            split_total,
            second,
        ),
    ]
    conv = Stream(plan["conv"], plan["conv_size"], bits, conv_total, 0)
    for load in loads:
        load.wait()
    sum_into(
        work,
        plan["own"],
        [(own_stage.at[k], 0) for k in range(mp_size)],
        quarter + share,
    )
    for stream in own + [conv]:
        stream.halve()
    sum_into(work, plan["split"], [(split_stage.at[k], 0) for k in range(mp_size)], quarter)
    steps = len(own_first)
    for step in range(steps):
        for stream in own + [conv]:
            stream.halve()
        if step == 0:
            for stream in split:
                stream.halve()
    squares = jnp.zeros((8, 128), F32)
    for stream in own:
        squares = squares + stream.squares(keep_own)
    orders = [
        list(reversed(own_first)) + xs + cores,
        list(reversed(own_second[1:])) + xs + own_second[:1] + cores,
    ]
    quarters = [Quarter(own[0], 0, orders[0]), Quarter(own[1], first, orders[1])]
    for piece in quarters:
        piece.double()
    for step in range(steps):
        for piece in quarters:
            piece.double()
        conv.halve()
        for stream in split:
            stream.halve()
    for stream in split:
        squares = squares + stream.squares(None)
        stream.turn()
        stream.double()
    while conv.flight is not None:
        for piece in quarters:
            piece.double()
        conv.halve()
    squares = squares + conv.squares(None)
    conv.turn()
    conv.double()
    tiles[0] = squares
    tile_flight = send(tiles.at[0], tile_in.at[0], bits[0])
    rounds = 1
    while rounds <= len(bits) or conv.flight is not None or quarters[0].flights:
        for stream in quarters + [conv] + split:
            stream.double()
        if rounds <= len(bits):
            tile_flight.wait()
            tiles[rounds] = tiles[rounds - 1] + tile_in[rounds - 1]
            if rounds < len(bits):
                tile_flight = send(tiles.at[rounds], tile_in.at[rounds], bits[rounds])
        rounds += 1
    square_out[...] = tiles[len(bits)]
    stores = [
        (conv_total.at[pl.ds(0, conv_tiles)], early_out.at[pl.ds(0, conv_tiles)]),
        (split_total.at[pl.ds(0, quarter)], split_out),
    ]
    for m in range(mp_size):
        rows = pl.ds(conv_tiles + m * quarter, quarter)
        stores.append((own_total.at[m, pl.ds(0, quarter)], early_out.at[rows]))
        rows = pl.ds(m * share, share)
        stores.append((own_total.at[m, pl.ds(quarter, share)], small_out.at[rows]))
    stores = [
        pltpu.make_async_copy(source, target, store_sem.at[number])
        for number, (source, target) in enumerate(stores)
    ]
    for copy in stores:
        copy.start()
    for copy in stores:
        copy.wait()


def reduce_all(split_parts, own_parts, conv, dp_size, mp_size):
    bits = mesh_bits(dp_size, mp_size)
    steps = sum(len(part) for part in bits)
    dp_steps = dp_size.bit_length() - 1
    quarter = split_parts[0].shape[0] // 8
    share = own_parts[0].shape[0] // 8 - quarter
    own_size = round_up(quarter + share, dp_size)
    split_size = round_up(quarter, dp_size)
    conv_size = round_up(CONV_ROWS // 8, dp_size * mp_size)
    places, at = {}, 0
    for name, size in [("split", split_size), ("own", own_size), ("conv", conv_size)]:
        places[name] = at
        at += size
    cut = (round_up(own_size // 2, dp_size), round_up(split_size // 2, dp_size))
    copies = 6 * dp_steps + 3 * steps + 2 * (dp_steps + mp_size * mp_size)
    plan = dict(
        places,
        mp_size=mp_size,
        quarter=quarter,
        share=share,
        bits=bits,
        copies=copies,
        split_size=split_size,
        own_size=own_size,
        conv_size=conv_size,
        cut=cut,
    )
    vmem = pl.BlockSpec(memory_space=pltpu.VMEM)
    any_spec = pl.BlockSpec(memory_space=pl.ANY)
    arrays = [*split_parts, *own_parts, conv]
    loads = len(arrays)

    def tiled(size, *lead):
        return pltpu.VMEM((*lead, size, 8, 128), F32)

    outs = [(EARLY_ROWS // 8, 8, 128), (share * mp_size, 8, 128), (quarter, 8, 128), (8, 128)]
    results = pl.pallas_call(
        partial(reduce_kernel, plan),
        in_specs=[any_spec] * loads,
        out_specs=[any_spec, any_spec, any_spec, vmem],
        out_shape=[jax.ShapeDtypeStruct(shape, F32) for shape in outs],
        scratch_shapes=[
            tiled(quarter, mp_size),
            tiled(quarter + share, mp_size),
            tiled(at),
            tiled(at),
            tiled(split_size),
            tiled(own_size, mp_size),
            tiled(conv_size),
            pltpu.VMEM((steps + 1, 8, 128), F32),
            pltpu.VMEM((steps, 8, 128), F32),
            pltpu.SemaphoreType.DMA((loads,)),
            pltpu.SemaphoreType.DMA((copies,)),
            pltpu.SemaphoreType.DMA((copies,)),
            pltpu.SemaphoreType.DMA((2 + 2 * mp_size,)),
        ],
        compiler_params=pltpu.CompilerParams(
            collective_id=1, has_side_effects=True, vmem_limit_bytes=20 * 1024 * 1024
        ),
        name="reduce_gradients",
    )(*[array.reshape(-1, 8, 128) for array in arrays])
    return [held.reshape(-1, 128) for held in results]


FLAT_ROWS = 7896
BLOCK_ROWS = 1024
LATE = 609
SPAN = 40


def adam_kernel(
    wins,
    early_ref,
    rows_ref,
    small_ref,
    split_ref,
    square_ref,
    weight_ref,
    first_ref,
    second_ref,
    split_weight_ref,
    split_first_ref,
    split_second_ref,
    new_ref,
    new_first_ref,
    new_second_ref,
    low_ref,
    split_new_ref,
    split_new_first_ref,
    split_new_second_ref,
    split_low_ref,
    scalar_ref,
    split_in,
    split_out,
    field,
    rows,
    notes,
    marks,
    pulled,
    factor_ref,
    pull_sem,
    load_sem,
    split_sem,
):
    step = pl.program_id(0)
    last = pl.num_programs(0) - 1
    lane = lax.broadcasted_iota(jnp.int32, (1, 128), 1)

    def pull(block, slot):
        start = pl.multiple_of(block * BLOCK_ROWS, BLOCK_ROWS)
        return pltpu.make_async_copy(
            field.at[pl.ds(start, BLOCK_ROWS + 8)], pulled.at[slot], pull_sem.at[slot]
        )

    def update(weights, first, second, grads):
        first = beta_first * first + (1 - beta_first) * grads
        second = beta_second * second + (1 - beta_second) * grads * grads
        fix_one = 1.0 / (1 - beta_first**STEP)
        fix_two = 1.0 / (1 - beta_second**STEP)
        weights = weights - learn_rate * (
            first * fix_one / (jnp.sqrt(second * fix_two) + adam_epsilon) + weight_decay * weights
        )
        return weights, first, second

    def sum_of(tile):
        held = jnp.sum(jnp.sum(tile, axis=0, keepdims=True), axis=1, keepdims=True)
        return jnp.broadcast_to(held, (1, 128))

    slot = lax.rem(step, 2)
    split_loads = [
        pltpu.make_async_copy(ref, split_in.at[k], split_sem.at[k])
        for k, ref in enumerate((split_weight_ref, split_first_ref, split_second_ref))
    ]
    split_stores = [
        pltpu.make_async_copy(split_out.at[k], ref, split_sem.at[3 + k])
        for k, ref in enumerate((split_new_ref, split_new_first_ref, split_new_second_ref))
    ]

    @pl.when(step == 0)
    def prepare():
        for load in split_loads:
            load.start()
        load_rows = pltpu.make_async_copy(rows_ref, rows, load_sem.at[0])
        load_early = pltpu.make_async_copy(
            early_ref, field.at[pl.ds(0, EARLY_ROWS)], load_sem.at[1]
        )
        load_rows.start()
        load_early.start()
        late = FIELD_ROWS - EARLY_ROWS
        field[EARLY_ROWS:FIELD_ROWS] = jnp.zeros((late, 128), F32)
        load_rows.wait()
        stride = ROOM + 8
        devices = rows.shape[0] // stride
        notes[...] = rows[pl.ds(ROOM, devices, stride=stride), :]
        mark = pltpu.make_async_copy(notes, marks, load_sem.at[2])
        mark.start()
        mark.wait()
        place = lax.broadcasted_iota(jnp.int32, (SPAN, ROOM), 0)
        slot_of = lax.broadcasted_iota(jnp.int32, (SPAN, ROOM), 1)

        def scatter(turn, carry):
            spots, found = [], []
            for k in range(4):
                device = turn * 4 + k
                begin = jnp.int32(0)
                picks = []
                for w in range(wins):
                    length = marks[device, w].astype(jnp.int32)
                    row = marks[device, wins + w].astype(jnp.int32) + TABLE_AT
                    low = lax.div(row, 8) * 8
                    inside = (slot_of >= begin) & (slot_of < begin + length)
                    inside = inside & (place - slot_of == row - low - begin)
                    picks.append(jnp.where(inside, 1.0, 0.0).astype(BF16))
                    spots.append(low)
                    begin = begin + length
                held = pair(rows[pl.ds(pl.multiple_of(device * stride, 8), ROOM)])
                found.append(fold_pair(dot(jnp.concatenate(picks, axis=0), held)))
            for k in range(4):
                for w in range(wins):
                    spot = pl.ds(pl.multiple_of(spots[k * wins + w], 8), SPAN)
                    field[spot] = field[spot] + found[k][w * SPAN : (w + 1) * SPAN]
            return carry

        lax.fori_loop(0, devices // 4, scatter, 0)

        def fold(turn, carry):
            spot = pl.multiple_of(EARLY_ROWS + turn * 64, 8)
            held = field[pl.ds(spot, 64)]
            return carry + jnp.sum((held * held).reshape(8, 8, 128), axis=0)

        squares = lax.fori_loop(0, late // 64, fold, square_ref[...])
        at = EARLY_ROWS
        for name_at, count in [(0, 17), (24, ACT)]:
            field[at : at + count] = small_ref[name_at : name_at + count]
            at += count
        at = TABLE_AT + TSTEPS
        field[at : at + ACT] = small_ref[48 : 48 + ACT]
        lane_all = lax.broadcasted_iota(jnp.int32, notes.shape, 1)
        count = sum_of(jnp.where(lane_all < wins, notes[...], 0.0))
        seed = 1.0 / count
        norm = jnp.sqrt(sum_of(squares)) * seed
        factor = jnp.minimum(1.0, clip_limit / (norm + 1e-06)) * seed
        factor_ref[...] = jnp.broadcast_to(factor, (8, 128))
        loss = small_ref[72:73]
        row = lax.broadcasted_iota(jnp.int32, (8, 128), 0)
        scalar_ref[...] = jnp.where(row == 0, norm, jnp.where(row == 1, loss, count))
        load_early.wait()
        pull(0, 0).start()

    @pl.when(step < last)
    def ahead():
        pull(step + 1, 1 - slot).start()

    @pl.when(step == 1)
    def split():
        for load in split_loads:
            load.wait()
        count = split_in.shape[1]
        outs = update(*[split_in[k] for k in range(3)], split_ref[0:count] * factor_ref[0:1])
        for k in range(3):
            split_out[k] = outs[k]
        split_low_ref[...] = outs[0].astype(BF16)
        for store in split_stores:
            store.start()

    @pl.when(step == last)
    def split_end():
        for store in split_stores:
            store.wait()

    pull(step, slot).wait()
    early = pulled[slot, 0:BLOCK_ROWS]
    own = pltpu.roll(pulled[slot, 7 : BLOCK_ROWS + 7], 32, 1)
    before = pltpu.roll(pulled[slot, 6 : BLOCK_ROWS + 6], 32, 1)
    row = lax.broadcasted_iota(jnp.int32, (BLOCK_ROWS, 1), 0) + step * BLOCK_ROWS
    grads = jnp.where(lane < 32, jnp.where(row == LATE, early, before), own)
    grads = jnp.where(row < LATE, early, grads)
    outs = update(weight_ref[...], first_ref[...], second_ref[...], grads * factor_ref[0:1])
    new_ref[...], new_first_ref[...], new_second_ref[...] = outs
    low_ref[...] = outs[0].astype(BF16)


def adam_all(early, rows, small, split_grad, square, shared, split, wins):
    grid = -(-FLAT_ROWS // BLOCK_ROWS)
    flat_spec = pl.BlockSpec((BLOCK_ROWS, 128), lambda i: (i, 0))
    split_rows = split[0].shape[0]
    devices = rows.shape[0]

    def whole(shape):
        return pl.BlockSpec(shape, lambda i: (0,) * len(shape))

    shared_out = jax.ShapeDtypeStruct((FLAT_ROWS, 128), F32)
    split_out = jax.ShapeDtypeStruct((split_rows, 128), F32)
    any_spec = pl.BlockSpec(memory_space=pl.ANY)
    return pl.pallas_call(
        partial(adam_kernel, wins),
        grid=(grid,),
        in_specs=[
            any_spec,
            any_spec,
            whole(small.shape),
            whole(split_grad.shape),
            whole((8, 128)),
            flat_spec,
            flat_spec,
            flat_spec,
            any_spec,
            any_spec,
            any_spec,
        ],
        out_specs=[flat_spec] * 4
        + [any_spec] * 3
        + [whole((split_rows, 128)), whole((8, 128))],
        out_shape=[shared_out] * 3
        + [jax.ShapeDtypeStruct((FLAT_ROWS, 128), BF16)]
        + [split_out] * 3
        + [jax.ShapeDtypeStruct((split_rows, 128), BF16)]
        + [jax.ShapeDtypeStruct((8, 128), F32)],
        scratch_shapes=[
            pltpu.VMEM((3, split_rows, 128), F32),
            pltpu.VMEM((3, split_rows, 128), F32),
            pltpu.VMEM((FIELD_ROWS, 128), F32),
            pltpu.VMEM((devices * (ROOM + 8), 128), F32),
            pltpu.VMEM((devices, 128), F32),
            pltpu.SMEM((devices, 128), F32),
            pltpu.VMEM((2, BLOCK_ROWS + 8, 128), F32),
            pltpu.VMEM((8, 128), F32),
            pltpu.SemaphoreType.DMA((2,)),
            pltpu.SemaphoreType.DMA((3,)),
            pltpu.SemaphoreType.DMA((6,)),
        ],
        compiler_params=pltpu.CompilerParams(vmem_limit_bytes=36 * 1024 * 1024),
        name="adam_update",
    )(
        early,
        rows.reshape(devices * (ROOM + 8), 128),
        small,
        split_grad,
        square,
        *shared,
        *split,
    )


def per_device(
    frames,
    returns,
    actions,
    starts,
    lengths,
    shared_weights,
    shared_first,
    shared_second,
    split_weights,
    split_first,
    split_second,
):
    dp_size, mp_size = lax.axis_size("dp"), lax.axis_size("mp")
    narrow = D // mp_size
    hidden_width = FF // mp_size
    wins, steps = returns.shape
    width = split_weights.shape[0]
    split_rows = width // 128
    packed = narrow == 32
    own_rows = split_weights.reshape(split_rows, 128)
    split_all = lax.all_gather(own_rows, "mp", axis=0)
    flat = shared_weights.reshape(FLAT_ROWS, 128)
    picked, z_one, z_two, z_three = conv_forward(lengths, frames, flat)
    if packed:
        weights = [split_all]
    else:
        layers, layers_back = jax.vjp(
            lambda held: assemble(held, mp_size, narrow, hidden_width), split_all.reshape(-1)
        )
        weights = [
            jnp.stack([layer["qkv"].transpose(1, 0, 2) for layer in layers]),
            jnp.stack([layer["output"] for layer in layers]),
            jnp.stack([layer["up"] for layer in layers]),
            jnp.stack([layer["up_bias"][None] for layer in layers]),
            jnp.stack([layer["down"] for layer in layers]),
        ]
    small_rows = round_up(sum(rows for name, rows in SMALL), 8 * mp_size)
    cores, ys, xs, zs = mesh_bits(dp_size, mp_size)
    seat = jnp.bitwise_and(lax.axis_index("mp"), 1)
    seat = seat + 2 * jnp.bitwise_and(lax.axis_index("dp"), (1 << len(xs)) - 1)
    index = jnp.stack([lax.axis_index("mp"), seat])
    results = former(
        lengths, starts, index, returns, actions, z_three, flat, weights, small_rows, packed
    )
    d_three, rows = results[:2]
    rows_all = lax.all_gather(rows, ("dp", "mp"), axis=0)
    quarter = 3136 // mp_size
    if packed:
        split_parts, own_parts = results[2:6], results[6:]
    else:
        d_encoder, d_small, d_qkv, d_output, d_up, d_up_bias, d_down = results[2:]
        grad_layers = [
            dict(
                qkv=d_qkv[layer].transpose(1, 0, 2),
                output=d_output[layer],
                up=d_up[layer],
                up_bias=d_up_bias[layer, 0],
                down=d_down[layer],
            )
            for layer in range(LAYERS)
        ]
        gathered = layers_back(grad_layers)[0].reshape(mp_size, split_rows, 128)
        gathered = jnp.pad(gathered, ((0, 0), (0, quarter - split_rows), (0, 0)))
        encoder = d_encoder.reshape(mp_size, quarter, 128)
        small = d_small.reshape(mp_size, -1, 128)
        every = jnp.concatenate([encoder, small], axis=1)

        def turned(held, own):
            return [
                lax.dynamic_index_in_dim(held, jnp.bitwise_xor(own, k), 0, keepdims=False)
                for k in range(mp_size)
            ]

        split_parts, own_parts = turned(gathered, index[0]), turned(every, index[1])
    split_parts, own_parts = list(split_parts), list(own_parts)
    for k in range(1, mp_size):
        turn = [(place, place ^ k) for place in range(mp_size)]
        split_parts[k] = lax.ppermute(split_parts[k], "mp", turn)
        turn = [
            (dp * mp_size + mp, (dp ^ (k >> 1)) * mp_size + (mp ^ (k & 1)))
            for dp in range(dp_size)
            for mp in range(mp_size)
        ]
        own_parts[k] = lax.ppermute(own_parts[k], ("dp", "mp"), turn)
    d_conv = conv_backward(lengths, picked, z_one, z_two, d_three, flat)
    early, small, split_sum, square = reduce_all(
        split_parts, own_parts, d_conv, dp_size, mp_size
    )
    shared_view = [a.reshape(FLAT_ROWS, 128) for a in (shared_weights, shared_first, shared_second)]
    split_view = [a.reshape(split_rows, 128) for a in (split_weights, split_first, split_second)]
    updated = adam_all(
        early, rows_all, small, split_sum, square, shared_view, split_view, wins
    )
    shared_out = [a.reshape(-1) for a in updated[:4]]
    split_out = [a.reshape(-1) for a in updated[4:8]]
    scalars = updated[8]
    return (*shared_out, *split_out, scalars[0, 0], scalars[1, 0], scalars[2, 0])


def solution(mesh):
    return jax.shard_map(
        per_device,
        mesh=mesh,
        in_specs=(
            P(("dp", "mp"), None, None, None, None),
            P(("dp", "mp"), None),
            P(("dp", "mp"), None),
            P(("dp", "mp")),
            P(("dp", "mp")),
            P(),
            P(),
            P(),
            P("mp"),
            P("mp"),
            P("mp"),
        ),
        out_specs=(P(), P(), P(), P(), P("mp"), P("mp"), P("mp"), P("mp"), P(), P(), P()),
        check_vma=False,
    )
```

```python
from functools import partial
import math

import jax
import jax.numpy as jnp
from jax import lax
from jax.experimental import pallas as pl
from jax.experimental.pallas import tpu as pltpu
from jax.sharding import PartitionSpec as P

D = 128
FF = 512
ACT = 18
C1 = 32
C2 = 64
TSTEPS = 4096
LAYERS = 2
STEP = 10
HD = 16


clip_limit = 0.1
learn_rate = 0.05
beta_first = 0.9
beta_second = 0.95
adam_epsilon = 1e-08
weight_decay = 0.1


def span_layout(narrow, hidden):
    return [
        ("qkv", (D, 3, narrow)),
        ("output", (narrow, D)),
        ("up", (D, hidden)),
        ("up_bias", (hidden,)),
        ("down", (hidden, D)),
    ]


def assemble(flat, copies, narrow, hidden):
    layout = span_layout(narrow, hidden)
    width = sum((math.prod(shape) for name, shape in layout))
    blocks = flat.reshape(copies, LAYERS, width)
    layers = []
    for layer in range(LAYERS):
        offset = 0
        pieces = {}
        for name, shape in layout:
            count = math.prod(shape)
            pieces[name] = blocks[:, layer, offset : offset + count].reshape((copies,) + shape)
            offset += count
        layers.append(
            {
                "qkv": jnp.moveaxis(pieces["qkv"], 0, 2).reshape(D, 3, copies * narrow),
                "output": pieces["output"].reshape(copies * narrow, D),
                "up": jnp.moveaxis(pieces["up"], 0, 1).reshape(D, copies * hidden),
                "up_bias": pieces["up_bias"].reshape(copies * hidden),
                "down": pieces["down"].reshape(copies * hidden, D),
            }
        )
    return layers


GROUP = 16
CONV_ROWS = 616
ROOM = 128
HALF = 64
BF16 = jnp.bfloat16
F32 = jnp.float32


def gelu_value(x):
    inner = 0.7978845608028654 * (x + 0.044715 * (x * x * x))
    return 0.5 * x * (1.0 + jnp.tanh(inner))


def gelu_both(x):
    square = x * x
    turn = jnp.tanh(0.7978845608028654 * x * (1.0 + 0.044715 * square))
    half = 0.5 * (1.0 + turn)
    slope = half + 0.5 * x * (1.0 - turn * turn) * (
        0.7978845608028654 * (1.0 + 3 * 0.044715 * square)
    )
    return x * half, slope


def two_parts(x):
    high = x.astype(BF16)
    return high, (x - high.astype(F32)).astype(BF16)


def pair(x):
    return jnp.concatenate(two_parts(x), axis=-1)


def fold_pair(x):
    return x[:, :128] + x[:, 128:]


def dot(a, b):
    return lax.dot_general(a, b, (((1,), (0,)), ((), ())), preferred_element_type=F32)


def dot_rows(a, b):
    return lax.dot_general(a, b, (((0,), (0,)), ((), ())), preferred_element_type=F32)


def lanes():
    return lax.broadcasted_iota(jnp.int32, (1, 128), 1)


def conv_biases(flat_ref):
    lane = lanes()
    one = jnp.where(lane < 32, flat_ref[64:65], 0.0)
    one = one + pltpu.roll(one, 32, 1)
    one = one + pltpu.roll(one, 64, 1)
    two = jnp.where(lane < 64, pltpu.roll(flat_ref[320:321], 96, 1), 0.0)
    two = two + pltpu.roll(two, 64, 1)
    three = jnp.where(
        lane < 32,
        pltpu.roll(flat_ref[608:609], 32, 1),
        jnp.where(lane < 64, pltpu.roll(flat_ref[609:610], 32, 1), 0.0),
    )
    three = three + pltpu.roll(three, 64, 1)
    return one, two, three


def shifted(ref, start, rows, lane):
    first = pltpu.roll(ref[start : start + rows], 128 - lane, 1)
    second = pltpu.roll(ref[start + 1 : start + 1 + rows], 128 - lane, 1)
    return jnp.where(lanes() < 128 - lane, first, second)


def spread_one(flat_ref, put):
    halves = [jnp.transpose(flat_ref[pl.ds(side, 32, stride=2), :]) for side in range(2)]
    turned = jnp.concatenate(halves, axis=0)
    lane = lax.broadcasted_iota(jnp.int32, (8, 128), 1)
    row = lax.broadcasted_iota(jnp.int32, (8, 128), 0)
    low = row < 4
    column = lax.shift_right_logical(lane, 5)
    for ky in range(8):
        for c in range(4):
            held = turned[c * 64 + ky * 8 : c * 64 + ky * 8 + 8]
            wide = jnp.concatenate([held] * 4, axis=1)
            flipped = jnp.concatenate([wide[4:], wide[:4]], axis=0)
            zero = jnp.zeros((8, 128), F32)
            first = jnp.where(column == 0, wide, jnp.where((column == 1) & ~low, flipped, zero))
            second = jnp.where(
                column == 2,
                wide,
                jnp.where(((column == 1) & low) | ((column == 3) & ~low), flipped, zero),
            )
            third = jnp.where((column == 3) & low, flipped, zero)
            put(ky * 128 + c * 32, jnp.concatenate([first, second, third, zero], axis=0))


def spread_two(flat_ref, rows_ref, turned, put):
    lane = lax.broadcasted_iota(jnp.int32, (32, 128), 1)
    rows_ref[0:256] = shifted(flat_ref, 64, 256, 32)
    for j in range(4):
        block = jnp.transpose(rows_ref[pl.ds(j, 64, stride=4), :])
        turned[j * 128 : (j + 1) * 128] = jnp.concatenate([block, block], axis=1)
    for ky in range(4):
        rows = [turned[pl.ds(ky * 4 + kx, 32, stride=16)] for kx in range(4)]
        for i in range(8):
            left = rows[i] if i < 4 else jnp.zeros((32, 128), F32)
            right = rows[i - 2] if 2 <= i < 6 else jnp.zeros((32, 128), F32)
            put(ky * 256 + i * 32, jnp.where(lane < 64, left, right))


def spread_three(flat_ref, rows_ref, turned, put):
    lane = lax.broadcasted_iota(jnp.int32, (64, 128), 1)
    side = lax.broadcasted_iota(jnp.int32, (32, 128), 1) < 64
    rows_ref[0:288] = shifted(flat_ref, 320, 288, 96)
    nine = [rows_ref[pl.ds(k, 32, stride=9), :] for k in range(9)]
    flips = [pltpu.roll(nine[4 + k], 64, 1) for k in range(5)]
    for j in range(5):
        wide = min(128, 576 - j * 128)
        rows_ref[pl.ds(0, 32, stride=2), :] = nine[j]
        rows_ref[pl.ds(1, 32, stride=2), :] = (
            jnp.where(side, flips[j], flips[j + 1]) if j < 4 else flips[4]
        )
        block = jnp.transpose(rows_ref[0:64])[0:wide]
        turned[j * 128 : j * 128 + wide] = jnp.concatenate([block, block], axis=1)
    for ky in range(3):
        rows = [turned[pl.ds(ky * 3 + kx, 64, stride=9)] for kx in range(3)]
        for i in range(4):
            left = rows[i] if i < 3 else jnp.zeros((64, 128), F32)
            right = rows[i - 1] if i >= 1 else jnp.zeros((64, 128), F32)
            put(ky * 256 + i * 64, jnp.where(lane < 64, left, right))


def last_masks():
    return lanes() < 64


def conv_forward_kernel(
    lengths_from,
    frames_ref,
    shared_ref,
    picked_ref,
    z_one_ref,
    z_two_ref,
    z_three_ref,
    flat_ref,
    held,
    wide,
    picked,
    z_one,
    z_two,
    z_three,
    h_one,
    h_two,
    w_one,
    w_two,
    w_three,
    choose,
    rows_ref,
    turned,
    lengths_ref,
    frame_sem,
    out_sem,
):
    scalars = pltpu.make_async_copy(lengths_from, lengths_ref, out_sem.at[5])
    scalars.start()
    scalars.wait()
    wins = lengths_ref.shape[0]
    steps = frames_ref.shape[1]
    used = jnp.int32(0)
    for w in range(wins):
        used = used + lengths_ref[w]
    groups = lax.div(used + (GROUP - 1), GROUP)

    def frame_copy(group, spot, slot):
        state = jnp.minimum(group * GROUP + spot, used - 1)
        window, begin, end = jnp.int32(0), jnp.int32(0), jnp.int32(0)
        for w in range(wins - 1):
            end = end + lengths_ref[w]
            window = jnp.where(state >= end, w + 1, window)
            begin = jnp.where(state >= end, end, begin)
        return pltpu.make_async_copy(
            frames_ref.at[window, state - begin], held.at[slot, spot], frame_sem.at[slot, spot]
        )

    def fetch(group, slot):
        def one(spot, carry):
            frame_copy(group, spot, slot).start()
            return carry

        lax.fori_loop(0, GROUP, one, 0)

    weights = pltpu.make_async_copy(
        shared_ref.at[pl.ds(0, CONV_ROWS)], flat_ref, out_sem.at[4]
    )
    weights.start()
    fetch(0, 0)
    h_one[...] = jnp.zeros(h_one.shape, BF16)

    def put_one(row, block):
        w_one[row : row + 32] = pair(block)

    def put_two(row, block):
        w_two[row : row + 32] = pair(block)

    def put_three(row, block):
        w_three[row : row + 64] = pair(block)

    weights.wait()
    spread_one(flat_ref, put_one)
    spread_two(flat_ref, rows_ref, turned, put_two)
    spread_three(flat_ref, rows_ref, turned, put_three)
    bias_one, bias_two, bias_three = conv_biases(flat_ref)
    row = lax.broadcasted_iota(jnp.int32, (128, 640), 0)
    column = lax.broadcasted_iota(jnp.int32, (128, 640), 1)
    place = jnp.bitwise_and(column, 31)
    channel = jnp.bitwise_and(lax.shift_right_logical(column, 5), 3)
    block = lax.shift_right_logical(column, 7)
    right = (row == 16 * block + place) & (place < 20)
    for c in range(4):
        choose[c * 128 : (c + 1) * 128] = jnp.where(right & (channel == c), 1.0, 0.0).astype(BF16)

    def one_group(group, carry):
        slot = lax.rem(group, 2)

        @pl.when(group + 1 < groups)
        def ahead():
            fetch(group + 1, 1 - slot)

        def lay(step, carry):
            spots = [step * 4 + k for k in range(4)]
            for spot in spots:
                frame_copy(group, spot, slot).wait()
            for spot in spots:
                image = held[slot, spot].astype(F32).reshape(336, 84)
                image = jnp.concatenate([image, jnp.zeros((336, 44), F32)], axis=1)
                wide[pl.ds(spot, 336, stride=GROUP), :] = image
            return carry

        lax.fori_loop(0, GROUP // 4, lay, 0)
        for part in range(3):
            rows = wide[part * 1792 : (part + 1) * 1792].reshape(28, 4, GROUP, 128)
            rows = [rows[:, c].reshape(448, 128).astype(BF16) for c in range(4)]
            result = dot(jnp.concatenate(rows, axis=1), choose[...])
            picked[part * 7 : (part + 1) * 7] = result.astype(BF16).reshape(7, 4, GROUP, 640)
        keep_picked = pltpu.make_async_copy(picked, picked_ref.at[group], out_sem.at[0])
        keep_picked.start()
        for q in range(5):
            pieces = [
                picked[j : j + 20, b, :, q * 128 : (q + 1) * 128].reshape(20 * GROUP, 128)
                for j in range(2)
                for b in range(4)
            ]
            z = fold_pair(dot(jnp.concatenate(pieces, axis=1), w_one[...])) + bias_one
            z_one[:, :, q] = z.reshape(10, 2, GROUP, 128)
            high, low = two_parts(gelu_value(z))
            h_one[0, :, :, q] = high.reshape(10, 2, GROUP, 128)
            h_one[1, :, :, q] = low.reshape(10, 2, GROUP, 128)
        keep_one = pltpu.make_async_copy(z_one, z_one_ref.at[group], out_sem.at[1])
        keep_one.start()
        total = jnp.zeros((45 * GROUP, 128), F32)
        for part in range(2):
            pieces = []
            for j in range(2):
                for b in range(2):
                    pieces.append(h_one[part, j : j + 9, b, 0:5].reshape(45 * GROUP, 128))
                    pieces.append(h_one[part, j : j + 9, b, 1:6].reshape(45 * GROUP, 128))
            total = total + fold_pair(dot(jnp.concatenate(pieces, axis=1), w_two[...]))
        z = (total + bias_two).reshape(9, 5, GROUP, 128)
        z_two[...] = z
        h = gelu_value(z)
        high, low = two_parts(h)
        h_two[0] = high
        h_two[1] = low
        edge = jnp.where(last_masks(), h[:, 4].reshape(9 * GROUP, 128), 0.0)
        high, low = two_parts(edge)
        h_two[0, :, 4] = high.reshape(9, GROUP, 128)
        h_two[1, :, 4] = low.reshape(9, GROUP, 128)
        keep_two = pltpu.make_async_copy(z_two, z_two_ref.at[group], out_sem.at[2])
        keep_two.start()
        total = jnp.zeros((28 * GROUP, 128), F32)
        for part in range(2):
            pieces = []
            for ky in range(3):
                pieces.append(h_two[part, ky : ky + 7, 0:4].reshape(28 * GROUP, 128))
                pieces.append(h_two[part, ky : ky + 7, 1:5].reshape(28 * GROUP, 128))
            total = total + fold_pair(dot(jnp.concatenate(pieces, axis=1), w_three[...]))
        z_three[...] = (total + bias_three).reshape(28, GROUP, 128)
        spot = pl.multiple_of(group * GROUP, GROUP)
        keep_three = pltpu.make_async_copy(
            z_three, z_three_ref.at[:, pl.ds(spot, GROUP)], out_sem.at[3]
        )
        keep_three.start()
        keep_picked.wait()
        keep_one.wait()
        keep_two.wait()
        keep_three.wait()
        return carry

    lax.fori_loop(0, groups, one_group, 0)


def conv_forward(lengths, frames, flat):
    most = ROOM // GROUP
    any_spec = pl.BlockSpec(memory_space=pl.ANY)
    hbm = pl.BlockSpec(memory_space=pltpu.HBM)
    return pl.pallas_call(
        conv_forward_kernel,
        in_specs=[
            any_spec,
            any_spec,
            any_spec,
        ],
        out_specs=[hbm] * 4,
        out_shape=[
            jax.ShapeDtypeStruct((most, 21, 4, GROUP, 640), BF16),
            jax.ShapeDtypeStruct((most, 10, 2, 5, GROUP, 128), F32),
            jax.ShapeDtypeStruct((most, 9, 5, GROUP, 128), F32),
            jax.ShapeDtypeStruct((28, ROOM, 128), F32),
        ],
        scratch_shapes=[
            pltpu.VMEM((CONV_ROWS, 128), F32),
            pltpu.VMEM((2, GROUP, 84, 4, 84), BF16),
            pltpu.VMEM((336 * GROUP, 128), F32),
            pltpu.VMEM((21, 4, GROUP, 640), BF16),
            pltpu.VMEM((10, 2, 5, GROUP, 128), F32),
            pltpu.VMEM((9, 5, GROUP, 128), F32),
            pltpu.VMEM((28, GROUP, 128), F32),
            pltpu.VMEM((2, 10, 2, 6, GROUP, 128), BF16),
            pltpu.VMEM((2, 9, 5, GROUP, 128), BF16),
            pltpu.VMEM((1024, 256), BF16),
            pltpu.VMEM((1024, 256), BF16),
            pltpu.VMEM((768, 256), BF16),
            pltpu.VMEM((512, 640), BF16),
            pltpu.VMEM((288, 128), F32),
            pltpu.VMEM((576, 128), F32),
            pltpu.SMEM(lengths.shape, jnp.int32),
            pltpu.SemaphoreType.DMA((2, GROUP)),
            pltpu.SemaphoreType.DMA((6,)),
        ],
        compiler_params=pltpu.CompilerParams(vmem_limit_bytes=62 * 1024 * 1024),
        name="conv_forward",
    )(lengths, frames.transpose(0, 1, 3, 2, 4), flat)


def gather_one(total, out):
    lane = lax.broadcasted_iota(jnp.int32, (32, 128), 1)
    halves = [jnp.zeros((32, 128), F32) for side in range(2)]
    for ky in range(8):
        held = total[0:128, ky * 128 : (ky + 1) * 128] + total[128:256, ky * 128 : (ky + 1) * 128]
        summed = held[0:32]
        for o in range(1, 4):
            summed = summed + pltpu.roll(held[32 * o : 32 * o + 32], 128 - 4 * o, 1)
        for c in range(4):
            spot = (c % 2) * 64 + ky * 8
            shift = (spot - c * 32) % 128
            moved = pltpu.roll(summed, shift, 1) if shift else summed
            inside = (lane >= spot) & (lane < spot + 8)
            halves[c // 2] = halves[c // 2] + jnp.where(inside, moved, 0.0)
    for side in range(2):
        out[pl.ds(side, 32, stride=2), :] = halves[side]


def gather_two(total, turned, rows_ref, out):
    lane = lax.broadcasted_iota(jnp.int32, (64, 128), 1)
    for ky in range(4):
        near = total[0:128, ky * 256 : ky * 256 + 128] + total[128:256, ky * 256 : ky * 256 + 128]
        far = (
            total[0:128, ky * 256 + 128 : ky * 256 + 256]
            + total[128:256, ky * 256 + 128 : ky * 256 + 256]
        )
        summed = near[0:64] + jnp.where(
            lane < 64, pltpu.roll(near[64:128], 64, 1), pltpu.roll(far[64:128], 64, 1)
        )
        flipped = jnp.transpose(jnp.concatenate([summed, jnp.zeros((64, 128), F32)], axis=0))
        for kx in range(4):
            turned[pl.ds(ky * 4 + kx, 32, stride=16), :] = flipped[kx * 32 : (kx + 1) * 32]
    rows_ref[0:8] = jnp.zeros((8, 128), F32)
    rows_ref[264:272] = jnp.zeros((8, 128), F32)
    for j in range(4):
        block = jnp.transpose(turned[j * 128 : (j + 1) * 128])[0:64]
        rows_ref[pl.ds(8 + j, 64, stride=4), :] = block
    own = pltpu.roll(rows_ref[8:265], 32, 1)
    before = pltpu.roll(rows_ref[7:264], 32, 1)
    out[64:321] = jnp.where(lanes() >= 32, own, before)


def gather_three(total, turned, rows_ref, out):
    lane = lax.broadcasted_iota(jnp.int32, (64, 128), 1)
    side = lax.broadcasted_iota(jnp.int32, (32, 128), 1) < 64
    blank = jnp.zeros((64, 128), F32)
    for ky in range(3):
        near = total[0:128, ky * 256 : ky * 256 + 128] + total[128:256, ky * 256 : ky * 256 + 128]
        far = (
            total[0:128, ky * 256 + 128 : ky * 256 + 256]
            + total[128:256, ky * 256 + 128 : ky * 256 + 256]
        )
        first = near[0:64] + jnp.where(
            lane < 64, pltpu.roll(near[64:128], 64, 1), pltpu.roll(far[64:128], 64, 1)
        )
        second = far[0:64] + pltpu.roll(far[64:128], 64, 1)
        flipped = jnp.transpose(jnp.concatenate([first, blank], axis=0))
        turned[pl.ds(ky * 3, 64, stride=9), :] = flipped[0:64]
        turned[pl.ds(ky * 3 + 1, 64, stride=9), :] = flipped[64:128]
        flipped = jnp.transpose(jnp.concatenate([second, blank], axis=0))
        turned[pl.ds(ky * 3 + 2, 64, stride=9), :] = flipped[0:64]
    turned[576:640] = blank
    evens, odds = [], []
    for j in range(5):
        rows_ref[0:64] = jnp.transpose(turned[j * 128 : (j + 1) * 128])[0:64]
        evens.append(rows_ref[pl.ds(0, 32, stride=2), :])
        odds.append(pltpu.roll(rows_ref[pl.ds(1, 32, stride=2), :], 64, 1))
    rows_ref[0:8] = jnp.zeros((8, 128), F32)
    rows_ref[296:304] = jnp.zeros((8, 128), F32)
    for k in range(9):
        if k < 4:
            held = evens[k]
        elif k == 4:
            held = jnp.where(side, evens[4], odds[0])
        else:
            held = jnp.where(side, odds[k - 5], odds[k - 4])
        rows_ref[pl.ds(8 + k, 32, stride=9), :] = held
    own = pltpu.roll(rows_ref[8:297], 96, 1)
    before = pltpu.roll(rows_ref[7:296], 96, 1)
    edge = out[320:321]
    out[320:609] = jnp.where(lanes() >= 96, own, before)
    out[320:321] = out[320:321] + edge


def conv_backward_kernel(
    lengths_from,
    picked_ref,
    z_one_ref,
    z_two_ref,
    d_three_ref,
    shared_ref,
    flat_out,
    flat_ref,
    picked,
    z_one,
    z_two,
    d_three,
    h_one,
    h_two,
    slope_one,
    pad_three,
    pad_two,
    d_one,
    v_two,
    v_three,
    spread,
    rows_ref,
    turned,
    bias_out,
    total_one,
    total_two,
    total_three,
    lengths_ref,
    load_sem,
    weight_sem,
):
    scalars = pltpu.make_async_copy(lengths_from, lengths_ref, weight_sem)
    scalars.start()
    scalars.wait()
    used = jnp.int32(0)
    for w in range(lengths_ref.shape[0]):
        used = used + lengths_ref[w]
    groups = lax.div(used + (GROUP - 1), GROUP)

    def loads(group, slot):
        spot = pl.multiple_of(group * GROUP, GROUP)
        return [
            pltpu.make_async_copy(picked_ref.at[group], picked.at[slot], load_sem.at[slot, 0]),
            pltpu.make_async_copy(z_one_ref.at[group], z_one.at[slot], load_sem.at[slot, 1]),
            pltpu.make_async_copy(z_two_ref.at[group], z_two.at[slot], load_sem.at[slot, 2]),
            pltpu.make_async_copy(
                d_three_ref.at[:, pl.ds(spot, GROUP)], d_three.at[slot], load_sem.at[slot, 3]
            ),
        ]

    weights = pltpu.make_async_copy(
        shared_ref.at[pl.ds(0, CONV_ROWS)], flat_ref, weight_sem
    )
    weights.start()
    for load in loads(0, 0):
        load.start()

    def put_two(row, block):
        spread[row : row + 32] = block

    def put_three(row, block):
        spread[row : row + 64] = block

    weights.wait()
    spread_two(flat_ref, rows_ref, turned, put_two)
    for b in range(2):
        for j in range(2):
            for side in range(2):
                source = (2 * j + b) * 256 + side * 128
                target = (b * 2 + j) * 256 + side * 128
                v_two[target : target + 128] = pair(jnp.transpose(spread[source : source + 128]))
    spread_three(flat_ref, rows_ref, turned, put_three)
    for part in range(6):
        rows = pl.ds(part * 128, 128)
        v_three[rows] = pair(jnp.transpose(spread[rows]))
    total_one[...] = jnp.zeros(total_one.shape, F32)
    total_two[...] = jnp.zeros(total_two.shape, F32)
    total_three[...] = jnp.zeros(total_three.shape, F32)
    bias_out[...] = jnp.zeros(bias_out.shape, F32)
    h_one[...] = jnp.zeros(h_one.shape, BF16)
    pad_two[...] = jnp.zeros(pad_two.shape, BF16)
    pad_three[...] = jnp.zeros(pad_three.shape, BF16)

    def fold(rows):
        return jnp.sum(rows.reshape(-1, 8, 128), axis=0)

    def one_group(group, carry):
        slot = lax.rem(group, 2)

        @pl.when(group + 1 < groups)
        def ahead():
            for load in loads(group + 1, 1 - slot):
                load.start()

        for load in loads(group, slot):
            load.wait()
        rows = d_three[slot].reshape(28 * GROUP, 128)
        bias_out[2] += fold(rows)
        both = pair(rows)
        pad_three[0, 2:9, 1:5] = both[:, :128].reshape(7, 4, GROUP, 128)
        pad_three[1, 2:9, 1:5] = both[:, 128:].reshape(7, 4, GROUP, 128)
        h, slope_two = gelu_both(z_two[slot])
        high, low = two_parts(h)
        h_two[0] = high
        h_two[1] = low
        edge = jnp.where(last_masks(), h[:, 4].reshape(9 * GROUP, 128), 0.0)
        high, low = two_parts(edge)
        h_two[0, :, 4] = high.reshape(9, GROUP, 128)
        h_two[1, :, 4] = low.reshape(9, GROUP, 128)
        for part in range(2):
            pieces = []
            for ky in range(3):
                pieces.append(h_two[part, ky : ky + 7, 0:4].reshape(28 * GROUP, 128))
                pieces.append(h_two[part, ky : ky + 7, 1:5].reshape(28 * GROUP, 128))
            total_three[...] += dot_rows(both, jnp.concatenate(pieces, axis=1))
        spill = jnp.zeros((45 * GROUP, 128), F32)
        for part in range(2):
            pieces = []
            for ky in range(3):
                pieces.append(pad_three[part, 2 - ky : 11 - ky, 1:6].reshape(45 * GROUP, 128))
                pieces.append(pad_three[part, 2 - ky : 11 - ky, 0:5].reshape(45 * GROUP, 128))
            spill = spill + fold_pair(dot(jnp.concatenate(pieces, axis=1), v_three[...]))
        rows = spill * slope_two.reshape(45 * GROUP, 128)
        bias_out[1] += fold(rows)
        both = pair(rows)
        pad_two[0, 1:10, 1:6] = both[:, :128].reshape(9, 5, GROUP, 128)
        pad_two[1, 1:10, 1:6] = both[:, 128:].reshape(9, 5, GROUP, 128)
        for q in range(5):
            h, slope = gelu_both(z_one[slot, :, :, q])
            high, low = two_parts(h)
            h_one[0, :, :, q] = high
            h_one[1, :, :, q] = low
            slope_one[:, :, q] = slope
        for part in range(2):
            pieces = []
            for j in range(2):
                for b in range(2):
                    pieces.append(h_one[part, j : j + 9, b, 0:5].reshape(45 * GROUP, 128))
                    pieces.append(h_one[part, j : j + 9, b, 1:6].reshape(45 * GROUP, 128))
            total_two[...] += dot_rows(both, jnp.concatenate(pieces, axis=1))
        for b in range(2):
            spill = jnp.zeros((50 * GROUP, 128), F32)
            for part in range(2):
                pieces = []
                for j in range(2):
                    pieces.append(pad_two[part, 1 - j : 11 - j, 1:6].reshape(50 * GROUP, 128))
                    pieces.append(pad_two[part, 1 - j : 11 - j, 0:5].reshape(50 * GROUP, 128))
                spill = spill + fold_pair(
                    dot(jnp.concatenate(pieces, axis=1), v_two[b * 512 : (b + 1) * 512])
                )
            rows = spill * slope_one[:, b].reshape(50 * GROUP, 128)
            bias_out[0] += fold(rows)
            d_one[:, b] = pair(rows).reshape(10, 5, GROUP, 256)
        for q in range(5):
            pieces = [
                picked[slot, j : j + 20, b, :, q * 128 : (q + 1) * 128].reshape(20 * GROUP, 128)
                for j in range(2)
                for b in range(4)
            ]
            total_one[...] += dot_rows(
                d_one[:, :, q].reshape(20 * GROUP, 256), jnp.concatenate(pieces, axis=1)
            )
        return carry

    lax.fori_loop(0, groups, one_group, 0)
    gather_one(total_one, flat_out)
    gather_two(total_two, turned, rows_ref, flat_out)
    gather_three(total_three, turned, rows_ref, flat_out)
    lane = lanes()
    sums = [jnp.sum(bias_out[k], axis=0, keepdims=True) for k in range(3)]
    sums[0] = sums[0] + pltpu.roll(sums[0], 64, 1)
    sums[0] = sums[0] + pltpu.roll(sums[0], 32, 1)
    sums[1] = jnp.where(lane < 64, sums[1] + pltpu.roll(sums[1], 64, 1), 0.0)
    sums[2] = jnp.where(lane < 64, sums[2] + pltpu.roll(sums[2], 64, 1), 0.0)
    flat_out[64:65] = jnp.where(lane < 32, sums[0], flat_out[64:65])
    flat_out[320:321] = flat_out[320:321] + pltpu.roll(sums[1], 32, 1)
    late = pltpu.roll(sums[2], 96, 1)
    flat_out[608:609] = flat_out[608:609] + jnp.where(lane >= 96, late, 0.0)
    row = lax.broadcasted_iota(jnp.int32, (7, 128), 0)
    flat_out[609:616] = jnp.where((row == 0) & (lane < 32), late, 0.0)


def conv_backward(lengths, picked, z_one, z_two, d_three, flat):
    hbm = pl.BlockSpec(memory_space=pltpu.HBM)
    vmem = pl.BlockSpec(memory_space=pltpu.VMEM)
    return pl.pallas_call(
        conv_backward_kernel,
        in_specs=[hbm] * 6,
        out_specs=vmem,
        out_shape=jax.ShapeDtypeStruct((CONV_ROWS, 128), F32),
        scratch_shapes=[
            pltpu.VMEM((CONV_ROWS, 128), F32),
            pltpu.VMEM((2, 21, 4, GROUP, 640), BF16),
            pltpu.VMEM((2, 10, 2, 5, GROUP, 128), F32),
            pltpu.VMEM((2, 9, 5, GROUP, 128), F32),
            pltpu.VMEM((2, 28, GROUP, 128), F32),
            pltpu.VMEM((2, 10, 2, 6, GROUP, 128), BF16),
            pltpu.VMEM((2, 9, 5, GROUP, 128), BF16),
            pltpu.VMEM((10, 2, 5, GROUP, 128), F32),
            pltpu.VMEM((2, 11, 6, GROUP, 128), BF16),
            pltpu.VMEM((2, 11, 6, GROUP, 128), BF16),
            pltpu.VMEM((10, 2, 5, GROUP, 256), BF16),
            pltpu.VMEM((1024, 256), BF16),
            pltpu.VMEM((768, 256), BF16),
            pltpu.VMEM((1024, 128), F32),
            pltpu.VMEM((304, 128), F32),
            pltpu.VMEM((640, 128), F32),
            pltpu.VMEM((3, 8, 128), F32),
            pltpu.VMEM((256, 1024), F32),
            pltpu.VMEM((256, 1024), F32),
            pltpu.VMEM((256, 768), F32),
            pltpu.SMEM(lengths.shape, jnp.int32),
            pltpu.SemaphoreType.DMA((2, 4)),
            pltpu.SemaphoreType.DMA,
        ],
        compiler_params=pltpu.CompilerParams(vmem_limit_bytes=62 * 1024 * 1024),
        name="conv_backward",
    )(lengths, picked, z_one, z_two, d_three, flat)


HIGH = lax.Precision.HIGH
VECTORS_ROW = 3745
TIME_ROW = 3780


def mm(a, b):
    return lax.dot_general(
        a, b, (((1,), (0,)), ((), ())), precision=HIGH, preferred_element_type=F32
    )


def mm_nt(a, b):
    return lax.dot_general(
        a, b, (((1,), (1,)), ((), ())), precision=HIGH, preferred_element_type=F32
    )


def mm_tn(a, b):
    return lax.dot_general(
        a, b, (((0,), (0,)), ((), ())), precision=HIGH, preferred_element_type=F32
    )


def dot_nt(a, b):
    return lax.dot_general(a, b, (((1,), (1,)), ((), ())), preferred_element_type=F32)


def norm_parts(stream):
    centered = stream - jnp.mean(stream, -1, keepdims=True)
    spread = jnp.mean(centered * centered, -1, keepdims=True)
    scale = lax.rsqrt(spread + 1e-05)
    return centered * scale, scale


def norm_back(grad, unit, scale, gain):
    grad = grad * gain
    inner = jnp.mean(grad * unit, -1, keepdims=True)
    return scale * (grad - jnp.mean(grad, -1, keepdims=True) - unit * inner)


def column_sum(x):
    return jnp.sum(x, axis=0, keepdims=True)


def head_places():
    number = lax.broadcasted_iota(jnp.int32, (128, 128), 0) * ACT
    lane = lax.broadcasted_iota(jnp.int32, (128, 128), 1)
    row = lax.shift_right_logical(number, 7)
    return row + jnp.where(lane < jnp.bitwise_and(number, 127), 1, 0)


def roll_rows(held, sign):
    number = lax.broadcasted_iota(jnp.int32, (128, 128), 0) * ACT
    for k in range(7):
        moved = pltpu.roll(held, (sign * (1 << k)) % 128, 1)
        held = jnp.where(jnp.bitwise_and(number, 1 << k) > 0, moved, held)
    return held


def square_head(rows):
    place = head_places()
    held = jnp.zeros((128, 128), F32)
    for k in range(ACT):
        held = jnp.where(place == k, rows[k : k + 1], held)
    held = roll_rows(held, -1)
    lane = lax.broadcasted_iota(jnp.int32, (128, 128), 1)
    return jnp.where(lane < ACT, held, 0.0)


def flat_head(grads):
    place = head_places()
    lane = lax.broadcasted_iota(jnp.int32, (128, 128), 1)
    held = roll_rows(jnp.where(lane < ACT, grads, 0.0), 1)
    rows = [
        jnp.sum(jnp.where(place == k, held, 0.0), axis=0, keepdims=True) for k in range(ACT)
    ]
    return jnp.concatenate(rows + [jnp.zeros((24 - ACT, 128), F32)], axis=0)


def unpack_split(split_ref, qkv, output, up, up_bias, down):
    lane = lax.broadcasted_iota(jnp.int32, (32, 128), 1)
    for layer in range(LAYERS):
        base = layer * 385
        kinds = [[jnp.zeros((32, 128), F32) for j in range(4)] for kind in range(3)]
        for m in range(4):
            rows = [split_ref[m, pl.ds(base + k, 32, stride=3), :] for k in range(3)]
            inside = (lane >= 32 * m) & (lane < 32 * m + 32)
            for j in range(4):
                for kind in range(3):
                    spot = j * 96 + kind * 32
                    source = rows[spot // 128]
                    shift = (32 * m - spot % 128) % 128
                    moved = pltpu.roll(source, shift, 1) if shift else source
                    kinds[kind][j] = jnp.where(inside, moved, kinds[kind][j])
            output[layer, 32 * m : 32 * m + 32] = split_ref[m, base + 96 : base + 128]
            up[layer, :, 128 * m : 128 * m + 128] = split_ref[m, base + 128 : base + 256]
            up_bias[layer, :, 128 * m : 128 * m + 128] = split_ref[m, base + 256 : base + 257]
            down[layer, 128 * m : 128 * m + 128] = split_ref[m, base + 257 : base + 385]
        for kind in range(3):
            for j in range(4):
                qkv[layer, kind, pl.ds(j, 32, stride=4), :] = kinds[kind][j]


def pack_split(out_ref, qkv, output, up, up_bias, down):
    lane = lax.broadcasted_iota(jnp.int32, (32, 128), 1)
    for layer in range(LAYERS):
        base = layer * 385
        parts = [[qkv[layer, kind, pl.ds(j, 32, stride=4), :] for j in range(4)] for kind in range(3)]
        for m in range(4):
            rows = [jnp.zeros((32, 128), F32) for k in range(3)]
            for j in range(4):
                for kind in range(3):
                    spot = j * 96 + kind * 32
                    low = spot % 128
                    shift = (low - 32 * m) % 128
                    moved = pltpu.roll(parts[kind][j], shift, 1) if shift else parts[kind][j]
                    inside = (lane >= low) & (lane < low + 32)
                    rows[spot // 128] = jnp.where(inside, moved, rows[spot // 128])
            for k in range(3):
                out_ref[m, pl.ds(base + k, 32, stride=3), :] = rows[k]
            out_ref[m, base + 96 : base + 128] = output[layer, 32 * m : 32 * m + 32]
            out_ref[m, base + 128 : base + 256] = up[layer, :, 128 * m : 128 * m + 128]
            out_ref[m, base + 256 : base + 257] = up_bias[layer, :, 128 * m : 128 * m + 128]
            out_ref[m, base + 257 : base + 385] = down[layer, 128 * m : 128 * m + 128]
    for m in range(4):
        out_ref[m, 770:784] = jnp.zeros((14, 128), F32)


def former_body(
    slots,
    used,
    lengths_ref,
    returns_ref,
    actions_ref,
    head_ref,
    z_ref,
    small,
    times_all,
    encoder,
    weights,
    d_three_ref,
    d_encoder_ref,
    d_small_ref,
    d_times_ref,
    grads,
    chances,
    kept,
    sums,
    flats,
):
    qkv, output, up, up_bias, down = weights
    d_qkv, d_output, d_up, d_up_bias, d_down = grads
    rows = 3 * slots
    wins, steps = returns_ref.shape
    vec = [small[k : k + 1] for k in range(17)]
    table = small[17 : 17 + ACT]
    slot = lax.broadcasted_iota(jnp.int32, (slots, 1), 0)
    window = jnp.zeros((slots, 1), jnp.int32)
    begin = jnp.zeros((slots, 1), jnp.int32)
    end = jnp.int32(0)
    for w in range(wins - 1):
        end = end + lengths_ref[w]
        window = jnp.where(slot >= end, w + 1, window)
        begin = jnp.where(slot >= end, end, begin)
    moment = slot - begin
    valid = slot < used
    time_lane = lax.broadcasted_iota(jnp.int32, (slots, steps), 1)
    amount = jnp.zeros((slots, 1), F32)
    action = jnp.zeros((slots, 1), jnp.int32)
    for w in range(wins):
        here = (time_lane == moment) & (window == w)
        amount = amount + jnp.sum(
            jnp.where(here, returns_ref[w : w + 1], 0.0), axis=1, keepdims=True
        )
        action = action + jnp.sum(jnp.where(here, actions_ref[w : w + 1], 0), axis=1, keepdims=True)
    lane = lax.broadcasted_iota(jnp.int32, (slots, 128), 1)
    picks = jnp.where((lane == action) & valid, 1.0, 0.0)
    reward = jnp.tanh(amount * vec[14] + vec[15])
    table = jnp.concatenate([table, jnp.zeros((128 - ACT, 128), F32)], axis=0)
    move = jnp.tanh(mm(picks, table))
    sum_state = jnp.zeros((slots, 128), F32)
    for k in range(28):
        z = jnp.where(valid, z_ref[k, 0:slots], 0.0)
        high, low = two_parts(gelu_value(z))
        flats[0, 0:slots, k * 128 : (k + 1) * 128] = high
        flats[1, 0:slots, k * 128 : (k + 1) * 128] = low
    for part in range(2):
        sum_state = sum_state + fold_pair(dot(flats[part, 0:slots], encoder[...]))
    state = jnp.tanh(sum_state + vec[16])
    times = times_all[0:slots]
    stream = jnp.concatenate([reward + times, state + times, move + times], axis=0)

    def ids(axis):
        shape = (rows, 1) if axis == 0 else (1, rows)
        number = lax.broadcasted_iota(jnp.int32, shape, axis)
        kind = jnp.where(number >= 2 * slots, 2, jnp.where(number >= slots, 1, 0))
        return number - kind * slots, kind

    (slot_q, kind_q), (slot_k, kind_k) = ids(0), ids(1)

    def begin_of(slot_ids):
        found = jnp.zeros(slot_ids.shape, jnp.int32)
        end = jnp.int32(0)
        for w in range(wins - 1):
            end = end + lengths_ref[w]
            found = jnp.where(slot_ids >= end, end, found)
        return found

    order_q = slot_q * 3 + kind_q
    order_k = slot_k * 3 + kind_k
    allowed = (order_q >= order_k) & (slot_k >= begin_of(slot_q)) & (slot_k < used)
    head_of = lax.shift_right_logical(lax.broadcasted_iota(jnp.int32, (1, 128), 1), 4)
    heads = D // HD
    batch = 4 if slots <= HALF else 2

    def masked(x, masks):
        return jnp.concatenate([jnp.where(mask, x, jnp.zeros_like(x)) for mask in masks], axis=0)

    def unmasked(x, masks):
        held = jnp.where(masks[0], x[0:rows], 0.0)
        for k in range(1, batch):
            held = held + jnp.where(masks[k], x[k * rows : (k + 1) * rows], 0.0)
        return held

    tape = []
    for layer in range(LAYERS):
        gains = vec[6 * layer : 6 * layer + 6]
        unit_one, scale_one = norm_parts(stream)
        normed = unit_one * gains[0] + gains[1]
        wide = jnp.concatenate([qkv[layer, k] for k in range(3)], axis=1)
        mixed = mm(normed, wide)
        query_high, query_low = two_parts(mixed[:, :128] * 0.25)
        keys, values = pair(mixed[:, 128:256]), pair(mixed[:, 256:])
        kept[layer, 0, 0:rows] = query_high
        kept[layer, 1, 0:rows] = query_low
        for k in range(2):
            kept[layer, 2 + k, 0:rows] = keys[:, k * 128 : (k + 1) * 128]
            kept[layer, 4 + k, 0:rows] = values[:, k * 128 : (k + 1) * 128]
        sums[0, 0:rows] = jnp.zeros((rows, 128), F32)

        def attend(turn, carry, layer=layer):
            masks = [head_of == turn * batch + k for k in range(batch)]
            parts = [masked(kept[layer, k, 0:rows], masks) for k in range(2)]
            keys = [kept[layer, 2 + k, 0:rows] for k in range(2)]
            values = [kept[layer, 4 + k, 0:rows] for k in range(2)]
            scores = dot_nt(
                jnp.concatenate([parts[0], parts[0]], axis=1), jnp.concatenate(keys, axis=1)
            )
            scores = (scores + dot_nt(parts[1], keys[0])).reshape(batch, rows, rows)
            scores = jnp.where(allowed[None], scores, -1e30)
            peak = jnp.max(scores, -1, keepdims=True)
            chance = jnp.exp(scores - peak)
            chance = chance / jnp.sum(chance, -1, keepdims=True)
            high, low = two_parts(chance.reshape(batch * rows, rows))
            spot = pl.ds(pl.multiple_of(turn * (batch * rows), 64), batch * rows)
            chances[layer, 0, spot, 0:rows] = high
            chances[layer, 1, spot, 0:rows] = low
            seen = fold_pair(dot(high, jnp.concatenate(values, axis=1))) + dot(low, values[0])
            sums[0, 0:rows] += unmasked(seen, masks)
            return carry

        lax.fori_loop(0, heads // batch, attend, 0)
        context = sums[0, 0:rows]
        stream = stream + mm(context, output[layer]) + gains[4]
        unit_two, scale_two = norm_parts(stream)
        normed_two = unit_two * gains[2] + gains[3]
        inner, slope = gelu_both(mm(normed_two, up[layer]) + up_bias[layer])
        stream = stream + mm(inner, down[layer]) + gains[5]
        tape.append((unit_one, scale_one, unit_two, scale_two, inner, slope, context))
    end_stream = stream[slots : 2 * slots]
    unit, scale = norm_parts(end_stream)
    final = unit * vec[12] + vec[13]
    logits = jnp.where(lane < ACT, mm(final, head_ref[...]), -1e30)
    peak = jnp.max(logits, -1, keepdims=True)
    powers = jnp.exp(logits - peak)
    total = jnp.sum(powers, -1, keepdims=True)
    chosen = jnp.sum(jnp.where(lane == action, logits, 0.0), -1, keepdims=True)
    terms = jnp.where(valid, jnp.log(total) + peak - chosen, 0.0)
    loss = jnp.sum(terms, axis=0, keepdims=True)
    d_small_ref[72:80] = jnp.broadcast_to(loss, (8, 128))
    d_logits = jnp.where(valid, powers / total, 0.0) - picks
    d_small_ref[48:72] = flat_head(mm_tn(final, d_logits))
    d_final = mm_nt(d_logits, head_ref[...])
    d_vec = [None] * 17
    d_vec[12] = column_sum(d_final * unit)
    d_vec[13] = column_sum(d_final)
    d_end = norm_back(d_final, unit, scale, vec[12])
    blank = jnp.zeros((slots, 128), F32)
    d_stream = jnp.concatenate([blank, d_end, blank], axis=0)
    for layer in reversed(range(LAYERS)):
        unit_one, scale_one, unit_two, scale_two, inner, slope, context = tape[layer]
        gains = vec[6 * layer : 6 * layer + 6]
        d_vec[6 * layer + 5] = column_sum(d_stream)
        d_down[layer] = mm_tn(inner, d_stream)
        d_inner = mm_nt(d_stream, down[layer]) * slope
        d_up_bias[layer] = column_sum(d_inner)
        normed_two = unit_two * gains[2] + gains[3]
        d_up[layer] = mm_tn(normed_two, d_inner)
        d_normed = mm_nt(d_inner, up[layer])
        d_vec[6 * layer + 2] = column_sum(d_normed * unit_two)
        d_vec[6 * layer + 3] = column_sum(d_normed)
        d_stream = d_stream + norm_back(d_normed, unit_two, scale_two, gains[2])
        d_vec[6 * layer + 4] = column_sum(d_stream)
        d_output[layer] = mm_tn(context, d_stream)
        d_context = mm_nt(d_stream, output[layer])
        bases = d_context * context
        high, low = two_parts(d_context)
        for k in range(3):
            sums[k, 0:rows] = jnp.zeros((rows, 128), F32)
        kept[layer, 6, 0:rows] = high
        kept[layer, 7, 0:rows] = low
        sums[3, 0:rows] = bases

        def attend_back(turn, carry, layer=layer):
            masks = [head_of == turn * batch + k for k in range(batch)]
            query = [masked(kept[layer, k, 0:rows], masks) for k in range(2)]
            keys = [kept[layer, 2 + k, 0:rows] for k in range(2)]
            values = [kept[layer, 4 + k, 0:rows] for k in range(2)]
            d_seen = [masked(kept[layer, 6 + k, 0:rows], masks) for k in range(2)]
            base = jnp.sum(masked(sums[3, 0:rows], masks), -1, keepdims=True)
            spot = pl.ds(pl.multiple_of(turn * (batch * rows), 64), batch * rows)
            chance = [chances[layer, k, spot, 0:rows] for k in range(2)]
            d_chance = dot_nt(
                jnp.concatenate([d_seen[0], d_seen[0]], axis=1), jnp.concatenate(values, axis=1)
            )
            d_chance = d_chance + dot_nt(d_seen[1], values[0])
            d_scores = (chance[0].astype(F32) + chance[1].astype(F32)) * (d_chance - base)
            high, low = two_parts(d_scores)
            d_query = fold_pair(dot(high, jnp.concatenate(keys, axis=1))) + dot(low, keys[0])
            sums[0, 0:rows] += unmasked(d_query, masks)
            d_keys = fold_pair(dot_rows(high, jnp.concatenate(query, axis=1)))
            sums[1, 0:rows] += d_keys + dot_rows(low, query[0])
            d_values = fold_pair(dot_rows(chance[0], jnp.concatenate(d_seen, axis=1)))
            sums[2, 0:rows] += d_values + dot_rows(chance[1], d_seen[0])
            return carry

        lax.fori_loop(0, heads // batch, attend_back, 0)
        normed = unit_one * gains[0] + gains[1]
        d_mixed = jnp.concatenate(
            [sums[0, 0:rows] * 0.25, sums[1, 0:rows], sums[2, 0:rows]], axis=1
        )
        wide = jnp.concatenate([qkv[layer, k] for k in range(3)], axis=1)
        d_wide = mm_tn(normed, d_mixed)
        for k in range(3):
            d_qkv[layer, k] = d_wide[:, k * 128 : (k + 1) * 128]
        d_normed = mm_nt(d_mixed, wide)
        d_vec[6 * layer] = column_sum(d_normed * unit_one)
        d_vec[6 * layer + 1] = column_sum(d_normed)
        d_stream = d_stream + norm_back(d_normed, unit_one, scale_one, gains[0])
    d_reward, d_state, d_move = (d_stream[k * slots : (k + 1) * slots] for k in range(3))
    d_times_ref[0:slots] = jnp.where(valid, d_reward + d_state + d_move, 0.0)
    d_reward = d_reward * (1.0 - reward * reward)
    d_vec[14] = column_sum(d_reward * amount)
    d_vec[15] = column_sum(d_reward)
    d_move = d_move * (1.0 - move * move)
    d_small_ref[24:48] = mm_tn(picks, d_move)[0:24]
    d_state = jnp.where(valid, d_state * (1.0 - state * state), 0.0)
    d_vec[16] = column_sum(d_state)
    d_small_ref[0:24] = jnp.concatenate(d_vec + [jnp.zeros((7, 128), F32)], axis=0)
    high, low = two_parts(d_state)
    twice = jnp.concatenate([high, high], axis=1)
    both = jnp.concatenate([high, low], axis=1)
    d_flat = dot_nt(twice, encoder[...]) + dot_nt(low, encoder[:, 0:128])
    d_block = dot_rows(flats[0, 0:slots], both) + dot_rows(flats[1, 0:slots], both)
    d_block = fold_pair(d_block)
    for k in range(28):
        z = jnp.where(valid, z_ref[k, 0:slots], 0.0)
        d_three_ref[k, 0:slots] = d_flat[:, k * 128 : (k + 1) * 128] * gelu_both(z)[1]
        y, v = divmod(k, 4)
        for o in range(2):
            if 2 * v + o < 7:
                d_encoder_ref[pl.ds(y * 7 + 2 * v + o, 64, stride=49), :] = d_block[
                    k * 128 + o * 64 : k * 128 + (o + 1) * 64
                ]


def former_kernel(
    packed,
    lengths_from,
    starts_from,
    index_from,
    returns_ref,
    actions_ref,
    z_from,
    flat_ref,
    *refs,
):
    if packed:
        split_ref, refs = refs[0], refs[1:]
    else:
        given, refs = refs[:5], refs[5:]
    (d_three_to, rows_ref), refs = refs[:2], refs[2:]
    if packed:
        parts, refs = refs[:8], refs[8:]
        (d_encoder_ref, d_small_ref, d_split), refs = refs[:3], refs[3:]
        weights, grads, refs = refs[:5], refs[5:10], refs[10:]
    else:
        (d_encoder_ref, d_small_ref), grads, refs = refs[:2], refs[2:7], refs[7:]
        weights = given
    (raw, near, small, rows_raw, times_all, encoder, chances, kept, sums, flats), refs = (
        refs[:10],
        refs[10:],
    )
    z_ref, d_three_ref, head_ref, lengths_ref, starts_ref, index_ref, sem = refs
    used = jnp.int32(0)
    wins = lengths_ref.shape[0]
    scalars = [
        pltpu.make_async_copy(source, target, sem.at[wins + 4 + number])
        for number, (source, target) in enumerate(
            ((lengths_from, lengths_ref), (starts_from, starts_ref), (index_from, index_ref))
        )
    ]
    for copy in scalars:
        copy.start()
    for copy in scalars:
        copy.wait()
    for w in range(wins):
        used = used + lengths_ref[w]

    def z_copy(slots):
        return pltpu.make_async_copy(
            z_from.at[:, pl.ds(0, slots)], z_ref.at[:, pl.ds(0, slots)], sem.at[wins + 3]
        )

    def z_back(slots):
        return pltpu.make_async_copy(
            d_three_ref.at[:, pl.ds(0, slots)], d_three_to.at[:, pl.ds(0, slots)], sem.at[wins + 3]
        )

    copies = [
        pltpu.make_async_copy(flat_ref.at[pl.ds(608, 3144)], raw, sem.at[0]),
        pltpu.make_async_copy(flat_ref.at[pl.ds(3744, 48)], rows_raw.at[wins], sem.at[1]),
        pltpu.make_async_copy(
            flat_ref.at[pl.ds(7872, 24)], rows_raw.at[wins + 1, pl.ds(0, 24)], sem.at[2]
        ),
    ]
    offsets = []
    for w in range(wins):
        row = TIME_ROW + starts_ref[w]
        low = pl.multiple_of(lax.div(row, 8) * 8, 8)
        offsets.append(row - low)
        copies.append(
            pltpu.make_async_copy(
                flat_ref.at[pl.ds(low, 40)], rows_raw.at[w, pl.ds(0, 40)], sem.at[3 + w]
            )
        )
    for copy in copies:
        copy.start()

    @pl.when(used <= HALF)
    def few_states():
        z_copy(HALF).start()

    @pl.when(used > HALF)
    def many_states():
        z_copy(ROOM).start()

    if packed:
        unpack_split(split_ref, *weights)
    for copy in copies:
        copy.wait()
    lane = lanes()

    def straight(first, second):
        return jnp.where(lane < 96, pltpu.roll(first, 96, 1), pltpu.roll(second, 96, 1))

    def turn(step, carry):
        spot = pl.multiple_of(step * 64, 64)
        near[pl.ds(spot, 64)] = straight(raw[pl.ds(spot + 1, 64)], raw[pl.ds(spot + 2, 64)])
        return carry

    lax.fori_loop(0, 49, turn, 0)
    for k in range(28):
        y, v = divmod(k, 4)
        halves = []
        for o in range(2):
            if 2 * v + o < 7:
                halves.append(near[pl.ds(y * 7 + 2 * v + o, 64, stride=49), :])
            else:
                halves.append(jnp.zeros((64, 128), F32))
        encoder[k * 128 : (k + 1) * 128] = pair(jnp.concatenate(halves, axis=0))
    small[...] = straight(rows_raw[wins, 1:41], rows_raw[wins, 2:42])
    head_ref[...] = square_head(
        straight(rows_raw[wins + 1, 4:22], rows_raw[wins + 1, 5:23])
    )
    times_all[...] = jnp.zeros(times_all.shape, F32)
    begin = 0
    row = lax.broadcasted_iota(jnp.int32, (32, 1), 0)
    for w in range(wins):
        rows = straight(
            rows_raw[w, pl.ds(offsets[w], 32)], rows_raw[w, pl.ds(offsets[w] + 1, 32)]
        )
        times_all[pl.ds(begin, 32)] = jnp.where(row < lengths_ref[w], rows, 0.0)
        begin = begin + lengths_ref[w]
    rows_ref[...] = jnp.zeros(rows_ref.shape, F32)
    note = jnp.zeros((1, 128), F32)
    for w in range(wins):
        note = jnp.where(lane == w, lengths_ref[w].astype(F32), note)
        note = jnp.where(lane == wins + w, starts_ref[w].astype(F32), note)
    rows_ref[ROOM : ROOM + 1] = note
    d_small_ref[...] = jnp.zeros(d_small_ref.shape, F32)

    def run(slots):
        z_copy(slots).wait()
        former_body(
            slots,
            used,
            lengths_ref,
            returns_ref,
            actions_ref,
            head_ref,
            z_ref,
            small,
            times_all,
            encoder,
            weights,
            d_three_ref,
            d_encoder_ref,
            d_small_ref,
            rows_ref,
            grads,
            chances,
            kept,
            sums,
            flats,
        )
        z_back(slots).start()

    @pl.when(used <= HALF)
    def few():
        run(HALF)

    @pl.when(used > HALF)
    def many():
        run(ROOM)

    if packed:
        count = d_small_ref.shape[0] // 4
        pack_split(d_split, *grads)
        for k in range(4):
            parts[k][...] = d_split[jnp.bitwise_xor(index_ref[0], k)]
            e = jnp.bitwise_xor(index_ref[1], k)
            held = d_encoder_ref[pl.ds(pl.multiple_of(e * 784, 8), 784)]
            parts[4 + k][0:784] = held
            held = d_small_ref[pl.ds(pl.multiple_of(e * count, 8), count)]
            parts[4 + k][784 : 784 + count] = held

    @pl.when(used <= HALF)
    def few_end():
        z_back(HALF).wait()

    @pl.when(used > HALF)
    def many_end():
        z_back(ROOM).wait()


def former(lengths, starts, index, returns, actions, z_three, flat, weights, small_rows, packed):
    vmem = pl.BlockSpec(memory_space=pltpu.VMEM)
    hbm = pl.BlockSpec(memory_space=pltpu.HBM)
    wins = lengths.shape[0]
    canonical = [
        (LAYERS, 3, 128, 128),
        (LAYERS, 128, 128),
        (LAYERS, 128, FF),
        (LAYERS, 1, FF),
        (LAYERS, FF, 128),
    ]
    outs, out_specs = [(28, ROOM, 128), (ROOM + 8, 128)], [hbm, vmem]
    if packed:
        outs += [(784, 128)] * 4 + [(784 + small_rows // 4, 128)] * 4
        out_specs += [vmem] * 8
        scratch = [
            pltpu.VMEM((3136, 128), F32),
            pltpu.VMEM((small_rows, 128), F32),
            pltpu.VMEM((4, 784, 128), F32),
        ]
        scratch += [pltpu.VMEM(shape, F32) for shape in canonical] * 2
    else:
        outs += [(3136, 128), (small_rows, 128)] + canonical
        out_specs += [vmem] * 7
        scratch = []
    rows = 3 * ROOM
    scratch += [
        pltpu.VMEM((3144, 128), F32),
        pltpu.VMEM((3136, 128), F32),
        pltpu.VMEM((40, 128), F32),
        pltpu.VMEM((wins + 2, 48, 128), F32),
        pltpu.VMEM((ROOM + 32, 128), F32),
        pltpu.VMEM((3584, 256), BF16),
        pltpu.VMEM((LAYERS, 2, 8 * rows, rows), BF16),
        pltpu.VMEM((LAYERS, 8, rows, 128), BF16),
        pltpu.VMEM((4, rows, 128), F32),
        pltpu.VMEM((2, ROOM, 3584), BF16),
        pltpu.VMEM((28, ROOM, 128), F32),
        pltpu.VMEM((28, ROOM, 128), F32),
        pltpu.VMEM((128, 128), F32),
        pltpu.SMEM((wins,), jnp.int32),
        pltpu.SMEM((wins,), jnp.int32),
        pltpu.SMEM((2,), jnp.int32),
        pltpu.SemaphoreType.DMA((wins + 7,)),
    ]
    return pl.pallas_call(
        partial(former_kernel, packed),
        in_specs=[hbm] * 3 + [vmem] * 2 + [hbm] * 2 + [vmem] * len(weights),
        out_specs=out_specs,
        out_shape=[jax.ShapeDtypeStruct(shape, F32) for shape in outs],
        scratch_shapes=scratch,
        compiler_params=pltpu.CompilerParams(vmem_limit_bytes=62 * 1024 * 1024),
        name="transformer_step",
    )(lengths, starts, index, returns, actions, z_three, flat, *weights)


SMALL = [("vectors", 24), ("action_table", 24), ("head", 24), ("loss", 8)]
FIELD_ROWS = 8200
EARLY_ROWS = CONV_ROWS + 3136
TABLE_AT = CONV_ROWS + 3136 + 17 + ACT


def round_up(number, grain):
    return -(-number // grain) * grain


def chunk_of(tiles):
    return max(size for size in range(1, 9) if tiles % size == 0)


def mesh_bits(dp_size, mp_size):
    dp_bits = [("dp", k) for k in range(dp_size.bit_length() - 1)]
    mp_bits = [("mp", k) for k in range(mp_size.bit_length() - 1)]
    middle = (len(dp_bits) - 1) // 2
    return mp_bits[:1], mp_bits[1:], dp_bits[:middle], dp_bits[middle:]


def reduce_kernel(plan, *refs):
    mp_size, quarter, share = plan["mp_size"], plan["quarter"], plan["share"]
    split_parts, own_parts, conv_ref = refs[:mp_size], refs[mp_size : 2 * mp_size], refs[2 * mp_size]
    refs = refs[2 * mp_size + 1 :]
    (early_out, small_out, split_out, square_out), refs = refs[:4], refs[4:]
    (split_stage, own_stage, work, landing, split_total, own_total, conv_total), refs = (
        refs[:7],
        refs[7:],
    )
    tiles, tile_in, load_sem, send_sem, recv_sem, store_sem = refs
    spots = {"dp": lax.axis_index("dp"), "mp": lax.axis_index("mp")}
    cores, ys, xs, zs = plan["bits"]
    slots = iter(range(plan["copies"]))

    def value(bit):
        return lax.rem(lax.div(spots[bit[0]], 1 << bit[1]), 2)

    def turned(stage, mask):
        index = 0
        for k, bit in enumerate(stage):
            own = value(bit)
            index = index + ((1 - own) if mask & (1 << k) else own) * (1 << k)
        return index

    def partner(stage, mask):
        place = dict(spots)
        for k, bit in enumerate(stage):
            if mask & (1 << k):
                place[bit[0]] = place[bit[0]] + (1 - 2 * value(bit)) * (1 << bit[1])
        return (place["dp"], place["mp"])

    def masks_of(stage):
        return range(1, 1 << len(stage))

    def send(source, target, stage, mask):
        slot = next(slots)
        copy = pltpu.make_async_remote_copy(
            src_ref=source,
            dst_ref=target,
            send_sem=send_sem.at[slot],
            recv_sem=recv_sem.at[slot],
            device_id=partner(stage, mask),
            device_id_type=pl.DeviceIdType.MESH,
        )
        copy.start()
        return copy

    loads = []
    for k in range(mp_size):
        for parts, stage in ((own_parts, own_stage), (split_parts, split_stage)):
            copy = pltpu.make_async_copy(parts[k], stage.at[k], load_sem.at[len(loads)])
            loads.append(copy)
    conv_tiles = CONV_ROWS // 8
    target = work.at[pl.ds(plan["conv"], conv_tiles)]
    loads.append(pltpu.make_async_copy(conv_ref, target, load_sem.at[len(loads)]))
    for load in loads:
        load.start()

    def wipe(target, start, count):
        if count > 0:
            target[start : start + count] = jnp.zeros((count, 8, 128), F32)

    wipe(work, plan["conv"] + conv_tiles, plan["conv_size"] - conv_tiles)
    wipe(work, plan["split"] + quarter, plan["split_size"] - quarter)
    wipe(work, plan["own"] + quarter + share, plan["own_size"] - quarter - share)
    barrier = pltpu.get_barrier_semaphore()
    greeted = [(stage, mask) for stage in (cores + ys, xs, zs) for mask in masks_of(stage)]
    for stage, mask in greeted:
        pl.semaphore_signal(
            barrier,
            inc=1,
            device_id=partner(stage, mask),
            device_id_type=pl.DeviceIdType.MESH,
        )
    pl.semaphore_wait(barrier, len(greeted))

    def sum_into(target, start, pieces, count):
        chunk = chunk_of(count)

        def body(turn, carry):
            held = pieces[0][0][pl.ds(pieces[0][1] + turn * chunk, chunk)]
            for source, at in pieces[1:]:
                held = held + source[pl.ds(at + turn * chunk, chunk)]
            target[pl.ds(start + turn * chunk, chunk)] = held
            return carry

        lax.fori_loop(0, count // chunk, body, 0)

    class Stream:
        def __init__(self, base, size, stages, total, total_at):
            self.base, self.size, self.stages = base, size, stages
            self.total, self.at = total, total_at
            self.land = base
            self.flight = None
            self.step = 0
            self.start = base

        def reduce(self):
            if self.flight is not None:
                copies, piece, lands, keep = self.flight
                for copy in copies:
                    copy.wait()
                pieces = [(work, keep)] + [(landing, land) for land in lands]
                sum_into(work, keep, pieces, piece)
                self.base, self.size, self.flight = keep, piece, None
            if self.step < len(self.stages):
                stage = self.stages[self.step]
                piece = self.size >> len(stage)
                keep = self.base + turned(stage, 0) * piece
                copies, lands = [], []
                for mask in masks_of(stage):
                    give = self.base + turned(stage, mask) * piece
                    target = landing.at[pl.ds(self.land, piece)]
                    copies.append(send(work.at[pl.ds(give, piece)], target, stage, mask))
                    lands.append(self.land)
                    self.land += piece
                self.flight = (copies, piece, lands, keep)
                self.step += 1

        def turn(self):
            self.at = self.at + (self.base - self.start)
            sum_into(self.total, self.at, [(work, self.base)], self.size)
            self.step = 0

        def double(self):
            if self.flight is not None:
                for copy in self.flight:
                    copy.wait()
                stage = self.stages[len(self.stages) - self.step]
                self.at = self.at - turned(stage, 0) * self.size
                self.size, self.flight = self.size << len(stage), None
            if self.step < len(self.stages):
                stage = self.stages[len(self.stages) - 1 - self.step]
                region = self.total.at[pl.ds(self.at, self.size)]
                self.flight = [send(region, region, stage, mask) for mask in masks_of(stage)]
                self.step += 1

        def squares(self, keep):
            held = work[pl.ds(self.base, self.size)]
            if keep is not None:
                tile = lax.broadcasted_iota(jnp.int32, (self.size, 8, 128), 0)
                held = jnp.where(keep(tile + self.base), held, 0.0)
            return jnp.sum(held * held, axis=0)

    sharing = cores + xs
    seat = sum(value(bit) * (1 << k) for k, bit in enumerate(sharing))

    def keep_own(tile):
        place = tile - plan["own"] - quarter
        return (place < 0) | (place + seat * share < 9)

    class Quarter:
        def __init__(self, stream, offset, stages):
            self.at = stream.base - stream.start + offset
            self.size, self.stages = stream.size, stages
            self.held, self.flights, self.step = [0], [], 0
            sum_into(own_total.at[seat], self.at, [(work, stream.base)], stream.size)

        def region(self, offset):
            return own_total.at[turned(sharing, offset), pl.ds(self.at, self.size)]

        def double(self):
            if self.flights:
                for copy in self.flights:
                    copy.wait()
                stage = self.stages[self.step - 1]
                if stage[0] in sharing:
                    changed = 1 << sharing.index(stage[0])
                    self.held = self.held + [offset | changed for offset in self.held]
                else:
                    self.at = self.at - turned(stage, 0) * self.size
                    self.size <<= len(stage)
                self.flights = []
            if self.step < len(self.stages):
                stage = self.stages[self.step]
                for offset in self.held:
                    region = self.region(offset)
                    self.flights += [send(region, region, stage, mask) for mask in masks_of(stage)]
                self.step += 1

    first, second = plan["cut"]
    own = [
        Stream(plan["own"], first, [ys, zs], None, 0),
        Stream(plan["own"] + first, plan["own_size"] - first, [zs, ys], None, 0),
    ]
    split = [
        Stream(plan["split"], second, [xs, zs], split_total, 0),
        Stream(
            plan["split"] + second,
            plan["split_size"] - second,
            [zs, xs],
            split_total,
            second,
        ),
    ]
    conv = Stream(plan["conv"], plan["conv_size"], [cores + ys, xs, zs], conv_total, 0)
    for load in loads:
        load.wait()
    sum_into(
        work,
        plan["own"],
        [(own_stage.at[k], 0) for k in range(mp_size)],
        quarter + share,
    )
    for stream in own + [conv]:
        stream.reduce()
    sum_into(work, plan["split"], [(split_stage.at[k], 0) for k in range(mp_size)], quarter)
    for stream in own + [conv]:
        stream.reduce()
    for stream in split:
        stream.reduce()
    for stream in own:
        stream.reduce()
    squares = jnp.zeros((8, 128), F32)
    singles = [[bit] for bit in xs]
    quarters = [
        Quarter(own[0], 0, [zs, ys] + singles + [cores]),
        Quarter(own[1], first, [ys] + singles + [zs, cores]),
    ]
    for piece in quarters:
        piece.double()
    conv.reduce()
    for stream in split:
        stream.reduce()
    for stream in own:
        squares = squares + stream.squares(keep_own)
    for piece in quarters:
        piece.double()
    conv.reduce()
    squares = squares + conv.squares(None)
    conv.turn()
    conv.double()
    for stream in split:
        stream.reduce()
        squares = squares + stream.squares(None)
    tiles[0] = squares
    tile_stages = [cores + ys, xs, zs]

    def send_tiles(number):
        stage = tile_stages[number]
        spot = number * 8 - 1
        return [
            send(tiles.at[number], tile_in.at[spot + mask], stage, mask)
            for mask in masks_of(stage)
        ]

    tile_flights = send_tiles(0)
    for stream in split:
        stream.turn()
        stream.double()
    rounds = 1
    while rounds <= len(tile_stages) or conv.flight is not None or quarters[0].flights:
        for stream in quarters + [conv]:
            stream.double()
        if rounds <= len(tile_stages):
            for copy in tile_flights:
                copy.wait()
            held = tiles[rounds - 1]
            for mask in masks_of(tile_stages[rounds - 1]):
                held = held + tile_in[(rounds - 1) * 8 - 1 + mask]
            tiles[rounds] = held
            if rounds < len(tile_stages):
                tile_flights = send_tiles(rounds)
        for stream in split:
            stream.double()
        rounds += 1
    square_out[...] = tiles[len(tile_stages)]
    stores = [
        (conv_total.at[pl.ds(0, conv_tiles)], early_out.at[pl.ds(0, conv_tiles)]),
        (split_total.at[pl.ds(0, quarter)], split_out),
    ]
    for m in range(mp_size):
        rows = pl.ds(conv_tiles + m * quarter, quarter)
        stores.append((own_total.at[m, pl.ds(0, quarter)], early_out.at[rows]))
        rows = pl.ds(m * share, share)
        stores.append((own_total.at[m, pl.ds(quarter, share)], small_out.at[rows]))
    stores = [
        pltpu.make_async_copy(source, target, store_sem.at[number])
        for number, (source, target) in enumerate(stores)
    ]
    for copy in stores:
        copy.start()
    for copy in stores:
        copy.wait()


def reduce_all(split_parts, own_parts, conv, dp_size, mp_size):
    bits = mesh_bits(dp_size, mp_size)
    quarter = split_parts[0].shape[0] // 8
    share = own_parts[0].shape[0] // 8 - quarter
    own_size = round_up(quarter + share, dp_size)
    split_size = round_up(quarter, dp_size)
    conv_size = round_up(CONV_ROWS // 8, dp_size * mp_size)
    places, at = {}, 0
    for name, size in [("split", split_size), ("own", own_size), ("conv", conv_size)]:
        places[name] = at
        at += size
    cut = (round_up(own_size // 2, dp_size), round_up(split_size // 2, dp_size))
    copies = 16 * (dp_size + mp_size) + 2 * mp_size * dp_size
    plan = dict(
        places,
        mp_size=mp_size,
        quarter=quarter,
        share=share,
        bits=bits,
        copies=copies,
        split_size=split_size,
        own_size=own_size,
        conv_size=conv_size,
        cut=cut,
    )
    vmem = pl.BlockSpec(memory_space=pltpu.VMEM)
    any_spec = pl.BlockSpec(memory_space=pl.ANY)
    arrays = [*split_parts, *own_parts, conv]
    loads = len(arrays)

    def tiled(size, *lead):
        return pltpu.VMEM((*lead, size, 8, 128), F32)

    outs = [(EARLY_ROWS // 8, 8, 128), (share * mp_size, 8, 128), (quarter, 8, 128), (8, 128)]
    results = pl.pallas_call(
        partial(reduce_kernel, plan),
        in_specs=[any_spec] * loads,
        out_specs=[any_spec, any_spec, any_spec, vmem],
        out_shape=[jax.ShapeDtypeStruct(shape, F32) for shape in outs],
        scratch_shapes=[
            tiled(quarter, mp_size),
            tiled(quarter + share, mp_size),
            tiled(at),
            tiled(at),
            tiled(split_size),
            tiled(own_size, mp_size),
            tiled(conv_size),
            pltpu.VMEM((4, 8, 128), F32),
            pltpu.VMEM((24, 8, 128), F32),
            pltpu.SemaphoreType.DMA((loads,)),
            pltpu.SemaphoreType.DMA((copies,)),
            pltpu.SemaphoreType.DMA((copies,)),
            pltpu.SemaphoreType.DMA((2 + 2 * mp_size,)),
        ],
        compiler_params=pltpu.CompilerParams(
            collective_id=1, has_side_effects=True, vmem_limit_bytes=62 * 1024 * 1024
        ),
        name="reduce_gradients",
    )(*[array.reshape(-1, 8, 128) for array in arrays])
    return [held.reshape(-1, 128) for held in results]


FLAT_ROWS = 7896
BLOCK_ROWS = 1024
LATE = 609
SPAN = 40


def adam_kernel(
    wins,
    early_ref,
    rows_ref,
    small_ref,
    split_ref,
    square_ref,
    weight_ref,
    first_ref,
    second_ref,
    split_weight_ref,
    split_first_ref,
    split_second_ref,
    new_ref,
    new_first_ref,
    new_second_ref,
    low_ref,
    split_new_ref,
    split_new_first_ref,
    split_new_second_ref,
    split_low_ref,
    scalar_ref,
    split_in,
    split_out,
    field,
    rows,
    notes,
    marks,
    pulled,
    factor_ref,
    pull_sem,
    load_sem,
    split_sem,
):
    step = pl.program_id(0)
    last = pl.num_programs(0) - 1
    lane = lax.broadcasted_iota(jnp.int32, (1, 128), 1)

    def pull(block, slot):
        start = pl.multiple_of(block * BLOCK_ROWS, BLOCK_ROWS)
        return pltpu.make_async_copy(
            field.at[pl.ds(start, BLOCK_ROWS + 8)], pulled.at[slot], pull_sem.at[slot]
        )

    def update(weights, first, second, grads):
        first = beta_first * first + (1 - beta_first) * grads
        second = beta_second * second + (1 - beta_second) * grads * grads
        fix_one = 1.0 / (1 - beta_first**STEP)
        fix_two = 1.0 / (1 - beta_second**STEP)
        weights = weights - learn_rate * (
            first * fix_one / (jnp.sqrt(second * fix_two) + adam_epsilon) + weight_decay * weights
        )
        return weights, first, second

    def sum_of(tile):
        held = jnp.sum(jnp.sum(tile, axis=0, keepdims=True), axis=1, keepdims=True)
        return jnp.broadcast_to(held, (1, 128))

    slot = lax.rem(step, 2)
    split_loads = [
        pltpu.make_async_copy(ref, split_in.at[k], split_sem.at[k])
        for k, ref in enumerate((split_weight_ref, split_first_ref, split_second_ref))
    ]
    split_stores = [
        pltpu.make_async_copy(split_out.at[k], ref, split_sem.at[3 + k])
        for k, ref in enumerate((split_new_ref, split_new_first_ref, split_new_second_ref))
    ]

    @pl.when(step == 0)
    def prepare():
        for load in split_loads:
            load.start()
        load_rows = pltpu.make_async_copy(rows_ref, rows, load_sem.at[0])
        load_early = pltpu.make_async_copy(
            early_ref, field.at[pl.ds(0, EARLY_ROWS)], load_sem.at[1]
        )
        load_rows.start()
        load_early.start()
        late = FIELD_ROWS - EARLY_ROWS
        field[EARLY_ROWS:FIELD_ROWS] = jnp.zeros((late, 128), F32)
        load_rows.wait()
        stride = ROOM + 8
        devices = rows.shape[0] // stride
        notes[...] = rows[pl.ds(ROOM, devices, stride=stride), :]
        mark = pltpu.make_async_copy(notes, marks, load_sem.at[2])
        mark.start()
        mark.wait()
        place = lax.broadcasted_iota(jnp.int32, (SPAN, ROOM), 0)
        slot_of = lax.broadcasted_iota(jnp.int32, (SPAN, ROOM), 1)

        def scatter(turn, carry):
            spots, found = [], []
            for k in range(4):
                device = turn * 4 + k
                begin = jnp.int32(0)
                picks = []
                for w in range(wins):
                    length = marks[device, w].astype(jnp.int32)
                    row = marks[device, wins + w].astype(jnp.int32) + TABLE_AT
                    low = lax.div(row, 8) * 8
                    inside = (slot_of >= begin) & (slot_of < begin + length)
                    inside = inside & (place - slot_of == row - low - begin)
                    picks.append(jnp.where(inside, 1.0, 0.0).astype(BF16))
                    spots.append(low)
                    begin = begin + length
                held = pair(rows[pl.ds(pl.multiple_of(device * stride, 8), ROOM)])
                found.append(fold_pair(dot(jnp.concatenate(picks, axis=0), held)))
            for k in range(4):
                for w in range(wins):
                    spot = pl.ds(pl.multiple_of(spots[k * wins + w], 8), SPAN)
                    field[spot] = field[spot] + found[k][w * SPAN : (w + 1) * SPAN]
            return carry

        lax.fori_loop(0, devices // 4, scatter, 0)

        def fold(turn, carry):
            spot = pl.multiple_of(EARLY_ROWS + turn * 64, 8)
            held = field[pl.ds(spot, 64)]
            return carry + jnp.sum((held * held).reshape(8, 8, 128), axis=0)

        squares = lax.fori_loop(0, late // 64, fold, square_ref[...])
        at = EARLY_ROWS
        for name_at, count in [(0, 17), (24, ACT)]:
            field[at : at + count] = small_ref[name_at : name_at + count]
            at += count
        at = TABLE_AT + TSTEPS
        field[at : at + ACT] = small_ref[48 : 48 + ACT]
        lane_all = lax.broadcasted_iota(jnp.int32, notes.shape, 1)
        count = sum_of(jnp.where(lane_all < wins, notes[...], 0.0))
        seed = 1.0 / count
        norm = jnp.sqrt(sum_of(squares)) * seed
        factor = jnp.minimum(1.0, clip_limit / (norm + 1e-06)) * seed
        factor_ref[...] = jnp.broadcast_to(factor, (8, 128))
        loss = small_ref[72:73]
        row = lax.broadcasted_iota(jnp.int32, (8, 128), 0)
        scalar_ref[...] = jnp.where(row == 0, norm, jnp.where(row == 1, loss, count))
        load_early.wait()
        pull(0, 0).start()

    @pl.when(step < last)
    def ahead():
        pull(step + 1, 1 - slot).start()

    @pl.when(step == 1)
    def split():
        for load in split_loads:
            load.wait()
        count = split_in.shape[1]
        outs = update(*[split_in[k] for k in range(3)], split_ref[0:count] * factor_ref[0:1])
        for k in range(3):
            split_out[k] = outs[k]
        split_low_ref[...] = outs[0].astype(BF16)
        for store in split_stores:
            store.start()

    @pl.when(step == last)
    def split_end():
        for store in split_stores:
            store.wait()

    pull(step, slot).wait()
    early = pulled[slot, 0:BLOCK_ROWS]
    own = pltpu.roll(pulled[slot, 7 : BLOCK_ROWS + 7], 32, 1)
    before = pltpu.roll(pulled[slot, 6 : BLOCK_ROWS + 6], 32, 1)
    row = lax.broadcasted_iota(jnp.int32, (BLOCK_ROWS, 1), 0) + step * BLOCK_ROWS
    grads = jnp.where(lane < 32, jnp.where(row == LATE, early, before), own)
    grads = jnp.where(row < LATE, early, grads)
    outs = update(weight_ref[...], first_ref[...], second_ref[...], grads * factor_ref[0:1])
    new_ref[...], new_first_ref[...], new_second_ref[...] = outs
    low_ref[...] = outs[0].astype(BF16)


def adam_all(early, rows, small, split_grad, square, shared, split, wins):
    grid = -(-FLAT_ROWS // BLOCK_ROWS)
    flat_spec = pl.BlockSpec((BLOCK_ROWS, 128), lambda i: (i, 0))
    split_rows = split[0].shape[0]
    devices = rows.shape[0]

    def whole(shape):
        return pl.BlockSpec(shape, lambda i: (0,) * len(shape))

    shared_out = jax.ShapeDtypeStruct((FLAT_ROWS, 128), F32)
    split_out = jax.ShapeDtypeStruct((split_rows, 128), F32)
    any_spec = pl.BlockSpec(memory_space=pl.ANY)
    return pl.pallas_call(
        partial(adam_kernel, wins),
        grid=(grid,),
        in_specs=[
            any_spec,
            any_spec,
            whole(small.shape),
            whole(split_grad.shape),
            whole((8, 128)),
            flat_spec,
            flat_spec,
            flat_spec,
            any_spec,
            any_spec,
            any_spec,
        ],
        out_specs=[flat_spec] * 4
        + [any_spec] * 3
        + [whole((split_rows, 128)), whole((8, 128))],
        out_shape=[shared_out] * 3
        + [jax.ShapeDtypeStruct((FLAT_ROWS, 128), BF16)]
        + [split_out] * 3
        + [jax.ShapeDtypeStruct((split_rows, 128), BF16)]
        + [jax.ShapeDtypeStruct((8, 128), F32)],
        scratch_shapes=[
            pltpu.VMEM((3, split_rows, 128), F32),
            pltpu.VMEM((3, split_rows, 128), F32),
            pltpu.VMEM((FIELD_ROWS, 128), F32),
            pltpu.VMEM((devices * (ROOM + 8), 128), F32),
            pltpu.VMEM((devices, 128), F32),
            pltpu.SMEM((devices, 128), F32),
            pltpu.VMEM((2, BLOCK_ROWS + 8, 128), F32),
            pltpu.VMEM((8, 128), F32),
            pltpu.SemaphoreType.DMA((2,)),
            pltpu.SemaphoreType.DMA((3,)),
            pltpu.SemaphoreType.DMA((6,)),
        ],
        compiler_params=pltpu.CompilerParams(vmem_limit_bytes=62 * 1024 * 1024),
        name="adam_update",
    )(
        early,
        rows.reshape(devices * (ROOM + 8), 128),
        small,
        split_grad,
        square,
        *shared,
        *split,
    )


def per_device(
    frames,
    returns,
    actions,
    starts,
    lengths,
    shared_weights,
    shared_first,
    shared_second,
    split_weights,
    split_first,
    split_second,
):
    dp_size, mp_size = lax.axis_size("dp"), lax.axis_size("mp")
    narrow = D // mp_size
    hidden_width = FF // mp_size
    wins, steps = returns.shape
    width = split_weights.shape[0]
    split_rows = width // 128
    packed = narrow == 32
    own_rows = split_weights.reshape(split_rows, 128)
    split_all = lax.all_gather(own_rows, "mp", axis=0)
    flat = shared_weights.reshape(FLAT_ROWS, 128)
    picked, z_one, z_two, z_three = conv_forward(lengths, frames, flat)
    if packed:
        weights = [split_all]
    else:
        layers, layers_back = jax.vjp(
            lambda held: assemble(held, mp_size, narrow, hidden_width), split_all.reshape(-1)
        )
        weights = [
            jnp.stack([layer["qkv"].transpose(1, 0, 2) for layer in layers]),
            jnp.stack([layer["output"] for layer in layers]),
            jnp.stack([layer["up"] for layer in layers]),
            jnp.stack([layer["up_bias"][None] for layer in layers]),
            jnp.stack([layer["down"] for layer in layers]),
        ]
    small_rows = round_up(sum(rows for name, rows in SMALL), 8 * mp_size)
    cores, ys, xs, zs = mesh_bits(dp_size, mp_size)
    seat = jnp.bitwise_and(lax.axis_index("mp"), 1)
    seat = seat + 2 * jnp.bitwise_and(lax.axis_index("dp"), (1 << len(xs)) - 1)
    index = jnp.stack([lax.axis_index("mp"), seat])
    results = former(
        lengths, starts, index, returns, actions, z_three, flat, weights, small_rows, packed
    )
    d_three, rows = results[:2]
    rows_all = lax.all_gather(rows, ("dp", "mp"), axis=0)
    quarter = 3136 // mp_size
    if packed:
        split_parts, own_parts = results[2:6], results[6:]
    else:
        d_encoder, d_small, d_qkv, d_output, d_up, d_up_bias, d_down = results[2:]
        grad_layers = [
            dict(
                qkv=d_qkv[layer].transpose(1, 0, 2),
                output=d_output[layer],
                up=d_up[layer],
                up_bias=d_up_bias[layer, 0],
                down=d_down[layer],
            )
            for layer in range(LAYERS)
        ]
        gathered = layers_back(grad_layers)[0].reshape(mp_size, split_rows, 128)
        gathered = jnp.pad(gathered, ((0, 0), (0, quarter - split_rows), (0, 0)))
        encoder = d_encoder.reshape(mp_size, quarter, 128)
        small = d_small.reshape(mp_size, -1, 128)
        every = jnp.concatenate([encoder, small], axis=1)

        def turned(held, own):
            return [
                lax.dynamic_index_in_dim(held, jnp.bitwise_xor(own, k), 0, keepdims=False)
                for k in range(mp_size)
            ]

        split_parts, own_parts = turned(gathered, index[0]), turned(every, index[1])
    split_parts, own_parts = list(split_parts), list(own_parts)
    for k in range(1, mp_size):
        turn = [(place, place ^ k) for place in range(mp_size)]
        split_parts[k] = lax.ppermute(split_parts[k], "mp", turn)
        turn = [
            (dp * mp_size + mp, (dp ^ (k >> 1)) * mp_size + (mp ^ (k & 1)))
            for dp in range(dp_size)
            for mp in range(mp_size)
        ]
        own_parts[k] = lax.ppermute(own_parts[k], ("dp", "mp"), turn)
    d_conv = conv_backward(lengths, picked, z_one, z_two, d_three, flat)
    early, small, split_sum, square = reduce_all(
        split_parts, own_parts, d_conv, dp_size, mp_size
    )
    shared_view = [a.reshape(FLAT_ROWS, 128) for a in (shared_weights, shared_first, shared_second)]
    split_view = [a.reshape(split_rows, 128) for a in (split_weights, split_first, split_second)]
    updated = adam_all(
        early, rows_all, small, split_sum, square, shared_view, split_view, wins
    )
    shared_out = [a.reshape(-1) for a in updated[:4]]
    split_out = [a.reshape(-1) for a in updated[4:8]]
    scalars = updated[8]
    return (*shared_out, *split_out, scalars[0, 0], scalars[1, 0], scalars[2, 0])


def solution(mesh):
    return jax.shard_map(
        per_device,
        mesh=mesh,
        in_specs=(
            P(("dp", "mp"), None, None, None, None),
            P(("dp", "mp"), None),
            P(("dp", "mp"), None),
            P(("dp", "mp")),
            P(("dp", "mp")),
            P(),
            P(),
            P(),
            P("mp"),
            P("mp"),
            P("mp"),
        ),
        out_specs=(P(), P(), P(), P(), P("mp"), P("mp"), P("mp"), P("mp"), P(), P(), P()),
        check_vma=False,
    )
```

```python
from functools import partial
import math

import jax
import jax.numpy as jnp
from jax import lax
from jax.experimental import pallas as pl
from jax.experimental.pallas import tpu as pltpu
from jax.sharding import PartitionSpec as P

D = 128
FF = 512
ACT = 18
C1 = 32
C2 = 64
TSTEPS = 4096
LAYERS = 2
STEP = 10
HD = 16


clip_limit = 0.1
learn_rate = 0.05
beta_first = 0.9
beta_second = 0.95
adam_epsilon = 1e-08
weight_decay = 0.1


def span_layout(narrow, hidden):
    return [
        ("qkv", (D, 3, narrow)),
        ("output", (narrow, D)),
        ("up", (D, hidden)),
        ("up_bias", (hidden,)),
        ("down", (hidden, D)),
    ]


def assemble(flat, copies, narrow, hidden):
    layout = span_layout(narrow, hidden)
    width = sum((math.prod(shape) for name, shape in layout))
    blocks = flat.reshape(copies, LAYERS, width)
    layers = []
    for layer in range(LAYERS):
        offset = 0
        pieces = {}
        for name, shape in layout:
            count = math.prod(shape)
            pieces[name] = blocks[:, layer, offset : offset + count].reshape((copies,) + shape)
            offset += count
        layers.append(
            {
                "qkv": jnp.moveaxis(pieces["qkv"], 0, 2).reshape(D, 3, copies * narrow),
                "output": pieces["output"].reshape(copies * narrow, D),
                "up": jnp.moveaxis(pieces["up"], 0, 1).reshape(D, copies * hidden),
                "up_bias": pieces["up_bias"].reshape(copies * hidden),
                "down": pieces["down"].reshape(copies * hidden, D),
            }
        )
    return layers


GROUP = 16
CONV_ROWS = 616
FAST_ROWS = 768
ROOM = 128
HALF = 64
BF16 = jnp.bfloat16
F32 = jnp.float32


def gelu_value(x):
    inner = 0.7978845608028654 * (x + 0.044715 * (x * x * x))
    return 0.5 * x * (1.0 + jnp.tanh(inner))


def gelu_both(x):
    square = x * x
    turn = jnp.tanh(0.7978845608028654 * x * (1.0 + 0.044715 * square))
    half = 0.5 * (1.0 + turn)
    slope = half + 0.5 * x * (1.0 - turn * turn) * (
        0.7978845608028654 * (1.0 + 3 * 0.044715 * square)
    )
    return x * half, slope


def two_parts(x):
    high = x.astype(BF16)
    return high, (x - high.astype(F32)).astype(BF16)


def pair(x):
    return jnp.concatenate(two_parts(x), axis=-1)


def fold_pair(x):
    return x[:, :128] + x[:, 128:]


def dot(a, b):
    return lax.dot_general(a, b, (((1,), (0,)), ((), ())), preferred_element_type=F32)


def dot_rows(a, b):
    return lax.dot_general(a, b, (((0,), (0,)), ((), ())), preferred_element_type=F32)


def lanes():
    return lax.broadcasted_iota(jnp.int32, (1, 128), 1)


def conv_biases(flat_ref):
    lane = lanes()
    one = jnp.where(lane < 32, flat_ref[64:65], 0.0)
    one = one + pltpu.roll(one, 32, 1)
    one = one + pltpu.roll(one, 64, 1)
    two = jnp.where(lane < 64, pltpu.roll(flat_ref[320:321], 96, 1), 0.0)
    two = two + pltpu.roll(two, 64, 1)
    three = jnp.where(
        lane < 32,
        pltpu.roll(flat_ref[608:609], 32, 1),
        jnp.where(lane < 64, pltpu.roll(flat_ref[609:610], 32, 1), 0.0),
    )
    three = three + pltpu.roll(three, 64, 1)
    return one, two, three


def shifted(ref, start, rows, lane):
    first = pltpu.roll(ref[start : start + rows], 128 - lane, 1)
    second = pltpu.roll(ref[start + 1 : start + 1 + rows], 128 - lane, 1)
    return jnp.where(lanes() < 128 - lane, first, second)


def spread_one(flat_ref, put):
    halves = [jnp.transpose(flat_ref[pl.ds(side, 32, stride=2), :]) for side in range(2)]
    turned = jnp.concatenate(halves, axis=0)
    lane = lax.broadcasted_iota(jnp.int32, (8, 128), 1)
    row = lax.broadcasted_iota(jnp.int32, (8, 128), 0)
    low = row < 4
    column = lax.shift_right_logical(lane, 5)
    for ky in range(8):
        for c in range(4):
            held = turned[c * 64 + ky * 8 : c * 64 + ky * 8 + 8]
            wide = jnp.concatenate([held] * 4, axis=1)
            flipped = jnp.concatenate([wide[4:], wide[:4]], axis=0)
            zero = jnp.zeros((8, 128), F32)
            first = jnp.where(column == 0, wide, jnp.where((column == 1) & ~low, flipped, zero))
            second = jnp.where(
                column == 2,
                wide,
                jnp.where(((column == 1) & low) | ((column == 3) & ~low), flipped, zero),
            )
            third = jnp.where((column == 3) & low, flipped, zero)
            put(ky * 128 + c * 32, jnp.concatenate([first, second, third, zero], axis=0))


def spread_two(flat_ref, rows_ref, turned, put):
    lane = lax.broadcasted_iota(jnp.int32, (32, 128), 1)
    rows_ref[0:256] = shifted(flat_ref, 64, 256, 32)
    for j in range(4):
        block = jnp.transpose(rows_ref[pl.ds(j, 64, stride=4), :])
        turned[j * 128 : (j + 1) * 128] = jnp.concatenate([block, block], axis=1)
    for ky in range(4):
        rows = [turned[pl.ds(ky * 4 + kx, 32, stride=16)] for kx in range(4)]
        for i in range(8):
            left = rows[i] if i < 4 else jnp.zeros((32, 128), F32)
            right = rows[i - 2] if 2 <= i < 6 else jnp.zeros((32, 128), F32)
            put(ky * 256 + i * 32, jnp.where(lane < 64, left, right))


def spread_three(flat_ref, rows_ref, turned, put):
    lane = lax.broadcasted_iota(jnp.int32, (64, 128), 1)
    side = lax.broadcasted_iota(jnp.int32, (32, 128), 1) < 64
    rows_ref[0:288] = shifted(flat_ref, 320, 288, 96)
    nine = [rows_ref[pl.ds(k, 32, stride=9), :] for k in range(9)]
    flips = [pltpu.roll(nine[4 + k], 64, 1) for k in range(5)]
    for j in range(5):
        wide = min(128, 576 - j * 128)
        rows_ref[pl.ds(0, 32, stride=2), :] = nine[j]
        rows_ref[pl.ds(1, 32, stride=2), :] = (
            jnp.where(side, flips[j], flips[j + 1]) if j < 4 else flips[4]
        )
        block = jnp.transpose(rows_ref[0:64])[0:wide]
        turned[j * 128 : j * 128 + wide] = jnp.concatenate([block, block], axis=1)
    for ky in range(3):
        rows = [turned[pl.ds(ky * 3 + kx, 64, stride=9)] for kx in range(3)]
        for i in range(4):
            left = rows[i] if i < 3 else jnp.zeros((64, 128), F32)
            right = rows[i - 1] if i >= 1 else jnp.zeros((64, 128), F32)
            put(ky * 256 + i * 64, jnp.where(lane < 64, left, right))


def last_masks():
    return lanes() < 64


def conv_forward_kernel(
    lengths_from,
    frames_ref,
    shared_ref,
    picked_ref,
    z_one_ref,
    z_two_ref,
    z_three_ref,
    flat_ref,
    held,
    wide,
    picked,
    z_one,
    z_two,
    z_three,
    h_one,
    h_two,
    w_one,
    w_two,
    w_three,
    choose,
    rows_ref,
    turned,
    lengths_ref,
    frame_sem,
    out_sem,
):
    scalars = pltpu.make_async_copy(lengths_from, lengths_ref, out_sem.at[5])
    scalars.start()
    scalars.wait()
    wins = lengths_ref.shape[0]
    steps = frames_ref.shape[1]
    used = jnp.int32(0)
    for w in range(wins):
        used = used + lengths_ref[w]
    groups = lax.div(used + (GROUP - 1), GROUP)

    def frame_copy(group, spot, slot):
        state = jnp.minimum(group * GROUP + spot, used - 1)
        window, begin, end = jnp.int32(0), jnp.int32(0), jnp.int32(0)
        for w in range(wins - 1):
            end = end + lengths_ref[w]
            window = jnp.where(state >= end, w + 1, window)
            begin = jnp.where(state >= end, end, begin)
        return pltpu.make_async_copy(
            frames_ref.at[window, state - begin], held.at[slot, spot], frame_sem.at[slot, spot]
        )

    def fetch(group, slot):
        def one(spot, carry):
            frame_copy(group, spot, slot).start()
            return carry

        lax.fori_loop(0, GROUP, one, 0)

    weights = pltpu.make_async_copy(
        shared_ref.at[pl.ds(0, CONV_ROWS)], flat_ref, out_sem.at[4]
    )
    weights.start()
    fetch(0, 0)
    h_one[...] = jnp.zeros(h_one.shape, BF16)

    def put_one(row, block):
        w_one[row : row + 32] = pair(block)

    def put_two(row, block):
        w_two[row : row + 32] = pair(block)

    def put_three(row, block):
        w_three[row : row + 64] = pair(block)

    weights.wait()
    spread_one(flat_ref, put_one)
    spread_two(flat_ref, rows_ref, turned, put_two)
    spread_three(flat_ref, rows_ref, turned, put_three)
    bias_one, bias_two, bias_three = conv_biases(flat_ref)
    row = lax.broadcasted_iota(jnp.int32, (128, 640), 0)
    column = lax.broadcasted_iota(jnp.int32, (128, 640), 1)
    place = jnp.bitwise_and(column, 31)
    channel = jnp.bitwise_and(lax.shift_right_logical(column, 5), 3)
    block = lax.shift_right_logical(column, 7)
    right = (row == 16 * block + place) & (place < 20)
    for c in range(4):
        choose[c * 128 : (c + 1) * 128] = jnp.where(right & (channel == c), 1.0, 0.0).astype(BF16)

    def one_group(group, carry):
        slot = lax.rem(group, 2)

        @pl.when(group + 1 < groups)
        def ahead():
            fetch(group + 1, 1 - slot)

        def lay(step, carry):
            spots = [step * 4 + k for k in range(4)]
            for spot in spots:
                frame_copy(group, spot, slot).wait()
            for spot in spots:
                image = held[slot, spot].astype(F32).reshape(336, 84)
                image = jnp.concatenate([image, jnp.zeros((336, 44), F32)], axis=1)
                wide[pl.ds(spot, 336, stride=GROUP), :] = image
            return carry

        lax.fori_loop(0, GROUP // 4, lay, 0)
        for part in range(3):
            rows = wide[part * 1792 : (part + 1) * 1792].reshape(28, 4, GROUP, 128)
            rows = [rows[:, c].reshape(448, 128).astype(BF16) for c in range(4)]
            result = dot(jnp.concatenate(rows, axis=1), choose[...])
            picked[part * 7 : (part + 1) * 7] = result.astype(BF16).reshape(7, 4, GROUP, 640)
        keep_picked = pltpu.make_async_copy(picked, picked_ref.at[group], out_sem.at[0])
        keep_picked.start()
        for q in range(5):
            pieces = [
                picked[j : j + 20, b, :, q * 128 : (q + 1) * 128].reshape(20 * GROUP, 128)
                for j in range(2)
                for b in range(4)
            ]
            z = fold_pair(dot(jnp.concatenate(pieces, axis=1), w_one[...])) + bias_one
            z_one[:, :, q] = z.reshape(10, 2, GROUP, 128)
            high, low = two_parts(gelu_value(z))
            h_one[0, :, :, q] = high.reshape(10, 2, GROUP, 128)
            h_one[1, :, :, q] = low.reshape(10, 2, GROUP, 128)
        keep_one = pltpu.make_async_copy(z_one, z_one_ref.at[group], out_sem.at[1])
        keep_one.start()
        total = jnp.zeros((45 * GROUP, 128), F32)
        for part in range(2):
            pieces = []
            for j in range(2):
                for b in range(2):
                    pieces.append(h_one[part, j : j + 9, b, 0:5].reshape(45 * GROUP, 128))
                    pieces.append(h_one[part, j : j + 9, b, 1:6].reshape(45 * GROUP, 128))
            total = total + fold_pair(dot(jnp.concatenate(pieces, axis=1), w_two[...]))
        z = (total + bias_two).reshape(9, 5, GROUP, 128)
        z_two[...] = z
        h = gelu_value(z)
        high, low = two_parts(h)
        h_two[0] = high
        h_two[1] = low
        edge = jnp.where(last_masks(), h[:, 4].reshape(9 * GROUP, 128), 0.0)
        high, low = two_parts(edge)
        h_two[0, :, 4] = high.reshape(9, GROUP, 128)
        h_two[1, :, 4] = low.reshape(9, GROUP, 128)
        keep_two = pltpu.make_async_copy(z_two, z_two_ref.at[group], out_sem.at[2])
        keep_two.start()
        total = jnp.zeros((28 * GROUP, 128), F32)
        for part in range(2):
            pieces = []
            for ky in range(3):
                pieces.append(h_two[part, ky : ky + 7, 0:4].reshape(28 * GROUP, 128))
                pieces.append(h_two[part, ky : ky + 7, 1:5].reshape(28 * GROUP, 128))
            total = total + fold_pair(dot(jnp.concatenate(pieces, axis=1), w_three[...]))
        z_three[...] = (total + bias_three).reshape(28, GROUP, 128)
        spot = pl.multiple_of(group * GROUP, GROUP)
        keep_three = pltpu.make_async_copy(
            z_three, z_three_ref.at[:, pl.ds(spot, GROUP)], out_sem.at[3]
        )
        keep_three.start()
        keep_picked.wait()
        keep_one.wait()
        keep_two.wait()
        keep_three.wait()
        return carry

    lax.fori_loop(0, groups, one_group, 0)


def conv_forward(lengths, frames, flat):
    most = ROOM // GROUP
    any_spec = pl.BlockSpec(memory_space=pl.ANY)
    hbm = pl.BlockSpec(memory_space=pltpu.HBM)
    return pl.pallas_call(
        conv_forward_kernel,
        in_specs=[
            any_spec,
            any_spec,
            any_spec,
        ],
        out_specs=[hbm] * 4,
        out_shape=[
            jax.ShapeDtypeStruct((most, 21, 4, GROUP, 640), BF16),
            jax.ShapeDtypeStruct((most, 10, 2, 5, GROUP, 128), F32),
            jax.ShapeDtypeStruct((most, 9, 5, GROUP, 128), F32),
            jax.ShapeDtypeStruct((28, ROOM, 128), F32),
        ],
        scratch_shapes=[
            pltpu.VMEM((CONV_ROWS, 128), F32),
            pltpu.VMEM((2, GROUP, 84, 4, 84), BF16),
            pltpu.VMEM((336 * GROUP, 128), F32),
            pltpu.VMEM((21, 4, GROUP, 640), BF16),
            pltpu.VMEM((10, 2, 5, GROUP, 128), F32),
            pltpu.VMEM((9, 5, GROUP, 128), F32),
            pltpu.VMEM((28, GROUP, 128), F32),
            pltpu.VMEM((2, 10, 2, 6, GROUP, 128), BF16),
            pltpu.VMEM((2, 9, 5, GROUP, 128), BF16),
            pltpu.VMEM((1024, 256), BF16),
            pltpu.VMEM((1024, 256), BF16),
            pltpu.VMEM((768, 256), BF16),
            pltpu.VMEM((512, 640), BF16),
            pltpu.VMEM((288, 128), F32),
            pltpu.VMEM((576, 128), F32),
            pltpu.SMEM(lengths.shape, jnp.int32),
            pltpu.SemaphoreType.DMA((2, GROUP)),
            pltpu.SemaphoreType.DMA((6,)),
        ],
        compiler_params=pltpu.CompilerParams(vmem_limit_bytes=62 * 1024 * 1024),
        name="conv_forward",
    )(lengths, frames.transpose(0, 1, 3, 2, 4), flat)


def gather_one(total, out):
    lane = lax.broadcasted_iota(jnp.int32, (32, 128), 1)
    halves = [jnp.zeros((32, 128), F32) for side in range(2)]
    for ky in range(8):
        held = total[0:128, ky * 128 : (ky + 1) * 128] + total[128:256, ky * 128 : (ky + 1) * 128]
        summed = held[0:32]
        for o in range(1, 4):
            summed = summed + pltpu.roll(held[32 * o : 32 * o + 32], 128 - 4 * o, 1)
        for c in range(4):
            spot = (c % 2) * 64 + ky * 8
            shift = (spot - c * 32) % 128
            moved = pltpu.roll(summed, shift, 1) if shift else summed
            inside = (lane >= spot) & (lane < spot + 8)
            halves[c // 2] = halves[c // 2] + jnp.where(inside, moved, 0.0)
    for side in range(2):
        out[pl.ds(side, 32, stride=2), :] = halves[side]


def gather_two(total, turned, rows_ref, out):
    lane = lax.broadcasted_iota(jnp.int32, (64, 128), 1)
    for ky in range(4):
        near = total[0:128, ky * 256 : ky * 256 + 128] + total[128:256, ky * 256 : ky * 256 + 128]
        far = (
            total[0:128, ky * 256 + 128 : ky * 256 + 256]
            + total[128:256, ky * 256 + 128 : ky * 256 + 256]
        )
        summed = near[0:64] + jnp.where(
            lane < 64, pltpu.roll(near[64:128], 64, 1), pltpu.roll(far[64:128], 64, 1)
        )
        flipped = jnp.transpose(jnp.concatenate([summed, jnp.zeros((64, 128), F32)], axis=0))
        for kx in range(4):
            turned[pl.ds(ky * 4 + kx, 32, stride=16), :] = flipped[kx * 32 : (kx + 1) * 32]
    rows_ref[0:8] = jnp.zeros((8, 128), F32)
    rows_ref[264:272] = jnp.zeros((8, 128), F32)
    for j in range(4):
        block = jnp.transpose(turned[j * 128 : (j + 1) * 128])[0:64]
        rows_ref[pl.ds(8 + j, 64, stride=4), :] = block
    own = pltpu.roll(rows_ref[8:265], 32, 1)
    before = pltpu.roll(rows_ref[7:264], 32, 1)
    out[64:321] = jnp.where(lanes() >= 32, own, before)


def gather_three(total, turned, rows_ref, out):
    lane = lax.broadcasted_iota(jnp.int32, (64, 128), 1)
    side = lax.broadcasted_iota(jnp.int32, (32, 128), 1) < 64
    blank = jnp.zeros((64, 128), F32)
    for ky in range(3):
        near = total[0:128, ky * 256 : ky * 256 + 128] + total[128:256, ky * 256 : ky * 256 + 128]
        far = (
            total[0:128, ky * 256 + 128 : ky * 256 + 256]
            + total[128:256, ky * 256 + 128 : ky * 256 + 256]
        )
        first = near[0:64] + jnp.where(
            lane < 64, pltpu.roll(near[64:128], 64, 1), pltpu.roll(far[64:128], 64, 1)
        )
        second = far[0:64] + pltpu.roll(far[64:128], 64, 1)
        flipped = jnp.transpose(jnp.concatenate([first, blank], axis=0))
        turned[pl.ds(ky * 3, 64, stride=9), :] = flipped[0:64]
        turned[pl.ds(ky * 3 + 1, 64, stride=9), :] = flipped[64:128]
        flipped = jnp.transpose(jnp.concatenate([second, blank], axis=0))
        turned[pl.ds(ky * 3 + 2, 64, stride=9), :] = flipped[0:64]
    turned[576:640] = blank
    evens, odds = [], []
    for j in range(5):
        rows_ref[0:64] = jnp.transpose(turned[j * 128 : (j + 1) * 128])[0:64]
        evens.append(rows_ref[pl.ds(0, 32, stride=2), :])
        odds.append(pltpu.roll(rows_ref[pl.ds(1, 32, stride=2), :], 64, 1))
    rows_ref[0:8] = jnp.zeros((8, 128), F32)
    rows_ref[296:304] = jnp.zeros((8, 128), F32)
    for k in range(9):
        if k < 4:
            held = evens[k]
        elif k == 4:
            held = jnp.where(side, evens[4], odds[0])
        else:
            held = jnp.where(side, odds[k - 5], odds[k - 4])
        rows_ref[pl.ds(8 + k, 32, stride=9), :] = held
    own = pltpu.roll(rows_ref[8:297], 96, 1)
    before = pltpu.roll(rows_ref[7:296], 96, 1)
    edge = out[320:321]
    out[320:609] = jnp.where(lanes() >= 96, own, before)
    out[320:321] = out[320:321] + edge


def conv_backward_kernel(
    lengths_from,
    index_from,
    table_ref,
    times_ref,
    picked_ref,
    z_one_ref,
    z_two_ref,
    d_three_ref,
    shared_ref,
    flat_out,
    flag_out,
    flat_ref,
    picked,
    z_one,
    z_two,
    d_three,
    h_one,
    h_two,
    slope_one,
    pad_three,
    pad_two,
    d_one,
    v_two,
    v_three,
    spread,
    rows_ref,
    turned,
    bias_out,
    total_one,
    total_two,
    total_three,
    field,
    lengths_ref,
    index_ref,
    load_sem,
    weight_sem,
):
    for source, target in ((lengths_from, lengths_ref), (index_from, index_ref)):
        scalars = pltpu.make_async_copy(source, target, weight_sem)
        scalars.start()
        scalars.wait()
    used = jnp.int32(0)
    for w in range(lengths_ref.shape[0]):
        used = used + lengths_ref[w]
    groups = lax.div(used + (GROUP - 1), GROUP)

    def loads(group, slot):
        spot = pl.multiple_of(group * GROUP, GROUP)
        return [
            pltpu.make_async_copy(picked_ref.at[group], picked.at[slot], load_sem.at[slot, 0]),
            pltpu.make_async_copy(z_one_ref.at[group], z_one.at[slot], load_sem.at[slot, 1]),
            pltpu.make_async_copy(z_two_ref.at[group], z_two.at[slot], load_sem.at[slot, 2]),
            pltpu.make_async_copy(
                d_three_ref.at[:, pl.ds(spot, GROUP)], d_three.at[slot], load_sem.at[slot, 3]
            ),
        ]

    weights = pltpu.make_async_copy(
        shared_ref.at[pl.ds(0, CONV_ROWS)], flat_ref, weight_sem
    )
    weights.start()
    for load in loads(0, 0):
        load.start()

    def put_two(row, block):
        spread[row : row + 32] = block

    def put_three(row, block):
        spread[row : row + 64] = block

    weights.wait()
    spread_two(flat_ref, rows_ref, turned, put_two)
    for b in range(2):
        for j in range(2):
            for side in range(2):
                source = (2 * j + b) * 256 + side * 128
                target = (b * 2 + j) * 256 + side * 128
                v_two[target : target + 128] = pair(jnp.transpose(spread[source : source + 128]))
    spread_three(flat_ref, rows_ref, turned, put_three)
    for part in range(6):
        rows = pl.ds(part * 128, 128)
        v_three[rows] = pair(jnp.transpose(spread[rows]))
    total_one[...] = jnp.zeros(total_one.shape, F32)
    total_two[...] = jnp.zeros(total_two.shape, F32)
    total_three[...] = jnp.zeros(total_three.shape, F32)
    bias_out[...] = jnp.zeros(bias_out.shape, F32)
    h_one[...] = jnp.zeros(h_one.shape, BF16)
    pad_two[...] = jnp.zeros(pad_two.shape, BF16)
    pad_three[...] = jnp.zeros(pad_three.shape, BF16)

    def fold(rows):
        return jnp.sum(rows.reshape(-1, 8, 128), axis=0)

    def one_group(group, carry):
        slot = lax.rem(group, 2)

        @pl.when(group + 1 < groups)
        def ahead():
            for load in loads(group + 1, 1 - slot):
                load.start()

        for load in loads(group, slot):
            load.wait()
        rows = d_three[slot].reshape(28 * GROUP, 128)
        bias_out[2] += fold(rows)
        both = pair(rows)
        pad_three[0, 2:9, 1:5] = both[:, :128].reshape(7, 4, GROUP, 128)
        pad_three[1, 2:9, 1:5] = both[:, 128:].reshape(7, 4, GROUP, 128)
        h, slope_two = gelu_both(z_two[slot])
        high, low = two_parts(h)
        h_two[0] = high
        h_two[1] = low
        edge = jnp.where(last_masks(), h[:, 4].reshape(9 * GROUP, 128), 0.0)
        high, low = two_parts(edge)
        h_two[0, :, 4] = high.reshape(9, GROUP, 128)
        h_two[1, :, 4] = low.reshape(9, GROUP, 128)
        for part in range(2):
            pieces = []
            for ky in range(3):
                pieces.append(h_two[part, ky : ky + 7, 0:4].reshape(28 * GROUP, 128))
                pieces.append(h_two[part, ky : ky + 7, 1:5].reshape(28 * GROUP, 128))
            total_three[...] += dot_rows(both, jnp.concatenate(pieces, axis=1))
        spill = jnp.zeros((45 * GROUP, 128), F32)
        for part in range(2):
            pieces = []
            for ky in range(3):
                pieces.append(pad_three[part, 2 - ky : 11 - ky, 1:6].reshape(45 * GROUP, 128))
                pieces.append(pad_three[part, 2 - ky : 11 - ky, 0:5].reshape(45 * GROUP, 128))
            spill = spill + fold_pair(dot(jnp.concatenate(pieces, axis=1), v_three[...]))
        rows = spill * slope_two.reshape(45 * GROUP, 128)
        bias_out[1] += fold(rows)
        both = pair(rows)
        pad_two[0, 1:10, 1:6] = both[:, :128].reshape(9, 5, GROUP, 128)
        pad_two[1, 1:10, 1:6] = both[:, 128:].reshape(9, 5, GROUP, 128)
        for q in range(5):
            h, slope = gelu_both(z_one[slot, :, :, q])
            high, low = two_parts(h)
            h_one[0, :, :, q] = high
            h_one[1, :, :, q] = low
            slope_one[:, :, q] = slope
        for part in range(2):
            pieces = []
            for j in range(2):
                for b in range(2):
                    pieces.append(h_one[part, j : j + 9, b, 0:5].reshape(45 * GROUP, 128))
                    pieces.append(h_one[part, j : j + 9, b, 1:6].reshape(45 * GROUP, 128))
            total_two[...] += dot_rows(both, jnp.concatenate(pieces, axis=1))
        for b in range(2):
            spill = jnp.zeros((50 * GROUP, 128), F32)
            for part in range(2):
                pieces = []
                for j in range(2):
                    pieces.append(pad_two[part, 1 - j : 11 - j, 1:6].reshape(50 * GROUP, 128))
                    pieces.append(pad_two[part, 1 - j : 11 - j, 0:5].reshape(50 * GROUP, 128))
                spill = spill + fold_pair(
                    dot(jnp.concatenate(pieces, axis=1), v_two[b * 512 : (b + 1) * 512])
                )
            rows = spill * slope_one[:, b].reshape(50 * GROUP, 128)
            bias_out[0] += fold(rows)
            d_one[:, b] = pair(rows).reshape(10, 5, GROUP, 256)
        for q in range(5):
            pieces = [
                picked[slot, j : j + 20, b, :, q * 128 : (q + 1) * 128].reshape(20 * GROUP, 128)
                for j in range(2)
                for b in range(4)
            ]
            total_one[...] += dot_rows(
                d_one[:, :, q].reshape(20 * GROUP, 256), jnp.concatenate(pieces, axis=1)
            )
        return carry

    lax.fori_loop(0, groups, one_group, 0)
    gather_one(total_one, flat_out)
    gather_two(total_two, turned, rows_ref, flat_out)
    gather_three(total_three, turned, rows_ref, flat_out)
    lane = lanes()
    sums = [jnp.sum(bias_out[k], axis=0, keepdims=True) for k in range(3)]
    sums[0] = sums[0] + pltpu.roll(sums[0], 64, 1)
    sums[0] = sums[0] + pltpu.roll(sums[0], 32, 1)
    sums[1] = jnp.where(lane < 64, sums[1] + pltpu.roll(sums[1], 64, 1), 0.0)
    sums[2] = jnp.where(lane < 64, sums[2] + pltpu.roll(sums[2], 64, 1), 0.0)
    flat_out[64:65] = jnp.where(lane < 32, sums[0], flat_out[64:65])
    flat_out[320:321] = flat_out[320:321] + pltpu.roll(sums[1], 32, 1)
    late = pltpu.roll(sums[2], 96, 1)
    flat_out[608:609] = flat_out[608:609] + jnp.where(lane >= 96, late, 0.0)
    row = lax.broadcasted_iota(jnp.int32, (7, 128), 0)
    flat_out[609:616] = jnp.where((row == 0) & (lane < 32), late, 0.0)
    wins = lengths_ref.shape[0]
    shape = table_ref.shape
    row = lax.broadcasted_iota(jnp.int32, shape, 0)
    lane = lax.broadcasted_iota(jnp.int32, shape, 1)
    counts = jnp.where(jnp.bitwise_and(lane, 2 * wins - 1) < wins, table_ref[...], 0.0)
    ahead = (row < index_ref[2]) | ((row == index_ref[2]) & (lane < index_ref[0] * (2 * wins)))
    before = jnp.sum(jnp.where(ahead, counts, 0.0)).astype(jnp.int32)
    flag_out[0] = jnp.sum(counts).astype(jnp.int32)
    field[...] = jnp.zeros(field.shape, F32)
    field[pl.ds(jnp.minimum(before, FAST_ROWS), ROOM)] = times_ref[...]
    flat_out[CONV_ROWS : CONV_ROWS + FAST_ROWS] = field[0:FAST_ROWS]


def conv_backward(lengths, index, table, times, picked, z_one, z_two, d_three, flat):
    hbm = pl.BlockSpec(memory_space=pltpu.HBM)
    vmem = pl.BlockSpec(memory_space=pltpu.VMEM)
    return pl.pallas_call(
        conv_backward_kernel,
        in_specs=[hbm] * 2 + [vmem] * 2 + [hbm] * 5,
        out_specs=[vmem, pl.BlockSpec(memory_space=pltpu.SMEM)],
        out_shape=[
            jax.ShapeDtypeStruct((CONV_ROWS + FAST_ROWS, 128), F32),
            jax.ShapeDtypeStruct((1,), jnp.int32),
        ],
        scratch_shapes=[
            pltpu.VMEM((CONV_ROWS, 128), F32),
            pltpu.VMEM((2, 21, 4, GROUP, 640), BF16),
            pltpu.VMEM((2, 10, 2, 5, GROUP, 128), F32),
            pltpu.VMEM((2, 9, 5, GROUP, 128), F32),
            pltpu.VMEM((2, 28, GROUP, 128), F32),
            pltpu.VMEM((2, 10, 2, 6, GROUP, 128), BF16),
            pltpu.VMEM((2, 9, 5, GROUP, 128), BF16),
            pltpu.VMEM((10, 2, 5, GROUP, 128), F32),
            pltpu.VMEM((2, 11, 6, GROUP, 128), BF16),
            pltpu.VMEM((2, 11, 6, GROUP, 128), BF16),
            pltpu.VMEM((10, 2, 5, GROUP, 256), BF16),
            pltpu.VMEM((1024, 256), BF16),
            pltpu.VMEM((768, 256), BF16),
            pltpu.VMEM((1024, 128), F32),
            pltpu.VMEM((304, 128), F32),
            pltpu.VMEM((640, 128), F32),
            pltpu.VMEM((3, 8, 128), F32),
            pltpu.VMEM((256, 1024), F32),
            pltpu.VMEM((256, 1024), F32),
            pltpu.VMEM((256, 768), F32),
            pltpu.VMEM((FAST_ROWS + ROOM, 128), F32),
            pltpu.SMEM(lengths.shape, jnp.int32),
            pltpu.SMEM((3,), jnp.int32),
            pltpu.SemaphoreType.DMA((2, 4)),
            pltpu.SemaphoreType.DMA,
        ],
        compiler_params=pltpu.CompilerParams(vmem_limit_bytes=62 * 1024 * 1024),
        name="conv_backward",
    )(lengths, index, table, times, picked, z_one, z_two, d_three, flat)


HIGH = lax.Precision.HIGH
VECTORS_ROW = 3745
TIME_ROW = 3780


def mm(a, b):
    return lax.dot_general(
        a, b, (((1,), (0,)), ((), ())), precision=HIGH, preferred_element_type=F32
    )


def mm_nt(a, b):
    return lax.dot_general(
        a, b, (((1,), (1,)), ((), ())), precision=HIGH, preferred_element_type=F32
    )


def mm_tn(a, b):
    return lax.dot_general(
        a, b, (((0,), (0,)), ((), ())), precision=HIGH, preferred_element_type=F32
    )


def dot_nt(a, b):
    return lax.dot_general(a, b, (((1,), (1,)), ((), ())), preferred_element_type=F32)


def norm_parts(stream):
    centered = stream - jnp.mean(stream, -1, keepdims=True)
    spread = jnp.mean(centered * centered, -1, keepdims=True)
    scale = lax.rsqrt(spread + 1e-05)
    return centered * scale, scale


def norm_back(grad, unit, scale, gain):
    grad = grad * gain
    inner = jnp.mean(grad * unit, -1, keepdims=True)
    return scale * (grad - jnp.mean(grad, -1, keepdims=True) - unit * inner)


def column_sum(x):
    return jnp.sum(x, axis=0, keepdims=True)


def head_places():
    number = lax.broadcasted_iota(jnp.int32, (128, 128), 0) * ACT
    lane = lax.broadcasted_iota(jnp.int32, (128, 128), 1)
    row = lax.shift_right_logical(number, 7)
    return row + jnp.where(lane < jnp.bitwise_and(number, 127), 1, 0)


def roll_rows(held, sign):
    number = lax.broadcasted_iota(jnp.int32, (128, 128), 0) * ACT
    for k in range(7):
        moved = pltpu.roll(held, (sign * (1 << k)) % 128, 1)
        held = jnp.where(jnp.bitwise_and(number, 1 << k) > 0, moved, held)
    return held


def square_head(rows):
    place = head_places()
    held = jnp.zeros((128, 128), F32)
    for k in range(ACT):
        held = jnp.where(place == k, rows[k : k + 1], held)
    held = roll_rows(held, -1)
    lane = lax.broadcasted_iota(jnp.int32, (128, 128), 1)
    return jnp.where(lane < ACT, held, 0.0)


def flat_head(grads):
    place = head_places()
    lane = lax.broadcasted_iota(jnp.int32, (128, 128), 1)
    held = roll_rows(jnp.where(lane < ACT, grads, 0.0), 1)
    rows = [
        jnp.sum(jnp.where(place == k, held, 0.0), axis=0, keepdims=True) for k in range(ACT)
    ]
    return jnp.concatenate(rows + [jnp.zeros((24 - ACT, 128), F32)], axis=0)


def unpack_split(split_ref, qkv, output, up, up_bias, down):
    lane = lax.broadcasted_iota(jnp.int32, (32, 128), 1)
    for layer in range(LAYERS):
        base = layer * 385
        kinds = [[jnp.zeros((32, 128), F32) for j in range(4)] for kind in range(3)]
        for m in range(4):
            rows = [split_ref[m, pl.ds(base + k, 32, stride=3), :] for k in range(3)]
            inside = (lane >= 32 * m) & (lane < 32 * m + 32)
            for j in range(4):
                for kind in range(3):
                    spot = j * 96 + kind * 32
                    source = rows[spot // 128]
                    shift = (32 * m - spot % 128) % 128
                    moved = pltpu.roll(source, shift, 1) if shift else source
                    kinds[kind][j] = jnp.where(inside, moved, kinds[kind][j])
            output[layer, 32 * m : 32 * m + 32] = split_ref[m, base + 96 : base + 128]
            up[layer, :, 128 * m : 128 * m + 128] = split_ref[m, base + 128 : base + 256]
            up_bias[layer, :, 128 * m : 128 * m + 128] = split_ref[m, base + 256 : base + 257]
            down[layer, 128 * m : 128 * m + 128] = split_ref[m, base + 257 : base + 385]
        for kind in range(3):
            for j in range(4):
                qkv[layer, kind, pl.ds(j, 32, stride=4), :] = kinds[kind][j]


def pack_split(out_ref, qkv, output, up, up_bias, down):
    lane = lax.broadcasted_iota(jnp.int32, (32, 128), 1)
    for layer in range(LAYERS):
        base = layer * 385
        parts = [[qkv[layer, kind, pl.ds(j, 32, stride=4), :] for j in range(4)] for kind in range(3)]
        for m in range(4):
            rows = [jnp.zeros((32, 128), F32) for k in range(3)]
            for j in range(4):
                for kind in range(3):
                    spot = j * 96 + kind * 32
                    low = spot % 128
                    shift = (low - 32 * m) % 128
                    moved = pltpu.roll(parts[kind][j], shift, 1) if shift else parts[kind][j]
                    inside = (lane >= low) & (lane < low + 32)
                    rows[spot // 128] = jnp.where(inside, moved, rows[spot // 128])
            for k in range(3):
                out_ref[m, pl.ds(base + k, 32, stride=3), :] = rows[k]
            out_ref[m, base + 96 : base + 128] = output[layer, 32 * m : 32 * m + 32]
            out_ref[m, base + 128 : base + 256] = up[layer, :, 128 * m : 128 * m + 128]
            out_ref[m, base + 256 : base + 257] = up_bias[layer, :, 128 * m : 128 * m + 128]
            out_ref[m, base + 257 : base + 385] = down[layer, 128 * m : 128 * m + 128]
    for m in range(4):
        out_ref[m, 770:784] = jnp.zeros((14, 128), F32)


def former_body(
    slots,
    used,
    lengths_ref,
    returns_ref,
    actions_ref,
    head_ref,
    z_ref,
    small,
    times_all,
    encoder,
    weights,
    d_three_ref,
    d_encoder_ref,
    d_small_ref,
    d_times_ref,
    grads,
    chances,
    kept,
    sums,
    flats,
):
    qkv, output, up, up_bias, down = weights
    d_qkv, d_output, d_up, d_up_bias, d_down = grads
    rows = 3 * slots
    wins, steps = returns_ref.shape
    vec = [small[k : k + 1] for k in range(17)]
    table = small[17 : 17 + ACT]
    slot = lax.broadcasted_iota(jnp.int32, (slots, 1), 0)
    window = jnp.zeros((slots, 1), jnp.int32)
    begin = jnp.zeros((slots, 1), jnp.int32)
    end = jnp.int32(0)
    for w in range(wins - 1):
        end = end + lengths_ref[w]
        window = jnp.where(slot >= end, w + 1, window)
        begin = jnp.where(slot >= end, end, begin)
    moment = slot - begin
    valid = slot < used
    time_lane = lax.broadcasted_iota(jnp.int32, (slots, steps), 1)
    amount = jnp.zeros((slots, 1), F32)
    action = jnp.zeros((slots, 1), jnp.int32)
    for w in range(wins):
        here = (time_lane == moment) & (window == w)
        amount = amount + jnp.sum(
            jnp.where(here, returns_ref[w : w + 1], 0.0), axis=1, keepdims=True
        )
        action = action + jnp.sum(jnp.where(here, actions_ref[w : w + 1], 0), axis=1, keepdims=True)
    lane = lax.broadcasted_iota(jnp.int32, (slots, 128), 1)
    picks = jnp.where((lane == action) & valid, 1.0, 0.0)
    reward = jnp.tanh(amount * vec[14] + vec[15])
    table = jnp.concatenate([table, jnp.zeros((128 - ACT, 128), F32)], axis=0)
    move = jnp.tanh(mm(picks, table))
    sum_state = jnp.zeros((slots, 128), F32)
    for k in range(28):
        z = jnp.where(valid, z_ref[k, 0:slots], 0.0)
        high, low = two_parts(gelu_value(z))
        flats[0, 0:slots, k * 128 : (k + 1) * 128] = high
        flats[1, 0:slots, k * 128 : (k + 1) * 128] = low
    for part in range(2):
        sum_state = sum_state + fold_pair(dot(flats[part, 0:slots], encoder[...]))
    state = jnp.tanh(sum_state + vec[16])
    times = times_all[0:slots]
    stream = jnp.concatenate([reward + times, state + times, move + times], axis=0)

    def ids(axis):
        shape = (rows, 1) if axis == 0 else (1, rows)
        number = lax.broadcasted_iota(jnp.int32, shape, axis)
        kind = jnp.where(number >= 2 * slots, 2, jnp.where(number >= slots, 1, 0))
        return number - kind * slots, kind

    (slot_q, kind_q), (slot_k, kind_k) = ids(0), ids(1)

    def begin_of(slot_ids):
        found = jnp.zeros(slot_ids.shape, jnp.int32)
        end = jnp.int32(0)
        for w in range(wins - 1):
            end = end + lengths_ref[w]
            found = jnp.where(slot_ids >= end, end, found)
        return found

    order_q = slot_q * 3 + kind_q
    order_k = slot_k * 3 + kind_k
    allowed = (order_q >= order_k) & (slot_k >= begin_of(slot_q)) & (slot_k < used)
    head_of = lax.shift_right_logical(lax.broadcasted_iota(jnp.int32, (1, 128), 1), 4)
    heads = D // HD
    batch = 4 if slots <= HALF else 2

    def masked(x, masks):
        return jnp.concatenate([jnp.where(mask, x, jnp.zeros_like(x)) for mask in masks], axis=0)

    def unmasked(x, masks):
        held = jnp.where(masks[0], x[0:rows], 0.0)
        for k in range(1, batch):
            held = held + jnp.where(masks[k], x[k * rows : (k + 1) * rows], 0.0)
        return held

    tape = []
    for layer in range(LAYERS):
        gains = vec[6 * layer : 6 * layer + 6]
        unit_one, scale_one = norm_parts(stream)
        normed = unit_one * gains[0] + gains[1]
        wide = jnp.concatenate([qkv[layer, k] for k in range(3)], axis=1)
        mixed = mm(normed, wide)
        query_high, query_low = two_parts(mixed[:, :128] * 0.25)
        keys, values = pair(mixed[:, 128:256]), pair(mixed[:, 256:])
        kept[layer, 0, 0:rows] = query_high
        kept[layer, 1, 0:rows] = query_low
        for k in range(2):
            kept[layer, 2 + k, 0:rows] = keys[:, k * 128 : (k + 1) * 128]
            kept[layer, 4 + k, 0:rows] = values[:, k * 128 : (k + 1) * 128]
        sums[0, 0:rows] = jnp.zeros((rows, 128), F32)

        def attend(turn, carry, layer=layer):
            masks = [head_of == turn * batch + k for k in range(batch)]
            parts = [masked(kept[layer, k, 0:rows], masks) for k in range(2)]
            keys = [kept[layer, 2 + k, 0:rows] for k in range(2)]
            values = [kept[layer, 4 + k, 0:rows] for k in range(2)]
            scores = dot_nt(
                jnp.concatenate([parts[0], parts[0]], axis=1), jnp.concatenate(keys, axis=1)
            )
            scores = (scores + dot_nt(parts[1], keys[0])).reshape(batch, rows, rows)
            scores = jnp.where(allowed[None], scores, -1e30)
            peak = jnp.max(scores, -1, keepdims=True)
            chance = jnp.exp(scores - peak)
            chance = chance / jnp.sum(chance, -1, keepdims=True)
            high, low = two_parts(chance.reshape(batch * rows, rows))
            spot = pl.ds(pl.multiple_of(turn * (batch * rows), 64), batch * rows)
            chances[layer, 0, spot, 0:rows] = high
            chances[layer, 1, spot, 0:rows] = low
            seen = fold_pair(dot(high, jnp.concatenate(values, axis=1))) + dot(low, values[0])
            sums[0, 0:rows] += unmasked(seen, masks)
            return carry

        lax.fori_loop(0, heads // batch, attend, 0)
        context = sums[0, 0:rows]
        stream = stream + mm(context, output[layer]) + gains[4]
        unit_two, scale_two = norm_parts(stream)
        normed_two = unit_two * gains[2] + gains[3]
        inner, slope = gelu_both(mm(normed_two, up[layer]) + up_bias[layer])
        stream = stream + mm(inner, down[layer]) + gains[5]
        tape.append((unit_one, scale_one, unit_two, scale_two, inner, slope, context))
    end_stream = stream[slots : 2 * slots]
    unit, scale = norm_parts(end_stream)
    final = unit * vec[12] + vec[13]
    logits = jnp.where(lane < ACT, mm(final, head_ref[...]), -1e30)
    peak = jnp.max(logits, -1, keepdims=True)
    powers = jnp.exp(logits - peak)
    total = jnp.sum(powers, -1, keepdims=True)
    chosen = jnp.sum(jnp.where(lane == action, logits, 0.0), -1, keepdims=True)
    terms = jnp.where(valid, jnp.log(total) + peak - chosen, 0.0)
    loss = jnp.sum(terms, axis=0, keepdims=True)
    d_small_ref[72:80] = jnp.broadcast_to(loss, (8, 128))
    d_logits = jnp.where(valid, powers / total, 0.0) - picks
    d_small_ref[48:72] = flat_head(mm_tn(final, d_logits))
    d_final = mm_nt(d_logits, head_ref[...])
    d_vec = [None] * 17
    d_vec[12] = column_sum(d_final * unit)
    d_vec[13] = column_sum(d_final)
    d_end = norm_back(d_final, unit, scale, vec[12])
    blank = jnp.zeros((slots, 128), F32)
    d_stream = jnp.concatenate([blank, d_end, blank], axis=0)
    for layer in reversed(range(LAYERS)):
        unit_one, scale_one, unit_two, scale_two, inner, slope, context = tape[layer]
        gains = vec[6 * layer : 6 * layer + 6]
        d_vec[6 * layer + 5] = column_sum(d_stream)
        d_down[layer] = mm_tn(inner, d_stream)
        d_inner = mm_nt(d_stream, down[layer]) * slope
        d_up_bias[layer] = column_sum(d_inner)
        normed_two = unit_two * gains[2] + gains[3]
        d_up[layer] = mm_tn(normed_two, d_inner)
        d_normed = mm_nt(d_inner, up[layer])
        d_vec[6 * layer + 2] = column_sum(d_normed * unit_two)
        d_vec[6 * layer + 3] = column_sum(d_normed)
        d_stream = d_stream + norm_back(d_normed, unit_two, scale_two, gains[2])
        d_vec[6 * layer + 4] = column_sum(d_stream)
        d_output[layer] = mm_tn(context, d_stream)
        d_context = mm_nt(d_stream, output[layer])
        bases = d_context * context
        high, low = two_parts(d_context)
        for k in range(3):
            sums[k, 0:rows] = jnp.zeros((rows, 128), F32)
        kept[layer, 6, 0:rows] = high
        kept[layer, 7, 0:rows] = low
        sums[3, 0:rows] = bases

        def attend_back(turn, carry, layer=layer):
            masks = [head_of == turn * batch + k for k in range(batch)]
            query = [masked(kept[layer, k, 0:rows], masks) for k in range(2)]
            keys = [kept[layer, 2 + k, 0:rows] for k in range(2)]
            values = [kept[layer, 4 + k, 0:rows] for k in range(2)]
            d_seen = [masked(kept[layer, 6 + k, 0:rows], masks) for k in range(2)]
            base = jnp.sum(masked(sums[3, 0:rows], masks), -1, keepdims=True)
            spot = pl.ds(pl.multiple_of(turn * (batch * rows), 64), batch * rows)
            chance = [chances[layer, k, spot, 0:rows] for k in range(2)]
            d_chance = dot_nt(
                jnp.concatenate([d_seen[0], d_seen[0]], axis=1), jnp.concatenate(values, axis=1)
            )
            d_chance = d_chance + dot_nt(d_seen[1], values[0])
            d_scores = (chance[0].astype(F32) + chance[1].astype(F32)) * (d_chance - base)
            high, low = two_parts(d_scores)
            d_query = fold_pair(dot(high, jnp.concatenate(keys, axis=1))) + dot(low, keys[0])
            sums[0, 0:rows] += unmasked(d_query, masks)
            d_keys = fold_pair(dot_rows(high, jnp.concatenate(query, axis=1)))
            sums[1, 0:rows] += d_keys + dot_rows(low, query[0])
            d_values = fold_pair(dot_rows(chance[0], jnp.concatenate(d_seen, axis=1)))
            sums[2, 0:rows] += d_values + dot_rows(chance[1], d_seen[0])
            return carry

        lax.fori_loop(0, heads // batch, attend_back, 0)
        normed = unit_one * gains[0] + gains[1]
        d_mixed = jnp.concatenate(
            [sums[0, 0:rows] * 0.25, sums[1, 0:rows], sums[2, 0:rows]], axis=1
        )
        wide = jnp.concatenate([qkv[layer, k] for k in range(3)], axis=1)
        d_wide = mm_tn(normed, d_mixed)
        for k in range(3):
            d_qkv[layer, k] = d_wide[:, k * 128 : (k + 1) * 128]
        d_normed = mm_nt(d_mixed, wide)
        d_vec[6 * layer] = column_sum(d_normed * unit_one)
        d_vec[6 * layer + 1] = column_sum(d_normed)
        d_stream = d_stream + norm_back(d_normed, unit_one, scale_one, gains[0])
    d_reward, d_state, d_move = (d_stream[k * slots : (k + 1) * slots] for k in range(3))
    d_times_ref[0:slots] = jnp.where(valid, d_reward + d_state + d_move, 0.0)
    d_reward = d_reward * (1.0 - reward * reward)
    d_vec[14] = column_sum(d_reward * amount)
    d_vec[15] = column_sum(d_reward)
    d_move = d_move * (1.0 - move * move)
    d_small_ref[24:48] = mm_tn(picks, d_move)[0:24]
    d_state = jnp.where(valid, d_state * (1.0 - state * state), 0.0)
    d_vec[16] = column_sum(d_state)
    d_small_ref[0:24] = jnp.concatenate(d_vec + [jnp.zeros((7, 128), F32)], axis=0)
    high, low = two_parts(d_state)
    twice = jnp.concatenate([high, high], axis=1)
    both = jnp.concatenate([high, low], axis=1)
    d_flat = dot_nt(twice, encoder[...]) + dot_nt(low, encoder[:, 0:128])
    d_block = dot_rows(flats[0, 0:slots], both) + dot_rows(flats[1, 0:slots], both)
    d_block = fold_pair(d_block)
    for k in range(28):
        z = jnp.where(valid, z_ref[k, 0:slots], 0.0)
        d_three_ref[k, 0:slots] = d_flat[:, k * 128 : (k + 1) * 128] * gelu_both(z)[1]
        y, v = divmod(k, 4)
        for o in range(2):
            if 2 * v + o < 7:
                d_encoder_ref[pl.ds(y * 7 + 2 * v + o, 64, stride=49), :] = d_block[
                    k * 128 + o * 64 : k * 128 + (o + 1) * 64
                ]


def former_kernel(
    packed,
    lengths_from,
    starts_from,
    index_from,
    returns_ref,
    actions_ref,
    z_from,
    flat_ref,
    *refs,
):
    if packed:
        split_ref, refs = refs[0], refs[1:]
    else:
        given, refs = refs[:5], refs[5:]
    (d_three_to, rows_ref), refs = refs[:2], refs[2:]
    if packed:
        parts, refs = refs[:8], refs[8:]
        (d_encoder_ref, d_small_ref, d_split), refs = refs[:3], refs[3:]
        weights, grads, refs = refs[:5], refs[5:10], refs[10:]
    else:
        (d_encoder_ref, d_small_ref), grads, refs = refs[:2], refs[2:7], refs[7:]
        weights = given
    (raw, near, small, rows_raw, times_all, encoder, chances, kept, sums, flats), refs = (
        refs[:10],
        refs[10:],
    )
    z_ref, d_three_ref, head_ref, lengths_ref, starts_ref, index_ref, sem = refs
    used = jnp.int32(0)
    wins = lengths_ref.shape[0]
    scalars = [
        pltpu.make_async_copy(source, target, sem.at[wins + 4 + number])
        for number, (source, target) in enumerate(
            ((lengths_from, lengths_ref), (starts_from, starts_ref), (index_from, index_ref))
        )
    ]
    for copy in scalars:
        copy.start()
    for copy in scalars:
        copy.wait()
    for w in range(wins):
        used = used + lengths_ref[w]

    def z_copy(slots):
        return pltpu.make_async_copy(
            z_from.at[:, pl.ds(0, slots)], z_ref.at[:, pl.ds(0, slots)], sem.at[wins + 3]
        )

    def z_back(slots):
        return pltpu.make_async_copy(
            d_three_ref.at[:, pl.ds(0, slots)], d_three_to.at[:, pl.ds(0, slots)], sem.at[wins + 3]
        )

    copies = [
        pltpu.make_async_copy(flat_ref.at[pl.ds(608, 3144)], raw, sem.at[0]),
        pltpu.make_async_copy(flat_ref.at[pl.ds(3744, 48)], rows_raw.at[wins], sem.at[1]),
        pltpu.make_async_copy(
            flat_ref.at[pl.ds(7872, 24)], rows_raw.at[wins + 1, pl.ds(0, 24)], sem.at[2]
        ),
    ]
    offsets = []
    for w in range(wins):
        row = TIME_ROW + starts_ref[w]
        low = pl.multiple_of(lax.div(row, 8) * 8, 8)
        offsets.append(row - low)
        copies.append(
            pltpu.make_async_copy(
                flat_ref.at[pl.ds(low, 40)], rows_raw.at[w, pl.ds(0, 40)], sem.at[3 + w]
            )
        )
    for copy in copies:
        copy.start()

    @pl.when(used <= HALF)
    def few_states():
        z_copy(HALF).start()

    @pl.when(used > HALF)
    def many_states():
        z_copy(ROOM).start()

    if packed:
        unpack_split(split_ref, *weights)
    for copy in copies:
        copy.wait()
    lane = lanes()

    def straight(first, second):
        return jnp.where(lane < 96, pltpu.roll(first, 96, 1), pltpu.roll(second, 96, 1))

    def turn(step, carry):
        spot = pl.multiple_of(step * 64, 64)
        near[pl.ds(spot, 64)] = straight(raw[pl.ds(spot + 1, 64)], raw[pl.ds(spot + 2, 64)])
        return carry

    lax.fori_loop(0, 49, turn, 0)
    for k in range(28):
        y, v = divmod(k, 4)
        halves = []
        for o in range(2):
            if 2 * v + o < 7:
                halves.append(near[pl.ds(y * 7 + 2 * v + o, 64, stride=49), :])
            else:
                halves.append(jnp.zeros((64, 128), F32))
        encoder[k * 128 : (k + 1) * 128] = pair(jnp.concatenate(halves, axis=0))
    small[...] = straight(rows_raw[wins, 1:41], rows_raw[wins, 2:42])
    head_ref[...] = square_head(
        straight(rows_raw[wins + 1, 4:22], rows_raw[wins + 1, 5:23])
    )
    times_all[...] = jnp.zeros(times_all.shape, F32)
    begin = 0
    row = lax.broadcasted_iota(jnp.int32, (32, 1), 0)
    for w in range(wins):
        rows = straight(
            rows_raw[w, pl.ds(offsets[w], 32)], rows_raw[w, pl.ds(offsets[w] + 1, 32)]
        )
        times_all[pl.ds(begin, 32)] = jnp.where(row < lengths_ref[w], rows, 0.0)
        begin = begin + lengths_ref[w]
    rows_ref[...] = jnp.zeros(rows_ref.shape, F32)
    d_small_ref[...] = jnp.zeros(d_small_ref.shape, F32)

    def run(slots):
        z_copy(slots).wait()
        former_body(
            slots,
            used,
            lengths_ref,
            returns_ref,
            actions_ref,
            head_ref,
            z_ref,
            small,
            times_all,
            encoder,
            weights,
            d_three_ref,
            d_encoder_ref,
            d_small_ref,
            rows_ref,
            grads,
            chances,
            kept,
            sums,
            flats,
        )
        z_back(slots).start()

    @pl.when(used <= HALF)
    def few():
        run(HALF)

    @pl.when(used > HALF)
    def many():
        run(ROOM)

    if packed:
        count = d_small_ref.shape[0] // 4
        pack_split(d_split, *grads)
        for k in range(4):
            parts[k][...] = d_split[jnp.bitwise_xor(index_ref[0], k)]
            e = jnp.bitwise_xor(index_ref[1], k)
            held = d_encoder_ref[pl.ds(pl.multiple_of(e * 784, 8), 784)]
            parts[4 + k][0:784] = held
            held = d_small_ref[pl.ds(pl.multiple_of(e * count, 8), count)]
            parts[4 + k][784 : 784 + count] = held

    @pl.when(used <= HALF)
    def few_end():
        z_back(HALF).wait()

    @pl.when(used > HALF)
    def many_end():
        z_back(ROOM).wait()


def former(lengths, starts, index, returns, actions, z_three, flat, weights, small_rows, packed):
    vmem = pl.BlockSpec(memory_space=pltpu.VMEM)
    hbm = pl.BlockSpec(memory_space=pltpu.HBM)
    wins = lengths.shape[0]
    canonical = [
        (LAYERS, 3, 128, 128),
        (LAYERS, 128, 128),
        (LAYERS, 128, FF),
        (LAYERS, 1, FF),
        (LAYERS, FF, 128),
    ]
    outs, out_specs = [(28, ROOM, 128), (ROOM, 128)], [hbm, vmem]
    if packed:
        outs += [(784, 128)] * 4 + [(784 + small_rows // 4, 128)] * 4
        out_specs += [vmem] * 8
        scratch = [
            pltpu.VMEM((3136, 128), F32),
            pltpu.VMEM((small_rows, 128), F32),
            pltpu.VMEM((4, 784, 128), F32),
        ]
        scratch += [pltpu.VMEM(shape, F32) for shape in canonical] * 2
    else:
        outs += [(3136, 128), (small_rows, 128)] + canonical
        out_specs += [vmem] * 7
        scratch = []
    rows = 3 * ROOM
    scratch += [
        pltpu.VMEM((3144, 128), F32),
        pltpu.VMEM((3136, 128), F32),
        pltpu.VMEM((40, 128), F32),
        pltpu.VMEM((wins + 2, 48, 128), F32),
        pltpu.VMEM((ROOM + 32, 128), F32),
        pltpu.VMEM((3584, 256), BF16),
        pltpu.VMEM((LAYERS, 2, 8 * rows, rows), BF16),
        pltpu.VMEM((LAYERS, 8, rows, 128), BF16),
        pltpu.VMEM((4, rows, 128), F32),
        pltpu.VMEM((2, ROOM, 3584), BF16),
        pltpu.VMEM((28, ROOM, 128), F32),
        pltpu.VMEM((28, ROOM, 128), F32),
        pltpu.VMEM((128, 128), F32),
        pltpu.SMEM((wins,), jnp.int32),
        pltpu.SMEM((wins,), jnp.int32),
        pltpu.SMEM((3,), jnp.int32),
        pltpu.SemaphoreType.DMA((wins + 7,)),
    ]
    return pl.pallas_call(
        partial(former_kernel, packed),
        in_specs=[hbm] * 3 + [vmem] * 2 + [hbm] * 2 + [vmem] * len(weights),
        out_specs=out_specs,
        out_shape=[jax.ShapeDtypeStruct(shape, F32) for shape in outs],
        scratch_shapes=scratch,
        compiler_params=pltpu.CompilerParams(vmem_limit_bytes=62 * 1024 * 1024),
        name="transformer_step",
    )(lengths, starts, index, returns, actions, z_three, flat, *weights)


SMALL = [("vectors", 24), ("action_table", 24), ("head", 24), ("loss", 8)]
FIELD_ROWS = 8200
EARLY_ROWS = CONV_ROWS + 3136
TABLE_AT = CONV_ROWS + 3136 + 17 + ACT


def round_up(number, grain):
    return -(-number // grain) * grain


def chunk_of(tiles):
    return max(size for size in range(1, 9) if tiles % size == 0)


def mesh_bits(dp_size, mp_size):
    dp_bits = [("dp", k) for k in range(dp_size.bit_length() - 1)]
    mp_bits = [("mp", k) for k in range(mp_size.bit_length() - 1)]
    middle = (len(dp_bits) - 1) // 2
    return mp_bits[:1], mp_bits[1:], dp_bits[:middle], dp_bits[middle:]


def reduce_kernel(plan, *refs):
    mp_size, quarter, share = plan["mp_size"], plan["quarter"], plan["share"]
    split_parts, own_parts, conv_ref = refs[:mp_size], refs[mp_size : 2 * mp_size], refs[2 * mp_size]
    refs = refs[2 * mp_size + 1 :]
    (early_out, times_out, small_out, split_out, square_out), refs = refs[:5], refs[5:]
    (split_stage, own_stage, work, landing, split_total, own_total, conv_total), refs = (
        refs[:7],
        refs[7:],
    )
    tiles, tile_in, load_sem, send_sem, recv_sem, store_sem = refs
    spots = {"dp": lax.axis_index("dp"), "mp": lax.axis_index("mp")}
    cores, ys, xs, zs = plan["bits"]
    slots = iter(range(plan["copies"]))

    def value(bit):
        return lax.rem(lax.div(spots[bit[0]], 1 << bit[1]), 2)

    def turned(stage, mask):
        index = 0
        for k, bit in enumerate(stage):
            own = value(bit)
            index = index + ((1 - own) if mask & (1 << k) else own) * (1 << k)
        return index

    def partner(stage, mask):
        place = dict(spots)
        for k, bit in enumerate(stage):
            if mask & (1 << k):
                place[bit[0]] = place[bit[0]] + (1 - 2 * value(bit)) * (1 << bit[1])
        return (place["dp"], place["mp"])

    def masks_of(stage):
        return range(1, 1 << len(stage))

    def send(source, target, stage, mask):
        slot = next(slots)
        copy = pltpu.make_async_remote_copy(
            src_ref=source,
            dst_ref=target,
            send_sem=send_sem.at[slot],
            recv_sem=recv_sem.at[slot],
            device_id=partner(stage, mask),
            device_id_type=pl.DeviceIdType.MESH,
        )
        copy.start()
        return copy

    loads = []
    for k in range(mp_size):
        for parts, stage in ((own_parts, own_stage), (split_parts, split_stage)):
            copy = pltpu.make_async_copy(parts[k], stage.at[k], load_sem.at[len(loads)])
            loads.append(copy)
    conv_tiles, time_tiles = CONV_ROWS // 8, FAST_ROWS // 8
    target = work.at[pl.ds(plan["conv"], conv_tiles + time_tiles)]
    loads.append(pltpu.make_async_copy(conv_ref, target, load_sem.at[len(loads)]))
    for load in loads:
        load.start()

    def wipe(target, start, count):
        if count > 0:
            target[start : start + count] = jnp.zeros((count, 8, 128), F32)

    filled = conv_tiles + time_tiles
    wipe(work, plan["conv"] + filled, plan["conv_size"] - filled)
    wipe(work, plan["split"] + quarter, plan["split_size"] - quarter)
    wipe(work, plan["own"] + quarter + share, plan["own_size"] - quarter - share)
    barrier = pltpu.get_barrier_semaphore()
    greeted = [(stage, mask) for stage in (cores + ys, xs, zs) for mask in masks_of(stage)]
    for stage, mask in greeted:
        pl.semaphore_signal(
            barrier,
            inc=1,
            device_id=partner(stage, mask),
            device_id_type=pl.DeviceIdType.MESH,
        )
    pl.semaphore_wait(barrier, len(greeted))

    def sum_into(target, start, pieces, count):
        chunk = chunk_of(count)

        def body(turn, carry):
            held = pieces[0][0][pl.ds(pieces[0][1] + turn * chunk, chunk)]
            for source, at in pieces[1:]:
                held = held + source[pl.ds(at + turn * chunk, chunk)]
            target[pl.ds(start + turn * chunk, chunk)] = held
            return carry

        lax.fori_loop(0, count // chunk, body, 0)

    class Stream:
        def __init__(self, base, size, stages, total, total_at):
            self.base, self.size, self.stages = base, size, stages
            self.total, self.at = total, total_at
            self.land = base
            self.flight = None
            self.step = 0
            self.start = base

        def reduce(self):
            if self.flight is not None:
                copies, piece, lands, keep = self.flight
                for copy in copies:
                    copy.wait()
                pieces = [(work, keep)] + [(landing, land) for land in lands]
                sum_into(work, keep, pieces, piece)
                self.base, self.size, self.flight = keep, piece, None
            if self.step < len(self.stages):
                stage = self.stages[self.step]
                piece = self.size >> len(stage)
                keep = self.base + turned(stage, 0) * piece
                copies, lands = [], []
                for mask in masks_of(stage):
                    give = self.base + turned(stage, mask) * piece
                    target = landing.at[pl.ds(self.land, piece)]
                    copies.append(send(work.at[pl.ds(give, piece)], target, stage, mask))
                    lands.append(self.land)
                    self.land += piece
                self.flight = (copies, piece, lands, keep)
                self.step += 1

        def turn(self):
            self.at = self.at + (self.base - self.start)
            sum_into(self.total, self.at, [(work, self.base)], self.size)
            self.step = 0

        def double(self):
            if self.flight is not None:
                for copy in self.flight:
                    copy.wait()
                stage = self.stages[len(self.stages) - self.step]
                self.at = self.at - turned(stage, 0) * self.size
                self.size, self.flight = self.size << len(stage), None
            if self.step < len(self.stages):
                stage = self.stages[len(self.stages) - 1 - self.step]
                region = self.total.at[pl.ds(self.at, self.size)]
                self.flight = [send(region, region, stage, mask) for mask in masks_of(stage)]
                self.step += 1

        def squares(self, keep):
            held = work[pl.ds(self.base, self.size)]
            if keep is not None:
                tile = lax.broadcasted_iota(jnp.int32, (self.size, 8, 128), 0)
                held = jnp.where(keep(tile + self.base), held, 0.0)
            return jnp.sum(held * held, axis=0)

    sharing = cores + xs
    seat = sum(value(bit) * (1 << k) for k, bit in enumerate(sharing))

    def keep_own(tile):
        place = tile - plan["own"] - quarter
        return (place < 0) | (place + seat * share < 9)

    class Quarter:
        def __init__(self, stream, offset, stages):
            self.at = stream.base - stream.start + offset
            self.size, self.stages = stream.size, stages
            self.held, self.flights, self.step = [0], [], 0
            sum_into(own_total.at[seat], self.at, [(work, stream.base)], stream.size)

        def region(self, offset):
            return own_total.at[turned(sharing, offset), pl.ds(self.at, self.size)]

        def double(self):
            if self.flights:
                for copy in self.flights:
                    copy.wait()
                stage = self.stages[self.step - 1]
                if stage[0] in sharing:
                    changed = 1 << sharing.index(stage[0])
                    self.held = self.held + [offset | changed for offset in self.held]
                else:
                    self.at = self.at - turned(stage, 0) * self.size
                    self.size <<= len(stage)
                self.flights = []
            if self.step < len(self.stages):
                stage = self.stages[self.step]
                for offset in self.held:
                    region = self.region(offset)
                    self.flights += [send(region, region, stage, mask) for mask in masks_of(stage)]
                self.step += 1

    first, second = plan["cut"]
    own = [
        Stream(plan["own"], first, [ys, zs], None, 0),
        Stream(plan["own"] + first, plan["own_size"] - first, [zs, ys], None, 0),
    ]
    split = [
        Stream(plan["split"], second, [xs, zs], split_total, 0),
        Stream(
            plan["split"] + second,
            plan["split_size"] - second,
            [zs, xs],
            split_total,
            second,
        ),
    ]
    conv = Stream(plan["conv"], plan["conv_size"], [cores + ys, xs, zs], conv_total, 0)
    for load in loads:
        load.wait()
    sum_into(
        work,
        plan["own"],
        [(own_stage.at[k], 0) for k in range(mp_size)],
        quarter + share,
    )
    for stream in own + [conv]:
        stream.reduce()
    sum_into(work, plan["split"], [(split_stage.at[k], 0) for k in range(mp_size)], quarter)
    for stream in own + [conv]:
        stream.reduce()
    for stream in split:
        stream.reduce()
    for stream in own:
        stream.reduce()
    squares = jnp.zeros((8, 128), F32)
    singles = [[bit] for bit in xs]
    quarters = [
        Quarter(own[0], 0, [zs, ys] + singles + [cores]),
        Quarter(own[1], first, [ys] + singles + [zs, cores]),
    ]
    for piece in quarters:
        piece.double()
    conv.reduce()
    for stream in split:
        stream.reduce()
    for stream in own:
        squares = squares + stream.squares(keep_own)
    for piece in quarters:
        piece.double()
    conv.reduce()
    squares = squares + conv.squares(lambda tile: tile - plan["conv"] < conv_tiles)
    conv.turn()
    conv.double()
    for stream in split:
        stream.reduce()
        squares = squares + stream.squares(None)
    tiles[0] = squares
    tile_stages = [cores + ys, xs, zs]

    def send_tiles(number):
        stage = tile_stages[number]
        spot = number * 8 - 1
        return [
            send(tiles.at[number], tile_in.at[spot + mask], stage, mask)
            for mask in masks_of(stage)
        ]

    tile_flights = send_tiles(0)
    for stream in split:
        stream.turn()
        stream.double()
    rounds = 1
    while rounds <= len(tile_stages) or conv.flight is not None or quarters[0].flights:
        for stream in quarters + [conv]:
            stream.double()
        if rounds <= len(tile_stages):
            for copy in tile_flights:
                copy.wait()
            held = tiles[rounds - 1]
            for mask in masks_of(tile_stages[rounds - 1]):
                held = held + tile_in[(rounds - 1) * 8 - 1 + mask]
            tiles[rounds] = held
            if rounds < len(tile_stages):
                tile_flights = send_tiles(rounds)
        for stream in split:
            stream.double()
        rounds += 1
    square_out[...] = tiles[len(tile_stages)]
    stores = [
        (conv_total.at[pl.ds(0, conv_tiles)], early_out.at[pl.ds(0, conv_tiles)]),
        (conv_total.at[pl.ds(conv_tiles, time_tiles)], times_out),
        (split_total.at[pl.ds(0, quarter)], split_out),
    ]
    for m in range(mp_size):
        rows = pl.ds(conv_tiles + m * quarter, quarter)
        stores.append((own_total.at[m, pl.ds(0, quarter)], early_out.at[rows]))
        rows = pl.ds(m * share, share)
        stores.append((own_total.at[m, pl.ds(quarter, share)], small_out.at[rows]))
    stores = [
        pltpu.make_async_copy(source, target, store_sem.at[number])
        for number, (source, target) in enumerate(stores)
    ]
    for copy in stores:
        copy.start()
    for copy in stores:
        copy.wait()


def reduce_all(split_parts, own_parts, conv, dp_size, mp_size):
    bits = mesh_bits(dp_size, mp_size)
    quarter = split_parts[0].shape[0] // 8
    share = own_parts[0].shape[0] // 8 - quarter
    own_size = round_up(quarter + share, dp_size)
    split_size = round_up(quarter, dp_size)
    conv_size = round_up((CONV_ROWS + FAST_ROWS) // 8, dp_size * mp_size)
    places, at = {}, 0
    for name, size in [("split", split_size), ("own", own_size), ("conv", conv_size)]:
        places[name] = at
        at += size
    cut = (round_up(own_size // 2, dp_size), round_up(split_size // 2, dp_size))
    copies = 16 * (dp_size + mp_size) + 2 * mp_size * dp_size
    plan = dict(
        places,
        mp_size=mp_size,
        quarter=quarter,
        share=share,
        bits=bits,
        copies=copies,
        split_size=split_size,
        own_size=own_size,
        conv_size=conv_size,
        cut=cut,
    )
    vmem = pl.BlockSpec(memory_space=pltpu.VMEM)
    any_spec = pl.BlockSpec(memory_space=pl.ANY)
    arrays = [*split_parts, *own_parts, conv]
    loads = len(arrays)

    def tiled(size, *lead):
        return pltpu.VMEM((*lead, size, 8, 128), F32)

    outs = [(EARLY_ROWS // 8, 8, 128), (FAST_ROWS // 8, 8, 128), (share * mp_size, 8, 128), (quarter, 8, 128), (8, 128)]
    results = pl.pallas_call(
        partial(reduce_kernel, plan),
        in_specs=[any_spec] * loads,
        out_specs=[any_spec] * 4 + [vmem],
        out_shape=[jax.ShapeDtypeStruct(shape, F32) for shape in outs],
        scratch_shapes=[
            tiled(quarter, mp_size),
            tiled(quarter + share, mp_size),
            tiled(at),
            tiled(at),
            tiled(split_size),
            tiled(own_size, mp_size),
            tiled(conv_size),
            pltpu.VMEM((4, 8, 128), F32),
            pltpu.VMEM((24, 8, 128), F32),
            pltpu.SemaphoreType.DMA((loads,)),
            pltpu.SemaphoreType.DMA((copies,)),
            pltpu.SemaphoreType.DMA((copies,)),
            pltpu.SemaphoreType.DMA((3 + 2 * mp_size,)),
        ],
        compiler_params=pltpu.CompilerParams(
            collective_id=1, has_side_effects=True, vmem_limit_bytes=62 * 1024 * 1024
        ),
        name="reduce_gradients",
    )(*[array.reshape(-1, 8, 128) for array in arrays])
    return [held.reshape(-1, 128) for held in results]


FLAT_ROWS = 7896
BLOCK_ROWS = 1024
LATE = 609
SPAN = 40


def adam_kernel(
    wins,
    dp_size,
    mp_size,
    early_ref,
    times_ref,
    dense_ref,
    table_ref,
    small_ref,
    split_ref,
    square_ref,
    weight_ref,
    first_ref,
    second_ref,
    split_weight_ref,
    split_first_ref,
    split_second_ref,
    new_ref,
    new_first_ref,
    new_second_ref,
    low_ref,
    split_new_ref,
    split_new_first_ref,
    split_new_second_ref,
    split_low_ref,
    norm_out,
    loss_out,
    count_out,
    split_in,
    split_out,
    field,
    times,
    marks,
    pulled,
    factor_ref,
    pull_sem,
    load_sem,
    split_sem,
):
    step = pl.program_id(0)
    last = pl.num_programs(0) - 1
    scalar_refs = (norm_out, loss_out, count_out)
    lane = lax.broadcasted_iota(jnp.int32, (1, 128), 1)

    def pull(block, slot):
        start = pl.multiple_of(block * BLOCK_ROWS, BLOCK_ROWS)
        return pltpu.make_async_copy(
            field.at[pl.ds(start, BLOCK_ROWS + 8)], pulled.at[slot], pull_sem.at[slot]
        )

    def update(weights, first, second, grads):
        first = beta_first * first + (1 - beta_first) * grads
        second = beta_second * second + (1 - beta_second) * grads * grads
        fix_one = 1.0 / (1 - beta_first**STEP)
        fix_two = 1.0 / (1 - beta_second**STEP)
        weights = weights - learn_rate * (
            first * fix_one / (jnp.sqrt(second * fix_two) + adam_epsilon) + weight_decay * weights
        )
        return weights, first, second

    def sum_of(tile):
        held = jnp.sum(jnp.sum(tile, axis=0, keepdims=True), axis=1, keepdims=True)
        return jnp.broadcast_to(held, (1, 128))

    slot = lax.rem(step, 2)
    split_loads = [
        pltpu.make_async_copy(ref, split_in.at[k], split_sem.at[k])
        for k, ref in enumerate((split_weight_ref, split_first_ref, split_second_ref))
    ]
    split_stores = [
        pltpu.make_async_copy(split_out.at[k], ref, split_sem.at[3 + k])
        for k, ref in enumerate((split_new_ref, split_new_first_ref, split_new_second_ref))
    ]

    @pl.when(step == 0)
    def prepare():
        for load in split_loads:
            load.start()
        mark = pltpu.make_async_copy(table_ref, marks, load_sem.at[2])
        mark.start()
        load_times = pltpu.make_async_copy(
            times_ref, times.at[pl.ds(0, FAST_ROWS)], load_sem.at[0]
        )
        load_times.start()
        load_early = pltpu.make_async_copy(
            early_ref, field.at[pl.ds(0, EARLY_ROWS)], load_sem.at[1]
        )
        load_early.start()
        late = FIELD_ROWS - EARLY_ROWS
        field[EARLY_ROWS:FIELD_ROWS] = jnp.zeros((late, 128), F32)
        times[FAST_ROWS:] = jnp.zeros((times.shape[0] - FAST_ROWS, 128), F32)
        lane_all = lax.broadcasted_iota(jnp.int32, table_ref.shape, 1)
        counts = jnp.where(jnp.bitwise_and(lane_all, 2 * wins - 1) < wins, table_ref[...], 0.0)
        count = sum_of(counts)
        whole = jnp.sum(counts)
        mark.wait()
        load_times.wait()
        place = lax.broadcasted_iota(jnp.int32, (SPAN, ROOM), 0)
        slot_of = lax.broadcasted_iota(jnp.int32, (SPAN, ROOM), 1)

        def scatter(turn, begin):
            spots, found = [], []
            for m in range(mp_size):
                low = jnp.minimum(lax.div(begin, 8) * 8, FAST_ROWS)
                picks = []
                for w in range(wins):
                    length = marks[turn, m * 2 * wins + w].astype(jnp.int32)
                    row = marks[turn, m * 2 * wins + wins + w].astype(jnp.int32) + TABLE_AT
                    base = lax.div(row, 8) * 8
                    first = begin - low
                    inside = (slot_of >= first) & (slot_of < first + length)
                    inside = inside & (place - slot_of == row - base - first)
                    picks.append(jnp.where(inside, 1.0, 0.0).astype(BF16))
                    spots.append(base)
                    begin = begin + length
                held = pair(times[pl.ds(pl.multiple_of(low, 8), ROOM)])
                found.append(fold_pair(dot(jnp.concatenate(picks, axis=0), held)))
            for m in range(mp_size):
                for w in range(wins):
                    spot = pl.ds(pl.multiple_of(spots[m * wins + w], 8), SPAN)
                    field[spot] = field[spot] + found[m][w * SPAN : (w + 1) * SPAN]
            return begin

        @pl.when(whole <= FAST_ROWS)
        def few():
            lax.fori_loop(0, dp_size, scatter, jnp.int32(0))

        @pl.when(whole > FAST_ROWS)
        def many():
            pull_dense = pltpu.make_async_copy(
                dense_ref, field.at[pl.ds(EARLY_ROWS, late)], load_sem.at[0]
            )
            pull_dense.start()
            pull_dense.wait()

        def fold(turn, carry):
            spot = pl.multiple_of(EARLY_ROWS + turn * 256, 8)
            held = field[pl.ds(spot, 256)]
            return carry + jnp.sum((held * held).reshape(32, 8, 128), axis=0)

        squares = lax.fori_loop(0, late // 256, fold, square_ref[...])
        at = EARLY_ROWS
        for name_at, size in [(0, 17), (24, ACT)]:
            field[at : at + size] = small_ref[name_at : name_at + size]
            at += size
        at = TABLE_AT + TSTEPS
        field[at : at + ACT] = small_ref[48 : 48 + ACT]
        seed = 1.0 / count
        norm = jnp.sqrt(sum_of(squares)) * seed
        factor = jnp.minimum(1.0, clip_limit / (norm + 1e-06)) * seed
        factor_ref[...] = jnp.broadcast_to(factor, (8, 128))
        loss = small_ref[72:73]
        for number, held in enumerate((norm, loss, count)):
            scalar_refs[number][0] = jnp.sum(jnp.where(lane == 0, held, 0.0))
        load_early.wait()
        pull(0, 0).start()

    @pl.when(step < last)
    def ahead():
        pull(step + 1, 1 - slot).start()

    @pl.when(step == 1)
    def split():
        for load in split_loads:
            load.wait()
        count = split_in.shape[1]
        outs = update(*[split_in[k] for k in range(3)], split_ref[0:count] * factor_ref[0:1])
        for k in range(3):
            split_out[k] = outs[k]
        split_low_ref[...] = outs[0].astype(BF16)
        for store in split_stores:
            store.start()

    @pl.when(step == last)
    def split_end():
        for store in split_stores:
            store.wait()

    pull(step, slot).wait()
    early = pulled[slot, 0:BLOCK_ROWS]
    own = pltpu.roll(pulled[slot, 7 : BLOCK_ROWS + 7], 32, 1)
    before = pltpu.roll(pulled[slot, 6 : BLOCK_ROWS + 6], 32, 1)
    row = lax.broadcasted_iota(jnp.int32, (BLOCK_ROWS, 1), 0) + step * BLOCK_ROWS
    grads = jnp.where(lane < 32, jnp.where(row == LATE, early, before), own)
    grads = jnp.where(row < LATE, early, grads)
    outs = update(weight_ref[...], first_ref[...], second_ref[...], grads * factor_ref[0:1])
    new_ref[...], new_first_ref[...], new_second_ref[...] = outs
    low_ref[...] = outs[0].astype(BF16)


def adam_all(
    early, times, dense, table, small, split_grad, square, shared, split, wins, dp_size, mp_size
):
    grid = -(-FLAT_ROWS // BLOCK_ROWS)
    flat_spec = pl.BlockSpec((BLOCK_ROWS, 128), lambda i: (i, 0))
    split_rows = split[0].shape[0]

    def whole(shape):
        return pl.BlockSpec(shape, lambda i: (0,) * len(shape))

    shared_out = jax.ShapeDtypeStruct((FLAT_ROWS, 128), F32)
    split_out = jax.ShapeDtypeStruct((split_rows, 128), F32)
    any_spec = pl.BlockSpec(memory_space=pl.ANY)
    return pl.pallas_call(
        partial(adam_kernel, wins, dp_size, mp_size),
        grid=(grid,),
        in_specs=[
            any_spec,
            any_spec,
            any_spec,
            pl.BlockSpec(memory_space=pltpu.VMEM),
            whole(small.shape),
            whole(split_grad.shape),
            whole((8, 128)),
            flat_spec,
            flat_spec,
            flat_spec,
            any_spec,
            any_spec,
            any_spec,
        ],
        out_specs=[flat_spec] * 4
        + [any_spec] * 3
        + [whole((split_rows, 128))]
        + [pl.BlockSpec(memory_space=pltpu.SMEM)] * 3,
        out_shape=[shared_out] * 3
        + [jax.ShapeDtypeStruct((FLAT_ROWS, 128), BF16)]
        + [split_out] * 3
        + [jax.ShapeDtypeStruct((split_rows, 128), BF16)]
        + [jax.ShapeDtypeStruct((1,), F32)] * 3,
        scratch_shapes=[
            pltpu.VMEM((3, split_rows, 128), F32),
            pltpu.VMEM((3, split_rows, 128), F32),
            pltpu.VMEM((FIELD_ROWS, 128), F32),
            pltpu.VMEM((FAST_ROWS + ROOM, 128), F32),
            pltpu.SMEM(table.shape, F32),
            pltpu.VMEM((2, BLOCK_ROWS + 8, 128), F32),
            pltpu.VMEM((8, 128), F32),
            pltpu.SemaphoreType.DMA((2,)),
            pltpu.SemaphoreType.DMA((3,)),
            pltpu.SemaphoreType.DMA((6,)),
        ],
        compiler_params=pltpu.CompilerParams(vmem_limit_bytes=62 * 1024 * 1024),
        name="adam_update",
    )(
        early,
        times,
        dense,
        table,
        small,
        split_grad,
        square,
        *shared,
        *split,
    )


def per_device(
    frames,
    returns,
    actions,
    starts,
    lengths,
    shared_weights,
    shared_first,
    shared_second,
    split_weights,
    split_first,
    split_second,
):
    dp_size, mp_size = lax.axis_size("dp"), lax.axis_size("mp")
    narrow = D // mp_size
    hidden_width = FF // mp_size
    wins, steps = returns.shape
    width = split_weights.shape[0]
    split_rows = width // 128
    packed = narrow == 32
    own_rows = split_weights.reshape(split_rows, 128)
    split_all = lax.all_gather(own_rows, "mp", axis=0)
    notes = jnp.concatenate([lengths, starts]).astype(F32)
    line = lax.dynamic_update_slice(
        jnp.zeros((128,), F32), notes, (lax.axis_index("mp") * (2 * wins),)
    )
    here = jnp.arange(round_up(dp_size, 8)) == lax.axis_index("dp")
    table = jnp.where(here[:, None], line[None, :], 0.0)
    group = [table]
    for k in range(1, mp_size):
        turn = [(place, place ^ k) for place in range(mp_size)]
        group.append(lax.ppermute(table, "mp", turn))
    flat = shared_weights.reshape(FLAT_ROWS, 128)
    picked, z_one, z_two, z_three = conv_forward(lengths, frames, flat)
    z_three, group = lax.optimization_barrier((z_three, group))
    table = sum(group[1:], group[0])
    group = [table]
    for k in range(1, dp_size):
        turn = [(place, place ^ k) for place in range(dp_size)]
        group.append(lax.ppermute(table, "dp", turn))
    if packed:
        weights = [split_all]
    else:
        layers, layers_back = jax.vjp(
            lambda held: assemble(held, mp_size, narrow, hidden_width), split_all.reshape(-1)
        )
        weights = [
            jnp.stack([layer["qkv"].transpose(1, 0, 2) for layer in layers]),
            jnp.stack([layer["output"] for layer in layers]),
            jnp.stack([layer["up"] for layer in layers]),
            jnp.stack([layer["up_bias"][None] for layer in layers]),
            jnp.stack([layer["down"] for layer in layers]),
        ]
    small_rows = round_up(sum(rows for name, rows in SMALL), 8 * mp_size)
    cores, ys, xs, zs = mesh_bits(dp_size, mp_size)
    seat = jnp.bitwise_and(lax.axis_index("mp"), 1)
    seat = seat + 2 * jnp.bitwise_and(lax.axis_index("dp"), (1 << len(xs)) - 1)
    row, column = lax.axis_index("dp"), lax.axis_index("mp")
    index = jnp.stack([column, seat, row])
    results = former(
        lengths, starts, index, returns, actions, z_three, flat, weights, small_rows, packed
    )
    d_three, rows = results[:2]
    rows, group = lax.optimization_barrier((rows, group))
    table = sum(group[1:], group[0])
    quarter = 3136 // mp_size
    if packed:
        split_parts, own_parts = results[2:6], results[6:]
    else:
        d_encoder, d_small, d_qkv, d_output, d_up, d_up_bias, d_down = results[2:]
        grad_layers = [
            dict(
                qkv=d_qkv[layer].transpose(1, 0, 2),
                output=d_output[layer],
                up=d_up[layer],
                up_bias=d_up_bias[layer, 0],
                down=d_down[layer],
            )
            for layer in range(LAYERS)
        ]
        gathered = layers_back(grad_layers)[0].reshape(mp_size, split_rows, 128)
        gathered = jnp.pad(gathered, ((0, 0), (0, quarter - split_rows), (0, 0)))
        encoder = d_encoder.reshape(mp_size, quarter, 128)
        small = d_small.reshape(mp_size, -1, 128)
        every = jnp.concatenate([encoder, small], axis=1)

        def turned(held, own):
            return [
                lax.dynamic_index_in_dim(held, jnp.bitwise_xor(own, k), 0, keepdims=False)
                for k in range(mp_size)
            ]

        split_parts, own_parts = turned(gathered, index[0]), turned(every, index[1])
    split_parts, own_parts = list(split_parts), list(own_parts)
    for k in range(1, mp_size):
        turn = [(place, place ^ k) for place in range(mp_size)]
        split_parts[k] = lax.ppermute(split_parts[k], "mp", turn)
        turn = [
            (dp * mp_size + mp, (dp ^ (k >> 1)) * mp_size + (mp ^ (k & 1)))
            for dp in range(dp_size)
            for mp in range(mp_size)
        ]
        own_parts[k] = lax.ppermute(own_parts[k], ("dp", "mp"), turn)
    d_conv, total = conv_backward(
        lengths, index, table, rows, picked, z_one, z_two, d_three, flat
    )

    def whole():
        ends = jnp.cumsum(lengths)
        slot = jnp.arange(ROOM, dtype=jnp.int32)
        past = slot[:, None] >= ends[None, :-1]
        begin = jnp.sum(jnp.where(past, lengths[None, :-1], 0), axis=1)
        gaps = starts[1:] - starts[:-1]
        spot = slot - begin + starts[0] + jnp.sum(jnp.where(past, gaps[None, :], 0), axis=1)
        spot = jnp.where(slot < ends[-1], spot, 0) + TABLE_AT - EARLY_ROWS
        held = jnp.zeros((FIELD_ROWS - EARLY_ROWS, D), F32).at[spot].add(rows)
        return lax.psum(held, ("dp", "mp"))

    dense = lax.cond(
        total[0] > FAST_ROWS, whole, lambda: jnp.zeros((FIELD_ROWS - EARLY_ROWS, D), F32)
    )
    early, times, small, split_sum, square = reduce_all(
        split_parts, own_parts, d_conv, dp_size, mp_size
    )
    shared_view = [a.reshape(FLAT_ROWS, 128) for a in (shared_weights, shared_first, shared_second)]
    split_view = [a.reshape(split_rows, 128) for a in (split_weights, split_first, split_second)]
    updated = adam_all(
        early,
        times,
        dense,
        table,
        small,
        split_sum,
        square,
        shared_view,
        split_view,
        wins,
        dp_size,
        mp_size,
    )
    shared_out = [a.reshape(-1) for a in updated[:4]]
    split_out = [a.reshape(-1) for a in updated[4:8]]
    return (*shared_out, *split_out, *[held.reshape(()) for held in updated[8:]])


def solution(mesh):
    return jax.shard_map(
        per_device,
        mesh=mesh,
        in_specs=(
            P(("dp", "mp"), None, None, None, None),
            P(("dp", "mp"), None),
            P(("dp", "mp"), None),
            P(("dp", "mp")),
            P(("dp", "mp")),
            P(),
            P(),
            P(),
            P("mp"),
            P("mp"),
            P("mp"),
        ),
        out_specs=(P(), P(), P(), P(), P("mp"), P("mp"), P("mp"), P("mp"), P(), P(), P()),
        check_vma=False,
    )
```

```python
from functools import partial
import math

import jax
import jax.numpy as jnp
from jax import lax
from jax.experimental import pallas as pl
from jax.experimental.pallas import tpu as pltpu
from jax.sharding import PartitionSpec as P

D = 128
FF = 512
ACT = 18
C1 = 32
C2 = 64
TSTEPS = 4096
LAYERS = 2
STEP = 10
HD = 16


clip_limit = 0.1
learn_rate = 0.05
beta_first = 0.9
beta_second = 0.95
adam_epsilon = 1e-08
weight_decay = 0.1


def span_layout(narrow, hidden):
    return [
        ("qkv", (D, 3, narrow)),
        ("output", (narrow, D)),
        ("up", (D, hidden)),
        ("up_bias", (hidden,)),
        ("down", (hidden, D)),
    ]


def assemble(flat, copies, narrow, hidden):
    layout = span_layout(narrow, hidden)
    width = sum((math.prod(shape) for name, shape in layout))
    blocks = flat.reshape(copies, LAYERS, width)
    layers = []
    for layer in range(LAYERS):
        offset = 0
        pieces = {}
        for name, shape in layout:
            count = math.prod(shape)
            pieces[name] = blocks[:, layer, offset : offset + count].reshape((copies,) + shape)
            offset += count
        layers.append(
            {
                "qkv": jnp.moveaxis(pieces["qkv"], 0, 2).reshape(D, 3, copies * narrow),
                "output": pieces["output"].reshape(copies * narrow, D),
                "up": jnp.moveaxis(pieces["up"], 0, 1).reshape(D, copies * hidden),
                "up_bias": pieces["up_bias"].reshape(copies * hidden),
                "down": pieces["down"].reshape(copies * hidden, D),
            }
        )
    return layers


GROUP = 16
CONV_ROWS = 616
ROOM = 128
HALF = 64
BF16 = jnp.bfloat16
F32 = jnp.float32


def gelu_value(x):
    inner = 0.7978845608028654 * (x + 0.044715 * (x * x * x))
    return 0.5 * x * (1.0 + jnp.tanh(inner))


def gelu_both(x):
    square = x * x
    turn = jnp.tanh(0.7978845608028654 * x * (1.0 + 0.044715 * square))
    half = 0.5 * (1.0 + turn)
    slope = half + 0.5 * x * (1.0 - turn * turn) * (
        0.7978845608028654 * (1.0 + 3 * 0.044715 * square)
    )
    return x * half, slope


def two_parts(x):
    high = x.astype(BF16)
    return high, (x - high.astype(F32)).astype(BF16)


def pair(x):
    return jnp.concatenate(two_parts(x), axis=-1)


def fold_pair(x):
    return x[:, :128] + x[:, 128:]


def dot(a, b):
    return lax.dot_general(a, b, (((1,), (0,)), ((), ())), preferred_element_type=F32)


def dot_rows(a, b):
    return lax.dot_general(a, b, (((0,), (0,)), ((), ())), preferred_element_type=F32)


def lanes():
    return lax.broadcasted_iota(jnp.int32, (1, 128), 1)


def conv_biases(flat_ref):
    lane = lanes()
    one = jnp.where(lane < 32, flat_ref[64:65], 0.0)
    one = one + pltpu.roll(one, 32, 1)
    one = one + pltpu.roll(one, 64, 1)
    two = jnp.where(lane < 64, pltpu.roll(flat_ref[320:321], 96, 1), 0.0)
    two = two + pltpu.roll(two, 64, 1)
    three = jnp.where(
        lane < 32,
        pltpu.roll(flat_ref[608:609], 32, 1),
        jnp.where(lane < 64, pltpu.roll(flat_ref[609:610], 32, 1), 0.0),
    )
    three = three + pltpu.roll(three, 64, 1)
    return one, two, three


def shifted(ref, start, rows, lane):
    first = pltpu.roll(ref[start : start + rows], 128 - lane, 1)
    second = pltpu.roll(ref[start + 1 : start + 1 + rows], 128 - lane, 1)
    return jnp.where(lanes() < 128 - lane, first, second)


def spread_one(flat_ref, put):
    halves = [jnp.transpose(flat_ref[pl.ds(side, 32, stride=2), :]) for side in range(2)]
    turned = jnp.concatenate(halves, axis=0)
    lane = lax.broadcasted_iota(jnp.int32, (8, 128), 1)
    row = lax.broadcasted_iota(jnp.int32, (8, 128), 0)
    low = row < 4
    column = lax.shift_right_logical(lane, 5)
    for ky in range(8):
        for c in range(4):
            held = turned[c * 64 + ky * 8 : c * 64 + ky * 8 + 8]
            wide = jnp.concatenate([held] * 4, axis=1)
            flipped = jnp.concatenate([wide[4:], wide[:4]], axis=0)
            zero = jnp.zeros((8, 128), F32)
            first = jnp.where(column == 0, wide, jnp.where((column == 1) & ~low, flipped, zero))
            second = jnp.where(
                column == 2,
                wide,
                jnp.where(((column == 1) & low) | ((column == 3) & ~low), flipped, zero),
            )
            third = jnp.where((column == 3) & low, flipped, zero)
            put(ky * 128 + c * 32, jnp.concatenate([first, second, third, zero], axis=0))


def spread_two(flat_ref, rows_ref, turned, put):
    lane = lax.broadcasted_iota(jnp.int32, (32, 128), 1)
    rows_ref[0:256] = shifted(flat_ref, 64, 256, 32)
    for j in range(4):
        block = jnp.transpose(rows_ref[pl.ds(j, 64, stride=4), :])
        turned[j * 128 : (j + 1) * 128] = jnp.concatenate([block, block], axis=1)
    for ky in range(4):
        rows = [turned[pl.ds(ky * 4 + kx, 32, stride=16)] for kx in range(4)]
        for i in range(8):
            left = rows[i] if i < 4 else jnp.zeros((32, 128), F32)
            right = rows[i - 2] if 2 <= i < 6 else jnp.zeros((32, 128), F32)
            put(ky * 256 + i * 32, jnp.where(lane < 64, left, right))


def spread_three(flat_ref, rows_ref, turned, put):
    lane = lax.broadcasted_iota(jnp.int32, (64, 128), 1)
    side = lax.broadcasted_iota(jnp.int32, (32, 128), 1) < 64
    rows_ref[0:288] = shifted(flat_ref, 320, 288, 96)
    nine = [rows_ref[pl.ds(k, 32, stride=9), :] for k in range(9)]
    flips = [pltpu.roll(nine[4 + k], 64, 1) for k in range(5)]
    for j in range(5):
        wide = min(128, 576 - j * 128)
        rows_ref[pl.ds(0, 32, stride=2), :] = nine[j]
        rows_ref[pl.ds(1, 32, stride=2), :] = (
            jnp.where(side, flips[j], flips[j + 1]) if j < 4 else flips[4]
        )
        block = jnp.transpose(rows_ref[0:64])[0:wide]
        turned[j * 128 : j * 128 + wide] = jnp.concatenate([block, block], axis=1)
    for ky in range(3):
        rows = [turned[pl.ds(ky * 3 + kx, 64, stride=9)] for kx in range(3)]
        for i in range(4):
            left = rows[i] if i < 3 else jnp.zeros((64, 128), F32)
            right = rows[i - 1] if i >= 1 else jnp.zeros((64, 128), F32)
            put(ky * 256 + i * 64, jnp.where(lane < 64, left, right))


def last_masks():
    return lanes() < 64


def conv_forward_kernel(
    lengths_from,
    frames_ref,
    shared_ref,
    picked_ref,
    z_one_ref,
    z_two_ref,
    z_three_ref,
    flat_ref,
    held,
    wide,
    picked,
    z_one,
    z_two,
    z_three,
    h_one,
    h_two,
    w_one,
    w_two,
    w_three,
    choose,
    rows_ref,
    turned,
    lengths_ref,
    frame_sem,
    out_sem,
):
    scalars = pltpu.make_async_copy(lengths_from, lengths_ref, out_sem.at[5])
    scalars.start()
    scalars.wait()
    wins = lengths_ref.shape[0]
    steps = frames_ref.shape[1]
    used = jnp.int32(0)
    for w in range(wins):
        used = used + lengths_ref[w]
    groups = lax.div(used + (GROUP - 1), GROUP)

    def frame_copy(group, spot, slot):
        state = jnp.minimum(group * GROUP + spot, used - 1)
        window, begin, end = jnp.int32(0), jnp.int32(0), jnp.int32(0)
        for w in range(wins - 1):
            end = end + lengths_ref[w]
            window = jnp.where(state >= end, w + 1, window)
            begin = jnp.where(state >= end, end, begin)
        return pltpu.make_async_copy(
            frames_ref.at[window, state - begin], held.at[slot, spot], frame_sem.at[slot, spot]
        )

    def fetch(group, slot):
        def one(spot, carry):
            frame_copy(group, spot, slot).start()
            return carry

        lax.fori_loop(0, GROUP, one, 0)

    weights = pltpu.make_async_copy(
        shared_ref.at[pl.ds(0, CONV_ROWS)], flat_ref, out_sem.at[4]
    )
    weights.start()
    fetch(0, 0)
    h_one[...] = jnp.zeros(h_one.shape, BF16)

    def put_one(row, block):
        w_one[row : row + 32] = pair(block)

    def put_two(row, block):
        w_two[row : row + 32] = pair(block)

    def put_three(row, block):
        w_three[row : row + 64] = pair(block)

    weights.wait()
    spread_one(flat_ref, put_one)
    spread_two(flat_ref, rows_ref, turned, put_two)
    spread_three(flat_ref, rows_ref, turned, put_three)
    bias_one, bias_two, bias_three = conv_biases(flat_ref)
    row = lax.broadcasted_iota(jnp.int32, (128, 640), 0)
    column = lax.broadcasted_iota(jnp.int32, (128, 640), 1)
    place = jnp.bitwise_and(column, 31)
    channel = jnp.bitwise_and(lax.shift_right_logical(column, 5), 3)
    block = lax.shift_right_logical(column, 7)
    right = (row == 16 * block + place) & (place < 20)
    for c in range(4):
        choose[c * 128 : (c + 1) * 128] = jnp.where(right & (channel == c), 1.0, 0.0).astype(BF16)

    def one_group(group, carry):
        slot = lax.rem(group, 2)

        @pl.when(group + 1 < groups)
        def ahead():
            fetch(group + 1, 1 - slot)

        def lay(step, carry):
            spots = [step * 4 + k for k in range(4)]
            for spot in spots:
                frame_copy(group, spot, slot).wait()
            for spot in spots:
                image = held[slot, spot].astype(F32).reshape(336, 84)
                image = jnp.concatenate([image, jnp.zeros((336, 44), F32)], axis=1)
                wide[pl.ds(spot, 336, stride=GROUP), :] = image
            return carry

        lax.fori_loop(0, GROUP // 4, lay, 0)
        for part in range(3):
            rows = wide[part * 1792 : (part + 1) * 1792].reshape(28, 4, GROUP, 128)
            rows = [rows[:, c].reshape(448, 128).astype(BF16) for c in range(4)]
            result = dot(jnp.concatenate(rows, axis=1), choose[...])
            picked[part * 7 : (part + 1) * 7] = result.astype(BF16).reshape(7, 4, GROUP, 640)
        keep_picked = pltpu.make_async_copy(picked, picked_ref.at[group], out_sem.at[0])
        keep_picked.start()
        for q in range(5):
            pieces = [
                picked[j : j + 20, b, :, q * 128 : (q + 1) * 128].reshape(20 * GROUP, 128)
                for j in range(2)
                for b in range(4)
            ]
            z = fold_pair(dot(jnp.concatenate(pieces, axis=1), w_one[...])) + bias_one
            z_one[:, :, q] = z.reshape(10, 2, GROUP, 128)
            high, low = two_parts(gelu_value(z))
            h_one[0, :, :, q] = high.reshape(10, 2, GROUP, 128)
            h_one[1, :, :, q] = low.reshape(10, 2, GROUP, 128)
        keep_one = pltpu.make_async_copy(z_one, z_one_ref.at[group], out_sem.at[1])
        keep_one.start()
        total = jnp.zeros((45 * GROUP, 128), F32)
        for part in range(2):
            pieces = []
            for j in range(2):
                for b in range(2):
                    pieces.append(h_one[part, j : j + 9, b, 0:5].reshape(45 * GROUP, 128))
                    pieces.append(h_one[part, j : j + 9, b, 1:6].reshape(45 * GROUP, 128))
            total = total + fold_pair(dot(jnp.concatenate(pieces, axis=1), w_two[...]))
        z = (total + bias_two).reshape(9, 5, GROUP, 128)
        z_two[...] = z
        h = gelu_value(z)
        high, low = two_parts(h)
        h_two[0] = high
        h_two[1] = low
        edge = jnp.where(last_masks(), h[:, 4].reshape(9 * GROUP, 128), 0.0)
        high, low = two_parts(edge)
        h_two[0, :, 4] = high.reshape(9, GROUP, 128)
        h_two[1, :, 4] = low.reshape(9, GROUP, 128)
        keep_two = pltpu.make_async_copy(z_two, z_two_ref.at[group], out_sem.at[2])
        keep_two.start()
        total = jnp.zeros((28 * GROUP, 128), F32)
        for part in range(2):
            pieces = []
            for ky in range(3):
                pieces.append(h_two[part, ky : ky + 7, 0:4].reshape(28 * GROUP, 128))
                pieces.append(h_two[part, ky : ky + 7, 1:5].reshape(28 * GROUP, 128))
            total = total + fold_pair(dot(jnp.concatenate(pieces, axis=1), w_three[...]))
        z_three[...] = (total + bias_three).reshape(28, GROUP, 128)
        spot = pl.multiple_of(group * GROUP, GROUP)
        keep_three = pltpu.make_async_copy(
            z_three, z_three_ref.at[:, pl.ds(spot, GROUP)], out_sem.at[3]
        )
        keep_three.start()
        keep_picked.wait()
        keep_one.wait()
        keep_two.wait()
        keep_three.wait()
        return carry

    lax.fori_loop(0, groups, one_group, 0)


def conv_forward(lengths, frames, flat):
    most = ROOM // GROUP
    any_spec = pl.BlockSpec(memory_space=pl.ANY)
    hbm = pl.BlockSpec(memory_space=pltpu.HBM)
    return pl.pallas_call(
        conv_forward_kernel,
        in_specs=[
            any_spec,
            any_spec,
            any_spec,
        ],
        out_specs=[hbm] * 4,
        out_shape=[
            jax.ShapeDtypeStruct((most, 21, 4, GROUP, 640), BF16),
            jax.ShapeDtypeStruct((most, 10, 2, 5, GROUP, 128), F32),
            jax.ShapeDtypeStruct((most, 9, 5, GROUP, 128), F32),
            jax.ShapeDtypeStruct((28, ROOM, 128), F32),
        ],
        scratch_shapes=[
            pltpu.VMEM((CONV_ROWS, 128), F32),
            pltpu.VMEM((2, GROUP, 84, 4, 84), BF16),
            pltpu.VMEM((336 * GROUP, 128), F32),
            pltpu.VMEM((21, 4, GROUP, 640), BF16),
            pltpu.VMEM((10, 2, 5, GROUP, 128), F32),
            pltpu.VMEM((9, 5, GROUP, 128), F32),
            pltpu.VMEM((28, GROUP, 128), F32),
            pltpu.VMEM((2, 10, 2, 6, GROUP, 128), BF16),
            pltpu.VMEM((2, 9, 5, GROUP, 128), BF16),
            pltpu.VMEM((1024, 256), BF16),
            pltpu.VMEM((1024, 256), BF16),
            pltpu.VMEM((768, 256), BF16),
            pltpu.VMEM((512, 640), BF16),
            pltpu.VMEM((288, 128), F32),
            pltpu.VMEM((576, 128), F32),
            pltpu.SMEM(lengths.shape, jnp.int32),
            pltpu.SemaphoreType.DMA((2, GROUP)),
            pltpu.SemaphoreType.DMA((6,)),
        ],
        compiler_params=pltpu.CompilerParams(vmem_limit_bytes=62 * 1024 * 1024),
        name="conv_forward",
    )(lengths, frames.transpose(0, 1, 3, 2, 4), flat)


def gather_one(total, out):
    lane = lax.broadcasted_iota(jnp.int32, (32, 128), 1)
    halves = [jnp.zeros((32, 128), F32) for side in range(2)]
    for ky in range(8):
        held = total[0:128, ky * 128 : (ky + 1) * 128] + total[128:256, ky * 128 : (ky + 1) * 128]
        summed = held[0:32]
        for o in range(1, 4):
            summed = summed + pltpu.roll(held[32 * o : 32 * o + 32], 128 - 4 * o, 1)
        for c in range(4):
            spot = (c % 2) * 64 + ky * 8
            shift = (spot - c * 32) % 128
            moved = pltpu.roll(summed, shift, 1) if shift else summed
            inside = (lane >= spot) & (lane < spot + 8)
            halves[c // 2] = halves[c // 2] + jnp.where(inside, moved, 0.0)
    for side in range(2):
        out[pl.ds(side, 32, stride=2), :] = halves[side]


def gather_two(total, turned, rows_ref, out):
    lane = lax.broadcasted_iota(jnp.int32, (64, 128), 1)
    for ky in range(4):
        near = total[0:128, ky * 256 : ky * 256 + 128] + total[128:256, ky * 256 : ky * 256 + 128]
        far = (
            total[0:128, ky * 256 + 128 : ky * 256 + 256]
            + total[128:256, ky * 256 + 128 : ky * 256 + 256]
        )
        summed = near[0:64] + jnp.where(
            lane < 64, pltpu.roll(near[64:128], 64, 1), pltpu.roll(far[64:128], 64, 1)
        )
        flipped = jnp.transpose(jnp.concatenate([summed, jnp.zeros((64, 128), F32)], axis=0))
        for kx in range(4):
            turned[pl.ds(ky * 4 + kx, 32, stride=16), :] = flipped[kx * 32 : (kx + 1) * 32]
    rows_ref[0:8] = jnp.zeros((8, 128), F32)
    rows_ref[264:272] = jnp.zeros((8, 128), F32)
    for j in range(4):
        block = jnp.transpose(turned[j * 128 : (j + 1) * 128])[0:64]
        rows_ref[pl.ds(8 + j, 64, stride=4), :] = block
    own = pltpu.roll(rows_ref[8:265], 32, 1)
    before = pltpu.roll(rows_ref[7:264], 32, 1)
    out[64:321] = jnp.where(lanes() >= 32, own, before)


def gather_three(total, turned, rows_ref, out):
    lane = lax.broadcasted_iota(jnp.int32, (64, 128), 1)
    side = lax.broadcasted_iota(jnp.int32, (32, 128), 1) < 64
    blank = jnp.zeros((64, 128), F32)
    for ky in range(3):
        near = total[0:128, ky * 256 : ky * 256 + 128] + total[128:256, ky * 256 : ky * 256 + 128]
        far = (
            total[0:128, ky * 256 + 128 : ky * 256 + 256]
            + total[128:256, ky * 256 + 128 : ky * 256 + 256]
        )
        first = near[0:64] + jnp.where(
            lane < 64, pltpu.roll(near[64:128], 64, 1), pltpu.roll(far[64:128], 64, 1)
        )
        second = far[0:64] + pltpu.roll(far[64:128], 64, 1)
        flipped = jnp.transpose(jnp.concatenate([first, blank], axis=0))
        turned[pl.ds(ky * 3, 64, stride=9), :] = flipped[0:64]
        turned[pl.ds(ky * 3 + 1, 64, stride=9), :] = flipped[64:128]
        flipped = jnp.transpose(jnp.concatenate([second, blank], axis=0))
        turned[pl.ds(ky * 3 + 2, 64, stride=9), :] = flipped[0:64]
    turned[576:640] = blank
    evens, odds = [], []
    for j in range(5):
        rows_ref[0:64] = jnp.transpose(turned[j * 128 : (j + 1) * 128])[0:64]
        evens.append(rows_ref[pl.ds(0, 32, stride=2), :])
        odds.append(pltpu.roll(rows_ref[pl.ds(1, 32, stride=2), :], 64, 1))
    rows_ref[0:8] = jnp.zeros((8, 128), F32)
    rows_ref[296:304] = jnp.zeros((8, 128), F32)
    for k in range(9):
        if k < 4:
            held = evens[k]
        elif k == 4:
            held = jnp.where(side, evens[4], odds[0])
        else:
            held = jnp.where(side, odds[k - 5], odds[k - 4])
        rows_ref[pl.ds(8 + k, 32, stride=9), :] = held
    own = pltpu.roll(rows_ref[8:297], 96, 1)
    before = pltpu.roll(rows_ref[7:296], 96, 1)
    edge = out[320:321]
    out[320:609] = jnp.where(lanes() >= 96, own, before)
    out[320:321] = out[320:321] + edge


def conv_backward_kernel(
    lengths_from,
    picked_ref,
    z_one_ref,
    z_two_ref,
    d_three_ref,
    shared_ref,
    flat_out,
    flat_ref,
    picked,
    z_one,
    z_two,
    d_three,
    h_one,
    h_two,
    slope_one,
    pad_three,
    pad_two,
    d_one,
    v_two,
    v_three,
    spread,
    rows_ref,
    turned,
    bias_out,
    total_one,
    total_two,
    total_three,
    lengths_ref,
    load_sem,
    weight_sem,
):
    scalars = pltpu.make_async_copy(lengths_from, lengths_ref, weight_sem)
    scalars.start()
    scalars.wait()
    used = jnp.int32(0)
    for w in range(lengths_ref.shape[0]):
        used = used + lengths_ref[w]
    groups = lax.div(used + (GROUP - 1), GROUP)

    def loads(group, slot):
        spot = pl.multiple_of(group * GROUP, GROUP)
        return [
            pltpu.make_async_copy(picked_ref.at[group], picked.at[slot], load_sem.at[slot, 0]),
            pltpu.make_async_copy(z_one_ref.at[group], z_one.at[slot], load_sem.at[slot, 1]),
            pltpu.make_async_copy(z_two_ref.at[group], z_two.at[slot], load_sem.at[slot, 2]),
            pltpu.make_async_copy(
                d_three_ref.at[:, pl.ds(spot, GROUP)], d_three.at[slot], load_sem.at[slot, 3]
            ),
        ]

    weights = pltpu.make_async_copy(
        shared_ref.at[pl.ds(0, CONV_ROWS)], flat_ref, weight_sem
    )
    weights.start()
    for load in loads(0, 0):
        load.start()

    def put_two(row, block):
        spread[row : row + 32] = block

    def put_three(row, block):
        spread[row : row + 64] = block

    weights.wait()
    spread_two(flat_ref, rows_ref, turned, put_two)
    for b in range(2):
        for j in range(2):
            for side in range(2):
                source = (2 * j + b) * 256 + side * 128
                target = (b * 2 + j) * 256 + side * 128
                v_two[target : target + 128] = pair(jnp.transpose(spread[source : source + 128]))
    spread_three(flat_ref, rows_ref, turned, put_three)
    for part in range(6):
        rows = pl.ds(part * 128, 128)
        v_three[rows] = pair(jnp.transpose(spread[rows]))
    total_one[...] = jnp.zeros(total_one.shape, F32)
    total_two[...] = jnp.zeros(total_two.shape, F32)
    total_three[...] = jnp.zeros(total_three.shape, F32)
    bias_out[...] = jnp.zeros(bias_out.shape, F32)
    h_one[...] = jnp.zeros(h_one.shape, BF16)
    pad_two[...] = jnp.zeros(pad_two.shape, BF16)
    pad_three[...] = jnp.zeros(pad_three.shape, BF16)

    def fold(rows):
        return jnp.sum(rows.reshape(-1, 8, 128), axis=0)

    def one_group(group, carry):
        slot = lax.rem(group, 2)

        @pl.when(group + 1 < groups)
        def ahead():
            for load in loads(group + 1, 1 - slot):
                load.start()

        for load in loads(group, slot):
            load.wait()
        rows = d_three[slot].reshape(28 * GROUP, 128)
        bias_out[2] += fold(rows)
        both = pair(rows)
        pad_three[0, 2:9, 1:5] = both[:, :128].reshape(7, 4, GROUP, 128)
        pad_three[1, 2:9, 1:5] = both[:, 128:].reshape(7, 4, GROUP, 128)
        h, slope_two = gelu_both(z_two[slot])
        high, low = two_parts(h)
        h_two[0] = high
        h_two[1] = low
        edge = jnp.where(last_masks(), h[:, 4].reshape(9 * GROUP, 128), 0.0)
        high, low = two_parts(edge)
        h_two[0, :, 4] = high.reshape(9, GROUP, 128)
        h_two[1, :, 4] = low.reshape(9, GROUP, 128)
        for part in range(2):
            pieces = []
            for ky in range(3):
                pieces.append(h_two[part, ky : ky + 7, 0:4].reshape(28 * GROUP, 128))
                pieces.append(h_two[part, ky : ky + 7, 1:5].reshape(28 * GROUP, 128))
            total_three[...] += dot_rows(both, jnp.concatenate(pieces, axis=1))
        spill = jnp.zeros((45 * GROUP, 128), F32)
        for part in range(2):
            pieces = []
            for ky in range(3):
                pieces.append(pad_three[part, 2 - ky : 11 - ky, 1:6].reshape(45 * GROUP, 128))
                pieces.append(pad_three[part, 2 - ky : 11 - ky, 0:5].reshape(45 * GROUP, 128))
            spill = spill + fold_pair(dot(jnp.concatenate(pieces, axis=1), v_three[...]))
        rows = spill * slope_two.reshape(45 * GROUP, 128)
        bias_out[1] += fold(rows)
        both = pair(rows)
        pad_two[0, 1:10, 1:6] = both[:, :128].reshape(9, 5, GROUP, 128)
        pad_two[1, 1:10, 1:6] = both[:, 128:].reshape(9, 5, GROUP, 128)
        for q in range(5):
            h, slope = gelu_both(z_one[slot, :, :, q])
            high, low = two_parts(h)
            h_one[0, :, :, q] = high
            h_one[1, :, :, q] = low
            slope_one[:, :, q] = slope
        for part in range(2):
            pieces = []
            for j in range(2):
                for b in range(2):
                    pieces.append(h_one[part, j : j + 9, b, 0:5].reshape(45 * GROUP, 128))
                    pieces.append(h_one[part, j : j + 9, b, 1:6].reshape(45 * GROUP, 128))
            total_two[...] += dot_rows(both, jnp.concatenate(pieces, axis=1))
        for b in range(2):
            spill = jnp.zeros((50 * GROUP, 128), F32)
            for part in range(2):
                pieces = []
                for j in range(2):
                    pieces.append(pad_two[part, 1 - j : 11 - j, 1:6].reshape(50 * GROUP, 128))
                    pieces.append(pad_two[part, 1 - j : 11 - j, 0:5].reshape(50 * GROUP, 128))
                spill = spill + fold_pair(
                    dot(jnp.concatenate(pieces, axis=1), v_two[b * 512 : (b + 1) * 512])
                )
            rows = spill * slope_one[:, b].reshape(50 * GROUP, 128)
            bias_out[0] += fold(rows)
            d_one[:, b] = pair(rows).reshape(10, 5, GROUP, 256)
        for q in range(5):
            pieces = [
                picked[slot, j : j + 20, b, :, q * 128 : (q + 1) * 128].reshape(20 * GROUP, 128)
                for j in range(2)
                for b in range(4)
            ]
            total_one[...] += dot_rows(
                d_one[:, :, q].reshape(20 * GROUP, 256), jnp.concatenate(pieces, axis=1)
            )
        return carry

    lax.fori_loop(0, groups, one_group, 0)
    gather_one(total_one, flat_out)
    gather_two(total_two, turned, rows_ref, flat_out)
    gather_three(total_three, turned, rows_ref, flat_out)
    lane = lanes()
    sums = [jnp.sum(bias_out[k], axis=0, keepdims=True) for k in range(3)]
    sums[0] = sums[0] + pltpu.roll(sums[0], 64, 1)
    sums[0] = sums[0] + pltpu.roll(sums[0], 32, 1)
    sums[1] = jnp.where(lane < 64, sums[1] + pltpu.roll(sums[1], 64, 1), 0.0)
    sums[2] = jnp.where(lane < 64, sums[2] + pltpu.roll(sums[2], 64, 1), 0.0)
    flat_out[64:65] = jnp.where(lane < 32, sums[0], flat_out[64:65])
    flat_out[320:321] = flat_out[320:321] + pltpu.roll(sums[1], 32, 1)
    late = pltpu.roll(sums[2], 96, 1)
    flat_out[608:609] = flat_out[608:609] + jnp.where(lane >= 96, late, 0.0)
    row = lax.broadcasted_iota(jnp.int32, (7, 128), 0)
    flat_out[609:616] = jnp.where((row == 0) & (lane < 32), late, 0.0)


def conv_backward(lengths, picked, z_one, z_two, d_three, flat):
    hbm = pl.BlockSpec(memory_space=pltpu.HBM)
    vmem = pl.BlockSpec(memory_space=pltpu.VMEM)
    return pl.pallas_call(
        conv_backward_kernel,
        in_specs=[hbm] * 6,
        out_specs=vmem,
        out_shape=jax.ShapeDtypeStruct((CONV_ROWS, 128), F32),
        scratch_shapes=[
            pltpu.VMEM((CONV_ROWS, 128), F32),
            pltpu.VMEM((2, 21, 4, GROUP, 640), BF16),
            pltpu.VMEM((2, 10, 2, 5, GROUP, 128), F32),
            pltpu.VMEM((2, 9, 5, GROUP, 128), F32),
            pltpu.VMEM((2, 28, GROUP, 128), F32),
            pltpu.VMEM((2, 10, 2, 6, GROUP, 128), BF16),
            pltpu.VMEM((2, 9, 5, GROUP, 128), BF16),
            pltpu.VMEM((10, 2, 5, GROUP, 128), F32),
            pltpu.VMEM((2, 11, 6, GROUP, 128), BF16),
            pltpu.VMEM((2, 11, 6, GROUP, 128), BF16),
            pltpu.VMEM((10, 2, 5, GROUP, 256), BF16),
            pltpu.VMEM((1024, 256), BF16),
            pltpu.VMEM((768, 256), BF16),
            pltpu.VMEM((1024, 128), F32),
            pltpu.VMEM((304, 128), F32),
            pltpu.VMEM((640, 128), F32),
            pltpu.VMEM((3, 8, 128), F32),
            pltpu.VMEM((256, 1024), F32),
            pltpu.VMEM((256, 1024), F32),
            pltpu.VMEM((256, 768), F32),
            pltpu.SMEM(lengths.shape, jnp.int32),
            pltpu.SemaphoreType.DMA((2, 4)),
            pltpu.SemaphoreType.DMA,
        ],
        compiler_params=pltpu.CompilerParams(vmem_limit_bytes=62 * 1024 * 1024),
        name="conv_backward",
    )(lengths, picked, z_one, z_two, d_three, flat)


HIGH = lax.Precision.HIGH
VECTORS_ROW = 3745
TIME_ROW = 3780


def mm(a, b):
    return lax.dot_general(
        a, b, (((1,), (0,)), ((), ())), precision=HIGH, preferred_element_type=F32
    )


def mm_nt(a, b):
    return lax.dot_general(
        a, b, (((1,), (1,)), ((), ())), precision=HIGH, preferred_element_type=F32
    )


def mm_tn(a, b):
    return lax.dot_general(
        a, b, (((0,), (0,)), ((), ())), precision=HIGH, preferred_element_type=F32
    )


def dot_nt(a, b):
    return lax.dot_general(a, b, (((1,), (1,)), ((), ())), preferred_element_type=F32)


def norm_parts(stream):
    centered = stream - jnp.mean(stream, -1, keepdims=True)
    spread = jnp.mean(centered * centered, -1, keepdims=True)
    scale = lax.rsqrt(spread + 1e-05)
    return centered * scale, scale


def norm_back(grad, unit, scale, gain):
    grad = grad * gain
    inner = jnp.mean(grad * unit, -1, keepdims=True)
    return scale * (grad - jnp.mean(grad, -1, keepdims=True) - unit * inner)


def column_sum(x):
    return jnp.sum(x, axis=0, keepdims=True)


def head_places():
    number = lax.broadcasted_iota(jnp.int32, (128, 128), 0) * ACT
    lane = lax.broadcasted_iota(jnp.int32, (128, 128), 1)
    row = lax.shift_right_logical(number, 7)
    return row + jnp.where(lane < jnp.bitwise_and(number, 127), 1, 0)


def roll_rows(held, sign):
    number = lax.broadcasted_iota(jnp.int32, (128, 128), 0) * ACT
    for k in range(7):
        moved = pltpu.roll(held, (sign * (1 << k)) % 128, 1)
        held = jnp.where(jnp.bitwise_and(number, 1 << k) > 0, moved, held)
    return held


def square_head(rows):
    place = head_places()
    held = jnp.zeros((128, 128), F32)
    for k in range(ACT):
        held = jnp.where(place == k, rows[k : k + 1], held)
    held = roll_rows(held, -1)
    lane = lax.broadcasted_iota(jnp.int32, (128, 128), 1)
    return jnp.where(lane < ACT, held, 0.0)


def flat_head(grads):
    place = head_places()
    lane = lax.broadcasted_iota(jnp.int32, (128, 128), 1)
    held = roll_rows(jnp.where(lane < ACT, grads, 0.0), 1)
    rows = [
        jnp.sum(jnp.where(place == k, held, 0.0), axis=0, keepdims=True) for k in range(ACT)
    ]
    return jnp.concatenate(rows + [jnp.zeros((24 - ACT, 128), F32)], axis=0)


def unpack_split(split_ref, qkv, output, up, up_bias, down):
    lane = lax.broadcasted_iota(jnp.int32, (32, 128), 1)
    for layer in range(LAYERS):
        base = layer * 385
        kinds = [[jnp.zeros((32, 128), F32) for j in range(4)] for kind in range(3)]
        for m in range(4):
            rows = [split_ref[m, pl.ds(base + k, 32, stride=3), :] for k in range(3)]
            inside = (lane >= 32 * m) & (lane < 32 * m + 32)
            for j in range(4):
                for kind in range(3):
                    spot = j * 96 + kind * 32
                    source = rows[spot // 128]
                    shift = (32 * m - spot % 128) % 128
                    moved = pltpu.roll(source, shift, 1) if shift else source
                    kinds[kind][j] = jnp.where(inside, moved, kinds[kind][j])
            output[layer, 32 * m : 32 * m + 32] = split_ref[m, base + 96 : base + 128]
            up[layer, :, 128 * m : 128 * m + 128] = split_ref[m, base + 128 : base + 256]
            up_bias[layer, :, 128 * m : 128 * m + 128] = split_ref[m, base + 256 : base + 257]
            down[layer, 128 * m : 128 * m + 128] = split_ref[m, base + 257 : base + 385]
        for kind in range(3):
            for j in range(4):
                qkv[layer, kind, pl.ds(j, 32, stride=4), :] = kinds[kind][j]


def pack_split(out_ref, qkv, output, up, up_bias, down):
    lane = lax.broadcasted_iota(jnp.int32, (32, 128), 1)
    for layer in range(LAYERS):
        base = layer * 385
        parts = [[qkv[layer, kind, pl.ds(j, 32, stride=4), :] for j in range(4)] for kind in range(3)]
        for m in range(4):
            rows = [jnp.zeros((32, 128), F32) for k in range(3)]
            for j in range(4):
                for kind in range(3):
                    spot = j * 96 + kind * 32
                    low = spot % 128
                    shift = (low - 32 * m) % 128
                    moved = pltpu.roll(parts[kind][j], shift, 1) if shift else parts[kind][j]
                    inside = (lane >= low) & (lane < low + 32)
                    rows[spot // 128] = jnp.where(inside, moved, rows[spot // 128])
            for k in range(3):
                out_ref[m, pl.ds(base + k, 32, stride=3), :] = rows[k]
            out_ref[m, base + 96 : base + 128] = output[layer, 32 * m : 32 * m + 32]
            out_ref[m, base + 128 : base + 256] = up[layer, :, 128 * m : 128 * m + 128]
            out_ref[m, base + 256 : base + 257] = up_bias[layer, :, 128 * m : 128 * m + 128]
            out_ref[m, base + 257 : base + 385] = down[layer, 128 * m : 128 * m + 128]
    for m in range(4):
        out_ref[m, 770:784] = jnp.zeros((14, 128), F32)


def former_body(
    slots,
    used,
    lengths_ref,
    returns_ref,
    actions_ref,
    head_ref,
    z_ref,
    small,
    times_all,
    encoder,
    weights,
    d_three_ref,
    d_encoder_ref,
    d_small_ref,
    d_times_ref,
    grads,
    chances,
    kept,
    sums,
    flats,
):
    qkv, output, up, up_bias, down = weights
    d_qkv, d_output, d_up, d_up_bias, d_down = grads
    rows = 3 * slots
    wins, steps = returns_ref.shape
    vec = [small[k : k + 1] for k in range(17)]
    table = small[17 : 17 + ACT]
    slot = lax.broadcasted_iota(jnp.int32, (slots, 1), 0)
    window = jnp.zeros((slots, 1), jnp.int32)
    begin = jnp.zeros((slots, 1), jnp.int32)
    end = jnp.int32(0)
    for w in range(wins - 1):
        end = end + lengths_ref[w]
        window = jnp.where(slot >= end, w + 1, window)
        begin = jnp.where(slot >= end, end, begin)
    moment = slot - begin
    valid = slot < used
    time_lane = lax.broadcasted_iota(jnp.int32, (slots, steps), 1)
    amount = jnp.zeros((slots, 1), F32)
    action = jnp.zeros((slots, 1), jnp.int32)
    for w in range(wins):
        here = (time_lane == moment) & (window == w)
        amount = amount + jnp.sum(
            jnp.where(here, returns_ref[w : w + 1], 0.0), axis=1, keepdims=True
        )
        action = action + jnp.sum(jnp.where(here, actions_ref[w : w + 1], 0), axis=1, keepdims=True)
    lane = lax.broadcasted_iota(jnp.int32, (slots, 128), 1)
    picks = jnp.where((lane == action) & valid, 1.0, 0.0)
    reward = jnp.tanh(amount * vec[14] + vec[15])
    table = jnp.concatenate([table, jnp.zeros((128 - ACT, 128), F32)], axis=0)
    move = jnp.tanh(mm(picks, table))
    sum_state = jnp.zeros((slots, 128), F32)
    for k in range(28):
        z = jnp.where(valid, z_ref[k, 0:slots], 0.0)
        value, slope = gelu_both(z)
        d_three_ref[k, 0:slots] = slope
        high, low = two_parts(value)
        flats[0, 0:slots, k * 128 : (k + 1) * 128] = high
        flats[1, 0:slots, k * 128 : (k + 1) * 128] = low
    for part in range(2):
        sum_state = sum_state + fold_pair(dot(flats[part, 0:slots], encoder[...]))
    state = jnp.tanh(sum_state + vec[16])
    times = times_all[0:slots]
    stream = jnp.concatenate([reward + times, state + times, move + times], axis=0)

    def ids(axis):
        shape = (rows, 1) if axis == 0 else (1, rows)
        number = lax.broadcasted_iota(jnp.int32, shape, axis)
        kind = jnp.where(number >= 2 * slots, 2, jnp.where(number >= slots, 1, 0))
        return number - kind * slots, kind

    (slot_q, kind_q), (slot_k, kind_k) = ids(0), ids(1)

    def begin_of(slot_ids):
        found = jnp.zeros(slot_ids.shape, jnp.int32)
        end = jnp.int32(0)
        for w in range(wins - 1):
            end = end + lengths_ref[w]
            found = jnp.where(slot_ids >= end, end, found)
        return found

    order_q = slot_q * 3 + kind_q
    order_k = slot_k * 3 + kind_k
    allowed = (order_q >= order_k) & (slot_k >= begin_of(slot_q)) & (slot_k < used)
    head_of = lax.shift_right_logical(lax.broadcasted_iota(jnp.int32, (1, 128), 1), 4)
    heads = D // HD
    batch = 4 if slots <= HALF else 2

    def masked(x, masks):
        return jnp.concatenate([jnp.where(mask, x, jnp.zeros_like(x)) for mask in masks], axis=0)

    def unmasked(x, masks):
        held = jnp.where(masks[0], x[0:rows], 0.0)
        for k in range(1, batch):
            held = held + jnp.where(masks[k], x[k * rows : (k + 1) * rows], 0.0)
        return held

    tape = []
    for layer in range(LAYERS):
        gains = vec[6 * layer : 6 * layer + 6]
        unit_one, scale_one = norm_parts(stream)
        normed = unit_one * gains[0] + gains[1]
        wide = jnp.concatenate([qkv[layer, k] for k in range(3)], axis=1)
        mixed = mm(normed, wide)
        query_high, query_low = two_parts(mixed[:, :128] * 0.25)
        keys, values = pair(mixed[:, 128:256]), pair(mixed[:, 256:])
        kept[layer, 0, 0:rows] = query_high
        kept[layer, 1, 0:rows] = query_low
        for k in range(2):
            kept[layer, 2 + k, 0:rows] = keys[:, k * 128 : (k + 1) * 128]
            kept[layer, 4 + k, 0:rows] = values[:, k * 128 : (k + 1) * 128]
        sums[0, 0:rows] = jnp.zeros((rows, 128), F32)

        def attend(turn, carry, layer=layer):
            masks = [head_of == turn * batch + k for k in range(batch)]
            parts = [masked(kept[layer, k, 0:rows], masks) for k in range(2)]
            keys = [kept[layer, 2 + k, 0:rows] for k in range(2)]
            values = [kept[layer, 4 + k, 0:rows] for k in range(2)]
            scores = dot_nt(
                jnp.concatenate([parts[0], parts[0]], axis=1), jnp.concatenate(keys, axis=1)
            )
            scores = (scores + dot_nt(parts[1], keys[0])).reshape(batch, rows, rows)
            scores = jnp.where(allowed[None], scores, -1e30)
            peak = jnp.max(scores, -1, keepdims=True)
            chance = jnp.exp(scores - peak)
            chance = chance * (1.0 / jnp.sum(chance, -1, keepdims=True))
            high, low = two_parts(chance.reshape(batch * rows, rows))
            spot = pl.ds(pl.multiple_of(turn * (batch * rows), 64), batch * rows)
            chances[layer, 0, spot, 0:rows] = high
            chances[layer, 1, spot, 0:rows] = low
            seen = fold_pair(dot(high, jnp.concatenate(values, axis=1))) + dot(low, values[0])
            sums[0, 0:rows] += unmasked(seen, masks)
            return carry

        lax.fori_loop(0, heads // batch, attend, 0)
        context = sums[0, 0:rows]
        stream = stream + mm(context, output[layer]) + gains[4]
        unit_two, scale_two = norm_parts(stream)
        normed_two = unit_two * gains[2] + gains[3]
        inner, slope = gelu_both(mm(normed_two, up[layer]) + up_bias[layer])
        stream = stream + mm(inner, down[layer]) + gains[5]
        tape.append((unit_one, scale_one, unit_two, scale_two, inner, slope, context))
    end_stream = stream[slots : 2 * slots]
    unit, scale = norm_parts(end_stream)
    final = unit * vec[12] + vec[13]
    logits = jnp.where(lane < ACT, mm(final, head_ref[...]), -1e30)
    peak = jnp.max(logits, -1, keepdims=True)
    powers = jnp.exp(logits - peak)
    total = jnp.sum(powers, -1, keepdims=True)
    chosen = jnp.sum(jnp.where(lane == action, logits, 0.0), -1, keepdims=True)
    terms = jnp.where(valid, jnp.log(total) + peak - chosen, 0.0)
    loss = jnp.sum(terms, axis=0, keepdims=True)
    d_small_ref[72:80] = jnp.broadcast_to(loss, (8, 128))
    d_logits = jnp.where(valid, powers / total, 0.0) - picks
    d_small_ref[48:72] = flat_head(mm_tn(final, d_logits))
    d_final = mm_nt(d_logits, head_ref[...])
    d_vec = [None] * 17
    d_vec[12] = column_sum(d_final * unit)
    d_vec[13] = column_sum(d_final)
    d_end = norm_back(d_final, unit, scale, vec[12])
    blank = jnp.zeros((slots, 128), F32)
    d_stream = jnp.concatenate([blank, d_end, blank], axis=0)
    for layer in reversed(range(LAYERS)):
        unit_one, scale_one, unit_two, scale_two, inner, slope, context = tape[layer]
        gains = vec[6 * layer : 6 * layer + 6]
        d_vec[6 * layer + 5] = column_sum(d_stream)
        d_down[layer] = mm_tn(inner, d_stream)
        d_inner = mm_nt(d_stream, down[layer]) * slope
        d_up_bias[layer] = column_sum(d_inner)
        normed_two = unit_two * gains[2] + gains[3]
        d_up[layer] = mm_tn(normed_two, d_inner)
        d_normed = mm_nt(d_inner, up[layer])
        d_vec[6 * layer + 2] = column_sum(d_normed * unit_two)
        d_vec[6 * layer + 3] = column_sum(d_normed)
        d_stream = d_stream + norm_back(d_normed, unit_two, scale_two, gains[2])
        d_vec[6 * layer + 4] = column_sum(d_stream)
        d_output[layer] = mm_tn(context, d_stream)
        d_context = mm_nt(d_stream, output[layer])
        bases = d_context * context
        high, low = two_parts(d_context)
        for k in range(3):
            sums[k, 0:rows] = jnp.zeros((rows, 128), F32)
        kept[layer, 6, 0:rows] = high
        kept[layer, 7, 0:rows] = low
        sums[3, 0:rows] = bases

        def attend_back(turn, carry, layer=layer):
            masks = [head_of == turn * batch + k for k in range(batch)]
            query = [masked(kept[layer, k, 0:rows], masks) for k in range(2)]
            keys = [kept[layer, 2 + k, 0:rows] for k in range(2)]
            values = [kept[layer, 4 + k, 0:rows] for k in range(2)]
            d_seen = [masked(kept[layer, 6 + k, 0:rows], masks) for k in range(2)]
            base = jnp.sum(masked(sums[3, 0:rows], masks), -1, keepdims=True)
            spot = pl.ds(pl.multiple_of(turn * (batch * rows), 64), batch * rows)
            chance = [chances[layer, k, spot, 0:rows] for k in range(2)]
            d_chance = dot_nt(
                jnp.concatenate([d_seen[0], d_seen[0]], axis=1), jnp.concatenate(values, axis=1)
            )
            d_chance = d_chance + dot_nt(d_seen[1], values[0])
            d_scores = (chance[0].astype(F32) + chance[1].astype(F32)) * (d_chance - base)
            high, low = two_parts(d_scores)
            d_query = fold_pair(dot(high, jnp.concatenate(keys, axis=1))) + dot(low, keys[0])
            sums[0, 0:rows] += unmasked(d_query, masks)
            d_keys = fold_pair(dot_rows(high, jnp.concatenate(query, axis=1)))
            sums[1, 0:rows] += d_keys + dot_rows(low, query[0])
            d_values = fold_pair(dot_rows(chance[0], jnp.concatenate(d_seen, axis=1)))
            sums[2, 0:rows] += d_values + dot_rows(chance[1], d_seen[0])
            return carry

        lax.fori_loop(0, heads // batch, attend_back, 0)
        normed = unit_one * gains[0] + gains[1]
        d_mixed = jnp.concatenate(
            [sums[0, 0:rows] * 0.25, sums[1, 0:rows], sums[2, 0:rows]], axis=1
        )
        wide = jnp.concatenate([qkv[layer, k] for k in range(3)], axis=1)
        d_wide = mm_tn(normed, d_mixed)
        for k in range(3):
            d_qkv[layer, k] = d_wide[:, k * 128 : (k + 1) * 128]
        d_normed = mm_nt(d_mixed, wide)
        d_vec[6 * layer] = column_sum(d_normed * unit_one)
        d_vec[6 * layer + 1] = column_sum(d_normed)
        d_stream = d_stream + norm_back(d_normed, unit_one, scale_one, gains[0])
    d_reward, d_state, d_move = (d_stream[k * slots : (k + 1) * slots] for k in range(3))
    d_times_ref[0:slots] = jnp.where(valid, d_reward + d_state + d_move, 0.0)
    d_reward = d_reward * (1.0 - reward * reward)
    d_vec[14] = column_sum(d_reward * amount)
    d_vec[15] = column_sum(d_reward)
    d_move = d_move * (1.0 - move * move)
    d_small_ref[24:48] = mm_tn(picks, d_move)[0:24]
    d_state = jnp.where(valid, d_state * (1.0 - state * state), 0.0)
    d_vec[16] = column_sum(d_state)
    d_small_ref[0:24] = jnp.concatenate(d_vec + [jnp.zeros((7, 128), F32)], axis=0)
    high, low = two_parts(d_state)
    twice = jnp.concatenate([high, high], axis=1)
    both = jnp.concatenate([high, low], axis=1)
    d_flat = dot_nt(twice, encoder[...]) + dot_nt(low, encoder[:, 0:128])
    d_block = dot_rows(flats[0, 0:slots], both) + dot_rows(flats[1, 0:slots], both)
    d_block = fold_pair(d_block)
    for k in range(28):
        slope = d_three_ref[k, 0:slots]
        d_three_ref[k, 0:slots] = d_flat[:, k * 128 : (k + 1) * 128] * slope
        y, v = divmod(k, 4)
        for o in range(2):
            if 2 * v + o < 7:
                d_encoder_ref[pl.ds(y * 7 + 2 * v + o, 64, stride=49), :] = d_block[
                    k * 128 + o * 64 : k * 128 + (o + 1) * 64
                ]


def former_kernel(
    packed,
    lengths_from,
    starts_from,
    index_from,
    returns_ref,
    actions_ref,
    z_from,
    flat_ref,
    *refs,
):
    if packed:
        split_ref, refs = refs[0], refs[1:]
    else:
        given, refs = refs[:5], refs[5:]
    (d_three_to, rows_ref), refs = refs[:2], refs[2:]
    if packed:
        parts, refs = refs[:8], refs[8:]
        (d_encoder_ref, d_small_ref, d_split), refs = refs[:3], refs[3:]
        weights, grads, refs = refs[:5], refs[5:10], refs[10:]
    else:
        (d_encoder_ref, d_small_ref), grads, refs = refs[:2], refs[2:7], refs[7:]
        weights = given
    (raw, near, small, rows_raw, times_all, encoder, chances, kept, sums, flats), refs = (
        refs[:10],
        refs[10:],
    )
    z_ref, d_three_ref, head_ref, lengths_ref, starts_ref, index_ref, sem = refs
    used = jnp.int32(0)
    wins = lengths_ref.shape[0]
    scalars = [
        pltpu.make_async_copy(source, target, sem.at[wins + 4 + number])
        for number, (source, target) in enumerate(
            ((lengths_from, lengths_ref), (starts_from, starts_ref), (index_from, index_ref))
        )
    ]
    for copy in scalars:
        copy.start()
    for copy in scalars:
        copy.wait()
    for w in range(wins):
        used = used + lengths_ref[w]

    def z_copy(slots):
        return pltpu.make_async_copy(
            z_from.at[:, pl.ds(0, slots)], z_ref.at[:, pl.ds(0, slots)], sem.at[wins + 3]
        )

    def z_back(slots):
        return pltpu.make_async_copy(
            d_three_ref.at[:, pl.ds(0, slots)], d_three_to.at[:, pl.ds(0, slots)], sem.at[wins + 3]
        )

    copies = [
        pltpu.make_async_copy(flat_ref.at[pl.ds(608, 3144)], raw, sem.at[0]),
        pltpu.make_async_copy(flat_ref.at[pl.ds(3744, 48)], rows_raw.at[wins], sem.at[1]),
        pltpu.make_async_copy(
            flat_ref.at[pl.ds(7872, 24)], rows_raw.at[wins + 1, pl.ds(0, 24)], sem.at[2]
        ),
    ]
    offsets = []
    for w in range(wins):
        row = TIME_ROW + starts_ref[w]
        low = pl.multiple_of(lax.div(row, 8) * 8, 8)
        offsets.append(row - low)
        copies.append(
            pltpu.make_async_copy(
                flat_ref.at[pl.ds(low, 40)], rows_raw.at[w, pl.ds(0, 40)], sem.at[3 + w]
            )
        )
    for copy in copies:
        copy.start()

    @pl.when(used <= HALF)
    def few_states():
        z_copy(HALF).start()

    @pl.when(used > HALF)
    def many_states():
        z_copy(ROOM).start()

    if packed:
        unpack_split(split_ref, *weights)
    for copy in copies:
        copy.wait()
    lane = lanes()

    def straight(first, second):
        return jnp.where(lane < 96, pltpu.roll(first, 96, 1), pltpu.roll(second, 96, 1))

    def turn(step, carry):
        spot = pl.multiple_of(step * 64, 64)
        near[pl.ds(spot, 64)] = straight(raw[pl.ds(spot + 1, 64)], raw[pl.ds(spot + 2, 64)])
        return carry

    lax.fori_loop(0, 49, turn, 0)
    for k in range(28):
        y, v = divmod(k, 4)
        halves = []
        for o in range(2):
            if 2 * v + o < 7:
                halves.append(near[pl.ds(y * 7 + 2 * v + o, 64, stride=49), :])
            else:
                halves.append(jnp.zeros((64, 128), F32))
        encoder[k * 128 : (k + 1) * 128] = pair(jnp.concatenate(halves, axis=0))
    small[...] = straight(rows_raw[wins, 1:41], rows_raw[wins, 2:42])
    head_ref[...] = square_head(
        straight(rows_raw[wins + 1, 4:22], rows_raw[wins + 1, 5:23])
    )
    times_all[...] = jnp.zeros(times_all.shape, F32)
    begin = 0
    row = lax.broadcasted_iota(jnp.int32, (32, 1), 0)
    for w in range(wins):
        rows = straight(
            rows_raw[w, pl.ds(offsets[w], 32)], rows_raw[w, pl.ds(offsets[w] + 1, 32)]
        )
        times_all[pl.ds(begin, 32)] = jnp.where(row < lengths_ref[w], rows, 0.0)
        begin = begin + lengths_ref[w]
    rows_ref[...] = jnp.zeros(rows_ref.shape, F32)
    note = jnp.zeros((1, 128), F32)
    for w in range(wins):
        note = jnp.where(lane == w, lengths_ref[w].astype(F32), note)
        note = jnp.where(lane == wins + w, starts_ref[w].astype(F32), note)
    rows_ref[ROOM : ROOM + 1] = note
    d_small_ref[...] = jnp.zeros(d_small_ref.shape, F32)

    def run(slots):
        z_copy(slots).wait()
        former_body(
            slots,
            used,
            lengths_ref,
            returns_ref,
            actions_ref,
            head_ref,
            z_ref,
            small,
            times_all,
            encoder,
            weights,
            d_three_ref,
            d_encoder_ref,
            d_small_ref,
            rows_ref,
            grads,
            chances,
            kept,
            sums,
            flats,
        )
        z_back(slots).start()

    @pl.when(used <= HALF)
    def few():
        run(HALF)

    @pl.when(used > HALF)
    def many():
        run(ROOM)

    if packed:
        count = d_small_ref.shape[0] // 4
        pack_split(d_split, *grads)
        for k in range(4):
            parts[k][...] = d_split[jnp.bitwise_xor(index_ref[0], k)]
            e = jnp.bitwise_xor(index_ref[1], k)
            held = d_encoder_ref[pl.ds(pl.multiple_of(e * 784, 8), 784)]
            parts[4 + k][0:784] = held
            held = d_small_ref[pl.ds(pl.multiple_of(e * count, 8), count)]
            parts[4 + k][784 : 784 + count] = held

    @pl.when(used <= HALF)
    def few_end():
        z_back(HALF).wait()

    @pl.when(used > HALF)
    def many_end():
        z_back(ROOM).wait()


def former(lengths, starts, index, returns, actions, z_three, flat, weights, small_rows, packed):
    vmem = pl.BlockSpec(memory_space=pltpu.VMEM)
    hbm = pl.BlockSpec(memory_space=pltpu.HBM)
    wins = lengths.shape[0]
    canonical = [
        (LAYERS, 3, 128, 128),
        (LAYERS, 128, 128),
        (LAYERS, 128, FF),
        (LAYERS, 1, FF),
        (LAYERS, FF, 128),
    ]
    outs, out_specs = [(28, ROOM, 128), (ROOM + 8, 128)], [hbm, vmem]
    if packed:
        outs += [(784, 128)] * 4 + [(784 + small_rows // 4, 128)] * 4
        out_specs += [vmem] * 8
        scratch = [
            pltpu.VMEM((3136, 128), F32),
            pltpu.VMEM((small_rows, 128), F32),
            pltpu.VMEM((4, 784, 128), F32),
        ]
        scratch += [pltpu.VMEM(shape, F32) for shape in canonical] * 2
    else:
        outs += [(3136, 128), (small_rows, 128)] + canonical
        out_specs += [vmem] * 7
        scratch = []
    rows = 3 * ROOM
    scratch += [
        pltpu.VMEM((3144, 128), F32),
        pltpu.VMEM((3136, 128), F32),
        pltpu.VMEM((40, 128), F32),
        pltpu.VMEM((wins + 2, 48, 128), F32),
        pltpu.VMEM((ROOM + 32, 128), F32),
        pltpu.VMEM((3584, 256), BF16),
        pltpu.VMEM((LAYERS, 2, 8 * rows, rows), BF16),
        pltpu.VMEM((LAYERS, 8, rows, 128), BF16),
        pltpu.VMEM((4, rows, 128), F32),
        pltpu.VMEM((2, ROOM, 3584), BF16),
        pltpu.VMEM((28, ROOM, 128), F32),
        pltpu.VMEM((28, ROOM, 128), F32),
        pltpu.VMEM((128, 128), F32),
        pltpu.SMEM((wins,), jnp.int32),
        pltpu.SMEM((wins,), jnp.int32),
        pltpu.SMEM((2,), jnp.int32),
        pltpu.SemaphoreType.DMA((wins + 7,)),
    ]
    return pl.pallas_call(
        partial(former_kernel, packed),
        in_specs=[hbm] * 3 + [vmem] * 2 + [hbm] * 2 + [vmem] * len(weights),
        out_specs=out_specs,
        out_shape=[jax.ShapeDtypeStruct(shape, F32) for shape in outs],
        scratch_shapes=scratch,
        compiler_params=pltpu.CompilerParams(vmem_limit_bytes=62 * 1024 * 1024),
        name="transformer_step",
    )(lengths, starts, index, returns, actions, z_three, flat, *weights)


SMALL = [("vectors", 24), ("action_table", 24), ("head", 24), ("loss", 8)]
FIELD_ROWS = 8200
EARLY_ROWS = CONV_ROWS + 3136
TABLE_AT = CONV_ROWS + 3136 + 17 + ACT


def round_up(number, grain):
    return -(-number // grain) * grain


def chunk_of(tiles):
    return max(size for size in range(1, 9) if tiles % size == 0)


def mesh_bits(dp_size, mp_size):
    dp_bits = [("dp", k) for k in range(dp_size.bit_length() - 1)]
    mp_bits = [("mp", k) for k in range(mp_size.bit_length() - 1)]
    middle = (len(dp_bits) - 1) // 2
    return mp_bits[:1], mp_bits[1:], dp_bits[:middle], dp_bits[middle:]


def reduce_kernel(plan, *refs):
    mp_size, quarter, share = plan["mp_size"], plan["quarter"], plan["share"]
    split_parts, own_parts, conv_ref = refs[:mp_size], refs[mp_size : 2 * mp_size], refs[2 * mp_size]
    refs = refs[2 * mp_size + 1 :]
    (early_out, small_out, split_out, square_out), refs = refs[:4], refs[4:]
    (split_stage, own_stage, work, landing, split_total, own_total, conv_total), refs = (
        refs[:7],
        refs[7:],
    )
    tiles, tile_in, load_sem, send_sem, recv_sem, store_sem = refs
    spots = {"dp": lax.axis_index("dp"), "mp": lax.axis_index("mp")}
    cores, ys, xs, zs = plan["bits"]
    slots = iter(range(plan["copies"]))

    def value(bit):
        return lax.rem(lax.div(spots[bit[0]], 1 << bit[1]), 2)

    def turned(stage, mask):
        index = 0
        for k, bit in enumerate(stage):
            own = value(bit)
            index = index + ((1 - own) if mask & (1 << k) else own) * (1 << k)
        return index

    def partner(stage, mask):
        place = dict(spots)
        for k, bit in enumerate(stage):
            if mask & (1 << k):
                place[bit[0]] = place[bit[0]] + (1 - 2 * value(bit)) * (1 << bit[1])
        return (place["dp"], place["mp"])

    def masks_of(stage):
        return range(1, 1 << len(stage))

    def send(source, target, stage, mask):
        slot = next(slots)
        copy = pltpu.make_async_remote_copy(
            src_ref=source,
            dst_ref=target,
            send_sem=send_sem.at[slot],
            recv_sem=recv_sem.at[slot],
            device_id=partner(stage, mask),
            device_id_type=pl.DeviceIdType.MESH,
        )
        copy.start()
        return copy

    loads = []
    for k in range(mp_size):
        for parts, stage in ((own_parts, own_stage), (split_parts, split_stage)):
            copy = pltpu.make_async_copy(parts[k], stage.at[k], load_sem.at[len(loads)])
            loads.append(copy)
    conv_tiles = CONV_ROWS // 8
    target = work.at[pl.ds(plan["conv"], conv_tiles)]
    loads.append(pltpu.make_async_copy(conv_ref, target, load_sem.at[len(loads)]))
    for load in loads:
        load.start()

    def wipe(target, start, count):
        if count > 0:
            target[start : start + count] = jnp.zeros((count, 8, 128), F32)

    wipe(work, plan["conv"] + conv_tiles, plan["conv_size"] - conv_tiles)
    wipe(work, plan["split"] + quarter, plan["split_size"] - quarter)
    wipe(work, plan["own"] + quarter + share, plan["own_size"] - quarter - share)
    barrier = pltpu.get_barrier_semaphore()
    greeted = [(stage, mask) for stage in (cores + ys, xs, zs) for mask in masks_of(stage)]
    for stage, mask in greeted:
        pl.semaphore_signal(
            barrier,
            inc=1,
            device_id=partner(stage, mask),
            device_id_type=pl.DeviceIdType.MESH,
        )
    pl.semaphore_wait(barrier, len(greeted))

    def sum_into(target, start, pieces, count):
        chunk = chunk_of(count)

        def body(turn, carry):
            held = pieces[0][0][pl.ds(pieces[0][1] + turn * chunk, chunk)]
            for source, at in pieces[1:]:
                held = held + source[pl.ds(at + turn * chunk, chunk)]
            target[pl.ds(start + turn * chunk, chunk)] = held
            return carry

        lax.fori_loop(0, count // chunk, body, 0)

    class Stream:
        def __init__(self, base, size, stages, total, total_at):
            self.base, self.size, self.stages = base, size, stages
            self.total, self.at = total, total_at
            self.land = base
            self.flight = None
            self.step = 0
            self.start = base

        def reduce(self):
            if self.flight is not None:
                copies, piece, lands, keep = self.flight
                for copy in copies:
                    copy.wait()
                pieces = [(work, keep)] + [(landing, land) for land in lands]
                sum_into(work, keep, pieces, piece)
                self.base, self.size, self.flight = keep, piece, None
            if self.step < len(self.stages):
                stage = self.stages[self.step]
                piece = self.size >> len(stage)
                keep = self.base + turned(stage, 0) * piece
                copies, lands = [], []
                for mask in masks_of(stage):
                    give = self.base + turned(stage, mask) * piece
                    target = landing.at[pl.ds(self.land, piece)]
                    copies.append(send(work.at[pl.ds(give, piece)], target, stage, mask))
                    lands.append(self.land)
                    self.land += piece
                self.flight = (copies, piece, lands, keep)
                self.step += 1

        def turn(self):
            self.at = self.at + (self.base - self.start)
            sum_into(self.total, self.at, [(work, self.base)], self.size)
            self.step = 0

        def double(self):
            if self.flight is not None:
                for copy in self.flight:
                    copy.wait()
                stage = self.stages[len(self.stages) - self.step]
                self.at = self.at - turned(stage, 0) * self.size
                self.size, self.flight = self.size << len(stage), None
            if self.step < len(self.stages):
                stage = self.stages[len(self.stages) - 1 - self.step]
                region = self.total.at[pl.ds(self.at, self.size)]
                self.flight = [send(region, region, stage, mask) for mask in masks_of(stage)]
                self.step += 1

        def squares(self, keep):
            held = work[pl.ds(self.base, self.size)]
            if keep is not None:
                tile = lax.broadcasted_iota(jnp.int32, (self.size, 8, 128), 0)
                held = jnp.where(keep(tile + self.base), held, 0.0)
            return jnp.sum(held * held, axis=0)

    sharing = cores + xs
    seat = sum(value(bit) * (1 << k) for k, bit in enumerate(sharing))

    def keep_own(tile):
        place = tile - plan["own"] - quarter
        return (place < 0) | (place + seat * share < 9)

    class Quarter:
        def __init__(self, stream, offset, stages):
            self.at = stream.base - stream.start + offset
            self.size, self.stages = stream.size, stages
            self.held, self.flights, self.step = [0], [], 0
            sum_into(own_total.at[seat], self.at, [(work, stream.base)], stream.size)

        def region(self, offset):
            return own_total.at[turned(sharing, offset), pl.ds(self.at, self.size)]

        def double(self):
            if self.flights:
                for copy in self.flights:
                    copy.wait()
                stage = self.stages[self.step - 1]
                if stage[0] in sharing:
                    changed = 1 << sharing.index(stage[0])
                    self.held = self.held + [offset | changed for offset in self.held]
                else:
                    self.at = self.at - turned(stage, 0) * self.size
                    self.size <<= len(stage)
                self.flights = []
            if self.step < len(self.stages):
                stage = self.stages[self.step]
                for offset in self.held:
                    region = self.region(offset)
                    self.flights += [send(region, region, stage, mask) for mask in masks_of(stage)]
                self.step += 1

    first, second = plan["cut"]
    own = [
        Stream(plan["own"], first, [ys, zs], None, 0),
        Stream(plan["own"] + first, plan["own_size"] - first, [zs, ys], None, 0),
    ]
    split = [
        Stream(plan["split"], second, [xs, zs], split_total, 0),
        Stream(
            plan["split"] + second,
            plan["split_size"] - second,
            [zs, xs],
            split_total,
            second,
        ),
    ]
    conv = Stream(plan["conv"], plan["conv_size"], [cores, xs, zs, ys], conv_total, 0)
    for load in loads:
        load.wait()
    for at, count in ((0, quarter), (quarter, share)):
        pieces = [(own_stage.at[k], at) for k in range(mp_size)]
        sum_into(work, plan["own"] + at, pieces, count)
    for stream in own + [conv]:
        stream.reduce()
    sum_into(work, plan["split"], [(split_stage.at[k], 0) for k in range(mp_size)], quarter)
    for stream in own + [conv]:
        stream.reduce()
    for stream in split:
        stream.reduce()
    for stream in own:
        stream.reduce()
    squares = jnp.zeros((8, 128), F32)
    singles = [[bit] for bit in xs]
    quarters = [
        Quarter(own[0], 0, [zs, ys] + singles + [cores]),
        Quarter(own[1], first, [ys] + singles + [zs, cores]),
    ]
    for piece in quarters:
        piece.double()
    conv.reduce()
    for stream in split:
        stream.reduce()
    for stream in own:
        squares = squares + stream.squares(keep_own)
    for piece in quarters:
        piece.double()
    conv.reduce()
    for stream in split:
        stream.reduce()
    for piece in quarters:
        piece.double()
    conv.reduce()
    squares = squares + conv.squares(None)
    conv.turn()
    conv.double()
    for stream in split:
        squares = squares + stream.squares(None)
    tiles[0] = squares
    tile_stages = [cores + ys, xs, zs]

    def send_tiles(number):
        stage = tile_stages[number]
        spot = number * 8 - 1
        return [
            send(tiles.at[number], tile_in.at[spot + mask], stage, mask)
            for mask in masks_of(stage)
        ]

    tile_flights = send_tiles(0)
    for stream in split:
        stream.turn()
        stream.double()
    rounds = 1
    while rounds <= len(tile_stages) or conv.flight is not None or quarters[0].flights:
        for stream in quarters + [conv]:
            stream.double()
        if rounds <= len(tile_stages):
            for copy in tile_flights:
                copy.wait()
            held = tiles[rounds - 1]
            for mask in masks_of(tile_stages[rounds - 1]):
                held = held + tile_in[(rounds - 1) * 8 - 1 + mask]
            tiles[rounds] = held
            if rounds < len(tile_stages):
                tile_flights = send_tiles(rounds)
        for stream in split:
            stream.double()
        rounds += 1
    square_out[...] = tiles[len(tile_stages)]
    stores = [
        (conv_total.at[pl.ds(0, conv_tiles)], early_out.at[pl.ds(0, conv_tiles)]),
        (split_total.at[pl.ds(0, quarter)], split_out),
    ]
    for m in range(mp_size):
        rows = pl.ds(conv_tiles + m * quarter, quarter)
        stores.append((own_total.at[m, pl.ds(0, quarter)], early_out.at[rows]))
        rows = pl.ds(m * share, share)
        stores.append((own_total.at[m, pl.ds(quarter, share)], small_out.at[rows]))
    stores = [
        pltpu.make_async_copy(source, target, store_sem.at[number])
        for number, (source, target) in enumerate(stores)
    ]
    for copy in stores:
        copy.start()
    for copy in stores:
        copy.wait()


def reduce_all(split_parts, own_parts, conv, dp_size, mp_size):
    bits = mesh_bits(dp_size, mp_size)
    quarter = split_parts[0].shape[0] // 8
    share = own_parts[0].shape[0] // 8 - quarter
    own_size = round_up(quarter + share, dp_size)
    split_size = round_up(quarter, dp_size)
    conv_size = round_up(CONV_ROWS // 8, dp_size * mp_size)
    places, at = {}, 0
    for name, size in [("split", split_size), ("own", own_size), ("conv", conv_size)]:
        places[name] = at
        at += size
    cut = (
        min(round_up(own_size * 5 // 8, dp_size), own_size - dp_size),
        min(round_up(split_size * 9 // 16, dp_size), split_size - dp_size),
    )
    copies = 16 * (dp_size + mp_size) + 2 * mp_size * dp_size
    plan = dict(
        places,
        mp_size=mp_size,
        quarter=quarter,
        share=share,
        bits=bits,
        copies=copies,
        split_size=split_size,
        own_size=own_size,
        conv_size=conv_size,
        cut=cut,
    )
    vmem = pl.BlockSpec(memory_space=pltpu.VMEM)
    any_spec = pl.BlockSpec(memory_space=pl.ANY)
    arrays = [*split_parts, *own_parts, conv]
    loads = len(arrays)

    def tiled(size, *lead):
        return pltpu.VMEM((*lead, size, 8, 128), F32)

    outs = [(EARLY_ROWS // 8, 8, 128), (share * mp_size, 8, 128), (quarter, 8, 128), (8, 128)]
    results = pl.pallas_call(
        partial(reduce_kernel, plan),
        in_specs=[any_spec] * loads,
        out_specs=[any_spec, any_spec, any_spec, vmem],
        out_shape=[jax.ShapeDtypeStruct(shape, F32) for shape in outs],
        scratch_shapes=[
            tiled(quarter, mp_size),
            tiled(quarter + share, mp_size),
            tiled(at),
            tiled(at),
            tiled(split_size),
            tiled(own_size, mp_size),
            tiled(conv_size),
            pltpu.VMEM((4, 8, 128), F32),
            pltpu.VMEM((24, 8, 128), F32),
            pltpu.SemaphoreType.DMA((loads,)),
            pltpu.SemaphoreType.DMA((copies,)),
            pltpu.SemaphoreType.DMA((copies,)),
            pltpu.SemaphoreType.DMA((2 + 2 * mp_size,)),
        ],
        compiler_params=pltpu.CompilerParams(
            collective_id=1, has_side_effects=True, vmem_limit_bytes=62 * 1024 * 1024
        ),
        name="reduce_gradients",
    )(*[array.reshape(-1, 8, 128) for array in arrays])
    return [held.reshape(-1, 128) for held in results]


FLAT_ROWS = 7896
BLOCK_ROWS = 1024
LATE = 609
SPAN = 40


def adam_kernel(
    wins,
    early_ref,
    rows_ref,
    small_ref,
    split_ref,
    square_ref,
    weight_ref,
    first_ref,
    second_ref,
    split_weight_ref,
    split_first_ref,
    split_second_ref,
    new_ref,
    new_first_ref,
    new_second_ref,
    low_ref,
    split_new_ref,
    split_new_first_ref,
    split_new_second_ref,
    split_low_ref,
    norm_out,
    loss_out,
    count_out,
    split_in,
    split_out,
    field,
    rows,
    notes,
    marks,
    pulled,
    factor_ref,
    pull_sem,
    load_sem,
    split_sem,
):
    step = pl.program_id(0)
    last = pl.num_programs(0) - 1
    scalar_refs = (norm_out, loss_out, count_out)
    lane = lax.broadcasted_iota(jnp.int32, (1, 128), 1)

    def pull(block, slot):
        start = pl.multiple_of(block * BLOCK_ROWS, BLOCK_ROWS)
        return pltpu.make_async_copy(
            field.at[pl.ds(start, BLOCK_ROWS + 8)], pulled.at[slot], pull_sem.at[slot]
        )

    def update(weights, first, second, grads):
        first = beta_first * first + (1 - beta_first) * grads
        second = beta_second * second + (1 - beta_second) * grads * grads
        fix_one = 1.0 / (1 - beta_first**STEP)
        fix_two = 1.0 / (1 - beta_second**STEP)
        weights = weights - learn_rate * (
            first * fix_one / (jnp.sqrt(second * fix_two) + adam_epsilon) + weight_decay * weights
        )
        return weights, first, second

    def sum_of(tile):
        held = jnp.sum(jnp.sum(tile, axis=0, keepdims=True), axis=1, keepdims=True)
        return jnp.broadcast_to(held, (1, 128))

    slot = lax.rem(step, 2)
    split_loads = [
        pltpu.make_async_copy(ref, split_in.at[k], split_sem.at[k])
        for k, ref in enumerate((split_weight_ref, split_first_ref, split_second_ref))
    ]
    split_stores = [
        pltpu.make_async_copy(split_out.at[k], ref, split_sem.at[3 + k])
        for k, ref in enumerate((split_new_ref, split_new_first_ref, split_new_second_ref))
    ]

    @pl.when(step == 0)
    def prepare():
        for load in split_loads:
            load.start()
        load_rows = pltpu.make_async_copy(rows_ref, rows, load_sem.at[0])
        load_early = pltpu.make_async_copy(
            early_ref, field.at[pl.ds(0, EARLY_ROWS)], load_sem.at[1]
        )
        load_rows.start()
        load_early.start()
        late = FIELD_ROWS - EARLY_ROWS
        field[EARLY_ROWS:FIELD_ROWS] = jnp.zeros((late, 128), F32)
        load_rows.wait()
        stride = ROOM + 8
        devices = rows.shape[0] // stride
        notes[...] = rows[pl.ds(ROOM, devices, stride=stride), :]
        mark = pltpu.make_async_copy(notes, marks, load_sem.at[2])
        mark.start()
        mark.wait()
        place = lax.broadcasted_iota(jnp.int32, (SPAN, ROOM), 0)
        slot_of = lax.broadcasted_iota(jnp.int32, (SPAN, ROOM), 1)

        def scatter(turn, carry):
            spots, found = [], []
            for k in range(4):
                device = turn * 4 + k
                begin = jnp.int32(0)
                picks = []
                for w in range(wins):
                    length = marks[device, w].astype(jnp.int32)
                    row = marks[device, wins + w].astype(jnp.int32) + TABLE_AT
                    low = lax.div(row, 8) * 8
                    inside = (slot_of >= begin) & (slot_of < begin + length)
                    inside = inside & (place - slot_of == row - low - begin)
                    picks.append(jnp.where(inside, 1.0, 0.0).astype(BF16))
                    spots.append(low)
                    begin = begin + length
                held = pair(rows[pl.ds(pl.multiple_of(device * stride, 8), ROOM)])
                found.append(fold_pair(dot(jnp.concatenate(picks, axis=0), held)))
            for k in range(4):
                for w in range(wins):
                    spot = pl.ds(pl.multiple_of(spots[k * wins + w], 8), SPAN)
                    field[spot] = field[spot] + found[k][w * SPAN : (w + 1) * SPAN]
            return carry

        lax.fori_loop(0, devices // 4, scatter, 0)

        def fold(turn, carry):
            spot = pl.multiple_of(EARLY_ROWS + turn * 256, 8)
            held = field[pl.ds(spot, 256)]
            return carry + jnp.sum((held * held).reshape(32, 8, 128), axis=0)

        squares = lax.fori_loop(0, late // 256, fold, square_ref[...])
        at = EARLY_ROWS
        for name_at, size in [(0, 17), (24, ACT)]:
            field[at : at + size] = small_ref[name_at : name_at + size]
            at += size
        at = TABLE_AT + TSTEPS
        field[at : at + ACT] = small_ref[48 : 48 + ACT]
        lane_all = lax.broadcasted_iota(jnp.int32, notes.shape, 1)
        count = sum_of(jnp.where(lane_all < wins, notes[...], 0.0))
        seed = 1.0 / count
        norm = jnp.sqrt(sum_of(squares)) * seed
        factor = jnp.minimum(1.0, clip_limit / (norm + 1e-06)) * seed
        factor_ref[...] = jnp.broadcast_to(factor, (8, 128))
        loss = small_ref[72:73]
        for number, held in enumerate((norm, loss, count)):
            scalar_refs[number][0] = jnp.sum(jnp.where(lane == 0, held, 0.0))
        load_early.wait()
        pull(0, 0).start()

    @pl.when(step < last)
    def ahead():
        pull(step + 1, 1 - slot).start()

    @pl.when(step == 1)
    def split():
        for load in split_loads:
            load.wait()
        count = split_in.shape[1]
        outs = update(*[split_in[k] for k in range(3)], split_ref[0:count] * factor_ref[0:1])
        for k in range(3):
            split_out[k] = outs[k]
        split_low_ref[...] = outs[0].astype(BF16)
        for store in split_stores:
            store.start()

    @pl.when(step == last)
    def split_end():
        for store in split_stores:
            store.wait()

    pull(step, slot).wait()
    early = pulled[slot, 0:BLOCK_ROWS]
    own = pltpu.roll(pulled[slot, 7 : BLOCK_ROWS + 7], 32, 1)
    before = pltpu.roll(pulled[slot, 6 : BLOCK_ROWS + 6], 32, 1)
    row = lax.broadcasted_iota(jnp.int32, (BLOCK_ROWS, 1), 0) + step * BLOCK_ROWS
    grads = jnp.where(lane < 32, jnp.where(row == LATE, early, before), own)
    grads = jnp.where(row < LATE, early, grads)
    outs = update(weight_ref[...], first_ref[...], second_ref[...], grads * factor_ref[0:1])
    new_ref[...], new_first_ref[...], new_second_ref[...] = outs
    low_ref[...] = outs[0].astype(BF16)


def adam_all(early, rows, small, split_grad, square, shared, split, wins):
    grid = -(-FLAT_ROWS // BLOCK_ROWS)
    flat_spec = pl.BlockSpec((BLOCK_ROWS, 128), lambda i: (i, 0))
    split_rows = split[0].shape[0]
    devices = rows.shape[0]

    def whole(shape):
        return pl.BlockSpec(shape, lambda i: (0,) * len(shape))

    shared_out = jax.ShapeDtypeStruct((FLAT_ROWS, 128), F32)
    split_out = jax.ShapeDtypeStruct((split_rows, 128), F32)
    any_spec = pl.BlockSpec(memory_space=pl.ANY)
    return pl.pallas_call(
        partial(adam_kernel, wins),
        grid=(grid,),
        in_specs=[
            any_spec,
            any_spec,
            whole(small.shape),
            whole(split_grad.shape),
            whole((8, 128)),
            flat_spec,
            flat_spec,
            flat_spec,
            any_spec,
            any_spec,
            any_spec,
        ],
        out_specs=[flat_spec] * 4
        + [any_spec] * 3
        + [whole((split_rows, 128))]
        + [pl.BlockSpec(memory_space=pltpu.SMEM)] * 3,
        out_shape=[shared_out] * 3
        + [jax.ShapeDtypeStruct((FLAT_ROWS, 128), BF16)]
        + [split_out] * 3
        + [jax.ShapeDtypeStruct((split_rows, 128), BF16)]
        + [jax.ShapeDtypeStruct((1,), F32)] * 3,
        scratch_shapes=[
            pltpu.VMEM((3, split_rows, 128), F32),
            pltpu.VMEM((3, split_rows, 128), F32),
            pltpu.VMEM((FIELD_ROWS, 128), F32),
            pltpu.VMEM((devices * (ROOM + 8), 128), F32),
            pltpu.VMEM((devices, 128), F32),
            pltpu.SMEM((devices, 128), F32),
            pltpu.VMEM((2, BLOCK_ROWS + 8, 128), F32),
            pltpu.VMEM((8, 128), F32),
            pltpu.SemaphoreType.DMA((2,)),
            pltpu.SemaphoreType.DMA((3,)),
            pltpu.SemaphoreType.DMA((6,)),
        ],
        compiler_params=pltpu.CompilerParams(vmem_limit_bytes=62 * 1024 * 1024),
        name="adam_update",
    )(
        early,
        rows.reshape(devices * (ROOM + 8), 128),
        small,
        split_grad,
        square,
        *shared,
        *split,
    )


def per_device(
    frames,
    returns,
    actions,
    starts,
    lengths,
    shared_weights,
    shared_first,
    shared_second,
    split_weights,
    split_first,
    split_second,
):
    dp_size, mp_size = lax.axis_size("dp"), lax.axis_size("mp")
    narrow = D // mp_size
    hidden_width = FF // mp_size
    wins, steps = returns.shape
    width = split_weights.shape[0]
    split_rows = width // 128
    packed = narrow == 32
    own_rows = split_weights.reshape(split_rows, 128)
    split_all = lax.all_gather(own_rows, "mp", axis=0)
    flat = shared_weights.reshape(FLAT_ROWS, 128)
    picked, z_one, z_two, z_three = conv_forward(lengths, frames, flat)
    if packed:
        weights = [split_all]
    else:
        layers, layers_back = jax.vjp(
            lambda held: assemble(held, mp_size, narrow, hidden_width), split_all.reshape(-1)
        )
        weights = [
            jnp.stack([layer["qkv"].transpose(1, 0, 2) for layer in layers]),
            jnp.stack([layer["output"] for layer in layers]),
            jnp.stack([layer["up"] for layer in layers]),
            jnp.stack([layer["up_bias"][None] for layer in layers]),
            jnp.stack([layer["down"] for layer in layers]),
        ]
    small_rows = round_up(sum(rows for name, rows in SMALL), 8 * mp_size)
    cores, ys, xs, zs = mesh_bits(dp_size, mp_size)
    seat = jnp.bitwise_and(lax.axis_index("mp"), 1)
    seat = seat + 2 * jnp.bitwise_and(lax.axis_index("dp"), (1 << len(xs)) - 1)
    index = jnp.stack([lax.axis_index("mp"), seat])
    results = former(
        lengths, starts, index, returns, actions, z_three, flat, weights, small_rows, packed
    )
    d_three, rows = results[:2]
    rows_all = lax.all_gather(rows, ("dp", "mp"), axis=0)
    quarter = 3136 // mp_size
    if packed:
        split_parts, own_parts = results[2:6], results[6:]
    else:
        d_encoder, d_small, d_qkv, d_output, d_up, d_up_bias, d_down = results[2:]
        grad_layers = [
            dict(
                qkv=d_qkv[layer].transpose(1, 0, 2),
                output=d_output[layer],
                up=d_up[layer],
                up_bias=d_up_bias[layer, 0],
                down=d_down[layer],
            )
            for layer in range(LAYERS)
        ]
        gathered = layers_back(grad_layers)[0].reshape(mp_size, split_rows, 128)
        gathered = jnp.pad(gathered, ((0, 0), (0, quarter - split_rows), (0, 0)))
        encoder = d_encoder.reshape(mp_size, quarter, 128)
        small = d_small.reshape(mp_size, -1, 128)
        every = jnp.concatenate([encoder, small], axis=1)

        def turned(held, own):
            return [
                lax.dynamic_index_in_dim(held, jnp.bitwise_xor(own, k), 0, keepdims=False)
                for k in range(mp_size)
            ]

        split_parts, own_parts = turned(gathered, index[0]), turned(every, index[1])
    split_parts, own_parts = list(split_parts), list(own_parts)
    for k in range(1, mp_size):
        turn = [(place, place ^ k) for place in range(mp_size)]
        split_parts[k] = lax.ppermute(split_parts[k], "mp", turn)
        turn = [
            (dp * mp_size + mp, (dp ^ (k >> 1)) * mp_size + (mp ^ (k & 1)))
            for dp in range(dp_size)
            for mp in range(mp_size)
        ]
        own_parts[k] = lax.ppermute(own_parts[k], ("dp", "mp"), turn)
    d_conv = conv_backward(lengths, picked, z_one, z_two, d_three, flat)
    early, small, split_sum, square = reduce_all(
        split_parts, own_parts, d_conv, dp_size, mp_size
    )
    shared_view = [a.reshape(FLAT_ROWS, 128) for a in (shared_weights, shared_first, shared_second)]
    split_view = [a.reshape(split_rows, 128) for a in (split_weights, split_first, split_second)]
    updated = adam_all(
        early, rows_all, small, split_sum, square, shared_view, split_view, wins
    )
    shared_out = [a.reshape(-1) for a in updated[:4]]
    split_out = [a.reshape(-1) for a in updated[4:8]]
    return (*shared_out, *split_out, *[held.reshape(()) for held in updated[8:]])


def solution(mesh):
    return jax.shard_map(
        per_device,
        mesh=mesh,
        in_specs=(
            P(("dp", "mp"), None, None, None, None),
            P(("dp", "mp"), None),
            P(("dp", "mp"), None),
            P(("dp", "mp")),
            P(("dp", "mp")),
            P(),
            P(),
            P(),
            P("mp"),
            P("mp"),
            P("mp"),
        ),
        out_specs=(P(), P(), P(), P(), P("mp"), P("mp"), P("mp"), P("mp"), P(), P(), P()),
        check_vma=False,
    )
```

```python
from functools import partial
import math

import jax
import jax.numpy as jnp
from jax import lax
from jax.experimental import pallas as pl
from jax.experimental.pallas import tpu as pltpu
from jax.sharding import PartitionSpec as P

D = 128
FF = 512
ACT = 18
C1 = 32
C2 = 64
TSTEPS = 4096
LAYERS = 2
STEP = 10
HD = 16


clip_limit = 0.1
learn_rate = 0.05
beta_first = 0.9
beta_second = 0.95
adam_epsilon = 1e-08
weight_decay = 0.1


def span_layout(narrow, hidden):
    return [
        ("qkv", (D, 3, narrow)),
        ("output", (narrow, D)),
        ("up", (D, hidden)),
        ("up_bias", (hidden,)),
        ("down", (hidden, D)),
    ]


def assemble(flat, copies, narrow, hidden):
    layout = span_layout(narrow, hidden)
    width = sum((math.prod(shape) for name, shape in layout))
    blocks = flat.reshape(copies, LAYERS, width)
    layers = []
    for layer in range(LAYERS):
        offset = 0
        pieces = {}
        for name, shape in layout:
            count = math.prod(shape)
            pieces[name] = blocks[:, layer, offset : offset + count].reshape((copies,) + shape)
            offset += count
        layers.append(
            {
                "qkv": jnp.moveaxis(pieces["qkv"], 0, 2).reshape(D, 3, copies * narrow),
                "output": pieces["output"].reshape(copies * narrow, D),
                "up": jnp.moveaxis(pieces["up"], 0, 1).reshape(D, copies * hidden),
                "up_bias": pieces["up_bias"].reshape(copies * hidden),
                "down": pieces["down"].reshape(copies * hidden, D),
            }
        )
    return layers


GROUP = 16
CONV_ROWS = 616
ROOM = 128
HALF = 64
BF16 = jnp.bfloat16
F32 = jnp.float32


def gelu_value(x):
    inner = 0.7978845608028654 * (x + 0.044715 * (x * x * x))
    return 0.5 * x * (1.0 + jnp.tanh(inner))


def gelu_both(x):
    square = x * x
    turn = jnp.tanh(0.7978845608028654 * x * (1.0 + 0.044715 * square))
    half = 0.5 * (1.0 + turn)
    slope = half + 0.5 * x * (1.0 - turn * turn) * (
        0.7978845608028654 * (1.0 + 3 * 0.044715 * square)
    )
    return x * half, slope


def two_parts(x):
    high = x.astype(BF16)
    return high, (x - high.astype(F32)).astype(BF16)


def pair(x):
    return jnp.concatenate(two_parts(x), axis=-1)


def fold_pair(x):
    return x[:, :128] + x[:, 128:]


def dot(a, b):
    return lax.dot_general(a, b, (((1,), (0,)), ((), ())), preferred_element_type=F32)


def dot_rows(a, b):
    return lax.dot_general(a, b, (((0,), (0,)), ((), ())), preferred_element_type=F32)


def lanes():
    return lax.broadcasted_iota(jnp.int32, (1, 128), 1)


def conv_biases(flat_ref):
    lane = lanes()
    one = jnp.where(lane < 32, flat_ref[64:65], 0.0)
    one = one + pltpu.roll(one, 32, 1)
    one = one + pltpu.roll(one, 64, 1)
    two = jnp.where(lane < 64, pltpu.roll(flat_ref[320:321], 96, 1), 0.0)
    two = two + pltpu.roll(two, 64, 1)
    three = jnp.where(
        lane < 32,
        pltpu.roll(flat_ref[608:609], 32, 1),
        jnp.where(lane < 64, pltpu.roll(flat_ref[609:610], 32, 1), 0.0),
    )
    three = three + pltpu.roll(three, 64, 1)
    return one, two, three


def shifted(ref, start, rows, lane):
    first = pltpu.roll(ref[start : start + rows], 128 - lane, 1)
    second = pltpu.roll(ref[start + 1 : start + 1 + rows], 128 - lane, 1)
    return jnp.where(lanes() < 128 - lane, first, second)


def spread_one(flat_ref, put):
    halves = [jnp.transpose(flat_ref[pl.ds(side, 32, stride=2), :]) for side in range(2)]
    turned = jnp.concatenate(halves, axis=0)
    lane = lax.broadcasted_iota(jnp.int32, (8, 128), 1)
    row = lax.broadcasted_iota(jnp.int32, (8, 128), 0)
    low = row < 4
    column = lax.shift_right_logical(lane, 5)
    for ky in range(8):
        for c in range(4):
            held = turned[c * 64 + ky * 8 : c * 64 + ky * 8 + 8]
            wide = jnp.concatenate([held] * 4, axis=1)
            flipped = jnp.concatenate([wide[4:], wide[:4]], axis=0)
            zero = jnp.zeros((8, 128), F32)
            first = jnp.where(column == 0, wide, jnp.where((column == 1) & ~low, flipped, zero))
            second = jnp.where(
                column == 2,
                wide,
                jnp.where(((column == 1) & low) | ((column == 3) & ~low), flipped, zero),
            )
            third = jnp.where((column == 3) & low, flipped, zero)
            put(ky * 128 + c * 32, jnp.concatenate([first, second, third, zero], axis=0))


def spread_two(flat_ref, rows_ref, turned, put):
    lane = lax.broadcasted_iota(jnp.int32, (32, 128), 1)
    rows_ref[0:256] = shifted(flat_ref, 64, 256, 32)
    for j in range(4):
        block = jnp.transpose(rows_ref[pl.ds(j, 64, stride=4), :])
        turned[j * 128 : (j + 1) * 128] = jnp.concatenate([block, block], axis=1)
    for ky in range(4):
        rows = [turned[pl.ds(ky * 4 + kx, 32, stride=16)] for kx in range(4)]
        for i in range(8):
            left = rows[i] if i < 4 else jnp.zeros((32, 128), F32)
            right = rows[i - 2] if 2 <= i < 6 else jnp.zeros((32, 128), F32)
            put(ky * 256 + i * 32, jnp.where(lane < 64, left, right))


def spread_three(flat_ref, rows_ref, turned, put):
    lane = lax.broadcasted_iota(jnp.int32, (64, 128), 1)
    side = lax.broadcasted_iota(jnp.int32, (32, 128), 1) < 64
    rows_ref[0:288] = shifted(flat_ref, 320, 288, 96)
    nine = [rows_ref[pl.ds(k, 32, stride=9), :] for k in range(9)]
    flips = [pltpu.roll(nine[4 + k], 64, 1) for k in range(5)]
    for j in range(5):
        wide = min(128, 576 - j * 128)
        rows_ref[pl.ds(0, 32, stride=2), :] = nine[j]
        rows_ref[pl.ds(1, 32, stride=2), :] = (
            jnp.where(side, flips[j], flips[j + 1]) if j < 4 else flips[4]
        )
        block = jnp.transpose(rows_ref[0:64])[0:wide]
        turned[j * 128 : j * 128 + wide] = jnp.concatenate([block, block], axis=1)
    for ky in range(3):
        rows = [turned[pl.ds(ky * 3 + kx, 64, stride=9)] for kx in range(3)]
        for i in range(4):
            left = rows[i] if i < 3 else jnp.zeros((64, 128), F32)
            right = rows[i - 1] if i >= 1 else jnp.zeros((64, 128), F32)
            put(ky * 256 + i * 64, jnp.where(lane < 64, left, right))


def last_masks():
    return lanes() < 64


def conv_forward_kernel(
    lengths_from,
    frames_ref,
    shared_ref,
    picked_ref,
    z_one_ref,
    z_two_ref,
    z_three_ref,
    flat_ref,
    held,
    wide,
    picked,
    z_one,
    z_two,
    z_three,
    h_one,
    h_two,
    w_one,
    w_two,
    w_three,
    choose,
    rows_ref,
    turned,
    lengths_ref,
    frame_sem,
    out_sem,
):
    scalars = pltpu.make_async_copy(lengths_from, lengths_ref, out_sem.at[5])
    scalars.start()
    scalars.wait()
    wins = lengths_ref.shape[0]
    steps = frames_ref.shape[1]
    used = jnp.int32(0)
    for w in range(wins):
        used = used + lengths_ref[w]
    groups = lax.div(used + (GROUP - 1), GROUP)

    def frame_copy(group, spot, slot):
        state = jnp.minimum(group * GROUP + spot, used - 1)
        window, begin, end = jnp.int32(0), jnp.int32(0), jnp.int32(0)
        for w in range(wins - 1):
            end = end + lengths_ref[w]
            window = jnp.where(state >= end, w + 1, window)
            begin = jnp.where(state >= end, end, begin)
        return pltpu.make_async_copy(
            frames_ref.at[window, state - begin], held.at[slot, spot], frame_sem.at[slot, spot]
        )

    def fetch(group, slot):
        def one(spot, carry):
            frame_copy(group, spot, slot).start()
            return carry

        lax.fori_loop(0, GROUP, one, 0)

    weights = pltpu.make_async_copy(
        shared_ref.at[pl.ds(0, CONV_ROWS)], flat_ref, out_sem.at[4]
    )
    weights.start()
    fetch(0, 0)
    h_one[...] = jnp.zeros(h_one.shape, BF16)

    def put_one(row, block):
        w_one[row : row + 32] = pair(block)

    def put_two(row, block):
        w_two[row : row + 32] = pair(block)

    def put_three(row, block):
        w_three[row : row + 64] = pair(block)

    weights.wait()
    spread_one(flat_ref, put_one)
    spread_two(flat_ref, rows_ref, turned, put_two)
    spread_three(flat_ref, rows_ref, turned, put_three)
    bias_one, bias_two, bias_three = conv_biases(flat_ref)
    row = lax.broadcasted_iota(jnp.int32, (128, 640), 0)
    column = lax.broadcasted_iota(jnp.int32, (128, 640), 1)
    place = jnp.bitwise_and(column, 31)
    channel = jnp.bitwise_and(lax.shift_right_logical(column, 5), 3)
    block = lax.shift_right_logical(column, 7)
    right = (row == 16 * block + place) & (place < 20)
    for c in range(4):
        choose[c * 128 : (c + 1) * 128] = jnp.where(right & (channel == c), 1.0, 0.0).astype(BF16)

    def one_group(group, carry):
        slot = lax.rem(group, 2)

        @pl.when(group + 1 < groups)
        def ahead():
            fetch(group + 1, 1 - slot)

        def lay(step, carry):
            spots = [step * 4 + k for k in range(4)]
            for spot in spots:
                frame_copy(group, spot, slot).wait()
            for spot in spots:
                image = held[slot, spot].astype(F32).reshape(336, 84)
                image = jnp.concatenate([image, jnp.zeros((336, 44), F32)], axis=1)
                wide[pl.ds(spot, 336, stride=GROUP), :] = image
            return carry

        lax.fori_loop(0, GROUP // 4, lay, 0)
        for part in range(3):
            rows = wide[part * 1792 : (part + 1) * 1792].reshape(28, 4, GROUP, 128)
            rows = [rows[:, c].reshape(448, 128).astype(BF16) for c in range(4)]
            result = dot(jnp.concatenate(rows, axis=1), choose[...])
            picked[part * 7 : (part + 1) * 7] = result.astype(BF16).reshape(7, 4, GROUP, 640)
        keep_picked = pltpu.make_async_copy(picked, picked_ref.at[group], out_sem.at[0])
        keep_picked.start()
        for q in range(5):
            pieces = [
                picked[j : j + 20, b, :, q * 128 : (q + 1) * 128].reshape(20 * GROUP, 128)
                for j in range(2)
                for b in range(4)
            ]
            z = fold_pair(dot(jnp.concatenate(pieces, axis=1), w_one[...])) + bias_one
            z_one[:, :, q] = z.reshape(10, 2, GROUP, 128)
            high, low = two_parts(gelu_value(z))
            h_one[0, :, :, q] = high.reshape(10, 2, GROUP, 128)
            h_one[1, :, :, q] = low.reshape(10, 2, GROUP, 128)
        keep_one = pltpu.make_async_copy(z_one, z_one_ref.at[group], out_sem.at[1])
        keep_one.start()
        total = jnp.zeros((45 * GROUP, 128), F32)
        for part in range(2):
            pieces = []
            for j in range(2):
                for b in range(2):
                    pieces.append(h_one[part, j : j + 9, b, 0:5].reshape(45 * GROUP, 128))
                    pieces.append(h_one[part, j : j + 9, b, 1:6].reshape(45 * GROUP, 128))
            total = total + fold_pair(dot(jnp.concatenate(pieces, axis=1), w_two[...]))
        z = (total + bias_two).reshape(9, 5, GROUP, 128)
        z_two[...] = z
        h = gelu_value(z)
        high, low = two_parts(h)
        h_two[0] = high
        h_two[1] = low
        edge = jnp.where(last_masks(), h[:, 4].reshape(9 * GROUP, 128), 0.0)
        high, low = two_parts(edge)
        h_two[0, :, 4] = high.reshape(9, GROUP, 128)
        h_two[1, :, 4] = low.reshape(9, GROUP, 128)
        keep_two = pltpu.make_async_copy(z_two, z_two_ref.at[group], out_sem.at[2])
        keep_two.start()
        total = jnp.zeros((28 * GROUP, 128), F32)
        for part in range(2):
            pieces = []
            for ky in range(3):
                pieces.append(h_two[part, ky : ky + 7, 0:4].reshape(28 * GROUP, 128))
                pieces.append(h_two[part, ky : ky + 7, 1:5].reshape(28 * GROUP, 128))
            total = total + fold_pair(dot(jnp.concatenate(pieces, axis=1), w_three[...]))
        z_three[...] = (total + bias_three).reshape(28, GROUP, 128)
        spot = pl.multiple_of(group * GROUP, GROUP)
        keep_three = pltpu.make_async_copy(
            z_three, z_three_ref.at[:, pl.ds(spot, GROUP)], out_sem.at[3]
        )
        keep_three.start()
        keep_picked.wait()
        keep_one.wait()
        keep_two.wait()
        keep_three.wait()
        return carry

    lax.fori_loop(0, groups, one_group, 0)


def conv_forward(lengths, frames, flat):
    most = ROOM // GROUP
    any_spec = pl.BlockSpec(memory_space=pl.ANY)
    hbm = pl.BlockSpec(memory_space=pltpu.HBM)
    return pl.pallas_call(
        conv_forward_kernel,
        in_specs=[
            any_spec,
            any_spec,
            any_spec,
        ],
        out_specs=[hbm] * 4,
        out_shape=[
            jax.ShapeDtypeStruct((most, 21, 4, GROUP, 640), BF16),
            jax.ShapeDtypeStruct((most, 10, 2, 5, GROUP, 128), F32),
            jax.ShapeDtypeStruct((most, 9, 5, GROUP, 128), F32),
            jax.ShapeDtypeStruct((28, ROOM, 128), F32),
        ],
        scratch_shapes=[
            pltpu.VMEM((CONV_ROWS, 128), F32),
            pltpu.VMEM((2, GROUP, 84, 4, 84), BF16),
            pltpu.VMEM((336 * GROUP, 128), F32),
            pltpu.VMEM((21, 4, GROUP, 640), BF16),
            pltpu.VMEM((10, 2, 5, GROUP, 128), F32),
            pltpu.VMEM((9, 5, GROUP, 128), F32),
            pltpu.VMEM((28, GROUP, 128), F32),
            pltpu.VMEM((2, 10, 2, 6, GROUP, 128), BF16),
            pltpu.VMEM((2, 9, 5, GROUP, 128), BF16),
            pltpu.VMEM((1024, 256), BF16),
            pltpu.VMEM((1024, 256), BF16),
            pltpu.VMEM((768, 256), BF16),
            pltpu.VMEM((512, 640), BF16),
            pltpu.VMEM((288, 128), F32),
            pltpu.VMEM((576, 128), F32),
            pltpu.SMEM(lengths.shape, jnp.int32),
            pltpu.SemaphoreType.DMA((2, GROUP)),
            pltpu.SemaphoreType.DMA((6,)),
        ],
        compiler_params=pltpu.CompilerParams(vmem_limit_bytes=62 * 1024 * 1024),
        name="conv_forward",
    )(lengths, frames.transpose(0, 1, 3, 2, 4), flat)


def gather_one(total, out):
    lane = lax.broadcasted_iota(jnp.int32, (32, 128), 1)
    halves = [jnp.zeros((32, 128), F32) for side in range(2)]
    for ky in range(8):
        held = total[0:128, ky * 128 : (ky + 1) * 128] + total[128:256, ky * 128 : (ky + 1) * 128]
        summed = held[0:32]
        for o in range(1, 4):
            summed = summed + pltpu.roll(held[32 * o : 32 * o + 32], 128 - 4 * o, 1)
        for c in range(4):
            spot = (c % 2) * 64 + ky * 8
            shift = (spot - c * 32) % 128
            moved = pltpu.roll(summed, shift, 1) if shift else summed
            inside = (lane >= spot) & (lane < spot + 8)
            halves[c // 2] = halves[c // 2] + jnp.where(inside, moved, 0.0)
    for side in range(2):
        out[pl.ds(side, 32, stride=2), :] = halves[side]


def gather_two(total, turned, rows_ref, out):
    lane = lax.broadcasted_iota(jnp.int32, (64, 128), 1)
    for ky in range(4):
        near = total[0:128, ky * 256 : ky * 256 + 128] + total[128:256, ky * 256 : ky * 256 + 128]
        far = (
            total[0:128, ky * 256 + 128 : ky * 256 + 256]
            + total[128:256, ky * 256 + 128 : ky * 256 + 256]
        )
        summed = near[0:64] + jnp.where(
            lane < 64, pltpu.roll(near[64:128], 64, 1), pltpu.roll(far[64:128], 64, 1)
        )
        flipped = jnp.transpose(jnp.concatenate([summed, jnp.zeros((64, 128), F32)], axis=0))
        for kx in range(4):
            turned[pl.ds(ky * 4 + kx, 32, stride=16), :] = flipped[kx * 32 : (kx + 1) * 32]
    rows_ref[0:8] = jnp.zeros((8, 128), F32)
    rows_ref[264:272] = jnp.zeros((8, 128), F32)
    for j in range(4):
        block = jnp.transpose(turned[j * 128 : (j + 1) * 128])[0:64]
        rows_ref[pl.ds(8 + j, 64, stride=4), :] = block
    own = pltpu.roll(rows_ref[8:265], 32, 1)
    before = pltpu.roll(rows_ref[7:264], 32, 1)
    out[64:321] = jnp.where(lanes() >= 32, own, before)


def gather_three(total, turned, rows_ref, out):
    lane = lax.broadcasted_iota(jnp.int32, (64, 128), 1)
    side = lax.broadcasted_iota(jnp.int32, (32, 128), 1) < 64
    blank = jnp.zeros((64, 128), F32)
    for ky in range(3):
        near = total[0:128, ky * 256 : ky * 256 + 128] + total[128:256, ky * 256 : ky * 256 + 128]
        far = (
            total[0:128, ky * 256 + 128 : ky * 256 + 256]
            + total[128:256, ky * 256 + 128 : ky * 256 + 256]
        )
        first = near[0:64] + jnp.where(
            lane < 64, pltpu.roll(near[64:128], 64, 1), pltpu.roll(far[64:128], 64, 1)
        )
        second = far[0:64] + pltpu.roll(far[64:128], 64, 1)
        flipped = jnp.transpose(jnp.concatenate([first, blank], axis=0))
        turned[pl.ds(ky * 3, 64, stride=9), :] = flipped[0:64]
        turned[pl.ds(ky * 3 + 1, 64, stride=9), :] = flipped[64:128]
        flipped = jnp.transpose(jnp.concatenate([second, blank], axis=0))
        turned[pl.ds(ky * 3 + 2, 64, stride=9), :] = flipped[0:64]
    turned[576:640] = blank
    evens, odds = [], []
    for j in range(5):
        rows_ref[0:64] = jnp.transpose(turned[j * 128 : (j + 1) * 128])[0:64]
        evens.append(rows_ref[pl.ds(0, 32, stride=2), :])
        odds.append(pltpu.roll(rows_ref[pl.ds(1, 32, stride=2), :], 64, 1))
    rows_ref[0:8] = jnp.zeros((8, 128), F32)
    rows_ref[296:304] = jnp.zeros((8, 128), F32)
    for k in range(9):
        if k < 4:
            held = evens[k]
        elif k == 4:
            held = jnp.where(side, evens[4], odds[0])
        else:
            held = jnp.where(side, odds[k - 5], odds[k - 4])
        rows_ref[pl.ds(8 + k, 32, stride=9), :] = held
    own = pltpu.roll(rows_ref[8:297], 96, 1)
    before = pltpu.roll(rows_ref[7:296], 96, 1)
    edge = out[320:321]
    out[320:609] = jnp.where(lanes() >= 96, own, before)
    out[320:321] = out[320:321] + edge


def conv_backward_kernel(
    lengths_from,
    picked_ref,
    z_one_ref,
    z_two_ref,
    d_three_ref,
    shared_ref,
    flat_out,
    flat_ref,
    picked,
    z_one,
    z_two,
    d_three,
    h_one,
    h_two,
    slope_one,
    pad_three,
    pad_two,
    d_one,
    v_two,
    v_three,
    spread,
    rows_ref,
    turned,
    bias_out,
    total_one,
    total_two,
    total_three,
    lengths_ref,
    load_sem,
    weight_sem,
):
    scalars = pltpu.make_async_copy(lengths_from, lengths_ref, weight_sem)
    scalars.start()
    scalars.wait()
    used = jnp.int32(0)
    for w in range(lengths_ref.shape[0]):
        used = used + lengths_ref[w]
    groups = lax.div(used + (GROUP - 1), GROUP)

    def loads(group, slot):
        spot = pl.multiple_of(group * GROUP, GROUP)
        return [
            pltpu.make_async_copy(picked_ref.at[group], picked.at[slot], load_sem.at[slot, 0]),
            pltpu.make_async_copy(z_one_ref.at[group], z_one.at[slot], load_sem.at[slot, 1]),
            pltpu.make_async_copy(z_two_ref.at[group], z_two.at[slot], load_sem.at[slot, 2]),
            pltpu.make_async_copy(
                d_three_ref.at[:, pl.ds(spot, GROUP)], d_three.at[slot], load_sem.at[slot, 3]
            ),
        ]

    weights = pltpu.make_async_copy(
        shared_ref.at[pl.ds(0, CONV_ROWS)], flat_ref, weight_sem
    )
    weights.start()
    for load in loads(0, 0):
        load.start()

    def put_two(row, block):
        spread[row : row + 32] = block

    def put_three(row, block):
        spread[row : row + 64] = block

    weights.wait()
    spread_two(flat_ref, rows_ref, turned, put_two)
    for b in range(2):
        for j in range(2):
            for side in range(2):
                source = (2 * j + b) * 256 + side * 128
                target = (b * 2 + j) * 256 + side * 128
                v_two[target : target + 128] = pair(jnp.transpose(spread[source : source + 128]))
    spread_three(flat_ref, rows_ref, turned, put_three)
    for part in range(6):
        rows = pl.ds(part * 128, 128)
        v_three[rows] = pair(jnp.transpose(spread[rows]))
    total_one[...] = jnp.zeros(total_one.shape, F32)
    total_two[...] = jnp.zeros(total_two.shape, F32)
    total_three[...] = jnp.zeros(total_three.shape, F32)
    bias_out[...] = jnp.zeros(bias_out.shape, F32)
    h_one[...] = jnp.zeros(h_one.shape, BF16)
    pad_two[...] = jnp.zeros(pad_two.shape, BF16)
    pad_three[...] = jnp.zeros(pad_three.shape, BF16)

    def fold(rows):
        return jnp.sum(rows.reshape(-1, 8, 128), axis=0)

    def one_group(group, carry):
        slot = lax.rem(group, 2)

        @pl.when(group + 1 < groups)
        def ahead():
            for load in loads(group + 1, 1 - slot):
                load.start()

        for load in loads(group, slot):
            load.wait()
        rows = d_three[slot].reshape(28 * GROUP, 128)
        bias_out[2] += fold(rows)
        both = pair(rows)
        pad_three[0, 2:9, 1:5] = both[:, :128].reshape(7, 4, GROUP, 128)
        pad_three[1, 2:9, 1:5] = both[:, 128:].reshape(7, 4, GROUP, 128)
        h, slope_two = gelu_both(z_two[slot])
        high, low = two_parts(h)
        h_two[0] = high
        h_two[1] = low
        edge = jnp.where(last_masks(), h[:, 4].reshape(9 * GROUP, 128), 0.0)
        high, low = two_parts(edge)
        h_two[0, :, 4] = high.reshape(9, GROUP, 128)
        h_two[1, :, 4] = low.reshape(9, GROUP, 128)
        for part in range(2):
            pieces = []
            for ky in range(3):
                pieces.append(h_two[part, ky : ky + 7, 0:4].reshape(28 * GROUP, 128))
                pieces.append(h_two[part, ky : ky + 7, 1:5].reshape(28 * GROUP, 128))
            total_three[...] += dot_rows(both, jnp.concatenate(pieces, axis=1))
        spill = jnp.zeros((45 * GROUP, 128), F32)
        for part in range(2):
            pieces = []
            for ky in range(3):
                pieces.append(pad_three[part, 2 - ky : 11 - ky, 1:6].reshape(45 * GROUP, 128))
                pieces.append(pad_three[part, 2 - ky : 11 - ky, 0:5].reshape(45 * GROUP, 128))
            spill = spill + fold_pair(dot(jnp.concatenate(pieces, axis=1), v_three[...]))
        rows = spill * slope_two.reshape(45 * GROUP, 128)
        bias_out[1] += fold(rows)
        both = pair(rows)
        pad_two[0, 1:10, 1:6] = both[:, :128].reshape(9, 5, GROUP, 128)
        pad_two[1, 1:10, 1:6] = both[:, 128:].reshape(9, 5, GROUP, 128)
        for q in range(5):
            h, slope = gelu_both(z_one[slot, :, :, q])
            high, low = two_parts(h)
            h_one[0, :, :, q] = high
            h_one[1, :, :, q] = low
            slope_one[:, :, q] = slope
        for part in range(2):
            pieces = []
            for j in range(2):
                for b in range(2):
                    pieces.append(h_one[part, j : j + 9, b, 0:5].reshape(45 * GROUP, 128))
                    pieces.append(h_one[part, j : j + 9, b, 1:6].reshape(45 * GROUP, 128))
            total_two[...] += dot_rows(both, jnp.concatenate(pieces, axis=1))
        for b in range(2):
            spill = jnp.zeros((50 * GROUP, 128), F32)
            for part in range(2):
                pieces = []
                for j in range(2):
                    pieces.append(pad_two[part, 1 - j : 11 - j, 1:6].reshape(50 * GROUP, 128))
                    pieces.append(pad_two[part, 1 - j : 11 - j, 0:5].reshape(50 * GROUP, 128))
                spill = spill + fold_pair(
                    dot(jnp.concatenate(pieces, axis=1), v_two[b * 512 : (b + 1) * 512])
                )
            rows = spill * slope_one[:, b].reshape(50 * GROUP, 128)
            bias_out[0] += fold(rows)
            d_one[:, b] = pair(rows).reshape(10, 5, GROUP, 256)
        for q in range(5):
            pieces = [
                picked[slot, j : j + 20, b, :, q * 128 : (q + 1) * 128].reshape(20 * GROUP, 128)
                for j in range(2)
                for b in range(4)
            ]
            total_one[...] += dot_rows(
                d_one[:, :, q].reshape(20 * GROUP, 256), jnp.concatenate(pieces, axis=1)
            )
        return carry

    lax.fori_loop(0, groups, one_group, 0)
    gather_one(total_one, flat_out)
    gather_two(total_two, turned, rows_ref, flat_out)
    gather_three(total_three, turned, rows_ref, flat_out)
    lane = lanes()
    sums = [jnp.sum(bias_out[k], axis=0, keepdims=True) for k in range(3)]
    sums[0] = sums[0] + pltpu.roll(sums[0], 64, 1)
    sums[0] = sums[0] + pltpu.roll(sums[0], 32, 1)
    sums[1] = jnp.where(lane < 64, sums[1] + pltpu.roll(sums[1], 64, 1), 0.0)
    sums[2] = jnp.where(lane < 64, sums[2] + pltpu.roll(sums[2], 64, 1), 0.0)
    flat_out[64:65] = jnp.where(lane < 32, sums[0], flat_out[64:65])
    flat_out[320:321] = flat_out[320:321] + pltpu.roll(sums[1], 32, 1)
    late = pltpu.roll(sums[2], 96, 1)
    flat_out[608:609] = flat_out[608:609] + jnp.where(lane >= 96, late, 0.0)
    row = lax.broadcasted_iota(jnp.int32, (7, 128), 0)
    flat_out[609:616] = jnp.where((row == 0) & (lane < 32), late, 0.0)


def conv_backward(lengths, picked, z_one, z_two, d_three, flat):
    hbm = pl.BlockSpec(memory_space=pltpu.HBM)
    vmem = pl.BlockSpec(memory_space=pltpu.VMEM)
    return pl.pallas_call(
        conv_backward_kernel,
        in_specs=[hbm] * 6,
        out_specs=vmem,
        out_shape=jax.ShapeDtypeStruct((CONV_ROWS, 128), F32),
        scratch_shapes=[
            pltpu.VMEM((CONV_ROWS, 128), F32),
            pltpu.VMEM((2, 21, 4, GROUP, 640), BF16),
            pltpu.VMEM((2, 10, 2, 5, GROUP, 128), F32),
            pltpu.VMEM((2, 9, 5, GROUP, 128), F32),
            pltpu.VMEM((2, 28, GROUP, 128), F32),
            pltpu.VMEM((2, 10, 2, 6, GROUP, 128), BF16),
            pltpu.VMEM((2, 9, 5, GROUP, 128), BF16),
            pltpu.VMEM((10, 2, 5, GROUP, 128), F32),
            pltpu.VMEM((2, 11, 6, GROUP, 128), BF16),
            pltpu.VMEM((2, 11, 6, GROUP, 128), BF16),
            pltpu.VMEM((10, 2, 5, GROUP, 256), BF16),
            pltpu.VMEM((1024, 256), BF16),
            pltpu.VMEM((768, 256), BF16),
            pltpu.VMEM((1024, 128), F32),
            pltpu.VMEM((304, 128), F32),
            pltpu.VMEM((640, 128), F32),
            pltpu.VMEM((3, 8, 128), F32),
            pltpu.VMEM((256, 1024), F32),
            pltpu.VMEM((256, 1024), F32),
            pltpu.VMEM((256, 768), F32),
            pltpu.SMEM(lengths.shape, jnp.int32),
            pltpu.SemaphoreType.DMA((2, 4)),
            pltpu.SemaphoreType.DMA,
        ],
        compiler_params=pltpu.CompilerParams(vmem_limit_bytes=62 * 1024 * 1024),
        name="conv_backward",
    )(lengths, picked, z_one, z_two, d_three, flat)


HIGH = lax.Precision.HIGH
VECTORS_ROW = 3745
TIME_ROW = 3780


def mm(a, b):
    return lax.dot_general(
        a, b, (((1,), (0,)), ((), ())), precision=HIGH, preferred_element_type=F32
    )


def mm_nt(a, b):
    return lax.dot_general(
        a, b, (((1,), (1,)), ((), ())), precision=HIGH, preferred_element_type=F32
    )


def mm_tn(a, b):
    return lax.dot_general(
        a, b, (((0,), (0,)), ((), ())), precision=HIGH, preferred_element_type=F32
    )


def dot_nt(a, b):
    return lax.dot_general(a, b, (((1,), (1,)), ((), ())), preferred_element_type=F32)


def norm_parts(stream):
    centered = stream - jnp.mean(stream, -1, keepdims=True)
    spread = jnp.mean(centered * centered, -1, keepdims=True)
    scale = lax.rsqrt(spread + 1e-05)
    return centered * scale, scale


def norm_back(grad, unit, scale, gain):
    grad = grad * gain
    inner = jnp.mean(grad * unit, -1, keepdims=True)
    return scale * (grad - jnp.mean(grad, -1, keepdims=True) - unit * inner)


def column_sum(x):
    return jnp.sum(x, axis=0, keepdims=True)


def head_places():
    number = lax.broadcasted_iota(jnp.int32, (128, 128), 0) * ACT
    lane = lax.broadcasted_iota(jnp.int32, (128, 128), 1)
    row = lax.shift_right_logical(number, 7)
    return row + jnp.where(lane < jnp.bitwise_and(number, 127), 1, 0)


def roll_rows(held, sign):
    number = lax.broadcasted_iota(jnp.int32, (128, 128), 0) * ACT
    for k in range(7):
        moved = pltpu.roll(held, (sign * (1 << k)) % 128, 1)
        held = jnp.where(jnp.bitwise_and(number, 1 << k) > 0, moved, held)
    return held


def square_head(rows):
    place = head_places()
    held = jnp.zeros((128, 128), F32)
    for k in range(ACT):
        held = jnp.where(place == k, rows[k : k + 1], held)
    held = roll_rows(held, -1)
    lane = lax.broadcasted_iota(jnp.int32, (128, 128), 1)
    return jnp.where(lane < ACT, held, 0.0)


def flat_head(grads):
    place = head_places()
    lane = lax.broadcasted_iota(jnp.int32, (128, 128), 1)
    held = roll_rows(jnp.where(lane < ACT, grads, 0.0), 1)
    rows = [
        jnp.sum(jnp.where(place == k, held, 0.0), axis=0, keepdims=True) for k in range(ACT)
    ]
    return jnp.concatenate(rows + [jnp.zeros((24 - ACT, 128), F32)], axis=0)


def unpack_split(split_ref, qkv, output, up, up_bias, down):
    lane = lax.broadcasted_iota(jnp.int32, (32, 128), 1)
    for layer in range(LAYERS):
        base = layer * 385
        kinds = [[jnp.zeros((32, 128), F32) for j in range(4)] for kind in range(3)]
        for m in range(4):
            rows = [split_ref[m, pl.ds(base + k, 32, stride=3), :] for k in range(3)]
            inside = (lane >= 32 * m) & (lane < 32 * m + 32)
            for j in range(4):
                for kind in range(3):
                    spot = j * 96 + kind * 32
                    source = rows[spot // 128]
                    shift = (32 * m - spot % 128) % 128
                    moved = pltpu.roll(source, shift, 1) if shift else source
                    kinds[kind][j] = jnp.where(inside, moved, kinds[kind][j])
            output[layer, 32 * m : 32 * m + 32] = split_ref[m, base + 96 : base + 128]
            up[layer, :, 128 * m : 128 * m + 128] = split_ref[m, base + 128 : base + 256]
            up_bias[layer, :, 128 * m : 128 * m + 128] = split_ref[m, base + 256 : base + 257]
            down[layer, 128 * m : 128 * m + 128] = split_ref[m, base + 257 : base + 385]
        for kind in range(3):
            for j in range(4):
                qkv[layer, kind, pl.ds(j, 32, stride=4), :] = kinds[kind][j]


def pack_split(out_ref, qkv, output, up, up_bias, down):
    lane = lax.broadcasted_iota(jnp.int32, (32, 128), 1)
    for layer in range(LAYERS):
        base = layer * 385
        parts = [[qkv[layer, kind, pl.ds(j, 32, stride=4), :] for j in range(4)] for kind in range(3)]
        for m in range(4):
            rows = [jnp.zeros((32, 128), F32) for k in range(3)]
            for j in range(4):
                for kind in range(3):
                    spot = j * 96 + kind * 32
                    low = spot % 128
                    shift = (low - 32 * m) % 128
                    moved = pltpu.roll(parts[kind][j], shift, 1) if shift else parts[kind][j]
                    inside = (lane >= low) & (lane < low + 32)
                    rows[spot // 128] = jnp.where(inside, moved, rows[spot // 128])
            for k in range(3):
                out_ref[m, pl.ds(base + k, 32, stride=3), :] = rows[k]
            out_ref[m, base + 96 : base + 128] = output[layer, 32 * m : 32 * m + 32]
            out_ref[m, base + 128 : base + 256] = up[layer, :, 128 * m : 128 * m + 128]
            out_ref[m, base + 256 : base + 257] = up_bias[layer, :, 128 * m : 128 * m + 128]
            out_ref[m, base + 257 : base + 385] = down[layer, 128 * m : 128 * m + 128]
    for m in range(4):
        out_ref[m, 770:784] = jnp.zeros((14, 128), F32)


def former_body(
    slots,
    used,
    lengths_ref,
    returns_ref,
    actions_ref,
    head_ref,
    z_ref,
    small,
    times_all,
    encoder,
    weights,
    d_three_ref,
    d_encoder_ref,
    d_small_ref,
    d_times_ref,
    grads,
    chances,
    kept,
    sums,
    flats,
):
    qkv, output, up, up_bias, down = weights
    d_qkv, d_output, d_up, d_up_bias, d_down = grads
    rows = 3 * slots
    wins, steps = returns_ref.shape
    vec = [small[k : k + 1] for k in range(17)]
    table = small[17 : 17 + ACT]
    slot = lax.broadcasted_iota(jnp.int32, (slots, 1), 0)
    window = jnp.zeros((slots, 1), jnp.int32)
    begin = jnp.zeros((slots, 1), jnp.int32)
    end = jnp.int32(0)
    for w in range(wins - 1):
        end = end + lengths_ref[w]
        window = jnp.where(slot >= end, w + 1, window)
        begin = jnp.where(slot >= end, end, begin)
    moment = slot - begin
    valid = slot < used
    time_lane = lax.broadcasted_iota(jnp.int32, (slots, steps), 1)
    amount = jnp.zeros((slots, 1), F32)
    action = jnp.zeros((slots, 1), jnp.int32)
    for w in range(wins):
        here = (time_lane == moment) & (window == w)
        amount = amount + jnp.sum(
            jnp.where(here, returns_ref[w : w + 1], 0.0), axis=1, keepdims=True
        )
        action = action + jnp.sum(jnp.where(here, actions_ref[w : w + 1], 0), axis=1, keepdims=True)
    lane = lax.broadcasted_iota(jnp.int32, (slots, 128), 1)
    picks = jnp.where((lane == action) & valid, 1.0, 0.0)
    reward = jnp.tanh(amount * vec[14] + vec[15])
    table = jnp.concatenate([table, jnp.zeros((128 - ACT, 128), F32)], axis=0)
    move = jnp.tanh(mm(picks, table))
    sum_state = jnp.zeros((slots, 128), F32)
    for k in range(28):
        z = jnp.where(valid, z_ref[k, 0:slots], 0.0)
        high, low = two_parts(gelu_value(z))
        flats[0, 0:slots, k * 128 : (k + 1) * 128] = high
        flats[1, 0:slots, k * 128 : (k + 1) * 128] = low
    for part in range(2):
        sum_state = sum_state + fold_pair(dot(flats[part, 0:slots], encoder[...]))
    state = jnp.tanh(sum_state + vec[16])
    times = times_all[0:slots]
    stream = jnp.concatenate([reward + times, state + times, move + times], axis=0)

    def ids(axis):
        shape = (rows, 1) if axis == 0 else (1, rows)
        number = lax.broadcasted_iota(jnp.int32, shape, axis)
        kind = jnp.where(number >= 2 * slots, 2, jnp.where(number >= slots, 1, 0))
        return number - kind * slots, kind

    (slot_q, kind_q), (slot_k, kind_k) = ids(0), ids(1)

    def begin_of(slot_ids):
        found = jnp.zeros(slot_ids.shape, jnp.int32)
        end = jnp.int32(0)
        for w in range(wins - 1):
            end = end + lengths_ref[w]
            found = jnp.where(slot_ids >= end, end, found)
        return found

    order_q = slot_q * 3 + kind_q
    order_k = slot_k * 3 + kind_k
    allowed = (order_q >= order_k) & (slot_k >= begin_of(slot_q)) & (slot_k < used)
    head_of = lax.shift_right_logical(lax.broadcasted_iota(jnp.int32, (1, 128), 1), 4)
    heads = D // HD
    batch = 4 if slots <= HALF else 2

    def masked(x, masks):
        return jnp.concatenate([jnp.where(mask, x, jnp.zeros_like(x)) for mask in masks], axis=0)

    def unmasked(x, masks):
        held = jnp.where(masks[0], x[0:rows], 0.0)
        for k in range(1, batch):
            held = held + jnp.where(masks[k], x[k * rows : (k + 1) * rows], 0.0)
        return held

    tape = []
    for layer in range(LAYERS):
        gains = vec[6 * layer : 6 * layer + 6]
        unit_one, scale_one = norm_parts(stream)
        normed = unit_one * gains[0] + gains[1]
        wide = jnp.concatenate([qkv[layer, k] for k in range(3)], axis=1)
        mixed = mm(normed, wide)
        query_high, query_low = two_parts(mixed[:, :128] * 0.25)
        keys, values = pair(mixed[:, 128:256]), pair(mixed[:, 256:])
        kept[layer, 0, 0:rows] = query_high
        kept[layer, 1, 0:rows] = query_low
        for k in range(2):
            kept[layer, 2 + k, 0:rows] = keys[:, k * 128 : (k + 1) * 128]
            kept[layer, 4 + k, 0:rows] = values[:, k * 128 : (k + 1) * 128]
        sums[0, 0:rows] = jnp.zeros((rows, 128), F32)

        def attend(turn, carry, layer=layer):
            masks = [head_of == turn * batch + k for k in range(batch)]
            parts = [masked(kept[layer, k, 0:rows], masks) for k in range(2)]
            keys = [kept[layer, 2 + k, 0:rows] for k in range(2)]
            values = [kept[layer, 4 + k, 0:rows] for k in range(2)]
            scores = dot_nt(
                jnp.concatenate([parts[0], parts[0]], axis=1), jnp.concatenate(keys, axis=1)
            )
            scores = (scores + dot_nt(parts[1], keys[0])).reshape(batch, rows, rows)
            scores = jnp.where(allowed[None], scores, -1e30)
            peak = jnp.max(scores, -1, keepdims=True)
            chance = jnp.exp(scores - peak)
            chance = chance / jnp.sum(chance, -1, keepdims=True)
            high, low = two_parts(chance.reshape(batch * rows, rows))
            spot = pl.ds(pl.multiple_of(turn * (batch * rows), 64), batch * rows)
            chances[layer, 0, spot, 0:rows] = high
            chances[layer, 1, spot, 0:rows] = low
            seen = fold_pair(dot(high, jnp.concatenate(values, axis=1))) + dot(low, values[0])
            sums[0, 0:rows] += unmasked(seen, masks)
            return carry

        lax.fori_loop(0, heads // batch, attend, 0)
        context = sums[0, 0:rows]
        stream = stream + mm(context, output[layer]) + gains[4]
        unit_two, scale_two = norm_parts(stream)
        normed_two = unit_two * gains[2] + gains[3]
        inner, slope = gelu_both(mm(normed_two, up[layer]) + up_bias[layer])
        stream = stream + mm(inner, down[layer]) + gains[5]
        tape.append((unit_one, scale_one, unit_two, scale_two, inner, slope, context))
    end_stream = stream[slots : 2 * slots]
    unit, scale = norm_parts(end_stream)
    final = unit * vec[12] + vec[13]
    logits = jnp.where(lane < ACT, mm(final, head_ref[...]), -1e30)
    peak = jnp.max(logits, -1, keepdims=True)
    powers = jnp.exp(logits - peak)
    total = jnp.sum(powers, -1, keepdims=True)
    chosen = jnp.sum(jnp.where(lane == action, logits, 0.0), -1, keepdims=True)
    terms = jnp.where(valid, jnp.log(total) + peak - chosen, 0.0)
    loss = jnp.sum(terms, axis=0, keepdims=True)
    d_small_ref[72:80] = jnp.broadcast_to(loss, (8, 128))
    d_logits = jnp.where(valid, powers / total, 0.0) - picks
    d_small_ref[48:72] = flat_head(mm_tn(final, d_logits))
    d_final = mm_nt(d_logits, head_ref[...])
    d_vec = [None] * 17
    d_vec[12] = column_sum(d_final * unit)
    d_vec[13] = column_sum(d_final)
    d_end = norm_back(d_final, unit, scale, vec[12])
    blank = jnp.zeros((slots, 128), F32)
    d_stream = jnp.concatenate([blank, d_end, blank], axis=0)
    for layer in reversed(range(LAYERS)):
        unit_one, scale_one, unit_two, scale_two, inner, slope, context = tape[layer]
        gains = vec[6 * layer : 6 * layer + 6]
        d_vec[6 * layer + 5] = column_sum(d_stream)
        d_down[layer] = mm_tn(inner, d_stream)
        d_inner = mm_nt(d_stream, down[layer]) * slope
        d_up_bias[layer] = column_sum(d_inner)
        normed_two = unit_two * gains[2] + gains[3]
        d_up[layer] = mm_tn(normed_two, d_inner)
        d_normed = mm_nt(d_inner, up[layer])
        d_vec[6 * layer + 2] = column_sum(d_normed * unit_two)
        d_vec[6 * layer + 3] = column_sum(d_normed)
        d_stream = d_stream + norm_back(d_normed, unit_two, scale_two, gains[2])
        d_vec[6 * layer + 4] = column_sum(d_stream)
        d_output[layer] = mm_tn(context, d_stream)
        d_context = mm_nt(d_stream, output[layer])
        bases = d_context * context
        high, low = two_parts(d_context)
        for k in range(3):
            sums[k, 0:rows] = jnp.zeros((rows, 128), F32)
        kept[layer, 6, 0:rows] = high
        kept[layer, 7, 0:rows] = low
        sums[3, 0:rows] = bases

        def attend_back(turn, carry, layer=layer):
            masks = [head_of == turn * batch + k for k in range(batch)]
            query = [masked(kept[layer, k, 0:rows], masks) for k in range(2)]
            keys = [kept[layer, 2 + k, 0:rows] for k in range(2)]
            values = [kept[layer, 4 + k, 0:rows] for k in range(2)]
            d_seen = [masked(kept[layer, 6 + k, 0:rows], masks) for k in range(2)]
            base = jnp.sum(masked(sums[3, 0:rows], masks), -1, keepdims=True)
            spot = pl.ds(pl.multiple_of(turn * (batch * rows), 64), batch * rows)
            chance = [chances[layer, k, spot, 0:rows] for k in range(2)]
            d_chance = dot_nt(
                jnp.concatenate([d_seen[0], d_seen[0]], axis=1), jnp.concatenate(values, axis=1)
            )
            d_chance = d_chance + dot_nt(d_seen[1], values[0])
            d_scores = (chance[0].astype(F32) + chance[1].astype(F32)) * (d_chance - base)
            high, low = two_parts(d_scores)
            d_query = fold_pair(dot(high, jnp.concatenate(keys, axis=1))) + dot(low, keys[0])
            sums[0, 0:rows] += unmasked(d_query, masks)
            d_keys = fold_pair(dot_rows(high, jnp.concatenate(query, axis=1)))
            sums[1, 0:rows] += d_keys + dot_rows(low, query[0])
            d_values = fold_pair(dot_rows(chance[0], jnp.concatenate(d_seen, axis=1)))
            sums[2, 0:rows] += d_values + dot_rows(chance[1], d_seen[0])
            return carry

        lax.fori_loop(0, heads // batch, attend_back, 0)
        normed = unit_one * gains[0] + gains[1]
        d_mixed = jnp.concatenate(
            [sums[0, 0:rows] * 0.25, sums[1, 0:rows], sums[2, 0:rows]], axis=1
        )
        wide = jnp.concatenate([qkv[layer, k] for k in range(3)], axis=1)
        d_wide = mm_tn(normed, d_mixed)
        for k in range(3):
            d_qkv[layer, k] = d_wide[:, k * 128 : (k + 1) * 128]
        d_normed = mm_nt(d_mixed, wide)
        d_vec[6 * layer] = column_sum(d_normed * unit_one)
        d_vec[6 * layer + 1] = column_sum(d_normed)
        d_stream = d_stream + norm_back(d_normed, unit_one, scale_one, gains[0])
    d_reward, d_state, d_move = (d_stream[k * slots : (k + 1) * slots] for k in range(3))
    d_times_ref[0:slots] = jnp.where(valid, d_reward + d_state + d_move, 0.0)
    d_reward = d_reward * (1.0 - reward * reward)
    d_vec[14] = column_sum(d_reward * amount)
    d_vec[15] = column_sum(d_reward)
    d_move = d_move * (1.0 - move * move)
    d_small_ref[24:48] = mm_tn(picks, d_move)[0:24]
    d_state = jnp.where(valid, d_state * (1.0 - state * state), 0.0)
    d_vec[16] = column_sum(d_state)
    d_small_ref[0:24] = jnp.concatenate(d_vec + [jnp.zeros((7, 128), F32)], axis=0)
    high, low = two_parts(d_state)
    twice = jnp.concatenate([high, high], axis=1)
    both = jnp.concatenate([high, low], axis=1)
    d_flat = dot_nt(twice, encoder[...]) + dot_nt(low, encoder[:, 0:128])
    d_block = dot_rows(flats[0, 0:slots], both) + dot_rows(flats[1, 0:slots], both)
    d_block = fold_pair(d_block)
    for k in range(28):
        z = jnp.where(valid, z_ref[k, 0:slots], 0.0)
        d_three_ref[k, 0:slots] = d_flat[:, k * 128 : (k + 1) * 128] * gelu_both(z)[1]
        y, v = divmod(k, 4)
        for o in range(2):
            if 2 * v + o < 7:
                d_encoder_ref[pl.ds(y * 7 + 2 * v + o, 64, stride=49), :] = d_block[
                    k * 128 + o * 64 : k * 128 + (o + 1) * 64
                ]


def former_kernel(
    packed,
    slots,
    lengths_from,
    starts_from,
    index_from,
    returns_ref,
    actions_ref,
    z_from,
    flat_ref,
    *refs,
):
    if packed:
        split_ref, refs = refs[0], refs[1:]
    else:
        given, refs = refs[:5], refs[5:]
    (d_three_to, rows_ref), refs = refs[:2], refs[2:]
    if packed:
        parts, refs = refs[:8], refs[8:]
        (d_encoder_ref, d_small_ref, d_split), refs = refs[:3], refs[3:]
        weights, grads, refs = refs[:5], refs[5:10], refs[10:]
    else:
        (d_encoder_ref, d_small_ref), grads, refs = refs[:2], refs[2:7], refs[7:]
        weights = given
    (raw, near, small, rows_raw, times_all, encoder, chances, kept, sums, flats), refs = (
        refs[:10],
        refs[10:],
    )
    z_ref, d_three_ref, head_ref, lengths_ref, starts_ref, index_ref, sem = refs
    used = jnp.int32(0)
    wins = lengths_ref.shape[0]
    scalars = [
        pltpu.make_async_copy(source, target, sem.at[wins + 4 + number])
        for number, (source, target) in enumerate(
            ((lengths_from, lengths_ref), (starts_from, starts_ref), (index_from, index_ref))
        )
    ]
    for copy in scalars:
        copy.start()
    for copy in scalars:
        copy.wait()
    for w in range(wins):
        used = used + lengths_ref[w]

    def z_copy(slots):
        return pltpu.make_async_copy(
            z_from.at[:, pl.ds(0, slots)], z_ref.at[:, pl.ds(0, slots)], sem.at[wins + 3]
        )

    def z_back(slots):
        return pltpu.make_async_copy(
            d_three_ref.at[:, pl.ds(0, slots)], d_three_to.at[:, pl.ds(0, slots)], sem.at[wins + 3]
        )

    copies = [
        pltpu.make_async_copy(flat_ref.at[pl.ds(608, 3144)], raw, sem.at[0]),
        pltpu.make_async_copy(flat_ref.at[pl.ds(3744, 48)], rows_raw.at[wins], sem.at[1]),
        pltpu.make_async_copy(
            flat_ref.at[pl.ds(7872, 24)], rows_raw.at[wins + 1, pl.ds(0, 24)], sem.at[2]
        ),
    ]
    offsets = []
    for w in range(wins):
        row = TIME_ROW + starts_ref[w]
        low = pl.multiple_of(lax.div(row, 8) * 8, 8)
        offsets.append(row - low)
        copies.append(
            pltpu.make_async_copy(
                flat_ref.at[pl.ds(low, 40)], rows_raw.at[w, pl.ds(0, 40)], sem.at[3 + w]
            )
        )
    for copy in copies:
        copy.start()

    z_copy(slots).start()
    if packed:
        unpack_split(split_ref, *weights)
    for copy in copies:
        copy.wait()
    lane = lanes()

    def straight(first, second):
        return jnp.where(lane < 96, pltpu.roll(first, 96, 1), pltpu.roll(second, 96, 1))

    def turn(step, carry):
        spot = pl.multiple_of(step * 64, 64)
        near[pl.ds(spot, 64)] = straight(raw[pl.ds(spot + 1, 64)], raw[pl.ds(spot + 2, 64)])
        return carry

    lax.fori_loop(0, 49, turn, 0)
    for k in range(28):
        y, v = divmod(k, 4)
        halves = []
        for o in range(2):
            if 2 * v + o < 7:
                halves.append(near[pl.ds(y * 7 + 2 * v + o, 64, stride=49), :])
            else:
                halves.append(jnp.zeros((64, 128), F32))
        encoder[k * 128 : (k + 1) * 128] = pair(jnp.concatenate(halves, axis=0))
    small[...] = straight(rows_raw[wins, 1:41], rows_raw[wins, 2:42])
    head_ref[...] = square_head(
        straight(rows_raw[wins + 1, 4:22], rows_raw[wins + 1, 5:23])
    )
    times_all[...] = jnp.zeros(times_all.shape, F32)
    begin = 0
    row = lax.broadcasted_iota(jnp.int32, (32, 1), 0)
    for w in range(wins):
        rows = straight(
            rows_raw[w, pl.ds(offsets[w], 32)], rows_raw[w, pl.ds(offsets[w] + 1, 32)]
        )
        times_all[pl.ds(begin, 32)] = jnp.where(row < lengths_ref[w], rows, 0.0)
        begin = begin + lengths_ref[w]
    rows_ref[...] = jnp.zeros(rows_ref.shape, F32)
    note = jnp.zeros((1, 128), F32)
    for w in range(wins):
        note = jnp.where(lane == w, lengths_ref[w].astype(F32), note)
        note = jnp.where(lane == wins + w, starts_ref[w].astype(F32), note)
    rows_ref[ROOM : ROOM + 1] = note
    d_small_ref[...] = jnp.zeros(d_small_ref.shape, F32)

    z_copy(slots).wait()
    former_body(
        slots,
        used,
        lengths_ref,
        returns_ref,
        actions_ref,
        head_ref,
        z_ref,
        small,
        times_all,
        encoder,
        weights,
        d_three_ref,
        d_encoder_ref,
        d_small_ref,
        rows_ref,
        grads,
        chances,
        kept,
        sums,
        flats,
    )
    z_back(slots).start()

    if packed:
        count = d_small_ref.shape[0] // 4
        pack_split(d_split, *grads)
        for k in range(4):
            parts[k][...] = d_split[jnp.bitwise_xor(index_ref[0], k)]
            e = jnp.bitwise_xor(index_ref[1], k)
            held = d_encoder_ref[pl.ds(pl.multiple_of(e * 784, 8), 784)]
            parts[4 + k][0:784] = held
            held = d_small_ref[pl.ds(pl.multiple_of(e * count, 8), count)]
            parts[4 + k][784 : 784 + count] = held

    z_back(slots).wait()


def former(
    lengths, starts, index, returns, actions, z_three, flat, weights, small_rows, packed, slots
):
    vmem = pl.BlockSpec(memory_space=pltpu.VMEM)
    hbm = pl.BlockSpec(memory_space=pltpu.HBM)
    wins = lengths.shape[0]
    canonical = [
        (LAYERS, 3, 128, 128),
        (LAYERS, 128, 128),
        (LAYERS, 128, FF),
        (LAYERS, 1, FF),
        (LAYERS, FF, 128),
    ]
    outs, out_specs = [(28, ROOM, 128), (ROOM + 8, 128)], [hbm, vmem]
    if packed:
        outs += [(784, 128)] * 4 + [(784 + small_rows // 4, 128)] * 4
        out_specs += [vmem] * 8
        scratch = [
            pltpu.VMEM((3136, 128), F32),
            pltpu.VMEM((small_rows, 128), F32),
            pltpu.VMEM((4, 784, 128), F32),
        ]
        scratch += [pltpu.VMEM(shape, F32) for shape in canonical] * 2
    else:
        outs += [(3136, 128), (small_rows, 128)] + canonical
        out_specs += [vmem] * 7
        scratch = []
    rows = 3 * slots
    scratch += [
        pltpu.VMEM((3144, 128), F32),
        pltpu.VMEM((3136, 128), F32),
        pltpu.VMEM((40, 128), F32),
        pltpu.VMEM((wins + 2, 48, 128), F32),
        pltpu.VMEM((ROOM + 32, 128), F32),
        pltpu.VMEM((3584, 256), BF16),
        pltpu.VMEM((LAYERS, 2, 8 * rows, rows), BF16),
        pltpu.VMEM((LAYERS, 8, rows, 128), BF16),
        pltpu.VMEM((4, rows, 128), F32),
        pltpu.VMEM((2, ROOM, 3584), BF16),
        pltpu.VMEM((28, ROOM, 128), F32),
        pltpu.VMEM((28, ROOM, 128), F32),
        pltpu.VMEM((128, 128), F32),
        pltpu.SMEM((wins,), jnp.int32),
        pltpu.SMEM((wins,), jnp.int32),
        pltpu.SMEM((2,), jnp.int32),
        pltpu.SemaphoreType.DMA((wins + 7,)),
    ]
    return pl.pallas_call(
        partial(former_kernel, packed, slots),
        in_specs=[hbm] * 3 + [vmem] * 2 + [hbm] * 2 + [vmem] * len(weights),
        out_specs=out_specs,
        out_shape=[jax.ShapeDtypeStruct(shape, F32) for shape in outs],
        scratch_shapes=scratch,
        compiler_params=pltpu.CompilerParams(vmem_limit_bytes=62 * 1024 * 1024),
        name=f"transformer_step_{slots}",
    )(lengths, starts, index, returns, actions, z_three, flat, *weights)


SMALL = [("vectors", 24), ("action_table", 24), ("head", 24), ("loss", 8)]
FIELD_ROWS = 8200
EARLY_ROWS = CONV_ROWS + 3136
TABLE_AT = CONV_ROWS + 3136 + 17 + ACT


def round_up(number, grain):
    return -(-number // grain) * grain


def chunk_of(tiles):
    return max(size for size in range(1, 9) if tiles % size == 0)


def mesh_bits(dp_size, mp_size):
    dp_bits = [("dp", k) for k in range(dp_size.bit_length() - 1)]
    mp_bits = [("mp", k) for k in range(mp_size.bit_length() - 1)]
    middle = (len(dp_bits) - 1) // 2
    return mp_bits[:1], mp_bits[1:], dp_bits[:middle], dp_bits[middle:]


def reduce_kernel(plan, *refs):
    mp_size, quarter, share = plan["mp_size"], plan["quarter"], plan["share"]
    split_parts, own_parts, conv_ref = refs[:mp_size], refs[mp_size : 2 * mp_size], refs[2 * mp_size]
    refs = refs[2 * mp_size + 1 :]
    (early_out, small_out, split_out, square_out), refs = refs[:4], refs[4:]
    (split_stage, own_stage, work, landing, split_total, own_total, conv_total), refs = (
        refs[:7],
        refs[7:],
    )
    tiles, tile_in, load_sem, send_sem, recv_sem, store_sem = refs
    spots = {"dp": lax.axis_index("dp"), "mp": lax.axis_index("mp")}
    cores, ys, xs, zs = plan["bits"]
    slots = iter(range(plan["copies"]))

    def value(bit):
        return lax.rem(lax.div(spots[bit[0]], 1 << bit[1]), 2)

    def turned(stage, mask):
        index = 0
        for k, bit in enumerate(stage):
            own = value(bit)
            index = index + ((1 - own) if mask & (1 << k) else own) * (1 << k)
        return index

    def partner(stage, mask):
        place = dict(spots)
        for k, bit in enumerate(stage):
            if mask & (1 << k):
                place[bit[0]] = place[bit[0]] + (1 - 2 * value(bit)) * (1 << bit[1])
        return (place["dp"], place["mp"])

    def masks_of(stage):
        return range(1, 1 << len(stage))

    def send(source, target, stage, mask):
        slot = next(slots)
        copy = pltpu.make_async_remote_copy(
            src_ref=source,
            dst_ref=target,
            send_sem=send_sem.at[slot],
            recv_sem=recv_sem.at[slot],
            device_id=partner(stage, mask),
            device_id_type=pl.DeviceIdType.MESH,
        )
        copy.start()
        return copy

    loads = []
    for k in range(mp_size):
        for parts, stage in ((own_parts, own_stage), (split_parts, split_stage)):
            copy = pltpu.make_async_copy(parts[k], stage.at[k], load_sem.at[len(loads)])
            loads.append(copy)
    conv_tiles = CONV_ROWS // 8
    target = work.at[pl.ds(plan["conv"], conv_tiles)]
    loads.append(pltpu.make_async_copy(conv_ref, target, load_sem.at[len(loads)]))
    for load in loads:
        load.start()

    def wipe(target, start, count):
        if count > 0:
            target[start : start + count] = jnp.zeros((count, 8, 128), F32)

    wipe(work, plan["conv"] + conv_tiles, plan["conv_size"] - conv_tiles)
    wipe(work, plan["split"] + quarter, plan["split_size"] - quarter)
    wipe(work, plan["own"] + quarter + share, plan["own_size"] - quarter - share)
    barrier = pltpu.get_barrier_semaphore()
    greeted = [(stage, mask) for stage in (cores + ys, xs, zs) for mask in masks_of(stage)]
    for stage, mask in greeted:
        pl.semaphore_signal(
            barrier,
            inc=1,
            device_id=partner(stage, mask),
            device_id_type=pl.DeviceIdType.MESH,
        )
    pl.semaphore_wait(barrier, len(greeted))

    def sum_into(target, start, pieces, count):
        chunk = chunk_of(count)

        def body(turn, carry):
            held = pieces[0][0][pl.ds(pieces[0][1] + turn * chunk, chunk)]
            for source, at in pieces[1:]:
                held = held + source[pl.ds(at + turn * chunk, chunk)]
            target[pl.ds(start + turn * chunk, chunk)] = held
            return carry

        lax.fori_loop(0, count // chunk, body, 0)

    class Stream:
        def __init__(self, base, size, stages, total, total_at):
            self.base, self.size, self.stages = base, size, stages
            self.total, self.at = total, total_at
            self.land = base
            self.flight = None
            self.step = 0
            self.start = base

        def reduce(self):
            if self.flight is not None:
                copies, piece, lands, keep = self.flight
                for copy in copies:
                    copy.wait()
                pieces = [(work, keep)] + [(landing, land) for land in lands]
                sum_into(work, keep, pieces, piece)
                self.base, self.size, self.flight = keep, piece, None
            if self.step < len(self.stages):
                stage = self.stages[self.step]
                piece = self.size >> len(stage)
                keep = self.base + turned(stage, 0) * piece
                copies, lands = [], []
                for mask in masks_of(stage):
                    give = self.base + turned(stage, mask) * piece
                    target = landing.at[pl.ds(self.land, piece)]
                    copies.append(send(work.at[pl.ds(give, piece)], target, stage, mask))
                    lands.append(self.land)
                    self.land += piece
                self.flight = (copies, piece, lands, keep)
                self.step += 1

        def turn(self):
            self.at = self.at + (self.base - self.start)
            sum_into(self.total, self.at, [(work, self.base)], self.size)
            self.step = 0

        def double(self):
            if self.flight is not None:
                for copy in self.flight:
                    copy.wait()
                stage = self.stages[len(self.stages) - self.step]
                self.at = self.at - turned(stage, 0) * self.size
                self.size, self.flight = self.size << len(stage), None
            if self.step < len(self.stages):
                stage = self.stages[len(self.stages) - 1 - self.step]
                region = self.total.at[pl.ds(self.at, self.size)]
                self.flight = [send(region, region, stage, mask) for mask in masks_of(stage)]
                self.step += 1

        def squares(self, keep):
            held = work[pl.ds(self.base, self.size)]
            if keep is not None:
                tile = lax.broadcasted_iota(jnp.int32, (self.size, 8, 128), 0)
                held = jnp.where(keep(tile + self.base), held, 0.0)
            return jnp.sum(held * held, axis=0)

    sharing = cores + xs
    seat = sum(value(bit) * (1 << k) for k, bit in enumerate(sharing))

    def keep_own(tile):
        place = tile - plan["own"] - quarter
        return (place < 0) | (place + seat * share < 9)

    class Quarter:
        def __init__(self, stream, offset, stages):
            self.at = stream.base - stream.start + offset
            self.size, self.stages = stream.size, stages
            self.held, self.flights, self.step = [0], [], 0
            sum_into(own_total.at[seat], self.at, [(work, stream.base)], stream.size)

        def region(self, offset):
            return own_total.at[turned(sharing, offset), pl.ds(self.at, self.size)]

        def double(self):
            if self.flights:
                for copy in self.flights:
                    copy.wait()
                stage = self.stages[self.step - 1]
                if stage[0] in sharing:
                    changed = 1 << sharing.index(stage[0])
                    self.held = self.held + [offset | changed for offset in self.held]
                else:
                    self.at = self.at - turned(stage, 0) * self.size
                    self.size <<= len(stage)
                self.flights = []
            if self.step < len(self.stages):
                stage = self.stages[self.step]
                for offset in self.held:
                    region = self.region(offset)
                    self.flights += [send(region, region, stage, mask) for mask in masks_of(stage)]
                self.step += 1

    first, second = plan["cut"]
    own = [
        Stream(plan["own"], first, [ys, zs], None, 0),
        Stream(plan["own"] + first, plan["own_size"] - first, [zs, ys], None, 0),
    ]
    split = [
        Stream(plan["split"], second, [xs, zs], split_total, 0),
        Stream(
            plan["split"] + second,
            plan["split_size"] - second,
            [zs, xs],
            split_total,
            second,
        ),
    ]
    conv = Stream(plan["conv"], plan["conv_size"], [cores + ys, xs, zs], conv_total, 0)
    for load in loads:
        load.wait()
    sum_into(
        work,
        plan["own"],
        [(own_stage.at[k], 0) for k in range(mp_size)],
        quarter + share,
    )
    for stream in own + [conv]:
        stream.reduce()
    sum_into(work, plan["split"], [(split_stage.at[k], 0) for k in range(mp_size)], quarter)
    for stream in own + [conv]:
        stream.reduce()
    for stream in split:
        stream.reduce()
    for stream in own:
        stream.reduce()
    squares = jnp.zeros((8, 128), F32)
    singles = [[bit] for bit in xs]
    quarters = [
        Quarter(own[0], 0, [zs, ys] + singles + [cores]),
        Quarter(own[1], first, [ys] + singles + [zs, cores]),
    ]
    for piece in quarters:
        piece.double()
    conv.reduce()
    for stream in split:
        stream.reduce()
    for stream in own:
        squares = squares + stream.squares(keep_own)
    for piece in quarters:
        piece.double()
    conv.reduce()
    squares = squares + conv.squares(None)
    conv.turn()
    conv.double()
    for stream in split:
        stream.reduce()
        squares = squares + stream.squares(None)
    tiles[0] = squares
    tile_stages = [cores + ys, xs, zs]

    def send_tiles(number):
        stage = tile_stages[number]
        spot = number * 8 - 1
        return [
            send(tiles.at[number], tile_in.at[spot + mask], stage, mask)
            for mask in masks_of(stage)
        ]

    tile_flights = send_tiles(0)
    for stream in split:
        stream.turn()
        stream.double()
    rounds = 1
    while rounds <= len(tile_stages) or conv.flight is not None or quarters[0].flights:
        for stream in quarters + [conv]:
            stream.double()
        if rounds <= len(tile_stages):
            for copy in tile_flights:
                copy.wait()
            held = tiles[rounds - 1]
            for mask in masks_of(tile_stages[rounds - 1]):
                held = held + tile_in[(rounds - 1) * 8 - 1 + mask]
            tiles[rounds] = held
            if rounds < len(tile_stages):
                tile_flights = send_tiles(rounds)
        for stream in split:
            stream.double()
        rounds += 1
    square_out[...] = tiles[len(tile_stages)]
    stores = [
        (conv_total.at[pl.ds(0, conv_tiles)], early_out.at[pl.ds(0, conv_tiles)]),
        (split_total.at[pl.ds(0, quarter)], split_out),
    ]
    for m in range(mp_size):
        rows = pl.ds(conv_tiles + m * quarter, quarter)
        stores.append((own_total.at[m, pl.ds(0, quarter)], early_out.at[rows]))
        rows = pl.ds(m * share, share)
        stores.append((own_total.at[m, pl.ds(quarter, share)], small_out.at[rows]))
    stores = [
        pltpu.make_async_copy(source, target, store_sem.at[number])
        for number, (source, target) in enumerate(stores)
    ]
    for copy in stores:
        copy.start()
    for copy in stores:
        copy.wait()


def reduce_all(split_parts, own_parts, conv, dp_size, mp_size):
    bits = mesh_bits(dp_size, mp_size)
    quarter = split_parts[0].shape[0] // 8
    share = own_parts[0].shape[0] // 8 - quarter
    own_size = round_up(quarter + share, dp_size)
    split_size = round_up(quarter, dp_size)
    conv_size = round_up(CONV_ROWS // 8, dp_size * mp_size)
    places, at = {}, 0
    for name, size in [("split", split_size), ("own", own_size), ("conv", conv_size)]:
        places[name] = at
        at += size
    cut = (round_up(own_size // 2, dp_size), round_up(split_size // 2, dp_size))
    copies = 16 * (dp_size + mp_size) + 2 * mp_size * dp_size
    plan = dict(
        places,
        mp_size=mp_size,
        quarter=quarter,
        share=share,
        bits=bits,
        copies=copies,
        split_size=split_size,
        own_size=own_size,
        conv_size=conv_size,
        cut=cut,
    )
    vmem = pl.BlockSpec(memory_space=pltpu.VMEM)
    any_spec = pl.BlockSpec(memory_space=pl.ANY)
    arrays = [*split_parts, *own_parts, conv]
    loads = len(arrays)

    def tiled(size, *lead):
        return pltpu.VMEM((*lead, size, 8, 128), F32)

    outs = [(EARLY_ROWS // 8, 8, 128), (share * mp_size, 8, 128), (quarter, 8, 128), (8, 128)]
    results = pl.pallas_call(
        partial(reduce_kernel, plan),
        in_specs=[any_spec] * loads,
        out_specs=[any_spec, any_spec, any_spec, vmem],
        out_shape=[jax.ShapeDtypeStruct(shape, F32) for shape in outs],
        scratch_shapes=[
            tiled(quarter, mp_size),
            tiled(quarter + share, mp_size),
            tiled(at),
            tiled(at),
            tiled(split_size),
            tiled(own_size, mp_size),
            tiled(conv_size),
            pltpu.VMEM((4, 8, 128), F32),
            pltpu.VMEM((24, 8, 128), F32),
            pltpu.SemaphoreType.DMA((loads,)),
            pltpu.SemaphoreType.DMA((copies,)),
            pltpu.SemaphoreType.DMA((copies,)),
            pltpu.SemaphoreType.DMA((2 + 2 * mp_size,)),
        ],
        compiler_params=pltpu.CompilerParams(
            collective_id=1, has_side_effects=True, vmem_limit_bytes=62 * 1024 * 1024
        ),
        name="reduce_gradients",
    )(*[array.reshape(-1, 8, 128) for array in arrays])
    return [held.reshape(-1, 128) for held in results]


FLAT_ROWS = 7896
BLOCK_ROWS = 1024
LATE = 609
SPAN = 40


def adam_kernel(
    wins,
    early_ref,
    rows_ref,
    small_ref,
    split_ref,
    square_ref,
    weight_ref,
    first_ref,
    second_ref,
    split_weight_ref,
    split_first_ref,
    split_second_ref,
    new_ref,
    new_first_ref,
    new_second_ref,
    low_ref,
    split_new_ref,
    split_new_first_ref,
    split_new_second_ref,
    split_low_ref,
    norm_out,
    loss_out,
    count_out,
    split_in,
    split_out,
    field,
    rows,
    notes,
    marks,
    pulled,
    factor_ref,
    pull_sem,
    load_sem,
    split_sem,
):
    step = pl.program_id(0)
    last = pl.num_programs(0) - 1
    scalar_refs = (norm_out, loss_out, count_out)
    lane = lax.broadcasted_iota(jnp.int32, (1, 128), 1)

    def pull(block, slot):
        start = pl.multiple_of(block * BLOCK_ROWS, BLOCK_ROWS)
        return pltpu.make_async_copy(
            field.at[pl.ds(start, BLOCK_ROWS + 8)], pulled.at[slot], pull_sem.at[slot]
        )

    def update(weights, first, second, grads):
        first = beta_first * first + (1 - beta_first) * grads
        second = beta_second * second + (1 - beta_second) * grads * grads
        fix_one = 1.0 / (1 - beta_first**STEP)
        fix_two = 1.0 / (1 - beta_second**STEP)
        weights = weights - learn_rate * (
            first * fix_one / (jnp.sqrt(second * fix_two) + adam_epsilon) + weight_decay * weights
        )
        return weights, first, second

    def sum_of(tile):
        held = jnp.sum(jnp.sum(tile, axis=0, keepdims=True), axis=1, keepdims=True)
        return jnp.broadcast_to(held, (1, 128))

    slot = lax.rem(step, 2)
    split_loads = [
        pltpu.make_async_copy(ref, split_in.at[k], split_sem.at[k])
        for k, ref in enumerate((split_weight_ref, split_first_ref, split_second_ref))
    ]
    split_stores = [
        pltpu.make_async_copy(split_out.at[k], ref, split_sem.at[3 + k])
        for k, ref in enumerate((split_new_ref, split_new_first_ref, split_new_second_ref))
    ]

    @pl.when(step == 0)
    def prepare():
        for load in split_loads:
            load.start()
        load_rows = pltpu.make_async_copy(rows_ref, rows, load_sem.at[0])
        load_early = pltpu.make_async_copy(
            early_ref, field.at[pl.ds(0, EARLY_ROWS)], load_sem.at[1]
        )
        load_rows.start()
        load_early.start()
        late = FIELD_ROWS - EARLY_ROWS
        field[EARLY_ROWS:FIELD_ROWS] = jnp.zeros((late, 128), F32)
        load_rows.wait()
        stride = ROOM + 8
        devices = rows.shape[0] // stride
        notes[...] = rows[pl.ds(ROOM, devices, stride=stride), :]
        mark = pltpu.make_async_copy(notes, marks, load_sem.at[2])
        mark.start()
        mark.wait()
        place = lax.broadcasted_iota(jnp.int32, (SPAN, ROOM), 0)
        slot_of = lax.broadcasted_iota(jnp.int32, (SPAN, ROOM), 1)

        def scatter(turn, carry):
            spots, found = [], []
            for k in range(4):
                device = turn * 4 + k
                begin = jnp.int32(0)
                picks = []
                for w in range(wins):
                    length = marks[device, w].astype(jnp.int32)
                    row = marks[device, wins + w].astype(jnp.int32) + TABLE_AT
                    low = lax.div(row, 8) * 8
                    inside = (slot_of >= begin) & (slot_of < begin + length)
                    inside = inside & (place - slot_of == row - low - begin)
                    picks.append(jnp.where(inside, 1.0, 0.0).astype(BF16))
                    spots.append(low)
                    begin = begin + length
                held = pair(rows[pl.ds(pl.multiple_of(device * stride, 8), ROOM)])
                found.append(fold_pair(dot(jnp.concatenate(picks, axis=0), held)))
            for k in range(4):
                for w in range(wins):
                    spot = pl.ds(pl.multiple_of(spots[k * wins + w], 8), SPAN)
                    field[spot] = field[spot] + found[k][w * SPAN : (w + 1) * SPAN]
            return carry

        lax.fori_loop(0, devices // 4, scatter, 0)

        def fold(turn, carry):
            spot = pl.multiple_of(EARLY_ROWS + turn * 256, 8)
            held = field[pl.ds(spot, 256)]
            return carry + jnp.sum((held * held).reshape(32, 8, 128), axis=0)

        squares = lax.fori_loop(0, late // 256, fold, square_ref[...])
        at = EARLY_ROWS
        for name_at, size in [(0, 17), (24, ACT)]:
            field[at : at + size] = small_ref[name_at : name_at + size]
            at += size
        at = TABLE_AT + TSTEPS
        field[at : at + ACT] = small_ref[48 : 48 + ACT]
        lane_all = lax.broadcasted_iota(jnp.int32, notes.shape, 1)
        count = sum_of(jnp.where(lane_all < wins, notes[...], 0.0))
        seed = 1.0 / count
        norm = jnp.sqrt(sum_of(squares)) * seed
        factor = jnp.minimum(1.0, clip_limit / (norm + 1e-06)) * seed
        factor_ref[...] = jnp.broadcast_to(factor, (8, 128))
        loss = small_ref[72:73]
        for number, held in enumerate((norm, loss, count)):
            scalar_refs[number][0] = jnp.sum(jnp.where(lane == 0, held, 0.0))
        load_early.wait()
        pull(0, 0).start()

    @pl.when(step < last)
    def ahead():
        pull(step + 1, 1 - slot).start()

    @pl.when(step == 1)
    def split():
        for load in split_loads:
            load.wait()
        count = split_in.shape[1]
        outs = update(*[split_in[k] for k in range(3)], split_ref[0:count] * factor_ref[0:1])
        for k in range(3):
            split_out[k] = outs[k]
        split_low_ref[...] = outs[0].astype(BF16)
        for store in split_stores:
            store.start()

    @pl.when(step == last)
    def split_end():
        for store in split_stores:
            store.wait()

    pull(step, slot).wait()
    early = pulled[slot, 0:BLOCK_ROWS]
    own = pltpu.roll(pulled[slot, 7 : BLOCK_ROWS + 7], 32, 1)
    before = pltpu.roll(pulled[slot, 6 : BLOCK_ROWS + 6], 32, 1)
    row = lax.broadcasted_iota(jnp.int32, (BLOCK_ROWS, 1), 0) + step * BLOCK_ROWS
    grads = jnp.where(lane < 32, jnp.where(row == LATE, early, before), own)
    grads = jnp.where(row < LATE, early, grads)
    outs = update(weight_ref[...], first_ref[...], second_ref[...], grads * factor_ref[0:1])
    new_ref[...], new_first_ref[...], new_second_ref[...] = outs
    low_ref[...] = outs[0].astype(BF16)


def adam_all(early, rows, small, split_grad, square, shared, split, wins):
    grid = -(-FLAT_ROWS // BLOCK_ROWS)
    flat_spec = pl.BlockSpec((BLOCK_ROWS, 128), lambda i: (i, 0))
    split_rows = split[0].shape[0]
    devices = rows.shape[0]

    def whole(shape):
        return pl.BlockSpec(shape, lambda i: (0,) * len(shape))

    shared_out = jax.ShapeDtypeStruct((FLAT_ROWS, 128), F32)
    split_out = jax.ShapeDtypeStruct((split_rows, 128), F32)
    any_spec = pl.BlockSpec(memory_space=pl.ANY)
    return pl.pallas_call(
        partial(adam_kernel, wins),
        grid=(grid,),
        in_specs=[
            any_spec,
            any_spec,
            whole(small.shape),
            whole(split_grad.shape),
            whole((8, 128)),
            flat_spec,
            flat_spec,
            flat_spec,
            any_spec,
            any_spec,
            any_spec,
        ],
        out_specs=[flat_spec] * 4
        + [any_spec] * 3
        + [whole((split_rows, 128))]
        + [pl.BlockSpec(memory_space=pltpu.SMEM)] * 3,
        out_shape=[shared_out] * 3
        + [jax.ShapeDtypeStruct((FLAT_ROWS, 128), BF16)]
        + [split_out] * 3
        + [jax.ShapeDtypeStruct((split_rows, 128), BF16)]
        + [jax.ShapeDtypeStruct((1,), F32)] * 3,
        scratch_shapes=[
            pltpu.VMEM((3, split_rows, 128), F32),
            pltpu.VMEM((3, split_rows, 128), F32),
            pltpu.VMEM((FIELD_ROWS, 128), F32),
            pltpu.VMEM((devices * (ROOM + 8), 128), F32),
            pltpu.VMEM((devices, 128), F32),
            pltpu.SMEM((devices, 128), F32),
            pltpu.VMEM((2, BLOCK_ROWS + 8, 128), F32),
            pltpu.VMEM((8, 128), F32),
            pltpu.SemaphoreType.DMA((2,)),
            pltpu.SemaphoreType.DMA((3,)),
            pltpu.SemaphoreType.DMA((6,)),
        ],
        compiler_params=pltpu.CompilerParams(vmem_limit_bytes=62 * 1024 * 1024),
        name="adam_update",
    )(
        early,
        rows.reshape(devices * (ROOM + 8), 128),
        small,
        split_grad,
        square,
        *shared,
        *split,
    )


def per_device(
    frames,
    returns,
    actions,
    starts,
    lengths,
    shared_weights,
    shared_first,
    shared_second,
    split_weights,
    split_first,
    split_second,
):
    dp_size, mp_size = lax.axis_size("dp"), lax.axis_size("mp")
    narrow = D // mp_size
    hidden_width = FF // mp_size
    wins, steps = returns.shape
    width = split_weights.shape[0]
    split_rows = width // 128
    packed = narrow == 32
    own_rows = split_weights.reshape(split_rows, 128)
    split_all = lax.all_gather(own_rows, "mp", axis=0)
    flat = shared_weights.reshape(FLAT_ROWS, 128)
    picked, z_one, z_two, z_three = conv_forward(lengths, frames, flat)
    if packed:
        weights = [split_all]
    else:
        layers, layers_back = jax.vjp(
            lambda held: assemble(held, mp_size, narrow, hidden_width), split_all.reshape(-1)
        )
        weights = [
            jnp.stack([layer["qkv"].transpose(1, 0, 2) for layer in layers]),
            jnp.stack([layer["output"] for layer in layers]),
            jnp.stack([layer["up"] for layer in layers]),
            jnp.stack([layer["up_bias"][None] for layer in layers]),
            jnp.stack([layer["down"] for layer in layers]),
        ]
    small_rows = round_up(sum(rows for name, rows in SMALL), 8 * mp_size)
    cores, ys, xs, zs = mesh_bits(dp_size, mp_size)
    seat = jnp.bitwise_and(lax.axis_index("mp"), 1)
    seat = seat + 2 * jnp.bitwise_and(lax.axis_index("dp"), (1 << len(xs)) - 1)
    index = jnp.stack([lax.axis_index("mp"), seat])
    def step_of(slots):
        def run(operands):
            return tuple(former(*operands, small_rows, packed, slots))

        return run

    results = lax.cond(
        jnp.sum(lengths) <= HALF,
        step_of(HALF),
        step_of(ROOM),
        (lengths, starts, index, returns, actions, z_three, flat, weights),
    )
    d_three, rows = results[:2]
    rows_all = lax.all_gather(rows, ("dp", "mp"), axis=0)
    quarter = 3136 // mp_size
    if packed:
        split_parts, own_parts = results[2:6], results[6:]
    else:
        d_encoder, d_small, d_qkv, d_output, d_up, d_up_bias, d_down = results[2:]
        grad_layers = [
            dict(
                qkv=d_qkv[layer].transpose(1, 0, 2),
                output=d_output[layer],
                up=d_up[layer],
                up_bias=d_up_bias[layer, 0],
                down=d_down[layer],
            )
            for layer in range(LAYERS)
        ]
        gathered = layers_back(grad_layers)[0].reshape(mp_size, split_rows, 128)
        gathered = jnp.pad(gathered, ((0, 0), (0, quarter - split_rows), (0, 0)))
        encoder = d_encoder.reshape(mp_size, quarter, 128)
        small = d_small.reshape(mp_size, -1, 128)
        every = jnp.concatenate([encoder, small], axis=1)

        def turned(held, own):
            return [
                lax.dynamic_index_in_dim(held, jnp.bitwise_xor(own, k), 0, keepdims=False)
                for k in range(mp_size)
            ]

        split_parts, own_parts = turned(gathered, index[0]), turned(every, index[1])
    split_parts, own_parts = list(split_parts), list(own_parts)
    for k in range(1, mp_size):
        turn = [(place, place ^ k) for place in range(mp_size)]
        split_parts[k] = lax.ppermute(split_parts[k], "mp", turn)
        turn = [
            (dp * mp_size + mp, (dp ^ (k >> 1)) * mp_size + (mp ^ (k & 1)))
            for dp in range(dp_size)
            for mp in range(mp_size)
        ]
        own_parts[k] = lax.ppermute(own_parts[k], ("dp", "mp"), turn)
    d_conv = conv_backward(lengths, picked, z_one, z_two, d_three, flat)
    early, small, split_sum, square = reduce_all(
        split_parts, own_parts, d_conv, dp_size, mp_size
    )
    shared_view = [a.reshape(FLAT_ROWS, 128) for a in (shared_weights, shared_first, shared_second)]
    split_view = [a.reshape(split_rows, 128) for a in (split_weights, split_first, split_second)]
    updated = adam_all(
        early, rows_all, small, split_sum, square, shared_view, split_view, wins
    )
    shared_out = [a.reshape(-1) for a in updated[:4]]
    split_out = [a.reshape(-1) for a in updated[4:8]]
    return (*shared_out, *split_out, *[held.reshape(()) for held in updated[8:]])


def solution(mesh):
    return jax.shard_map(
        per_device,
        mesh=mesh,
        in_specs=(
            P(("dp", "mp"), None, None, None, None),
            P(("dp", "mp"), None),
            P(("dp", "mp"), None),
            P(("dp", "mp")),
            P(("dp", "mp")),
            P(),
            P(),
            P(),
            P("mp"),
            P("mp"),
            P("mp"),
        ),
        out_specs=(P(), P(), P(), P(), P("mp"), P("mp"), P("mp"), P("mp"), P(), P(), P()),
        check_vma=False,
    )
```
